128 devices in a mesh: panel: 2 (over y_lo), lon: 16 (over y_hi, z, core), colat: 4 (over x).
Axes of the slice: x: 4, y: 4 (y_hi: 2, y_lo: 2; y = y_hi * 2 + y_lo), z: 4, core: 2. Of those that a mesh axis runs over, the one named last changes fastest.
Arguments:
- state: float32 [2, 8, 4, 768, 512], P('panel', None, None, 'lon', 'colat'), may hold values from -2 to 2
- send_base: int32 [2, 64, 240], P('panel', ('lon', 'colat')), may hold values from 0 to 6014, as said below
- send_frac: float32 [2, 64, 2, 240], P('panel', ('lon', 'colat')), may hold values from 0 to 1
- recv_slots: int32 [2, 64, 1056], P('panel', ('lon', 'colat')), may hold values from -1 to 15359, as said below
Outputs:
- new_state: float32 [2, 8, 4, 768, 512], P('panel', None, None, 'lon', 'colat')
The draws below stay inside these ranges and needn't reach their ends.
Inputs may be any that keep to these rules, and one draw needn't show every extreme that they name: `send_base`: A flat offset on the sender tile's block whose four stencil cells base, base + 1, base + 128, base + 129 lie on that block, in every slot. `recv_slots`: -1 exactly on the sides of a tile that lie inside its panel; every border cell outside the panel names a slot s * 240 + c of sender tile s of the other panel, each slot at most once. Which slots are used is drawn; some sender tile has all 240 of its slots used.
All inputs are finite; a program needn't handle non-finite values.
Results may differ from the reference program's by a relative error of at most 0.0003.
Values sent between devices are 32-bit elements; how exact they have to be, the bound alone decides.
A program may use at most 64 MiB of HBM per device.

```python
import math
import jax
import jax.numpy as jnp
from jax import lax

PH = 48
TH = 128
R = 4
STATE_QUANTITIES = 8
HALO = 3
TILES = 64
NPH = 768
NTH = 512
CYCLE = 1056
OUT = 240
N_LON = 16
N_COLAT = 4


def draw_send_base(key, part):
    key = jax.random.fold_in(key, 5)
    row_key, col_key, first_key, second_key = jax.random.split(key, 4)
    total = 2 * TILES * OUT
    rows = jax.random.randint(row_key, (total,), 0, PH - 1, dtype=jnp.int32)
    cols = jax.random.randint(col_key, (total,), 0, TH - 1, dtype=jnp.int32)
    bases = rows * TH + cols
    first = jax.random.randint(first_key, (), 0, total, dtype=jnp.int32)
    second = (first + 1 + jax.random.randint(second_key, (), 0, total - 1, dtype=jnp.int32)) % total
    bases = bases.at[first].set(PH * TH - TH - 2).at[second].set(0)
    return bases.reshape(2, TILES, OUT).astype(jnp.int32)


def one_panel(key):
    used = HALO * (2 * N_LON * PH + 2 * N_COLAT * TH)
    side = jnp.concatenate([jnp.zeros((HALO * PH,), jnp.int32), jnp.ones((HALO * PH,), jnp.int32), jnp.full((HALO * TH,), 2, jnp.int32), jnp.full((HALO * TH,), 3, jnp.int32)])
    tiles = jnp.arange(TILES, dtype=jnp.int32)
    lon_ids = (tiles // N_COLAT)[:, None]
    col_ids = (tiles % N_COLAT)[:, None]
    side = side[None, :]
    live = (side == 0) & (col_ids == 0) | (side == 1) & (col_ids == N_COLAT - 1) | (side == 2) & (lon_ids == 0) | (side == 3) & (lon_ids == N_LON - 1)
    order = jnp.argsort(jnp.where(live.reshape(-1), 0, 1).astype(jnp.int32), stable=True)
    live_list = order[:used]
    prio_key, hot_key, cell_key = jax.random.split(key, 3)
    slot_count = TILES * OUT
    priority = jax.random.permutation(prio_key, slot_count).astype(jnp.int32)
    hot = jax.random.randint(hot_key, (), 0, TILES, dtype=jnp.int32)
    slot_ids = jnp.arange(slot_count, dtype=jnp.int32)
    boosted = priority + jnp.where((slot_ids // OUT == hot) | (slot_ids == slot_count - 1), slot_count, 0)
    chosen = jnp.argsort(-boosted, stable=True)[:used].astype(jnp.int32)
    shuffle = jax.random.permutation(cell_key, used)
    result = jnp.full((TILES * CYCLE,), -1, jnp.int32).at[live_list[shuffle]].set(chosen)
    return result.reshape(TILES, CYCLE)


def draw_recv_slots(key, part):
    key = jax.random.fold_in(key, 7)
    return jnp.stack([one_panel(jax.random.fold_in(key, 1)), one_panel(jax.random.fold_in(key, 2))])


def level_of(own_key, shape, cuts, low, largest):
    def one(axis_at, shards_of):
        steps = jax.random.uniform(jax.random.fold_in(jax.random.fold_in(own_key, 6), axis_at), (shards_of,), jnp.float32, low / len(cuts), largest / len(cuts))
        return jnp.repeat(jnp.exp(steps), shape[axis_at] // shards_of).reshape((-1,) + (1,) * (len(shape) - axis_at - 1))

    level = one(*cuts[0])
    for cut in cuts[1:]:
        level = level * one(*cut)
    return level


def noise(own_key, shape, scale, limit, cuts=(), kind=jnp.bfloat16):
    loudness = level_of(own_key, shape, cuts, -0.22, 0.18) if cuts else 1.0
    array = jax.random.normal(own_key, shape, jnp.float32) * scale * loudness
    return jnp.minimum(jnp.maximum(array, -limit), limit).astype(kind)


def setup_inputs(seed: int = 0) -> dict:
    key_of = jax.random.split(jax.random.key(seed), 5)
    return {
        "state": noise(key_of[0], (2, STATE_QUANTITIES, R, NPH, NTH), 0.5, 2.0, ((0, 2), (3, 16), (4, 4)), jnp.float32),
        "send_base": draw_send_base(jax.random.fold_in(key_of[4], 71), 0),
        "send_frac": jnp.clip(1.0 * jax.random.uniform(key_of[2], (2, TILES, 2, OUT), jnp.float32) ** level_of(key_of[2], (2, TILES, 2, OUT), ((0, 2), (1, 64)), -0.2, 0.2), 0.0, 1.0),
        "recv_slots": draw_recv_slots(jax.random.fold_in(key_of[4], 71), 0),
    }


VISCOSITY = 0.1
RESISTIVITY = 0.1
THERMAL_SPREAD = 0.1
ISENTROPIC_INDEX = 5.0 / 3.0
TIME_STEP = 0.25


def shifted_array(padded, direction_axis, offset):
    selector = [slice(None)] * padded.ndim
    for direction in (-3, -2, -1):
        extent = padded.shape[direction]
        if direction == direction_axis:
            selector[direction] = slice(HALO + offset, extent - HALO + offset)
        else:
            selector[direction] = slice(HALO, extent - HALO)
    return padded[tuple(selector)]


def first_derivative(padded, direction_axis):
    first_pair = shifted_array(padded, direction_axis, 1) - shifted_array(padded, direction_axis, -1)
    second_pair = shifted_array(padded, direction_axis, 2) - shifted_array(padded, direction_axis, -2)
    third_pair = shifted_array(padded, direction_axis, 3) - shifted_array(padded, direction_axis, -3)
    return (45.0 * first_pair - 9.0 * second_pair + third_pair) / 60.0


def second_derivative(padded, direction_axis):
    centre = shifted_array(padded, direction_axis, 0)
    first_pair = shifted_array(padded, direction_axis, 1) + shifted_array(padded, direction_axis, -1)
    second_pair = shifted_array(padded, direction_axis, 2) + shifted_array(padded, direction_axis, -2)
    third_pair = shifted_array(padded, direction_axis, 3) + shifted_array(padded, direction_axis, -3)
    return (2.0 * third_pair - 27.0 * second_pair + 270.0 * first_pair - 490.0 * centre) / 180.0


def spatial_slope(padded, scale_factors):
    return (first_derivative(padded, -3), first_derivative(padded, -1), scale_factors * first_derivative(padded, -2))


def second_order_spread(padded, scale_factors):
    return second_derivative(padded, -3) + second_derivative(padded, -1) + scale_factors * scale_factors * second_derivative(padded, -2)


def rotation(comp_r, comp_t, comp_p, scale_factors):
    grad_r = spatial_slope(comp_r, scale_factors)
    grad_t = spatial_slope(comp_t, scale_factors)
    grad_p = spatial_slope(comp_p, scale_factors)
    return (grad_p[1] - grad_t[2], grad_r[2] - grad_p[0], grad_t[0] - grad_r[1])


def tendency(stencil_frame, scale_factors):
    logarithmic_mass, velocity_radial, velocity_polar, velocity_azimuthal, magnetic_radial, magnetic_polar, magnetic_azimuthal, logarithmic_warmth = [stencil_frame[quantity_count] for quantity_count in range(STATE_QUANTITIES)]
    flows = (velocity_radial, velocity_polar, velocity_azimuthal)
    fields = (magnetic_radial, magnetic_polar, magnetic_azimuthal)
    velocity = [shifted_array(directional_entry, -1, 0) for directional_entry in flows]
    magnetic = [shifted_array(directional_entry, -1, 0) for directional_entry in fields]

    def transport_contribution(slope):
        return velocity[0] * slope[0] + velocity[1] * slope[1] + velocity[2] * slope[2]

    mass_slope_triple = spatial_slope(logarithmic_mass, scale_factors)
    warmth_slope_triple = spatial_slope(logarithmic_warmth, scale_factors)
    velocity_slopes = [spatial_slope(directional_entry, scale_factors) for directional_entry in flows]
    outward_spread = velocity_slopes[0][0] + velocity_slopes[1][1] + velocity_slopes[2][2]
    current_density = rotation(magnetic_radial, magnetic_polar, magnetic_azimuthal, scale_factors)
    lorentz = (current_density[1] * magnetic[2] - current_density[2] * magnetic[1],
               current_density[2] * magnetic[0] - current_density[0] * magnetic[2],
               current_density[0] * magnetic[1] - current_density[1] * magnetic[0])
    motive = (velocity_polar * magnetic_azimuthal - velocity_azimuthal * magnetic_polar, velocity_azimuthal * magnetic_radial - velocity_radial * magnetic_azimuthal, velocity_radial * magnetic_polar - velocity_polar * magnetic_radial)
    induction = rotation(motive[0], motive[1], motive[2], scale_factors)
    thermal_energy = jnp.exp(shifted_array(logarithmic_warmth, -1, 0))
    inverse_density = jnp.exp(-shifted_array(logarithmic_mass, -1, 0))
    result_sequence = [-transport_contribution(mass_slope_triple) - outward_spread]
    for directional_entry in range(3):
        result_sequence.append(-transport_contribution(velocity_slopes[directional_entry]) - thermal_energy * (mass_slope_triple[directional_entry] + warmth_slope_triple[directional_entry])
                       + inverse_density * lorentz[directional_entry] + VISCOSITY * second_order_spread(flows[directional_entry], scale_factors))
    for directional_entry in range(3):
        result_sequence.append(induction[directional_entry] + RESISTIVITY * second_order_spread(fields[directional_entry], scale_factors))
    result_sequence.append(-transport_contribution(warmth_slope_triple) - (ISENTROPIC_INDEX - 1.0) * outward_spread + THERMAL_SPREAD * second_order_spread(logarithmic_warmth, scale_factors))
    return jnp.stack(result_sequence)


def interpolate(flat_tile, stencil_base, fraction, stride):
    def sample_at(offset):
        return flat_tile[:, stencil_base + offset]

    along = fraction[0]
    across = fraction[1]
    return ((1.0 - along) * (1.0 - across) * sample_at(0) + (1.0 - along) * across * sample_at(1)
            + along * (1.0 - across) * sample_at(stride) + along * across * sample_at(stride + 1))


def cycle_positions(rows, cols):
    width = cols + 2 * HALO
    first = jnp.arange(HALO * rows, dtype=jnp.int32)
    second = jnp.arange(HALO * cols, dtype=jnp.int32)
    low_col = (HALO + first // HALO) * width + first % HALO
    high_col = (HALO + first // HALO) * width + cols + HALO + first % HALO
    low_lon = (second // cols) * width + HALO + second % cols
    high_lon = (rows + HALO + second // cols) * width + HALO + second % cols
    return jnp.concatenate([low_col, high_col, low_lon, high_lon]).astype(jnp.int32)


def inverse_sine(start, count, total):
    place = (start + jnp.arange(count, dtype=jnp.int32)).astype(jnp.float32)
    colatitude = math.pi / 4.0 + (place + 0.5) * (math.pi / 2.0 / total)
    return 1.0 / jnp.sin(colatitude)


def reference(state, send_base, send_frac, recv_slots):
    flat_rows = STATE_QUANTITIES * R
    live_slots = recv_slots >= 0
    picks = jnp.where(live_slots, recv_slots, 0).astype(jnp.int32)
    positions = cycle_positions(PH, TH)
    bases_all = send_base.reshape(2 * TILES, OUT)
    fracs_all = send_frac.reshape(2 * TILES, 2, OUT)

    def sender_side(pieces):
        tile_flat, stencil_base, fraction = pieces
        return interpolate(tile_flat, stencil_base, fraction, TH)

    def rates_of(current):
        tile_blocks = current.reshape(2, STATE_QUANTITIES, R, N_LON, PH, N_COLAT, TH).transpose(0, 3, 5, 1, 2, 4, 6)
        tile_blocks = tile_blocks.reshape(2 * TILES, flat_rows, PH * TH)
        sent_values = lax.map(sender_side, (tile_blocks, bases_all, fracs_all))
        sent_values = sent_values.reshape(2, TILES, flat_rows, OUT)
        available = jnp.flip(sent_values, 0).transpose(0, 2, 1, 3).reshape(2, flat_rows, TILES * OUT)
        extended = jnp.pad(current, ((0, 0), (0, 0), (0, 0), (HALO, HALO), (HALO, HALO)))

        def one_tile(tile_number):
            panel_index = tile_number // TILES
            tile_index = tile_number % TILES
            lon_index = tile_index // N_COLAT
            col_index = tile_index % N_COLAT
            anchor = jnp.zeros((), jnp.int32)
            stencil_frame = lax.dynamic_slice(extended, (panel_index, anchor, anchor, lon_index * PH, col_index * TH),
                                       (1, STATE_QUANTITIES, R, PH + 2 * HALO, TH + 2 * HALO))[0]
            cycle = available[panel_index][:, picks[panel_index, tile_index]]
            cycle = jnp.where(live_slots[panel_index, tile_index][None], cycle, 0.0)
            stencil_frame = stencil_frame.reshape(flat_rows, -1).at[:, positions].add(cycle)
            stencil_frame = stencil_frame.reshape(STATE_QUANTITIES, R, PH + 2 * HALO, TH + 2 * HALO)
            stencil_frame = jnp.pad(stencil_frame, ((0, 0), (HALO, HALO), (0, 0), (0, 0)), mode="edge")
            return tendency(stencil_frame, inverse_sine(col_index * TH, TH, NTH))

        result_sequence = lax.map(one_tile, jnp.arange(2 * TILES, dtype=jnp.int32))
        result_sequence = result_sequence.reshape(2, N_LON, N_COLAT, STATE_QUANTITIES, R, PH, TH).transpose(0, 3, 4, 1, 5, 2, 6)
        return result_sequence.reshape(2, STATE_QUANTITIES, R, NPH, NTH)

    middle = state + TIME_STEP * rates_of(state)
    return 0.5 * (state + middle + TIME_STEP * rates_of(middle))
```

```python
import math

import jax
import jax.numpy as jnp
from jax import lax
from jax.experimental import pallas as pl
from jax.experimental.pallas import tpu as pltpu
from jax.sharding import PartitionSpec as P

MESH = pl.DeviceIdType.MESH
F32, BF16, I32 = jnp.float32, jnp.bfloat16, jnp.int32

QUANTITIES = 8
SHELLS = 4
FLAT = QUANTITIES * SHELLS
LON = 48
COL = 128
HALO = 3
OUT = 240
SIDE = HALO * LON
SLOTS = 256
GROUP = 8
GROUPS = 8
STRIDE = LON + 16
TIME_STEP = 0.25
SPREAD = 0.1 / 3.0
S, MR, MT, MP, BR, BT, BP, WARM = range(QUANTITIES)


def dot(left, right):
    return jnp.dot(left, right, preferred_element_type=F32)


def split(value):
    high = value.astype(BF16)
    return high, (value - high.astype(F32)).astype(BF16)


def iota(shape, dim):
    return lax.broadcasted_iota(I32, shape, dim)


def cross_radial(m, b):
    return m[1] * b[2] - m[2] * b[1]


def cross_polar(m, b):
    return m[2] * b[0] - m[0] * b[2]


def cross_azimuthal(m, b):
    return m[0] * b[1] - m[1] * b[0]


def edge_rates(own, d, lap, emf_first, emf_second, along_lanes):
    grow, thin = jnp.exp(own[WARM]), jnp.exp(-own[S])
    b = own[BR:WARM]
    if along_lanes:
        vel, out = own[MT], MT
        lorentz = (d[BR] * b[1], -d[BR] * b[0] - d[BP] * b[2], d[BP] * b[1])
        turn = (emf_first, None, -emf_second)
    else:
        vel, out = own[MP], MP
        lorentz = (d[BR] * b[2], d[BT] * b[2], -d[BT] * b[1] - d[BR] * b[0])
        turn = (-emf_first, emf_second, None)
    result = [-vel * d[S] - d[out]]
    for i in range(3):
        rate = -vel * d[MR + i] + thin * lorentz[i] + SPREAD * lap[MR + i]
        if MR + i == out:
            rate = rate - grow * (d[S] + d[WARM])
        result.append(rate)
    for i in range(3):
        rate = SPREAD * lap[BR + i]
        result.append(rate if turn[i] is None else rate + turn[i])
    result.append(-vel * d[WARM] - (2.0 / 3.0) * d[out] + SPREAD * lap[WARM])
    return result


def shell_first(x):
    a, b = 8.0 * (x[3] - x[0]), 45.0
    return (
        b * (x[1] - x[0]) - 9.0 * (x[2] - x[0]) + (x[3] - x[0]),
        b * (x[2] - x[0]) - a,
        b * (x[3] - x[1]) - a,
        b * (x[3] - x[2]) - 9.0 * (x[3] - x[1]) + (x[3] - x[0]),
    )


def shell_second(x):
    return (
        2.0 * x[3] - 27.0 * x[2] + 270.0 * x[1] - 245.0 * x[0],
        245.0 * x[0] - 490.0 * x[1] + 270.0 * x[2] - 25.0 * x[3],
        245.0 * x[3] - 490.0 * x[2] + 270.0 * x[1] - 25.0 * x[0],
        2.0 * x[0] - 27.0 * x[1] + 270.0 * x[2] - 245.0 * x[3],
    )


def kernel(
    x_ref, base_ref, frac_ref, slots_ref, scale_ref, out_ref,
    frame, emf, lanes, rate, mix, rows_mix, take, rows_take, band, put, onehot, owner,
    table, idx_out, idx_in, picked, got_cols, got_rows, row_out, row_in, col_out, col_in,
    row_halo, col_halo, row_add, col_add,
    idx_send, idx_recv, a_send, a_recv, b_send, b_recv, l_send, l_recv, r_send, r_recv, c_send, c_recv,
):
    panel, lon, col = lax.axis_index("panel"), lax.axis_index("lon"), lax.axis_index("colat")
    n_lon, n_col = lax.axis_size("lon"), lax.axis_size("colat")
    core, mine = lax.rem(lon, 2), lax.div(lon, 2)
    member = core * n_col + col
    other = 1 - panel
    lon_up, lon_down = lax.rem(lon + 1, n_lon), lax.rem(lon + n_lon - 1, n_lon)
    col_up, col_down = lax.rem(col + 1, n_col), lax.rem(col + n_col - 1, n_col)
    outer = lax.rem(lon + 2 * core - 1 + n_lon, n_lon)
    col_edge = jnp.logical_or(col == 0, col == n_col - 1)
    lon_edge = jnp.logical_or(lon == 0, lon == n_lon - 1)
    edge_group = core * (GROUPS - 1)
    shift = 16 * mine

    def group_device(step):
        there = lax.rem(member + step, GROUP)
        return (panel, 2 * mine + lax.div(there, n_col), lax.rem(there, n_col)), there

    def cross_device(step):
        there = lax.rem(mine + step, GROUPS)
        return (other, 2 * there + core, col), there

    def remote(src, dst, send, recv, device):
        return pltpu.make_async_remote_copy(
            src_ref=src, dst_ref=dst, send_sem=send, recv_sem=recv, device_id=device, device_id_type=MESH
        )

    barrier = pltpu.get_barrier_semaphore()
    for step in range(1, GROUP):
        pl.semaphore_signal(barrier, inc=1, device_id=group_device(step)[0], device_id_type=MESH)
    for step in range(GROUPS):
        pl.semaphore_signal(barrier, inc=1, device_id=cross_device(step)[0], device_id_type=MESH)
    pl.semaphore_signal(barrier, inc=1, device_id=(panel, outer, col), device_id_type=MESH)

    zero_rows = jnp.zeros((8, COL), F32)
    for f in range(FLAT):
        for part in range(2):
            frame[part, f * STRIDE : f * STRIDE + 8, :] = zero_rows
            frame[part, f * STRIDE + 8 + LON : (f + 1) * STRIDE, :] = zero_rows
        frame[0, f * STRIDE + 8 : f * STRIDE + 8 + LON, :] = x_ref[f * LON : (f + 1) * LON, :]
    for f in range(3 * SHELLS):
        emf[f * STRIDE : f * STRIDE + 8, :] = zero_rows
        emf[f * STRIDE + 8 + LON : (f + 1) * STRIDE, :] = zero_rows

    base = base_ref[...]
    base_row, base_col = lax.div(base, COL), lax.rem(base, COL)
    along, across = frac_ref[0:1, :], frac_ref[1:2, :]
    cells = iota((COL, SLOTS), 0)
    weight = jnp.where(cells == base_col, 1.0 - across, 0.0) + jnp.where(cells == base_col + 1, across, 0.0)
    weight_high, weight_low = split(weight)
    mix[0:COL, :] = weight_high
    mix[COL : 2 * COL, :] = weight_high
    mix[2 * COL : 3 * COL, :] = weight_low
    cells = iota((LON, SLOTS), 0)
    rows_mix[...] = jnp.where(cells == base_row, 1.0 - along, 0.0) + jnp.where(cells == base_row + 1, along, 0.0)

    place = iota((1, SLOTS), 1) - shift
    inside = jnp.logical_and(place >= 0, place < SIDE)
    place = jnp.where(inside, place, 0)
    place_row = lax.shift_right_logical(place * 171, 9)
    place_layer = jnp.where(inside, place - HALO * place_row, 8)
    place_row = jnp.where(inside, place_row, 64)
    cells = iota((COL, SLOTS), 0)
    low = jnp.where(cells == place_layer, 1.0, 0.0).astype(BF16)
    high = jnp.where(cells == place_layer + (COL - HALO), 1.0, 0.0).astype(BF16)
    for part in range(2):
        take[part * COL : (part + 1) * COL, 0:SLOTS] = low
        take[part * COL : (part + 1) * COL, SLOTS : 2 * SLOTS] = high
    rows_take[...] = jnp.where(iota((LON, SLOTS), 0) == place_row, 1.0, 0.0)

    place = iota((SLOTS, COL), 0) - shift
    inside = jnp.logical_and(place >= 0, place < SIDE)
    place = jnp.where(inside, place, 0)
    layer = jnp.where(inside, place - HALO * lax.shift_right_logical(place * 171, 9), 8)
    cells = iota((SLOTS, COL), 1)
    low = jnp.where(jnp.logical_and(inside, cells == layer), 1.0, 0.0).astype(BF16)
    high = jnp.where(jnp.logical_and(inside, cells == layer + (COL - HALO)), 1.0, 0.0).astype(BF16)
    for part in range(2):
        put[part * SLOTS : (part + 1) * SLOTS, :] = low
        put[(2 + part) * SLOTS : (3 + part) * SLOTS, :] = high

    apart = iota((COL, COL), 0) - iota((COL, COL), 1)
    reach = jnp.abs(apart)
    first = jnp.where(reach == 1, 45.0, jnp.where(reach == 2, -9.0, jnp.where(reach == 3, 1.0, 0.0)))
    first = jnp.where(apart < 0, -first, first).astype(BF16)
    second = jnp.where(
        reach == 0, -490.0, jnp.where(reach == 1, 270.0, jnp.where(reach == 2, -27.0, jnp.where(reach == 3, 2.0, 0.0)))
    ).astype(BF16)
    for part in range(2):
        band[part * COL : (part + 1) * COL, 0:COL] = first
        band[part * COL : (part + 1) * COL, COL : 2 * COL] = second

    spot = iota((1, SLOTS), 1)
    sides = jnp.where(spot < SIDE, jnp.maximum(slots_ref[:, 0:SLOTS], slots_ref[:, SIDE : SIDE + SLOTS]), -1)
    sides = pltpu.roll(jnp.broadcast_to(sides, (8, SLOTS)), shift, 1)
    idx_out[0:1, :] = sides[0:1, 0:COL]
    idx_out[1:2, :] = sides[0:1, COL : 2 * COL]
    for h in range(HALO):
        at = 2 * SIDE + h * COL
        idx_out[2 + h : 3 + h, :] = jnp.maximum(
            slots_ref[:, at : at + COL], slots_ref[:, at + HALO * COL : at + HALO * COL + COL]
        )
    idx_out[5:8, :] = jnp.full((3, COL), -1, I32)

    layer_lane = place_layer
    scale = scale_ref[...]

    def load_split(part, pair):
        block = jnp.concatenate(
            [frame[part, pl.ds(pl.multiple_of((8 * pair + q) * STRIDE, 8) + 8, LON), :] for q in range(8)], axis=0
        )
        return split(block)

    def interpolate(part):
        def body(pair, carry):
            high, low = load_split(part, pair)
            value = dot(jnp.concatenate([high, low, high], axis=1), mix[...])
            value = jnp.sum(value.reshape(8, LON, SLOTS) * rows_mix[...][None], axis=1)
            table[part, member, pl.ds(pl.multiple_of(8 * pair, 8), 8), :] = value
            return carry

        lax.fori_loop(0, FLAT // 8, body, 0)

    def lane_pass(part):
        def body(pair, carry):
            high, low = load_split(part, pair)
            both = jnp.concatenate([high, low], axis=1)
            value = dot(both, take[...]).reshape(8, LON, 2 * SLOTS)
            value = jnp.sum(value * jnp.concatenate([rows_take[...]] * 2, axis=1)[None], axis=1)
            rows = pl.ds(pl.multiple_of(8 * pair, 8), 8)
            col_out[part, 0, rows, :] = value[:, 0:SLOTS]
            col_out[part, 1, rows, :] = value[:, SLOTS : 2 * SLOTS]
            lanes[pl.ds(pl.multiple_of(8 * LON * pair, 8), 8 * LON), :] = dot(both, band[...])
            return carry

        lax.fori_loop(0, FLAT // 8, body, 0)

    def emf_pass(part):
        for r in range(SHELLS):
            def field(q):
                at = (q * SHELLS + r) * STRIDE + 8
                return frame[part, at : at + LON, :]

            m, b = [field(MR + i) for i in range(3)], [field(BR + i) for i in range(3)]
            for i, form in enumerate((cross_radial, cross_polar, cross_azimuthal)):
                at = (i * SHELLS + r) * STRIDE + 8
                emf[at : at + LON, :] = form(m, b)
        for i, at in ((0, FLAT), (2, FLAT + SHELLS)):
            block = jnp.concatenate(
                [emf[(i * SHELLS + r) * STRIDE + 8 : (i * SHELLS + r) * STRIDE + 8 + LON, :] for r in range(SHELLS)],
                axis=0,
            )
            high, low = split(block)
            lanes[at * LON : (at + SHELLS) * LON, 0:COL] = dot(
                jnp.concatenate([high, low], axis=1), band[:, 0:COL]
            )

    def main_pass(part, start, stop):
        def body(block, carry):
            here = pl.multiple_of(8 * block, 8)

            def near(f, apart):
                return frame[part, pl.ds(f * STRIDE + 8 + here + apart, 8), :]

            def near_emf(f, apart):
                return emf[pl.ds(f * STRIDE + 8 + here + apart, 8), :]

            def lane_first(f):
                return lanes[pl.ds(f * LON + here, 8), 0:COL]

            def lane_second(f):
                return lanes[pl.ds(f * LON + here, 8), COL : 2 * COL]

            def row_first(at):
                return 45.0 * (at[1] - at[-1]) - 9.0 * (at[2] - at[-2]) + (at[3] - at[-3])

            def row_second(at, centre):
                return (
                    270.0 * (at[1] + at[-1]) - 27.0 * (at[2] + at[-2]) + 2.0 * (at[3] + at[-3]) - 490.0 * centre
                )

            centre = [[near(q * SHELLS + r, 0) for r in range(SHELLS)] for q in range(QUANTITIES)]
            radial = [shell_first(x) for x in centre]
            radial_second = [None if q == S else shell_second(centre[q]) for q in range(QUANTITIES)]
            emf_centre = [[near_emf(i * SHELLS + r, 0) for r in range(SHELLS)] for i in range(3)]
            emf_radial = [None, shell_first(emf_centre[1]), shell_first(emf_centre[2])]
            for r in range(SHELLS):
                own = [centre[q][r] for q in range(QUANTITIES)]
                g, lap = [], []
                for q in range(QUANTITIES):
                    f = q * SHELLS + r
                    at = {d: near(f, d) for d in (-3, -2, -1, 1, 2, 3)}
                    g.append((radial[q][r], lane_first(f), scale * row_first(at)))
                    if q == S:
                        lap.append(None)
                    else:
                        lap.append(
                            radial_second[q][r] + lane_second(f) + (scale * scale) * row_second(at, own[q])
                        )
                m, b = own[MR:BR], own[BR:WARM]

                def advect(q):
                    return m[0] * g[q][0] + m[1] * g[q][1] + m[2] * g[q][2]

                div = g[MR][0] + g[MT][1] + g[MP][2]
                current = (g[BP][1] - g[BT][2], g[BR][2] - g[BP][0], g[BT][0] - g[BR][1])
                lorentz = (
                    current[1] * b[2] - current[2] * b[1],
                    current[2] * b[0] - current[0] * b[2],
                    current[0] * b[1] - current[1] * b[0],
                )
                grow, thin = jnp.exp(own[WARM]), jnp.exp(-own[S])
                emf_rows = {}
                for i in (0, 1):
                    f = i * SHELLS + r
                    emf_rows[i] = scale * row_first({d: near_emf(f, d) for d in (-3, -2, -1, 1, 2, 3)})
                turn = (
                    lane_first(FLAT + SHELLS + r) - emf_rows[1],
                    emf_rows[0] - emf_radial[2][r],
                    emf_radial[1][r] - lane_first(FLAT + r),
                )
                result = [-advect(S) - div]
                for i in range(3):
                    result.append(
                        -advect(MR + i) - grow * (g[S][i] + g[WARM][i]) + thin * lorentz[i] + SPREAD * lap[MR + i]
                    )
                for i in range(3):
                    result.append(turn[i] + SPREAD * lap[BR + i])
                result.append(-advect(WARM) - (2.0 / 3.0) * div + SPREAD * lap[WARM])
                for q in range(QUANTITIES):
                    rate[pl.ds((q * SHELLS + r) * LON + here, 8), :] = result[q]
            return carry

        lax.fori_loop(start, stop, body, 0)

    def rows_of(part):
        for h in range(HALO):
            row_out[part, 0, h] = frame[part, pl.ds(8 + h, FLAT, stride=STRIDE), :]
            row_out[part, 1, h] = frame[part, pl.ds(8 + LON - HALO + h, FLAT, stride=STRIDE), :]

    def prepare_picks():
        for lane_tile in range(12):
            if lane_tile < 9:
                pieces = []
                if lane_tile < 8:
                    pieces.append(idx_in[lane_tile, 0:1, :])
                if lane_tile > 0:
                    pieces.append(idx_in[lane_tile - 1, 1:2, :])
                slot = pieces[0] if len(pieces) == 1 else jnp.maximum(pieces[0], pieces[1])
            else:
                slot = idx_in[edge_group, lane_tile - 7 : lane_tile - 6, :]
            slot = slot - mine * (GROUP * OUT)
            who = jnp.zeros_like(slot)
            for q in range(1, GROUP):
                who = who + jnp.where(slot >= q * OUT, 1, 0)
            cell = slot - who * OUT
            who = jnp.where(jnp.logical_and(slot >= 0, slot < GROUP * OUT), who, -1)
            at = (lane_tile % 2) * COL
            owner[lane_tile // 2, :, at : at + COL] = jnp.broadcast_to(who, (8, COL))
            hot = jnp.where(iota((SLOTS, COL), 0) == cell, 1.0, 0.0).astype(BF16)
            for copy in range(2):
                onehot[lane_tile // 2, copy * SLOTS : (copy + 1) * SLOTS, at : at + COL] = hot

    def pick(part):
        high, low = split(table[part].reshape(GROUP * FLAT, SLOTS))
        both = jnp.concatenate([high, low], axis=1)

        def body(tile, carry):
            value = dot(both, onehot[tile])
            who = jnp.broadcast_to(owner[tile, 0:1, :], (FLAT, SLOTS))
            total = jnp.zeros((FLAT, SLOTS), F32)
            for q in range(GROUP):
                total = total + jnp.where(who == q, value[q * FLAT : (q + 1) * FLAT, :], 0.0)
            picked[part, 2 * tile] = total[:, 0:COL]
            picked[part, 2 * tile + 1] = total[:, COL : 2 * COL]
            return carry

        lax.fori_loop(jnp.where(col_edge, 0, 4), 6, body, 0)

    def row_corrections(part):
        for side in range(2):
            halo = [
                [row_halo[side, h, q * SHELLS : (q + 1) * SHELLS, :] for q in range(QUANTITIES)] for h in range(HALO)
            ]
            halo_emf = [(cross_radial(x[MR:BR], x[BR:WARM]), cross_polar(x[MR:BR], x[BR:WARM])) for x in halo]
            for j in range(HALO):
                own = [row_out[part, side, j, q * SHELLS : (q + 1) * SHELLS, :] for q in range(QUANTITIES)]

                def total(weights, of):
                    result = None
                    for m in (1, 2, 3):
                        h = j + 3 - m if side == 0 else m - 3 + j
                        if 0 <= h < HALO:
                            term = weights[m - 1] * of(h)
                            result = term if result is None else result + term
                    return result

                sign = -1.0 if side == 0 else 1.0
                firsts = (45.0 * sign, -9.0 * sign, sign)
                d = [scale * total(firsts, lambda h, q=q: halo[h][q]) for q in range(QUANTITIES)]
                lap = [
                    None if q == S else (scale * scale) * total((270.0, -27.0, 2.0), lambda h, q=q: halo[h][q])
                    for q in range(QUANTITIES)
                ]
                emf_radial = scale * total(firsts, lambda h: halo_emf[h][0])
                emf_polar = scale * total(firsts, lambda h: halo_emf[h][1])
                result = edge_rates(own, d, lap, emf_polar, emf_radial, False)
                for q in range(QUANTITIES):
                    row_add[side, j, q * SHELLS : (q + 1) * SHELLS, :] = result[q]
        for side in range(2):
            for j in range(HALO):
                rows = pl.ds(j if side == 0 else LON - HALO + j, FLAT, stride=LON)
                rate[rows, :] = rate[rows, :] + row_add[side, j]

    def col_corrections(part):
        for side in range(2):
            halo = [col_halo[side, q * SHELLS : (q + 1) * SHELLS, :] for q in range(QUANTITIES)]
            own = [col_out[part, side, q * SHELLS : (q + 1) * SHELLS, :] for q in range(QUANTITIES)]
            sign = -1.0 if side == 0 else 1.0

            def both(value):
                firsts = seconds = None
                for m, one, two in ((1, 45.0, 270.0), (2, -9.0, -27.0), (3, 1.0, 2.0)):
                    if side == 0:
                        moved = value if m == 3 else pltpu.roll(value, SLOTS - (3 - m), 1)
                        valid = layer_lane <= m - 1
                    else:
                        moved = value if m == 3 else pltpu.roll(value, 3 - m, 1)
                        valid = jnp.logical_and(layer_lane >= 3 - m, layer_lane < HALO)
                    moved = jnp.where(valid, moved, 0.0)
                    first_term, second_term = (one * sign) * moved, two * moved
                    firsts = first_term if firsts is None else firsts + first_term
                    seconds = second_term if seconds is None else seconds + second_term
                return firsts, seconds

            pairs = [both(x) for x in halo]
            emf_azimuthal = both(cross_azimuthal(halo[MR:BR], halo[BR:WARM]))[0]
            emf_radial = both(cross_radial(halo[MR:BR], halo[BR:WARM]))[0]
            result = edge_rates(
                own, [x[0] for x in pairs], [x[1] for x in pairs], emf_azimuthal, emf_radial, True
            )
            for q in range(QUANTITIES):
                col_add[side, q * SHELLS : (q + 1) * SHELLS, :] = result[q]

    def finish(part):
        def body(pair, carry):
            pieces = []
            for side in range(2):
                block = col_add[side, pl.ds(pl.multiple_of(8 * pair, 8), 8), :]
                high = block.astype(BF16).astype(F32)
                for value in (high, block - high):
                    spread = value.reshape(8, 1, SLOTS) * rows_take[...][None]
                    pieces.append(spread.reshape(8 * LON, SLOTS).astype(BF16))
            added = dot(jnp.concatenate(pieces, axis=1), put[...])
            rows = pl.ds(pl.multiple_of(8 * LON * pair, 8), 8 * LON)
            change = (TIME_STEP / 60.0) * (rate[rows, :] + added)
            start = x_ref[rows, :]
            if part == 0:
                middle = start + change
                for q in range(8):
                    at = pl.multiple_of((8 * pair + q) * STRIDE, 8) + 8
                    frame[1, pl.ds(at, LON), :] = middle[q * LON : (q + 1) * LON, :]
            else:
                middle = jnp.concatenate(
                    [frame[1, pl.ds(pl.multiple_of((8 * pair + q) * STRIDE, 8) + 8, LON), :] for q in range(8)], axis=0
                )
                out_ref[rows, :] = 0.5 * (start + middle + change)
            return carry

        lax.fori_loop(0, FLAT // 8, body, 0)

    def a_copy(part, step):
        device, _ = group_device(step)
        return remote(
            table.at[part, member], table.at[part, member], a_send.at[part, step], a_recv.at[part, member], device
        )

    def a_arrival(part, step):
        device, there = group_device(step)
        return remote(
            table.at[part, member], table.at[part, there], a_send.at[part, step], a_recv.at[part, there], device
        )

    def b_copy(part, step):
        device, there = cross_device(step)
        return remote(
            picked.at[part, pl.ds(there, 2)], got_cols.at[part, mine], b_send.at[part, step], b_recv.at[part, mine],
            device,
        )

    def b_arrival(part, group):
        return remote(
            picked.at[part, pl.ds(0, 2)], got_cols.at[part, group], b_send.at[part, 0], b_recv.at[part, group],
            (other, lon, col),
        )

    def l_copy(part):
        return remote(
            picked.at[part, pl.ds(9, HALO)], got_rows.at[part, mine], l_send.at[part], l_recv.at[part, mine],
            (other, 2 * edge_group + core, col),
        )

    def l_arrival(part, group):
        return remote(
            picked.at[part, pl.ds(9, HALO)], got_rows.at[part, group], l_send.at[part], l_recv.at[part, group],
            (other, lon, col),
        )

    def row_copy(part, side):
        return remote(
            row_out.at[part, 1 - side], row_in.at[part, side], r_send.at[part, side], r_recv.at[part, side],
            (panel, lon_up if side == 0 else lon_down, col),
        )

    def col_copy(part, side):
        return remote(
            col_out.at[part, 1 - side], col_in.at[part, side], c_send.at[part, side], c_recv.at[part, side],
            (panel, lon, col_up if side == 0 else col_down),
        )

    def idx_copy(step):
        device, _ = cross_device(step)
        return remote(idx_out, idx_in.at[mine], idx_send.at[step], idx_recv.at[mine], device)

    def idx_arrival(group):
        return remote(idx_out, idx_in.at[group], idx_send.at[0], idx_recv.at[group], (other, lon, col))

    interpolate(0)
    pl.semaphore_wait(barrier, GROUP + GROUPS)

    for part in range(2):
        if part == 1:
            interpolate(1)
        for step in range(1, GROUP):
            a_copy(part, step).start()
        if part == 0:
            for step in range(GROUPS):
                idx_copy(step).start()
        rows_of(part)
        for side in range(2):
            row_copy(part, side).start()
        lane_pass(part)
        for side in range(2):
            col_copy(part, side).start()
        emf_pass(part)
        if part == 0:
            for group in range(GROUPS):
                idx_arrival(group).wait_recv()
            prepare_picks()
        main_pass(part, 0, 4)
        for step in range(1, GROUP):
            a_arrival(part, step).wait_recv()
        pick(part)
        l_copy(part).start()

        @pl.when(col_edge)
        def _():
            for step in range(GROUPS):
                b_copy(part, step).start()

        main_pass(part, 4, 6)
        for side in range(2):
            row_copy(part, side).wait_recv()
            col_copy(part, side).wait_recv()

        for side in range(2):
            at_edge = lon == (0 if side == 0 else n_lon - 1)

            @pl.when(at_edge)
            def _():
                for group in range(GROUPS):
                    l_arrival(part, group).wait_recv()
                total = got_rows[part, 0]
                for group in range(1, GROUPS):
                    total = total + got_rows[part, group]
                row_halo[side] = total

            @pl.when(jnp.logical_not(at_edge))
            def _():
                row_halo[side] = row_in[part, side]

        row_corrections(part)

        for side in range(2):
            at_edge = col == (0 if side == 0 else n_col - 1)

            @pl.when(at_edge)
            def _():
                for group in range(GROUPS):
                    b_arrival(part, group).wait_recv()
                total = got_cols[part, 0]
                for group in range(1, GROUPS):
                    total = total + got_cols[part, group]
                col_halo[side, :, 0:COL] = total[0]
                col_halo[side, :, COL : 2 * COL] = total[1]

            @pl.when(jnp.logical_not(at_edge))
            def _():
                col_halo[side] = col_in[part, side]

        col_corrections(part)
        finish(part)

    for step in range(GROUPS):
        idx_copy(step).wait_send()
    for part in range(2):
        for step in range(1, GROUP):
            a_copy(part, step).wait_send()
        for side in range(2):
            row_copy(part, side).wait_send()
            col_copy(part, side).wait_send()
        l_copy(part).wait_send()

        @pl.when(col_edge)
        def _():
            for step in range(GROUPS):
                b_copy(part, step).wait_send()


def inverse_sine(start, count, total):
    place = (start + jnp.arange(count, dtype=jnp.int32)).astype(jnp.float32)
    colatitude = math.pi / 4.0 + (place + 0.5) * (math.pi / 2.0 / total)
    return 1.0 / jnp.sin(colatitude)


def shards(state, send_base, send_frac, recv_slots):
    rows = FLAT * LON
    scale = inverse_sine(lax.axis_index("colat") * COL, COL, COL * lax.axis_size("colat"))[None]
    base = jnp.pad(send_base[0], ((0, 0), (0, SLOTS - OUT)))
    frac = jnp.pad(send_frac[0, 0], ((0, 0), (0, SLOTS - OUT)))
    dma = pltpu.SemaphoreType.DMA
    vmem = pltpu.VMEM
    scratch = [
        vmem((2, FLAT * STRIDE, COL), F32),
        vmem((3 * SHELLS * STRIDE, COL), F32),
        vmem(((FLAT + 2 * SHELLS) * LON, 2 * COL), F32),
        vmem((rows, COL), F32),
        vmem((3 * COL, SLOTS), BF16),
        vmem((LON, SLOTS), F32),
        vmem((2 * COL, 2 * SLOTS), BF16),
        vmem((LON, SLOTS), F32),
        vmem((2 * COL, 2 * COL), BF16),
        vmem((4 * SLOTS, COL), BF16),
        vmem((6, 2 * SLOTS, 2 * COL), BF16),
        vmem((6, 8, 2 * COL), I32),
        vmem((2, GROUP, FLAT, SLOTS), F32),
        vmem((8, COL), I32),
        vmem((GROUPS, 8, COL), I32),
        vmem((2, 12, FLAT, COL), F32),
        vmem((2, GROUPS, 2, FLAT, COL), F32),
        vmem((2, GROUPS, HALO, FLAT, COL), F32),
        vmem((2, 2, HALO, FLAT, COL), F32),
        vmem((2, 2, HALO, FLAT, COL), F32),
        vmem((2, 2, FLAT, SLOTS), F32),
        vmem((2, 2, FLAT, SLOTS), F32),
        vmem((2, HALO, FLAT, COL), F32),
        vmem((2, FLAT, SLOTS), F32),
        vmem((2, HALO, FLAT, COL), F32),
        vmem((2, FLAT, SLOTS), F32),
        dma((GROUPS,)),
        dma((GROUPS,)),
        dma((2, GROUP)),
        dma((2, GROUP)),
        dma((2, GROUPS)),
        dma((2, GROUPS)),
        dma((2,)),
        dma((2, GROUPS)),
        dma((2, 2)),
        dma((2, 2)),
        dma((2, 2)),
        dma((2, 2)),
    ]
    result = pl.pallas_call(
        kernel,
        out_shape=jax.ShapeDtypeStruct((rows, COL), F32),
        in_specs=[pl.BlockSpec(memory_space=pltpu.VMEM)] * 5,
        out_specs=pl.BlockSpec(memory_space=pltpu.VMEM),
        scratch_shapes=scratch,
        compiler_params=pltpu.CompilerParams(
            collective_id=0, has_side_effects=True, vmem_limit_bytes=40 * 1024 * 1024
        ),
    )(state.reshape(rows, COL), base, frac, recv_slots[0], scale)
    return result.reshape(state.shape)


def solution(mesh):
    placed = (
        P("panel", None, None, "lon", "colat"),
        P("panel", ("lon", "colat"), None),
        P("panel", ("lon", "colat"), None, None),
        P("panel", ("lon", "colat"), None),
    )
    return jax.shard_map(
        shards,
        mesh=mesh,
        in_specs=placed,
        out_specs=P("panel", None, None, "lon", "colat"),
        check_vma=False,
    )
```

```python
import math

import jax
import jax.numpy as jnp
from jax import lax
from jax.experimental import pallas as pl
from jax.experimental.pallas import tpu as pltpu
from jax.sharding import PartitionSpec as P

MESH = pl.DeviceIdType.MESH
F32, BF16, I32 = jnp.float32, jnp.bfloat16, jnp.int32

QUANTITIES = 8
SHELLS = 4
FLAT = QUANTITIES * SHELLS
LON = 48
COL = 128
HALO = 3
OUT = 240
SIDE = HALO * LON
SLOTS = 256
GROUP = 8
GROUPS = 8
STRIDE = LON + 16
TIME_STEP = 0.25
SPREAD = 0.1 / 3.0
S, MR, MT, MP, BR, BT, BP, WARM = range(QUANTITIES)


def dot(left, right):
    return jnp.dot(left, right, preferred_element_type=F32)


def split(value):
    high = value.astype(BF16)
    return high, (value - high.astype(F32)).astype(BF16)


def iota(shape, dim):
    return lax.broadcasted_iota(I32, shape, dim)


def cross_radial(m, b):
    return m[1] * b[2] - m[2] * b[1]


def cross_polar(m, b):
    return m[2] * b[0] - m[0] * b[2]


def cross_azimuthal(m, b):
    return m[0] * b[1] - m[1] * b[0]


def edge_rates(own, d, lap, emf_first, emf_second, along_lanes):
    grow, thin = jnp.exp(own[WARM]), jnp.exp(-own[S])
    b = own[BR:WARM]
    if along_lanes:
        vel, out = own[MT], MT
        lorentz = (d[BR] * b[1], -d[BR] * b[0] - d[BP] * b[2], d[BP] * b[1])
        turn = (emf_first, None, -emf_second)
    else:
        vel, out = own[MP], MP
        lorentz = (d[BR] * b[2], d[BT] * b[2], -d[BT] * b[1] - d[BR] * b[0])
        turn = (-emf_first, emf_second, None)
    result = [-vel * d[S] - d[out]]
    for i in range(3):
        rate = -vel * d[MR + i] + thin * lorentz[i] + SPREAD * lap[MR + i]
        if MR + i == out:
            rate = rate - grow * (d[S] + d[WARM])
        result.append(rate)
    for i in range(3):
        rate = SPREAD * lap[BR + i]
        result.append(rate if turn[i] is None else rate + turn[i])
    result.append(-vel * d[WARM] - (2.0 / 3.0) * d[out] + SPREAD * lap[WARM])
    return result


def shell_first(x):
    a, b = 8.0 * (x[3] - x[0]), 45.0
    return (
        b * (x[1] - x[0]) - 9.0 * (x[2] - x[0]) + (x[3] - x[0]),
        b * (x[2] - x[0]) - a,
        b * (x[3] - x[1]) - a,
        b * (x[3] - x[2]) - 9.0 * (x[3] - x[1]) + (x[3] - x[0]),
    )


def shell_second(x):
    return (
        2.0 * x[3] - 27.0 * x[2] + 270.0 * x[1] - 245.0 * x[0],
        245.0 * x[0] - 490.0 * x[1] + 270.0 * x[2] - 25.0 * x[3],
        245.0 * x[3] - 490.0 * x[2] + 270.0 * x[1] - 25.0 * x[0],
        2.0 * x[0] - 27.0 * x[1] + 270.0 * x[2] - 245.0 * x[3],
    )


def kernel(
    x_ref, base_ref, frac_ref, slots_ref, scale_ref, out_ref,
    frame, emf, lanes, rate, mix, rows_mix, take, rows_take, band, put, onehot, owner,
    table, idx_out, idx_in, picked, got_cols, got_rows, row_out, row_in, col_out, col_in,
    row_halo, col_halo, row_add, col_add,
    idx_send, idx_recv, a_send, a_recv, b_send, b_recv, l_send, l_recv, r_send, r_recv, c_send, c_recv,
):
    panel, lon, col = lax.axis_index("panel"), lax.axis_index("lon"), lax.axis_index("colat")
    n_lon, n_col = lax.axis_size("lon"), lax.axis_size("colat")
    core, mine = lax.rem(lon, 2), lax.div(lon, 2)
    member = core * n_col + col
    other = 1 - panel
    lon_up, lon_down = lax.rem(lon + 1, n_lon), lax.rem(lon + n_lon - 1, n_lon)
    col_up, col_down = lax.rem(col + 1, n_col), lax.rem(col + n_col - 1, n_col)
    outer = lax.rem(lon + 2 * core - 1 + n_lon, n_lon)
    col_edge = jnp.logical_or(col == 0, col == n_col - 1)
    lon_edge = jnp.logical_or(lon == 0, lon == n_lon - 1)
    edge_group = core * (GROUPS - 1)
    shift = 16 * mine

    def group_device(step):
        there = lax.rem(member + step, GROUP)
        return (panel, 2 * mine + lax.div(there, n_col), lax.rem(there, n_col)), there

    def cross_device(step):
        there = lax.rem(mine + step, GROUPS)
        return (other, 2 * there + core, col), there

    def remote(src, dst, send, recv, device):
        return pltpu.make_async_remote_copy(
            src_ref=src, dst_ref=dst, send_sem=send, recv_sem=recv, device_id=device, device_id_type=MESH
        )

    barrier = pltpu.get_barrier_semaphore()
    for step in range(1, GROUP):
        pl.semaphore_signal(barrier, inc=1, device_id=group_device(step)[0], device_id_type=MESH)
    for step in range(GROUPS):
        pl.semaphore_signal(barrier, inc=1, device_id=cross_device(step)[0], device_id_type=MESH)
    pl.semaphore_signal(barrier, inc=1, device_id=(panel, outer, col), device_id_type=MESH)

    zero_rows = jnp.zeros((8, COL), F32)
    for f in range(FLAT):
        for part in range(2):
            frame[part, f * STRIDE : f * STRIDE + 8, :] = zero_rows
            frame[part, f * STRIDE + 8 + LON : (f + 1) * STRIDE, :] = zero_rows
        frame[0, f * STRIDE + 8 : f * STRIDE + 8 + LON, :] = x_ref[f * LON : (f + 1) * LON, :]
    for f in range(3 * SHELLS):
        emf[f * STRIDE : f * STRIDE + 8, :] = zero_rows
        emf[f * STRIDE + 8 + LON : (f + 1) * STRIDE, :] = zero_rows

    base = base_ref[...]
    base_row, base_col = lax.div(base, COL), lax.rem(base, COL)
    along, across = frac_ref[0:1, :], frac_ref[1:2, :]
    cells = iota((COL, SLOTS), 0)
    weight = jnp.where(cells == base_col, 1.0 - across, 0.0) + jnp.where(cells == base_col + 1, across, 0.0)
    weight_high, weight_low = split(weight)
    mix[0:COL, :] = weight_high
    mix[COL : 2 * COL, :] = weight_high
    mix[2 * COL : 3 * COL, :] = weight_low
    cells = iota((LON, SLOTS), 0)
    rows_mix[...] = jnp.where(cells == base_row, 1.0 - along, 0.0) + jnp.where(cells == base_row + 1, along, 0.0)

    place = iota((1, SLOTS), 1) - shift
    inside = jnp.logical_and(place >= 0, place < SIDE)
    place = jnp.where(inside, place, 0)
    place_row = lax.shift_right_logical(place * 171, 9)
    place_layer = jnp.where(inside, place - HALO * place_row, 8)
    place_row = jnp.where(inside, place_row, 64)
    cells = iota((COL, SLOTS), 0)
    low = jnp.where(cells == place_layer, 1.0, 0.0).astype(BF16)
    high = jnp.where(cells == place_layer + (COL - HALO), 1.0, 0.0).astype(BF16)
    for part in range(2):
        take[part * COL : (part + 1) * COL, 0:SLOTS] = low
        take[part * COL : (part + 1) * COL, SLOTS : 2 * SLOTS] = high
    rows_take[...] = jnp.where(iota((LON, SLOTS), 0) == place_row, 1.0, 0.0)

    place = iota((SLOTS, COL), 0) - shift
    inside = jnp.logical_and(place >= 0, place < SIDE)
    place = jnp.where(inside, place, 0)
    layer = jnp.where(inside, place - HALO * lax.shift_right_logical(place * 171, 9), 8)
    cells = iota((SLOTS, COL), 1)
    low = jnp.where(jnp.logical_and(inside, cells == layer), 1.0, 0.0).astype(BF16)
    high = jnp.where(jnp.logical_and(inside, cells == layer + (COL - HALO)), 1.0, 0.0).astype(BF16)
    for part in range(2):
        put[part * SLOTS : (part + 1) * SLOTS, :] = low
        put[(2 + part) * SLOTS : (3 + part) * SLOTS, :] = high

    apart = iota((COL, COL), 0) - iota((COL, COL), 1)
    reach = jnp.abs(apart)
    first = jnp.where(reach == 1, 45.0, jnp.where(reach == 2, -9.0, jnp.where(reach == 3, 1.0, 0.0)))
    first = jnp.where(apart < 0, -first, first).astype(BF16)
    second = jnp.where(
        reach == 0, -490.0, jnp.where(reach == 1, 270.0, jnp.where(reach == 2, -27.0, jnp.where(reach == 3, 2.0, 0.0)))
    ).astype(BF16)
    for part in range(2):
        band[part * COL : (part + 1) * COL, 0:COL] = first
        band[part * COL : (part + 1) * COL, COL : 2 * COL] = second

    spot = iota((1, SLOTS), 1)
    sides = jnp.where(spot < SIDE, jnp.maximum(slots_ref[:, 0:SLOTS], slots_ref[:, SIDE : SIDE + SLOTS]), -1)
    sides = pltpu.roll(jnp.broadcast_to(sides, (8, SLOTS)), shift, 1)
    idx_out[0:1, :] = sides[0:1, 0:COL]
    idx_out[1:2, :] = sides[0:1, COL : 2 * COL]
    for h in range(HALO):
        at = 2 * SIDE + h * COL
        idx_out[2 + h : 3 + h, :] = jnp.maximum(
            slots_ref[:, at : at + COL], slots_ref[:, at + HALO * COL : at + HALO * COL + COL]
        )
    idx_out[5:8, :] = jnp.full((3, COL), -1, I32)

    layer_lane = place_layer
    scale = scale_ref[...]

    def load_split(part, pair):
        block = jnp.concatenate(
            [frame[part, pl.ds(pl.multiple_of((8 * pair + q) * STRIDE, 8) + 8, LON), :] for q in range(8)], axis=0
        )
        return split(block)

    def interpolate(part):
        def body(pair, carry):
            high, low = load_split(part, pair)
            value = dot(jnp.concatenate([high, low, high], axis=1), mix[...])
            value = jnp.sum(value.reshape(8, LON, SLOTS) * rows_mix[...][None], axis=1)
            table[part, member, pl.ds(pl.multiple_of(8 * pair, 8), 8), :] = value
            return carry

        lax.fori_loop(0, FLAT // 8, body, 0)

    def lane_pass(part):
        def body(pair, carry):
            high, low = load_split(part, pair)
            both = jnp.concatenate([high, low], axis=1)
            value = dot(both, take[...]).reshape(8, LON, 2 * SLOTS)
            value = jnp.sum(value * jnp.concatenate([rows_take[...]] * 2, axis=1)[None], axis=1)
            rows = pl.ds(pl.multiple_of(8 * pair, 8), 8)
            col_out[part, 0, rows, :] = value[:, 0:SLOTS]
            col_out[part, 1, rows, :] = value[:, SLOTS : 2 * SLOTS]
            lanes[pl.ds(pl.multiple_of(8 * LON * pair, 8), 8 * LON), :] = dot(both, band[...])
            return carry

        lax.fori_loop(0, FLAT // 8, body, 0)

    def emf_pass(part):
        for r in range(SHELLS):
            def field(q):
                at = (q * SHELLS + r) * STRIDE + 8
                return frame[part, at : at + LON, :]

            m, b = [field(MR + i) for i in range(3)], [field(BR + i) for i in range(3)]
            for i, form in enumerate((cross_radial, cross_polar, cross_azimuthal)):
                at = (i * SHELLS + r) * STRIDE + 8
                emf[at : at + LON, :] = form(m, b)
        for i, at in ((0, FLAT), (2, FLAT + SHELLS)):
            block = jnp.concatenate(
                [emf[(i * SHELLS + r) * STRIDE + 8 : (i * SHELLS + r) * STRIDE + 8 + LON, :] for r in range(SHELLS)],
                axis=0,
            )
            high, low = split(block)
            lanes[at * LON : (at + SHELLS) * LON, 0:COL] = dot(
                jnp.concatenate([high, low], axis=1), band[:, 0:COL]
            )

    def main_pass(part, start, stop):
        def body(block, carry):
            here = pl.multiple_of(8 * block, 8)

            def near(f, apart):
                return frame[part, pl.ds(f * STRIDE + 8 + here + apart, 8), :]

            def near_emf(f, apart):
                return emf[pl.ds(f * STRIDE + 8 + here + apart, 8), :]

            def lane_first(f):
                return lanes[pl.ds(f * LON + here, 8), 0:COL]

            def lane_second(f):
                return lanes[pl.ds(f * LON + here, 8), COL : 2 * COL]

            def row_first(at):
                return 45.0 * (at[1] - at[-1]) - 9.0 * (at[2] - at[-2]) + (at[3] - at[-3])

            def row_second(at, centre):
                return (
                    270.0 * (at[1] + at[-1]) - 27.0 * (at[2] + at[-2]) + 2.0 * (at[3] + at[-3]) - 490.0 * centre
                )

            centre = [[near(q * SHELLS + r, 0) for r in range(SHELLS)] for q in range(QUANTITIES)]
            radial = [shell_first(x) for x in centre]
            radial_second = [None if q == S else shell_second(centre[q]) for q in range(QUANTITIES)]
            emf_centre = [[near_emf(i * SHELLS + r, 0) for r in range(SHELLS)] for i in range(3)]
            emf_radial = [None, shell_first(emf_centre[1]), shell_first(emf_centre[2])]
            for r in range(SHELLS):
                own = [centre[q][r] for q in range(QUANTITIES)]
                g, lap = [], []
                for q in range(QUANTITIES):
                    f = q * SHELLS + r
                    at = {d: near(f, d) for d in (-3, -2, -1, 1, 2, 3)}
                    g.append((radial[q][r], lane_first(f), scale * row_first(at)))
                    if q == S:
                        lap.append(None)
                    else:
                        lap.append(
                            radial_second[q][r] + lane_second(f) + (scale * scale) * row_second(at, own[q])
                        )
                m, b = own[MR:BR], own[BR:WARM]

                def advect(q):
                    return m[0] * g[q][0] + m[1] * g[q][1] + m[2] * g[q][2]

                div = g[MR][0] + g[MT][1] + g[MP][2]
                current = (g[BP][1] - g[BT][2], g[BR][2] - g[BP][0], g[BT][0] - g[BR][1])
                lorentz = (
                    current[1] * b[2] - current[2] * b[1],
                    current[2] * b[0] - current[0] * b[2],
                    current[0] * b[1] - current[1] * b[0],
                )
                grow, thin = jnp.exp(own[WARM]), jnp.exp(-own[S])
                emf_rows = {}
                for i in (0, 1):
                    f = i * SHELLS + r
                    emf_rows[i] = scale * row_first({d: near_emf(f, d) for d in (-3, -2, -1, 1, 2, 3)})
                turn = (
                    lane_first(FLAT + SHELLS + r) - emf_rows[1],
                    emf_rows[0] - emf_radial[2][r],
                    emf_radial[1][r] - lane_first(FLAT + r),
                )
                result = [-advect(S) - div]
                for i in range(3):
                    result.append(
                        -advect(MR + i) - grow * (g[S][i] + g[WARM][i]) + thin * lorentz[i] + SPREAD * lap[MR + i]
                    )
                for i in range(3):
                    result.append(turn[i] + SPREAD * lap[BR + i])
                result.append(-advect(WARM) - (2.0 / 3.0) * div + SPREAD * lap[WARM])
                for q in range(QUANTITIES):
                    rate[pl.ds((q * SHELLS + r) * LON + here, 8), :] = result[q]
            return carry

        lax.fori_loop(start, stop, body, 0)

    def rows_of(part):
        for h in range(HALO):
            row_out[part, 0, h] = frame[part, pl.ds(8 + h, FLAT, stride=STRIDE), :]
            row_out[part, 1, h] = frame[part, pl.ds(8 + LON - HALO + h, FLAT, stride=STRIDE), :]

    def prepare_picks():
        for lane_tile in range(12):
            if lane_tile < 9:
                pieces = []
                if lane_tile < 8:
                    pieces.append(idx_in[lane_tile, 0:1, :])
                if lane_tile > 0:
                    pieces.append(idx_in[lane_tile - 1, 1:2, :])
                slot = pieces[0] if len(pieces) == 1 else jnp.maximum(pieces[0], pieces[1])
            else:
                slot = idx_in[edge_group, lane_tile - 7 : lane_tile - 6, :]
            slot = slot - mine * (GROUP * OUT)
            who = jnp.zeros_like(slot)
            for q in range(1, GROUP):
                who = who + jnp.where(slot >= q * OUT, 1, 0)
            cell = slot - who * OUT
            who = jnp.where(jnp.logical_and(slot >= 0, slot < GROUP * OUT), who, -1)
            at = (lane_tile % 2) * COL
            owner[lane_tile // 2, :, at : at + COL] = jnp.broadcast_to(who, (8, COL))
            hot = jnp.where(iota((SLOTS, COL), 0) == cell, 1.0, 0.0).astype(BF16)
            for copy in range(2):
                onehot[lane_tile // 2, copy * SLOTS : (copy + 1) * SLOTS, at : at + COL] = hot

    def pick(part):
        high, low = split(table[part].reshape(GROUP * FLAT, SLOTS))
        both = jnp.concatenate([high, low], axis=1)

        def body(tile, carry):
            value = dot(both, onehot[tile])
            who = jnp.broadcast_to(owner[tile, 0:1, :], (FLAT, SLOTS))
            total = jnp.zeros((FLAT, SLOTS), F32)
            for q in range(GROUP):
                total = total + jnp.where(who == q, value[q * FLAT : (q + 1) * FLAT, :], 0.0)
            picked[part, 2 * tile] = total[:, 0:COL]
            picked[part, 2 * tile + 1] = total[:, COL : 2 * COL]
            return carry

        lax.fori_loop(jnp.where(col_edge, 0, 4), 6, body, 0)

    def row_corrections(part):
        for side in range(2):
            halo = [
                [row_halo[side, h, q * SHELLS : (q + 1) * SHELLS, :] for q in range(QUANTITIES)] for h in range(HALO)
            ]
            halo_emf = [(cross_radial(x[MR:BR], x[BR:WARM]), cross_polar(x[MR:BR], x[BR:WARM])) for x in halo]
            for j in range(HALO):
                own = [row_out[part, side, j, q * SHELLS : (q + 1) * SHELLS, :] for q in range(QUANTITIES)]

                def total(weights, of):
                    result = None
                    for m in (1, 2, 3):
                        h = j + 3 - m if side == 0 else m - 3 + j
                        if 0 <= h < HALO:
                            term = weights[m - 1] * of(h)
                            result = term if result is None else result + term
                    return result

                sign = -1.0 if side == 0 else 1.0
                firsts = (45.0 * sign, -9.0 * sign, sign)
                d = [scale * total(firsts, lambda h, q=q: halo[h][q]) for q in range(QUANTITIES)]
                lap = [
                    None if q == S else (scale * scale) * total((270.0, -27.0, 2.0), lambda h, q=q: halo[h][q])
                    for q in range(QUANTITIES)
                ]
                emf_radial = scale * total(firsts, lambda h: halo_emf[h][0])
                emf_polar = scale * total(firsts, lambda h: halo_emf[h][1])
                result = edge_rates(own, d, lap, emf_polar, emf_radial, False)
                for q in range(QUANTITIES):
                    row_add[side, j, q * SHELLS : (q + 1) * SHELLS, :] = result[q]
        for side in range(2):
            for j in range(HALO):
                rows = pl.ds(j if side == 0 else LON - HALO + j, FLAT, stride=LON)
                rate[rows, :] = rate[rows, :] + row_add[side, j]

    def col_corrections(part):
        for side in range(2):
            halo = [col_halo[side, q * SHELLS : (q + 1) * SHELLS, :] for q in range(QUANTITIES)]
            own = [col_out[part, side, q * SHELLS : (q + 1) * SHELLS, :] for q in range(QUANTITIES)]
            sign = -1.0 if side == 0 else 1.0

            def both(value):
                firsts = seconds = None
                for m, one, two in ((1, 45.0, 270.0), (2, -9.0, -27.0), (3, 1.0, 2.0)):
                    if side == 0:
                        moved = value if m == 3 else pltpu.roll(value, SLOTS - (3 - m), 1)
                        valid = layer_lane <= m - 1
                    else:
                        moved = value if m == 3 else pltpu.roll(value, 3 - m, 1)
                        valid = jnp.logical_and(layer_lane >= 3 - m, layer_lane < HALO)
                    moved = jnp.where(valid, moved, 0.0)
                    first_term, second_term = (one * sign) * moved, two * moved
                    firsts = first_term if firsts is None else firsts + first_term
                    seconds = second_term if seconds is None else seconds + second_term
                return firsts, seconds

            pairs = [both(x) for x in halo]
            emf_azimuthal = both(cross_azimuthal(halo[MR:BR], halo[BR:WARM]))[0]
            emf_radial = both(cross_radial(halo[MR:BR], halo[BR:WARM]))[0]
            result = edge_rates(
                own, [x[0] for x in pairs], [x[1] for x in pairs], emf_azimuthal, emf_radial, True
            )
            for q in range(QUANTITIES):
                col_add[side, q * SHELLS : (q + 1) * SHELLS, :] = result[q]

    def finish(part):
        def body(pair, carry):
            pieces = []
            for side in range(2):
                block = col_add[side, pl.ds(pl.multiple_of(8 * pair, 8), 8), :]
                high = block.astype(BF16).astype(F32)
                for value in (high, block - high):
                    spread = value.reshape(8, 1, SLOTS) * rows_take[...][None]
                    pieces.append(spread.reshape(8 * LON, SLOTS).astype(BF16))
            added = dot(jnp.concatenate(pieces, axis=1), put[...])
            rows = pl.ds(pl.multiple_of(8 * LON * pair, 8), 8 * LON)
            change = (TIME_STEP / 60.0) * (rate[rows, :] + added)
            start = x_ref[rows, :]
            if part == 0:
                middle = start + change
                for q in range(8):
                    at = pl.multiple_of((8 * pair + q) * STRIDE, 8) + 8
                    frame[1, pl.ds(at, LON), :] = middle[q * LON : (q + 1) * LON, :]
            else:
                middle = jnp.concatenate(
                    [frame[1, pl.ds(pl.multiple_of((8 * pair + q) * STRIDE, 8) + 8, LON), :] for q in range(8)], axis=0
                )
                out_ref[rows, :] = 0.5 * (start + middle + change)
            return carry

        lax.fori_loop(0, FLAT // 8, body, 0)

    def a_copy(part, step):
        device, _ = group_device(step)
        return remote(
            table.at[part, member], table.at[part, member], a_send.at[part, step], a_recv.at[part, member], device
        )

    def a_arrival(part, step):
        device, there = group_device(step)
        return remote(
            table.at[part, member], table.at[part, there], a_send.at[part, step], a_recv.at[part, there], device
        )

    def b_copy(part, step):
        device, there = cross_device(step)
        return remote(
            picked.at[part, pl.ds(there, 2)], got_cols.at[part, mine], b_send.at[part, step], b_recv.at[part, mine],
            device,
        )

    def b_arrival(part, group):
        return remote(
            picked.at[part, pl.ds(0, 2)], got_cols.at[part, group], b_send.at[part, 0], b_recv.at[part, group],
            (other, lon, col),
        )

    def l_copy(part):
        return remote(
            picked.at[part, pl.ds(9, HALO)], got_rows.at[part, mine], l_send.at[part], l_recv.at[part, mine],
            (other, 2 * edge_group + core, col),
        )

    def l_arrival(part, group):
        return remote(
            picked.at[part, pl.ds(9, HALO)], got_rows.at[part, group], l_send.at[part], l_recv.at[part, group],
            (other, lon, col),
        )

    def row_copy(part, side):
        return remote(
            row_out.at[part, 1 - side], row_in.at[part, side], r_send.at[part, side], r_recv.at[part, side],
            (panel, lon_up if side == 0 else lon_down, col),
        )

    def col_copy(part, side):
        return remote(
            col_out.at[part, 1 - side], col_in.at[part, side], c_send.at[part, side], c_recv.at[part, side],
            (panel, lon, col_up if side == 0 else col_down),
        )

    def idx_copy(step):
        device, _ = cross_device(step)
        return remote(idx_out, idx_in.at[mine], idx_send.at[step], idx_recv.at[mine], device)

    def idx_arrival(group):
        return remote(idx_out, idx_in.at[group], idx_send.at[0], idx_recv.at[group], (other, lon, col))

    interpolate(0)
    pl.semaphore_wait(barrier, GROUP + GROUPS)

    for part in range(2):
        if part == 1:
            interpolate(1)
        for step in range(1, GROUP):
            a_copy(part, step).start()
        if part == 0:
            for step in range(GROUPS):
                idx_copy(step).start()
        rows_of(part)
        for side in range(2):
            row_copy(part, side).start()
        lane_pass(part)
        for side in range(2):
            col_copy(part, side).start()
        emf_pass(part)
        if part == 0:
            for group in range(GROUPS):
                idx_arrival(group).wait_recv()
            prepare_picks()
        main_pass(part, 0, 2)
        for step in range(1, GROUP):
            a_arrival(part, step).wait_recv()
        pick(part)
        l_copy(part).start()

        @pl.when(col_edge)
        def _():
            for step in range(GROUPS):
                b_copy(part, step).start()

        main_pass(part, 2, 6)
        for side in range(2):
            row_copy(part, side).wait_recv()
            col_copy(part, side).wait_recv()

        for side in range(2):
            at_edge = lon == (0 if side == 0 else n_lon - 1)

            @pl.when(at_edge)
            def _():
                for group in range(GROUPS):
                    l_arrival(part, group).wait_recv()
                total = got_rows[part, 0]
                for group in range(1, GROUPS):
                    total = total + got_rows[part, group]
                row_halo[side] = total

            @pl.when(jnp.logical_not(at_edge))
            def _():
                row_halo[side] = row_in[part, side]

        row_corrections(part)

        for side in range(2):
            at_edge = col == (0 if side == 0 else n_col - 1)

            @pl.when(at_edge)
            def _():
                for group in range(GROUPS):
                    b_arrival(part, group).wait_recv()
                total = got_cols[part, 0]
                for group in range(1, GROUPS):
                    total = total + got_cols[part, group]
                col_halo[side, :, 0:COL] = total[0]
                col_halo[side, :, COL : 2 * COL] = total[1]

            @pl.when(jnp.logical_not(at_edge))
            def _():
                col_halo[side] = col_in[part, side]

        col_corrections(part)
        finish(part)

    for step in range(GROUPS):
        idx_copy(step).wait_send()
    for part in range(2):
        for step in range(1, GROUP):
            a_copy(part, step).wait_send()
        for side in range(2):
            row_copy(part, side).wait_send()
            col_copy(part, side).wait_send()
        l_copy(part).wait_send()

        @pl.when(col_edge)
        def _():
            for step in range(GROUPS):
                b_copy(part, step).wait_send()


def inverse_sine(start, count, total):
    place = (start + jnp.arange(count, dtype=jnp.int32)).astype(jnp.float32)
    colatitude = math.pi / 4.0 + (place + 0.5) * (math.pi / 2.0 / total)
    return 1.0 / jnp.sin(colatitude)


def shards(state, send_base, send_frac, recv_slots):
    rows = FLAT * LON
    scale = inverse_sine(lax.axis_index("colat") * COL, COL, COL * lax.axis_size("colat"))[None]
    base = jnp.pad(send_base[0], ((0, 0), (0, SLOTS - OUT)))
    frac = jnp.pad(send_frac[0, 0], ((0, 0), (0, SLOTS - OUT)))
    dma = pltpu.SemaphoreType.DMA
    vmem = pltpu.VMEM
    scratch = [
        vmem((2, FLAT * STRIDE, COL), F32),
        vmem((3 * SHELLS * STRIDE, COL), F32),
        vmem(((FLAT + 2 * SHELLS) * LON, 2 * COL), F32),
        vmem((rows, COL), F32),
        vmem((3 * COL, SLOTS), BF16),
        vmem((LON, SLOTS), F32),
        vmem((2 * COL, 2 * SLOTS), BF16),
        vmem((LON, SLOTS), F32),
        vmem((2 * COL, 2 * COL), BF16),
        vmem((4 * SLOTS, COL), BF16),
        vmem((6, 2 * SLOTS, 2 * COL), BF16),
        vmem((6, 8, 2 * COL), I32),
        vmem((2, GROUP, FLAT, SLOTS), F32),
        vmem((8, COL), I32),
        vmem((GROUPS, 8, COL), I32),
        vmem((2, 12, FLAT, COL), F32),
        vmem((2, GROUPS, 2, FLAT, COL), F32),
        vmem((2, GROUPS, HALO, FLAT, COL), F32),
        vmem((2, 2, HALO, FLAT, COL), F32),
        vmem((2, 2, HALO, FLAT, COL), F32),
        vmem((2, 2, FLAT, SLOTS), F32),
        vmem((2, 2, FLAT, SLOTS), F32),
        vmem((2, HALO, FLAT, COL), F32),
        vmem((2, FLAT, SLOTS), F32),
        vmem((2, HALO, FLAT, COL), F32),
        vmem((2, FLAT, SLOTS), F32),
        dma((GROUPS,)),
        dma((GROUPS,)),
        dma((2, GROUP)),
        dma((2, GROUP)),
        dma((2, GROUPS)),
        dma((2, GROUPS)),
        dma((2,)),
        dma((2, GROUPS)),
        dma((2, 2)),
        dma((2, 2)),
        dma((2, 2)),
        dma((2, 2)),
    ]
    result = pl.pallas_call(
        kernel,
        out_shape=jax.ShapeDtypeStruct((rows, COL), F32),
        in_specs=[pl.BlockSpec(memory_space=pltpu.VMEM)] * 5,
        out_specs=pl.BlockSpec(memory_space=pltpu.VMEM),
        scratch_shapes=scratch,
        compiler_params=pltpu.CompilerParams(
            collective_id=0, has_side_effects=True, vmem_limit_bytes=40 * 1024 * 1024
        ),
    )(state.reshape(rows, COL), base, frac, recv_slots[0], scale)
    return result.reshape(state.shape)


def solution(mesh):
    placed = (
        P("panel", None, None, "lon", "colat"),
        P("panel", ("lon", "colat"), None),
        P("panel", ("lon", "colat"), None, None),
        P("panel", ("lon", "colat"), None),
    )
    return jax.shard_map(
        shards,
        mesh=mesh,
        in_specs=placed,
        out_specs=P("panel", None, None, "lon", "colat"),
        check_vma=False,
    )
```

```python
import math

import jax
import jax.numpy as jnp
from jax import lax
from jax.experimental import pallas as pl
from jax.experimental.pallas import tpu as pltpu
from jax.sharding import PartitionSpec as P

MESH = pl.DeviceIdType.MESH
F32, BF16, I32 = jnp.float32, jnp.bfloat16, jnp.int32

QUANTITIES = 8
SHELLS = 4
FLAT = QUANTITIES * SHELLS
LON = 48
COL = 128
HALO = 3
OUT = 240
SIDE = HALO * LON
SLOTS = 256
GROUP = 8
GROUPS = 8
AROUND = (1, 3, 2)
SPARE = SIDE - COL
STRIDE = LON + 16
TIME_STEP = 0.25
SPREAD = 0.1 / 3.0
S, MR, MT, MP, BR, BT, BP, WARM = range(QUANTITIES)


def dot(left, right):
    return jnp.dot(left, right, preferred_element_type=F32)


def split(value):
    high = value.astype(BF16)
    return high, (value - high.astype(F32)).astype(BF16)


def iota(shape, dim):
    return lax.broadcasted_iota(I32, shape, dim)


def cross_radial(m, b):
    return m[1] * b[2] - m[2] * b[1]


def cross_polar(m, b):
    return m[2] * b[0] - m[0] * b[2]


def cross_azimuthal(m, b):
    return m[0] * b[1] - m[1] * b[0]


def edge_rates(own, d, lap, emf_first, emf_second, along_lanes):
    grow, thin = jnp.exp(own[WARM]), jnp.exp(-own[S])
    b = own[BR:WARM]
    if along_lanes:
        vel, out = own[MT], MT
        lorentz = (d[BR] * b[1], -d[BR] * b[0] - d[BP] * b[2], d[BP] * b[1])
        turn = (emf_first, None, -emf_second)
    else:
        vel, out = own[MP], MP
        lorentz = (d[BR] * b[2], d[BT] * b[2], -d[BT] * b[1] - d[BR] * b[0])
        turn = (-emf_first, emf_second, None)
    result = [-vel * d[S] - d[out]]
    for i in range(3):
        rate = -vel * d[MR + i] + thin * lorentz[i] + SPREAD * lap[MR + i]
        if MR + i == out:
            rate = rate - grow * (d[S] + d[WARM])
        result.append(rate)
    for i in range(3):
        rate = SPREAD * lap[BR + i]
        result.append(rate if turn[i] is None else rate + turn[i])
    result.append(-vel * d[WARM] - (2.0 / 3.0) * d[out] + SPREAD * lap[WARM])
    return result


def shell_first(x):
    a, b = 8.0 * (x[3] - x[0]), 45.0
    return (
        b * (x[1] - x[0]) - 9.0 * (x[2] - x[0]) + (x[3] - x[0]),
        b * (x[2] - x[0]) - a,
        b * (x[3] - x[1]) - a,
        b * (x[3] - x[2]) - 9.0 * (x[3] - x[1]) + (x[3] - x[0]),
    )


def shell_second(x):
    return (
        2.0 * x[3] - 27.0 * x[2] + 270.0 * x[1] - 245.0 * x[0],
        245.0 * x[0] - 490.0 * x[1] + 270.0 * x[2] - 25.0 * x[3],
        245.0 * x[3] - 490.0 * x[2] + 270.0 * x[1] - 25.0 * x[0],
        2.0 * x[0] - 27.0 * x[1] + 270.0 * x[2] - 245.0 * x[3],
    )


def kernel(
    x_ref, base_ref, frac_ref, slots_ref, scale_ref, out_ref,
    frame, emf, lanes, rate, mix, rows_mix, take, rows_take, band, put, onehot, owner,
    table, idx_out, idx_in, picked, picked_rows, got_cols, got_rows, row_out, row_in, col_out, col_in,
    row_halo, col_halo, row_add, col_add,
    idx_send, idx_recv, a_send, a_recv, f_send, b_send, b_recv, l_send, l_recv, r_send, r_recv, c_send, c_recv,
):
    panel, lon, col = lax.axis_index("panel"), lax.axis_index("lon"), lax.axis_index("colat")
    n_lon, n_col = lax.axis_size("lon"), lax.axis_size("colat")
    core, mine = lax.rem(lon, 2), lax.div(lon, 2)
    member = core * n_col + col
    other = 1 - panel
    lon_up, lon_down = lax.rem(lon + 1, n_lon), lax.rem(lon + n_lon - 1, n_lon)
    col_up, col_down = lax.rem(col + 1, n_col), lax.rem(col + n_col - 1, n_col)
    outer = lax.rem(lon + 2 * core - 1 + n_lon, n_lon)
    col_edge = jnp.logical_or(col == 0, col == n_col - 1)
    lon_edge = jnp.logical_or(lon == 0, lon == n_lon - 1)
    edge_group = core * (GROUPS - 1)

    sibling = (panel, lon + 1 - 2 * core, col)

    def row_member(step):
        return core * n_col + lax.rem(col + step, n_col)

    def row_device(step):
        return (panel, lon, lax.rem(col + step, n_col))

    def cross_device(step):
        there = lax.rem(mine + step, GROUPS)
        return (other, 2 * there + core, col), there

    def remote(src, dst, send, recv, device):
        return pltpu.make_async_remote_copy(
            src_ref=src, dst_ref=dst, send_sem=send, recv_sem=recv, device_id=device, device_id_type=MESH
        )

    barrier = pltpu.get_barrier_semaphore()
    for step in AROUND:
        pl.semaphore_signal(barrier, inc=1, device_id=row_device(step), device_id_type=MESH)
    pl.semaphore_signal(barrier, inc=1, device_id=sibling, device_id_type=MESH)
    for step in range(GROUPS):
        pl.semaphore_signal(barrier, inc=1, device_id=cross_device(step)[0], device_id_type=MESH)
    pl.semaphore_signal(barrier, inc=1, device_id=(panel, outer, col), device_id_type=MESH)

    zero_rows = jnp.zeros((8, COL), F32)
    for f in range(FLAT):
        for part in range(2):
            frame[part, f * STRIDE : f * STRIDE + 8, :] = zero_rows
            frame[part, f * STRIDE + 8 + LON : (f + 1) * STRIDE, :] = zero_rows
        frame[0, f * STRIDE + 8 : f * STRIDE + 8 + LON, :] = x_ref[f * LON : (f + 1) * LON, :]
    for f in range(3 * SHELLS):
        emf[f * STRIDE : f * STRIDE + 8, :] = zero_rows
        emf[f * STRIDE + 8 + LON : (f + 1) * STRIDE, :] = zero_rows

    base = base_ref[...]
    base_row, base_col = lax.div(base, COL), lax.rem(base, COL)
    along, across = frac_ref[0:1, :], frac_ref[1:2, :]
    cells = iota((COL, SLOTS), 0)
    weight = jnp.where(cells == base_col, 1.0 - across, 0.0) + jnp.where(cells == base_col + 1, across, 0.0)
    weight_high, weight_low = split(weight)
    mix[0:COL, :] = weight_high
    mix[COL : 2 * COL, :] = weight_high
    mix[2 * COL : 3 * COL, :] = weight_low
    cells = iota((LON, SLOTS), 0)
    rows_mix[...] = jnp.where(cells == base_row, 1.0 - along, 0.0) + jnp.where(cells == base_row + 1, along, 0.0)

    place = iota((1, SLOTS), 1)
    inside = place < SIDE
    place = jnp.where(inside, place, 0)
    place_row = lax.shift_right_logical(place * 171, 9)
    place_layer = jnp.where(inside, place - HALO * place_row, 8)
    place_row = jnp.where(inside, place_row, 64)
    cells = iota((COL, SLOTS), 0)
    low = jnp.where(cells == place_layer, 1.0, 0.0).astype(BF16)
    high = jnp.where(cells == place_layer + (COL - HALO), 1.0, 0.0).astype(BF16)
    for part in range(2):
        take[part * COL : (part + 1) * COL, 0:SLOTS] = low
        take[part * COL : (part + 1) * COL, SLOTS : 2 * SLOTS] = high
    rows_take[...] = jnp.where(iota((LON, SLOTS), 0) == place_row, 1.0, 0.0)

    place = iota((SLOTS, COL), 0)
    inside = place < SIDE
    place = jnp.where(inside, place, 0)
    layer = jnp.where(inside, place - HALO * lax.shift_right_logical(place * 171, 9), 8)
    cells = iota((SLOTS, COL), 1)
    low = jnp.where(jnp.logical_and(inside, cells == layer), 1.0, 0.0).astype(BF16)
    high = jnp.where(jnp.logical_and(inside, cells == layer + (COL - HALO)), 1.0, 0.0).astype(BF16)
    for part in range(2):
        put[part * SLOTS : (part + 1) * SLOTS, :] = low
        put[(2 + part) * SLOTS : (3 + part) * SLOTS, :] = high

    apart = iota((COL, COL), 0) - iota((COL, COL), 1)
    reach = jnp.abs(apart)
    first = jnp.where(reach == 1, 45.0, jnp.where(reach == 2, -9.0, jnp.where(reach == 3, 1.0, 0.0)))
    first = jnp.where(apart < 0, -first, first).astype(BF16)
    second = jnp.where(
        reach == 0, -490.0, jnp.where(reach == 1, 270.0, jnp.where(reach == 2, -27.0, jnp.where(reach == 3, 2.0, 0.0)))
    ).astype(BF16)
    for part in range(2):
        band[part * COL : (part + 1) * COL, 0:COL] = first
        band[part * COL : (part + 1) * COL, COL : 2 * COL] = second

    spot = iota((1, SLOTS), 1)
    sides = jnp.where(spot < SIDE, jnp.maximum(slots_ref[:, 0:SLOTS], slots_ref[:, SIDE : SIDE + SLOTS]), -1)
    idx_out[0:1, :] = sides[:, 0:COL]
    idx_out[1:2, :] = sides[:, COL : 2 * COL]
    for h in range(HALO):
        at = 2 * SIDE + h * COL
        idx_out[2 + h : 3 + h, :] = jnp.maximum(
            slots_ref[:, at : at + COL], slots_ref[:, at + HALO * COL : at + HALO * COL + COL]
        )
    idx_out[5:8, :] = jnp.full((3, COL), -1, I32)

    layer_lane = place_layer
    scale = scale_ref[...]

    def load_split(part, pair):
        block = jnp.concatenate(
            [frame[part, pl.ds(pl.multiple_of((8 * pair + q) * STRIDE, 8) + 8, LON), :] for q in range(8)], axis=0
        )
        return split(block)

    def interpolate(part):
        def body(pair, carry):
            high, low = load_split(part, pair)
            value = dot(jnp.concatenate([high, low, high], axis=1), mix[...])
            value = jnp.sum(value.reshape(8, LON, SLOTS) * rows_mix[...][None], axis=1)
            table[part, member, pl.ds(pl.multiple_of(8 * pair, 8), 8), :] = value
            return carry

        lax.fori_loop(0, FLAT // 8, body, 0)

    def lane_pass(part):
        def body(pair, carry):
            high, low = load_split(part, pair)
            both = jnp.concatenate([high, low], axis=1)
            value = dot(both, take[...]).reshape(8, LON, 2 * SLOTS)
            value = jnp.sum(value * jnp.concatenate([rows_take[...]] * 2, axis=1)[None], axis=1)
            rows = pl.ds(pl.multiple_of(8 * pair, 8), 8)
            col_out[part, 0, rows, :] = value[:, 0:SLOTS]
            col_out[part, 1, rows, :] = value[:, SLOTS : 2 * SLOTS]
            lanes[pl.ds(pl.multiple_of(8 * LON * pair, 8), 8 * LON), :] = dot(both, band[...])
            return carry

        lax.fori_loop(0, FLAT // 8, body, 0)

    def emf_pass(part):
        for r in range(SHELLS):
            def field(q):
                at = (q * SHELLS + r) * STRIDE + 8
                return frame[part, at : at + LON, :]

            m, b = [field(MR + i) for i in range(3)], [field(BR + i) for i in range(3)]
            for i, form in enumerate((cross_radial, cross_polar, cross_azimuthal)):
                at = (i * SHELLS + r) * STRIDE + 8
                emf[at : at + LON, :] = form(m, b)
        for i, at in ((0, FLAT), (2, FLAT + SHELLS)):
            block = jnp.concatenate(
                [emf[(i * SHELLS + r) * STRIDE + 8 : (i * SHELLS + r) * STRIDE + 8 + LON, :] for r in range(SHELLS)],
                axis=0,
            )
            high, low = split(block)
            lanes[at * LON : (at + SHELLS) * LON, 0:COL] = dot(
                jnp.concatenate([high, low], axis=1), band[:, 0:COL]
            )

    def main_pass(part, start, stop):
        def body(block, carry):
            here = pl.multiple_of(8 * block, 8)

            def near(f, apart):
                return frame[part, pl.ds(f * STRIDE + 8 + here + apart, 8), :]

            def near_emf(f, apart):
                return emf[pl.ds(f * STRIDE + 8 + here + apart, 8), :]

            def lane_first(f):
                return lanes[pl.ds(f * LON + here, 8), 0:COL]

            def lane_second(f):
                return lanes[pl.ds(f * LON + here, 8), COL : 2 * COL]

            def row_first(at):
                return 45.0 * (at[1] - at[-1]) - 9.0 * (at[2] - at[-2]) + (at[3] - at[-3])

            def row_second(at, centre):
                return (
                    270.0 * (at[1] + at[-1]) - 27.0 * (at[2] + at[-2]) + 2.0 * (at[3] + at[-3]) - 490.0 * centre
                )

            centre = [[near(q * SHELLS + r, 0) for r in range(SHELLS)] for q in range(QUANTITIES)]
            radial = [shell_first(x) for x in centre]
            radial_second = [None if q == S else shell_second(centre[q]) for q in range(QUANTITIES)]
            emf_centre = [[near_emf(i * SHELLS + r, 0) for r in range(SHELLS)] for i in range(3)]
            emf_radial = [None, shell_first(emf_centre[1]), shell_first(emf_centre[2])]
            for r in range(SHELLS):
                own = [centre[q][r] for q in range(QUANTITIES)]
                g, lap = [], []
                for q in range(QUANTITIES):
                    f = q * SHELLS + r
                    at = {d: near(f, d) for d in (-3, -2, -1, 1, 2, 3)}
                    g.append((radial[q][r], lane_first(f), scale * row_first(at)))
                    if q == S:
                        lap.append(None)
                    else:
                        lap.append(
                            radial_second[q][r] + lane_second(f) + (scale * scale) * row_second(at, own[q])
                        )
                m, b = own[MR:BR], own[BR:WARM]

                def advect(q):
                    return m[0] * g[q][0] + m[1] * g[q][1] + m[2] * g[q][2]

                div = g[MR][0] + g[MT][1] + g[MP][2]
                current = (g[BP][1] - g[BT][2], g[BR][2] - g[BP][0], g[BT][0] - g[BR][1])
                lorentz = (
                    current[1] * b[2] - current[2] * b[1],
                    current[2] * b[0] - current[0] * b[2],
                    current[0] * b[1] - current[1] * b[0],
                )
                grow, thin = jnp.exp(own[WARM]), jnp.exp(-own[S])
                emf_rows = {}
                for i in (0, 1):
                    f = i * SHELLS + r
                    emf_rows[i] = scale * row_first({d: near_emf(f, d) for d in (-3, -2, -1, 1, 2, 3)})
                turn = (
                    lane_first(FLAT + SHELLS + r) - emf_rows[1],
                    emf_rows[0] - emf_radial[2][r],
                    emf_radial[1][r] - lane_first(FLAT + r),
                )
                result = [-advect(S) - div]
                for i in range(3):
                    result.append(
                        -advect(MR + i) - grow * (g[S][i] + g[WARM][i]) + thin * lorentz[i] + SPREAD * lap[MR + i]
                    )
                for i in range(3):
                    result.append(turn[i] + SPREAD * lap[BR + i])
                result.append(-advect(WARM) - (2.0 / 3.0) * div + SPREAD * lap[WARM])
                for q in range(QUANTITIES):
                    rate[pl.ds((q * SHELLS + r) * LON + here, 8), :] = result[q]
            return carry

        lax.fori_loop(start, stop, body, 0)

    def rows_of(part):
        for h in range(HALO):
            row_out[part, 0, h] = frame[part, pl.ds(8 + h, FLAT, stride=STRIDE), :]
            row_out[part, 1, h] = frame[part, pl.ds(8 + LON - HALO + h, FLAT, stride=STRIDE), :]

    def prepare_picks():
        for lane_tile in range(12):
            if lane_tile < GROUPS:
                slot = idx_in[lane_tile, 0:1, :]
            elif lane_tile == GROUPS:
                slot = idx_in[0, 1:2, :]
                for q in range(1, GROUPS):
                    slot = jnp.maximum(slot, pltpu.roll(idx_in[q], SPARE * q, 1)[1:2, :])
            else:
                slot = idx_in[edge_group, lane_tile - 7 : lane_tile - 6, :]
            slot = slot - mine * (GROUP * OUT)
            who = jnp.zeros_like(slot)
            for q in range(1, GROUP):
                who = who + jnp.where(slot >= q * OUT, 1, 0)
            cell = slot - who * OUT
            who = jnp.where(jnp.logical_and(slot >= 0, slot < GROUP * OUT), who, -1)
            at = (lane_tile % 2) * COL
            owner[lane_tile // 2, :, at : at + COL] = jnp.broadcast_to(who, (8, COL))
            hot = jnp.where(iota((SLOTS, COL), 0) == cell, 1.0, 0.0).astype(BF16)
            for copy in range(2):
                onehot[lane_tile // 2, copy * SLOTS : (copy + 1) * SLOTS, at : at + COL] = hot

    def table_split(part):
        high, low = split(table[part].reshape(GROUP * FLAT, SLOTS))
        return jnp.concatenate([high, low], axis=1)

    def pick(both, tile):
        value = dot(both, onehot[tile])
        who = jnp.broadcast_to(owner[tile, 0:1, :], (FLAT, SLOTS))
        total = jnp.zeros((FLAT, SLOTS), F32)
        for q in range(GROUP):
            total = total + jnp.where(who == q, value[q * FLAT : (q + 1) * FLAT, :], 0.0)
        return total[:, 0:COL], total[:, COL : 2 * COL]

    def pick_sides(part, both, last):
        def body(tile, carry):
            first, second = pick(both, tile)
            picked[part, 2 * tile, 0:FLAT, :] = first
            picked[part, 2 * tile + 1, 0:FLAT, :] = second
            return carry

        lax.fori_loop(0, GROUPS // 2, body, 0)
        spot = lax.div(iota((8, COL), 1), SPARE)
        for there in range(GROUPS):
            total = jnp.zeros((8, COL), F32)
            for q in range(FLAT // 8):
                turn = (q - there) % GROUPS
                rows = last[8 * q : 8 * q + 8, :]
                total = jnp.where(spot == q, rows if turn == 0 else pltpu.roll(rows, SPARE * turn, 1), total)
            picked[part, there, FLAT : FLAT + 8, :] = total

    def row_corrections(part):
        for side in range(2):
            halo = [
                [row_halo[side, h, q * SHELLS : (q + 1) * SHELLS, :] for q in range(QUANTITIES)] for h in range(HALO)
            ]
            halo_emf = [(cross_radial(x[MR:BR], x[BR:WARM]), cross_polar(x[MR:BR], x[BR:WARM])) for x in halo]
            for j in range(HALO):
                own = [row_out[part, side, j, q * SHELLS : (q + 1) * SHELLS, :] for q in range(QUANTITIES)]

                def total(weights, of):
                    result = None
                    for m in (1, 2, 3):
                        h = j + 3 - m if side == 0 else m - 3 + j
                        if 0 <= h < HALO:
                            term = weights[m - 1] * of(h)
                            result = term if result is None else result + term
                    return result

                sign = -1.0 if side == 0 else 1.0
                firsts = (45.0 * sign, -9.0 * sign, sign)
                d = [scale * total(firsts, lambda h, q=q: halo[h][q]) for q in range(QUANTITIES)]
                lap = [
                    None if q == S else (scale * scale) * total((270.0, -27.0, 2.0), lambda h, q=q: halo[h][q])
                    for q in range(QUANTITIES)
                ]
                emf_radial = scale * total(firsts, lambda h: halo_emf[h][0])
                emf_polar = scale * total(firsts, lambda h: halo_emf[h][1])
                result = edge_rates(own, d, lap, emf_polar, emf_radial, False)
                for q in range(QUANTITIES):
                    row_add[side, j, q * SHELLS : (q + 1) * SHELLS, :] = result[q]
        for side in range(2):
            for j in range(HALO):
                rows = pl.ds(j if side == 0 else LON - HALO + j, FLAT, stride=LON)
                rate[rows, :] = rate[rows, :] + row_add[side, j]

    def col_corrections(part):
        for side in range(2):
            halo = [col_halo[side, q * SHELLS : (q + 1) * SHELLS, :] for q in range(QUANTITIES)]
            own = [col_out[part, side, q * SHELLS : (q + 1) * SHELLS, :] for q in range(QUANTITIES)]
            sign = -1.0 if side == 0 else 1.0

            def both(value):
                firsts = seconds = None
                for m, one, two in ((1, 45.0, 270.0), (2, -9.0, -27.0), (3, 1.0, 2.0)):
                    if side == 0:
                        moved = value if m == 3 else pltpu.roll(value, SLOTS - (3 - m), 1)
                        valid = layer_lane <= m - 1
                    else:
                        moved = value if m == 3 else pltpu.roll(value, 3 - m, 1)
                        valid = jnp.logical_and(layer_lane >= 3 - m, layer_lane < HALO)
                    moved = jnp.where(valid, moved, 0.0)
                    first_term, second_term = (one * sign) * moved, two * moved
                    firsts = first_term if firsts is None else firsts + first_term
                    seconds = second_term if seconds is None else seconds + second_term
                return firsts, seconds

            pairs = [both(x) for x in halo]
            emf_azimuthal = both(cross_azimuthal(halo[MR:BR], halo[BR:WARM]))[0]
            emf_radial = both(cross_radial(halo[MR:BR], halo[BR:WARM]))[0]
            result = edge_rates(
                own, [x[0] for x in pairs], [x[1] for x in pairs], emf_azimuthal, emf_radial, True
            )
            for q in range(QUANTITIES):
                col_add[side, q * SHELLS : (q + 1) * SHELLS, :] = result[q]

    def finish(part):
        def body(pair, carry):
            pieces = []
            for side in range(2):
                block = col_add[side, pl.ds(pl.multiple_of(8 * pair, 8), 8), :]
                high = block.astype(BF16).astype(F32)
                for value in (high, block - high):
                    spread = value.reshape(8, 1, SLOTS) * rows_take[...][None]
                    pieces.append(spread.reshape(8 * LON, SLOTS).astype(BF16))
            added = dot(jnp.concatenate(pieces, axis=1), put[...])
            rows = pl.ds(pl.multiple_of(8 * LON * pair, 8), 8 * LON)
            change = (TIME_STEP / 60.0) * (rate[rows, :] + added)
            start = x_ref[rows, :]
            if part == 0:
                middle = start + change
                for q in range(8):
                    at = pl.multiple_of((8 * pair + q) * STRIDE, 8) + 8
                    frame[1, pl.ds(at, LON), :] = middle[q * LON : (q + 1) * LON, :]
            else:
                middle = jnp.concatenate(
                    [frame[1, pl.ds(pl.multiple_of((8 * pair + q) * STRIDE, 8) + 8, LON), :] for q in range(8)], axis=0
                )
                out_ref[rows, :] = 0.5 * (start + middle + change)
            return carry

        lax.fori_loop(0, FLAT // 8, body, 0)

    def a_copy(part, step):
        block = table.at[part, member]
        return remote(block, block, a_send.at[part, step], a_recv.at[part, member], row_device(step))

    def a_arrival(part, step):
        block = table.at[part, row_member(step)]
        return remote(block, block, a_send.at[part, step], a_recv.at[part, row_member(step)], row_device(step))

    def f_copy(part, step):
        block = table.at[part, row_member(step)]
        return remote(block, block, f_send.at[part, step], a_recv.at[part, row_member(step)], sibling)

    def f_arrival(part, q):
        there = (1 - core) * n_col + q
        block = table.at[part, there]
        return remote(block, block, f_send.at[part, q], a_recv.at[part, there], sibling)

    def b_copy(part, step):
        device, there = cross_device(step)
        return remote(
            picked.at[part, there], got_cols.at[part, mine], b_send.at[part, step], b_recv.at[part, mine], device
        )

    def b_arrival(part, group):
        return remote(
            picked.at[part, 0], got_cols.at[part, group], b_send.at[part, 0], b_recv.at[part, group],
            (other, lon, col),
        )

    def l_copy(part):
        return remote(
            picked_rows.at[part], got_rows.at[part, mine], l_send.at[part], l_recv.at[part, mine],
            (other, 2 * edge_group + core, col),
        )

    def l_arrival(part, group):
        return remote(
            picked_rows.at[part], got_rows.at[part, group], l_send.at[part], l_recv.at[part, group],
            (other, lon, col),
        )

    def row_copy(part, side):
        return remote(
            row_out.at[part, 1 - side], row_in.at[part, side], r_send.at[part, side], r_recv.at[part, side],
            (panel, lon_up if side == 0 else lon_down, col),
        )

    def col_copy(part, side):
        return remote(
            col_out.at[part, 1 - side], col_in.at[part, side], c_send.at[part, side], c_recv.at[part, side],
            (panel, lon, col_up if side == 0 else col_down),
        )

    def idx_copy(step):
        device, _ = cross_device(step)
        return remote(idx_out, idx_in.at[mine], idx_send.at[step], idx_recv.at[mine], device)

    def idx_arrival(group):
        return remote(idx_out, idx_in.at[group], idx_send.at[0], idx_recv.at[group], (other, lon, col))

    interpolate(0)
    pl.semaphore_wait(barrier, len(AROUND) + 2 + GROUPS)

    for part in range(2):
        if part == 1:
            interpolate(1)
        for step in AROUND:
            a_copy(part, step).start()
        f_copy(part, 0).start()
        if part == 0:
            for step in range(GROUPS):
                idx_copy(step).start()
        rows_of(part)
        for side in range(2):
            row_copy(part, side).start()
        lane_pass(part)
        for side in range(2):
            col_copy(part, side).start()
        emf_pass(part)
        if part == 0:
            for group in range(GROUPS):
                idx_arrival(group).wait_recv()
            prepare_picks()
        main_pass(part, 0, 1)
        for step in AROUND:
            a_arrival(part, step).wait_recv()
            f_copy(part, step).start()
        main_pass(part, 1, 2)
        for q in range(GROUP // 2):
            f_arrival(part, q).wait_recv()
        both = table_split(part)
        last, picked_rows[part, 0] = pick(both, 4)
        picked_rows[part, 1], picked_rows[part, 2] = pick(both, 5)
        l_copy(part).start()

        @pl.when(col_edge)
        def _():
            pick_sides(part, both, last)
            for step in range(GROUPS):
                b_copy(part, step).start()

        main_pass(part, 2, 6)
        for side in range(2):
            row_copy(part, side).wait_recv()
            col_copy(part, side).wait_recv()

        for side in range(2):
            at_edge = lon == (0 if side == 0 else n_lon - 1)

            @pl.when(at_edge)
            def _():
                for group in range(GROUPS):
                    l_arrival(part, group).wait_recv()
                total = got_rows[part, 0]
                for group in range(1, GROUPS):
                    total = total + got_rows[part, group]
                row_halo[side] = total

            @pl.when(jnp.logical_not(at_edge))
            def _():
                row_halo[side] = row_in[part, side]

        row_corrections(part)

        for side in range(2):
            at_edge = col == (0 if side == 0 else n_col - 1)

            @pl.when(at_edge)
            def _():
                for group in range(GROUPS):
                    b_arrival(part, group).wait_recv()
                total = got_cols[part, 0]
                for group in range(1, GROUPS):
                    total = total + got_cols[part, group]
                col_halo[side, :, 0:COL] = total[0:FLAT]
                rest = total[FLAT : FLAT + 8]
                for q in range(FLAT // 8):
                    col_halo[side, 8 * q : 8 * q + 8, COL : 2 * COL] = (
                        rest if q == 0 else pltpu.roll(rest, COL - SPARE * q, 1)
                    )

            @pl.when(jnp.logical_not(at_edge))
            def _():
                col_halo[side] = col_in[part, side]

        col_corrections(part)
        finish(part)

    for step in range(GROUPS):
        idx_copy(step).wait_send()
    for part in range(2):
        for step in AROUND:
            a_copy(part, step).wait_send()
        for step in range(GROUP // 2):
            f_copy(part, step).wait_send()
        for side in range(2):
            row_copy(part, side).wait_send()
            col_copy(part, side).wait_send()
        l_copy(part).wait_send()

        @pl.when(col_edge)
        def _():
            for step in range(GROUPS):
                b_copy(part, step).wait_send()


def inverse_sine(start, count, total):
    place = (start + jnp.arange(count, dtype=jnp.int32)).astype(jnp.float32)
    colatitude = math.pi / 4.0 + (place + 0.5) * (math.pi / 2.0 / total)
    return 1.0 / jnp.sin(colatitude)


def shards(state, send_base, send_frac, recv_slots):
    rows = FLAT * LON
    scale = inverse_sine(lax.axis_index("colat") * COL, COL, COL * lax.axis_size("colat"))[None]
    base = jnp.pad(send_base[0], ((0, 0), (0, SLOTS - OUT)))
    frac = jnp.pad(send_frac[0, 0], ((0, 0), (0, SLOTS - OUT)))
    dma = pltpu.SemaphoreType.DMA
    vmem = pltpu.VMEM
    scratch = [
        vmem((2, FLAT * STRIDE, COL), F32),
        vmem((3 * SHELLS * STRIDE, COL), F32),
        vmem(((FLAT + 2 * SHELLS) * LON, 2 * COL), F32),
        vmem((rows, COL), F32),
        vmem((3 * COL, SLOTS), BF16),
        vmem((LON, SLOTS), F32),
        vmem((2 * COL, 2 * SLOTS), BF16),
        vmem((LON, SLOTS), F32),
        vmem((2 * COL, 2 * COL), BF16),
        vmem((4 * SLOTS, COL), BF16),
        vmem((6, 2 * SLOTS, 2 * COL), BF16),
        vmem((6, 8, 2 * COL), I32),
        vmem((2, GROUP, FLAT, SLOTS), F32),
        vmem((8, COL), I32),
        vmem((GROUPS, 8, COL), I32),
        vmem((2, GROUPS, FLAT + 8, COL), F32),
        vmem((2, HALO, FLAT, COL), F32),
        vmem((2, GROUPS, FLAT + 8, COL), F32),
        vmem((2, GROUPS, HALO, FLAT, COL), F32),
        vmem((2, 2, HALO, FLAT, COL), F32),
        vmem((2, 2, HALO, FLAT, COL), F32),
        vmem((2, 2, FLAT, SLOTS), F32),
        vmem((2, 2, FLAT, SLOTS), F32),
        vmem((2, HALO, FLAT, COL), F32),
        vmem((2, FLAT, SLOTS), F32),
        vmem((2, HALO, FLAT, COL), F32),
        vmem((2, FLAT, SLOTS), F32),
        dma((GROUPS,)),
        dma((GROUPS,)),
        dma((2, GROUP // 2)),
        dma((2, GROUP)),
        dma((2, GROUP // 2)),
        dma((2, GROUPS)),
        dma((2, GROUPS)),
        dma((2,)),
        dma((2, GROUPS)),
        dma((2, 2)),
        dma((2, 2)),
        dma((2, 2)),
        dma((2, 2)),
    ]
    result = pl.pallas_call(
        kernel,
        out_shape=jax.ShapeDtypeStruct((rows, COL), F32),
        in_specs=[pl.BlockSpec(memory_space=pltpu.VMEM)] * 5,
        out_specs=pl.BlockSpec(memory_space=pltpu.VMEM),
        scratch_shapes=scratch,
        compiler_params=pltpu.CompilerParams(
            collective_id=0, has_side_effects=True, vmem_limit_bytes=40 * 1024 * 1024
        ),
    )(state.reshape(rows, COL), base, frac, recv_slots[0], scale)
    return result.reshape(state.shape)


def solution(mesh):
    placed = (
        P("panel", None, None, "lon", "colat"),
        P("panel", ("lon", "colat"), None),
        P("panel", ("lon", "colat"), None, None),
        P("panel", ("lon", "colat"), None),
    )
    return jax.shard_map(
        shards,
        mesh=mesh,
        in_specs=placed,
        out_specs=P("panel", None, None, "lon", "colat"),
        check_vma=False,
    )
```

```python
import math

import jax
import jax.numpy as jnp
from jax import lax
from jax.experimental import pallas as pl
from jax.experimental.pallas import tpu as pltpu
from jax.sharding import PartitionSpec as P

MESH = pl.DeviceIdType.MESH
F32, BF16, I32 = jnp.float32, jnp.bfloat16, jnp.int32

QUANTITIES = 8
SHELLS = 4
FLAT = QUANTITIES * SHELLS
LON = 48
COL = 128
HALO = 3
OUT = 240
SIDE = HALO * LON
SLOTS = 256
GROUP = 8
GROUPS = 8
AROUND = (1, 3, 2)
SPARE = SIDE - COL
STRIDE = LON + 16
TIME_STEP = 0.25
SPREAD = 0.1 / 3.0
S, MR, MT, MP, BR, BT, BP, WARM = range(QUANTITIES)


def dot(left, right):
    return jnp.dot(left, right, preferred_element_type=F32)


def split(value):
    high = value.astype(BF16)
    return high, (value - high.astype(F32)).astype(BF16)


def iota(shape, dim):
    return lax.broadcasted_iota(I32, shape, dim)


def cross_radial(m, b):
    return m[1] * b[2] - m[2] * b[1]


def cross_polar(m, b):
    return m[2] * b[0] - m[0] * b[2]


def cross_azimuthal(m, b):
    return m[0] * b[1] - m[1] * b[0]


def edge_rates(own, d, lap, emf_first, emf_second, along_lanes):
    grow, thin = jnp.exp(own[WARM]), jnp.exp(-own[S])
    b = own[BR:WARM]
    if along_lanes:
        vel, out = own[MT], MT
        lorentz = (d[BR] * b[1], -d[BR] * b[0] - d[BP] * b[2], d[BP] * b[1])
        turn = (emf_first, None, -emf_second)
    else:
        vel, out = own[MP], MP
        lorentz = (d[BR] * b[2], d[BT] * b[2], -d[BT] * b[1] - d[BR] * b[0])
        turn = (-emf_first, emf_second, None)
    result = [-vel * d[S] - d[out]]
    for i in range(3):
        rate = -vel * d[MR + i] + thin * lorentz[i] + SPREAD * lap[MR + i]
        if MR + i == out:
            rate = rate - grow * (d[S] + d[WARM])
        result.append(rate)
    for i in range(3):
        rate = SPREAD * lap[BR + i]
        result.append(rate if turn[i] is None else rate + turn[i])
    result.append(-vel * d[WARM] - (2.0 / 3.0) * d[out] + SPREAD * lap[WARM])
    return result


def shell_first(x):
    a, b = 8.0 * (x[3] - x[0]), 45.0
    return (
        b * (x[1] - x[0]) - 9.0 * (x[2] - x[0]) + (x[3] - x[0]),
        b * (x[2] - x[0]) - a,
        b * (x[3] - x[1]) - a,
        b * (x[3] - x[2]) - 9.0 * (x[3] - x[1]) + (x[3] - x[0]),
    )


def shell_second(x):
    return (
        2.0 * x[3] - 27.0 * x[2] + 270.0 * x[1] - 245.0 * x[0],
        245.0 * x[0] - 490.0 * x[1] + 270.0 * x[2] - 25.0 * x[3],
        245.0 * x[3] - 490.0 * x[2] + 270.0 * x[1] - 25.0 * x[0],
        2.0 * x[0] - 27.0 * x[1] + 270.0 * x[2] - 245.0 * x[3],
    )


def kernel(
    x_ref, base_ref, frac_ref, slots_ref, scale_ref, out_ref,
    frame, emf, lanes, rate, mix, rows_mix, band, onehot, owner, turned,
    table, idx_out, idx_in, picked, picked_rows, got_cols, got_rows, row_out, row_in, col_own, col_out, col_in,
    row_halo, col_halo, edge_add,
    idx_send, idx_recv, a_send, a_recv, f_send, b_send, b_recv, l_send, l_recv, r_send, r_recv, c_send, c_recv,
):
    panel, lon, col = lax.axis_index("panel"), lax.axis_index("lon"), lax.axis_index("colat")
    n_lon, n_col = lax.axis_size("lon"), lax.axis_size("colat")
    core, mine = lax.rem(lon, 2), lax.div(lon, 2)
    member = core * n_col + col
    other = 1 - panel
    lon_up, lon_down = lax.rem(lon + 1, n_lon), lax.rem(lon + n_lon - 1, n_lon)
    col_up, col_down = lax.rem(col + 1, n_col), lax.rem(col + n_col - 1, n_col)
    outer = lax.rem(lon + 2 * core - 1 + n_lon, n_lon)
    col_edge = jnp.logical_or(col == 0, col == n_col - 1)
    lon_edge = jnp.logical_or(lon == 0, lon == n_lon - 1)
    edge_group = core * (GROUPS - 1)

    sibling = (panel, lon + 1 - 2 * core, col)

    def row_member(step):
        return core * n_col + lax.rem(col + step, n_col)

    def row_device(step):
        return (panel, lon, lax.rem(col + step, n_col))

    def cross_device(step):
        there = lax.rem(mine + step, GROUPS)
        return (other, 2 * there + core, col), there

    def remote(src, dst, send, recv, device):
        return pltpu.make_async_remote_copy(
            src_ref=src, dst_ref=dst, send_sem=send, recv_sem=recv, device_id=device, device_id_type=MESH
        )

    barrier = pltpu.get_barrier_semaphore()
    for step in AROUND:
        pl.semaphore_signal(barrier, inc=1, device_id=row_device(step), device_id_type=MESH)
    pl.semaphore_signal(barrier, inc=1, device_id=sibling, device_id_type=MESH)
    for step in range(GROUPS):
        pl.semaphore_signal(barrier, inc=1, device_id=cross_device(step)[0], device_id_type=MESH)
    pl.semaphore_signal(barrier, inc=1, device_id=(panel, outer, col), device_id_type=MESH)

    zero_rows = jnp.zeros((8, COL), F32)
    for f in range(FLAT):
        for part in range(2):
            frame[part, f * STRIDE : f * STRIDE + 8, :] = zero_rows
            frame[part, f * STRIDE + 8 + LON : (f + 1) * STRIDE, :] = zero_rows
        frame[0, f * STRIDE + 8 : f * STRIDE + 8 + LON, :] = x_ref[f * LON : (f + 1) * LON, :]
    for f in range(3 * SHELLS):
        emf[f * STRIDE : f * STRIDE + 8, :] = zero_rows
        emf[f * STRIDE + 8 + LON : (f + 1) * STRIDE, :] = zero_rows

    base = base_ref[...]
    base_row, base_col = lax.div(base, COL), lax.rem(base, COL)
    along, across = frac_ref[0:1, :], frac_ref[1:2, :]
    cells = iota((COL, SLOTS), 0)
    weight = jnp.where(cells == base_col, 1.0 - across, 0.0) + jnp.where(cells == base_col + 1, across, 0.0)
    weight_high, weight_low = split(weight)
    mix[0:COL, :] = weight_high
    mix[COL : 2 * COL, :] = weight_high
    mix[2 * COL : 3 * COL, :] = weight_low
    cells = iota((LON, SLOTS), 0)
    rows_mix[...] = jnp.where(cells == base_row, 1.0 - along, 0.0) + jnp.where(cells == base_row + 1, along, 0.0)

    for half in range(2):
        turned[half, :, :] = jnp.zeros((COL, COL), F32)

    apart = iota((COL, COL), 0) - iota((COL, COL), 1)
    reach = jnp.abs(apart)
    first = jnp.where(reach == 1, 45.0, jnp.where(reach == 2, -9.0, jnp.where(reach == 3, 1.0, 0.0)))
    first = jnp.where(apart < 0, -first, first).astype(BF16)
    second = jnp.where(
        reach == 0, -490.0, jnp.where(reach == 1, 270.0, jnp.where(reach == 2, -27.0, jnp.where(reach == 3, 2.0, 0.0)))
    ).astype(BF16)
    for part in range(2):
        band[part * COL : (part + 1) * COL, 0:COL] = first
        band[part * COL : (part + 1) * COL, COL : 2 * COL] = second

    spot = iota((1, SLOTS), 1)
    sides = jnp.where(spot < SIDE, jnp.maximum(slots_ref[:, 0:SLOTS], slots_ref[:, SIDE : SIDE + SLOTS]) + 1, 0)
    digits = jnp.concatenate([lax.div(sides, COL), lax.rem(sides, COL), jnp.zeros((6, SLOTS), I32)], axis=0)
    source, target = iota((SLOTS, SLOTS), 0), iota((SLOTS, SLOTS), 1)
    layer = jnp.where(target >= LON, 1, 0) + jnp.where(target >= 2 * LON, 1, 0)
    order = jnp.logical_and(target < SIDE, source == HALO * (target - LON * layer) + layer)
    digits = dot(digits.astype(F32).astype(BF16), jnp.where(order, 1.0, 0.0).astype(BF16)).astype(I32)
    sides = digits[0:1, :] * COL + digits[1:2, :] - 1
    idx_out[0:1, :] = sides[:, 0:COL]
    idx_out[1:2, :] = sides[:, COL : 2 * COL]
    for h in range(HALO):
        at = 2 * SIDE + h * COL
        idx_out[2 + h : 3 + h, :] = jnp.maximum(
            slots_ref[:, at : at + COL], slots_ref[:, at + HALO * COL : at + HALO * COL + COL]
        )
    idx_out[5:8, :] = jnp.full((3, COL), -1, I32)

    scale = scale_ref[...]

    def load_split(part, pair):
        block = jnp.concatenate(
            [frame[part, pl.ds(pl.multiple_of((8 * pair + q) * STRIDE, 8) + 8, LON), :] for q in range(8)], axis=0
        )
        return split(block)

    def interpolate(part):
        def body(pair, carry):
            high, low = load_split(part, pair)
            value = dot(jnp.concatenate([high, low, high], axis=1), mix[...])
            value = jnp.sum(value.reshape(8, LON, SLOTS) * rows_mix[...][None], axis=1)
            table[part, member, pl.ds(pl.multiple_of(8 * pair, 8), 8), :] = value
            return carry

        lax.fori_loop(0, FLAT // 8, body, 0)

    def lane_pass(part):
        def body(pair, carry):
            high, low = load_split(part, pair)
            both = jnp.concatenate([high, low], axis=1)
            lanes[pl.ds(pl.multiple_of(8 * LON * pair, 8), 8 * LON), :] = dot(both, band[...])
            return carry

        lax.fori_loop(0, FLAT // 8, body, 0)

    def cols_of(part):
        lane = iota((LON, COL), 1)
        for half in range(2):
            edge = jnp.zeros((LON, COL), F32)
            for g in range(FLAT // 2):
                at = (half * (FLAT // 2) + g) * STRIDE + 8
                moved = pltpu.roll(frame[part, at : at + LON, :], 8 * g + HALO, 1)
                edge = jnp.where(jnp.logical_and(lane >= 8 * g, lane < 8 * g + 2 * HALO), moved, edge)
            turned[half, :, 0:LON] = jnp.transpose(edge)
        for side in range(2):
            for j in range(HALO):
                first = (1 - side) * HALO + j
                for half in range(2):
                    col_own[part, side, j, half * (FLAT // 2) : (half + 1) * (FLAT // 2), :] = turned[
                        half, pl.ds(first, FLAT // 2, stride=8), :
                    ]
            col_out[part, side, 0] = jnp.where(
                iota((FLAT, COL), 1) < COL // 2, col_own[part, side, 0], pltpu.roll(col_own[part, side, 1], COL // 2, 1)
            )
            col_out[part, side, 1] = col_own[part, side, 2]

    def emf_pass(part):
        for r in range(SHELLS):
            def field(q):
                at = (q * SHELLS + r) * STRIDE + 8
                return frame[part, at : at + LON, :]

            m, b = [field(MR + i) for i in range(3)], [field(BR + i) for i in range(3)]
            for i, form in enumerate((cross_radial, cross_polar, cross_azimuthal)):
                at = (i * SHELLS + r) * STRIDE + 8
                emf[at : at + LON, :] = form(m, b)
        for i, at in ((0, FLAT), (2, FLAT + SHELLS)):
            block = jnp.concatenate(
                [emf[(i * SHELLS + r) * STRIDE + 8 : (i * SHELLS + r) * STRIDE + 8 + LON, :] for r in range(SHELLS)],
                axis=0,
            )
            high, low = split(block)
            lanes[at * LON : (at + SHELLS) * LON, 0:COL] = dot(
                jnp.concatenate([high, low], axis=1), band[:, 0:COL]
            )

    def main_pass(part, start, stop):
        def body(block, carry):
            here = pl.multiple_of(8 * block, 8)

            def near(f, apart):
                return frame[part, pl.ds(f * STRIDE + 8 + here + apart, 8), :]

            def near_emf(f, apart):
                return emf[pl.ds(f * STRIDE + 8 + here + apart, 8), :]

            def lane_first(f):
                return lanes[pl.ds(f * LON + here, 8), 0:COL]

            def lane_second(f):
                return lanes[pl.ds(f * LON + here, 8), COL : 2 * COL]

            def row_first(at):
                return 45.0 * (at[1] - at[-1]) - 9.0 * (at[2] - at[-2]) + (at[3] - at[-3])

            def row_second(at, centre):
                return (
                    270.0 * (at[1] + at[-1]) - 27.0 * (at[2] + at[-2]) + 2.0 * (at[3] + at[-3]) - 490.0 * centre
                )

            centre = [[near(q * SHELLS + r, 0) for r in range(SHELLS)] for q in range(QUANTITIES)]
            radial = [shell_first(x) for x in centre]
            radial_second = [None if q == S else shell_second(centre[q]) for q in range(QUANTITIES)]
            emf_centre = [[near_emf(i * SHELLS + r, 0) for r in range(SHELLS)] for i in range(3)]
            emf_radial = [None, shell_first(emf_centre[1]), shell_first(emf_centre[2])]
            for r in range(SHELLS):
                own = [centre[q][r] for q in range(QUANTITIES)]
                g, lap = [], []
                for q in range(QUANTITIES):
                    f = q * SHELLS + r
                    at = {d: near(f, d) for d in (-3, -2, -1, 1, 2, 3)}
                    g.append((radial[q][r], lane_first(f), scale * row_first(at)))
                    if q == S:
                        lap.append(None)
                    else:
                        lap.append(
                            radial_second[q][r] + lane_second(f) + (scale * scale) * row_second(at, own[q])
                        )
                m, b = own[MR:BR], own[BR:WARM]

                def advect(q):
                    return m[0] * g[q][0] + m[1] * g[q][1] + m[2] * g[q][2]

                div = g[MR][0] + g[MT][1] + g[MP][2]
                current = (g[BP][1] - g[BT][2], g[BR][2] - g[BP][0], g[BT][0] - g[BR][1])
                lorentz = (
                    current[1] * b[2] - current[2] * b[1],
                    current[2] * b[0] - current[0] * b[2],
                    current[0] * b[1] - current[1] * b[0],
                )
                grow, thin = jnp.exp(own[WARM]), jnp.exp(-own[S])
                emf_rows = {}
                for i in (0, 1):
                    f = i * SHELLS + r
                    emf_rows[i] = scale * row_first({d: near_emf(f, d) for d in (-3, -2, -1, 1, 2, 3)})
                turn = (
                    lane_first(FLAT + SHELLS + r) - emf_rows[1],
                    emf_rows[0] - emf_radial[2][r],
                    emf_radial[1][r] - lane_first(FLAT + r),
                )
                result = [-advect(S) - div]
                for i in range(3):
                    result.append(
                        -advect(MR + i) - grow * (g[S][i] + g[WARM][i]) + thin * lorentz[i] + SPREAD * lap[MR + i]
                    )
                for i in range(3):
                    result.append(turn[i] + SPREAD * lap[BR + i])
                result.append(-advect(WARM) - (2.0 / 3.0) * div + SPREAD * lap[WARM])
                for q in range(QUANTITIES):
                    rate[pl.ds((q * SHELLS + r) * LON + here, 8), :] = result[q]
            return carry

        lax.fori_loop(start, stop, body, 0)

    def rows_of(part):
        for h in range(HALO):
            row_out[part, 0, h] = frame[part, pl.ds(8 + h, FLAT, stride=STRIDE), :]
            row_out[part, 1, h] = frame[part, pl.ds(8 + LON - HALO + h, FLAT, stride=STRIDE), :]

    def prepare_picks():
        for lane_tile in range(12):
            if lane_tile < GROUPS:
                slot = idx_in[lane_tile, 0:1, :]
            elif lane_tile == GROUPS:
                slot = idx_in[0, 1:2, :]
                for q in range(1, GROUPS):
                    slot = jnp.maximum(slot, pltpu.roll(idx_in[q], SPARE * q, 1)[1:2, :])
            else:
                slot = idx_in[edge_group, lane_tile - 7 : lane_tile - 6, :]
            slot = slot - mine * (GROUP * OUT)
            who = jnp.zeros_like(slot)
            for q in range(1, GROUP):
                who = who + jnp.where(slot >= q * OUT, 1, 0)
            cell = slot - who * OUT
            who = jnp.where(jnp.logical_and(slot >= 0, slot < GROUP * OUT), who, -1)
            at = (lane_tile % 2) * COL
            owner[lane_tile // 2, :, at : at + COL] = jnp.broadcast_to(who, (8, COL))
            hot = jnp.where(iota((SLOTS, COL), 0) == cell, 1.0, 0.0).astype(BF16)
            for copy in range(2):
                onehot[lane_tile // 2, copy * SLOTS : (copy + 1) * SLOTS, at : at + COL] = hot

    def table_split(part):
        high, low = split(table[part].reshape(GROUP * FLAT, SLOTS))
        return jnp.concatenate([high, low], axis=1)

    def pick(both, tile):
        value = dot(both, onehot[tile])
        who = jnp.broadcast_to(owner[tile, 0:1, :], (FLAT, SLOTS))
        total = jnp.zeros((FLAT, SLOTS), F32)
        for q in range(GROUP):
            total = total + jnp.where(who == q, value[q * FLAT : (q + 1) * FLAT, :], 0.0)
        return total[:, 0:COL], total[:, COL : 2 * COL]

    def pick_sides(part, both, last):
        def body(tile, carry):
            first, second = pick(both, tile)
            picked[part, 2 * tile, 0:FLAT, :] = first
            picked[part, 2 * tile + 1, 0:FLAT, :] = second
            return carry

        lax.fori_loop(0, GROUPS // 2, body, 0)
        spot = lax.div(iota((8, COL), 1), SPARE)
        for there in range(GROUPS):
            total = jnp.zeros((8, COL), F32)
            for q in range(FLAT // 8):
                turn = (q - there) % GROUPS
                rows = last[8 * q : 8 * q + 8, :]
                total = jnp.where(spot == q, rows if turn == 0 else pltpu.roll(rows, SPARE * turn, 1), total)
            picked[part, there, FLAT : FLAT + 8, :] = total

    def corrections(part, halo_ref, own_ref, along_lanes):
        factor = None if along_lanes else scale

        def scaled(value, power):
            for _ in range(0 if along_lanes else power):
                value = factor * value
            return value

        for side in range(2):
            halo = [
                [halo_ref[side, h, q * SHELLS : (q + 1) * SHELLS, :] for q in range(QUANTITIES)] for h in range(HALO)
            ]
            form = cross_azimuthal if along_lanes else cross_polar
            halo_emf = [(cross_radial(x[MR:BR], x[BR:WARM]), form(x[MR:BR], x[BR:WARM])) for x in halo]
            sign = -1.0 if side == 0 else 1.0
            firsts, seconds = (45.0 * sign, -9.0 * sign, sign), (270.0, -27.0, 2.0)
            for j in range(HALO):
                own = [own_ref[part, side, j, q * SHELLS : (q + 1) * SHELLS, :] for q in range(QUANTITIES)]

                def total(weights, of):
                    result = None
                    for m in (1, 2, 3):
                        h = j + 3 - m if side == 0 else m - 3 + j
                        if 0 <= h < HALO:
                            term = weights[m - 1] * of(h)
                            result = term if result is None else result + term
                    return result

                d = [scaled(total(firsts, lambda h, q=q: halo[h][q]), 1) for q in range(QUANTITIES)]
                lap = [
                    None if q == S else scaled(total(seconds, lambda h, q=q: halo[h][q]), 2)
                    for q in range(QUANTITIES)
                ]
                radial = scaled(total(firsts, lambda h: halo_emf[h][0]), 1)
                second = scaled(total(firsts, lambda h: halo_emf[h][1]), 1)
                result = edge_rates(own, d, lap, second, radial, along_lanes)
                for q in range(QUANTITIES):
                    edge_add[side, j, q * SHELLS : (q + 1) * SHELLS, :] = result[q]

    def row_corrections(part):
        corrections(part, row_halo, row_out, False)
        for side in range(2):
            for j in range(HALO):
                rows = pl.ds(j if side == 0 else LON - HALO + j, FLAT, stride=LON)
                rate[rows, :] = rate[rows, :] + edge_add[side, j]

    def col_corrections(part):
        corrections(part, col_halo, col_own, True)
        for side in range(2):
            for j in range(HALO):
                for half in range(2):
                    turned[half, pl.ds((1 - side) * HALO + j, FLAT // 2, stride=8), :] = edge_add[
                        side, j, half * (FLAT // 2) : (half + 1) * (FLAT // 2), :
                    ]

    def finish(part):
        lane = iota((LON, COL), 1)
        border = jnp.logical_or(lane < HALO, lane >= COL - HALO)
        for half in range(2):
            edge = jnp.transpose(turned[half])[0:LON, :]
            for g in range(FLAT // 2):
                f = half * (FLAT // 2) + g
                added = jnp.where(border, pltpu.roll(edge, COL - 8 * g - HALO, 1), 0.0)
                change = (TIME_STEP / 60.0) * (rate[f * LON : (f + 1) * LON, :] + added)
                start = x_ref[f * LON : (f + 1) * LON, :]
                rows = slice(f * STRIDE + 8, f * STRIDE + 8 + LON)
                if part == 0:
                    frame[1, rows, :] = start + change
                else:
                    out_ref[f * LON : (f + 1) * LON, :] = 0.5 * (start + frame[1, rows, :] + change)

    def a_copy(part, step):
        block = table.at[part, member]
        return remote(block, block, a_send.at[part, step], a_recv.at[part, member], row_device(step))

    def a_arrival(part, step):
        block = table.at[part, row_member(step)]
        return remote(block, block, a_send.at[part, step], a_recv.at[part, row_member(step)], row_device(step))

    def f_copy(part, step):
        block = table.at[part, row_member(step)]
        return remote(block, block, f_send.at[part, step], a_recv.at[part, row_member(step)], sibling)

    def f_arrival(part, q):
        there = (1 - core) * n_col + q
        block = table.at[part, there]
        return remote(block, block, f_send.at[part, q], a_recv.at[part, there], sibling)

    def b_copy(part, step):
        device, there = cross_device(step)
        return remote(
            picked.at[part, there], got_cols.at[part, mine], b_send.at[part, step], b_recv.at[part, mine], device
        )

    def b_arrival(part, group):
        return remote(
            picked.at[part, 0], got_cols.at[part, group], b_send.at[part, 0], b_recv.at[part, group],
            (other, lon, col),
        )

    def l_copy(part):
        return remote(
            picked_rows.at[part], got_rows.at[part, mine], l_send.at[part], l_recv.at[part, mine],
            (other, 2 * edge_group + core, col),
        )

    def l_arrival(part, group):
        return remote(
            picked_rows.at[part], got_rows.at[part, group], l_send.at[part], l_recv.at[part, group],
            (other, lon, col),
        )

    def row_copy(part, side):
        return remote(
            row_out.at[part, 1 - side], row_in.at[part, side], r_send.at[part, side], r_recv.at[part, side],
            (panel, lon_up if side == 0 else lon_down, col),
        )

    def col_copy(part, side):
        return remote(
            col_out.at[part, 1 - side], col_in.at[part, side], c_send.at[part, side], c_recv.at[part, side],
            (panel, lon, col_up if side == 0 else col_down),
        )

    def idx_copy(step):
        device, _ = cross_device(step)
        return remote(idx_out, idx_in.at[mine], idx_send.at[step], idx_recv.at[mine], device)

    def idx_arrival(group):
        return remote(idx_out, idx_in.at[group], idx_send.at[0], idx_recv.at[group], (other, lon, col))

    interpolate(0)
    pl.semaphore_wait(barrier, len(AROUND) + 2 + GROUPS)

    for part in range(2):
        if part == 1:
            interpolate(1)
        for step in AROUND:
            a_copy(part, step).start()
        f_copy(part, 0).start()
        if part == 0:
            for step in range(GROUPS):
                idx_copy(step).start()
        rows_of(part)
        for side in range(2):
            row_copy(part, side).start()
        cols_of(part)
        for side in range(2):
            col_copy(part, side).start()
        lane_pass(part)
        emf_pass(part)
        if part == 0:
            for group in range(GROUPS):
                idx_arrival(group).wait_recv()
            prepare_picks()
        main_pass(part, 0, 1)
        for step in AROUND:
            a_arrival(part, step).wait_recv()
            f_copy(part, step).start()
        main_pass(part, 1, 2)
        for q in range(GROUP // 2):
            f_arrival(part, q).wait_recv()
        both = table_split(part)
        last, picked_rows[part, 0] = pick(both, 4)
        picked_rows[part, 1], picked_rows[part, 2] = pick(both, 5)
        l_copy(part).start()

        @pl.when(col_edge)
        def _():
            pick_sides(part, both, last)
            for step in range(GROUPS):
                b_copy(part, step).start()

        main_pass(part, 2, 6)
        for side in range(2):
            row_copy(part, side).wait_recv()
            col_copy(part, side).wait_recv()

        for side in range(2):
            at_edge = lon == (0 if side == 0 else n_lon - 1)

            @pl.when(at_edge)
            def _():
                for group in range(GROUPS):
                    l_arrival(part, group).wait_recv()
                total = got_rows[part, 0]
                for group in range(1, GROUPS):
                    total = total + got_rows[part, group]
                row_halo[side] = total

            @pl.when(jnp.logical_not(at_edge))
            def _():
                row_halo[side] = row_in[part, side]

        row_corrections(part)

        for side in range(2):
            at_edge = col == (0 if side == 0 else n_col - 1)

            @pl.when(at_edge)
            def _():
                for group in range(GROUPS):
                    b_arrival(part, group).wait_recv()
                total = got_cols[part, 0]
                for group in range(1, GROUPS):
                    total = total + got_cols[part, group]
                main, rest = total[0:FLAT], total[FLAT : FLAT + 8]
                col_halo[side, 0] = main
                col_halo[side, 1] = pltpu.roll(main, COL - LON, 1)
                main = pltpu.roll(main, COL - 2 * LON, 1)
                for q in range(FLAT // 8):
                    col_halo[side, 2, 8 * q : 8 * q + 8, :] = jnp.where(
                        iota((8, COL), 1) < COL - 2 * LON,
                        main[8 * q : 8 * q + 8, :],
                        pltpu.roll(rest, (COL + COL - 2 * LON - SPARE * q) % COL, 1),
                    )

            @pl.when(jnp.logical_not(at_edge))
            def _():
                pair = col_in[part, side, 0]
                col_halo[side, 0] = pair
                col_halo[side, 1] = pltpu.roll(pair, COL // 2, 1)
                col_halo[side, 2] = col_in[part, side, 1]

        col_corrections(part)
        finish(part)

    for step in range(GROUPS):
        idx_copy(step).wait_send()
    for part in range(2):
        for step in AROUND:
            a_copy(part, step).wait_send()
        for step in range(GROUP // 2):
            f_copy(part, step).wait_send()
        for side in range(2):
            row_copy(part, side).wait_send()
            col_copy(part, side).wait_send()
        l_copy(part).wait_send()

        @pl.when(col_edge)
        def _():
            for step in range(GROUPS):
                b_copy(part, step).wait_send()


def inverse_sine(start, count, total):
    place = (start + jnp.arange(count, dtype=jnp.int32)).astype(jnp.float32)
    colatitude = math.pi / 4.0 + (place + 0.5) * (math.pi / 2.0 / total)
    return 1.0 / jnp.sin(colatitude)


def shards(state, send_base, send_frac, recv_slots):
    rows = FLAT * LON
    scale = inverse_sine(lax.axis_index("colat") * COL, COL, COL * lax.axis_size("colat"))[None]
    base = jnp.pad(send_base[0], ((0, 0), (0, SLOTS - OUT)))
    frac = jnp.pad(send_frac[0, 0], ((0, 0), (0, SLOTS - OUT)))
    dma = pltpu.SemaphoreType.DMA
    vmem = pltpu.VMEM
    scratch = [
        vmem((2, FLAT * STRIDE, COL), F32),
        vmem((3 * SHELLS * STRIDE, COL), F32),
        vmem(((FLAT + 2 * SHELLS) * LON, 2 * COL), F32),
        vmem((rows, COL), F32),
        vmem((3 * COL, SLOTS), BF16),
        vmem((LON, SLOTS), F32),
        vmem((2 * COL, 2 * COL), BF16),
        vmem((6, 2 * SLOTS, 2 * COL), BF16),
        vmem((6, 8, 2 * COL), I32),
        vmem((2, COL, COL), F32),
        vmem((2, GROUP, FLAT, SLOTS), F32),
        vmem((8, COL), I32),
        vmem((GROUPS, 8, COL), I32),
        vmem((2, GROUPS, FLAT + 8, COL), F32),
        vmem((2, HALO, FLAT, COL), F32),
        vmem((2, GROUPS, FLAT + 8, COL), F32),
        vmem((2, GROUPS, HALO, FLAT, COL), F32),
        vmem((2, 2, HALO, FLAT, COL), F32),
        vmem((2, 2, HALO, FLAT, COL), F32),
        vmem((2, 2, HALO, FLAT, COL), F32),
        vmem((2, 2, 2, FLAT, COL), F32),
        vmem((2, 2, 2, FLAT, COL), F32),
        vmem((2, HALO, FLAT, COL), F32),
        vmem((2, HALO, FLAT, COL), F32),
        vmem((2, HALO, FLAT, COL), F32),
        dma((GROUPS,)),
        dma((GROUPS,)),
        dma((2, GROUP // 2)),
        dma((2, GROUP)),
        dma((2, GROUP // 2)),
        dma((2, GROUPS)),
        dma((2, GROUPS)),
        dma((2,)),
        dma((2, GROUPS)),
        dma((2, 2)),
        dma((2, 2)),
        dma((2, 2)),
        dma((2, 2)),
    ]
    result = pl.pallas_call(
        kernel,
        out_shape=jax.ShapeDtypeStruct((rows, COL), F32),
        in_specs=[pl.BlockSpec(memory_space=pltpu.VMEM)] * 5,
        out_specs=pl.BlockSpec(memory_space=pltpu.VMEM),
        scratch_shapes=scratch,
        compiler_params=pltpu.CompilerParams(
            collective_id=0, has_side_effects=True, vmem_limit_bytes=40 * 1024 * 1024
        ),
    )(state.reshape(rows, COL), base, frac, recv_slots[0], scale)
    return result.reshape(state.shape)


def solution(mesh):
    placed = (
        P("panel", None, None, "lon", "colat"),
        P("panel", ("lon", "colat"), None),
        P("panel", ("lon", "colat"), None, None),
        P("panel", ("lon", "colat"), None),
    )
    return jax.shard_map(
        shards,
        mesh=mesh,
        in_specs=placed,
        out_specs=P("panel", None, None, "lon", "colat"),
        check_vma=False,
    )
```

```python
import math

import jax
import jax.numpy as jnp
from jax import lax
from jax.experimental import pallas as pl
from jax.experimental.pallas import tpu as pltpu
from jax.sharding import PartitionSpec as P

MESH = pl.DeviceIdType.MESH
F32, BF16, I32 = jnp.float32, jnp.bfloat16, jnp.int32

QUANTITIES = 8
SHELLS = 4
FLAT = QUANTITIES * SHELLS
LON = 48
COL = 128
HALO = 3
OUT = 240
SIDE = HALO * LON
SLOTS = 256
GROUP = 8
GROUPS = 8
AROUND = (1, 3, 2)
SPARE = SIDE - COL
RING = 4
STRIDE = LON + 16
TIME_STEP = 0.25
SPREAD = 0.1 / 3.0
S, MR, MT, MP, BR, BT, BP, WARM = range(QUANTITIES)


def dot(left, right):
    return jnp.dot(left, right, preferred_element_type=F32)


def split(value):
    high = value.astype(BF16)
    return high, (value - high.astype(F32)).astype(BF16)


def iota(shape, dim):
    return lax.broadcasted_iota(I32, shape, dim)


def cross_radial(m, b):
    return m[1] * b[2] - m[2] * b[1]


def cross_polar(m, b):
    return m[2] * b[0] - m[0] * b[2]


def cross_azimuthal(m, b):
    return m[0] * b[1] - m[1] * b[0]


def edge_rates(own, d, lap, emf_first, emf_second, along_lanes):
    grow, thin = jnp.exp(own[WARM]), jnp.exp(-own[S])
    b = own[BR:WARM]
    if along_lanes:
        vel, out = own[MT], MT
        lorentz = (d[BR] * b[1], -d[BR] * b[0] - d[BP] * b[2], d[BP] * b[1])
        turn = (emf_first, None, -emf_second)
    else:
        vel, out = own[MP], MP
        lorentz = (d[BR] * b[2], d[BT] * b[2], -d[BT] * b[1] - d[BR] * b[0])
        turn = (-emf_first, emf_second, None)
    result = [-vel * d[S] - d[out]]
    for i in range(3):
        rate = -vel * d[MR + i] + thin * lorentz[i] + SPREAD * lap[MR + i]
        if MR + i == out:
            rate = rate - grow * (d[S] + d[WARM])
        result.append(rate)
    for i in range(3):
        rate = SPREAD * lap[BR + i]
        result.append(rate if turn[i] is None else rate + turn[i])
    result.append(-vel * d[WARM] - (2.0 / 3.0) * d[out] + SPREAD * lap[WARM])
    return result


def shell_first(x):
    a, b = 8.0 * (x[3] - x[0]), 45.0
    return (
        b * (x[1] - x[0]) - 9.0 * (x[2] - x[0]) + (x[3] - x[0]),
        b * (x[2] - x[0]) - a,
        b * (x[3] - x[1]) - a,
        b * (x[3] - x[2]) - 9.0 * (x[3] - x[1]) + (x[3] - x[0]),
    )


def shell_second(x):
    return (
        2.0 * x[3] - 27.0 * x[2] + 270.0 * x[1] - 245.0 * x[0],
        245.0 * x[0] - 490.0 * x[1] + 270.0 * x[2] - 25.0 * x[3],
        245.0 * x[3] - 490.0 * x[2] + 270.0 * x[1] - 25.0 * x[0],
        2.0 * x[0] - 27.0 * x[1] + 270.0 * x[2] - 245.0 * x[3],
    )


def kernel(
    x_ref, base_ref, frac_ref, slots_ref, scale_ref, out_ref,
    frame, emf, lanes, rate, mix, rows_mix, band, onehot, owner, turned,
    table, idx_out, idx_in, picked, picked_rows, ring_rows, sum_rows, got_cols, got_rows, row_out, row_in, col_own, col_out, col_in,
    row_halo, col_halo, edge_add,
    idx_send, idx_recv, a_send, a_recv, f_send, b_send, b_recv, z_send, z_recv, l_send, l_recv, r_send, r_recv, c_send, c_recv,
):
    panel, lon, col = lax.axis_index("panel"), lax.axis_index("lon"), lax.axis_index("colat")
    n_lon, n_col = lax.axis_size("lon"), lax.axis_size("colat")
    core, mine = lax.rem(lon, 2), lax.div(lon, 2)
    member = core * n_col + col
    other = 1 - panel
    lon_up, lon_down = lax.rem(lon + 1, n_lon), lax.rem(lon + n_lon - 1, n_lon)
    col_up, col_down = lax.rem(col + 1, n_col), lax.rem(col + n_col - 1, n_col)
    outer = lax.rem(lon + 2 * core - 1 + n_lon, n_lon)
    col_edge = jnp.logical_or(col == 0, col == n_col - 1)
    lon_edge = jnp.logical_or(lon == 0, lon == n_lon - 1)
    edge_group = core * (GROUPS - 1)

    sibling = (panel, lon + 1 - 2 * core, col)

    ring_base, ring_place = RING * lax.div(mine, RING), lax.rem(mine, RING)

    def ring_device(step):
        there = lax.rem(ring_place + step, RING)
        return (panel, 2 * (ring_base + there) + core, col), there

    def row_member(step):
        return core * n_col + lax.rem(col + step, n_col)

    def row_device(step):
        return (panel, lon, lax.rem(col + step, n_col))

    def cross_device(step):
        there = lax.rem(mine + step, GROUPS)
        return (other, 2 * there + core, col), there

    def remote(src, dst, send, recv, device):
        return pltpu.make_async_remote_copy(
            src_ref=src, dst_ref=dst, send_sem=send, recv_sem=recv, device_id=device, device_id_type=MESH
        )

    barrier = pltpu.get_barrier_semaphore()
    for step in AROUND:
        pl.semaphore_signal(barrier, inc=1, device_id=row_device(step), device_id_type=MESH)
        pl.semaphore_signal(barrier, inc=1, device_id=ring_device(step)[0], device_id_type=MESH)
    pl.semaphore_signal(barrier, inc=1, device_id=sibling, device_id_type=MESH)
    for step in range(GROUPS):
        pl.semaphore_signal(barrier, inc=1, device_id=cross_device(step)[0], device_id_type=MESH)
    pl.semaphore_signal(barrier, inc=1, device_id=(panel, outer, col), device_id_type=MESH)

    zero_rows = jnp.zeros((8, COL), F32)
    for f in range(FLAT):
        for part in range(2):
            frame[part, f * STRIDE : f * STRIDE + 8, :] = zero_rows
            frame[part, f * STRIDE + 8 + LON : (f + 1) * STRIDE, :] = zero_rows
        frame[0, f * STRIDE + 8 : f * STRIDE + 8 + LON, :] = x_ref[f * LON : (f + 1) * LON, :]
    for f in range(3 * SHELLS):
        emf[f * STRIDE : f * STRIDE + 8, :] = zero_rows
        emf[f * STRIDE + 8 + LON : (f + 1) * STRIDE, :] = zero_rows

    base = base_ref[...]
    base_row, base_col = lax.div(base, COL), lax.rem(base, COL)
    along, across = frac_ref[0:1, :], frac_ref[1:2, :]
    cells = iota((COL, SLOTS), 0)
    weight = jnp.where(cells == base_col, 1.0 - across, 0.0) + jnp.where(cells == base_col + 1, across, 0.0)
    weight_high, weight_low = split(weight)
    mix[0:COL, :] = weight_high
    mix[COL : 2 * COL, :] = weight_high
    mix[2 * COL : 3 * COL, :] = weight_low
    cells = iota((LON, SLOTS), 0)
    rows_mix[...] = jnp.where(cells == base_row, 1.0 - along, 0.0) + jnp.where(cells == base_row + 1, along, 0.0)

    for half in range(2):
        turned[half, :, :] = jnp.zeros((COL, COL), F32)

    apart = iota((COL, COL), 0) - iota((COL, COL), 1)
    reach = jnp.abs(apart)
    first = jnp.where(reach == 1, 45.0, jnp.where(reach == 2, -9.0, jnp.where(reach == 3, 1.0, 0.0)))
    first = jnp.where(apart < 0, -first, first).astype(BF16)
    second = jnp.where(
        reach == 0, -490.0, jnp.where(reach == 1, 270.0, jnp.where(reach == 2, -27.0, jnp.where(reach == 3, 2.0, 0.0)))
    ).astype(BF16)
    for part in range(2):
        band[part * COL : (part + 1) * COL, 0:COL] = first
        band[part * COL : (part + 1) * COL, COL : 2 * COL] = second

    spot = iota((1, SLOTS), 1)
    sides = jnp.where(spot < SIDE, jnp.maximum(slots_ref[:, 0:SLOTS], slots_ref[:, SIDE : SIDE + SLOTS]) + 1, 0)
    digits = jnp.concatenate([lax.div(sides, COL), lax.rem(sides, COL), jnp.zeros((6, SLOTS), I32)], axis=0)
    source, target = iota((SLOTS, SLOTS), 0), iota((SLOTS, SLOTS), 1)
    layer = jnp.where(target >= LON, 1, 0) + jnp.where(target >= 2 * LON, 1, 0)
    order = jnp.logical_and(target < SIDE, source == HALO * (target - LON * layer) + layer)
    digits = dot(digits.astype(F32).astype(BF16), jnp.where(order, 1.0, 0.0).astype(BF16)).astype(I32)
    sides = digits[0:1, :] * COL + digits[1:2, :] - 1
    idx_out[0:1, :] = sides[:, 0:COL]
    idx_out[1:2, :] = sides[:, COL : 2 * COL]
    for h in range(HALO):
        at = 2 * SIDE + h * COL
        idx_out[2 + h : 3 + h, :] = jnp.maximum(
            slots_ref[:, at : at + COL], slots_ref[:, at + HALO * COL : at + HALO * COL + COL]
        )
    idx_out[5:8, :] = jnp.full((3, COL), -1, I32)

    scale = scale_ref[...]

    def load_split(part, pair):
        block = jnp.concatenate(
            [frame[part, pl.ds(pl.multiple_of((8 * pair + q) * STRIDE, 8) + 8, LON), :] for q in range(8)], axis=0
        )
        return split(block)

    def interpolate(part):
        def body(pair, carry):
            high, low = load_split(part, pair)
            value = dot(jnp.concatenate([high, low, high], axis=1), mix[...])
            value = jnp.sum(value.reshape(8, LON, SLOTS) * rows_mix[...][None], axis=1)
            table[part, member, pl.ds(pl.multiple_of(8 * pair, 8), 8), :] = value
            return carry

        lax.fori_loop(0, FLAT // 8, body, 0)

    def lane_pass(part):
        def body(pair, carry):
            high, low = load_split(part, pair)
            both = jnp.concatenate([high, low], axis=1)
            lanes[pl.ds(pl.multiple_of(8 * LON * pair, 8), 8 * LON), :] = dot(both, band[...])
            return carry

        lax.fori_loop(0, FLAT // 8, body, 0)

    def cols_of(part):
        lane = iota((LON, COL), 1)
        for half in range(2):
            edge = jnp.zeros((LON, COL), F32)
            for g in range(FLAT // 2):
                at = (half * (FLAT // 2) + g) * STRIDE + 8
                moved = pltpu.roll(frame[part, at : at + LON, :], 8 * g + HALO, 1)
                edge = jnp.where(jnp.logical_and(lane >= 8 * g, lane < 8 * g + 2 * HALO), moved, edge)
            turned[half, :, 0:LON] = jnp.transpose(edge)
        for side in range(2):
            for j in range(HALO):
                first = (1 - side) * HALO + j
                for half in range(2):
                    col_own[part, side, j, half * (FLAT // 2) : (half + 1) * (FLAT // 2), :] = turned[
                        half, pl.ds(first, FLAT // 2, stride=8), :
                    ]
            col_out[part, side, 0] = jnp.where(
                iota((FLAT, COL), 1) < COL // 2, col_own[part, side, 0], pltpu.roll(col_own[part, side, 1], COL // 2, 1)
            )
            col_out[part, side, 1] = col_own[part, side, 2]

    def emf_pass(part):
        for r in range(SHELLS):
            def field(q):
                at = (q * SHELLS + r) * STRIDE + 8
                return frame[part, at : at + LON, :]

            m, b = [field(MR + i) for i in range(3)], [field(BR + i) for i in range(3)]
            for i, form in enumerate((cross_radial, cross_polar, cross_azimuthal)):
                at = (i * SHELLS + r) * STRIDE + 8
                emf[at : at + LON, :] = form(m, b)
        for i, at in ((0, FLAT), (2, FLAT + SHELLS)):
            block = jnp.concatenate(
                [emf[(i * SHELLS + r) * STRIDE + 8 : (i * SHELLS + r) * STRIDE + 8 + LON, :] for r in range(SHELLS)],
                axis=0,
            )
            high, low = split(block)
            lanes[at * LON : (at + SHELLS) * LON, 0:COL] = dot(
                jnp.concatenate([high, low], axis=1), band[:, 0:COL]
            )

    def main_pass(part, start, stop):
        def body(block, carry):
            here = pl.multiple_of(8 * block, 8)

            def near(f, apart):
                return frame[part, pl.ds(f * STRIDE + 8 + here + apart, 8), :]

            def near_emf(f, apart):
                return emf[pl.ds(f * STRIDE + 8 + here + apart, 8), :]

            def lane_first(f):
                return lanes[pl.ds(f * LON + here, 8), 0:COL]

            def lane_second(f):
                return lanes[pl.ds(f * LON + here, 8), COL : 2 * COL]

            def row_first(at):
                return 45.0 * (at[1] - at[-1]) - 9.0 * (at[2] - at[-2]) + (at[3] - at[-3])

            def row_second(at, centre):
                return (
                    270.0 * (at[1] + at[-1]) - 27.0 * (at[2] + at[-2]) + 2.0 * (at[3] + at[-3]) - 490.0 * centre
                )

            centre = [[near(q * SHELLS + r, 0) for r in range(SHELLS)] for q in range(QUANTITIES)]
            radial = [shell_first(x) for x in centre]
            radial_second = [None if q == S else shell_second(centre[q]) for q in range(QUANTITIES)]
            emf_centre = [[near_emf(i * SHELLS + r, 0) for r in range(SHELLS)] for i in range(3)]
            emf_radial = [None, shell_first(emf_centre[1]), shell_first(emf_centre[2])]
            for r in range(SHELLS):
                own = [centre[q][r] for q in range(QUANTITIES)]
                g, lap = [], []
                for q in range(QUANTITIES):
                    f = q * SHELLS + r
                    at = {d: near(f, d) for d in (-3, -2, -1, 1, 2, 3)}
                    g.append((radial[q][r], lane_first(f), scale * row_first(at)))
                    if q == S:
                        lap.append(None)
                    else:
                        lap.append(
                            radial_second[q][r] + lane_second(f) + (scale * scale) * row_second(at, own[q])
                        )
                m, b = own[MR:BR], own[BR:WARM]

                def advect(q):
                    return m[0] * g[q][0] + m[1] * g[q][1] + m[2] * g[q][2]

                div = g[MR][0] + g[MT][1] + g[MP][2]
                current = (g[BP][1] - g[BT][2], g[BR][2] - g[BP][0], g[BT][0] - g[BR][1])
                lorentz = (
                    current[1] * b[2] - current[2] * b[1],
                    current[2] * b[0] - current[0] * b[2],
                    current[0] * b[1] - current[1] * b[0],
                )
                grow, thin = jnp.exp(own[WARM]), jnp.exp(-own[S])
                emf_rows = {}
                for i in (0, 1):
                    f = i * SHELLS + r
                    emf_rows[i] = scale * row_first({d: near_emf(f, d) for d in (-3, -2, -1, 1, 2, 3)})
                turn = (
                    lane_first(FLAT + SHELLS + r) - emf_rows[1],
                    emf_rows[0] - emf_radial[2][r],
                    emf_radial[1][r] - lane_first(FLAT + r),
                )
                result = [-advect(S) - div]
                for i in range(3):
                    result.append(
                        -advect(MR + i) - grow * (g[S][i] + g[WARM][i]) + thin * lorentz[i] + SPREAD * lap[MR + i]
                    )
                for i in range(3):
                    result.append(turn[i] + SPREAD * lap[BR + i])
                result.append(-advect(WARM) - (2.0 / 3.0) * div + SPREAD * lap[WARM])
                for q in range(QUANTITIES):
                    rate[pl.ds((q * SHELLS + r) * LON + here, 8), :] = result[q]
            return carry

        lax.fori_loop(start, stop, body, 0)

    def rows_of(part):
        for h in range(HALO):
            row_out[part, 0, h] = frame[part, pl.ds(8 + h, FLAT, stride=STRIDE), :]
            row_out[part, 1, h] = frame[part, pl.ds(8 + LON - HALO + h, FLAT, stride=STRIDE), :]

    def prepare_picks():
        for lane_tile in range(12):
            if lane_tile < GROUPS:
                slot = idx_in[lane_tile, 0:1, :]
            elif lane_tile == GROUPS:
                slot = idx_in[0, 1:2, :]
                for q in range(1, GROUPS):
                    slot = jnp.maximum(slot, pltpu.roll(idx_in[q], SPARE * q, 1)[1:2, :])
            else:
                slot = idx_in[edge_group, lane_tile - 7 : lane_tile - 6, :]
            slot = slot - mine * (GROUP * OUT)
            who = jnp.zeros_like(slot)
            for q in range(1, GROUP):
                who = who + jnp.where(slot >= q * OUT, 1, 0)
            cell = slot - who * OUT
            who = jnp.where(jnp.logical_and(slot >= 0, slot < GROUP * OUT), who, -1)
            at = (lane_tile % 2) * COL
            owner[lane_tile // 2, :, at : at + COL] = jnp.broadcast_to(who, (8, COL))
            hot = jnp.where(iota((SLOTS, COL), 0) == cell, 1.0, 0.0).astype(BF16)
            for copy in range(2):
                onehot[lane_tile // 2, copy * SLOTS : (copy + 1) * SLOTS, at : at + COL] = hot

    def table_split(part):
        high, low = split(table[part].reshape(GROUP * FLAT, SLOTS))
        return jnp.concatenate([high, low], axis=1)

    def pick(both, tile):
        value = dot(both, onehot[tile])
        who = jnp.broadcast_to(owner[tile, 0:1, :], (FLAT, SLOTS))
        total = jnp.zeros((FLAT, SLOTS), F32)
        for q in range(GROUP):
            total = total + jnp.where(who == q, value[q * FLAT : (q + 1) * FLAT, :], 0.0)
        return total[:, 0:COL], total[:, COL : 2 * COL]

    def pick_sides(part, both, last):
        def body(tile, carry):
            first, second = pick(both, tile)
            picked[part, 2 * tile, 0:FLAT, :] = first
            picked[part, 2 * tile + 1, 0:FLAT, :] = second
            return carry

        lax.fori_loop(0, GROUPS // 2, body, 0)
        spot = lax.div(iota((8, COL), 1), SPARE)
        for there in range(GROUPS):
            total = jnp.zeros((8, COL), F32)
            for q in range(FLAT // 8):
                turn = (q - there) % GROUPS
                rows = last[8 * q : 8 * q + 8, :]
                total = jnp.where(spot == q, rows if turn == 0 else pltpu.roll(rows, SPARE * turn, 1), total)
            picked[part, there, FLAT : FLAT + 8, :] = total

    def corrections(part, halo_ref, own_ref, along_lanes):
        factor = None if along_lanes else scale

        def scaled(value, power):
            for _ in range(0 if along_lanes else power):
                value = factor * value
            return value

        for side in range(2):
            halo = [
                [halo_ref[side, h, q * SHELLS : (q + 1) * SHELLS, :] for q in range(QUANTITIES)] for h in range(HALO)
            ]
            form = cross_azimuthal if along_lanes else cross_polar
            halo_emf = [(cross_radial(x[MR:BR], x[BR:WARM]), form(x[MR:BR], x[BR:WARM])) for x in halo]
            sign = -1.0 if side == 0 else 1.0
            firsts, seconds = (45.0 * sign, -9.0 * sign, sign), (270.0, -27.0, 2.0)
            for j in range(HALO):
                own = [own_ref[part, side, j, q * SHELLS : (q + 1) * SHELLS, :] for q in range(QUANTITIES)]

                def total(weights, of):
                    result = None
                    for m in (1, 2, 3):
                        h = j + 3 - m if side == 0 else m - 3 + j
                        if 0 <= h < HALO:
                            term = weights[m - 1] * of(h)
                            result = term if result is None else result + term
                    return result

                d = [scaled(total(firsts, lambda h, q=q: halo[h][q]), 1) for q in range(QUANTITIES)]
                lap = [
                    None if q == S else scaled(total(seconds, lambda h, q=q: halo[h][q]), 2)
                    for q in range(QUANTITIES)
                ]
                radial = scaled(total(firsts, lambda h: halo_emf[h][0]), 1)
                second = scaled(total(firsts, lambda h: halo_emf[h][1]), 1)
                result = edge_rates(own, d, lap, second, radial, along_lanes)
                for q in range(QUANTITIES):
                    edge_add[side, j, q * SHELLS : (q + 1) * SHELLS, :] = result[q]

    def row_corrections(part):
        corrections(part, row_halo, row_out, False)
        for side in range(2):
            for j in range(HALO):
                rows = pl.ds(j if side == 0 else LON - HALO + j, FLAT, stride=LON)
                rate[rows, :] = rate[rows, :] + edge_add[side, j]

    def col_corrections(part):
        corrections(part, col_halo, col_own, True)
        for side in range(2):
            for j in range(HALO):
                for half in range(2):
                    turned[half, pl.ds((1 - side) * HALO + j, FLAT // 2, stride=8), :] = edge_add[
                        side, j, half * (FLAT // 2) : (half + 1) * (FLAT // 2), :
                    ]

    def finish(part):
        lane = iota((LON, COL), 1)
        border = jnp.logical_or(lane < HALO, lane >= COL - HALO)
        for half in range(2):
            edge = jnp.transpose(turned[half])[0:LON, :]
            for g in range(FLAT // 2):
                f = half * (FLAT // 2) + g
                added = jnp.where(border, pltpu.roll(edge, COL - 8 * g - HALO, 1), 0.0)
                change = (TIME_STEP / 60.0) * (rate[f * LON : (f + 1) * LON, :] + added)
                start = x_ref[f * LON : (f + 1) * LON, :]
                rows = slice(f * STRIDE + 8, f * STRIDE + 8 + LON)
                if part == 0:
                    frame[1, rows, :] = start + change
                else:
                    out_ref[f * LON : (f + 1) * LON, :] = 0.5 * (start + frame[1, rows, :] + change)

    def a_copy(part, step):
        block = table.at[part, member]
        return remote(block, block, a_send.at[part, step], a_recv.at[part, member], row_device(step))

    def a_arrival(part, step):
        block = table.at[part, row_member(step)]
        return remote(block, block, a_send.at[part, step], a_recv.at[part, row_member(step)], row_device(step))

    def f_copy(part, step):
        block = table.at[part, row_member(step)]
        return remote(block, block, f_send.at[part, step], a_recv.at[part, row_member(step)], sibling)

    def f_arrival(part, q):
        there = (1 - core) * n_col + q
        block = table.at[part, there]
        return remote(block, block, f_send.at[part, q], a_recv.at[part, there], sibling)

    def b_copy(part, step):
        device, there = cross_device(step)
        return remote(
            picked.at[part, there], got_cols.at[part, mine], b_send.at[part, step], b_recv.at[part, mine], device
        )

    def b_arrival(part, group):
        return remote(
            picked.at[part, 0], got_cols.at[part, group], b_send.at[part, 0], b_recv.at[part, group],
            (other, lon, col),
        )

    def z_copy(part, step):
        device, there = ring_device(step)
        return remote(
            picked_rows.at[part, there], ring_rows.at[part, ring_place], z_send.at[part, step],
            z_recv.at[part, ring_place], device,
        )

    def z_arrival(part, step):
        device, there = ring_device(step)
        return remote(
            picked_rows.at[part, there], ring_rows.at[part, there], z_send.at[part, step], z_recv.at[part, there], device
        )

    def l_copy(part):
        return remote(
            sum_rows.at[part], got_rows.at[part, mine], l_send.at[part], l_recv.at[part, mine],
            (other, 2 * edge_group + core, col),
        )

    def l_arrival(part, group):
        return remote(
            sum_rows.at[part], got_rows.at[part, group], l_send.at[part], l_recv.at[part, group],
            (other, lon, col),
        )

    def row_copy(part, side):
        return remote(
            row_out.at[part, 1 - side], row_in.at[part, side], r_send.at[part, side], r_recv.at[part, side],
            (panel, lon_up if side == 0 else lon_down, col),
        )

    def col_copy(part, side):
        return remote(
            col_out.at[part, 1 - side], col_in.at[part, side], c_send.at[part, side], c_recv.at[part, side],
            (panel, lon, col_up if side == 0 else col_down),
        )

    def idx_copy(step):
        device, _ = cross_device(step)
        return remote(idx_out, idx_in.at[mine], idx_send.at[step], idx_recv.at[mine], device)

    def idx_arrival(group):
        return remote(idx_out, idx_in.at[group], idx_send.at[0], idx_recv.at[group], (other, lon, col))

    interpolate(0)
    pl.semaphore_wait(barrier, 2 * len(AROUND) + 2 + GROUPS)

    for part in range(2):
        if part == 1:
            interpolate(1)
        for step in AROUND:
            a_copy(part, step).start()
        f_copy(part, 0).start()
        if part == 0:
            for step in range(GROUPS):
                idx_copy(step).start()
        rows_of(part)
        for side in range(2):
            row_copy(part, side).start()
        cols_of(part)
        for side in range(2):
            col_copy(part, side).start()
        lane_pass(part)
        emf_pass(part)
        if part == 0:
            for group in range(GROUPS):
                idx_arrival(group).wait_recv()
            prepare_picks()
        main_pass(part, 0, 1)
        for step in AROUND:
            a_arrival(part, step).wait_recv()
            f_copy(part, step).start()
        main_pass(part, 1, 2)
        for q in range(GROUP // 2):
            f_arrival(part, q).wait_recv()
        both = table_split(part)
        last, *ends = pick(both, 4) + pick(both, 5)
        for h in range(HALO):
            for q in range(RING):
                picked_rows[part, q, h] = ends[h][8 * q : 8 * q + 8, :]
        for step in AROUND:
            z_copy(part, step).start()

        @pl.when(col_edge)
        def _():
            pick_sides(part, both, last)
            for step in range(GROUPS):
                b_copy(part, step).start()

        main_pass(part, 2, 5)
        total = picked_rows[part, ring_place]
        for step in AROUND:
            z_arrival(part, step).wait_recv()
            total = total + ring_rows[part, ring_device(step)[1]]
        sum_rows[part] = total
        l_copy(part).start()
        main_pass(part, 5, 6)
        for side in range(2):
            row_copy(part, side).wait_recv()
            col_copy(part, side).wait_recv()

        for side in range(2):
            at_edge = lon == (0 if side == 0 else n_lon - 1)

            @pl.when(at_edge)
            def _():
                for group in range(GROUPS):
                    l_arrival(part, group).wait_recv()
                for q in range(RING):
                    total = got_rows[part, q] + got_rows[part, RING + q]
                    for h in range(HALO):
                        row_halo[side, h, 8 * q : 8 * q + 8, :] = total[h]

            @pl.when(jnp.logical_not(at_edge))
            def _():
                row_halo[side] = row_in[part, side]

        row_corrections(part)

        for side in range(2):
            at_edge = col == (0 if side == 0 else n_col - 1)

            @pl.when(at_edge)
            def _():
                for group in range(GROUPS):
                    b_arrival(part, group).wait_recv()
                total = got_cols[part, 0]
                for group in range(1, GROUPS):
                    total = total + got_cols[part, group]
                main, rest = total[0:FLAT], total[FLAT : FLAT + 8]
                col_halo[side, 0] = main
                col_halo[side, 1] = pltpu.roll(main, COL - LON, 1)
                main = pltpu.roll(main, COL - 2 * LON, 1)
                for q in range(FLAT // 8):
                    col_halo[side, 2, 8 * q : 8 * q + 8, :] = jnp.where(
                        iota((8, COL), 1) < COL - 2 * LON,
                        main[8 * q : 8 * q + 8, :],
                        pltpu.roll(rest, (COL + COL - 2 * LON - SPARE * q) % COL, 1),
                    )

            @pl.when(jnp.logical_not(at_edge))
            def _():
                pair = col_in[part, side, 0]
                col_halo[side, 0] = pair
                col_halo[side, 1] = pltpu.roll(pair, COL // 2, 1)
                col_halo[side, 2] = col_in[part, side, 1]

        col_corrections(part)
        finish(part)

    for step in range(GROUPS):
        idx_copy(step).wait_send()
    for part in range(2):
        for step in AROUND:
            a_copy(part, step).wait_send()
            z_copy(part, step).wait_send()
        for step in range(GROUP // 2):
            f_copy(part, step).wait_send()
        for side in range(2):
            row_copy(part, side).wait_send()
            col_copy(part, side).wait_send()
        l_copy(part).wait_send()

        @pl.when(col_edge)
        def _():
            for step in range(GROUPS):
                b_copy(part, step).wait_send()


def inverse_sine(start, count, total):
    place = (start + jnp.arange(count, dtype=jnp.int32)).astype(jnp.float32)
    colatitude = math.pi / 4.0 + (place + 0.5) * (math.pi / 2.0 / total)
    return 1.0 / jnp.sin(colatitude)


def shards(state, send_base, send_frac, recv_slots):
    rows = FLAT * LON
    scale = inverse_sine(lax.axis_index("colat") * COL, COL, COL * lax.axis_size("colat"))[None]
    base = jnp.pad(send_base[0], ((0, 0), (0, SLOTS - OUT)))
    frac = jnp.pad(send_frac[0, 0], ((0, 0), (0, SLOTS - OUT)))
    dma = pltpu.SemaphoreType.DMA
    vmem = pltpu.VMEM
    scratch = [
        vmem((2, FLAT * STRIDE, COL), F32),
        vmem((3 * SHELLS * STRIDE, COL), F32),
        vmem(((FLAT + 2 * SHELLS) * LON, 2 * COL), F32),
        vmem((rows, COL), F32),
        vmem((3 * COL, SLOTS), BF16),
        vmem((LON, SLOTS), F32),
        vmem((2 * COL, 2 * COL), BF16),
        vmem((6, 2 * SLOTS, 2 * COL), BF16),
        vmem((6, 8, 2 * COL), I32),
        vmem((2, COL, COL), F32),
        vmem((2, GROUP, FLAT, SLOTS), F32),
        vmem((8, COL), I32),
        vmem((GROUPS, 8, COL), I32),
        vmem((2, GROUPS, FLAT + 8, COL), F32),
        vmem((2, RING, HALO, 8, COL), F32),
        vmem((2, RING, HALO, 8, COL), F32),
        vmem((2, HALO, 8, COL), F32),
        vmem((2, GROUPS, FLAT + 8, COL), F32),
        vmem((2, GROUPS, HALO, 8, COL), F32),
        vmem((2, 2, HALO, FLAT, COL), F32),
        vmem((2, 2, HALO, FLAT, COL), F32),
        vmem((2, 2, HALO, FLAT, COL), F32),
        vmem((2, 2, 2, FLAT, COL), F32),
        vmem((2, 2, 2, FLAT, COL), F32),
        vmem((2, HALO, FLAT, COL), F32),
        vmem((2, HALO, FLAT, COL), F32),
        vmem((2, HALO, FLAT, COL), F32),
        dma((GROUPS,)),
        dma((GROUPS,)),
        dma((2, GROUP // 2)),
        dma((2, GROUP)),
        dma((2, GROUP // 2)),
        dma((2, GROUPS)),
        dma((2, GROUPS)),
        dma((2, RING)),
        dma((2, RING)),
        dma((2,)),
        dma((2, GROUPS)),
        dma((2, 2)),
        dma((2, 2)),
        dma((2, 2)),
        dma((2, 2)),
    ]
    result = pl.pallas_call(
        kernel,
        out_shape=jax.ShapeDtypeStruct((rows, COL), F32),
        in_specs=[pl.BlockSpec(memory_space=pltpu.VMEM)] * 5,
        out_specs=pl.BlockSpec(memory_space=pltpu.VMEM),
        scratch_shapes=scratch,
        compiler_params=pltpu.CompilerParams(
            collective_id=0, has_side_effects=True, vmem_limit_bytes=40 * 1024 * 1024
        ),
    )(state.reshape(rows, COL), base, frac, recv_slots[0], scale)
    return result.reshape(state.shape)


def solution(mesh):
    placed = (
        P("panel", None, None, "lon", "colat"),
        P("panel", ("lon", "colat"), None),
        P("panel", ("lon", "colat"), None, None),
        P("panel", ("lon", "colat"), None),
    )
    return jax.shard_map(
        shards,
        mesh=mesh,
        in_specs=placed,
        out_specs=P("panel", None, None, "lon", "colat"),
        check_vma=False,
    )
```

```python
import math

import jax
import jax.numpy as jnp
from jax import lax
from jax.experimental import pallas as pl
from jax.experimental.pallas import tpu as pltpu
from jax.sharding import PartitionSpec as P

MESH = pl.DeviceIdType.MESH
F32, BF16, I32 = jnp.float32, jnp.bfloat16, jnp.int32

QUANTITIES = 8
SHELLS = 4
FLAT = QUANTITIES * SHELLS
LON = 48
COL = 128
HALO = 3
OUT = 240
SIDE = HALO * LON
SLOTS = 256
GROUP = 8
GROUPS = 8
AROUND = (1, 3, 2)
SPARE = SIDE - COL
PART = FLAT // 2
TARGETS = 2 * GROUPS
TILES = 12
RING = 4
STRIDE = LON + 16
TIME_STEP = 0.25
SPREAD = 0.1 / 3.0
S, MR, MT, MP, BR, BT, BP, WARM = range(QUANTITIES)


def dot(left, right):
    return jnp.dot(left, right, preferred_element_type=F32)


def split(value):
    high = value.astype(BF16)
    return high, (value - high.astype(F32)).astype(BF16)


def iota(shape, dim):
    return lax.broadcasted_iota(I32, shape, dim)


def cross_radial(m, b):
    return m[1] * b[2] - m[2] * b[1]


def cross_polar(m, b):
    return m[2] * b[0] - m[0] * b[2]


def cross_azimuthal(m, b):
    return m[0] * b[1] - m[1] * b[0]


def edge_rates(own, d, lap, emf_first, emf_second, along_lanes):
    grow, thin = jnp.exp(own[WARM]), jnp.exp(-own[S])
    b = own[BR:WARM]
    if along_lanes:
        vel, out = own[MT], MT
        lorentz = (d[BR] * b[1], -d[BR] * b[0] - d[BP] * b[2], d[BP] * b[1])
        turn = (emf_first, None, -emf_second)
    else:
        vel, out = own[MP], MP
        lorentz = (d[BR] * b[2], d[BT] * b[2], -d[BT] * b[1] - d[BR] * b[0])
        turn = (-emf_first, emf_second, None)
    result = [-vel * d[S] - d[out]]
    for i in range(3):
        rate = -vel * d[MR + i] + thin * lorentz[i] + SPREAD * lap[MR + i]
        if MR + i == out:
            rate = rate - grow * (d[S] + d[WARM])
        result.append(rate)
    for i in range(3):
        rate = SPREAD * lap[BR + i]
        result.append(rate if turn[i] is None else rate + turn[i])
    result.append(-vel * d[WARM] - (2.0 / 3.0) * d[out] + SPREAD * lap[WARM])
    return result


def shell_first(x):
    a, b = 8.0 * (x[3] - x[0]), 45.0
    return (
        b * (x[1] - x[0]) - 9.0 * (x[2] - x[0]) + (x[3] - x[0]),
        b * (x[2] - x[0]) - a,
        b * (x[3] - x[1]) - a,
        b * (x[3] - x[2]) - 9.0 * (x[3] - x[1]) + (x[3] - x[0]),
    )


def shell_second(x):
    return (
        2.0 * x[3] - 27.0 * x[2] + 270.0 * x[1] - 245.0 * x[0],
        245.0 * x[0] - 490.0 * x[1] + 270.0 * x[2] - 25.0 * x[3],
        245.0 * x[3] - 490.0 * x[2] + 270.0 * x[1] - 25.0 * x[0],
        2.0 * x[0] - 27.0 * x[1] + 270.0 * x[2] - 245.0 * x[3],
    )


def kernel(
    x_ref, base_ref, frac_ref, slots_ref, scale_ref, out_ref,
    frame, emf, lanes, rate, mix, rows_mix, band, onehot, owner, turned,
    blocks, table, idx_out, idx_in, rest_rows, picked, picked_rows, got_cols, got_rows, row_out, row_in, col_own, col_out, col_in,
    row_halo, col_halo, edge_add,
    idx_send, idx_recv, a_send, a_recv, s_send, b_send, b_recv, l_send, l_recv, r_send, r_recv, c_send, c_recv,
):
    panel, lon, col = lax.axis_index("panel"), lax.axis_index("lon"), lax.axis_index("colat")
    n_lon, n_col = lax.axis_size("lon"), lax.axis_size("colat")
    core, mine = lax.rem(lon, 2), lax.div(lon, 2)
    member = core * n_col + col
    other = 1 - panel
    lon_up, lon_down = lax.rem(lon + 1, n_lon), lax.rem(lon + n_lon - 1, n_lon)
    col_up, col_down = lax.rem(col + 1, n_col), lax.rem(col + n_col - 1, n_col)
    outer = lax.rem(lon + 2 * core - 1 + n_lon, n_lon)
    col_edge = jnp.logical_or(col == 0, col == n_col - 1)
    lon_edge = jnp.logical_or(lon == 0, lon == n_lon - 1)

    sibling = (panel, lon + 1 - 2 * core, col)
    origin = core * GROUPS + mine

    def row_device(step, half):
        return (panel, 2 * mine + half, lax.rem(col + step, n_col))

    def target_device(target):
        return (other, 2 * lax.rem(target, GROUPS) + lax.div(target, GROUPS), col)

    def remote(src, dst, send, recv, device):
        return pltpu.make_async_remote_copy(
            src_ref=src, dst_ref=dst, send_sem=send, recv_sem=recv, device_id=device, device_id_type=MESH
        )

    barrier = pltpu.get_barrier_semaphore()
    for step in AROUND:
        for half in range(2):
            pl.semaphore_signal(barrier, inc=1, device_id=row_device(step, half), device_id_type=MESH)
    pl.semaphore_signal(barrier, inc=1, device_id=sibling, device_id_type=MESH)
    for target in range(TARGETS):
        pl.semaphore_signal(barrier, inc=1, device_id=target_device(target), device_id_type=MESH)
    pl.semaphore_signal(barrier, inc=1, device_id=(panel, outer, col), device_id_type=MESH)

    zero_rows = jnp.zeros((8, COL), F32)
    for f in range(FLAT):
        for part in range(2):
            frame[part, f * STRIDE : f * STRIDE + 8, :] = zero_rows
            frame[part, f * STRIDE + 8 + LON : (f + 1) * STRIDE, :] = zero_rows
        frame[0, f * STRIDE + 8 : f * STRIDE + 8 + LON, :] = x_ref[f * LON : (f + 1) * LON, :]
    for f in range(3 * SHELLS):
        emf[f * STRIDE : f * STRIDE + 8, :] = zero_rows
        emf[f * STRIDE + 8 + LON : (f + 1) * STRIDE, :] = zero_rows

    base = base_ref[...]
    base_row, base_col = lax.div(base, COL), lax.rem(base, COL)
    along, across = frac_ref[0:1, :], frac_ref[1:2, :]
    cells = iota((COL, SLOTS), 0)
    weight = jnp.where(cells == base_col, 1.0 - across, 0.0) + jnp.where(cells == base_col + 1, across, 0.0)
    weight_high, weight_low = split(weight)
    mix[0:COL, :] = weight_high
    mix[COL : 2 * COL, :] = weight_high
    mix[2 * COL : 3 * COL, :] = weight_low
    cells = iota((LON, SLOTS), 0)
    rows_mix[...] = jnp.where(cells == base_row, 1.0 - along, 0.0) + jnp.where(cells == base_row + 1, along, 0.0)

    for half in range(2):
        turned[half, :, :] = jnp.zeros((COL, COL), F32)

    apart = iota((COL, COL), 0) - iota((COL, COL), 1)
    reach = jnp.abs(apart)
    first = jnp.where(reach == 1, 45.0, jnp.where(reach == 2, -9.0, jnp.where(reach == 3, 1.0, 0.0)))
    first = jnp.where(apart < 0, -first, first).astype(BF16)
    second = jnp.where(
        reach == 0, -490.0, jnp.where(reach == 1, 270.0, jnp.where(reach == 2, -27.0, jnp.where(reach == 3, 2.0, 0.0)))
    ).astype(BF16)
    for part in range(2):
        band[part * COL : (part + 1) * COL, 0:COL] = first
        band[part * COL : (part + 1) * COL, COL : 2 * COL] = second

    spot = iota((1, SLOTS), 1)
    sides = jnp.where(spot < SIDE, jnp.maximum(slots_ref[:, 0:SLOTS], slots_ref[:, SIDE : SIDE + SLOTS]) + 1, 0)
    digits = jnp.concatenate([lax.div(sides, COL), lax.rem(sides, COL), jnp.zeros((6, SLOTS), I32)], axis=0)
    source, target = iota((SLOTS, SLOTS), 0), iota((SLOTS, SLOTS), 1)
    layer = jnp.where(target >= LON, 1, 0) + jnp.where(target >= 2 * LON, 1, 0)
    order = jnp.logical_and(target < SIDE, source == HALO * (target - LON * layer) + layer)
    digits = dot(digits.astype(F32).astype(BF16), jnp.where(order, 1.0, 0.0).astype(BF16)).astype(I32)
    sides = digits[0:1, :] * COL + digits[1:2, :] - 1
    idx_out[0:1, :] = sides[:, 0:COL]
    idx_out[1:2, :] = sides[:, COL : 2 * COL]
    for h in range(HALO):
        at = 2 * SIDE + h * COL
        idx_out[2 + h : 3 + h, :] = jnp.maximum(
            slots_ref[:, at : at + COL], slots_ref[:, at + HALO * COL : at + HALO * COL + COL]
        )
    idx_out[5:8, :] = jnp.full((3, COL), -1, I32)

    scale = scale_ref[...]

    def load_split(part, pair):
        block = jnp.concatenate(
            [frame[part, pl.ds(pl.multiple_of((8 * pair + q) * STRIDE, 8) + 8, LON), :] for q in range(8)], axis=0
        )
        return split(block)

    def interpolate(part, half):
        def body(pair, carry):
            high, low = load_split(part, 2 * half + pair)
            value = dot(jnp.concatenate([high, low, high], axis=1), mix[...])
            value = jnp.sum(value.reshape(8, LON, SLOTS) * rows_mix[...][None], axis=1)
            blocks[part, half, pl.ds(pl.multiple_of(8 * pair, 8), 8), :] = value
            return carry

        lax.fori_loop(0, PART // 8, body, 0)

    def interpolate_and_send(part):
        for half in range(2):
            interpolate(part, half)
            if part == 0 and half == 0:
                pl.semaphore_wait(barrier, 2 * len(AROUND) + 2 + TARGETS)
            for step in AROUND:
                a_copy(part, step, half).start()

            @pl.when(core != half)
            def _():
                s_copy(part, half).start()

            @pl.when(core == half)
            def _():
                table[part, member] = blocks[part, half]

    def lane_pass(part):
        def body(pair, carry):
            high, low = load_split(part, pair)
            both = jnp.concatenate([high, low], axis=1)
            lanes[pl.ds(pl.multiple_of(8 * LON * pair, 8), 8 * LON), :] = dot(both, band[...])
            return carry

        lax.fori_loop(0, FLAT // 8, body, 0)

    def cols_of(part):
        lane = iota((LON, COL), 1)
        for half in range(2):
            edge = jnp.zeros((LON, COL), F32)
            for g in range(FLAT // 2):
                at = (half * (FLAT // 2) + g) * STRIDE + 8
                moved = pltpu.roll(frame[part, at : at + LON, :], 8 * g + HALO, 1)
                edge = jnp.where(jnp.logical_and(lane >= 8 * g, lane < 8 * g + 2 * HALO), moved, edge)
            turned[half, :, 0:LON] = jnp.transpose(edge)
        for side in range(2):
            for j in range(HALO):
                first = (1 - side) * HALO + j
                for half in range(2):
                    col_own[part, side, j, half * (FLAT // 2) : (half + 1) * (FLAT // 2), :] = turned[
                        half, pl.ds(first, FLAT // 2, stride=8), :
                    ]
            col_out[part, side, 0] = jnp.where(
                iota((FLAT, COL), 1) < COL // 2, col_own[part, side, 0], pltpu.roll(col_own[part, side, 1], COL // 2, 1)
            )
            col_out[part, side, 1] = col_own[part, side, 2]

    def emf_pass(part):
        for r in range(SHELLS):
            def field(q):
                at = (q * SHELLS + r) * STRIDE + 8
                return frame[part, at : at + LON, :]

            m, b = [field(MR + i) for i in range(3)], [field(BR + i) for i in range(3)]
            for i, form in enumerate((cross_radial, cross_polar, cross_azimuthal)):
                at = (i * SHELLS + r) * STRIDE + 8
                emf[at : at + LON, :] = form(m, b)
        for i, at in ((0, FLAT), (2, FLAT + SHELLS)):
            block = jnp.concatenate(
                [emf[(i * SHELLS + r) * STRIDE + 8 : (i * SHELLS + r) * STRIDE + 8 + LON, :] for r in range(SHELLS)],
                axis=0,
            )
            high, low = split(block)
            lanes[at * LON : (at + SHELLS) * LON, 0:COL] = dot(
                jnp.concatenate([high, low], axis=1), band[:, 0:COL]
            )

    def main_pass(part, start, stop):
        def body(block, carry):
            here = pl.multiple_of(8 * block, 8)

            def near(f, apart):
                return frame[part, pl.ds(f * STRIDE + 8 + here + apart, 8), :]

            def near_emf(f, apart):
                return emf[pl.ds(f * STRIDE + 8 + here + apart, 8), :]

            def lane_first(f):
                return lanes[pl.ds(f * LON + here, 8), 0:COL]

            def lane_second(f):
                return lanes[pl.ds(f * LON + here, 8), COL : 2 * COL]

            def row_first(at):
                return 45.0 * (at[1] - at[-1]) - 9.0 * (at[2] - at[-2]) + (at[3] - at[-3])

            def row_second(at, centre):
                return (
                    270.0 * (at[1] + at[-1]) - 27.0 * (at[2] + at[-2]) + 2.0 * (at[3] + at[-3]) - 490.0 * centre
                )

            centre = [[near(q * SHELLS + r, 0) for r in range(SHELLS)] for q in range(QUANTITIES)]
            radial = [shell_first(x) for x in centre]
            radial_second = [None if q == S else shell_second(centre[q]) for q in range(QUANTITIES)]
            emf_centre = [[near_emf(i * SHELLS + r, 0) for r in range(SHELLS)] for i in range(3)]
            emf_radial = [None, shell_first(emf_centre[1]), shell_first(emf_centre[2])]
            for r in range(SHELLS):
                own = [centre[q][r] for q in range(QUANTITIES)]
                g, lap = [], []
                for q in range(QUANTITIES):
                    f = q * SHELLS + r
                    at = {d: near(f, d) for d in (-3, -2, -1, 1, 2, 3)}
                    g.append((radial[q][r], lane_first(f), scale * row_first(at)))
                    if q == S:
                        lap.append(None)
                    else:
                        lap.append(
                            radial_second[q][r] + lane_second(f) + (scale * scale) * row_second(at, own[q])
                        )
                m, b = own[MR:BR], own[BR:WARM]

                def advect(q):
                    return m[0] * g[q][0] + m[1] * g[q][1] + m[2] * g[q][2]

                div = g[MR][0] + g[MT][1] + g[MP][2]
                current = (g[BP][1] - g[BT][2], g[BR][2] - g[BP][0], g[BT][0] - g[BR][1])
                lorentz = (
                    current[1] * b[2] - current[2] * b[1],
                    current[2] * b[0] - current[0] * b[2],
                    current[0] * b[1] - current[1] * b[0],
                )
                grow, thin = jnp.exp(own[WARM]), jnp.exp(-own[S])
                emf_rows = {}
                for i in (0, 1):
                    f = i * SHELLS + r
                    emf_rows[i] = scale * row_first({d: near_emf(f, d) for d in (-3, -2, -1, 1, 2, 3)})
                turn = (
                    lane_first(FLAT + SHELLS + r) - emf_rows[1],
                    emf_rows[0] - emf_radial[2][r],
                    emf_radial[1][r] - lane_first(FLAT + r),
                )
                result = [-advect(S) - div]
                for i in range(3):
                    result.append(
                        -advect(MR + i) - grow * (g[S][i] + g[WARM][i]) + thin * lorentz[i] + SPREAD * lap[MR + i]
                    )
                for i in range(3):
                    result.append(turn[i] + SPREAD * lap[BR + i])
                result.append(-advect(WARM) - (2.0 / 3.0) * div + SPREAD * lap[WARM])
                for q in range(QUANTITIES):
                    rate[pl.ds((q * SHELLS + r) * LON + here, 8), :] = result[q]
            return carry

        lax.fori_loop(start, stop, body, 0)

    def rows_of(part):
        for h in range(HALO):
            row_out[part, 0, h] = frame[part, pl.ds(8 + h, FLAT, stride=STRIDE), :]
            row_out[part, 1, h] = frame[part, pl.ds(8 + LON - HALO + h, FLAT, stride=STRIDE), :]

    def prepare_picks():
        for tile in range(2 * TILES):
            if tile < TARGETS:
                slot = idx_in[tile, 0:1, :]
            elif tile < TARGETS + 2:
                first = (tile - TARGETS) * GROUPS
                slot = idx_in[first, 1:2, :]
                for q in range(1, GROUPS):
                    slot = jnp.maximum(slot, pltpu.roll(idx_in[first + q], SPARE * q, 1)[1:2, :])
            else:
                side, h = divmod(tile - TARGETS - 2, HALO)
                slot = idx_in[side * (TARGETS - 1), 2 + h : 3 + h, :]
            slot = slot - mine * (GROUP * OUT)
            who = jnp.zeros_like(slot)
            for q in range(1, GROUP):
                who = who + jnp.where(slot >= q * OUT, 1, 0)
            cell = slot - who * OUT
            who = jnp.where(jnp.logical_and(slot >= 0, slot < GROUP * OUT), who, -1)
            at = (tile % 2) * COL
            owner[tile // 2, :, at : at + COL] = jnp.broadcast_to(who, (8, COL))
            hot = jnp.where(iota((SLOTS, COL), 0) == cell, 1.0, 0.0).astype(BF16)
            onehot[tile // 2, :, at : at + COL] = hot

    def table_split(part):
        high, low = split(table[part].reshape(GROUP * PART, SLOTS))
        return jnp.concatenate([high, low], axis=0)

    def pick(both, tile):
        value = dot(both, onehot[tile])
        value = value[0 : GROUP * PART] + value[GROUP * PART :]
        who = jnp.broadcast_to(owner[tile, 0:1, :], (PART, SLOTS))
        total = jnp.zeros((PART, SLOTS), F32)
        for q in range(GROUP):
            total = jnp.where(who == q, value[q * PART : (q + 1) * PART, :], total)
        return total[:, 0:COL], total[:, COL : 2 * COL]

    def pick_sides(part, both):
        rest = pick(both, TARGETS // 2)
        rest_rows[0], rest_rows[1] = rest
        spot = lax.div(iota((8, COL), 1), SPARE)
        for step in range(TARGETS // 2):
            tile = lax.rem(step + mine, TARGETS // 2)
            ends = pick(both, tile)
            rows = rest_rows[lax.div(tile, GROUPS // 2)]
            for i in range(2):
                target = 2 * tile + i
                there = lax.rem(target, GROUPS)
                total = jnp.zeros((8, COL), F32)
                for q in range(PART // 8):
                    moved = pltpu.roll(rows[8 * q : 8 * q + 8, :], SPARE * lax.rem(q + GROUPS - there, GROUPS), 1)
                    total = jnp.where(spot == q, moved, total)
                picked[part, target, 0:PART, :] = ends[i]
                picked[part, target, PART : PART + 8, :] = total
                b_copy(part, target).start()

    def pick_ends(part, both):
        ends = []
        for tile in range(TARGETS // 2 + 1, TILES):
            ends += pick(both, tile)
        for side in range(2):
            for h in range(HALO):
                picked_rows[part, side, h] = ends[side * HALO + h]
            l_copy(part, side).start()

    def corrections(part, halo_ref, own_ref, along_lanes):
        factor = None if along_lanes else scale

        def scaled(value, power):
            for _ in range(0 if along_lanes else power):
                value = factor * value
            return value

        for side in range(2):
            halo = [
                [halo_ref[side, h, q * SHELLS : (q + 1) * SHELLS, :] for q in range(QUANTITIES)] for h in range(HALO)
            ]
            form = cross_azimuthal if along_lanes else cross_polar
            halo_emf = [(cross_radial(x[MR:BR], x[BR:WARM]), form(x[MR:BR], x[BR:WARM])) for x in halo]
            sign = -1.0 if side == 0 else 1.0
            firsts, seconds = (45.0 * sign, -9.0 * sign, sign), (270.0, -27.0, 2.0)
            for j in range(HALO):
                own = [own_ref[part, side, j, q * SHELLS : (q + 1) * SHELLS, :] for q in range(QUANTITIES)]

                def total(weights, of):
                    result = None
                    for m in (1, 2, 3):
                        h = j + 3 - m if side == 0 else m - 3 + j
                        if 0 <= h < HALO:
                            term = weights[m - 1] * of(h)
                            result = term if result is None else result + term
                    return result

                d = [scaled(total(firsts, lambda h, q=q: halo[h][q]), 1) for q in range(QUANTITIES)]
                lap = [
                    None if q == S else scaled(total(seconds, lambda h, q=q: halo[h][q]), 2)
                    for q in range(QUANTITIES)
                ]
                radial = scaled(total(firsts, lambda h: halo_emf[h][0]), 1)
                second = scaled(total(firsts, lambda h: halo_emf[h][1]), 1)
                result = edge_rates(own, d, lap, second, radial, along_lanes)
                for q in range(QUANTITIES):
                    edge_add[side, j, q * SHELLS : (q + 1) * SHELLS, :] = result[q]

    def row_corrections(part):
        corrections(part, row_halo, row_out, False)
        for side in range(2):
            for j in range(HALO):
                rows = pl.ds(j if side == 0 else LON - HALO + j, FLAT, stride=LON)
                rate[rows, :] = rate[rows, :] + edge_add[side, j]

    def col_corrections(part):
        corrections(part, col_halo, col_own, True)
        for side in range(2):
            for j in range(HALO):
                for half in range(2):
                    turned[half, pl.ds((1 - side) * HALO + j, FLAT // 2, stride=8), :] = edge_add[
                        side, j, half * (FLAT // 2) : (half + 1) * (FLAT // 2), :
                    ]

    def finish(part):
        lane = iota((LON, COL), 1)
        border = jnp.logical_or(lane < HALO, lane >= COL - HALO)
        for half in range(2):
            edge = jnp.transpose(turned[half])[0:LON, :]
            for g in range(FLAT // 2):
                f = half * (FLAT // 2) + g
                added = jnp.where(border, pltpu.roll(edge, COL - 8 * g - HALO, 1), 0.0)
                change = (TIME_STEP / 60.0) * (rate[f * LON : (f + 1) * LON, :] + added)
                start = x_ref[f * LON : (f + 1) * LON, :]
                rows = slice(f * STRIDE + 8, f * STRIDE + 8 + LON)
                if part == 0:
                    frame[1, rows, :] = start + change
                else:
                    out_ref[f * LON : (f + 1) * LON, :] = 0.5 * (start + frame[1, rows, :] + change)

    def a_copy(part, step, half):
        return remote(
            blocks.at[part, half], table.at[part, member], a_send.at[part, half, step], a_recv.at[part, member],
            row_device(step, half),
        )

    def s_copy(part, half):
        return remote(
            blocks.at[part, half], table.at[part, member], s_send.at[part], a_recv.at[part, member], sibling
        )

    def a_arrival(part, step):
        there = lax.rem(member + step, GROUP)
        return remote(blocks.at[part, 0], table.at[part, there], s_send.at[part], a_recv.at[part, there], sibling)

    def b_copy(part, target):
        return remote(
            picked.at[part, target], got_cols.at[part, origin], b_send.at[part, target], b_recv.at[part, origin],
            target_device(target),
        )

    def b_arrival(part, source):
        return remote(
            picked.at[part, 0], got_cols.at[part, source], b_send.at[part, 0], b_recv.at[part, source],
            (other, lon, col),
        )

    def l_copy(part, side):
        return remote(
            picked_rows.at[part, side], got_rows.at[part, origin], l_send.at[part, side], l_recv.at[part, origin],
            target_device(side * (TARGETS - 1)),
        )

    def l_arrival(part, source):
        return remote(
            picked_rows.at[part, 0], got_rows.at[part, source], l_send.at[part, 0], l_recv.at[part, source],
            (other, lon, col),
        )

    def row_copy(part, side):
        return remote(
            row_out.at[part, 1 - side], row_in.at[part, side], r_send.at[part, side], r_recv.at[part, side],
            (panel, lon_up if side == 0 else lon_down, col),
        )

    def col_copy(part, side):
        return remote(
            col_out.at[part, 1 - side], col_in.at[part, side], c_send.at[part, side], c_recv.at[part, side],
            (panel, lon, col_up if side == 0 else col_down),
        )

    def idx_copy(target):
        return remote(
            idx_out, idx_in.at[origin], idx_send.at[target], idx_recv.at[origin], target_device(target)
        )

    def idx_arrival(source):
        return remote(idx_out, idx_in.at[source], idx_send.at[0], idx_recv.at[source], (other, lon, col))

    for part in range(2):
        interpolate_and_send(part)
        if part == 0:
            for target in range(TARGETS):
                idx_copy(target).start()
        rows_of(part)
        for side in range(2):
            row_copy(part, side).start()
        cols_of(part)
        for side in range(2):
            col_copy(part, side).start()
        lane_pass(part)
        emf_pass(part)
        if part == 0:
            for source in range(TARGETS):
                idx_arrival(source).wait_recv()
            prepare_picks()
        main_pass(part, 0, 2)
        for step in range(1, GROUP):
            a_arrival(part, step).wait_recv()
        both = table_split(part)

        @pl.when(col_edge)
        def _():
            pick_sides(part, both)

        pick_ends(part, both)
        main_pass(part, 2, 6)
        for side in range(2):
            row_copy(part, side).wait_recv()
            col_copy(part, side).wait_recv()

        for side in range(2):
            at_edge = lon == (0 if side == 0 else n_lon - 1)

            @pl.when(at_edge)
            def _():
                for source in range(TARGETS):
                    l_arrival(part, source).wait_recv()
                for half in range(2):
                    total = got_rows[part, half * GROUPS]
                    for group in range(1, GROUPS):
                        total = total + got_rows[part, half * GROUPS + group]
                    row_halo[side, :, half * PART : (half + 1) * PART, :] = total

            @pl.when(jnp.logical_not(at_edge))
            def _():
                row_halo[side] = row_in[part, side]

        row_corrections(part)

        for side in range(2):
            at_edge = col == (0 if side == 0 else n_col - 1)

            @pl.when(at_edge)
            def _():
                for source in range(TARGETS):
                    b_arrival(part, source).wait_recv()
                for half in range(2):
                    total = got_cols[part, half * GROUPS]
                    for group in range(1, GROUPS):
                        total = total + got_cols[part, half * GROUPS + group]
                    main, rest = total[0:PART], total[PART : PART + 8]
                    rows = slice(half * PART, (half + 1) * PART)
                    col_halo[side, 0, rows, :] = main
                    col_halo[side, 1, rows, :] = pltpu.roll(main, COL - LON, 1)
                    main = pltpu.roll(main, COL - 2 * LON, 1)
                    for q in range(PART // 8):
                        at = half * PART + 8 * q
                        col_halo[side, 2, at : at + 8, :] = jnp.where(
                            iota((8, COL), 1) < COL - 2 * LON,
                            main[8 * q : 8 * q + 8, :],
                            pltpu.roll(rest, (COL + COL - 2 * LON - SPARE * q) % COL, 1),
                        )

            @pl.when(jnp.logical_not(at_edge))
            def _():
                pair = col_in[part, side, 0]
                col_halo[side, 0] = pair
                col_halo[side, 1] = pltpu.roll(pair, COL // 2, 1)
                col_halo[side, 2] = col_in[part, side, 1]

        col_corrections(part)
        finish(part)

    for target in range(TARGETS):
        idx_copy(target).wait_send()
    for part in range(2):
        for half in range(2):
            for step in AROUND:
                a_copy(part, step, half).wait_send()
        s_copy(part, 0).wait_send()
        for side in range(2):
            row_copy(part, side).wait_send()
            col_copy(part, side).wait_send()
            l_copy(part, side).wait_send()

        @pl.when(col_edge)
        def _():
            for target in range(TARGETS):
                b_copy(part, target).wait_send()


def inverse_sine(start, count, total):
    place = (start + jnp.arange(count, dtype=jnp.int32)).astype(jnp.float32)
    colatitude = math.pi / 4.0 + (place + 0.5) * (math.pi / 2.0 / total)
    return 1.0 / jnp.sin(colatitude)


def shards(state, send_base, send_frac, recv_slots):
    rows = FLAT * LON
    scale = inverse_sine(lax.axis_index("colat") * COL, COL, COL * lax.axis_size("colat"))[None]
    base = jnp.pad(send_base[0], ((0, 0), (0, SLOTS - OUT)))
    frac = jnp.pad(send_frac[0, 0], ((0, 0), (0, SLOTS - OUT)))
    dma = pltpu.SemaphoreType.DMA
    vmem = pltpu.VMEM
    scratch = [
        vmem((2, FLAT * STRIDE, COL), F32),
        vmem((3 * SHELLS * STRIDE, COL), F32),
        vmem(((FLAT + 2 * SHELLS) * LON, 2 * COL), F32),
        vmem((rows, COL), F32),
        vmem((3 * COL, SLOTS), BF16),
        vmem((LON, SLOTS), F32),
        vmem((2 * COL, 2 * COL), BF16),
        vmem((TILES, SLOTS, 2 * COL), BF16),
        vmem((TILES, 8, 2 * COL), I32),
        vmem((2, COL, COL), F32),
        vmem((2, 2, PART, SLOTS), F32),
        vmem((2, GROUP, PART, SLOTS), F32),
        vmem((8, COL), I32),
        vmem((TARGETS, 8, COL), I32),
        vmem((2, PART, COL), F32),
        vmem((2, TARGETS, PART + 8, COL), F32),
        vmem((2, 2, HALO, PART, COL), F32),
        vmem((2, TARGETS, PART + 8, COL), F32),
        vmem((2, TARGETS, HALO, PART, COL), F32),
        vmem((2, 2, HALO, FLAT, COL), F32),
        vmem((2, 2, HALO, FLAT, COL), F32),
        vmem((2, 2, HALO, FLAT, COL), F32),
        vmem((2, 2, 2, FLAT, COL), F32),
        vmem((2, 2, 2, FLAT, COL), F32),
        vmem((2, HALO, FLAT, COL), F32),
        vmem((2, HALO, FLAT, COL), F32),
        vmem((2, HALO, FLAT, COL), F32),
        dma((TARGETS,)),
        dma((TARGETS,)),
        dma((2, 2, RING)),
        dma((2, GROUP)),
        dma((2,)),
        dma((2, TARGETS)),
        dma((2, TARGETS)),
        dma((2, 2)),
        dma((2, TARGETS)),
        dma((2, 2)),
        dma((2, 2)),
        dma((2, 2)),
        dma((2, 2)),
    ]
    result = pl.pallas_call(
        kernel,
        out_shape=jax.ShapeDtypeStruct((rows, COL), F32),
        in_specs=[pl.BlockSpec(memory_space=pltpu.VMEM)] * 5,
        out_specs=pl.BlockSpec(memory_space=pltpu.VMEM),
        scratch_shapes=scratch,
        compiler_params=pltpu.CompilerParams(
            collective_id=0, has_side_effects=True, vmem_limit_bytes=40 * 1024 * 1024
        ),
    )(state.reshape(rows, COL), base, frac, recv_slots[0], scale)
    return result.reshape(state.shape)


def solution(mesh):
    placed = (
        P("panel", None, None, "lon", "colat"),
        P("panel", ("lon", "colat"), None),
        P("panel", ("lon", "colat"), None, None),
        P("panel", ("lon", "colat"), None),
    )
    return jax.shard_map(
        shards,
        mesh=mesh,
        in_specs=placed,
        out_specs=P("panel", None, None, "lon", "colat"),
        check_vma=False,
    )
```

```python
import math

import jax
import jax.numpy as jnp
from jax import lax
from jax.experimental import pallas as pl
from jax.experimental.pallas import tpu as pltpu
from jax.sharding import PartitionSpec as P

MESH = pl.DeviceIdType.MESH
F32, BF16, I32 = jnp.float32, jnp.bfloat16, jnp.int32

QUANTITIES = 8
SHELLS = 4
FLAT = QUANTITIES * SHELLS
LON = 48
COL = 128
HALO = 3
OUT = 240
SIDE = HALO * LON
SLOTS = 256
GROUP = 8
GROUPS = 8
AROUND = (1, 3, 2)
SPARE = SIDE - COL
PART = FLAT // 2
TARGETS = 2 * GROUPS
TILES = 12
RING = 4
STRIDE = LON + 16
TIME_STEP = 0.25
SPREAD = 0.1 / 3.0
S, MR, MT, MP, BR, BT, BP, WARM = range(QUANTITIES)


def dot(left, right):
    return jnp.dot(left, right, preferred_element_type=F32)


def split(value):
    high = value.astype(BF16)
    return high, (value - high.astype(F32)).astype(BF16)


def iota(shape, dim):
    return lax.broadcasted_iota(I32, shape, dim)


def cross_radial(m, b):
    return m[1] * b[2] - m[2] * b[1]


def cross_polar(m, b):
    return m[2] * b[0] - m[0] * b[2]


def cross_azimuthal(m, b):
    return m[0] * b[1] - m[1] * b[0]


def edge_rates(own, d, lap, emf_first, emf_second, along_lanes):
    grow, thin = jnp.exp(own[WARM]), jnp.exp(-own[S])
    b = own[BR:WARM]
    if along_lanes:
        vel, out = own[MT], MT
        lorentz = (d[BR] * b[1], -d[BR] * b[0] - d[BP] * b[2], d[BP] * b[1])
        turn = (emf_first, None, -emf_second)
    else:
        vel, out = own[MP], MP
        lorentz = (d[BR] * b[2], d[BT] * b[2], -d[BT] * b[1] - d[BR] * b[0])
        turn = (-emf_first, emf_second, None)
    result = [-vel * d[S] - d[out]]
    for i in range(3):
        rate = -vel * d[MR + i] + thin * lorentz[i] + SPREAD * lap[MR + i]
        if MR + i == out:
            rate = rate - grow * (d[S] + d[WARM])
        result.append(rate)
    for i in range(3):
        rate = SPREAD * lap[BR + i]
        result.append(rate if turn[i] is None else rate + turn[i])
    result.append(-vel * d[WARM] - (2.0 / 3.0) * d[out] + SPREAD * lap[WARM])
    return result


def shell_first(x):
    a, b = 8.0 * (x[3] - x[0]), 45.0
    return (
        b * (x[1] - x[0]) - 9.0 * (x[2] - x[0]) + (x[3] - x[0]),
        b * (x[2] - x[0]) - a,
        b * (x[3] - x[1]) - a,
        b * (x[3] - x[2]) - 9.0 * (x[3] - x[1]) + (x[3] - x[0]),
    )


def shell_second(x):
    return (
        2.0 * x[3] - 27.0 * x[2] + 270.0 * x[1] - 245.0 * x[0],
        245.0 * x[0] - 490.0 * x[1] + 270.0 * x[2] - 25.0 * x[3],
        245.0 * x[3] - 490.0 * x[2] + 270.0 * x[1] - 25.0 * x[0],
        2.0 * x[0] - 27.0 * x[1] + 270.0 * x[2] - 245.0 * x[3],
    )


def kernel(
    x_ref, base_ref, frac_ref, slots_ref, scale_ref, out_ref,
    frame, emf, lanes, rate, mix, rows_mix, band, onehot, owner, turned,
    blocks, table, idx_out, idx_in, rest_rows, picked, picked_rows, got_cols, got_rows, row_out, row_in, col_own, col_out, col_in,
    row_halo, col_halo, edge_add,
    idx_send, idx_recv, a_send, a_recv, s_send, b_send, b_recv, l_send, l_recv, r_send, r_recv, c_send, c_recv,
):
    panel, lon, col = lax.axis_index("panel"), lax.axis_index("lon"), lax.axis_index("colat")
    n_lon, n_col = lax.axis_size("lon"), lax.axis_size("colat")
    core, mine = lax.rem(lon, 2), lax.div(lon, 2)
    member = core * n_col + col
    other = 1 - panel
    lon_up, lon_down = lax.rem(lon + 1, n_lon), lax.rem(lon + n_lon - 1, n_lon)
    col_up, col_down = lax.rem(col + 1, n_col), lax.rem(col + n_col - 1, n_col)
    outer = lax.rem(lon + 2 * core - 1 + n_lon, n_lon)
    col_edge = jnp.logical_or(col == 0, col == n_col - 1)
    lon_edge = jnp.logical_or(lon == 0, lon == n_lon - 1)

    sibling = (panel, lon + 1 - 2 * core, col)
    origin = core * GROUPS + mine

    def row_device(step, half):
        return (panel, 2 * mine + half, lax.rem(col + step, n_col))

    def target_device(target):
        return (other, 2 * lax.rem(target, GROUPS) + lax.div(target, GROUPS), col)

    def remote(src, dst, send, recv, device):
        return pltpu.make_async_remote_copy(
            src_ref=src, dst_ref=dst, send_sem=send, recv_sem=recv, device_id=device, device_id_type=MESH
        )

    barrier = pltpu.get_barrier_semaphore()
    for step in AROUND:
        for half in range(2):
            pl.semaphore_signal(barrier, inc=1, device_id=row_device(step, half), device_id_type=MESH)
    pl.semaphore_signal(barrier, inc=1, device_id=sibling, device_id_type=MESH)
    for target in range(TARGETS):
        pl.semaphore_signal(barrier, inc=1, device_id=target_device(target), device_id_type=MESH)
    pl.semaphore_signal(barrier, inc=1, device_id=(panel, outer, col), device_id_type=MESH)

    zero_rows = jnp.zeros((8, COL), F32)
    for f in range(FLAT):
        for part in range(2):
            frame[part, f * STRIDE : f * STRIDE + 8, :] = zero_rows
            frame[part, f * STRIDE + 8 + LON : (f + 1) * STRIDE, :] = zero_rows
        frame[0, f * STRIDE + 8 : f * STRIDE + 8 + LON, :] = x_ref[f * LON : (f + 1) * LON, :]
    for f in range(3 * SHELLS):
        emf[f * STRIDE : f * STRIDE + 8, :] = zero_rows
        emf[f * STRIDE + 8 + LON : (f + 1) * STRIDE, :] = zero_rows

    base = base_ref[...]
    base_row, base_col = lax.div(base, COL), lax.rem(base, COL)
    along, across = frac_ref[0:1, :], frac_ref[1:2, :]
    cells = iota((COL, SLOTS), 0)
    weight = jnp.where(cells == base_col, 1.0 - across, 0.0) + jnp.where(cells == base_col + 1, across, 0.0)
    weight_high, weight_low = split(weight)
    mix[0:COL, :] = weight_high
    mix[COL : 2 * COL, :] = weight_high
    mix[2 * COL : 3 * COL, :] = weight_low
    cells = iota((LON, SLOTS), 0)
    rows_mix[...] = jnp.where(cells == base_row, 1.0 - along, 0.0) + jnp.where(cells == base_row + 1, along, 0.0)

    for half in range(2):
        turned[half, :, :] = jnp.zeros((COL, COL), F32)

    apart = iota((COL, COL), 0) - iota((COL, COL), 1)
    reach = jnp.abs(apart)
    first = jnp.where(reach == 1, 45.0, jnp.where(reach == 2, -9.0, jnp.where(reach == 3, 1.0, 0.0)))
    first = jnp.where(apart < 0, -first, first).astype(BF16)
    second = jnp.where(
        reach == 0, -490.0, jnp.where(reach == 1, 270.0, jnp.where(reach == 2, -27.0, jnp.where(reach == 3, 2.0, 0.0)))
    ).astype(BF16)
    for part in range(2):
        band[part * COL : (part + 1) * COL, 0:COL] = first
        band[part * COL : (part + 1) * COL, COL : 2 * COL] = second

    spot = iota((1, SLOTS), 1)
    sides = jnp.where(spot < SIDE, jnp.maximum(slots_ref[:, 0:SLOTS], slots_ref[:, SIDE : SIDE + SLOTS]) + 1, 0)
    digits = jnp.concatenate([lax.div(sides, COL), lax.rem(sides, COL), jnp.zeros((6, SLOTS), I32)], axis=0)
    source, target = iota((SLOTS, SLOTS), 0), iota((SLOTS, SLOTS), 1)
    layer = jnp.where(target >= LON, 1, 0) + jnp.where(target >= 2 * LON, 1, 0)
    order = jnp.logical_and(target < SIDE, source == HALO * (target - LON * layer) + layer)
    digits = dot(digits.astype(F32).astype(BF16), jnp.where(order, 1.0, 0.0).astype(BF16)).astype(I32)
    sides = digits[0:1, :] * COL + digits[1:2, :] - 1
    idx_out[0:1, :] = sides[:, 0:COL]
    idx_out[1:2, :] = sides[:, COL : 2 * COL]
    for h in range(HALO):
        at = 2 * SIDE + h * COL
        idx_out[2 + h : 3 + h, :] = jnp.maximum(
            slots_ref[:, at : at + COL], slots_ref[:, at + HALO * COL : at + HALO * COL + COL]
        )
    idx_out[5:8, :] = jnp.full((3, COL), -1, I32)

    scale = scale_ref[...]

    def load_split(part, pair):
        block = jnp.concatenate(
            [frame[part, pl.ds(pl.multiple_of((8 * pair + q) * STRIDE, 8) + 8, LON), :] for q in range(8)], axis=0
        )
        return split(block)

    def interpolate(part, half):
        def body(pair, carry):
            high, low = load_split(part, 2 * half + pair)
            value = dot(jnp.concatenate([high, low, high], axis=1), mix[...])
            value = jnp.sum(value.reshape(8, LON, SLOTS) * rows_mix[...][None], axis=1)
            blocks[part, half, pl.ds(pl.multiple_of(8 * pair, 8), 8), :] = value
            return carry

        lax.fori_loop(0, PART // 8, body, 0)

    def interpolate_and_send(part):
        for half in range(2):
            interpolate(part, half)
            if part == 0 and half == 0:
                pl.semaphore_wait(barrier, 2 * len(AROUND) + 2 + TARGETS)
            for step in AROUND:
                a_copy(part, step, half).start()

            @pl.when(core != half)
            def _():
                s_copy(part, half).start()

            @pl.when(core == half)
            def _():
                table[part, member] = blocks[part, half]

    def lane_pass(part):
        def body(pair, carry):
            high, low = load_split(part, pair)
            both = jnp.concatenate([high, low], axis=1)
            lanes[pl.ds(pl.multiple_of(8 * LON * pair, 8), 8 * LON), :] = dot(both, band[...])
            return carry

        lax.fori_loop(0, FLAT // 8, body, 0)

    def cols_of(part):
        lane = iota((LON, COL), 1)
        for half in range(2):
            edge = jnp.zeros((LON, COL), F32)
            for g in range(FLAT // 2):
                at = (half * (FLAT // 2) + g) * STRIDE + 8
                moved = pltpu.roll(frame[part, at : at + LON, :], 8 * g + HALO, 1)
                edge = jnp.where(jnp.logical_and(lane >= 8 * g, lane < 8 * g + 2 * HALO), moved, edge)
            turned[half, :, 0:LON] = jnp.transpose(edge)
        for side in range(2):
            for j in range(HALO):
                first = (1 - side) * HALO + j
                for half in range(2):
                    col_own[part, side, j, half * (FLAT // 2) : (half + 1) * (FLAT // 2), :] = turned[
                        half, pl.ds(first, FLAT // 2, stride=8), :
                    ]
            col_out[part, side, 0] = jnp.where(
                iota((FLAT, COL), 1) < COL // 2, col_own[part, side, 0], pltpu.roll(col_own[part, side, 1], COL // 2, 1)
            )
            col_out[part, side, 1] = col_own[part, side, 2]

    def emf_pass(part):
        for r in range(SHELLS):
            def field(q):
                at = (q * SHELLS + r) * STRIDE + 8
                return frame[part, at : at + LON, :]

            m, b = [field(MR + i) for i in range(3)], [field(BR + i) for i in range(3)]
            for i, form in enumerate((cross_radial, cross_polar, cross_azimuthal)):
                at = (i * SHELLS + r) * STRIDE + 8
                emf[at : at + LON, :] = form(m, b)
        for i, at in ((0, FLAT), (2, FLAT + SHELLS)):
            block = jnp.concatenate(
                [emf[(i * SHELLS + r) * STRIDE + 8 : (i * SHELLS + r) * STRIDE + 8 + LON, :] for r in range(SHELLS)],
                axis=0,
            )
            high, low = split(block)
            lanes[at * LON : (at + SHELLS) * LON, 0:COL] = dot(
                jnp.concatenate([high, low], axis=1), band[:, 0:COL]
            )

    def main_pass(part, start, stop):
        def body(block, carry):
            here = pl.multiple_of(8 * block, 8)

            def near(f, apart):
                return frame[part, pl.ds(f * STRIDE + 8 + here + apart, 8), :]

            def near_emf(f, apart):
                return emf[pl.ds(f * STRIDE + 8 + here + apart, 8), :]

            def lane_first(f):
                return lanes[pl.ds(f * LON + here, 8), 0:COL]

            def lane_second(f):
                return lanes[pl.ds(f * LON + here, 8), COL : 2 * COL]

            def row_first(at):
                return 45.0 * (at[1] - at[-1]) - 9.0 * (at[2] - at[-2]) + (at[3] - at[-3])

            def row_second(at, centre):
                return (
                    270.0 * (at[1] + at[-1]) - 27.0 * (at[2] + at[-2]) + 2.0 * (at[3] + at[-3]) - 490.0 * centre
                )

            centre = [[near(q * SHELLS + r, 0) for r in range(SHELLS)] for q in range(QUANTITIES)]
            radial = [shell_first(x) for x in centre]
            radial_second = [None if q == S else shell_second(centre[q]) for q in range(QUANTITIES)]
            emf_centre = [[near_emf(i * SHELLS + r, 0) for r in range(SHELLS)] for i in range(3)]
            emf_radial = [None, shell_first(emf_centre[1]), shell_first(emf_centre[2])]
            for r in range(SHELLS):
                own = [centre[q][r] for q in range(QUANTITIES)]
                g, lap = [], []
                for q in range(QUANTITIES):
                    f = q * SHELLS + r
                    at = {d: near(f, d) for d in (-3, -2, -1, 1, 2, 3)}
                    g.append((radial[q][r], lane_first(f), scale * row_first(at)))
                    if q == S:
                        lap.append(None)
                    else:
                        lap.append(
                            radial_second[q][r] + lane_second(f) + (scale * scale) * row_second(at, own[q])
                        )
                m, b = own[MR:BR], own[BR:WARM]

                def advect(q):
                    return m[0] * g[q][0] + m[1] * g[q][1] + m[2] * g[q][2]

                div = g[MR][0] + g[MT][1] + g[MP][2]
                current = (g[BP][1] - g[BT][2], g[BR][2] - g[BP][0], g[BT][0] - g[BR][1])
                lorentz = (
                    current[1] * b[2] - current[2] * b[1],
                    current[2] * b[0] - current[0] * b[2],
                    current[0] * b[1] - current[1] * b[0],
                )
                grow, thin = jnp.exp(own[WARM]), jnp.exp(-own[S])
                emf_rows = {}
                for i in (0, 1):
                    f = i * SHELLS + r
                    emf_rows[i] = scale * row_first({d: near_emf(f, d) for d in (-3, -2, -1, 1, 2, 3)})
                turn = (
                    lane_first(FLAT + SHELLS + r) - emf_rows[1],
                    emf_rows[0] - emf_radial[2][r],
                    emf_radial[1][r] - lane_first(FLAT + r),
                )
                result = [-advect(S) - div]
                for i in range(3):
                    result.append(
                        -advect(MR + i) - grow * (g[S][i] + g[WARM][i]) + thin * lorentz[i] + SPREAD * lap[MR + i]
                    )
                for i in range(3):
                    result.append(turn[i] + SPREAD * lap[BR + i])
                result.append(-advect(WARM) - (2.0 / 3.0) * div + SPREAD * lap[WARM])
                for q in range(QUANTITIES):
                    rate[pl.ds((q * SHELLS + r) * LON + here, 8), :] = result[q]
            return carry

        lax.fori_loop(start, stop, body, 0)

    def rows_of(part):
        for h in range(HALO):
            row_out[part, 0, h] = frame[part, pl.ds(8 + h, FLAT, stride=STRIDE), :]
            row_out[part, 1, h] = frame[part, pl.ds(8 + LON - HALO + h, FLAT, stride=STRIDE), :]

    def prepare_picks():
        for tile in range(2 * TILES):
            if tile < TARGETS:
                slot = idx_in[tile, 0:1, :]
            elif tile < TARGETS + 2:
                first = (tile - TARGETS) * GROUPS
                slot = idx_in[first, 1:2, :]
                for q in range(1, GROUPS):
                    slot = jnp.maximum(slot, pltpu.roll(idx_in[first + q], SPARE * q, 1)[1:2, :])
            else:
                side, h = divmod(tile - TARGETS - 2, HALO)
                slot = idx_in[side * (TARGETS - 1), 2 + h : 3 + h, :]
            slot = slot - mine * (GROUP * OUT)
            who = jnp.zeros_like(slot)
            for q in range(1, GROUP):
                who = who + jnp.where(slot >= q * OUT, 1, 0)
            cell = slot - who * OUT
            who = jnp.where(jnp.logical_and(slot >= 0, slot < GROUP * OUT), who, -1)
            at = (tile % 2) * COL
            owner[tile // 2, :, at : at + COL] = jnp.broadcast_to(who, (8, COL))
            hot = jnp.where(iota((SLOTS, COL), 0) == cell, 1.0, 0.0).astype(BF16)
            onehot[tile // 2, :, at : at + COL] = hot

    def table_split(part):
        high, low = split(table[part].reshape(GROUP * PART, SLOTS))
        return jnp.concatenate([high, low], axis=0)

    def pick(both, tile):
        value = dot(both, onehot[tile])
        value = value[0 : GROUP * PART] + value[GROUP * PART :]
        who = jnp.broadcast_to(owner[tile, 0:1, :], (PART, SLOTS))
        total = jnp.zeros((PART, SLOTS), F32)
        for q in range(GROUP):
            total = jnp.where(who == q, value[q * PART : (q + 1) * PART, :], total)
        return total[:, 0:COL], total[:, COL : 2 * COL]

    def pick_sides(part, both):
        rest = pick(both, TARGETS // 2)
        rest_rows[0], rest_rows[1] = rest
        spot = lax.div(iota((8, COL), 1), SPARE)
        for step in range(TARGETS // 2):
            tile = lax.rem(step + mine, TARGETS // 2)
            ends = pick(both, tile)
            rows = rest_rows[lax.div(tile, GROUPS // 2)]
            for i in range(2):
                target = 2 * tile + i
                there = lax.rem(target, GROUPS)
                total = jnp.zeros((8, COL), F32)
                for q in range(PART // 8):
                    moved = pltpu.roll(rows[8 * q : 8 * q + 8, :], SPARE * lax.rem(q + GROUPS - there, GROUPS), 1)
                    total = jnp.where(spot == q, moved, total)
                picked[part, target, 0:PART, :] = ends[i]
                picked[part, target, PART : PART + 8, :] = total
                b_copy(part, target).start()

    def pick_ends(part, both):
        ends = []
        for tile in range(TARGETS // 2 + 1, TILES):
            ends += pick(both, tile)
        for side in range(2):
            for h in range(HALO):
                picked_rows[part, side, h] = ends[side * HALO + h]
            l_copy(part, side).start()

    def corrections(part, halo_ref, own_ref, along_lanes):
        factor = None if along_lanes else scale

        def scaled(value, power):
            for _ in range(0 if along_lanes else power):
                value = factor * value
            return value

        for side in range(2):
            halo = [
                [halo_ref[side, h, q * SHELLS : (q + 1) * SHELLS, :] for q in range(QUANTITIES)] for h in range(HALO)
            ]
            form = cross_azimuthal if along_lanes else cross_polar
            halo_emf = [(cross_radial(x[MR:BR], x[BR:WARM]), form(x[MR:BR], x[BR:WARM])) for x in halo]
            sign = -1.0 if side == 0 else 1.0
            firsts, seconds = (45.0 * sign, -9.0 * sign, sign), (270.0, -27.0, 2.0)
            for j in range(HALO):
                own = [own_ref[part, side, j, q * SHELLS : (q + 1) * SHELLS, :] for q in range(QUANTITIES)]

                def total(weights, of):
                    result = None
                    for m in (1, 2, 3):
                        h = j + 3 - m if side == 0 else m - 3 + j
                        if 0 <= h < HALO:
                            term = weights[m - 1] * of(h)
                            result = term if result is None else result + term
                    return result

                d = [scaled(total(firsts, lambda h, q=q: halo[h][q]), 1) for q in range(QUANTITIES)]
                lap = [
                    None if q == S else scaled(total(seconds, lambda h, q=q: halo[h][q]), 2)
                    for q in range(QUANTITIES)
                ]
                radial = scaled(total(firsts, lambda h: halo_emf[h][0]), 1)
                second = scaled(total(firsts, lambda h: halo_emf[h][1]), 1)
                result = edge_rates(own, d, lap, second, radial, along_lanes)
                for q in range(QUANTITIES):
                    edge_add[side, j, q * SHELLS : (q + 1) * SHELLS, :] = result[q]

    def row_corrections(part):
        corrections(part, row_halo, row_out, False)
        for side in range(2):
            for j in range(HALO):
                rows = pl.ds(j if side == 0 else LON - HALO + j, FLAT, stride=LON)
                rate[rows, :] = rate[rows, :] + edge_add[side, j]

    def col_corrections(part):
        corrections(part, col_halo, col_own, True)
        for side in range(2):
            for j in range(HALO):
                for half in range(2):
                    turned[half, pl.ds((1 - side) * HALO + j, FLAT // 2, stride=8), :] = edge_add[
                        side, j, half * (FLAT // 2) : (half + 1) * (FLAT // 2), :
                    ]

    def finish(part):
        lane = iota((LON, COL), 1)
        border = jnp.logical_or(lane < HALO, lane >= COL - HALO)
        for half in range(2):
            edge = jnp.transpose(turned[half])[0:LON, :]
            for g in range(FLAT // 2):
                f = half * (FLAT // 2) + g
                added = jnp.where(border, pltpu.roll(edge, COL - 8 * g - HALO, 1), 0.0)
                change = (TIME_STEP / 60.0) * (rate[f * LON : (f + 1) * LON, :] + added)
                start = x_ref[f * LON : (f + 1) * LON, :]
                rows = slice(f * STRIDE + 8, f * STRIDE + 8 + LON)
                if part == 0:
                    frame[1, rows, :] = start + change
                else:
                    out_ref[f * LON : (f + 1) * LON, :] = 0.5 * (start + frame[1, rows, :] + change)

    def a_copy(part, step, half):
        return remote(
            blocks.at[part, half], table.at[part, member], a_send.at[part, half, step], a_recv.at[part, member],
            row_device(step, half),
        )

    def s_copy(part, half):
        return remote(
            blocks.at[part, half], table.at[part, member], s_send.at[part], a_recv.at[part, member], sibling
        )

    def a_arrival(part, step):
        there = lax.rem(member + step, GROUP)
        return remote(blocks.at[part, 0], table.at[part, there], s_send.at[part], a_recv.at[part, there], sibling)

    def b_copy(part, target):
        return remote(
            picked.at[part, target], got_cols.at[part, origin], b_send.at[part, target], b_recv.at[part, origin],
            target_device(target),
        )

    def b_arrival(part, source):
        return remote(
            picked.at[part, 0], got_cols.at[part, source], b_send.at[part, 0], b_recv.at[part, source],
            (other, lon, col),
        )

    def l_copy(part, side):
        return remote(
            picked_rows.at[part, side], got_rows.at[part, origin], l_send.at[part, side], l_recv.at[part, origin],
            target_device(side * (TARGETS - 1)),
        )

    def l_arrival(part, source):
        return remote(
            picked_rows.at[part, 0], got_rows.at[part, source], l_send.at[part, 0], l_recv.at[part, source],
            (other, lon, col),
        )

    def row_copy(part, side):
        return remote(
            row_out.at[part, 1 - side], row_in.at[part, side], r_send.at[part, side], r_recv.at[part, side],
            (panel, lon_up if side == 0 else lon_down, col),
        )

    def col_copy(part, side):
        return remote(
            col_out.at[part, 1 - side], col_in.at[part, side], c_send.at[part, side], c_recv.at[part, side],
            (panel, lon, col_up if side == 0 else col_down),
        )

    def idx_copy(target):
        return remote(
            idx_out, idx_in.at[origin], idx_send.at[target], idx_recv.at[origin], target_device(target)
        )

    def idx_arrival(source):
        return remote(idx_out, idx_in.at[source], idx_send.at[0], idx_recv.at[source], (other, lon, col))

    for part in range(2):
        interpolate_and_send(part)
        if part == 0:
            for target in range(TARGETS):
                idx_copy(target).start()
        rows_of(part)
        for side in range(2):
            row_copy(part, side).start()
        cols_of(part)
        for side in range(2):
            col_copy(part, side).start()
        if part == 0:
            for source in range(TARGETS):
                idx_arrival(source).wait_recv()
            prepare_picks()
        for step in range(1, GROUP):
            a_arrival(part, step).wait_recv()
        both = table_split(part)

        @pl.when(col_edge)
        def _():
            pick_sides(part, both)

        pick_ends(part, both)
        lane_pass(part)
        emf_pass(part)
        main_pass(part, 0, 6)
        for side in range(2):
            row_copy(part, side).wait_recv()
            col_copy(part, side).wait_recv()

        for side in range(2):
            at_edge = lon == (0 if side == 0 else n_lon - 1)

            @pl.when(at_edge)
            def _():
                for source in range(TARGETS):
                    l_arrival(part, source).wait_recv()
                for half in range(2):
                    total = got_rows[part, half * GROUPS]
                    for group in range(1, GROUPS):
                        total = total + got_rows[part, half * GROUPS + group]
                    row_halo[side, :, half * PART : (half + 1) * PART, :] = total

            @pl.when(jnp.logical_not(at_edge))
            def _():
                row_halo[side] = row_in[part, side]

        row_corrections(part)

        for side in range(2):
            at_edge = col == (0 if side == 0 else n_col - 1)

            @pl.when(at_edge)
            def _():
                for source in range(TARGETS):
                    b_arrival(part, source).wait_recv()
                for half in range(2):
                    total = got_cols[part, half * GROUPS]
                    for group in range(1, GROUPS):
                        total = total + got_cols[part, half * GROUPS + group]
                    main, rest = total[0:PART], total[PART : PART + 8]
                    rows = slice(half * PART, (half + 1) * PART)
                    col_halo[side, 0, rows, :] = main
                    col_halo[side, 1, rows, :] = pltpu.roll(main, COL - LON, 1)
                    main = pltpu.roll(main, COL - 2 * LON, 1)
                    for q in range(PART // 8):
                        at = half * PART + 8 * q
                        col_halo[side, 2, at : at + 8, :] = jnp.where(
                            iota((8, COL), 1) < COL - 2 * LON,
                            main[8 * q : 8 * q + 8, :],
                            pltpu.roll(rest, (COL + COL - 2 * LON - SPARE * q) % COL, 1),
                        )

            @pl.when(jnp.logical_not(at_edge))
            def _():
                pair = col_in[part, side, 0]
                col_halo[side, 0] = pair
                col_halo[side, 1] = pltpu.roll(pair, COL // 2, 1)
                col_halo[side, 2] = col_in[part, side, 1]

        col_corrections(part)
        finish(part)

    for target in range(TARGETS):
        idx_copy(target).wait_send()
    for part in range(2):
        for half in range(2):
            for step in AROUND:
                a_copy(part, step, half).wait_send()
        s_copy(part, 0).wait_send()
        for side in range(2):
            row_copy(part, side).wait_send()
            col_copy(part, side).wait_send()
            l_copy(part, side).wait_send()

        @pl.when(col_edge)
        def _():
            for target in range(TARGETS):
                b_copy(part, target).wait_send()


def inverse_sine(start, count, total):
    place = (start + jnp.arange(count, dtype=jnp.int32)).astype(jnp.float32)
    colatitude = math.pi / 4.0 + (place + 0.5) * (math.pi / 2.0 / total)
    return 1.0 / jnp.sin(colatitude)


def shards(state, send_base, send_frac, recv_slots):
    rows = FLAT * LON
    scale = inverse_sine(lax.axis_index("colat") * COL, COL, COL * lax.axis_size("colat"))[None]
    base = jnp.pad(send_base[0], ((0, 0), (0, SLOTS - OUT)))
    frac = jnp.pad(send_frac[0, 0], ((0, 0), (0, SLOTS - OUT)))
    dma = pltpu.SemaphoreType.DMA
    vmem = pltpu.VMEM
    scratch = [
        vmem((2, FLAT * STRIDE, COL), F32),
        vmem((3 * SHELLS * STRIDE, COL), F32),
        vmem(((FLAT + 2 * SHELLS) * LON, 2 * COL), F32),
        vmem((rows, COL), F32),
        vmem((3 * COL, SLOTS), BF16),
        vmem((LON, SLOTS), F32),
        vmem((2 * COL, 2 * COL), BF16),
        vmem((TILES, SLOTS, 2 * COL), BF16),
        vmem((TILES, 8, 2 * COL), I32),
        vmem((2, COL, COL), F32),
        vmem((2, 2, PART, SLOTS), F32),
        vmem((2, GROUP, PART, SLOTS), F32),
        vmem((8, COL), I32),
        vmem((TARGETS, 8, COL), I32),
        vmem((2, PART, COL), F32),
        vmem((2, TARGETS, PART + 8, COL), F32),
        vmem((2, 2, HALO, PART, COL), F32),
        vmem((2, TARGETS, PART + 8, COL), F32),
        vmem((2, TARGETS, HALO, PART, COL), F32),
        vmem((2, 2, HALO, FLAT, COL), F32),
        vmem((2, 2, HALO, FLAT, COL), F32),
        vmem((2, 2, HALO, FLAT, COL), F32),
        vmem((2, 2, 2, FLAT, COL), F32),
        vmem((2, 2, 2, FLAT, COL), F32),
        vmem((2, HALO, FLAT, COL), F32),
        vmem((2, HALO, FLAT, COL), F32),
        vmem((2, HALO, FLAT, COL), F32),
        dma((TARGETS,)),
        dma((TARGETS,)),
        dma((2, 2, RING)),
        dma((2, GROUP)),
        dma((2,)),
        dma((2, TARGETS)),
        dma((2, TARGETS)),
        dma((2, 2)),
        dma((2, TARGETS)),
        dma((2, 2)),
        dma((2, 2)),
        dma((2, 2)),
        dma((2, 2)),
    ]
    result = pl.pallas_call(
        kernel,
        out_shape=jax.ShapeDtypeStruct((rows, COL), F32),
        in_specs=[pl.BlockSpec(memory_space=pltpu.VMEM)] * 5,
        out_specs=pl.BlockSpec(memory_space=pltpu.VMEM),
        scratch_shapes=scratch,
        compiler_params=pltpu.CompilerParams(
            collective_id=0, has_side_effects=True, vmem_limit_bytes=40 * 1024 * 1024
        ),
    )(state.reshape(rows, COL), base, frac, recv_slots[0], scale)
    return result.reshape(state.shape)


def solution(mesh):
    placed = (
        P("panel", None, None, "lon", "colat"),
        P("panel", ("lon", "colat"), None),
        P("panel", ("lon", "colat"), None, None),
        P("panel", ("lon", "colat"), None),
    )
    return jax.shard_map(
        shards,
        mesh=mesh,
        in_specs=placed,
        out_specs=P("panel", None, None, "lon", "colat"),
        check_vma=False,
    )
```

```python
import math

import jax
import jax.numpy as jnp
from jax import lax
from jax.experimental import pallas as pl
from jax.experimental.pallas import tpu as pltpu
from jax.sharding import PartitionSpec as P

MESH = pl.DeviceIdType.MESH
F32, BF16, I32 = jnp.float32, jnp.bfloat16, jnp.int32

QUANTITIES = 8
SHELLS = 4
FLAT = QUANTITIES * SHELLS
LON = 48
COL = 128
HALO = 3
OUT = 240
SIDE = HALO * LON
SLOTS = 256
GROUP = 8
GROUPS = 8
AROUND = (1, 3, 2)
SPARE = SIDE - COL
PART = FLAT // 2
TARGETS = 2 * GROUPS
TILES = 12
RING = 4
STRIDE = LON + 16
TIME_STEP = 0.25
SPREAD = 0.1 / 3.0
S, MR, MT, MP, BR, BT, BP, WARM = range(QUANTITIES)


def dot(left, right):
    return jnp.dot(left, right, preferred_element_type=F32)


def split(value):
    high = value.astype(BF16)
    return high, (value - high.astype(F32)).astype(BF16)


def iota(shape, dim):
    return lax.broadcasted_iota(I32, shape, dim)


def cross_radial(m, b):
    return m[1] * b[2] - m[2] * b[1]


def cross_polar(m, b):
    return m[2] * b[0] - m[0] * b[2]


def cross_azimuthal(m, b):
    return m[0] * b[1] - m[1] * b[0]


def edge_rates(own, d, lap, emf_first, emf_second, along_lanes):
    grow, thin = jnp.exp(own[WARM]), jnp.exp(-own[S])
    b = own[BR:WARM]
    if along_lanes:
        vel, out = own[MT], MT
        lorentz = (d[BR] * b[1], -d[BR] * b[0] - d[BP] * b[2], d[BP] * b[1])
        turn = (emf_first, None, -emf_second)
    else:
        vel, out = own[MP], MP
        lorentz = (d[BR] * b[2], d[BT] * b[2], -d[BT] * b[1] - d[BR] * b[0])
        turn = (-emf_first, emf_second, None)
    result = [-vel * d[S] - d[out]]
    for i in range(3):
        rate = -vel * d[MR + i] + thin * lorentz[i] + SPREAD * lap[MR + i]
        if MR + i == out:
            rate = rate - grow * (d[S] + d[WARM])
        result.append(rate)
    for i in range(3):
        rate = SPREAD * lap[BR + i]
        result.append(rate if turn[i] is None else rate + turn[i])
    result.append(-vel * d[WARM] - (2.0 / 3.0) * d[out] + SPREAD * lap[WARM])
    return result


def shell_first(x):
    a, b = 8.0 * (x[3] - x[0]), 45.0
    return (
        b * (x[1] - x[0]) - 9.0 * (x[2] - x[0]) + (x[3] - x[0]),
        b * (x[2] - x[0]) - a,
        b * (x[3] - x[1]) - a,
        b * (x[3] - x[2]) - 9.0 * (x[3] - x[1]) + (x[3] - x[0]),
    )


def shell_second(x):
    return (
        2.0 * x[3] - 27.0 * x[2] + 270.0 * x[1] - 245.0 * x[0],
        245.0 * x[0] - 490.0 * x[1] + 270.0 * x[2] - 25.0 * x[3],
        245.0 * x[3] - 490.0 * x[2] + 270.0 * x[1] - 25.0 * x[0],
        2.0 * x[0] - 27.0 * x[1] + 270.0 * x[2] - 245.0 * x[3],
    )


def kernel(
    x_hbm, base_hbm, frac_hbm, slots_hbm, scale_ref, out_ref,
    deep, base_ref, frac_ref, slots_ref, emf, lanes, rate, mix, rows_mix, band, onehot, owner, turned,
    blocks, table, idx_out, idx_in, rest_rows, picked, picked_rows, got_cols, got_rows, row_out, row_in, col_own, col_out, col_in,
    row_halo, col_halo, edge_add,
    in_sem, idx_send, idx_recv, a_send, a_recv, s_send, b_send, b_recv, l_send, l_recv, r_send, r_recv, c_send, c_recv,
):
    panel, lon, col = lax.axis_index("panel"), lax.axis_index("lon"), lax.axis_index("colat")
    n_lon, n_col = lax.axis_size("lon"), lax.axis_size("colat")
    core, mine = lon & 1, lon >> 1
    member = core * n_col + col
    other = 1 - panel
    lon_up, lon_down = lax.rem(lon + 1, n_lon), lax.rem(lon + n_lon - 1, n_lon)
    col_up, col_down = lax.rem(col + 1, n_col), lax.rem(col + n_col - 1, n_col)
    outer = lax.rem(lon + 2 * core - 1 + n_lon, n_lon)
    col_edge = jnp.logical_or(col == 0, col == n_col - 1)
    lon_edge = jnp.logical_or(lon == 0, lon == n_lon - 1)

    sibling = (panel, lon + 1 - 2 * core, col)
    origin = core * GROUPS + mine

    def row_device(step, half):
        return (panel, 2 * mine + half, (col + step) & (n_col - 1))

    def target_device(target):
        return (other, 2 * (target & (GROUPS - 1)) + (target >> 3), col)

    def remote(src, dst, send, recv, device):
        return pltpu.make_async_remote_copy(
            src_ref=src, dst_ref=dst, send_sem=send, recv_sem=recv, device_id=device, device_id_type=MESH
        )

    frame = deep.reshape(2, FLAT * STRIDE, COL)
    copies = [
        pltpu.make_async_copy(src, dst, in_sem.at[i])
        for i, (src, dst) in enumerate(
            (
                (frac_hbm, frac_ref),
                (base_hbm, base_ref),
                (slots_hbm, slots_ref),
                (x_hbm, deep.at[0, :, pl.ds(8, LON), :]),
            )
        )
    ]
    for copy in copies:
        copy.start()

    barrier = pltpu.get_barrier_semaphore()
    for step in AROUND:
        for half in range(2):
            pl.semaphore_signal(barrier, inc=1, device_id=row_device(step, half), device_id_type=MESH)
    pl.semaphore_signal(barrier, inc=1, device_id=sibling, device_id_type=MESH)
    for target in range(TARGETS):
        pl.semaphore_signal(barrier, inc=1, device_id=target_device(target), device_id_type=MESH)
    pl.semaphore_signal(barrier, inc=1, device_id=(panel, outer, col), device_id_type=MESH)

    zero_rows = jnp.zeros((8, COL), F32)
    for f in range(FLAT):
        for part in range(2):
            frame[part, f * STRIDE : f * STRIDE + 8, :] = zero_rows
            frame[part, f * STRIDE + 8 + LON : (f + 1) * STRIDE, :] = zero_rows
    for f in range(3 * SHELLS):
        emf[f * STRIDE : f * STRIDE + 8, :] = zero_rows
        emf[f * STRIDE + 8 + LON : (f + 1) * STRIDE, :] = zero_rows

    for half in range(2):
        turned[half, :, :] = jnp.zeros((COL, COL), F32)

    apart = iota((COL, COL), 0) - iota((COL, COL), 1)
    reach = jnp.abs(apart)
    first = jnp.where(reach == 1, 45.0, jnp.where(reach == 2, -9.0, jnp.where(reach == 3, 1.0, 0.0)))
    first = jnp.where(apart < 0, -first, first).astype(BF16)
    second = jnp.where(
        reach == 0, -490.0, jnp.where(reach == 1, 270.0, jnp.where(reach == 2, -27.0, jnp.where(reach == 3, 2.0, 0.0)))
    ).astype(BF16)
    for part in range(2):
        band[part * COL : (part + 1) * COL, 0:COL] = first
        band[part * COL : (part + 1) * COL, COL : 2 * COL] = second

    copies[0].wait()
    copies[1].wait()
    base = jnp.concatenate([base_ref[...], jnp.zeros((1, SLOTS - OUT), I32)], axis=1)
    base_row, base_col = lax.div(base, COL), lax.rem(base, COL)
    share = jnp.concatenate([frac_ref[...], jnp.zeros((2, SLOTS - OUT), F32)], axis=1)
    along, across = share[0:1, :], share[1:2, :]
    cells = iota((COL, SLOTS), 0)
    weight = jnp.where(cells == base_col, 1.0 - across, 0.0) + jnp.where(cells == base_col + 1, across, 0.0)
    weight_high, weight_low = split(weight)
    mix[0:COL, :] = weight_high
    mix[COL : 2 * COL, :] = weight_high
    mix[2 * COL : 3 * COL, :] = weight_low
    cells = iota((LON, SLOTS), 0)
    rows_mix[...] = jnp.where(cells == base_row, 1.0 - along, 0.0) + jnp.where(cells == base_row + 1, along, 0.0)

    copies[2].wait()
    spot = iota((1, SLOTS), 1)
    sides = jnp.where(spot < SIDE, jnp.maximum(slots_ref[:, 0:SLOTS], slots_ref[:, SIDE : SIDE + SLOTS]) + 1, 0)
    digits = jnp.concatenate([lax.div(sides, COL), lax.rem(sides, COL), jnp.zeros((6, SLOTS), I32)], axis=0)
    source, target = iota((SLOTS, SLOTS), 0), iota((SLOTS, SLOTS), 1)
    layer = jnp.where(target >= LON, 1, 0) + jnp.where(target >= 2 * LON, 1, 0)
    order = jnp.logical_and(target < SIDE, source == HALO * (target - LON * layer) + layer)
    digits = dot(digits.astype(F32).astype(BF16), jnp.where(order, 1.0, 0.0).astype(BF16)).astype(I32)
    sides = digits[0:1, :] * COL + digits[1:2, :] - 1
    idx_out[0:1, :] = sides[:, 0:COL]
    idx_out[1:2, :] = sides[:, COL : 2 * COL]
    for h in range(HALO):
        at = 2 * SIDE + h * COL
        idx_out[2 + h : 3 + h, :] = jnp.maximum(
            slots_ref[:, at : at + COL], slots_ref[:, at + HALO * COL : at + HALO * COL + COL]
        )
    idx_out[5:8, :] = jnp.full((3, COL), -1, I32)

    scale = scale_ref[...]
    copies[3].wait()

    def load_split(part, pair):
        block = jnp.concatenate(
            [frame[part, pl.ds(pl.multiple_of((8 * pair + q) * STRIDE + 8, 8), LON), :] for q in range(8)], axis=0
        )
        return split(block)

    def interpolate(part, half):
        for pair in range(PART // 8):
            high, low = load_split(part, 2 * half + pair)
            value = dot(jnp.concatenate([high, low, high], axis=1), mix[...])
            value = jnp.sum(value.reshape(8, LON, SLOTS) * rows_mix[...][None], axis=1)
            blocks[part, half, 8 * pair : 8 * pair + 8, :] = value

    def interpolate_and_send(part):
        for half in range(2):
            interpolate(part, half)
            if part == 0 and half == 0:
                pl.semaphore_wait(barrier, 2 * len(AROUND) + 2 + TARGETS)
            for step in AROUND:
                a_copy(part, step, half).start()

            @pl.when(core != half)
            def _():
                s_copy(part, half).start()

            @pl.when(core == half)
            def _():
                table[part, member] = blocks[part, half]

    def lane_pass(part):
        def body(pair, carry):
            high, low = load_split(part, pair)
            both = jnp.concatenate([high, low], axis=1)
            lanes[pl.ds(pl.multiple_of(8 * LON * pair, 8), 8 * LON), :] = dot(both, band[...])
            return carry

        lax.fori_loop(0, FLAT // 8, body, 0)

    def cols_of(part):
        lane = iota((LON, COL), 1)
        for half in range(2):
            edge = jnp.zeros((LON, COL), F32)
            for g in range(FLAT // 2):
                at = (half * (FLAT // 2) + g) * STRIDE + 8
                moved = pltpu.roll(frame[part, at : at + LON, :], 8 * g + HALO, 1)
                edge = jnp.where(jnp.logical_and(lane >= 8 * g, lane < 8 * g + 2 * HALO), moved, edge)
            turned[half, :, 0:LON] = jnp.transpose(edge)
        for side in range(2):
            for j in range(HALO):
                first = (1 - side) * HALO + j
                for half in range(2):
                    col_own[part, side, j, half * (FLAT // 2) : (half + 1) * (FLAT // 2), :] = turned[
                        half, pl.ds(first, FLAT // 2, stride=8), :
                    ]
            col_out[part, side, 0] = jnp.where(
                iota((FLAT, COL), 1) < COL // 2, col_own[part, side, 0], pltpu.roll(col_own[part, side, 1], COL // 2, 1)
            )
            col_out[part, side, 1] = col_own[part, side, 2]

    def emf_pass(part):
        for r in range(SHELLS):
            def field(q):
                at = (q * SHELLS + r) * STRIDE + 8
                return frame[part, at : at + LON, :]

            m, b = [field(MR + i) for i in range(3)], [field(BR + i) for i in range(3)]
            for i, form in enumerate((cross_radial, cross_polar, cross_azimuthal)):
                at = (i * SHELLS + r) * STRIDE + 8
                emf[at : at + LON, :] = form(m, b)
        for i, at in ((0, FLAT), (2, FLAT + SHELLS)):
            block = jnp.concatenate(
                [emf[(i * SHELLS + r) * STRIDE + 8 : (i * SHELLS + r) * STRIDE + 8 + LON, :] for r in range(SHELLS)],
                axis=0,
            )
            high, low = split(block)
            lanes[at * LON : (at + SHELLS) * LON, 0:COL] = dot(
                jnp.concatenate([high, low], axis=1), band[:, 0:COL]
            )

    def main_pass(part, start, stop):
        def body(block, carry):
            here = pl.multiple_of(8 * block, 8)

            def near(f, apart):
                return frame[part, pl.ds(f * STRIDE + 8 + here + apart, 8), :]

            def near_emf(f, apart):
                return emf[pl.ds(f * STRIDE + 8 + here + apart, 8), :]

            def lane_first(f):
                return lanes[pl.ds(f * LON + here, 8), 0:COL]

            def lane_second(f):
                return lanes[pl.ds(f * LON + here, 8), COL : 2 * COL]

            def row_first(at):
                return 45.0 * (at[1] - at[-1]) - 9.0 * (at[2] - at[-2]) + (at[3] - at[-3])

            def row_second(at, centre):
                return (
                    270.0 * (at[1] + at[-1]) - 27.0 * (at[2] + at[-2]) + 2.0 * (at[3] + at[-3]) - 490.0 * centre
                )

            centre = [[near(q * SHELLS + r, 0) for r in range(SHELLS)] for q in range(QUANTITIES)]
            radial = [shell_first(x) for x in centre]
            radial_second = [None if q == S else shell_second(centre[q]) for q in range(QUANTITIES)]
            emf_centre = [[near_emf(i * SHELLS + r, 0) for r in range(SHELLS)] for i in range(3)]
            emf_radial = [None, shell_first(emf_centre[1]), shell_first(emf_centre[2])]
            for r in range(SHELLS):
                own = [centre[q][r] for q in range(QUANTITIES)]
                g, lap = [], []
                for q in range(QUANTITIES):
                    f = q * SHELLS + r
                    at = {d: near(f, d) for d in (-3, -2, -1, 1, 2, 3)}
                    g.append((radial[q][r], lane_first(f), scale * row_first(at)))
                    if q == S:
                        lap.append(None)
                    else:
                        lap.append(
                            radial_second[q][r] + lane_second(f) + (scale * scale) * row_second(at, own[q])
                        )
                m, b = own[MR:BR], own[BR:WARM]

                def advect(q):
                    return m[0] * g[q][0] + m[1] * g[q][1] + m[2] * g[q][2]

                div = g[MR][0] + g[MT][1] + g[MP][2]
                current = (g[BP][1] - g[BT][2], g[BR][2] - g[BP][0], g[BT][0] - g[BR][1])
                lorentz = (
                    current[1] * b[2] - current[2] * b[1],
                    current[2] * b[0] - current[0] * b[2],
                    current[0] * b[1] - current[1] * b[0],
                )
                grow, thin = jnp.exp(own[WARM]), jnp.exp(-own[S])
                emf_rows = {}
                for i in (0, 1):
                    f = i * SHELLS + r
                    emf_rows[i] = scale * row_first({d: near_emf(f, d) for d in (-3, -2, -1, 1, 2, 3)})
                turn = (
                    lane_first(FLAT + SHELLS + r) - emf_rows[1],
                    emf_rows[0] - emf_radial[2][r],
                    emf_radial[1][r] - lane_first(FLAT + r),
                )
                result = [-advect(S) - div]
                for i in range(3):
                    result.append(
                        -advect(MR + i) - grow * (g[S][i] + g[WARM][i]) + thin * lorentz[i] + SPREAD * lap[MR + i]
                    )
                for i in range(3):
                    result.append(turn[i] + SPREAD * lap[BR + i])
                result.append(-advect(WARM) - (2.0 / 3.0) * div + SPREAD * lap[WARM])
                for q in range(QUANTITIES):
                    rate[pl.ds((q * SHELLS + r) * LON + here, 8), :] = result[q]
            return carry

        lax.fori_loop(start, stop, body, 0)

    def rows_of(part):
        for h in range(HALO):
            row_out[part, 0, h] = frame[part, pl.ds(8 + h, FLAT, stride=STRIDE), :]
            row_out[part, 1, h] = frame[part, pl.ds(8 + LON - HALO + h, FLAT, stride=STRIDE), :]

    def prepare_picks():
        for tile in range(2 * TILES):
            if tile < TARGETS:
                slot = idx_in[tile, 0:1, :]
            elif tile < TARGETS + 2:
                first = (tile - TARGETS) * GROUPS
                slot = idx_in[first, 1:2, :]
                for q in range(1, GROUPS):
                    slot = jnp.maximum(slot, pltpu.roll(idx_in[first + q], SPARE * q, 1)[1:2, :])
            else:
                side, h = divmod(tile - TARGETS - 2, HALO)
                slot = idx_in[side * (TARGETS - 1), 2 + h : 3 + h, :]
            slot = slot - mine * (GROUP * OUT)
            who = jnp.zeros_like(slot)
            for q in range(1, GROUP):
                who = who + jnp.where(slot >= q * OUT, 1, 0)
            cell = slot - who * OUT
            who = jnp.where(jnp.logical_and(slot >= 0, slot < GROUP * OUT), who, -1)
            at = (tile % 2) * COL
            owner[tile // 2, :, at : at + COL] = jnp.broadcast_to(who, (8, COL))
            hot = jnp.where(iota((SLOTS, COL), 0) == cell, 1.0, 0.0).astype(BF16)
            onehot[tile // 2, :, at : at + COL] = hot

    def table_split(part):
        high, low = split(table[part].reshape(GROUP * PART, SLOTS))
        return jnp.concatenate([high, low], axis=0)

    def pick(both, tile):
        value = dot(both, onehot[tile])
        value = value[0 : GROUP * PART] + value[GROUP * PART :]
        who = jnp.broadcast_to(owner[tile, 0:1, :], (PART, SLOTS))
        total = jnp.zeros((PART, SLOTS), F32)
        for q in range(GROUP):
            total = jnp.where(who == q, value[q * PART : (q + 1) * PART, :], total)
        return total[:, 0:COL], total[:, COL : 2 * COL]

    def pick_sides(part, both):
        rest = pick(both, TARGETS // 2)
        rest_rows[0], rest_rows[1] = rest
        spot = lax.div(iota((8, COL), 1), SPARE)
        for step in range(TARGETS // 2):
            tile = (step + mine) & (TARGETS // 2 - 1)
            ends = pick(both, tile)
            rows = rest_rows[tile >> 2]
            for i in range(2):
                target = 2 * tile + i
                there = target & (GROUPS - 1)
                total = jnp.zeros((8, COL), F32)
                for q in range(PART // 8):
                    moved = pltpu.roll(rows[8 * q : 8 * q + 8, :], SPARE * ((q + GROUPS - there) & (GROUPS - 1)), 1)
                    total = jnp.where(spot == q, moved, total)
                picked[part, target, 0:PART, :] = ends[i]
                picked[part, target, PART : PART + 8, :] = total
                b_copy(part, target).start()

    def pick_ends(part, both):
        ends = []
        for tile in range(TARGETS // 2 + 1, TILES):
            ends += pick(both, tile)
        for side in range(2):
            for h in range(HALO):
                picked_rows[part, side, h] = ends[side * HALO + h]
            l_copy(part, side).start()

    def corrections(part, halo_ref, own_ref, along_lanes):
        factor = None if along_lanes else scale

        def scaled(value, power):
            for _ in range(0 if along_lanes else power):
                value = factor * value
            return value

        for side in range(2):
            halo = [
                [halo_ref[side, h, q * SHELLS : (q + 1) * SHELLS, :] for q in range(QUANTITIES)] for h in range(HALO)
            ]
            form = cross_azimuthal if along_lanes else cross_polar
            halo_emf = [(cross_radial(x[MR:BR], x[BR:WARM]), form(x[MR:BR], x[BR:WARM])) for x in halo]
            sign = -1.0 if side == 0 else 1.0
            firsts, seconds = (45.0 * sign, -9.0 * sign, sign), (270.0, -27.0, 2.0)
            for j in range(HALO):
                own = [own_ref[part, side, j, q * SHELLS : (q + 1) * SHELLS, :] for q in range(QUANTITIES)]

                def total(weights, of):
                    result = None
                    for m in (1, 2, 3):
                        h = j + 3 - m if side == 0 else m - 3 + j
                        if 0 <= h < HALO:
                            term = weights[m - 1] * of(h)
                            result = term if result is None else result + term
                    return result

                d = [scaled(total(firsts, lambda h, q=q: halo[h][q]), 1) for q in range(QUANTITIES)]
                lap = [
                    None if q == S else scaled(total(seconds, lambda h, q=q: halo[h][q]), 2)
                    for q in range(QUANTITIES)
                ]
                radial = scaled(total(firsts, lambda h: halo_emf[h][0]), 1)
                second = scaled(total(firsts, lambda h: halo_emf[h][1]), 1)
                result = edge_rates(own, d, lap, second, radial, along_lanes)
                for q in range(QUANTITIES):
                    edge_add[side, j, q * SHELLS : (q + 1) * SHELLS, :] = result[q]

    def row_corrections(part):
        corrections(part, row_halo, row_out, False)
        for side in range(2):
            for j in range(HALO):
                rows = pl.ds(j if side == 0 else LON - HALO + j, FLAT, stride=LON)
                rate[rows, :] = rate[rows, :] + edge_add[side, j]

    def col_corrections(part):
        corrections(part, col_halo, col_own, True)
        for side in range(2):
            for j in range(HALO):
                for half in range(2):
                    turned[half, pl.ds((1 - side) * HALO + j, FLAT // 2, stride=8), :] = edge_add[
                        side, j, half * (FLAT // 2) : (half + 1) * (FLAT // 2), :
                    ]

    def finish(part):
        lane = iota((LON, COL), 1)
        border = jnp.logical_or(lane < HALO, lane >= COL - HALO)
        for half in range(2):
            edge = jnp.transpose(turned[half])[0:LON, :]
            for g in range(FLAT // 2):
                f = half * (FLAT // 2) + g
                added = jnp.where(border, pltpu.roll(edge, COL - 8 * g - HALO, 1), 0.0)
                change = (TIME_STEP / 60.0) * (rate[f * LON : (f + 1) * LON, :] + added)
                rows = slice(f * STRIDE + 8, f * STRIDE + 8 + LON)
                start = frame[0, rows, :]
                if part == 0:
                    frame[1, rows, :] = start + change
                else:
                    out_ref[f * LON : (f + 1) * LON, :] = 0.5 * (start + frame[1, rows, :] + change)

    def a_copy(part, step, half):
        return remote(
            blocks.at[part, half], table.at[part, member], a_send.at[part, half, step], a_recv.at[part, member],
            row_device(step, half),
        )

    def s_copy(part, half):
        return remote(
            blocks.at[part, half], table.at[part, member], s_send.at[part], a_recv.at[part, member], sibling
        )

    def a_arrival(part, step):
        there = (member + step) & (GROUP - 1)
        return remote(blocks.at[part, 0], table.at[part, there], s_send.at[part], a_recv.at[part, there], sibling)

    def b_copy(part, target):
        return remote(
            picked.at[part, target], got_cols.at[part, origin], b_send.at[part, target], b_recv.at[part, origin],
            target_device(target),
        )

    def b_arrival(part, source):
        return remote(
            picked.at[part, 0], got_cols.at[part, source], b_send.at[part, 0], b_recv.at[part, source],
            (other, lon, col),
        )

    def l_copy(part, side):
        return remote(
            picked_rows.at[part, side], got_rows.at[part, origin], l_send.at[part, side], l_recv.at[part, origin],
            target_device(side * (TARGETS - 1)),
        )

    def l_arrival(part, source):
        return remote(
            picked_rows.at[part, 0], got_rows.at[part, source], l_send.at[part, 0], l_recv.at[part, source],
            (other, lon, col),
        )

    def row_copy(part, side):
        return remote(
            row_out.at[part, 1 - side], row_in.at[part, side], r_send.at[part, side], r_recv.at[part, side],
            (panel, lon_up if side == 0 else lon_down, col),
        )

    def col_copy(part, side):
        return remote(
            col_out.at[part, 1 - side], col_in.at[part, side], c_send.at[part, side], c_recv.at[part, side],
            (panel, lon, col_up if side == 0 else col_down),
        )

    def idx_copy(target):
        return remote(
            idx_out, idx_in.at[origin], idx_send.at[target], idx_recv.at[origin], target_device(target)
        )

    def idx_arrival(source):
        return remote(idx_out, idx_in.at[source], idx_send.at[0], idx_recv.at[source], (other, lon, col))

    for part in range(2):
        interpolate_and_send(part)
        if part == 0:
            for target in range(TARGETS):
                idx_copy(target).start()
        rows_of(part)
        for side in range(2):
            row_copy(part, side).start()
        cols_of(part)
        for side in range(2):
            col_copy(part, side).start()
        if part == 0:
            for source in range(TARGETS):
                idx_arrival(source).wait_recv()
            prepare_picks()
        for step in range(1, GROUP):
            a_arrival(part, step).wait_recv()
        both = table_split(part)

        @pl.when(col_edge)
        def _():
            pick_sides(part, both)

        pick_ends(part, both)
        lane_pass(part)
        emf_pass(part)
        main_pass(part, 0, 6)
        for side in range(2):
            row_copy(part, side).wait_recv()
            col_copy(part, side).wait_recv()

        for side in range(2):
            at_edge = lon == (0 if side == 0 else n_lon - 1)

            @pl.when(at_edge)
            def _():
                for source in range(TARGETS):
                    l_arrival(part, source).wait_recv()
                for half in range(2):
                    total = got_rows[part, half * GROUPS]
                    for group in range(1, GROUPS):
                        total = total + got_rows[part, half * GROUPS + group]
                    row_halo[side, :, half * PART : (half + 1) * PART, :] = total

            @pl.when(jnp.logical_not(at_edge))
            def _():
                row_halo[side] = row_in[part, side]

        row_corrections(part)

        for side in range(2):
            at_edge = col == (0 if side == 0 else n_col - 1)

            @pl.when(at_edge)
            def _():
                for source in range(TARGETS):
                    b_arrival(part, source).wait_recv()
                for half in range(2):
                    total = got_cols[part, half * GROUPS]
                    for group in range(1, GROUPS):
                        total = total + got_cols[part, half * GROUPS + group]
                    main, rest = total[0:PART], total[PART : PART + 8]
                    rows = slice(half * PART, (half + 1) * PART)
                    col_halo[side, 0, rows, :] = main
                    col_halo[side, 1, rows, :] = pltpu.roll(main, COL - LON, 1)
                    main = pltpu.roll(main, COL - 2 * LON, 1)
                    for q in range(PART // 8):
                        at = half * PART + 8 * q
                        col_halo[side, 2, at : at + 8, :] = jnp.where(
                            iota((8, COL), 1) < COL - 2 * LON,
                            main[8 * q : 8 * q + 8, :],
                            pltpu.roll(rest, (COL + COL - 2 * LON - SPARE * q) % COL, 1),
                        )

            @pl.when(jnp.logical_not(at_edge))
            def _():
                pair = col_in[part, side, 0]
                col_halo[side, 0] = pair
                col_halo[side, 1] = pltpu.roll(pair, COL // 2, 1)
                col_halo[side, 2] = col_in[part, side, 1]

        col_corrections(part)
        finish(part)

    for target in range(TARGETS):
        idx_copy(target).wait_send()
    for part in range(2):
        for half in range(2):
            for step in AROUND:
                a_copy(part, step, half).wait_send()
        s_copy(part, 0).wait_send()
        for side in range(2):
            row_copy(part, side).wait_send()
            col_copy(part, side).wait_send()
            l_copy(part, side).wait_send()

        @pl.when(col_edge)
        def _():
            for target in range(TARGETS):
                b_copy(part, target).wait_send()


def inverse_sine(start, count, total):
    place = (start + jnp.arange(count, dtype=jnp.int32)).astype(jnp.float32)
    colatitude = math.pi / 4.0 + (place + 0.5) * (math.pi / 2.0 / total)
    return 1.0 / jnp.sin(colatitude)


def shards(state, send_base, send_frac, recv_slots):
    rows = FLAT * LON
    scale = inverse_sine(lax.axis_index("colat") * COL, COL, COL * lax.axis_size("colat"))[None]
    dma = pltpu.SemaphoreType.DMA
    vmem = pltpu.VMEM
    scratch = [
        vmem((2, FLAT, STRIDE, COL), F32),
        vmem((1, OUT), I32),
        vmem((2, OUT), F32),
        vmem((1, recv_slots.shape[-1]), I32),
        vmem((3 * SHELLS * STRIDE, COL), F32),
        vmem(((FLAT + 2 * SHELLS) * LON, 2 * COL), F32),
        vmem((rows, COL), F32),
        vmem((3 * COL, SLOTS), BF16),
        vmem((LON, SLOTS), F32),
        vmem((2 * COL, 2 * COL), BF16),
        vmem((TILES, SLOTS, 2 * COL), BF16),
        vmem((TILES, 8, 2 * COL), I32),
        vmem((2, COL, COL), F32),
        vmem((2, 2, PART, SLOTS), F32),
        vmem((2, GROUP, PART, SLOTS), F32),
        vmem((8, COL), I32),
        vmem((TARGETS, 8, COL), I32),
        vmem((2, PART, COL), F32),
        vmem((2, TARGETS, PART + 8, COL), F32),
        vmem((2, 2, HALO, PART, COL), F32),
        vmem((2, TARGETS, PART + 8, COL), F32),
        vmem((2, TARGETS, HALO, PART, COL), F32),
        vmem((2, 2, HALO, FLAT, COL), F32),
        vmem((2, 2, HALO, FLAT, COL), F32),
        vmem((2, 2, HALO, FLAT, COL), F32),
        vmem((2, 2, 2, FLAT, COL), F32),
        vmem((2, 2, 2, FLAT, COL), F32),
        vmem((2, HALO, FLAT, COL), F32),
        vmem((2, HALO, FLAT, COL), F32),
        vmem((2, HALO, FLAT, COL), F32),
        dma((4,)),
        dma((TARGETS,)),
        dma((TARGETS,)),
        dma((2, 2, RING)),
        dma((2, GROUP)),
        dma((2,)),
        dma((2, TARGETS)),
        dma((2, TARGETS)),
        dma((2, 2)),
        dma((2, TARGETS)),
        dma((2, 2)),
        dma((2, 2)),
        dma((2, 2)),
        dma((2, 2)),
    ]
    result = pl.pallas_call(
        kernel,
        out_shape=jax.ShapeDtypeStruct((rows, COL), F32),
        in_specs=[pl.BlockSpec(memory_space=pltpu.HBM)] * 4 + [pl.BlockSpec(memory_space=pltpu.VMEM)],
        out_specs=pl.BlockSpec(memory_space=pltpu.VMEM),
        scratch_shapes=scratch,
        compiler_params=pltpu.CompilerParams(
            collective_id=0, has_side_effects=True, vmem_limit_bytes=60 * 1024 * 1024
        ),
    )(state.reshape(FLAT, LON, COL), send_base[0], send_frac[0, 0], recv_slots[0], scale)
    return result.reshape(state.shape)


def solution(mesh):
    placed = (
        P("panel", None, None, "lon", "colat"),
        P("panel", ("lon", "colat"), None),
        P("panel", ("lon", "colat"), None, None),
        P("panel", ("lon", "colat"), None),
    )
    return jax.shard_map(
        shards,
        mesh=mesh,
        in_specs=placed,
        out_specs=P("panel", None, None, "lon", "colat"),
        check_vma=False,
    )
```

```python
import math

import jax
import jax.numpy as jnp
from jax import lax
from jax.experimental import pallas as pl
from jax.experimental.pallas import tpu as pltpu
from jax.sharding import PartitionSpec as P

MESH = pl.DeviceIdType.MESH
F32, BF16, I32 = jnp.float32, jnp.bfloat16, jnp.int32

QUANTITIES = 8
SHELLS = 4
FLAT = QUANTITIES * SHELLS
LON = 48
COL = 128
HALO = 3
OUT = 240
SIDE = HALO * LON
SLOTS = 256
GROUP = 8
GROUPS = 8
AROUND = (1, 3, 2)
SPARE = SIDE - COL
PART = FLAT // 2
TARGETS = 2 * GROUPS
TILES = 12
RING = 4
STRIDE = LON + 16
TIME_STEP = 0.25
SPREAD = 0.1 / 3.0
S, MR, MT, MP, BR, BT, BP, WARM = range(QUANTITIES)


def dot(left, right):
    return jnp.dot(left, right, preferred_element_type=F32)


def split(value):
    high = value.astype(BF16)
    return high, (value - high.astype(F32)).astype(BF16)


def iota(shape, dim):
    return lax.broadcasted_iota(I32, shape, dim)


def cross_radial(m, b):
    return m[1] * b[2] - m[2] * b[1]


def cross_polar(m, b):
    return m[2] * b[0] - m[0] * b[2]


def cross_azimuthal(m, b):
    return m[0] * b[1] - m[1] * b[0]


def edge_rates(own, d, lap, emf_first, emf_second, along_lanes):
    grow, thin = jnp.exp(own[WARM]), jnp.exp(-own[S])
    b = own[BR:WARM]
    if along_lanes:
        vel, out = own[MT], MT
        lorentz = (d[BR] * b[1], -d[BR] * b[0] - d[BP] * b[2], d[BP] * b[1])
        turn = (emf_first, None, -emf_second)
    else:
        vel, out = own[MP], MP
        lorentz = (d[BR] * b[2], d[BT] * b[2], -d[BT] * b[1] - d[BR] * b[0])
        turn = (-emf_first, emf_second, None)
    result = [-vel * d[S] - d[out]]
    for i in range(3):
        rate = -vel * d[MR + i] + thin * lorentz[i] + SPREAD * lap[MR + i]
        if MR + i == out:
            rate = rate - grow * (d[S] + d[WARM])
        result.append(rate)
    for i in range(3):
        rate = SPREAD * lap[BR + i]
        result.append(rate if turn[i] is None else rate + turn[i])
    result.append(-vel * d[WARM] - (2.0 / 3.0) * d[out] + SPREAD * lap[WARM])
    return result


def shell_first(x):
    a, b = 8.0 * (x[3] - x[0]), 45.0
    return (
        b * (x[1] - x[0]) - 9.0 * (x[2] - x[0]) + (x[3] - x[0]),
        b * (x[2] - x[0]) - a,
        b * (x[3] - x[1]) - a,
        b * (x[3] - x[2]) - 9.0 * (x[3] - x[1]) + (x[3] - x[0]),
    )


def shell_second(x):
    return (
        2.0 * x[3] - 27.0 * x[2] + 270.0 * x[1] - 245.0 * x[0],
        245.0 * x[0] - 490.0 * x[1] + 270.0 * x[2] - 25.0 * x[3],
        245.0 * x[3] - 490.0 * x[2] + 270.0 * x[1] - 25.0 * x[0],
        2.0 * x[0] - 27.0 * x[1] + 270.0 * x[2] - 245.0 * x[3],
    )


def kernel(
    x_hbm, base_hbm, frac_hbm, slots_hbm, out_ref,
    deep, base_ref, frac_ref, slots_ref, emf, lanes, rate, mix, rows_mix, band, onehot, owner, turned,
    blocks, table, idx_out, idx_in, rest_rows, picked, picked_rows, got_cols, got_rows, row_out, row_in, col_own, col_out, col_in,
    row_halo, col_halo, edge_add,
    in_sem, idx_send, idx_recv, a_send, a_recv, s_send, b_send, b_recv, l_send, l_recv, r_send, r_recv, c_send, c_recv,
):
    panel, lon, col = lax.axis_index("panel"), lax.axis_index("lon"), lax.axis_index("colat")
    n_lon, n_col = lax.axis_size("lon"), lax.axis_size("colat")
    core, mine = lon & 1, lon >> 1
    member = core * n_col + col
    other = 1 - panel
    lon_up, lon_down = lax.rem(lon + 1, n_lon), lax.rem(lon + n_lon - 1, n_lon)
    col_up, col_down = lax.rem(col + 1, n_col), lax.rem(col + n_col - 1, n_col)
    outer = lax.rem(lon + 2 * core - 1 + n_lon, n_lon)
    col_edge = jnp.logical_or(col == 0, col == n_col - 1)
    lon_edge = jnp.logical_or(lon == 0, lon == n_lon - 1)

    sibling = (panel, lon + 1 - 2 * core, col)
    origin = core * GROUPS + mine

    def row_device(step, half):
        return (panel, 2 * mine + half, (col + step) & (n_col - 1))

    def target_device(target):
        return (other, 2 * (target & (GROUPS - 1)) + (target >> 3), col)

    def remote(src, dst, send, recv, device):
        return pltpu.make_async_remote_copy(
            src_ref=src, dst_ref=dst, send_sem=send, recv_sem=recv, device_id=device, device_id_type=MESH
        )

    frame = deep.reshape(2, FLAT * STRIDE, COL)
    copies = [
        pltpu.make_async_copy(src, dst, in_sem.at[i])
        for i, (src, dst) in enumerate(
            (
                (frac_hbm, frac_ref),
                (base_hbm, base_ref),
                (slots_hbm, slots_ref),
                (x_hbm, deep.at[0, :, pl.ds(8, LON), :]),
            )
        )
    ]
    for copy in copies:
        copy.start()

    barrier = pltpu.get_barrier_semaphore()
    for step in AROUND:
        for half in range(2):
            pl.semaphore_signal(barrier, inc=1, device_id=row_device(step, half), device_id_type=MESH)
    pl.semaphore_signal(barrier, inc=1, device_id=sibling, device_id_type=MESH)
    for target in range(TARGETS):
        pl.semaphore_signal(barrier, inc=1, device_id=target_device(target), device_id_type=MESH)
    pl.semaphore_signal(barrier, inc=1, device_id=(panel, outer, col), device_id_type=MESH)

    zero_rows = jnp.zeros((8, COL), F32)
    for f in range(FLAT):
        for part in range(2):
            frame[part, f * STRIDE : f * STRIDE + 8, :] = zero_rows
            frame[part, f * STRIDE + 8 + LON : (f + 1) * STRIDE, :] = zero_rows
    for f in range(3 * SHELLS):
        emf[f * STRIDE : f * STRIDE + 8, :] = zero_rows
        emf[f * STRIDE + 8 + LON : (f + 1) * STRIDE, :] = zero_rows

    for half in range(2):
        turned[half, :, :] = jnp.zeros((COL, COL), F32)

    apart = iota((COL, COL), 0) - iota((COL, COL), 1)
    reach = jnp.abs(apart)
    first = jnp.where(reach == 1, 45.0, jnp.where(reach == 2, -9.0, jnp.where(reach == 3, 1.0, 0.0)))
    first = jnp.where(apart < 0, -first, first).astype(BF16)
    second = jnp.where(
        reach == 0, -490.0, jnp.where(reach == 1, 270.0, jnp.where(reach == 2, -27.0, jnp.where(reach == 3, 2.0, 0.0)))
    ).astype(BF16)
    for part in range(2):
        band[part * COL : (part + 1) * COL, 0:COL] = first
        band[part * COL : (part + 1) * COL, COL : 2 * COL] = second

    copies[0].wait()
    copies[1].wait()
    base = jnp.concatenate([base_ref[...], jnp.zeros((1, SLOTS - OUT), I32)], axis=1)
    base_row, base_col = lax.div(base, COL), lax.rem(base, COL)
    share = jnp.concatenate([frac_ref[...], jnp.zeros((2, SLOTS - OUT), F32)], axis=1)
    along, across = share[0:1, :], share[1:2, :]
    cells = iota((COL, SLOTS), 0)
    weight = jnp.where(cells == base_col, 1.0 - across, 0.0) + jnp.where(cells == base_col + 1, across, 0.0)
    weight_high, weight_low = split(weight)
    mix[0:COL, :] = weight_high
    mix[COL : 2 * COL, :] = weight_high
    mix[2 * COL : 3 * COL, :] = weight_low
    cells = iota((LON, SLOTS), 0)
    rows_mix[...] = jnp.where(cells == base_row, 1.0 - along, 0.0) + jnp.where(cells == base_row + 1, along, 0.0)

    copies[2].wait()
    spot = iota((1, SLOTS), 1)
    sides = jnp.where(spot < SIDE, jnp.maximum(slots_ref[:, 0:SLOTS], slots_ref[:, SIDE : SIDE + SLOTS]) + 1, 0)
    digits = jnp.concatenate([lax.div(sides, COL), lax.rem(sides, COL), jnp.zeros((6, SLOTS), I32)], axis=0)
    source, target = iota((SLOTS, SLOTS), 0), iota((SLOTS, SLOTS), 1)
    layer = jnp.where(target >= LON, 1, 0) + jnp.where(target >= 2 * LON, 1, 0)
    order = jnp.logical_and(target < SIDE, source == HALO * (target - LON * layer) + layer)
    digits = dot(digits.astype(F32).astype(BF16), jnp.where(order, 1.0, 0.0).astype(BF16)).astype(I32)
    sides = digits[0:1, :] * COL + digits[1:2, :] - 1
    idx_out[0:1, :] = sides[:, 0:COL]
    idx_out[1:2, :] = sides[:, COL : 2 * COL]
    for h in range(HALO):
        at = 2 * SIDE + h * COL
        idx_out[2 + h : 3 + h, :] = jnp.maximum(
            slots_ref[:, at : at + COL], slots_ref[:, at + HALO * COL : at + HALO * COL + COL]
        )
    idx_out[5:8, :] = jnp.full((3, COL), -1, I32)

    place = (col * COL + iota((1, COL), 1)).astype(F32)
    scale = 1.0 / jnp.sin(math.pi / 4.0 + (place + 0.5) * (math.pi / 2.0 / (COL * n_col)))
    copies[3].wait()

    def load_split(part, pair):
        block = jnp.concatenate(
            [frame[part, pl.ds(pl.multiple_of((8 * pair + q) * STRIDE + 8, 8), LON), :] for q in range(8)], axis=0
        )
        return split(block)

    def interpolate(part, half):
        for pair in range(PART // 8):
            high, low = load_split(part, 2 * half + pair)
            value = dot(jnp.concatenate([high, low, high], axis=1), mix[...])
            value = jnp.sum(value.reshape(8, LON, SLOTS) * rows_mix[...][None], axis=1)
            blocks[part, half, 8 * pair : 8 * pair + 8, :] = value

    def interpolate_and_send(part):
        for half in range(2):
            interpolate(part, half)
            if part == 0 and half == 0:
                pl.semaphore_wait(barrier, 2 * len(AROUND) + 2 + TARGETS)
            for step in AROUND:
                a_copy(part, step, half).start()

            @pl.when(core != half)
            def _():
                s_copy(part, half).start()

            @pl.when(core == half)
            def _():
                table[part, member] = blocks[part, half]

    def lane_pass(part):
        def body(pair, carry):
            high, low = load_split(part, pair)
            both = jnp.concatenate([high, low], axis=1)
            lanes[pl.ds(pl.multiple_of(8 * LON * pair, 8), 8 * LON), :] = dot(both, band[...])
            return carry

        lax.fori_loop(0, FLAT // 8, body, 0)

    def cols_of(part):
        lane = iota((LON, COL), 1)
        for half in range(2):
            edge = jnp.zeros((LON, COL), F32)
            for g in range(FLAT // 2):
                at = (half * (FLAT // 2) + g) * STRIDE + 8
                moved = pltpu.roll(frame[part, at : at + LON, :], 8 * g + HALO, 1)
                edge = jnp.where(jnp.logical_and(lane >= 8 * g, lane < 8 * g + 2 * HALO), moved, edge)
            turned[half, :, 0:LON] = jnp.transpose(edge)
        for side in range(2):
            for j in range(HALO):
                first = (1 - side) * HALO + j
                for half in range(2):
                    col_own[part, side, j, half * (FLAT // 2) : (half + 1) * (FLAT // 2), :] = turned[
                        half, pl.ds(first, FLAT // 2, stride=8), :
                    ]
            col_out[part, side, 0] = jnp.where(
                iota((FLAT, COL), 1) < COL // 2, col_own[part, side, 0], pltpu.roll(col_own[part, side, 1], COL // 2, 1)
            )
            col_out[part, side, 1] = col_own[part, side, 2]

    def emf_pass(part):
        for r in range(SHELLS):
            def field(q):
                at = (q * SHELLS + r) * STRIDE + 8
                return frame[part, at : at + LON, :]

            m, b = [field(MR + i) for i in range(3)], [field(BR + i) for i in range(3)]
            for i, form in enumerate((cross_radial, cross_polar, cross_azimuthal)):
                at = (i * SHELLS + r) * STRIDE + 8
                emf[at : at + LON, :] = form(m, b)
        for i, at in ((0, FLAT), (2, FLAT + SHELLS)):
            block = jnp.concatenate(
                [emf[(i * SHELLS + r) * STRIDE + 8 : (i * SHELLS + r) * STRIDE + 8 + LON, :] for r in range(SHELLS)],
                axis=0,
            )
            high, low = split(block)
            lanes[at * LON : (at + SHELLS) * LON, 0:COL] = dot(
                jnp.concatenate([high, low], axis=1), band[:, 0:COL]
            )

    def main_pass(part, start, stop):
        def body(block, carry):
            here = pl.multiple_of(8 * block, 8)

            def near(f, apart):
                return frame[part, pl.ds(f * STRIDE + 8 + here + apart, 8), :]

            def near_emf(f, apart):
                return emf[pl.ds(f * STRIDE + 8 + here + apart, 8), :]

            def lane_first(f):
                return lanes[pl.ds(f * LON + here, 8), 0:COL]

            def lane_second(f):
                return lanes[pl.ds(f * LON + here, 8), COL : 2 * COL]

            def row_first(at):
                return 45.0 * (at[1] - at[-1]) - 9.0 * (at[2] - at[-2]) + (at[3] - at[-3])

            def row_second(at, centre):
                return (
                    270.0 * (at[1] + at[-1]) - 27.0 * (at[2] + at[-2]) + 2.0 * (at[3] + at[-3]) - 490.0 * centre
                )

            centre = [[near(q * SHELLS + r, 0) for r in range(SHELLS)] for q in range(QUANTITIES)]
            radial = [shell_first(x) for x in centre]
            radial_second = [None if q == S else shell_second(centre[q]) for q in range(QUANTITIES)]
            emf_centre = [[near_emf(i * SHELLS + r, 0) for r in range(SHELLS)] for i in range(3)]
            emf_radial = [None, shell_first(emf_centre[1]), shell_first(emf_centre[2])]
            for r in range(SHELLS):
                own = [centre[q][r] for q in range(QUANTITIES)]
                g, lap = [], []
                for q in range(QUANTITIES):
                    f = q * SHELLS + r
                    at = {d: near(f, d) for d in (-3, -2, -1, 1, 2, 3)}
                    g.append((radial[q][r], lane_first(f), scale * row_first(at)))
                    if q == S:
                        lap.append(None)
                    else:
                        lap.append(
                            radial_second[q][r] + lane_second(f) + (scale * scale) * row_second(at, own[q])
                        )
                m, b = own[MR:BR], own[BR:WARM]

                def advect(q):
                    return m[0] * g[q][0] + m[1] * g[q][1] + m[2] * g[q][2]

                div = g[MR][0] + g[MT][1] + g[MP][2]
                current = (g[BP][1] - g[BT][2], g[BR][2] - g[BP][0], g[BT][0] - g[BR][1])
                lorentz = (
                    current[1] * b[2] - current[2] * b[1],
                    current[2] * b[0] - current[0] * b[2],
                    current[0] * b[1] - current[1] * b[0],
                )
                grow, thin = jnp.exp(own[WARM]), jnp.exp(-own[S])
                emf_rows = {}
                for i in (0, 1):
                    f = i * SHELLS + r
                    emf_rows[i] = scale * row_first({d: near_emf(f, d) for d in (-3, -2, -1, 1, 2, 3)})
                turn = (
                    lane_first(FLAT + SHELLS + r) - emf_rows[1],
                    emf_rows[0] - emf_radial[2][r],
                    emf_radial[1][r] - lane_first(FLAT + r),
                )
                result = [-advect(S) - div]
                for i in range(3):
                    result.append(
                        -advect(MR + i) - grow * (g[S][i] + g[WARM][i]) + thin * lorentz[i] + SPREAD * lap[MR + i]
                    )
                for i in range(3):
                    result.append(turn[i] + SPREAD * lap[BR + i])
                result.append(-advect(WARM) - (2.0 / 3.0) * div + SPREAD * lap[WARM])
                for q in range(QUANTITIES):
                    rate[pl.ds((q * SHELLS + r) * LON + here, 8), :] = result[q]
            return carry

        lax.fori_loop(start, stop, body, 0)

    def rows_of(part):
        for h in range(HALO):
            row_out[part, 0, h] = frame[part, pl.ds(8 + h, FLAT, stride=STRIDE), :]
            row_out[part, 1, h] = frame[part, pl.ds(8 + LON - HALO + h, FLAT, stride=STRIDE), :]

    def prepare_picks():
        for tile in range(2 * TILES):
            if tile < TARGETS:
                slot = idx_in[tile, 0:1, :]
            elif tile < TARGETS + 2:
                first = (tile - TARGETS) * GROUPS
                slot = idx_in[first, 1:2, :]
                for q in range(1, GROUPS):
                    slot = jnp.maximum(slot, pltpu.roll(idx_in[first + q], SPARE * q, 1)[1:2, :])
            else:
                side, h = divmod(tile - TARGETS - 2, HALO)
                slot = idx_in[side * (TARGETS - 1), 2 + h : 3 + h, :]
            slot = slot - mine * (GROUP * OUT)
            who = jnp.zeros_like(slot)
            for q in range(1, GROUP):
                who = who + jnp.where(slot >= q * OUT, 1, 0)
            cell = slot - who * OUT
            who = jnp.where(jnp.logical_and(slot >= 0, slot < GROUP * OUT), who, -1)
            at = (tile % 2) * COL
            owner[tile // 2, :, at : at + COL] = jnp.broadcast_to(who, (8, COL))
            hot = jnp.where(iota((SLOTS, COL), 0) == cell, 1.0, 0.0).astype(BF16)
            onehot[tile // 2, :, at : at + COL] = hot

    def table_split(part):
        high, low = split(table[part].reshape(GROUP * PART, SLOTS))
        return jnp.concatenate([high, low], axis=0)

    def pick(both, tile):
        value = dot(both, onehot[tile])
        value = value[0 : GROUP * PART] + value[GROUP * PART :]
        who = jnp.broadcast_to(owner[tile, 0:1, :], (PART, SLOTS))
        total = jnp.zeros((PART, SLOTS), F32)
        for q in range(GROUP):
            total = jnp.where(who == q, value[q * PART : (q + 1) * PART, :], total)
        return total[:, 0:COL], total[:, COL : 2 * COL]

    def pick_sides(part, both):
        rest = pick(both, TARGETS // 2)
        rest_rows[0], rest_rows[1] = rest
        spot = lax.div(iota((8, COL), 1), SPARE)
        for step in range(TARGETS // 2):
            tile = (step + mine) & (TARGETS // 2 - 1)
            ends = pick(both, tile)
            rows = rest_rows[tile >> 2]
            for i in range(2):
                target = 2 * tile + i
                there = target & (GROUPS - 1)
                total = jnp.zeros((8, COL), F32)
                for q in range(PART // 8):
                    moved = pltpu.roll(rows[8 * q : 8 * q + 8, :], SPARE * ((q + GROUPS - there) & (GROUPS - 1)), 1)
                    total = jnp.where(spot == q, moved, total)
                picked[part, target, 0:PART, :] = ends[i]
                picked[part, target, PART : PART + 8, :] = total
                b_copy(part, target).start()

    def pick_ends(part, both):
        ends = []
        for tile in range(TARGETS // 2 + 1, TILES):
            ends += pick(both, tile)
        for side in range(2):
            for h in range(HALO):
                picked_rows[part, side, h] = ends[side * HALO + h]
            l_copy(part, side).start()

    def corrections(part, halo_ref, own_ref, along_lanes):
        factor = None if along_lanes else scale

        def scaled(value, power):
            for _ in range(0 if along_lanes else power):
                value = factor * value
            return value

        for side in range(2):
            halo = [
                [halo_ref[side, h, q * SHELLS : (q + 1) * SHELLS, :] for q in range(QUANTITIES)] for h in range(HALO)
            ]
            form = cross_azimuthal if along_lanes else cross_polar
            halo_emf = [(cross_radial(x[MR:BR], x[BR:WARM]), form(x[MR:BR], x[BR:WARM])) for x in halo]
            sign = -1.0 if side == 0 else 1.0
            firsts, seconds = (45.0 * sign, -9.0 * sign, sign), (270.0, -27.0, 2.0)
            for j in range(HALO):
                own = [own_ref[part, side, j, q * SHELLS : (q + 1) * SHELLS, :] for q in range(QUANTITIES)]

                def total(weights, of):
                    result = None
                    for m in (1, 2, 3):
                        h = j + 3 - m if side == 0 else m - 3 + j
                        if 0 <= h < HALO:
                            term = weights[m - 1] * of(h)
                            result = term if result is None else result + term
                    return result

                d = [scaled(total(firsts, lambda h, q=q: halo[h][q]), 1) for q in range(QUANTITIES)]
                lap = [
                    None if q == S else scaled(total(seconds, lambda h, q=q: halo[h][q]), 2)
                    for q in range(QUANTITIES)
                ]
                radial = scaled(total(firsts, lambda h: halo_emf[h][0]), 1)
                second = scaled(total(firsts, lambda h: halo_emf[h][1]), 1)
                result = edge_rates(own, d, lap, second, radial, along_lanes)
                for q in range(QUANTITIES):
                    edge_add[side, j, q * SHELLS : (q + 1) * SHELLS, :] = result[q]

    def row_corrections(part):
        corrections(part, row_halo, row_out, False)
        for side in range(2):
            for j in range(HALO):
                rows = pl.ds(j if side == 0 else LON - HALO + j, FLAT, stride=LON)
                rate[rows, :] = rate[rows, :] + edge_add[side, j]

    def col_corrections(part):
        corrections(part, col_halo, col_own, True)
        for side in range(2):
            for j in range(HALO):
                for half in range(2):
                    turned[half, pl.ds((1 - side) * HALO + j, FLAT // 2, stride=8), :] = edge_add[
                        side, j, half * (FLAT // 2) : (half + 1) * (FLAT // 2), :
                    ]

    def finish(part):
        lane = iota((LON, COL), 1)
        border = jnp.logical_or(lane < HALO, lane >= COL - HALO)
        for half in range(2):
            edge = jnp.transpose(turned[half])[0:LON, :]
            for g in range(FLAT // 2):
                f = half * (FLAT // 2) + g
                added = jnp.where(border, pltpu.roll(edge, COL - 8 * g - HALO, 1), 0.0)
                change = (TIME_STEP / 60.0) * (rate[f * LON : (f + 1) * LON, :] + added)
                rows = slice(f * STRIDE + 8, f * STRIDE + 8 + LON)
                start = frame[0, rows, :]
                if part == 0:
                    frame[1, rows, :] = start + change
                else:
                    out_ref[f * LON : (f + 1) * LON, :] = 0.5 * (start + frame[1, rows, :] + change)

    def a_copy(part, step, half):
        return remote(
            blocks.at[part, half], table.at[part, member], a_send.at[part, half, step], a_recv.at[part, member],
            row_device(step, half),
        )

    def s_copy(part, half):
        return remote(
            blocks.at[part, half], table.at[part, member], s_send.at[part], a_recv.at[part, member], sibling
        )

    def a_arrival(part, step):
        there = (member + step) & (GROUP - 1)
        return remote(blocks.at[part, 0], table.at[part, there], s_send.at[part], a_recv.at[part, there], sibling)

    def b_copy(part, target):
        return remote(
            picked.at[part, target], got_cols.at[part, origin], b_send.at[part, target], b_recv.at[part, origin],
            target_device(target),
        )

    def b_arrival(part, source):
        return remote(
            picked.at[part, 0], got_cols.at[part, source], b_send.at[part, 0], b_recv.at[part, source],
            (other, lon, col),
        )

    def l_copy(part, side):
        return remote(
            picked_rows.at[part, side], got_rows.at[part, origin], l_send.at[part, side], l_recv.at[part, origin],
            target_device(side * (TARGETS - 1)),
        )

    def l_arrival(part, source):
        return remote(
            picked_rows.at[part, 0], got_rows.at[part, source], l_send.at[part, 0], l_recv.at[part, source],
            (other, lon, col),
        )

    def row_copy(part, side):
        return remote(
            row_out.at[part, 1 - side], row_in.at[part, side], r_send.at[part, side], r_recv.at[part, side],
            (panel, lon_up if side == 0 else lon_down, col),
        )

    def col_copy(part, side):
        return remote(
            col_out.at[part, 1 - side], col_in.at[part, side], c_send.at[part, side], c_recv.at[part, side],
            (panel, lon, col_up if side == 0 else col_down),
        )

    def idx_copy(target):
        return remote(
            idx_out, idx_in.at[origin], idx_send.at[target], idx_recv.at[origin], target_device(target)
        )

    def idx_arrival(source):
        return remote(idx_out, idx_in.at[source], idx_send.at[0], idx_recv.at[source], (other, lon, col))

    for part in range(2):
        interpolate_and_send(part)
        if part == 0:
            for target in range(TARGETS):
                idx_copy(target).start()
        rows_of(part)
        for side in range(2):
            row_copy(part, side).start()
        cols_of(part)
        for side in range(2):
            col_copy(part, side).start()
        if part == 0:
            for source in range(TARGETS):
                idx_arrival(source).wait_recv()
            prepare_picks()
        for step in range(1, GROUP):
            a_arrival(part, step).wait_recv()
        both = table_split(part)

        @pl.when(col_edge)
        def _():
            pick_sides(part, both)

        pick_ends(part, both)
        lane_pass(part)
        emf_pass(part)
        main_pass(part, 0, 6)
        for side in range(2):
            row_copy(part, side).wait_recv()
            col_copy(part, side).wait_recv()

        for side in range(2):
            at_edge = lon == (0 if side == 0 else n_lon - 1)

            @pl.when(at_edge)
            def _():
                for source in range(TARGETS):
                    l_arrival(part, source).wait_recv()
                for half in range(2):
                    total = got_rows[part, half * GROUPS]
                    for group in range(1, GROUPS):
                        total = total + got_rows[part, half * GROUPS + group]
                    row_halo[side, :, half * PART : (half + 1) * PART, :] = total

            @pl.when(jnp.logical_not(at_edge))
            def _():
                row_halo[side] = row_in[part, side]

        row_corrections(part)

        for side in range(2):
            at_edge = col == (0 if side == 0 else n_col - 1)

            @pl.when(at_edge)
            def _():
                for source in range(TARGETS):
                    b_arrival(part, source).wait_recv()
                for half in range(2):
                    total = got_cols[part, half * GROUPS]
                    for group in range(1, GROUPS):
                        total = total + got_cols[part, half * GROUPS + group]
                    main, rest = total[0:PART], total[PART : PART + 8]
                    rows = slice(half * PART, (half + 1) * PART)
                    col_halo[side, 0, rows, :] = main
                    col_halo[side, 1, rows, :] = pltpu.roll(main, COL - LON, 1)
                    main = pltpu.roll(main, COL - 2 * LON, 1)
                    for q in range(PART // 8):
                        at = half * PART + 8 * q
                        col_halo[side, 2, at : at + 8, :] = jnp.where(
                            iota((8, COL), 1) < COL - 2 * LON,
                            main[8 * q : 8 * q + 8, :],
                            pltpu.roll(rest, (COL + COL - 2 * LON - SPARE * q) % COL, 1),
                        )

            @pl.when(jnp.logical_not(at_edge))
            def _():
                pair = col_in[part, side, 0]
                col_halo[side, 0] = pair
                col_halo[side, 1] = pltpu.roll(pair, COL // 2, 1)
                col_halo[side, 2] = col_in[part, side, 1]

        col_corrections(part)
        finish(part)

    for target in range(TARGETS):
        idx_copy(target).wait_send()
    for part in range(2):
        for half in range(2):
            for step in AROUND:
                a_copy(part, step, half).wait_send()
        s_copy(part, 0).wait_send()
        for side in range(2):
            row_copy(part, side).wait_send()
            col_copy(part, side).wait_send()
            l_copy(part, side).wait_send()

        @pl.when(col_edge)
        def _():
            for target in range(TARGETS):
                b_copy(part, target).wait_send()


def shards(state, send_base, send_frac, recv_slots):
    rows = FLAT * LON
    dma = pltpu.SemaphoreType.DMA
    vmem = pltpu.VMEM
    scratch = [
        vmem((2, FLAT, STRIDE, COL), F32),
        vmem((1, OUT), I32),
        vmem((2, OUT), F32),
        vmem((1, recv_slots.shape[-1]), I32),
        vmem((3 * SHELLS * STRIDE, COL), F32),
        vmem(((FLAT + 2 * SHELLS) * LON, 2 * COL), F32),
        vmem((rows, COL), F32),
        vmem((3 * COL, SLOTS), BF16),
        vmem((LON, SLOTS), F32),
        vmem((2 * COL, 2 * COL), BF16),
        vmem((TILES, SLOTS, 2 * COL), BF16),
        vmem((TILES, 8, 2 * COL), I32),
        vmem((2, COL, COL), F32),
        vmem((2, 2, PART, SLOTS), F32),
        vmem((2, GROUP, PART, SLOTS), F32),
        vmem((8, COL), I32),
        vmem((TARGETS, 8, COL), I32),
        vmem((2, PART, COL), F32),
        vmem((2, TARGETS, PART + 8, COL), F32),
        vmem((2, 2, HALO, PART, COL), F32),
        vmem((2, TARGETS, PART + 8, COL), F32),
        vmem((2, TARGETS, HALO, PART, COL), F32),
        vmem((2, 2, HALO, FLAT, COL), F32),
        vmem((2, 2, HALO, FLAT, COL), F32),
        vmem((2, 2, HALO, FLAT, COL), F32),
        vmem((2, 2, 2, FLAT, COL), F32),
        vmem((2, 2, 2, FLAT, COL), F32),
        vmem((2, HALO, FLAT, COL), F32),
        vmem((2, HALO, FLAT, COL), F32),
        vmem((2, HALO, FLAT, COL), F32),
        dma((4,)),
        dma((TARGETS,)),
        dma((TARGETS,)),
        dma((2, 2, RING)),
        dma((2, GROUP)),
        dma((2,)),
        dma((2, TARGETS)),
        dma((2, TARGETS)),
        dma((2, 2)),
        dma((2, TARGETS)),
        dma((2, 2)),
        dma((2, 2)),
        dma((2, 2)),
        dma((2, 2)),
    ]
    result = pl.pallas_call(
        kernel,
        out_shape=jax.ShapeDtypeStruct((rows, COL), F32),
        in_specs=[pl.BlockSpec(memory_space=pltpu.HBM)] * 4,
        out_specs=pl.BlockSpec(memory_space=pltpu.VMEM),
        scratch_shapes=scratch,
        compiler_params=pltpu.CompilerParams(
            collective_id=0, has_side_effects=True, vmem_limit_bytes=40 * 1024 * 1024
        ),
    )(*(
        pltpu.with_memory_space_constraint(x, pltpu.HBM)
        for x in (state.reshape(FLAT, LON, COL), send_base[0], send_frac[0, 0], recv_slots[0])
    ))
    return result.reshape(state.shape)


def solution(mesh):
    placed = (
        P("panel", None, None, "lon", "colat"),
        P("panel", ("lon", "colat"), None),
        P("panel", ("lon", "colat"), None, None),
        P("panel", ("lon", "colat"), None),
    )
    return jax.shard_map(
        shards,
        mesh=mesh,
        in_specs=placed,
        out_specs=P("panel", None, None, "lon", "colat"),
        check_vma=False,
    )
```

```python
import math

import jax
import jax.numpy as jnp
from jax import lax
from jax.experimental import pallas as pl
from jax.experimental.pallas import tpu as pltpu
from jax.sharding import PartitionSpec as P

MESH = pl.DeviceIdType.MESH
F32, BF16, I32 = jnp.float32, jnp.bfloat16, jnp.int32

QUANTITIES = 8
SHELLS = 4
FLAT = QUANTITIES * SHELLS
LON = 48
COL = 128
HALO = 3
OUT = 240
SIDE = HALO * LON
SLOTS = 256
GROUP = 8
GROUPS = 8
AROUND = (1, 3, 2)
SPARE = SIDE - COL
PART = FLAT // 2
TARGETS = 2 * GROUPS
TILES = 12
RING = 4
STRIDE = LON + 16
TIME_STEP = 0.25
SPREAD = 0.1 / 3.0
S, MR, MT, MP, BR, BT, BP, WARM = range(QUANTITIES)


def dot(left, right):
    return jnp.dot(left, right, preferred_element_type=F32)


def split(value):
    high = value.astype(BF16)
    return high, (value - high.astype(F32)).astype(BF16)


def iota(shape, dim):
    return lax.broadcasted_iota(I32, shape, dim)


def cross_radial(m, b):
    return m[1] * b[2] - m[2] * b[1]


def cross_polar(m, b):
    return m[2] * b[0] - m[0] * b[2]


def cross_azimuthal(m, b):
    return m[0] * b[1] - m[1] * b[0]


def edge_rates(own, d, lap, emf_first, emf_second, along_lanes):
    grow, thin = jnp.exp(own[WARM]), jnp.exp(-own[S])
    b = own[BR:WARM]
    if along_lanes:
        vel, out = own[MT], MT
        lorentz = (d[BR] * b[1], -d[BR] * b[0] - d[BP] * b[2], d[BP] * b[1])
        turn = (emf_first, None, -emf_second)
    else:
        vel, out = own[MP], MP
        lorentz = (d[BR] * b[2], d[BT] * b[2], -d[BT] * b[1] - d[BR] * b[0])
        turn = (-emf_first, emf_second, None)
    result = [-vel * d[S] - d[out]]
    for i in range(3):
        rate = -vel * d[MR + i] + thin * lorentz[i] + SPREAD * lap[MR + i]
        if MR + i == out:
            rate = rate - grow * (d[S] + d[WARM])
        result.append(rate)
    for i in range(3):
        rate = SPREAD * lap[BR + i]
        result.append(rate if turn[i] is None else rate + turn[i])
    result.append(-vel * d[WARM] - (2.0 / 3.0) * d[out] + SPREAD * lap[WARM])
    return result


def shell_first(x):
    a, b = 8.0 * (x[3] - x[0]), 45.0
    return (
        b * (x[1] - x[0]) - 9.0 * (x[2] - x[0]) + (x[3] - x[0]),
        b * (x[2] - x[0]) - a,
        b * (x[3] - x[1]) - a,
        b * (x[3] - x[2]) - 9.0 * (x[3] - x[1]) + (x[3] - x[0]),
    )


def shell_second(x):
    return (
        2.0 * x[3] - 27.0 * x[2] + 270.0 * x[1] - 245.0 * x[0],
        245.0 * x[0] - 490.0 * x[1] + 270.0 * x[2] - 25.0 * x[3],
        245.0 * x[3] - 490.0 * x[2] + 270.0 * x[1] - 25.0 * x[0],
        2.0 * x[0] - 27.0 * x[1] + 270.0 * x[2] - 245.0 * x[3],
    )


def kernel(
    x_hbm, base_hbm, frac_hbm, slots_hbm, out_ref,
    deep, base_ref, frac_ref, slots_ref, emf, lanes, mix, cols_mix, rows_mix, rows_split, band, onehot, owner, turned,
    blocks, table, idx_out, idx_in, rest_rows, picked, picked_rows, got_cols, got_rows, row_out, row_in, col_own, col_out, col_in,
    row_halo, col_halo, row_add, col_add,
    in_sem, idx_send, idx_recv, a_send, a_recv, s_send, b_send, b_recv, l_send, l_recv, r_send, r_recv, c_send, c_recv,
):
    panel, lon, col = lax.axis_index("panel"), lax.axis_index("lon"), lax.axis_index("colat")
    n_lon, n_col = lax.axis_size("lon"), lax.axis_size("colat")
    core, mine = lon & 1, lon >> 1
    member = core * n_col + col
    other = 1 - panel
    lon_up, lon_down = lax.rem(lon + 1, n_lon), lax.rem(lon + n_lon - 1, n_lon)
    col_up, col_down = lax.rem(col + 1, n_col), lax.rem(col + n_col - 1, n_col)
    outer = lax.rem(lon + 2 * core - 1 + n_lon, n_lon)
    col_edge = jnp.logical_or(col == 0, col == n_col - 1)

    sibling = (panel, lon + 1 - 2 * core, col)
    origin = core * GROUPS + mine

    def row_device(step, half):
        return (panel, 2 * mine + half, (col + step) & (n_col - 1))

    def target_device(target):
        return (other, 2 * (target & (GROUPS - 1)) + (target >> 3), col)

    def remote(src, dst, send, recv, device):
        return pltpu.make_async_remote_copy(
            src_ref=src, dst_ref=dst, send_sem=send, recv_sem=recv, device_id=device, device_id_type=MESH
        )

    frame = deep.reshape(2, FLAT * STRIDE, COL)
    copies = [
        pltpu.make_async_copy(src, dst, in_sem.at[i])
        for i, (src, dst) in enumerate(
            (
                (frac_hbm, frac_ref),
                (base_hbm, base_ref),
                (slots_hbm, slots_ref),
                (x_hbm, deep.at[0, :, pl.ds(8, LON), :]),
            )
        )
    ]
    for copy in copies:
        copy.start()

    barrier = pltpu.get_barrier_semaphore()
    for step in AROUND:
        for half in range(2):
            pl.semaphore_signal(barrier, inc=1, device_id=row_device(step, half), device_id_type=MESH)
    pl.semaphore_signal(barrier, inc=1, device_id=sibling, device_id_type=MESH)
    for target in range(TARGETS):
        pl.semaphore_signal(barrier, inc=1, device_id=target_device(target), device_id_type=MESH)
    pl.semaphore_signal(barrier, inc=1, device_id=(panel, outer, col), device_id_type=MESH)

    zero_rows = jnp.zeros((8, COL), F32)
    for f in range(FLAT):
        for part in range(2):
            frame[part, f * STRIDE : f * STRIDE + 8, :] = zero_rows
            frame[part, f * STRIDE + 8 + LON : (f + 1) * STRIDE, :] = zero_rows
    for f in range(3 * SHELLS):
        emf[f * STRIDE : f * STRIDE + 8, :] = zero_rows
        emf[f * STRIDE + 8 + LON : (f + 1) * STRIDE, :] = zero_rows

    for half in range(2):
        turned[half, :, :] = jnp.zeros((COL, COL), F32)

    apart = iota((COL, COL), 0) - iota((COL, COL), 1)
    reach = jnp.abs(apart)
    first = jnp.where(reach == 1, 45.0, jnp.where(reach == 2, -9.0, jnp.where(reach == 3, 1.0, 0.0)))
    first = jnp.where(apart < 0, -first, first).astype(BF16)
    second = jnp.where(
        reach == 0, -490.0, jnp.where(reach == 1, 270.0, jnp.where(reach == 2, -27.0, jnp.where(reach == 3, 2.0, 0.0)))
    ).astype(BF16)
    for part in range(2):
        band[part * COL : (part + 1) * COL, 0:COL] = first
        band[part * COL : (part + 1) * COL, COL : 2 * COL] = second

    copies[0].wait()
    copies[1].wait()
    base = jnp.concatenate([base_ref[...], jnp.zeros((1, SLOTS - OUT), I32)], axis=1)
    base_row, base_col = lax.div(base, COL), lax.rem(base, COL)
    share = jnp.concatenate([frac_ref[...], jnp.zeros((2, SLOTS - OUT), F32)], axis=1)
    along, across = share[0:1, :], share[1:2, :]
    cells = iota((COL, SLOTS), 0)
    weight = jnp.where(cells == base_col, 1.0 - across, 0.0) + jnp.where(cells == base_col + 1, across, 0.0)
    weight_high, weight_low = split(weight)
    cols_mix[...] = weight
    mix[0:COL, :] = weight_high
    mix[COL : 2 * COL, :] = weight_high
    mix[2 * COL : 3 * COL, :] = weight_low
    cells = iota((LON, SLOTS), 0)
    weight = jnp.where(cells == base_row, 1.0 - along, 0.0) + jnp.where(cells == base_row + 1, along, 0.0)
    rows_mix[...] = weight
    weight_high, weight_low = split(jnp.concatenate([weight, jnp.zeros((COL - LON, SLOTS), F32)], axis=0))
    rows_split[0:COL, :] = weight_high
    rows_split[COL : 2 * COL, :] = weight_high
    rows_split[2 * COL : 3 * COL, :] = weight_low

    copies[2].wait()
    spot = iota((1, SLOTS), 1)
    sides = jnp.where(spot < SIDE, jnp.maximum(slots_ref[:, 0:SLOTS], slots_ref[:, SIDE : SIDE + SLOTS]) + 1, 0)
    digits = jnp.concatenate([lax.div(sides, COL), lax.rem(sides, COL), jnp.zeros((6, SLOTS), I32)], axis=0)
    source, target = iota((SLOTS, SLOTS), 0), iota((SLOTS, SLOTS), 1)
    layer = jnp.where(target >= LON, 1, 0) + jnp.where(target >= 2 * LON, 1, 0)
    order = jnp.logical_and(target < SIDE, source == HALO * (target - LON * layer) + layer)
    digits = dot(digits.astype(F32).astype(BF16), jnp.where(order, 1.0, 0.0).astype(BF16)).astype(I32)
    sides = digits[0:1, :] * COL + digits[1:2, :] - 1
    idx_out[0:1, :] = sides[:, 0:COL]
    idx_out[1:2, :] = sides[:, COL : 2 * COL]
    for h in range(HALO):
        at = 2 * SIDE + h * COL
        idx_out[2 + h : 3 + h, :] = jnp.maximum(
            slots_ref[:, at : at + COL], slots_ref[:, at + HALO * COL : at + HALO * COL + COL]
        )
    idx_out[5:8, :] = jnp.full((3, COL), -1, I32)

    place = (col * COL + iota((1, COL), 1)).astype(F32)
    scale = 1.0 / jnp.sin(math.pi / 4.0 + (place + 0.5) * (math.pi / 2.0 / (COL * n_col)))
    copies[3].wait()

    def load_split(part, pair):
        block = jnp.concatenate(
            [frame[part, pl.ds(pl.multiple_of((8 * pair + q) * STRIDE + 8, 8), LON), :] for q in range(8)], axis=0
        )
        return split(block)

    def interpolate(part, half):
        for pair in range(PART // 8):
            high, low = load_split(part, 2 * half + pair)
            value = dot(jnp.concatenate([high, low, high], axis=1), mix[...])
            value = jnp.sum(value.reshape(8, LON, SLOTS) * rows_mix[...][None], axis=1)
            blocks[part, half, 8 * pair : 8 * pair + 8, :] = value

    def send(part, half):
        for step in AROUND:
            a_copy(part, step, half).start()

        @pl.when(core != half)
        def _():
            s_copy(part, half).start()

        @pl.when(core == half)
        def _():
            table[part, member] = blocks[part, half]

    def lane_pass(part):
        def body(pair, carry):
            high, low = load_split(part, pair)
            both = jnp.concatenate([high, low], axis=1)
            lanes[pl.ds(pl.multiple_of(8 * LON * pair, 8), 8 * LON), :] = dot(both, band[...])
            return carry

        lax.fori_loop(0, FLAT // 8, body, 0)

    def cols_of(part):
        lane = iota((LON, COL), 1)
        for half in range(2):
            edge = jnp.zeros((LON, COL), F32)
            for g in range(FLAT // 2):
                at = (half * (FLAT // 2) + g) * STRIDE + 8
                moved = pltpu.roll(frame[part, at : at + LON, :], 8 * g + HALO, 1)
                edge = jnp.where(jnp.logical_and(lane >= 8 * g, lane < 8 * g + 2 * HALO), moved, edge)
            turned[half, :, 0:LON] = jnp.transpose(edge)
        for side in range(2):
            for j in range(HALO):
                first = (1 - side) * HALO + j
                for half in range(2):
                    col_own[part, side, j, half * (FLAT // 2) : (half + 1) * (FLAT // 2), :] = turned[
                        half, pl.ds(first, FLAT // 2, stride=8), :
                    ]
            col_out[part, side, 0] = jnp.where(
                iota((FLAT, COL), 1) < COL // 2, col_own[part, side, 0], pltpu.roll(col_own[part, side, 1], COL // 2, 1)
            )
            col_out[part, side, 1] = col_own[part, side, 2]

    def emf_pass(part):
        for r in range(SHELLS):
            def field(q):
                at = (q * SHELLS + r) * STRIDE + 8
                return frame[part, at : at + LON, :]

            m, b = [field(MR + i) for i in range(3)], [field(BR + i) for i in range(3)]
            for i, form in enumerate((cross_radial, cross_polar, cross_azimuthal)):
                at = (i * SHELLS + r) * STRIDE + 8
                emf[at : at + LON, :] = form(m, b)
        for i, at in ((0, FLAT), (2, FLAT + SHELLS)):
            block = jnp.concatenate(
                [emf[(i * SHELLS + r) * STRIDE + 8 : (i * SHELLS + r) * STRIDE + 8 + LON, :] for r in range(SHELLS)],
                axis=0,
            )
            high, low = split(block)
            lanes[at * LON : (at + SHELLS) * LON, 0:COL] = dot(
                jnp.concatenate([high, low], axis=1), band[:, 0:COL]
            )

    def main_pass(part, start, stop):
        def body(block, carry):
            here = pl.multiple_of(8 * block, 8)

            def near(f, apart):
                return frame[part, pl.ds(f * STRIDE + 8 + here + apart, 8), :]

            def near_emf(f, apart):
                return emf[pl.ds(f * STRIDE + 8 + here + apart, 8), :]

            def lane_first(f):
                return lanes[pl.ds(f * LON + here, 8), 0:COL]

            def lane_second(f):
                return lanes[pl.ds(f * LON + here, 8), COL : 2 * COL]

            def row_first(at):
                return 45.0 * (at[1] - at[-1]) - 9.0 * (at[2] - at[-2]) + (at[3] - at[-3])

            def row_second(at, centre):
                return (
                    270.0 * (at[1] + at[-1]) - 27.0 * (at[2] + at[-2]) + 2.0 * (at[3] + at[-3]) - 490.0 * centre
                )

            centre = [[near(q * SHELLS + r, 0) for r in range(SHELLS)] for q in range(QUANTITIES)]
            radial = [shell_first(x) for x in centre]
            radial_second = [None if q == S else shell_second(centre[q]) for q in range(QUANTITIES)]
            emf_centre = [[near_emf(i * SHELLS + r, 0) for r in range(SHELLS)] for i in range(3)]
            emf_radial = [None, shell_first(emf_centre[1]), shell_first(emf_centre[2])]
            for r in range(SHELLS):
                own = [centre[q][r] for q in range(QUANTITIES)]
                g, lap = [], []
                for q in range(QUANTITIES):
                    f = q * SHELLS + r
                    at = {d: near(f, d) for d in (-3, -2, -1, 1, 2, 3)}
                    g.append((radial[q][r], lane_first(f), scale * row_first(at)))
                    if q == S:
                        lap.append(None)
                    else:
                        lap.append(
                            radial_second[q][r] + lane_second(f) + (scale * scale) * row_second(at, own[q])
                        )
                m, b = own[MR:BR], own[BR:WARM]

                def advect(q):
                    return m[0] * g[q][0] + m[1] * g[q][1] + m[2] * g[q][2]

                div = g[MR][0] + g[MT][1] + g[MP][2]
                current = (g[BP][1] - g[BT][2], g[BR][2] - g[BP][0], g[BT][0] - g[BR][1])
                lorentz = (
                    current[1] * b[2] - current[2] * b[1],
                    current[2] * b[0] - current[0] * b[2],
                    current[0] * b[1] - current[1] * b[0],
                )
                grow, thin = jnp.exp(own[WARM]), jnp.exp(-own[S])
                emf_rows = {}
                for i in (0, 1):
                    f = i * SHELLS + r
                    emf_rows[i] = scale * row_first({d: near_emf(f, d) for d in (-3, -2, -1, 1, 2, 3)})
                turn = (
                    lane_first(FLAT + SHELLS + r) - emf_rows[1],
                    emf_rows[0] - emf_radial[2][r],
                    emf_radial[1][r] - lane_first(FLAT + r),
                )
                result = [-advect(S) - div]
                for i in range(3):
                    result.append(
                        -advect(MR + i) - grow * (g[S][i] + g[WARM][i]) + thin * lorentz[i] + SPREAD * lap[MR + i]
                    )
                for i in range(3):
                    result.append(turn[i] + SPREAD * lap[BR + i])
                result.append(-advect(WARM) - (2.0 / 3.0) * div + SPREAD * lap[WARM])
                for q in range(QUANTITIES):
                    f = q * SHELLS + r
                    value = own[q] + (TIME_STEP / 60.0) * result[q]
                    if part == 0:
                        frame[1, pl.ds(f * STRIDE + 8 + here, 8), :] = value
                    else:
                        start = frame[0, pl.ds(f * STRIDE + 8 + here, 8), :]
                        out_ref[pl.ds(f * LON + here, 8), :] = 0.5 * (start + value)
            return carry

        lax.fori_loop(start, stop, body, 0)

    def rows_of(part):
        for h in range(HALO):
            row_out[part, 0, h] = frame[part, pl.ds(8 + h, FLAT, stride=STRIDE), :]
            row_out[part, 1, h] = frame[part, pl.ds(8 + LON - HALO + h, FLAT, stride=STRIDE), :]

    def prepare_picks():
        for tile in range(2 * TILES):
            if tile < TARGETS:
                slot = idx_in[tile, 0:1, :]
            elif tile < TARGETS + 2:
                first = (tile - TARGETS) * GROUPS
                slot = idx_in[first, 1:2, :]
                for q in range(1, GROUPS):
                    slot = jnp.maximum(slot, pltpu.roll(idx_in[first + q], SPARE * q, 1)[1:2, :])
            else:
                side, h = divmod(tile - TARGETS - 2, HALO)
                slot = idx_in[side * (TARGETS - 1), 2 + h : 3 + h, :]
            slot = slot - mine * (GROUP * OUT)
            who = jnp.zeros_like(slot)
            for q in range(1, GROUP):
                who = who + jnp.where(slot >= q * OUT, 1, 0)
            cell = slot - who * OUT
            who = jnp.where(jnp.logical_and(slot >= 0, slot < GROUP * OUT), who, -1)
            at = (tile % 2) * COL
            owner[tile // 2, :, at : at + COL] = jnp.broadcast_to(who, (8, COL))
            hot = jnp.where(iota((SLOTS, COL), 0) == cell, 1.0, 0.0).astype(BF16)
            onehot[tile // 2, :, at : at + COL] = hot

    def table_split(part):
        high, low = split(table[part].reshape(GROUP * PART, SLOTS))
        return jnp.concatenate([high, low], axis=0)

    def pick(both, tile):
        value = dot(both, onehot[tile])
        value = value[0 : GROUP * PART] + value[GROUP * PART :]
        who = jnp.broadcast_to(owner[tile, 0:1, :], (PART, SLOTS))
        total = jnp.zeros((PART, SLOTS), F32)
        for q in range(GROUP):
            total = jnp.where(who == q, value[q * PART : (q + 1) * PART, :], total)
        return total[:, 0:COL], total[:, COL : 2 * COL]

    def pick_sides(part, both):
        rest = pick(both, TARGETS // 2)
        rest_rows[0], rest_rows[1] = rest
        spot = lax.div(iota((8, COL), 1), SPARE)
        for step in range(TARGETS // 2):
            tile = (step + mine) & (TARGETS // 2 - 1)
            ends = pick(both, tile)
            rows = rest_rows[tile >> 2]
            for i in range(2):
                target = 2 * tile + i
                there = target & (GROUPS - 1)
                total = jnp.zeros((8, COL), F32)
                for q in range(PART // 8):
                    moved = pltpu.roll(rows[8 * q : 8 * q + 8, :], SPARE * ((q + GROUPS - there) & (GROUPS - 1)), 1)
                    total = jnp.where(spot == q, moved, total)
                picked[part, target, 0:PART, :] = ends[i]
                picked[part, target, PART : PART + 8, :] = total
                b_copy(part, target).start()

    def pick_ends(part, both):
        ends = []
        for tile in range(TARGETS // 2 + 1, TILES):
            ends += pick(both, tile)
        for side in range(2):
            for h in range(HALO):
                picked_rows[part, side, h] = ends[side * HALO + h]
            l_copy(part, side).start()

    def corrections(part, side, along_lanes):
        halo_ref, own_ref, add_ref = (col_halo, col_own, col_add) if along_lanes else (row_halo, row_out, row_add)

        def scaled(value, power):
            for _ in range(0 if along_lanes else power):
                value = scale * value
            return value

        halo = [[halo_ref[side, h, q * SHELLS : (q + 1) * SHELLS, :] for q in range(QUANTITIES)] for h in range(HALO)]
        form = cross_azimuthal if along_lanes else cross_polar
        halo_emf = [(cross_radial(x[MR:BR], x[BR:WARM]), form(x[MR:BR], x[BR:WARM])) for x in halo]
        sign = -1.0 if side == 0 else 1.0
        firsts, seconds = (45.0 * sign, -9.0 * sign, sign), (270.0, -27.0, 2.0)
        for j in range(HALO):
            own = [own_ref[part, side, j, q * SHELLS : (q + 1) * SHELLS, :] for q in range(QUANTITIES)]

            def total(weights, of):
                result = None
                for m in (1, 2, 3):
                    h = j + 3 - m if side == 0 else m - 3 + j
                    if 0 <= h < HALO:
                        term = weights[m - 1] * of(h)
                        result = term if result is None else result + term
                return result

            d = [scaled(total(firsts, lambda h, q=q: halo[h][q]), 1) for q in range(QUANTITIES)]
            lap = [
                None if q == S else scaled(total(seconds, lambda h, q=q: halo[h][q]), 2) for q in range(QUANTITIES)
            ]
            radial = scaled(total(firsts, lambda h: halo_emf[h][0]), 1)
            second = scaled(total(firsts, lambda h: halo_emf[h][1]), 1)
            result = edge_rates(own, d, lap, second, radial, along_lanes)
            for q in range(QUANTITIES):
                add_ref[side, j, q * SHELLS : (q + 1) * SHELLS, :] = (TIME_STEP / 60.0 / (1 + part)) * result[q]

    def contribute(side, along_lanes):
        add_ref = col_add if along_lanes else row_add
        value = jnp.concatenate([add_ref[side, j] for j in range(HALO)], axis=0)
        if along_lanes:
            value = jnp.where(iota((HALO * FLAT, COL), 1) < LON, value, 0.0)
        high, low = split(value)
        value = dot(jnp.concatenate([high, low, high], axis=1), rows_split[...] if along_lanes else mix[...])
        total = jnp.zeros((FLAT, SLOTS), F32)
        for j in range(HALO):
            if along_lanes:
                at = j if side == 0 else COL - HALO + j
                weight = cols_mix[at : at + 1, :]
            else:
                at = j if side == 0 else LON - HALO + j
                weight = rows_mix[at : at + 1, :]
            total = total + weight * value[j * FLAT : (j + 1) * FLAT, :]
        for half in range(2):
            blocks[1, half] = blocks[1, half] + total[half * PART : (half + 1) * PART, :]

    def apply_edges(part):
        lane = iota((LON, COL), 1)
        border = jnp.logical_or(lane < HALO, lane >= COL - HALO)
        stride, lead = (STRIDE, 8) if part == 0 else (LON, 0)

        def get(rows):
            return frame[1, rows, :] if part == 0 else out_ref[rows, :]

        def put(rows, value):
            if part == 0:
                frame[1, rows, :] = value
            else:
                out_ref[rows, :] = value

        for side in range(2):
            for j in range(HALO):
                rows = pl.ds(lead + (j if side == 0 else LON - HALO + j), FLAT, stride=stride)
                put(rows, get(rows) + row_add[side, j])
                for half in range(2):
                    turned[half, pl.ds((1 - side) * HALO + j, FLAT // 2, stride=8), :] = col_add[
                        side, j, half * (FLAT // 2) : (half + 1) * (FLAT // 2), :
                    ]
        for half in range(2):
            edge = jnp.transpose(turned[half])[0:LON, :]
            for g in range(FLAT // 2):
                f = half * (FLAT // 2) + g
                added = jnp.where(border, pltpu.roll(edge, COL - 8 * g - HALO, 1), 0.0)
                rows = slice(f * stride + lead, f * stride + lead + LON)
                put(rows, get(rows) + added)

    def a_copy(part, step, half):
        return remote(
            blocks.at[part, half], table.at[part, member], a_send.at[part, half, step], a_recv.at[part, member],
            row_device(step, half),
        )

    def s_copy(part, half):
        return remote(
            blocks.at[part, half], table.at[part, member], s_send.at[part], a_recv.at[part, member], sibling
        )

    def a_arrival(part, step):
        there = (member + step) & (GROUP - 1)
        return remote(blocks.at[part, 0], table.at[part, there], s_send.at[part], a_recv.at[part, there], sibling)

    def b_copy(part, target):
        return remote(
            picked.at[part, target], got_cols.at[part, origin], b_send.at[part, target], b_recv.at[part, origin],
            target_device(target),
        )

    def b_arrival(part, source):
        return remote(
            picked.at[part, 0], got_cols.at[part, source], b_send.at[part, 0], b_recv.at[part, source],
            (other, lon, col),
        )

    def l_copy(part, side):
        return remote(
            picked_rows.at[part, side], got_rows.at[part, origin], l_send.at[part, side], l_recv.at[part, origin],
            target_device(side * (TARGETS - 1)),
        )

    def l_arrival(part, source):
        return remote(
            picked_rows.at[part, 0], got_rows.at[part, source], l_send.at[part, 0], l_recv.at[part, source],
            (other, lon, col),
        )

    def row_copy(part, side):
        return remote(
            row_out.at[part, 1 - side], row_in.at[part, side], r_send.at[part, side], r_recv.at[part, side],
            (panel, lon_up if side == 0 else lon_down, col),
        )

    def col_copy(part, side):
        return remote(
            col_out.at[part, 1 - side], col_in.at[part, side], c_send.at[part, side], c_recv.at[part, side],
            (panel, lon, col_up if side == 0 else col_down),
        )

    def idx_copy(target):
        return remote(
            idx_out, idx_in.at[origin], idx_send.at[target], idx_recv.at[origin], target_device(target)
        )

    def idx_arrival(source):
        return remote(idx_out, idx_in.at[source], idx_send.at[0], idx_recv.at[source], (other, lon, col))

    def inner_sides(part):
        for side in range(2):
            row_copy(part, side).wait_recv()

            @pl.when(lon != (0 if side == 0 else n_lon - 1))
            def _():
                row_halo[side] = row_in[part, side]
                corrections(part, side, False)
                if part == 0:
                    contribute(side, False)

            col_copy(part, side).wait_recv()

            @pl.when(col != (0 if side == 0 else n_col - 1))
            def _():
                pair = col_in[part, side, 0]
                col_halo[side, 0] = pair
                col_halo[side, 1] = pltpu.roll(pair, COL // 2, 1)
                col_halo[side, 2] = col_in[part, side, 1]
                corrections(part, side, True)
                if part == 0:
                    contribute(side, True)

    def outer_sides(part):
        for side in range(2):

            @pl.when(col == (0 if side == 0 else n_col - 1))
            def _():
                for source in range(TARGETS):
                    b_arrival(part, source).wait_recv()
                for half in range(2):
                    total = got_cols[part, half * GROUPS]
                    for group in range(1, GROUPS):
                        total = total + got_cols[part, half * GROUPS + group]
                    main, rest = total[0:PART], total[PART : PART + 8]
                    rows = slice(half * PART, (half + 1) * PART)
                    col_halo[side, 0, rows, :] = main
                    col_halo[side, 1, rows, :] = pltpu.roll(main, COL - LON, 1)
                    main = pltpu.roll(main, COL - 2 * LON, 1)
                    for q in range(PART // 8):
                        at = half * PART + 8 * q
                        col_halo[side, 2, at : at + 8, :] = jnp.where(
                            iota((8, COL), 1) < COL - 2 * LON,
                            main[8 * q : 8 * q + 8, :],
                            pltpu.roll(rest, (COL + COL - 2 * LON - SPARE * q) % COL, 1),
                        )
                corrections(part, side, True)
                if part == 0:
                    contribute(side, True)

            @pl.when(lon == (0 if side == 0 else n_lon - 1))
            def _():
                for source in range(TARGETS):
                    l_arrival(part, source).wait_recv()
                for half in range(2):
                    total = got_rows[part, half * GROUPS]
                    for group in range(1, GROUPS):
                        total = total + got_rows[part, half * GROUPS + group]
                    row_halo[side, :, half * PART : (half + 1) * PART, :] = total
                corrections(part, side, False)
                if part == 0:
                    contribute(side, False)

    for part in range(2):
        if part == 0:
            interpolate(0, 0)
            pl.semaphore_wait(barrier, 2 * len(AROUND) + 2 + TARGETS)
            send(0, 0)
            interpolate(0, 1)
            send(0, 1)
            for target in range(TARGETS):
                idx_copy(target).start()
        else:
            send(1, 0)
            send(1, 1)
            apply_edges(0)
        rows_of(part)
        for side in range(2):
            row_copy(part, side).start()
        cols_of(part)
        for side in range(2):
            col_copy(part, side).start()
        if part == 0:
            for source in range(TARGETS):
                idx_arrival(source).wait_recv()
            prepare_picks()
        for step in range(1, GROUP):
            a_arrival(part, step).wait_recv()
        both = table_split(part)

        @pl.when(col_edge)
        def _():
            pick_sides(part, both)

        pick_ends(part, both)
        lane_pass(part)
        emf_pass(part)
        main_pass(part, 0, 6)
        if part == 0:
            interpolate(1, 0)
            interpolate(1, 1)
        inner_sides(part)
        outer_sides(part)
    apply_edges(1)

    for target in range(TARGETS):
        idx_copy(target).wait_send()
    for part in range(2):
        for half in range(2):
            for step in AROUND:
                a_copy(part, step, half).wait_send()
        s_copy(part, 0).wait_send()
        for side in range(2):
            row_copy(part, side).wait_send()
            col_copy(part, side).wait_send()
            l_copy(part, side).wait_send()

        @pl.when(col_edge)
        def _():
            for target in range(TARGETS):
                b_copy(part, target).wait_send()


def shards(state, send_base, send_frac, recv_slots):
    rows = FLAT * LON
    dma = pltpu.SemaphoreType.DMA
    vmem = pltpu.VMEM
    scratch = [
        vmem((2, FLAT, STRIDE, COL), F32),
        vmem((1, OUT), I32),
        vmem((2, OUT), F32),
        vmem((1, recv_slots.shape[-1]), I32),
        vmem((3 * SHELLS * STRIDE, COL), F32),
        vmem(((FLAT + 2 * SHELLS) * LON, 2 * COL), F32),
        vmem((3 * COL, SLOTS), BF16),
        vmem((COL, SLOTS), F32),
        vmem((LON, SLOTS), F32),
        vmem((3 * COL, SLOTS), BF16),
        vmem((2 * COL, 2 * COL), BF16),
        vmem((TILES, SLOTS, 2 * COL), BF16),
        vmem((TILES, 8, 2 * COL), I32),
        vmem((2, COL, COL), F32),
        vmem((2, 2, PART, SLOTS), F32),
        vmem((2, GROUP, PART, SLOTS), F32),
        vmem((8, COL), I32),
        vmem((TARGETS, 8, COL), I32),
        vmem((2, PART, COL), F32),
        vmem((2, TARGETS, PART + 8, COL), F32),
        vmem((2, 2, HALO, PART, COL), F32),
        vmem((2, TARGETS, PART + 8, COL), F32),
        vmem((2, TARGETS, HALO, PART, COL), F32),
        vmem((2, 2, HALO, FLAT, COL), F32),
        vmem((2, 2, HALO, FLAT, COL), F32),
        vmem((2, 2, HALO, FLAT, COL), F32),
        vmem((2, 2, 2, FLAT, COL), F32),
        vmem((2, 2, 2, FLAT, COL), F32),
        vmem((2, HALO, FLAT, COL), F32),
        vmem((2, HALO, FLAT, COL), F32),
        vmem((2, HALO, FLAT, COL), F32),
        vmem((2, HALO, FLAT, COL), F32),
        dma((4,)),
        dma((TARGETS,)),
        dma((TARGETS,)),
        dma((2, 2, RING)),
        dma((2, GROUP)),
        dma((2,)),
        dma((2, TARGETS)),
        dma((2, TARGETS)),
        dma((2, 2)),
        dma((2, TARGETS)),
        dma((2, 2)),
        dma((2, 2)),
        dma((2, 2)),
        dma((2, 2)),
    ]
    result = pl.pallas_call(
        kernel,
        out_shape=jax.ShapeDtypeStruct((rows, COL), F32),
        in_specs=[pl.BlockSpec(memory_space=pltpu.HBM)] * 4,
        out_specs=pl.BlockSpec(memory_space=pltpu.VMEM),
        scratch_shapes=scratch,
        compiler_params=pltpu.CompilerParams(
            collective_id=0, has_side_effects=True, vmem_limit_bytes=40 * 1024 * 1024
        ),
    )(*(
        pltpu.with_memory_space_constraint(x, pltpu.HBM)
        for x in (state.reshape(FLAT, LON, COL), send_base[0], send_frac[0, 0], recv_slots[0])
    ))
    return result.reshape(state.shape)


def solution(mesh):
    placed = (
        P("panel", None, None, "lon", "colat"),
        P("panel", ("lon", "colat"), None),
        P("panel", ("lon", "colat"), None, None),
        P("panel", ("lon", "colat"), None),
    )
    return jax.shard_map(
        shards,
        mesh=mesh,
        in_specs=placed,
        out_specs=P("panel", None, None, "lon", "colat"),
        check_vma=False,
    )
```

```python
import math

import jax
import jax.numpy as jnp
from jax import lax
from jax.experimental import pallas as pl
from jax.experimental.pallas import tpu as pltpu
from jax.sharding import PartitionSpec as P

MESH = pl.DeviceIdType.MESH
F32, BF16, I32 = jnp.float32, jnp.bfloat16, jnp.int32

QUANTITIES = 8
SHELLS = 4
FLAT = QUANTITIES * SHELLS
LON = 48
COL = 128
HALO = 3
OUT = 240
SIDE = HALO * LON
SLOTS = 256
GROUP = 8
GROUPS = 8
AROUND = (1, 3, 2)
SPARE = SIDE - COL
PART = FLAT // 2
TARGETS = 2 * GROUPS
TILES = 8
RING = 4
STRIDE = LON + 16
TIME_STEP = 0.25
SPREAD = 0.1 / 3.0
S, MR, MT, MP, BR, BT, BP, WARM = range(QUANTITIES)


def dot(left, right):
    return jnp.dot(left, right, preferred_element_type=F32)


def split(value):
    high = value.astype(BF16)
    return high, (value - high.astype(F32)).astype(BF16)


def iota(shape, dim):
    return lax.broadcasted_iota(I32, shape, dim)


def cross_radial(m, b):
    return m[1] * b[2] - m[2] * b[1]


def cross_polar(m, b):
    return m[2] * b[0] - m[0] * b[2]


def cross_azimuthal(m, b):
    return m[0] * b[1] - m[1] * b[0]


def edge_rates(own, d, lap, emf_first, emf_second, along_lanes):
    grow, thin = jnp.exp(own[WARM]), jnp.exp(-own[S])
    b = own[BR:WARM]
    if along_lanes:
        vel, out = own[MT], MT
        lorentz = (d[BR] * b[1], -d[BR] * b[0] - d[BP] * b[2], d[BP] * b[1])
        turn = (emf_first, None, -emf_second)
    else:
        vel, out = own[MP], MP
        lorentz = (d[BR] * b[2], d[BT] * b[2], -d[BT] * b[1] - d[BR] * b[0])
        turn = (-emf_first, emf_second, None)
    result = [-vel * d[S] - d[out]]
    for i in range(3):
        rate = -vel * d[MR + i] + thin * lorentz[i] + SPREAD * lap[MR + i]
        if MR + i == out:
            rate = rate - grow * (d[S] + d[WARM])
        result.append(rate)
    for i in range(3):
        rate = SPREAD * lap[BR + i]
        result.append(rate if turn[i] is None else rate + turn[i])
    result.append(-vel * d[WARM] - (2.0 / 3.0) * d[out] + SPREAD * lap[WARM])
    return result


def shell_first(x):
    a, b = 8.0 * (x[3] - x[0]), 45.0
    return (
        b * (x[1] - x[0]) - 9.0 * (x[2] - x[0]) + (x[3] - x[0]),
        b * (x[2] - x[0]) - a,
        b * (x[3] - x[1]) - a,
        b * (x[3] - x[2]) - 9.0 * (x[3] - x[1]) + (x[3] - x[0]),
    )


def shell_second(x):
    return (
        2.0 * x[3] - 27.0 * x[2] + 270.0 * x[1] - 245.0 * x[0],
        245.0 * x[0] - 490.0 * x[1] + 270.0 * x[2] - 25.0 * x[3],
        245.0 * x[3] - 490.0 * x[2] + 270.0 * x[1] - 25.0 * x[0],
        2.0 * x[0] - 27.0 * x[1] + 270.0 * x[2] - 245.0 * x[3],
    )


def kernel(
    x_hbm, base_hbm, frac_hbm, slots_hbm, out_ref,
    deep, base_ref, frac_ref, slots_ref, emf, lanes, mix, cols_mix, rows_mix, rows_split, band, onehot, owner, turned,
    blocks, table, idx_out, idx_in, idx_ends, picked, picked_rows, got_cols, got_rows, row_out, row_in, col_own, col_out, col_in,
    row_halo, col_halo, row_add, col_add,
    in_sem, idx_send, idx_recv, e_send, e_recv, a_send, a_recv, s_send, b_send, b_recv, l_send, l_recv, r_send, r_recv, c_send, c_recv,
):
    panel, lon, col = lax.axis_index("panel"), lax.axis_index("lon"), lax.axis_index("colat")
    n_lon, n_col = lax.axis_size("lon"), lax.axis_size("colat")
    core, mine = lon & 1, lon >> 1
    member = core * n_col + col
    other = 1 - panel
    lon_up, lon_down = lax.rem(lon + 1, n_lon), lax.rem(lon + n_lon - 1, n_lon)
    col_up, col_down = lax.rem(col + 1, n_col), lax.rem(col + n_col - 1, n_col)
    outer = lax.rem(lon + 2 * core - 1 + n_lon, n_lon)
    col_edge = jnp.logical_or(col == 0, col == n_col - 1)

    sibling = (panel, lon + 1 - 2 * core, col)
    origin = core * GROUPS + mine
    lon_edge = jnp.logical_or(lon == 0, lon == n_lon - 1)
    target_col, target_core = (col >> 1) * (n_col - 1), (col ^ (col >> 1)) & 1
    source_col = col ^ core

    def row_device(step, half):
        return (panel, 2 * mine + half, (col + step) & (n_col - 1))

    def side_device(target):
        return (other, 2 * target + target_core, target_col)

    def end_device(side):
        return (other, side * (n_lon - 1), col)

    def side_source(source):
        return (other, 2 * (source % GROUPS) + source // GROUPS, source_col)

    def end_source(source):
        return (other, 2 * (source % GROUPS) + source // GROUPS, col)

    def remote(src, dst, send, recv, device):
        return pltpu.make_async_remote_copy(
            src_ref=src, dst_ref=dst, send_sem=send, recv_sem=recv, device_id=device, device_id_type=MESH
        )

    frame = deep.reshape(2, FLAT * STRIDE, COL)
    copies = [
        pltpu.make_async_copy(src, dst, in_sem.at[i])
        for i, (src, dst) in enumerate(
            (
                (frac_hbm, frac_ref),
                (base_hbm, base_ref),
                (slots_hbm, slots_ref),
                (x_hbm, deep.at[0, :, pl.ds(8, LON), :]),
            )
        )
    ]
    for copy in copies:
        copy.start()

    barrier = pltpu.get_barrier_semaphore()
    for step in AROUND:
        for half in range(2):
            pl.semaphore_signal(barrier, inc=1, device_id=row_device(step, half), device_id_type=MESH)
    pl.semaphore_signal(barrier, inc=1, device_id=sibling, device_id_type=MESH)
    for target in range(GROUPS):
        pl.semaphore_signal(barrier, inc=1, device_id=side_device(target), device_id_type=MESH)
    for side in range(2):
        pl.semaphore_signal(barrier, inc=1, device_id=end_device(side), device_id_type=MESH)

    @pl.when(col_edge)
    def _():
        for source in range(TARGETS):
            pl.semaphore_signal(barrier, inc=1, device_id=side_source(source), device_id_type=MESH)

    @pl.when(lon_edge)
    def _():
        for source in range(TARGETS):
            pl.semaphore_signal(barrier, inc=1, device_id=end_source(source), device_id_type=MESH)

    pl.semaphore_signal(barrier, inc=1, device_id=(panel, outer, col), device_id_type=MESH)

    zero_rows = jnp.zeros((8, COL), F32)
    for f in range(FLAT):
        for part in range(2):
            frame[part, f * STRIDE : f * STRIDE + 8, :] = zero_rows
            frame[part, f * STRIDE + 8 + LON : (f + 1) * STRIDE, :] = zero_rows
    for f in range(3 * SHELLS):
        emf[f * STRIDE : f * STRIDE + 8, :] = zero_rows
        emf[f * STRIDE + 8 + LON : (f + 1) * STRIDE, :] = zero_rows

    for half in range(2):
        turned[half, :, :] = jnp.zeros((COL, COL), F32)

    apart = iota((COL, COL), 0) - iota((COL, COL), 1)
    reach = jnp.abs(apart)
    first = jnp.where(reach == 1, 45.0, jnp.where(reach == 2, -9.0, jnp.where(reach == 3, 1.0, 0.0)))
    first = jnp.where(apart < 0, -first, first).astype(BF16)
    second = jnp.where(
        reach == 0, -490.0, jnp.where(reach == 1, 270.0, jnp.where(reach == 2, -27.0, jnp.where(reach == 3, 2.0, 0.0)))
    ).astype(BF16)
    for part in range(2):
        band[part * COL : (part + 1) * COL, 0:COL] = first
        band[part * COL : (part + 1) * COL, COL : 2 * COL] = second

    copies[0].wait()
    copies[1].wait()
    base = jnp.concatenate([base_ref[...], jnp.zeros((1, SLOTS - OUT), I32)], axis=1)
    base_row, base_col = lax.div(base, COL), lax.rem(base, COL)
    share = jnp.concatenate([frac_ref[...], jnp.zeros((2, SLOTS - OUT), F32)], axis=1)
    along, across = share[0:1, :], share[1:2, :]
    cells = iota((COL, SLOTS), 0)
    weight = jnp.where(cells == base_col, 1.0 - across, 0.0) + jnp.where(cells == base_col + 1, across, 0.0)
    weight_high, weight_low = split(weight)
    cols_mix[...] = weight
    mix[0:COL, :] = weight_high
    mix[COL : 2 * COL, :] = weight_high
    mix[2 * COL : 3 * COL, :] = weight_low
    cells = iota((LON, SLOTS), 0)
    weight = jnp.where(cells == base_row, 1.0 - along, 0.0) + jnp.where(cells == base_row + 1, along, 0.0)
    rows_mix[...] = weight
    weight_high, weight_low = split(jnp.concatenate([weight, jnp.zeros((COL - LON, SLOTS), F32)], axis=0))
    rows_split[0:COL, :] = weight_high
    rows_split[COL : 2 * COL, :] = weight_high
    rows_split[2 * COL : 3 * COL, :] = weight_low

    copies[2].wait()
    spot = iota((1, SLOTS), 1)
    sides = jnp.where(spot < SIDE, jnp.maximum(slots_ref[:, 0:SLOTS], slots_ref[:, SIDE : SIDE + SLOTS]) + 1, 0)
    digits = jnp.concatenate([lax.div(sides, COL), lax.rem(sides, COL), jnp.zeros((6, SLOTS), I32)], axis=0)
    source, target = iota((SLOTS, SLOTS), 0), iota((SLOTS, SLOTS), 1)
    layer = jnp.where(target >= LON, 1, 0) + jnp.where(target >= 2 * LON, 1, 0)
    order = jnp.logical_and(target < SIDE, source == HALO * (target - LON * layer) + layer)
    digits = dot(digits.astype(F32).astype(BF16), jnp.where(order, 1.0, 0.0).astype(BF16)).astype(I32)
    sides = digits[0:1, :] * COL + digits[1:2, :] - 1
    idx_out[0:1, :] = sides[:, 0:COL]
    idx_out[1:2, :] = sides[:, COL : 2 * COL]
    for h in range(HALO):
        at = 2 * SIDE + h * COL
        idx_out[2 + h : 3 + h, :] = jnp.maximum(
            slots_ref[:, at : at + COL], slots_ref[:, at + HALO * COL : at + HALO * COL + COL]
        )
    idx_out[5:8, :] = jnp.full((3, COL), -1, I32)

    place = (col * COL + iota((1, COL), 1)).astype(F32)
    scale = 1.0 / jnp.sin(math.pi / 4.0 + (place + 0.5) * (math.pi / 2.0 / (COL * n_col)))
    copies[3].wait()

    def load_split(part, pair):
        block = jnp.concatenate(
            [frame[part, pl.ds(pl.multiple_of((8 * pair + q) * STRIDE + 8, 8), LON), :] for q in range(8)], axis=0
        )
        return split(block)

    def interpolate(part, half):
        for pair in range(PART // 8):
            high, low = load_split(part, 2 * half + pair)
            value = dot(jnp.concatenate([high, low, high], axis=1), mix[...])
            value = jnp.sum(value.reshape(8, LON, SLOTS) * rows_mix[...][None], axis=1)
            blocks[part, half, 8 * pair : 8 * pair + 8, :] = value

    def send(part, half):
        for step in AROUND:
            a_copy(part, step, half).start()

        @pl.when(core != half)
        def _():
            s_copy(part, half).start()

        @pl.when(core == half)
        def _():
            table[part, member] = blocks[part, half]

    def lane_pass(part):
        def body(pair, carry):
            high, low = load_split(part, pair)
            both = jnp.concatenate([high, low], axis=1)
            lanes[pl.ds(pl.multiple_of(8 * LON * pair, 8), 8 * LON), :] = dot(both, band[...])
            return carry

        lax.fori_loop(0, FLAT // 8, body, 0)

    def cols_of(part):
        lane = iota((LON, COL), 1)
        for half in range(2):
            edge = jnp.zeros((LON, COL), F32)
            for g in range(FLAT // 2):
                at = (half * (FLAT // 2) + g) * STRIDE + 8
                moved = pltpu.roll(frame[part, at : at + LON, :], 8 * g + HALO, 1)
                edge = jnp.where(jnp.logical_and(lane >= 8 * g, lane < 8 * g + 2 * HALO), moved, edge)
            turned[half, :, 0:LON] = jnp.transpose(edge)
        for side in range(2):
            for j in range(HALO):
                first = (1 - side) * HALO + j
                for half in range(2):
                    col_own[part, side, j, half * (FLAT // 2) : (half + 1) * (FLAT // 2), :] = turned[
                        half, pl.ds(first, FLAT // 2, stride=8), :
                    ]
            col_out[part, side, 0] = jnp.where(
                iota((FLAT, COL), 1) < COL // 2, col_own[part, side, 0], pltpu.roll(col_own[part, side, 1], COL // 2, 1)
            )
            col_out[part, side, 1] = col_own[part, side, 2]

    def emf_pass(part):
        for r in range(SHELLS):
            def field(q):
                at = (q * SHELLS + r) * STRIDE + 8
                return frame[part, at : at + LON, :]

            m, b = [field(MR + i) for i in range(3)], [field(BR + i) for i in range(3)]
            for i, form in enumerate((cross_radial, cross_polar, cross_azimuthal)):
                at = (i * SHELLS + r) * STRIDE + 8
                emf[at : at + LON, :] = form(m, b)
        for i, at in ((0, FLAT), (2, FLAT + SHELLS)):
            block = jnp.concatenate(
                [emf[(i * SHELLS + r) * STRIDE + 8 : (i * SHELLS + r) * STRIDE + 8 + LON, :] for r in range(SHELLS)],
                axis=0,
            )
            high, low = split(block)
            lanes[at * LON : (at + SHELLS) * LON, 0:COL] = dot(
                jnp.concatenate([high, low], axis=1), band[:, 0:COL]
            )

    def main_pass(part, start, stop):
        def body(block, carry):
            here = pl.multiple_of(8 * block, 8)

            def near(f, apart):
                return frame[part, pl.ds(f * STRIDE + 8 + here + apart, 8), :]

            def near_emf(f, apart):
                return emf[pl.ds(f * STRIDE + 8 + here + apart, 8), :]

            def lane_first(f):
                return lanes[pl.ds(f * LON + here, 8), 0:COL]

            def lane_second(f):
                return lanes[pl.ds(f * LON + here, 8), COL : 2 * COL]

            def row_first(at):
                return 45.0 * (at[1] - at[-1]) - 9.0 * (at[2] - at[-2]) + (at[3] - at[-3])

            def row_second(at, centre):
                return (
                    270.0 * (at[1] + at[-1]) - 27.0 * (at[2] + at[-2]) + 2.0 * (at[3] + at[-3]) - 490.0 * centre
                )

            centre = [[near(q * SHELLS + r, 0) for r in range(SHELLS)] for q in range(QUANTITIES)]
            radial = [shell_first(x) for x in centre]
            radial_second = [None if q == S else shell_second(centre[q]) for q in range(QUANTITIES)]
            emf_centre = [[near_emf(i * SHELLS + r, 0) for r in range(SHELLS)] for i in range(3)]
            emf_radial = [None, shell_first(emf_centre[1]), shell_first(emf_centre[2])]
            for r in range(SHELLS):
                own = [centre[q][r] for q in range(QUANTITIES)]
                g, lap = [], []
                for q in range(QUANTITIES):
                    f = q * SHELLS + r
                    at = {d: near(f, d) for d in (-3, -2, -1, 1, 2, 3)}
                    g.append((radial[q][r], lane_first(f), scale * row_first(at)))
                    if q == S:
                        lap.append(None)
                    else:
                        lap.append(
                            radial_second[q][r] + lane_second(f) + (scale * scale) * row_second(at, own[q])
                        )
                m, b = own[MR:BR], own[BR:WARM]

                def advect(q):
                    return m[0] * g[q][0] + m[1] * g[q][1] + m[2] * g[q][2]

                div = g[MR][0] + g[MT][1] + g[MP][2]
                current = (g[BP][1] - g[BT][2], g[BR][2] - g[BP][0], g[BT][0] - g[BR][1])
                lorentz = (
                    current[1] * b[2] - current[2] * b[1],
                    current[2] * b[0] - current[0] * b[2],
                    current[0] * b[1] - current[1] * b[0],
                )
                grow, thin = jnp.exp(own[WARM]), jnp.exp(-own[S])
                emf_rows = {}
                for i in (0, 1):
                    f = i * SHELLS + r
                    emf_rows[i] = scale * row_first({d: near_emf(f, d) for d in (-3, -2, -1, 1, 2, 3)})
                turn = (
                    lane_first(FLAT + SHELLS + r) - emf_rows[1],
                    emf_rows[0] - emf_radial[2][r],
                    emf_radial[1][r] - lane_first(FLAT + r),
                )
                result = [-advect(S) - div]
                for i in range(3):
                    result.append(
                        -advect(MR + i) - grow * (g[S][i] + g[WARM][i]) + thin * lorentz[i] + SPREAD * lap[MR + i]
                    )
                for i in range(3):
                    result.append(turn[i] + SPREAD * lap[BR + i])
                result.append(-advect(WARM) - (2.0 / 3.0) * div + SPREAD * lap[WARM])
                for q in range(QUANTITIES):
                    f = q * SHELLS + r
                    value = own[q] + (TIME_STEP / 60.0) * result[q]
                    if part == 0:
                        frame[1, pl.ds(f * STRIDE + 8 + here, 8), :] = value
                    else:
                        start = frame[0, pl.ds(f * STRIDE + 8 + here, 8), :]
                        out_ref[pl.ds(f * LON + here, 8), :] = 0.5 * (start + value)
            return carry

        lax.fori_loop(start, stop, body, 0)

    def rows_of(part):
        for h in range(HALO):
            row_out[part, 0, h] = frame[part, pl.ds(8 + h, FLAT, stride=STRIDE), :]
            row_out[part, 1, h] = frame[part, pl.ds(8 + LON - HALO + h, FLAT, stride=STRIDE), :]

    def prepare_picks():
        for tile in range(2 * TILES):
            if tile < GROUPS:
                slot = idx_in[tile, 0:1, :]
            elif tile == GROUPS:
                slot = idx_in[0, 1:2, :]
                for q in range(1, GROUPS):
                    slot = jnp.maximum(slot, pltpu.roll(idx_in[q], SPARE * q, 1)[1:2, :])
            elif tile <= GROUPS + 2 * HALO:
                side, h = divmod(tile - GROUPS - 1, HALO)
                slot = idx_ends[side, 2 + h : 3 + h, :]
            else:
                slot = jnp.full((1, COL), -1, I32)
            slot = slot - mine * (GROUP * OUT)
            who = jnp.zeros_like(slot)
            for q in range(1, GROUP):
                who = who + jnp.where(slot >= q * OUT, 1, 0)
            cell = slot - who * OUT
            who = jnp.where(jnp.logical_and(slot >= 0, slot < GROUP * OUT), who, -1)
            at = (tile % 2) * COL
            owner[tile // 2, :, at : at + COL] = jnp.broadcast_to(who, (8, COL))
            hot = jnp.where(iota((SLOTS, COL), 0) == cell, 1.0, 0.0).astype(BF16)
            onehot[tile // 2, :, at : at + COL] = hot

    def table_split(part):
        high, low = split(table[part].reshape(GROUP * PART, SLOTS))
        return jnp.concatenate([high, low], axis=0)

    def pick(both, tile):
        value = dot(both, onehot[tile])
        value = value[0 : GROUP * PART] + value[GROUP * PART :]
        who = jnp.broadcast_to(owner[tile, 0:1, :], (PART, SLOTS))
        total = jnp.zeros((PART, SLOTS), F32)
        for q in range(GROUP):
            total = jnp.where(who == q, value[q * PART : (q + 1) * PART, :], total)
        return total[:, 0:COL], total[:, COL : 2 * COL]

    def pick_all(part, both):
        ends = []
        for tile in range(GROUPS // 2, TILES):
            ends += pick(both, tile)
        rest = ends[0]
        for side in range(2):
            for h in range(HALO):
                picked_rows[part, side, h] = ends[1 + side * HALO + h]
            l_copy(part, side).start()
        spot = lax.div(iota((8, COL), 1), SPARE)
        for tile in range(GROUPS // 2):
            ends = pick(both, tile)
            for i in range(2):
                target = 2 * tile + i
                total = jnp.zeros((8, COL), F32)
                for q in range(PART // 8):
                    rows, turn = rest[8 * q : 8 * q + 8, :], (q - target) % GROUPS
                    total = jnp.where(spot == q, pltpu.roll(rows, SPARE * turn, 1) if turn else rows, total)
                picked[part, target, 0:PART, :] = ends[i]
                picked[part, target, PART : PART + 8, :] = total
                b_copy(part, target).start()

    def corrections(part, side, along_lanes):
        halo_ref, own_ref, add_ref = (col_halo, col_own, col_add) if along_lanes else (row_halo, row_out, row_add)

        def scaled(value, power):
            for _ in range(0 if along_lanes else power):
                value = scale * value
            return value

        halo = [[halo_ref[side, h, q * SHELLS : (q + 1) * SHELLS, :] for q in range(QUANTITIES)] for h in range(HALO)]
        form = cross_azimuthal if along_lanes else cross_polar
        halo_emf = [(cross_radial(x[MR:BR], x[BR:WARM]), form(x[MR:BR], x[BR:WARM])) for x in halo]
        sign = -1.0 if side == 0 else 1.0
        firsts, seconds = (45.0 * sign, -9.0 * sign, sign), (270.0, -27.0, 2.0)
        for j in range(HALO):
            own = [own_ref[part, side, j, q * SHELLS : (q + 1) * SHELLS, :] for q in range(QUANTITIES)]

            def total(weights, of):
                result = None
                for m in (1, 2, 3):
                    h = j + 3 - m if side == 0 else m - 3 + j
                    if 0 <= h < HALO:
                        term = weights[m - 1] * of(h)
                        result = term if result is None else result + term
                return result

            d = [scaled(total(firsts, lambda h, q=q: halo[h][q]), 1) for q in range(QUANTITIES)]
            lap = [
                None if q == S else scaled(total(seconds, lambda h, q=q: halo[h][q]), 2) for q in range(QUANTITIES)
            ]
            radial = scaled(total(firsts, lambda h: halo_emf[h][0]), 1)
            second = scaled(total(firsts, lambda h: halo_emf[h][1]), 1)
            result = edge_rates(own, d, lap, second, radial, along_lanes)
            for q in range(QUANTITIES):
                add_ref[side, j, q * SHELLS : (q + 1) * SHELLS, :] = (TIME_STEP / 60.0 / (1 + part)) * result[q]

    def contribute(side, along_lanes):
        add_ref = col_add if along_lanes else row_add
        value = jnp.concatenate([add_ref[side, j] for j in range(HALO)], axis=0)
        if along_lanes:
            value = jnp.where(iota((HALO * FLAT, COL), 1) < LON, value, 0.0)
        high, low = split(value)
        value = dot(jnp.concatenate([high, low, high], axis=1), rows_split[...] if along_lanes else mix[...])
        total = jnp.zeros((FLAT, SLOTS), F32)
        for j in range(HALO):
            if along_lanes:
                at = j if side == 0 else COL - HALO + j
                weight = cols_mix[at : at + 1, :]
            else:
                at = j if side == 0 else LON - HALO + j
                weight = rows_mix[at : at + 1, :]
            total = total + weight * value[j * FLAT : (j + 1) * FLAT, :]
        for half in range(2):
            blocks[1, half] = blocks[1, half] + total[half * PART : (half + 1) * PART, :]

    def apply_edges(part):
        lane = iota((LON, COL), 1)
        border = jnp.logical_or(lane < HALO, lane >= COL - HALO)
        stride, lead = (STRIDE, 8) if part == 0 else (LON, 0)

        def get(rows):
            return frame[1, rows, :] if part == 0 else out_ref[rows, :]

        def put(rows, value):
            if part == 0:
                frame[1, rows, :] = value
            else:
                out_ref[rows, :] = value

        for side in range(2):
            for j in range(HALO):
                rows = pl.ds(lead + (j if side == 0 else LON - HALO + j), FLAT, stride=stride)
                put(rows, get(rows) + row_add[side, j])
                for half in range(2):
                    turned[half, pl.ds((1 - side) * HALO + j, FLAT // 2, stride=8), :] = col_add[
                        side, j, half * (FLAT // 2) : (half + 1) * (FLAT // 2), :
                    ]
        for half in range(2):
            edge = jnp.transpose(turned[half])[0:LON, :]
            for g in range(FLAT // 2):
                f = half * (FLAT // 2) + g
                added = jnp.where(border, pltpu.roll(edge, COL - 8 * g - HALO, 1), 0.0)
                rows = slice(f * stride + lead, f * stride + lead + LON)
                put(rows, get(rows) + added)

    def a_copy(part, step, half):
        return remote(
            blocks.at[part, half], table.at[part, member], a_send.at[part, half, step], a_recv.at[part, member],
            row_device(step, half),
        )

    def s_copy(part, half):
        return remote(
            blocks.at[part, half], table.at[part, member], s_send.at[part], a_recv.at[part, member], sibling
        )

    def a_arrival(part, step):
        there = (member + step) & (GROUP - 1)
        return remote(blocks.at[part, 0], table.at[part, there], s_send.at[part], a_recv.at[part, there], sibling)

    def b_copy(part, target):
        return remote(
            picked.at[part, target], got_cols.at[part, origin], b_send.at[part, target], b_recv.at[part, origin],
            side_device(target),
        )

    def b_arrival(part, source):
        return remote(
            picked.at[part, 0], got_cols.at[part, source], b_send.at[part, 0], b_recv.at[part, source],
            (other, lon, col),
        )

    def l_copy(part, side):
        return remote(
            picked_rows.at[part, side], got_rows.at[part, origin], l_send.at[part, side], l_recv.at[part, origin],
            end_device(side),
        )

    def l_arrival(part, source):
        return remote(
            picked_rows.at[part, 0], got_rows.at[part, source], l_send.at[part, 0], l_recv.at[part, source],
            (other, lon, col),
        )

    def row_copy(part, side):
        return remote(
            row_out.at[part, 1 - side], row_in.at[part, side], r_send.at[part, side], r_recv.at[part, side],
            (panel, lon_up if side == 0 else lon_down, col),
        )

    def col_copy(part, side):
        return remote(
            col_out.at[part, 1 - side], col_in.at[part, side], c_send.at[part, side], c_recv.at[part, side],
            (panel, lon, col_up if side == 0 else col_down),
        )

    def idx_copy(source):
        return remote(idx_out, idx_in.at[mine], idx_send.at[source], idx_recv.at[mine], side_source(source))

    def idx_arrival(target):
        return remote(idx_out, idx_in.at[target], idx_send.at[0], idx_recv.at[target], (other, lon, col))

    def end_copy(source):
        return remote(idx_out, idx_ends.at[core], e_send.at[source], e_recv.at[core], end_source(source))

    def end_arrival(side):
        return remote(idx_out, idx_ends.at[side], e_send.at[0], e_recv.at[side], (other, lon, col))

    def inner_sides(part):
        for side in range(2):
            row_copy(part, side).wait_recv()

            @pl.when(lon != (0 if side == 0 else n_lon - 1))
            def _():
                row_halo[side] = row_in[part, side]
                corrections(part, side, False)
                if part == 0:
                    contribute(side, False)

            col_copy(part, side).wait_recv()

            @pl.when(col != (0 if side == 0 else n_col - 1))
            def _():
                pair = col_in[part, side, 0]
                col_halo[side, 0] = pair
                col_halo[side, 1] = pltpu.roll(pair, COL // 2, 1)
                col_halo[side, 2] = col_in[part, side, 1]
                corrections(part, side, True)
                if part == 0:
                    contribute(side, True)

    def outer_sides(part):
        for side in range(2):

            @pl.when(col == (0 if side == 0 else n_col - 1))
            def _():
                for source in range(TARGETS):
                    b_arrival(part, source).wait_recv()
                for half in range(2):
                    total = got_cols[part, half * GROUPS]
                    for group in range(1, GROUPS):
                        total = total + got_cols[part, half * GROUPS + group]
                    main, rest = total[0:PART], total[PART : PART + 8]
                    rows = slice(half * PART, (half + 1) * PART)
                    col_halo[side, 0, rows, :] = main
                    col_halo[side, 1, rows, :] = pltpu.roll(main, COL - LON, 1)
                    main = pltpu.roll(main, COL - 2 * LON, 1)
                    for q in range(PART // 8):
                        at = half * PART + 8 * q
                        col_halo[side, 2, at : at + 8, :] = jnp.where(
                            iota((8, COL), 1) < COL - 2 * LON,
                            main[8 * q : 8 * q + 8, :],
                            pltpu.roll(rest, (COL + COL - 2 * LON - SPARE * q) % COL, 1),
                        )
                corrections(part, side, True)
                if part == 0:
                    contribute(side, True)

            @pl.when(lon == (0 if side == 0 else n_lon - 1))
            def _():
                for source in range(TARGETS):
                    l_arrival(part, source).wait_recv()
                for half in range(2):
                    total = got_rows[part, half * GROUPS]
                    for group in range(1, GROUPS):
                        total = total + got_rows[part, half * GROUPS + group]
                    row_halo[side, :, half * PART : (half + 1) * PART, :] = total
                corrections(part, side, False)
                if part == 0:
                    contribute(side, False)

    for part in range(2):
        if part == 0:
            interpolate(0, 0)
            greetings = 2 * len(AROUND) + 2 + GROUPS + 2
            greetings = greetings + jnp.where(col_edge, TARGETS, 0) + jnp.where(lon_edge, TARGETS, 0)
            pl.semaphore_wait(barrier, greetings)
            send(0, 0)
            interpolate(0, 1)
            send(0, 1)

            @pl.when(col_edge)
            def _():
                for source in range(TARGETS):
                    idx_copy(source).start()

            @pl.when(lon_edge)
            def _():
                for source in range(TARGETS):
                    end_copy(source).start()

        else:
            send(1, 0)
            send(1, 1)
            apply_edges(0)
        rows_of(part)
        for side in range(2):
            row_copy(part, side).start()
        cols_of(part)
        for side in range(2):
            col_copy(part, side).start()
        if part == 0:
            for target in range(GROUPS):
                idx_arrival(target).wait_recv()
            for side in range(2):
                end_arrival(side).wait_recv()
            prepare_picks()
        lane_pass(part)
        emf_pass(part)
        for step in range(1, GROUP):
            a_arrival(part, step).wait_recv()
        both = table_split(part)
        pick_all(part, both)
        main_pass(part, 0, 6)
        if part == 0:
            interpolate(1, 0)
            interpolate(1, 1)
        inner_sides(part)
        outer_sides(part)
    apply_edges(1)

    @pl.when(col_edge)
    def _():
        for source in range(TARGETS):
            idx_copy(source).wait_send()

    @pl.when(lon_edge)
    def _():
        for source in range(TARGETS):
            end_copy(source).wait_send()

    for part in range(2):
        for half in range(2):
            for step in AROUND:
                a_copy(part, step, half).wait_send()
        s_copy(part, 0).wait_send()
        for side in range(2):
            row_copy(part, side).wait_send()
            col_copy(part, side).wait_send()
            l_copy(part, side).wait_send()
        for target in range(GROUPS):
            b_copy(part, target).wait_send()


def shards(state, send_base, send_frac, recv_slots):
    rows = FLAT * LON
    dma = pltpu.SemaphoreType.DMA
    vmem = pltpu.VMEM
    scratch = [
        vmem((2, FLAT, STRIDE, COL), F32),
        vmem((1, OUT), I32),
        vmem((2, OUT), F32),
        vmem((1, recv_slots.shape[-1]), I32),
        vmem((3 * SHELLS * STRIDE, COL), F32),
        vmem(((FLAT + 2 * SHELLS) * LON, 2 * COL), F32),
        vmem((3 * COL, SLOTS), BF16),
        vmem((COL, SLOTS), F32),
        vmem((LON, SLOTS), F32),
        vmem((3 * COL, SLOTS), BF16),
        vmem((2 * COL, 2 * COL), BF16),
        vmem((TILES, SLOTS, 2 * COL), BF16),
        vmem((TILES, 8, 2 * COL), I32),
        vmem((2, COL, COL), F32),
        vmem((2, 2, PART, SLOTS), F32),
        vmem((2, GROUP, PART, SLOTS), F32),
        vmem((8, COL), I32),
        vmem((GROUPS, 8, COL), I32),
        vmem((2, 8, COL), I32),
        vmem((2, GROUPS, PART + 8, COL), F32),
        vmem((2, 2, HALO, PART, COL), F32),
        vmem((2, TARGETS, PART + 8, COL), F32),
        vmem((2, TARGETS, HALO, PART, COL), F32),
        vmem((2, 2, HALO, FLAT, COL), F32),
        vmem((2, 2, HALO, FLAT, COL), F32),
        vmem((2, 2, HALO, FLAT, COL), F32),
        vmem((2, 2, 2, FLAT, COL), F32),
        vmem((2, 2, 2, FLAT, COL), F32),
        vmem((2, HALO, FLAT, COL), F32),
        vmem((2, HALO, FLAT, COL), F32),
        vmem((2, HALO, FLAT, COL), F32),
        vmem((2, HALO, FLAT, COL), F32),
        dma((4,)),
        dma((TARGETS,)),
        dma((GROUPS,)),
        dma((TARGETS,)),
        dma((2,)),
        dma((2, 2, RING)),
        dma((2, GROUP)),
        dma((2,)),
        dma((2, GROUPS)),
        dma((2, TARGETS)),
        dma((2, 2)),
        dma((2, TARGETS)),
        dma((2, 2)),
        dma((2, 2)),
        dma((2, 2)),
        dma((2, 2)),
    ]
    result = pl.pallas_call(
        kernel,
        out_shape=jax.ShapeDtypeStruct((rows, COL), F32),
        in_specs=[pl.BlockSpec(memory_space=pltpu.HBM)] * 4,
        out_specs=pl.BlockSpec(memory_space=pltpu.VMEM),
        scratch_shapes=scratch,
        compiler_params=pltpu.CompilerParams(
            collective_id=0, has_side_effects=True, vmem_limit_bytes=40 * 1024 * 1024
        ),
    )(*(
        pltpu.with_memory_space_constraint(x, pltpu.HBM)
        for x in (state.reshape(FLAT, LON, COL), send_base[0], send_frac[0, 0], recv_slots[0])
    ))
    return result.reshape(state.shape)


def solution(mesh):
    placed = (
        P("panel", None, None, "lon", "colat"),
        P("panel", ("lon", "colat"), None),
        P("panel", ("lon", "colat"), None, None),
        P("panel", ("lon", "colat"), None),
    )
    return jax.shard_map(
        shards,
        mesh=mesh,
        in_specs=placed,
        out_specs=P("panel", None, None, "lon", "colat"),
        check_vma=False,
    )
```

```python
import math

import jax
import jax.numpy as jnp
from jax import lax
from jax.experimental import pallas as pl
from jax.experimental.pallas import tpu as pltpu
from jax.sharding import PartitionSpec as P

MESH = pl.DeviceIdType.MESH
F32, BF16, I32 = jnp.float32, jnp.bfloat16, jnp.int32

QUANTITIES = 8
SHELLS = 4
FLAT = QUANTITIES * SHELLS
LON = 48
COL = 128
HALO = 3
OUT = 240
SIDE = HALO * LON
SLOTS = 256
GROUP = 8
GROUPS = 8
AROUND = (1, 3, 2)
SPARE = SIDE - COL
PART = FLAT // 2
TARGETS = 2 * GROUPS
TILES = 12
RING = 4
FOLD = PART // 8
STRIDE = LON + 16
TIME_STEP = 0.25
SPREAD = 0.1 / 3.0
S, MR, MT, MP, BR, BT, BP, WARM = range(QUANTITIES)


def dot(left, right):
    return jnp.dot(left, right, preferred_element_type=F32)


def split(value):
    high = value.astype(BF16)
    return high, (value - high.astype(F32)).astype(BF16)


def iota(shape, dim):
    return lax.broadcasted_iota(I32, shape, dim)


def cross_radial(m, b):
    return m[1] * b[2] - m[2] * b[1]


def cross_polar(m, b):
    return m[2] * b[0] - m[0] * b[2]


def cross_azimuthal(m, b):
    return m[0] * b[1] - m[1] * b[0]


def edge_rates(own, d, lap, emf_first, emf_second, along_lanes):
    grow, thin = jnp.exp(own[WARM]), jnp.exp(-own[S])
    b = own[BR:WARM]
    if along_lanes:
        vel, out = own[MT], MT
        lorentz = (d[BR] * b[1], -d[BR] * b[0] - d[BP] * b[2], d[BP] * b[1])
        turn = (emf_first, None, -emf_second)
    else:
        vel, out = own[MP], MP
        lorentz = (d[BR] * b[2], d[BT] * b[2], -d[BT] * b[1] - d[BR] * b[0])
        turn = (-emf_first, emf_second, None)
    result = [-vel * d[S] - d[out]]
    for i in range(3):
        rate = -vel * d[MR + i] + thin * lorentz[i] + SPREAD * lap[MR + i]
        if MR + i == out:
            rate = rate - grow * (d[S] + d[WARM])
        result.append(rate)
    for i in range(3):
        rate = SPREAD * lap[BR + i]
        result.append(rate if turn[i] is None else rate + turn[i])
    result.append(-vel * d[WARM] - (2.0 / 3.0) * d[out] + SPREAD * lap[WARM])
    return result


def shell_first(x):
    a, b = 8.0 * (x[3] - x[0]), 45.0
    return (
        b * (x[1] - x[0]) - 9.0 * (x[2] - x[0]) + (x[3] - x[0]),
        b * (x[2] - x[0]) - a,
        b * (x[3] - x[1]) - a,
        b * (x[3] - x[2]) - 9.0 * (x[3] - x[1]) + (x[3] - x[0]),
    )


def shell_second(x):
    return (
        2.0 * x[3] - 27.0 * x[2] + 270.0 * x[1] - 245.0 * x[0],
        245.0 * x[0] - 490.0 * x[1] + 270.0 * x[2] - 25.0 * x[3],
        245.0 * x[3] - 490.0 * x[2] + 270.0 * x[1] - 25.0 * x[0],
        2.0 * x[0] - 27.0 * x[1] + 270.0 * x[2] - 245.0 * x[3],
    )


def kernel(
    x_hbm, base_hbm, frac_hbm, slots_hbm, out_ref,
    deep, base_ref, frac_ref, slots_ref, emf, lanes, mix, cols_mix, rows_mix, rows_split, band, onehot, owner, turned,
    blocks, table, idx_out, idx_in, rest_rows, picked, picked_rows, got_cols, got_rows, row_out, row_in, col_own, col_out, col_in,
    row_halo, col_halo, row_add, col_add,
    in_sem, idx_send, idx_recv, a_send, a_recv, s_send, b_send, b_recv, l_send, l_recv, r_send, r_recv, c_send, c_recv,
):
    panel, lon, col = lax.axis_index("panel"), lax.axis_index("lon"), lax.axis_index("colat")
    n_lon, n_col = lax.axis_size("lon"), lax.axis_size("colat")
    core, mine = lon & 1, lon >> 1
    member = core * n_col + col
    other = 1 - panel
    lon_up, lon_down = lax.rem(lon + 1, n_lon), lax.rem(lon + n_lon - 1, n_lon)
    col_up, col_down = lax.rem(col + 1, n_col), lax.rem(col + n_col - 1, n_col)
    outer = lax.rem(lon + 2 * core - 1 + n_lon, n_lon)
    col_edge = jnp.logical_or(col == 0, col == n_col - 1)

    sibling = (panel, lon + 1 - 2 * core, col)
    origin = core * GROUPS + mine

    def row_device(step, half):
        return (panel, 2 * mine + half, (col + step) & (n_col - 1))

    def target_device(target):
        return (other, 2 * (target & (GROUPS - 1)) + (target >> 3), col)

    def remote(src, dst, send, recv, device):
        return pltpu.make_async_remote_copy(
            src_ref=src, dst_ref=dst, send_sem=send, recv_sem=recv, device_id=device, device_id_type=MESH
        )

    frame = deep.reshape(2, FLAT * STRIDE, COL)
    copies = [
        pltpu.make_async_copy(src, dst, in_sem.at[i])
        for i, (src, dst) in enumerate(
            (
                (frac_hbm, frac_ref),
                (base_hbm, base_ref),
                (slots_hbm, slots_ref),
                (x_hbm, deep.at[0, :, pl.ds(8, LON), :]),
            )
        )
    ]
    for copy in copies:
        copy.start()

    barrier = pltpu.get_barrier_semaphore()
    for step in AROUND:
        for half in range(2):
            pl.semaphore_signal(barrier, inc=1, device_id=row_device(step, half), device_id_type=MESH)
    pl.semaphore_signal(barrier, inc=1, device_id=sibling, device_id_type=MESH)
    for target in range(TARGETS):
        pl.semaphore_signal(barrier, inc=1, device_id=target_device(target), device_id_type=MESH)
    pl.semaphore_signal(barrier, inc=1, device_id=(panel, outer, col), device_id_type=MESH)

    copies[0].wait()
    copies[1].wait()
    base = jnp.concatenate([base_ref[...], jnp.zeros((1, SLOTS - OUT), I32)], axis=1)
    base_row, base_col = lax.div(base, COL), lax.rem(base, COL)
    share = jnp.concatenate([frac_ref[...], jnp.zeros((2, SLOTS - OUT), F32)], axis=1)
    along, across = share[0:1, :], share[1:2, :]
    cells = iota((COL, SLOTS), 0)
    weight = jnp.where(cells == base_col, 1.0 - across, 0.0) + jnp.where(cells == base_col + 1, across, 0.0)
    weight_high, weight_low = split(weight)
    cols_mix[...] = weight
    mix[0:COL, :] = weight_high
    mix[COL : 2 * COL, :] = weight_high
    mix[2 * COL : 3 * COL, :] = weight_low
    cells = iota((LON, SLOTS), 0)
    weight = jnp.where(cells == base_row, 1.0 - along, 0.0) + jnp.where(cells == base_row + 1, along, 0.0)
    rows_mix[...] = weight
    place = (col * COL + iota((1, COL), 1)).astype(F32)
    scale = 1.0 / jnp.sin(math.pi / 4.0 + (place + 0.5) * (math.pi / 2.0 / (COL * n_col)))
    copies[3].wait()

    def message_tables():
        copies[2].wait()
        spot = iota((1, SLOTS), 1)
        sides = jnp.where(spot < SIDE, jnp.maximum(slots_ref[:, 0:SLOTS], slots_ref[:, SIDE : SIDE + SLOTS]) + 1, 0)
        digits = jnp.concatenate([lax.div(sides, COL), lax.rem(sides, COL), jnp.zeros((6, SLOTS), I32)], axis=0)
        source, target = iota((SLOTS, SLOTS), 0), iota((SLOTS, SLOTS), 1)
        layer = jnp.where(target >= LON, 1, 0) + jnp.where(target >= 2 * LON, 1, 0)
        order = jnp.logical_and(target < SIDE, source == HALO * (target - LON * layer) + layer)
        digits = dot(digits.astype(F32).astype(BF16), jnp.where(order, 1.0, 0.0).astype(BF16)).astype(I32)
        sides = digits[0:1, :] * COL + digits[1:2, :] - 1
        idx_out[0:1, :] = sides[:, 0:COL]
        idx_out[1:2, :] = sides[:, COL : 2 * COL]
        for h in range(HALO):
            at = 2 * SIDE + h * COL
            idx_out[2 + h : 3 + h, :] = jnp.maximum(
                slots_ref[:, at : at + COL], slots_ref[:, at + HALO * COL : at + HALO * COL + COL]
            )
        idx_out[5:8, :] = jnp.full((3, COL), -1, I32)

    def other_tables():
        zero_rows = jnp.zeros((8, COL), F32)
        for f in range(FLAT):
            for part in range(2):
                frame[part, f * STRIDE : f * STRIDE + 8, :] = zero_rows
                frame[part, f * STRIDE + 8 + LON : (f + 1) * STRIDE, :] = zero_rows
        for f in range(3 * SHELLS):
            emf[f * STRIDE : f * STRIDE + 8, :] = zero_rows
            emf[f * STRIDE + 8 + LON : (f + 1) * STRIDE, :] = zero_rows

        for half in range(2):
            turned[half, :, :] = jnp.zeros((COL, COL), F32)

        apart = iota((COL, COL), 0) - iota((COL, COL), 1)
        reach = jnp.abs(apart)
        first = jnp.where(reach == 1, 45.0, jnp.where(reach == 2, -9.0, jnp.where(reach == 3, 1.0, 0.0)))
        first = jnp.where(apart < 0, -first, first).astype(BF16)
        second = jnp.where(
            reach == 0, -490.0, jnp.where(reach == 1, 270.0, jnp.where(reach == 2, -27.0, jnp.where(reach == 3, 2.0, 0.0)))
        ).astype(BF16)
        for part in range(2):
            band[part * COL : (part + 1) * COL, 0:COL] = first
            band[part * COL : (part + 1) * COL, COL : 2 * COL] = second
        weight_high, weight_low = split(jnp.concatenate([rows_mix[...], jnp.zeros((COL - LON, SLOTS), F32)], axis=0))
        rows_split[0:COL, :] = weight_high
        rows_split[COL : 2 * COL, :] = weight_high
        rows_split[2 * COL : 3 * COL, :] = weight_low

    def load_split(part, pair):
        block = jnp.concatenate(
            [frame[part, pl.ds(pl.multiple_of((8 * pair + q) * STRIDE + 8, 8), LON), :] for q in range(8)], axis=0
        )
        return split(block)

    def interpolate(part, half):
        for pair in range(PART // 8):
            high, low = load_split(part, 2 * half + pair)
            value = dot(jnp.concatenate([high, low, high], axis=1), mix[...])
            value = jnp.sum(value.reshape(8, LON, SLOTS) * rows_mix[...][None], axis=1)
            blocks[part, half, 8 * pair : 8 * pair + 8, :] = value

    def send(part, half):
        for step in AROUND:
            a_copy(part, step, half).start()

        @pl.when(core != half)
        def _():
            s_copy(part, half).start()

        @pl.when(core == half)
        def _():
            table[part, member] = blocks[part, half]

    def lane_pass(part):
        def body(pair, carry):
            high, low = load_split(part, pair)
            both = jnp.concatenate([high, low], axis=1)
            lanes[pl.ds(pl.multiple_of(8 * LON * pair, 8), 8 * LON), :] = dot(both, band[...])
            return carry

        lax.fori_loop(0, FLAT // 8, body, 0)

    def cols_of(part):
        lane = iota((LON, COL), 1)
        for half in range(2):
            edge = jnp.zeros((LON, COL), F32)
            for g in range(FLAT // 2):
                at = (half * (FLAT // 2) + g) * STRIDE + 8
                moved = pltpu.roll(frame[part, at : at + LON, :], 8 * g + HALO, 1)
                edge = jnp.where(jnp.logical_and(lane >= 8 * g, lane < 8 * g + 2 * HALO), moved, edge)
            turned[half, :, 0:LON] = jnp.transpose(edge)
        for side in range(2):
            for j in range(HALO):
                first = (1 - side) * HALO + j
                for half in range(2):
                    col_own[part, side, j, half * (FLAT // 2) : (half + 1) * (FLAT // 2), :] = turned[
                        half, pl.ds(first, FLAT // 2, stride=8), :
                    ]
            col_out[part, side, 0] = jnp.where(
                iota((FLAT, COL), 1) < COL // 2, col_own[part, side, 0], pltpu.roll(col_own[part, side, 1], COL // 2, 1)
            )
            col_out[part, side, 1] = col_own[part, side, 2]

    def emf_pass(part):
        for r in range(SHELLS):
            def field(q):
                at = (q * SHELLS + r) * STRIDE + 8
                return frame[part, at : at + LON, :]

            m, b = [field(MR + i) for i in range(3)], [field(BR + i) for i in range(3)]
            for i, form in enumerate((cross_radial, cross_polar, cross_azimuthal)):
                at = (i * SHELLS + r) * STRIDE + 8
                emf[at : at + LON, :] = form(m, b)
        for i, at in ((0, FLAT), (2, FLAT + SHELLS)):
            block = jnp.concatenate(
                [emf[(i * SHELLS + r) * STRIDE + 8 : (i * SHELLS + r) * STRIDE + 8 + LON, :] for r in range(SHELLS)],
                axis=0,
            )
            high, low = split(block)
            lanes[at * LON : (at + SHELLS) * LON, 0:COL] = dot(
                jnp.concatenate([high, low], axis=1), band[:, 0:COL]
            )

    def main_pass(part, start, stop):
        def body(block, carry):
            here = pl.multiple_of(8 * block, 8)

            def near(f, apart):
                return frame[part, pl.ds(f * STRIDE + 8 + here + apart, 8), :]

            def near_emf(f, apart):
                return emf[pl.ds(f * STRIDE + 8 + here + apart, 8), :]

            def lane_first(f):
                return lanes[pl.ds(f * LON + here, 8), 0:COL]

            def lane_second(f):
                return lanes[pl.ds(f * LON + here, 8), COL : 2 * COL]

            def row_first(at):
                return 45.0 * (at[1] - at[-1]) - 9.0 * (at[2] - at[-2]) + (at[3] - at[-3])

            def row_second(at, centre):
                return (
                    270.0 * (at[1] + at[-1]) - 27.0 * (at[2] + at[-2]) + 2.0 * (at[3] + at[-3]) - 490.0 * centre
                )

            centre = [[near(q * SHELLS + r, 0) for r in range(SHELLS)] for q in range(QUANTITIES)]
            radial = [shell_first(x) for x in centre]
            radial_second = [None if q == S else shell_second(centre[q]) for q in range(QUANTITIES)]
            emf_centre = [[near_emf(i * SHELLS + r, 0) for r in range(SHELLS)] for i in range(3)]
            emf_radial = [None, shell_first(emf_centre[1]), shell_first(emf_centre[2])]
            for r in range(SHELLS):
                own = [centre[q][r] for q in range(QUANTITIES)]
                g, lap = [], []
                for q in range(QUANTITIES):
                    f = q * SHELLS + r
                    at = {d: near(f, d) for d in (-3, -2, -1, 1, 2, 3)}
                    g.append((radial[q][r], lane_first(f), scale * row_first(at)))
                    if q == S:
                        lap.append(None)
                    else:
                        lap.append(
                            radial_second[q][r] + lane_second(f) + (scale * scale) * row_second(at, own[q])
                        )
                m, b = own[MR:BR], own[BR:WARM]

                def advect(q):
                    return m[0] * g[q][0] + m[1] * g[q][1] + m[2] * g[q][2]

                div = g[MR][0] + g[MT][1] + g[MP][2]
                current = (g[BP][1] - g[BT][2], g[BR][2] - g[BP][0], g[BT][0] - g[BR][1])
                lorentz = (
                    current[1] * b[2] - current[2] * b[1],
                    current[2] * b[0] - current[0] * b[2],
                    current[0] * b[1] - current[1] * b[0],
                )
                grow, thin = jnp.exp(own[WARM]), jnp.exp(-own[S])
                emf_rows = {}
                for i in (0, 1):
                    f = i * SHELLS + r
                    emf_rows[i] = scale * row_first({d: near_emf(f, d) for d in (-3, -2, -1, 1, 2, 3)})
                turn = (
                    lane_first(FLAT + SHELLS + r) - emf_rows[1],
                    emf_rows[0] - emf_radial[2][r],
                    emf_radial[1][r] - lane_first(FLAT + r),
                )
                result = [-advect(S) - div]
                for i in range(3):
                    result.append(
                        -advect(MR + i) - grow * (g[S][i] + g[WARM][i]) + thin * lorentz[i] + SPREAD * lap[MR + i]
                    )
                for i in range(3):
                    result.append(turn[i] + SPREAD * lap[BR + i])
                result.append(-advect(WARM) - (2.0 / 3.0) * div + SPREAD * lap[WARM])
                for q in range(QUANTITIES):
                    f = q * SHELLS + r
                    value = own[q] + (TIME_STEP / 60.0) * result[q]
                    if part == 0:
                        frame[1, pl.ds(f * STRIDE + 8 + here, 8), :] = value
                    else:
                        start = frame[0, pl.ds(f * STRIDE + 8 + here, 8), :]
                        out_ref[pl.ds(f * LON + here, 8), :] = 0.5 * (start + value)
            return carry

        lax.fori_loop(start, stop, body, 0)

    def rows_of(part):
        for h in range(HALO):
            row_out[part, 0, h] = frame[part, pl.ds(8 + h, FLAT, stride=STRIDE), :]
            row_out[part, 1, h] = frame[part, pl.ds(8 + LON - HALO + h, FLAT, stride=STRIDE), :]

    def prepare_picks():
        for tile in range(2 * TILES):
            if tile < TARGETS:
                slot = idx_in[tile, 0:1, :]
            elif tile < TARGETS + 2:
                first = (tile - TARGETS) * GROUPS
                slot = idx_in[first, 1:2, :]
                for q in range(1, GROUPS):
                    slot = jnp.maximum(slot, pltpu.roll(idx_in[first + q], SPARE * q, 1)[1:2, :])
            else:
                side, h = divmod(tile - TARGETS - 2, HALO)
                slot = idx_in[side * (TARGETS - 1), 2 + h : 3 + h, :]
            slot = slot - mine * (GROUP * OUT)
            who = jnp.zeros_like(slot)
            for q in range(1, GROUP):
                who = who + jnp.where(slot >= q * OUT, 1, 0)
            cell = slot - who * OUT
            who = jnp.where(jnp.logical_and(slot >= 0, slot < GROUP * OUT), who, -1)
            at = (tile % 2) * COL
            owner[tile // 2, :, at : at + COL] = jnp.broadcast_to(who, (8, COL))
            hot = jnp.where(iota((SLOTS, COL), 0) == cell, 1.0, 0.0).astype(BF16)
            onehot[tile // 2, :, at : at + COL] = hot

    def table_split(part):
        high, low = split(table[part].reshape(GROUP * PART, SLOTS))
        return jnp.concatenate([high, low], axis=0)

    def pick(both, tile):
        value = dot(both, onehot[tile])
        value = value[0 : GROUP * PART] + value[GROUP * PART :]
        who = jnp.broadcast_to(owner[tile, 0:1, :], (PART, SLOTS))
        total = jnp.zeros((PART, SLOTS), F32)
        for q in range(GROUP):
            total = jnp.where(who == q, value[q * PART : (q + 1) * PART, :], total)
        return total[:, 0:COL], total[:, COL : 2 * COL]

    def pick_sides(part, both):
        turn = (lax.div(iota((8, COL), 1), SPARE) - iota((8, COL), 0)) & 7
        for half, rest in enumerate(pick(both, TARGETS // 2)):
            for s in range(FOLD):
                total = jnp.zeros((8, COL), F32)
                for d in range(8):
                    moved = rest[8 * s : 8 * s + 8, :]
                    if d:
                        moved = pltpu.roll(pltpu.roll(moved, SPARE * d, 1), 8 - d, 0)
                    total = jnp.where(turn == d, moved, total)
                rest_rows[half, s] = total
        for step in range(TARGETS // 2):
            tile = (step + mine) & (TARGETS // 2 - 1)
            ends = pick(both, tile)
            for i in range(2):
                target = 2 * tile + i
                there = target & (GROUPS - 1)
                picked[part, target, 0:PART, :] = ends[i]
                for s in range(FOLD):
                    picked[part, target, PART + s : PART + s + 1, :] = rest_rows[tile >> 2, s, pl.ds(there, 1), :]
                b_copy(part, target).start()

    def pick_ends(part, both):
        ends = []
        for tile in range(TARGETS // 2 + 1, TILES):
            ends += pick(both, tile)
        for side in range(2):
            for h in range(HALO):
                picked_rows[part, side, h] = ends[side * HALO + h]
            l_copy(part, side).start()

    def corrections(part, side, along_lanes):
        halo_ref, own_ref, add_ref = (col_halo, col_own, col_add) if along_lanes else (row_halo, row_out, row_add)

        def scaled(value, power):
            for _ in range(0 if along_lanes else power):
                value = scale * value
            return value

        halo = [[halo_ref[side, h, q * SHELLS : (q + 1) * SHELLS, :] for q in range(QUANTITIES)] for h in range(HALO)]
        form = cross_azimuthal if along_lanes else cross_polar
        halo_emf = [(cross_radial(x[MR:BR], x[BR:WARM]), form(x[MR:BR], x[BR:WARM])) for x in halo]
        sign = -1.0 if side == 0 else 1.0
        firsts, seconds = (45.0 * sign, -9.0 * sign, sign), (270.0, -27.0, 2.0)
        for j in range(HALO):
            own = [own_ref[part, side, j, q * SHELLS : (q + 1) * SHELLS, :] for q in range(QUANTITIES)]

            def total(weights, of):
                result = None
                for m in (1, 2, 3):
                    h = j + 3 - m if side == 0 else m - 3 + j
                    if 0 <= h < HALO:
                        term = weights[m - 1] * of(h)
                        result = term if result is None else result + term
                return result

            d = [scaled(total(firsts, lambda h, q=q: halo[h][q]), 1) for q in range(QUANTITIES)]
            lap = [
                None if q == S else scaled(total(seconds, lambda h, q=q: halo[h][q]), 2) for q in range(QUANTITIES)
            ]
            radial = scaled(total(firsts, lambda h: halo_emf[h][0]), 1)
            second = scaled(total(firsts, lambda h: halo_emf[h][1]), 1)
            result = edge_rates(own, d, lap, second, radial, along_lanes)
            for q in range(QUANTITIES):
                add_ref[side, j, q * SHELLS : (q + 1) * SHELLS, :] = (TIME_STEP / 60.0 / (1 + part)) * result[q]

    def contribute(side, along_lanes):
        add_ref = col_add if along_lanes else row_add
        value = jnp.concatenate([add_ref[side, j] for j in range(HALO)], axis=0)
        if along_lanes:
            value = jnp.where(iota((HALO * FLAT, COL), 1) < LON, value, 0.0)
        high, low = split(value)
        value = dot(jnp.concatenate([high, low, high], axis=1), rows_split[...] if along_lanes else mix[...])
        total = jnp.zeros((FLAT, SLOTS), F32)
        for j in range(HALO):
            if along_lanes:
                at = j if side == 0 else COL - HALO + j
                weight = cols_mix[at : at + 1, :]
            else:
                at = j if side == 0 else LON - HALO + j
                weight = rows_mix[at : at + 1, :]
            total = total + weight * value[j * FLAT : (j + 1) * FLAT, :]
        for half in range(2):
            blocks[1, half] = blocks[1, half] + total[half * PART : (half + 1) * PART, :]

    def apply_edges(part):
        lane = iota((LON, COL), 1)
        border = jnp.logical_or(lane < HALO, lane >= COL - HALO)
        stride, lead = (STRIDE, 8) if part == 0 else (LON, 0)

        def get(rows):
            return frame[1, rows, :] if part == 0 else out_ref[rows, :]

        def put(rows, value):
            if part == 0:
                frame[1, rows, :] = value
            else:
                out_ref[rows, :] = value

        for side in range(2):
            for j in range(HALO):
                rows = pl.ds(lead + (j if side == 0 else LON - HALO + j), FLAT, stride=stride)
                put(rows, get(rows) + row_add[side, j])
                for half in range(2):
                    turned[half, pl.ds((1 - side) * HALO + j, FLAT // 2, stride=8), :] = col_add[
                        side, j, half * (FLAT // 2) : (half + 1) * (FLAT // 2), :
                    ]
        for half in range(2):
            edge = jnp.transpose(turned[half])[0:LON, :]
            for g in range(FLAT // 2):
                f = half * (FLAT // 2) + g
                added = jnp.where(border, pltpu.roll(edge, COL - 8 * g - HALO, 1), 0.0)
                rows = slice(f * stride + lead, f * stride + lead + LON)
                put(rows, get(rows) + added)

    def a_copy(part, step, half):
        return remote(
            blocks.at[part, half], table.at[part, member], a_send.at[part, half, step], a_recv.at[part, member],
            row_device(step, half),
        )

    def s_copy(part, half):
        return remote(
            blocks.at[part, half], table.at[part, member], s_send.at[part], a_recv.at[part, member], sibling
        )

    def a_arrival(part, step):
        there = (member + step) & (GROUP - 1)
        return remote(blocks.at[part, 0], table.at[part, there], s_send.at[part], a_recv.at[part, there], sibling)

    def b_copy(part, target):
        return remote(
            picked.at[part, target], got_cols.at[part, origin], b_send.at[part, target], b_recv.at[part, origin],
            target_device(target),
        )

    def b_arrival(part, source):
        return remote(
            picked.at[part, 0], got_cols.at[part, source], b_send.at[part, 0], b_recv.at[part, source],
            (other, lon, col),
        )

    def l_copy(part, side):
        return remote(
            picked_rows.at[part, side], got_rows.at[part, origin], l_send.at[part, side], l_recv.at[part, origin],
            target_device(side * (TARGETS - 1)),
        )

    def l_arrival(part, source):
        return remote(
            picked_rows.at[part, 0], got_rows.at[part, source], l_send.at[part, 0], l_recv.at[part, source],
            (other, lon, col),
        )

    def row_copy(part, side):
        return remote(
            row_out.at[part, 1 - side], row_in.at[part, side], r_send.at[part, side], r_recv.at[part, side],
            (panel, lon_up if side == 0 else lon_down, col),
        )

    def col_copy(part, side):
        return remote(
            col_out.at[part, 1 - side], col_in.at[part, side], c_send.at[part, side], c_recv.at[part, side],
            (panel, lon, col_up if side == 0 else col_down),
        )

    def idx_copy(target):
        return remote(
            idx_out, idx_in.at[origin], idx_send.at[target], idx_recv.at[origin], target_device(target)
        )

    def idx_arrival(source):
        return remote(idx_out, idx_in.at[source], idx_send.at[0], idx_recv.at[source], (other, lon, col))

    def inner_sides(part):
        for side in range(2):
            row_copy(part, side).wait_recv()

            @pl.when(lon != (0 if side == 0 else n_lon - 1))
            def _():
                row_halo[side] = row_in[part, side]
                corrections(part, side, False)
                if part == 0:
                    contribute(side, False)

            col_copy(part, side).wait_recv()

            @pl.when(col != (0 if side == 0 else n_col - 1))
            def _():
                pair = col_in[part, side, 0]
                col_halo[side, 0] = pair
                col_halo[side, 1] = pltpu.roll(pair, COL // 2, 1)
                col_halo[side, 2] = col_in[part, side, 1]
                corrections(part, side, True)
                if part == 0:
                    contribute(side, True)

    def outer_sides(part):
        for side in range(2):

            @pl.when(col == (0 if side == 0 else n_col - 1))
            def _():
                for source in range(TARGETS):
                    b_arrival(part, source).wait_recv()
                for half in range(2):
                    total = got_cols[part, half * GROUPS]
                    for group in range(1, GROUPS):
                        total = total + got_cols[part, half * GROUPS + group]
                    main = total[0:PART]
                    rows = slice(half * PART, (half + 1) * PART)
                    col_halo[side, 0, rows, :] = main
                    col_halo[side, 1, rows, :] = pltpu.roll(main, COL - LON, 1)
                    main = pltpu.roll(main, COL - 2 * LON, 1)
                    row, lane = iota((8, COL), 0), iota((8, COL), 1)
                    for s in range(FOLD):
                        value = main[8 * s : 8 * s + 8, :]
                        rest = jnp.broadcast_to(total[PART + s : PART + s + 1], (8, COL))
                        for q in range(8):
                            moved = pltpu.roll(rest, (2 * COL - 2 * LON - SPARE * q) % COL, 1)
                            value = jnp.where(jnp.logical_and(row == q, lane >= COL - 2 * LON), moved, value)
                        at = half * PART + 8 * s
                        col_halo[side, 2, at : at + 8, :] = value
                corrections(part, side, True)
                if part == 0:
                    contribute(side, True)

            @pl.when(lon == (0 if side == 0 else n_lon - 1))
            def _():
                for source in range(TARGETS):
                    l_arrival(part, source).wait_recv()
                for half in range(2):
                    total = got_rows[part, half * GROUPS]
                    for group in range(1, GROUPS):
                        total = total + got_rows[part, half * GROUPS + group]
                    row_halo[side, :, half * PART : (half + 1) * PART, :] = total
                corrections(part, side, False)
                if part == 0:
                    contribute(side, False)

    for part in range(2):
        if part == 0:
            interpolate(0, 0)
            pl.semaphore_wait(barrier, 2 * len(AROUND) + 2 + TARGETS)
            send(0, 0)
            interpolate(0, 1)
            send(0, 1)
            message_tables()
            for target in range(TARGETS):
                idx_copy(target).start()
            other_tables()
        else:
            send(1, 0)
            send(1, 1)
            apply_edges(0)
        rows_of(part)
        for side in range(2):
            row_copy(part, side).start()
        cols_of(part)
        for side in range(2):
            col_copy(part, side).start()
        if part == 0:
            for source in range(TARGETS):
                idx_arrival(source).wait_recv()
            prepare_picks()
        lane_pass(part)
        emf_pass(part)
        for step in range(1, GROUP):
            a_arrival(part, step).wait_recv()
        both = table_split(part)

        @pl.when(col_edge)
        def _():
            pick_sides(part, both)

        pick_ends(part, both)
        main_pass(part, 0, 6)
        if part == 0:
            interpolate(1, 0)
            interpolate(1, 1)
        inner_sides(part)
        outer_sides(part)
    apply_edges(1)

    for target in range(TARGETS):
        idx_copy(target).wait_send()
    for part in range(2):
        for half in range(2):
            for step in AROUND:
                a_copy(part, step, half).wait_send()
        s_copy(part, 0).wait_send()
        for side in range(2):
            row_copy(part, side).wait_send()
            col_copy(part, side).wait_send()
            l_copy(part, side).wait_send()

        @pl.when(col_edge)
        def _():
            for target in range(TARGETS):
                b_copy(part, target).wait_send()


def shards(state, send_base, send_frac, recv_slots):
    rows = FLAT * LON
    dma = pltpu.SemaphoreType.DMA
    vmem = pltpu.VMEM
    scratch = [
        vmem((2, FLAT, STRIDE, COL), F32),
        vmem((1, OUT), I32),
        vmem((2, OUT), F32),
        vmem((1, recv_slots.shape[-1]), I32),
        vmem((3 * SHELLS * STRIDE, COL), F32),
        vmem(((FLAT + 2 * SHELLS) * LON, 2 * COL), F32),
        vmem((3 * COL, SLOTS), BF16),
        vmem((COL, SLOTS), F32),
        vmem((LON, SLOTS), F32),
        vmem((3 * COL, SLOTS), BF16),
        vmem((2 * COL, 2 * COL), BF16),
        vmem((TILES, SLOTS, 2 * COL), BF16),
        vmem((TILES, 8, 2 * COL), I32),
        vmem((2, COL, COL), F32),
        vmem((2, 2, PART, SLOTS), F32),
        vmem((2, GROUP, PART, SLOTS), F32),
        vmem((8, COL), I32),
        vmem((TARGETS, 8, COL), I32),
        vmem((2, FOLD, 8, COL), F32),
        vmem((2, TARGETS, PART + FOLD, COL), F32),
        vmem((2, 2, HALO, PART, COL), F32),
        vmem((2, TARGETS, PART + FOLD, COL), F32),
        vmem((2, TARGETS, HALO, PART, COL), F32),
        vmem((2, 2, HALO, FLAT, COL), F32),
        vmem((2, 2, HALO, FLAT, COL), F32),
        vmem((2, 2, HALO, FLAT, COL), F32),
        vmem((2, 2, 2, FLAT, COL), F32),
        vmem((2, 2, 2, FLAT, COL), F32),
        vmem((2, HALO, FLAT, COL), F32),
        vmem((2, HALO, FLAT, COL), F32),
        vmem((2, HALO, FLAT, COL), F32),
        vmem((2, HALO, FLAT, COL), F32),
        dma((4,)),
        dma((TARGETS,)),
        dma((TARGETS,)),
        dma((2, 2, RING)),
        dma((2, GROUP)),
        dma((2,)),
        dma((2, TARGETS)),
        dma((2, TARGETS)),
        dma((2, 2)),
        dma((2, TARGETS)),
        dma((2, 2)),
        dma((2, 2)),
        dma((2, 2)),
        dma((2, 2)),
    ]
    result = pl.pallas_call(
        kernel,
        out_shape=jax.ShapeDtypeStruct((rows, COL), F32),
        in_specs=[pl.BlockSpec(memory_space=pltpu.HBM)] * 4,
        out_specs=pl.BlockSpec(memory_space=pltpu.VMEM),
        scratch_shapes=scratch,
        compiler_params=pltpu.CompilerParams(
            collective_id=0, has_side_effects=True, vmem_limit_bytes=40 * 1024 * 1024
        ),
    )(*(
        pltpu.with_memory_space_constraint(x, pltpu.HBM)
        for x in (state.reshape(FLAT, LON, COL), send_base[0], send_frac[0, 0], recv_slots[0])
    ))
    return result.reshape(state.shape)


def solution(mesh):
    placed = (
        P("panel", None, None, "lon", "colat"),
        P("panel", ("lon", "colat"), None),
        P("panel", ("lon", "colat"), None, None),
        P("panel", ("lon", "colat"), None),
    )
    return jax.shard_map(
        shards,
        mesh=mesh,
        in_specs=placed,
        out_specs=P("panel", None, None, "lon", "colat"),
        check_vma=False,
    )
```

```python
import math

import jax
import jax.numpy as jnp
from jax import lax
from jax.experimental import pallas as pl
from jax.experimental.pallas import tpu as pltpu
from jax.sharding import PartitionSpec as P

MESH = pl.DeviceIdType.MESH
F32, BF16, I32 = jnp.float32, jnp.bfloat16, jnp.int32

QUANTITIES = 8
SHELLS = 4
FLAT = QUANTITIES * SHELLS
LON = 48
COL = 128
HALO = 3
OUT = 240
SIDE = HALO * LON
SLOTS = 256
GROUP = 8
GROUPS = 8
AROUND = (1, 3, 2)
SPARE = SIDE - COL
PART = FLAT // 2
TARGETS = 2 * GROUPS
TILES = 12
RING = 4
FOLD = PART // 8
STRIDE = LON + 16
TIME_STEP = 0.25
SPREAD = 0.1 / 3.0
S, MR, MT, MP, BR, BT, BP, WARM = range(QUANTITIES)


def dot(left, right):
    return jnp.dot(left, right, preferred_element_type=F32)


def split(value):
    high = value.astype(BF16)
    return high, (value - high.astype(F32)).astype(BF16)


def iota(shape, dim):
    return lax.broadcasted_iota(I32, shape, dim)


def cross_radial(m, b):
    return m[1] * b[2] - m[2] * b[1]


def cross_polar(m, b):
    return m[2] * b[0] - m[0] * b[2]


def cross_azimuthal(m, b):
    return m[0] * b[1] - m[1] * b[0]


def edge_rates(own, d, lap, emf_first, emf_second, along_lanes):
    grow, thin = jnp.exp(own[WARM]), jnp.exp(-own[S])
    b = own[BR:WARM]
    if along_lanes:
        vel, out = own[MT], MT
        lorentz = (d[BR] * b[1], -d[BR] * b[0] - d[BP] * b[2], d[BP] * b[1])
        turn = (emf_first, None, -emf_second)
    else:
        vel, out = own[MP], MP
        lorentz = (d[BR] * b[2], d[BT] * b[2], -d[BT] * b[1] - d[BR] * b[0])
        turn = (-emf_first, emf_second, None)
    result = [-vel * d[S] - d[out]]
    for i in range(3):
        rate = -vel * d[MR + i] + thin * lorentz[i] + SPREAD * lap[MR + i]
        if MR + i == out:
            rate = rate - grow * (d[S] + d[WARM])
        result.append(rate)
    for i in range(3):
        rate = SPREAD * lap[BR + i]
        result.append(rate if turn[i] is None else rate + turn[i])
    result.append(-vel * d[WARM] - (2.0 / 3.0) * d[out] + SPREAD * lap[WARM])
    return result


def shell_first(x):
    a, b = 8.0 * (x[3] - x[0]), 45.0
    return (
        b * (x[1] - x[0]) - 9.0 * (x[2] - x[0]) + (x[3] - x[0]),
        b * (x[2] - x[0]) - a,
        b * (x[3] - x[1]) - a,
        b * (x[3] - x[2]) - 9.0 * (x[3] - x[1]) + (x[3] - x[0]),
    )


def shell_second(x):
    return (
        2.0 * x[3] - 27.0 * x[2] + 270.0 * x[1] - 245.0 * x[0],
        245.0 * x[0] - 490.0 * x[1] + 270.0 * x[2] - 25.0 * x[3],
        245.0 * x[3] - 490.0 * x[2] + 270.0 * x[1] - 25.0 * x[0],
        2.0 * x[0] - 27.0 * x[1] + 270.0 * x[2] - 245.0 * x[3],
    )


def kernel(
    x_hbm, base_hbm, frac_hbm, slots_hbm, out_ref,
    deep, base_ref, frac_ref, slots_ref, emf, lanes, mix, cols_mix, rows_mix, rows_split, band, onehot, owner, turned,
    blocks, table, idx_out, idx_in, rest_rows, picked, picked_rows, got_cols, got_rows, row_out, row_in, col_own, col_out, col_in,
    row_halo, col_halo, row_add, col_add,
    in_sem, idx_send, idx_recv, a_send, a_recv, s_send, b_send, b_recv, l_send, l_recv, r_send, r_recv, c_send, c_recv,
):
    panel, lon, col = lax.axis_index("panel"), lax.axis_index("lon"), lax.axis_index("colat")
    n_lon, n_col = lax.axis_size("lon"), lax.axis_size("colat")
    core, mine = lon & 1, lon >> 1
    member = core * n_col + col
    other = 1 - panel
    lon_up, lon_down = lax.rem(lon + 1, n_lon), lax.rem(lon + n_lon - 1, n_lon)
    col_up, col_down = lax.rem(col + 1, n_col), lax.rem(col + n_col - 1, n_col)
    outer = lax.rem(lon + 2 * core - 1 + n_lon, n_lon)
    col_edge = jnp.logical_or(col == 0, col == n_col - 1)

    sibling = (panel, lon + 1 - 2 * core, col)
    origin = core * GROUPS + mine

    def row_device(step, half):
        return (panel, 2 * mine + half, (col + step) & (n_col - 1))

    def target_device(target):
        return (other, 2 * (target & (GROUPS - 1)) + (target >> 3), col)

    def remote(src, dst, send, recv, device):
        return pltpu.make_async_remote_copy(
            src_ref=src, dst_ref=dst, send_sem=send, recv_sem=recv, device_id=device, device_id_type=MESH
        )

    frame = deep.reshape(2, FLAT * STRIDE, COL)
    copies = [
        pltpu.make_async_copy(src, dst, in_sem.at[i])
        for i, (src, dst) in enumerate(
            (
                (frac_hbm, frac_ref),
                (base_hbm, base_ref),
                (slots_hbm, slots_ref),
                (x_hbm, deep.at[0, :, pl.ds(8, LON), :]),
            )
        )
    ]
    for copy in copies:
        copy.start()

    barrier = pltpu.get_barrier_semaphore()
    for step in AROUND:
        for half in range(2):
            pl.semaphore_signal(barrier, inc=1, device_id=row_device(step, half), device_id_type=MESH)
    pl.semaphore_signal(barrier, inc=1, device_id=sibling, device_id_type=MESH)
    for target in range(TARGETS):
        pl.semaphore_signal(barrier, inc=1, device_id=target_device(target), device_id_type=MESH)
    pl.semaphore_signal(barrier, inc=1, device_id=(panel, outer, col), device_id_type=MESH)

    copies[0].wait()
    copies[1].wait()
    base = jnp.concatenate([base_ref[...], jnp.zeros((1, SLOTS - OUT), I32)], axis=1)
    base_row, base_col = lax.div(base, COL), lax.rem(base, COL)
    share = jnp.concatenate([frac_ref[...], jnp.zeros((2, SLOTS - OUT), F32)], axis=1)
    along, across = share[0:1, :], share[1:2, :]
    cells = iota((COL, SLOTS), 0)
    weight = jnp.where(cells == base_col, 1.0 - across, 0.0) + jnp.where(cells == base_col + 1, across, 0.0)
    weight_high, weight_low = split(weight)
    cols_mix[...] = weight
    mix[0:COL, :] = weight_high
    mix[COL : 2 * COL, :] = weight_high
    mix[2 * COL : 3 * COL, :] = weight_low
    cells = iota((LON, SLOTS), 0)
    weight = jnp.where(cells == base_row, 1.0 - along, 0.0) + jnp.where(cells == base_row + 1, along, 0.0)
    rows_mix[...] = weight
    place = (col * COL + iota((1, COL), 1)).astype(F32)
    scale = 1.0 / jnp.sin(math.pi / 4.0 + (place + 0.5) * (math.pi / 2.0 / (COL * n_col)))
    copies[3].wait()

    def message_tables():
        copies[2].wait()
        spot = iota((1, SLOTS), 1)
        sides = jnp.where(spot < SIDE, jnp.maximum(slots_ref[:, 0:SLOTS], slots_ref[:, SIDE : SIDE + SLOTS]) + 1, 0)
        digits = jnp.concatenate([lax.div(sides, COL), lax.rem(sides, COL), jnp.zeros((6, SLOTS), I32)], axis=0)
        source, target = iota((SLOTS, SLOTS), 0), iota((SLOTS, SLOTS), 1)
        layer = jnp.where(target >= LON, 1, 0) + jnp.where(target >= 2 * LON, 1, 0)
        order = jnp.logical_and(target < SIDE, source == HALO * (target - LON * layer) + layer)
        digits = dot(digits.astype(F32).astype(BF16), jnp.where(order, 1.0, 0.0).astype(BF16)).astype(I32)
        sides = digits[0:1, :] * COL + digits[1:2, :] - 1
        idx_out[0:1, :] = sides[:, 0:COL]
        idx_out[1:2, :] = sides[:, COL : 2 * COL]
        for h in range(HALO):
            at = 2 * SIDE + h * COL
            idx_out[2 + h : 3 + h, :] = jnp.maximum(
                slots_ref[:, at : at + COL], slots_ref[:, at + HALO * COL : at + HALO * COL + COL]
            )
        idx_out[5:8, :] = jnp.full((3, COL), -1, I32)

    def other_tables():
        zero_rows = jnp.zeros((8, COL), F32)
        for f in range(FLAT):
            for part in range(2):
                frame[part, f * STRIDE : f * STRIDE + 8, :] = zero_rows
                frame[part, f * STRIDE + 8 + LON : (f + 1) * STRIDE, :] = zero_rows
        for f in range(3 * SHELLS):
            emf[f * STRIDE : f * STRIDE + 8, :] = zero_rows
            emf[f * STRIDE + 8 + LON : (f + 1) * STRIDE, :] = zero_rows

        for half in range(2):
            turned[half, :, :] = jnp.zeros((COL, COL), F32)

        apart = iota((COL, COL), 0) - iota((COL, COL), 1)
        reach = jnp.abs(apart)
        first = jnp.where(reach == 1, 45.0, jnp.where(reach == 2, -9.0, jnp.where(reach == 3, 1.0, 0.0)))
        first = jnp.where(apart < 0, -first, first).astype(BF16)
        second = jnp.where(
            reach == 0, -490.0, jnp.where(reach == 1, 270.0, jnp.where(reach == 2, -27.0, jnp.where(reach == 3, 2.0, 0.0)))
        ).astype(BF16)
        for part in range(2):
            band[part * COL : (part + 1) * COL, 0:COL] = first
            band[part * COL : (part + 1) * COL, COL : 2 * COL] = second
        weight_high, weight_low = split(jnp.concatenate([rows_mix[...], jnp.zeros((COL - LON, SLOTS), F32)], axis=0))
        rows_split[0:COL, :] = weight_high
        rows_split[COL : 2 * COL, :] = weight_high
        rows_split[2 * COL : 3 * COL, :] = weight_low

    def load_split(part, pair):
        block = jnp.concatenate(
            [frame[part, pl.ds(pl.multiple_of((8 * pair + q) * STRIDE + 8, 8), LON), :] for q in range(8)], axis=0
        )
        return split(block)

    def interpolate(part, half):
        for pair in range(PART // 8):
            high, low = load_split(part, 2 * half + pair)
            value = dot(jnp.concatenate([high, low, high], axis=1), mix[...])
            value = jnp.sum(value.reshape(8, LON, SLOTS) * rows_mix[...][None], axis=1)
            blocks[part, half, 8 * pair : 8 * pair + 8, :] = value

    def send(part, half):
        for step in AROUND:
            a_copy(part, step, half).start()

        @pl.when(core != half)
        def _():
            s_copy(part, half).start()

        @pl.when(core == half)
        def _():
            table[part, member] = blocks[part, half]

    def lane_pass(part):
        def body(pair, carry):
            high, low = load_split(part, pair)
            both = jnp.concatenate([high, low], axis=1)
            lanes[pl.ds(pl.multiple_of(8 * LON * pair, 8), 8 * LON), :] = dot(both, band[...])
            return carry

        lax.fori_loop(0, FLAT // 8, body, 0)

    def cols_of(part):
        lane = iota((LON, COL), 1)
        for half in range(2):
            edge = jnp.zeros((LON, COL), F32)
            for g in range(FLAT // 2):
                at = (half * (FLAT // 2) + g) * STRIDE + 8
                moved = pltpu.roll(frame[part, at : at + LON, :], 8 * g + HALO, 1)
                edge = jnp.where(jnp.logical_and(lane >= 8 * g, lane < 8 * g + 2 * HALO), moved, edge)
            turned[half, :, 0:LON] = jnp.transpose(edge)
        for side in range(2):
            for j in range(HALO):
                first = (1 - side) * HALO + j
                for half in range(2):
                    col_own[part, side, j, half * (FLAT // 2) : (half + 1) * (FLAT // 2), :] = turned[
                        half, pl.ds(first, FLAT // 2, stride=8), :
                    ]
            col_out[part, side, 0] = jnp.where(
                iota((FLAT, COL), 1) < COL // 2, col_own[part, side, 0], pltpu.roll(col_own[part, side, 1], COL // 2, 1)
            )
            col_out[part, side, 1] = col_own[part, side, 2]

    def emf_pass(part):
        for r in range(SHELLS):
            def field(q):
                at = (q * SHELLS + r) * STRIDE + 8
                return frame[part, at : at + LON, :]

            m, b = [field(MR + i) for i in range(3)], [field(BR + i) for i in range(3)]
            for i, form in enumerate((cross_radial, cross_polar, cross_azimuthal)):
                at = (i * SHELLS + r) * STRIDE + 8
                emf[at : at + LON, :] = form(m, b)
        for i, at in ((0, FLAT), (2, FLAT + SHELLS)):
            block = jnp.concatenate(
                [emf[(i * SHELLS + r) * STRIDE + 8 : (i * SHELLS + r) * STRIDE + 8 + LON, :] for r in range(SHELLS)],
                axis=0,
            )
            high, low = split(block)
            lanes[at * LON : (at + SHELLS) * LON, 0:COL] = dot(
                jnp.concatenate([high, low], axis=1), band[:, 0:COL]
            )

    def main_pass(part, start, stop):
        def body(block, carry):
            here = pl.multiple_of(8 * block, 8)

            def near(f, apart):
                return frame[part, pl.ds(f * STRIDE + 8 + here + apart, 8), :]

            def near_emf(f, apart):
                return emf[pl.ds(f * STRIDE + 8 + here + apart, 8), :]

            def lane_first(f):
                return lanes[pl.ds(f * LON + here, 8), 0:COL]

            def lane_second(f):
                return lanes[pl.ds(f * LON + here, 8), COL : 2 * COL]

            def row_first(at):
                return 45.0 * (at[1] - at[-1]) - 9.0 * (at[2] - at[-2]) + (at[3] - at[-3])

            def row_second(at, centre):
                return (
                    270.0 * (at[1] + at[-1]) - 27.0 * (at[2] + at[-2]) + 2.0 * (at[3] + at[-3]) - 490.0 * centre
                )

            centre = [[near(q * SHELLS + r, 0) for r in range(SHELLS)] for q in range(QUANTITIES)]
            radial = [shell_first(x) for x in centre]
            radial_second = [None if q == S else shell_second(centre[q]) for q in range(QUANTITIES)]
            emf_centre = [[near_emf(i * SHELLS + r, 0) for r in range(SHELLS)] for i in range(3)]
            emf_radial = [None, shell_first(emf_centre[1]), shell_first(emf_centre[2])]
            for r in range(SHELLS):
                own = [centre[q][r] for q in range(QUANTITIES)]
                g, lap = [], []
                for q in range(QUANTITIES):
                    f = q * SHELLS + r
                    at = {d: near(f, d) for d in (-3, -2, -1, 1, 2, 3)}
                    g.append((radial[q][r], lane_first(f), scale * row_first(at)))
                    if q == S:
                        lap.append(None)
                    else:
                        lap.append(
                            radial_second[q][r] + lane_second(f) + (scale * scale) * row_second(at, own[q])
                        )
                m, b = own[MR:BR], own[BR:WARM]

                def advect(q):
                    return m[0] * g[q][0] + m[1] * g[q][1] + m[2] * g[q][2]

                div = g[MR][0] + g[MT][1] + g[MP][2]
                current = (g[BP][1] - g[BT][2], g[BR][2] - g[BP][0], g[BT][0] - g[BR][1])
                lorentz = (
                    current[1] * b[2] - current[2] * b[1],
                    current[2] * b[0] - current[0] * b[2],
                    current[0] * b[1] - current[1] * b[0],
                )
                grow, thin = jnp.exp(own[WARM]), jnp.exp(-own[S])
                emf_rows = {}
                for i in (0, 1):
                    f = i * SHELLS + r
                    emf_rows[i] = scale * row_first({d: near_emf(f, d) for d in (-3, -2, -1, 1, 2, 3)})
                turn = (
                    lane_first(FLAT + SHELLS + r) - emf_rows[1],
                    emf_rows[0] - emf_radial[2][r],
                    emf_radial[1][r] - lane_first(FLAT + r),
                )
                result = [-advect(S) - div]
                for i in range(3):
                    result.append(
                        -advect(MR + i) - grow * (g[S][i] + g[WARM][i]) + thin * lorentz[i] + SPREAD * lap[MR + i]
                    )
                for i in range(3):
                    result.append(turn[i] + SPREAD * lap[BR + i])
                result.append(-advect(WARM) - (2.0 / 3.0) * div + SPREAD * lap[WARM])
                for q in range(QUANTITIES):
                    f = q * SHELLS + r
                    value = own[q] + (TIME_STEP / 60.0) * result[q]
                    if part == 0:
                        frame[1, pl.ds(f * STRIDE + 8 + here, 8), :] = value
                    else:
                        start = frame[0, pl.ds(f * STRIDE + 8 + here, 8), :]
                        out_ref[pl.ds(f * LON + here, 8), :] = 0.5 * (start + value)
            return carry

        lax.fori_loop(start, stop, body, 0)

    def rows_of(part):
        for h in range(HALO):
            row_out[part, 0, h] = frame[part, pl.ds(8 + h, FLAT, stride=STRIDE), :]
            row_out[part, 1, h] = frame[part, pl.ds(8 + LON - HALO + h, FLAT, stride=STRIDE), :]

    def prepare_picks():
        for tile in range(2 * TILES):
            if tile < TARGETS:
                slot = idx_in[tile, 0:1, :]
            elif tile < TARGETS + 2:
                first = (tile - TARGETS) * GROUPS
                slot = idx_in[first, 1:2, :]
                for q in range(1, GROUPS):
                    slot = jnp.maximum(slot, pltpu.roll(idx_in[first + q], SPARE * q, 1)[1:2, :])
            else:
                side, h = divmod(tile - TARGETS - 2, HALO)
                slot = idx_in[side * (TARGETS - 1), 2 + h : 3 + h, :]
            slot = slot - mine * (GROUP * OUT)
            who = jnp.zeros_like(slot)
            for q in range(1, GROUP):
                who = who + jnp.where(slot >= q * OUT, 1, 0)
            cell = slot - who * OUT
            who = jnp.where(jnp.logical_and(slot >= 0, slot < GROUP * OUT), who, -1)
            at = (tile % 2) * COL
            owner[tile // 2, :, at : at + COL] = jnp.broadcast_to(who, (8, COL))
            hot = jnp.where(iota((SLOTS, COL), 0) == cell, 1.0, 0.0).astype(BF16)
            onehot[tile // 2, :, at : at + COL] = hot

    def table_split(part):
        high, low = split(table[part].reshape(GROUP * PART, SLOTS))
        return jnp.concatenate([high, low], axis=0)

    def product(both, tile):
        return dot(both, onehot[tile])

    def chosen(value, tile):
        value = value[0 : GROUP * PART] + value[GROUP * PART :]
        who = jnp.broadcast_to(owner[tile, 0:1, :], (PART, SLOTS))
        total = jnp.zeros((PART, SLOTS), F32)
        for q in range(GROUP):
            total = jnp.where(who == q, value[q * PART : (q + 1) * PART, :], total)
        return total[:, 0:COL], total[:, COL : 2 * COL]

    def fold(rests):
        turn = (lax.div(iota((8, COL), 1), SPARE) - iota((8, COL), 0)) & 7
        for half, rest in enumerate(rests):
            for s in range(FOLD):
                total = jnp.zeros((8, COL), F32)
                for d in range(8):
                    moved = rest[8 * s : 8 * s + 8, :]
                    if d:
                        moved = pltpu.roll(pltpu.roll(moved, SPARE * d, 1), 8 - d, 0)
                    total = jnp.where(turn == d, moved, total)
                rest_rows[half, s] = total

    def pick_all(part, both):
        sides = [(step + mine) & (TARGETS // 2 - 1) for step in range(TARGETS // 2)]
        extra = list(range(TARGETS // 2 + 1, TILES))
        ends, value = [], product(both, extra[0])
        for tile, after in zip(extra, extra[1:] + [None]):
            now = value
            if after is not None:
                value = product(both, after)
            ends += chosen(now, tile)
        for side in range(2):
            for h in range(HALO):
                picked_rows[part, side, h] = ends[side * HALO + h]
        for side in range(2):
            l_copy(part, side).start()

        @pl.when(col_edge)
        def _():
            now, value = product(both, TARGETS // 2), product(both, sides[0])
            fold(chosen(now, TARGETS // 2))
            for step, tile in enumerate(sides):
                now = value
                if step + 1 < len(sides):
                    value = product(both, sides[step + 1])
                for i, end in enumerate(chosen(now, tile)):
                    target = 2 * tile + i
                    picked[part, target, 0:PART, :] = end
                    for s in range(FOLD):
                        picked[part, target, PART + s : PART + s + 1, :] = rest_rows[
                            tile >> 2, s, pl.ds(target & (GROUPS - 1), 1), :
                        ]
                for i in range(2):
                    b_copy(part, 2 * tile + i).start()

    def corrections(part, side, along_lanes):
        halo_ref, own_ref, add_ref = (col_halo, col_own, col_add) if along_lanes else (row_halo, row_out, row_add)

        def scaled(value, power):
            for _ in range(0 if along_lanes else power):
                value = scale * value
            return value

        halo = [[halo_ref[side, h, q * SHELLS : (q + 1) * SHELLS, :] for q in range(QUANTITIES)] for h in range(HALO)]
        form = cross_azimuthal if along_lanes else cross_polar
        halo_emf = [(cross_radial(x[MR:BR], x[BR:WARM]), form(x[MR:BR], x[BR:WARM])) for x in halo]
        sign = -1.0 if side == 0 else 1.0
        firsts, seconds = (45.0 * sign, -9.0 * sign, sign), (270.0, -27.0, 2.0)
        for j in range(HALO):
            own = [own_ref[part, side, j, q * SHELLS : (q + 1) * SHELLS, :] for q in range(QUANTITIES)]

            def total(weights, of):
                result = None
                for m in (1, 2, 3):
                    h = j + 3 - m if side == 0 else m - 3 + j
                    if 0 <= h < HALO:
                        term = weights[m - 1] * of(h)
                        result = term if result is None else result + term
                return result

            d = [scaled(total(firsts, lambda h, q=q: halo[h][q]), 1) for q in range(QUANTITIES)]
            lap = [
                None if q == S else scaled(total(seconds, lambda h, q=q: halo[h][q]), 2) for q in range(QUANTITIES)
            ]
            radial = scaled(total(firsts, lambda h: halo_emf[h][0]), 1)
            second = scaled(total(firsts, lambda h: halo_emf[h][1]), 1)
            result = edge_rates(own, d, lap, second, radial, along_lanes)
            for q in range(QUANTITIES):
                add_ref[side, j, q * SHELLS : (q + 1) * SHELLS, :] = (TIME_STEP / 60.0 / (1 + part)) * result[q]

    def contribute(side, along_lanes):
        add_ref = col_add if along_lanes else row_add
        value = jnp.concatenate([add_ref[side, j] for j in range(HALO)], axis=0)
        if along_lanes:
            value = jnp.where(iota((HALO * FLAT, COL), 1) < LON, value, 0.0)
        high, low = split(value)
        value = dot(jnp.concatenate([high, low, high], axis=1), rows_split[...] if along_lanes else mix[...])
        total = jnp.zeros((FLAT, SLOTS), F32)
        for j in range(HALO):
            if along_lanes:
                at = j if side == 0 else COL - HALO + j
                weight = cols_mix[at : at + 1, :]
            else:
                at = j if side == 0 else LON - HALO + j
                weight = rows_mix[at : at + 1, :]
            total = total + weight * value[j * FLAT : (j + 1) * FLAT, :]
        for half in range(2):
            blocks[1, half] = blocks[1, half] + total[half * PART : (half + 1) * PART, :]

    def apply_edges(part):
        lane = iota((LON, COL), 1)
        border = jnp.logical_or(lane < HALO, lane >= COL - HALO)
        stride, lead = (STRIDE, 8) if part == 0 else (LON, 0)

        def get(rows):
            return frame[1, rows, :] if part == 0 else out_ref[rows, :]

        def put(rows, value):
            if part == 0:
                frame[1, rows, :] = value
            else:
                out_ref[rows, :] = value

        for side in range(2):
            for j in range(HALO):
                rows = pl.ds(lead + (j if side == 0 else LON - HALO + j), FLAT, stride=stride)
                put(rows, get(rows) + row_add[side, j])
                for half in range(2):
                    turned[half, pl.ds((1 - side) * HALO + j, FLAT // 2, stride=8), :] = col_add[
                        side, j, half * (FLAT // 2) : (half + 1) * (FLAT // 2), :
                    ]
        for half in range(2):
            edge = jnp.transpose(turned[half])[0:LON, :]
            for g in range(FLAT // 2):
                f = half * (FLAT // 2) + g
                added = jnp.where(border, pltpu.roll(edge, COL - 8 * g - HALO, 1), 0.0)
                rows = slice(f * stride + lead, f * stride + lead + LON)
                put(rows, get(rows) + added)

    def a_copy(part, step, half):
        return remote(
            blocks.at[part, half], table.at[part, member], a_send.at[part, half, step], a_recv.at[part, member],
            row_device(step, half),
        )

    def s_copy(part, half):
        return remote(
            blocks.at[part, half], table.at[part, member], s_send.at[part], a_recv.at[part, member], sibling
        )

    def a_arrival(part, step):
        there = (member + step) & (GROUP - 1)
        return remote(blocks.at[part, 0], table.at[part, there], s_send.at[part], a_recv.at[part, there], sibling)

    def b_copy(part, target):
        return remote(
            picked.at[part, target], got_cols.at[part, origin], b_send.at[part, target], b_recv.at[part, origin],
            target_device(target),
        )

    def b_arrival(part, source):
        return remote(
            picked.at[part, 0], got_cols.at[part, source], b_send.at[part, 0], b_recv.at[part, source],
            (other, lon, col),
        )

    def l_copy(part, side):
        return remote(
            picked_rows.at[part, side], got_rows.at[part, origin], l_send.at[part, side], l_recv.at[part, origin],
            target_device(side * (TARGETS - 1)),
        )

    def l_arrival(part, source):
        return remote(
            picked_rows.at[part, 0], got_rows.at[part, source], l_send.at[part, 0], l_recv.at[part, source],
            (other, lon, col),
        )

    def row_copy(part, side):
        return remote(
            row_out.at[part, 1 - side], row_in.at[part, side], r_send.at[part, side], r_recv.at[part, side],
            (panel, lon_up if side == 0 else lon_down, col),
        )

    def col_copy(part, side):
        return remote(
            col_out.at[part, 1 - side], col_in.at[part, side], c_send.at[part, side], c_recv.at[part, side],
            (panel, lon, col_up if side == 0 else col_down),
        )

    def idx_copy(target):
        return remote(
            idx_out, idx_in.at[origin], idx_send.at[target], idx_recv.at[origin], target_device(target)
        )

    def idx_arrival(source):
        return remote(idx_out, idx_in.at[source], idx_send.at[0], idx_recv.at[source], (other, lon, col))

    def inner_sides(part):
        for side in range(2):
            row_copy(part, side).wait_recv()

            @pl.when(lon != (0 if side == 0 else n_lon - 1))
            def _():
                row_halo[side] = row_in[part, side]
                corrections(part, side, False)
                if part == 0:
                    contribute(side, False)

            col_copy(part, side).wait_recv()

            @pl.when(col != (0 if side == 0 else n_col - 1))
            def _():
                pair = col_in[part, side, 0]
                col_halo[side, 0] = pair
                col_halo[side, 1] = pltpu.roll(pair, COL // 2, 1)
                col_halo[side, 2] = col_in[part, side, 1]
                corrections(part, side, True)
                if part == 0:
                    contribute(side, True)

    def outer_sides(part):
        for side in range(2):

            @pl.when(col == (0 if side == 0 else n_col - 1))
            def _():
                for source in range(TARGETS):
                    b_arrival(part, source).wait_recv()
                for half in range(2):
                    total = got_cols[part, half * GROUPS]
                    for group in range(1, GROUPS):
                        total = total + got_cols[part, half * GROUPS + group]
                    main = total[0:PART]
                    rows = slice(half * PART, (half + 1) * PART)
                    col_halo[side, 0, rows, :] = main
                    col_halo[side, 1, rows, :] = pltpu.roll(main, COL - LON, 1)
                    main = pltpu.roll(main, COL - 2 * LON, 1)
                    row, lane = iota((8, COL), 0), iota((8, COL), 1)
                    for s in range(FOLD):
                        value = main[8 * s : 8 * s + 8, :]
                        rest = jnp.broadcast_to(total[PART + s : PART + s + 1], (8, COL))
                        for q in range(8):
                            moved = pltpu.roll(rest, (2 * COL - 2 * LON - SPARE * q) % COL, 1)
                            value = jnp.where(jnp.logical_and(row == q, lane >= COL - 2 * LON), moved, value)
                        at = half * PART + 8 * s
                        col_halo[side, 2, at : at + 8, :] = value
                corrections(part, side, True)
                if part == 0:
                    contribute(side, True)

            @pl.when(lon == (0 if side == 0 else n_lon - 1))
            def _():
                for source in range(TARGETS):
                    l_arrival(part, source).wait_recv()
                for half in range(2):
                    total = got_rows[part, half * GROUPS]
                    for group in range(1, GROUPS):
                        total = total + got_rows[part, half * GROUPS + group]
                    row_halo[side, :, half * PART : (half + 1) * PART, :] = total
                corrections(part, side, False)
                if part == 0:
                    contribute(side, False)

    for part in range(2):
        if part == 0:
            interpolate(0, 0)
            pl.semaphore_wait(barrier, 2 * len(AROUND) + 2 + TARGETS)
            send(0, 0)
            interpolate(0, 1)
            send(0, 1)
            message_tables()
            for target in range(TARGETS):
                idx_copy(target).start()
            other_tables()
        else:
            send(1, 0)
            send(1, 1)
            apply_edges(0)
        rows_of(part)
        for side in range(2):
            row_copy(part, side).start()
        cols_of(part)
        for side in range(2):
            col_copy(part, side).start()
        if part == 0:
            for source in range(TARGETS):
                idx_arrival(source).wait_recv()
            prepare_picks()
        lane_pass(part)
        emf_pass(part)
        for step in range(1, GROUP):
            a_arrival(part, step).wait_recv()
        both = table_split(part)
        pick_all(part, both)
        main_pass(part, 0, 6)
        if part == 0:
            interpolate(1, 0)
            interpolate(1, 1)
        inner_sides(part)
        outer_sides(part)
    apply_edges(1)

    for target in range(TARGETS):
        idx_copy(target).wait_send()
    for part in range(2):
        for half in range(2):
            for step in AROUND:
                a_copy(part, step, half).wait_send()
        s_copy(part, 0).wait_send()
        for side in range(2):
            row_copy(part, side).wait_send()
            col_copy(part, side).wait_send()
            l_copy(part, side).wait_send()

        @pl.when(col_edge)
        def _():
            for target in range(TARGETS):
                b_copy(part, target).wait_send()


def shards(state, send_base, send_frac, recv_slots):
    rows = FLAT * LON
    dma = pltpu.SemaphoreType.DMA
    vmem = pltpu.VMEM
    scratch = [
        vmem((2, FLAT, STRIDE, COL), F32),
        vmem((1, OUT), I32),
        vmem((2, OUT), F32),
        vmem((1, recv_slots.shape[-1]), I32),
        vmem((3 * SHELLS * STRIDE, COL), F32),
        vmem(((FLAT + 2 * SHELLS) * LON, 2 * COL), F32),
        vmem((3 * COL, SLOTS), BF16),
        vmem((COL, SLOTS), F32),
        vmem((LON, SLOTS), F32),
        vmem((3 * COL, SLOTS), BF16),
        vmem((2 * COL, 2 * COL), BF16),
        vmem((TILES, SLOTS, 2 * COL), BF16),
        vmem((TILES, 8, 2 * COL), I32),
        vmem((2, COL, COL), F32),
        vmem((2, 2, PART, SLOTS), F32),
        vmem((2, GROUP, PART, SLOTS), F32),
        vmem((8, COL), I32),
        vmem((TARGETS, 8, COL), I32),
        vmem((2, FOLD, 8, COL), F32),
        vmem((2, TARGETS, PART + FOLD, COL), F32),
        vmem((2, 2, HALO, PART, COL), F32),
        vmem((2, TARGETS, PART + FOLD, COL), F32),
        vmem((2, TARGETS, HALO, PART, COL), F32),
        vmem((2, 2, HALO, FLAT, COL), F32),
        vmem((2, 2, HALO, FLAT, COL), F32),
        vmem((2, 2, HALO, FLAT, COL), F32),
        vmem((2, 2, 2, FLAT, COL), F32),
        vmem((2, 2, 2, FLAT, COL), F32),
        vmem((2, HALO, FLAT, COL), F32),
        vmem((2, HALO, FLAT, COL), F32),
        vmem((2, HALO, FLAT, COL), F32),
        vmem((2, HALO, FLAT, COL), F32),
        dma((4,)),
        dma((TARGETS,)),
        dma((TARGETS,)),
        dma((2, 2, RING)),
        dma((2, GROUP)),
        dma((2,)),
        dma((2, TARGETS)),
        dma((2, TARGETS)),
        dma((2, 2)),
        dma((2, TARGETS)),
        dma((2, 2)),
        dma((2, 2)),
        dma((2, 2)),
        dma((2, 2)),
    ]
    result = pl.pallas_call(
        kernel,
        out_shape=jax.ShapeDtypeStruct((rows, COL), F32),
        in_specs=[pl.BlockSpec(memory_space=pltpu.HBM)] * 4,
        out_specs=pl.BlockSpec(memory_space=pltpu.VMEM),
        scratch_shapes=scratch,
        compiler_params=pltpu.CompilerParams(
            collective_id=0, has_side_effects=True, vmem_limit_bytes=40 * 1024 * 1024
        ),
    )(*(
        pltpu.with_memory_space_constraint(x, pltpu.HBM)
        for x in (state.reshape(FLAT, LON, COL), send_base[0], send_frac[0, 0], recv_slots[0])
    ))
    return result.reshape(state.shape)


def solution(mesh):
    placed = (
        P("panel", None, None, "lon", "colat"),
        P("panel", ("lon", "colat"), None),
        P("panel", ("lon", "colat"), None, None),
        P("panel", ("lon", "colat"), None),
    )
    return jax.shard_map(
        shards,
        mesh=mesh,
        in_specs=placed,
        out_specs=P("panel", None, None, "lon", "colat"),
        check_vma=False,
    )
```

```python
import math

import jax
import jax.numpy as jnp
from jax import lax
from jax.experimental import pallas as pl
from jax.experimental.pallas import tpu as pltpu
from jax.sharding import PartitionSpec as P

MESH = pl.DeviceIdType.MESH
F32, BF16, I32 = jnp.float32, jnp.bfloat16, jnp.int32

QUANTITIES = 8
SHELLS = 4
FLAT = QUANTITIES * SHELLS
LON = 48
COL = 128
HALO = 3
OUT = 240
SIDE = HALO * LON
SLOTS = 256
GROUP = 8
GROUPS = 8
AROUND = (1, 3, 2)
SPARE = SIDE - COL
PART = FLAT // 2
TARGETS = 2 * GROUPS
TILES = 12
RING = 4
FOLD = PART // 8
STRIDE = LON + 16
TIME_STEP = 0.25
SPREAD = 0.1 / 3.0
S, MR, MT, MP, BR, BT, BP, WARM = range(QUANTITIES)


def dot(left, right):
    return jnp.dot(left, right, preferred_element_type=F32)


def split(value):
    high = value.astype(BF16)
    return high, (value - high.astype(F32)).astype(BF16)


def iota(shape, dim):
    return lax.broadcasted_iota(I32, shape, dim)


def cross_radial(m, b):
    return m[1] * b[2] - m[2] * b[1]


def cross_polar(m, b):
    return m[2] * b[0] - m[0] * b[2]


def cross_azimuthal(m, b):
    return m[0] * b[1] - m[1] * b[0]


def edge_rates(own, d, lap, emf_first, emf_second, along_lanes):
    grow, thin = jnp.exp(own[WARM]), jnp.exp(-own[S])
    b = own[BR:WARM]
    if along_lanes:
        vel, out = own[MT], MT
        lorentz = (d[BR] * b[1], -d[BR] * b[0] - d[BP] * b[2], d[BP] * b[1])
        turn = (emf_first, None, -emf_second)
    else:
        vel, out = own[MP], MP
        lorentz = (d[BR] * b[2], d[BT] * b[2], -d[BT] * b[1] - d[BR] * b[0])
        turn = (-emf_first, emf_second, None)
    result = [-vel * d[S] - d[out]]
    for i in range(3):
        rate = -vel * d[MR + i] + thin * lorentz[i] + SPREAD * lap[MR + i]
        if MR + i == out:
            rate = rate - grow * (d[S] + d[WARM])
        result.append(rate)
    for i in range(3):
        rate = SPREAD * lap[BR + i]
        result.append(rate if turn[i] is None else rate + turn[i])
    result.append(-vel * d[WARM] - (2.0 / 3.0) * d[out] + SPREAD * lap[WARM])
    return result


def shell_first(x):
    a, b = 8.0 * (x[3] - x[0]), 45.0
    return (
        b * (x[1] - x[0]) - 9.0 * (x[2] - x[0]) + (x[3] - x[0]),
        b * (x[2] - x[0]) - a,
        b * (x[3] - x[1]) - a,
        b * (x[3] - x[2]) - 9.0 * (x[3] - x[1]) + (x[3] - x[0]),
    )


def shell_second(x):
    return (
        2.0 * x[3] - 27.0 * x[2] + 270.0 * x[1] - 245.0 * x[0],
        245.0 * x[0] - 490.0 * x[1] + 270.0 * x[2] - 25.0 * x[3],
        245.0 * x[3] - 490.0 * x[2] + 270.0 * x[1] - 25.0 * x[0],
        2.0 * x[0] - 27.0 * x[1] + 270.0 * x[2] - 245.0 * x[3],
    )


def turn_edges(col_add, turned):
    for side in range(2):
        for j in range(HALO):
            for half in range(2):
                turned[half, pl.ds((1 - side) * HALO + j, FLAT // 2, stride=8), :] = col_add[
                    side, j, half * (FLAT // 2) : (half + 1) * (FLAT // 2), :
                ]


def field_edge(edge, g):
    lane = iota((LON, COL), 1)
    border = jnp.logical_or(lane < HALO, lane >= COL - HALO)
    return jnp.where(border, pltpu.roll(edge, COL - 8 * g - HALO, 1), 0.0)


def closing(value_ref, row_add, col_add, out_hbm, turned, ready, sem):
    turn_edges(col_add, turned)
    copies = []
    for half in range(2):
        edge = jnp.transpose(turned[half])[0:LON, :]
        for chunk in range(2):
            first = half * (FLAT // 2) + 8 * chunk
            for q in range(8):
                at = (first + q) * LON
                ready[at : at + LON, :] = value_ref[at : at + LON, :] + field_edge(edge, 8 * chunk + q)
            for side in range(2):
                for j in range(HALO):
                    rows = pl.ds(first * LON + (j if side == 0 else LON - HALO + j), 8, stride=LON)
                    ready[rows, :] = ready[rows, :] + row_add[side, j, first : first + 8, :]
            rows = pl.ds(first * LON, 8 * LON)
            copy = pltpu.make_async_copy(ready.at[rows, :], out_hbm.at[rows, :], sem.at[2 * half + chunk])
            copy.start()
            copies.append(copy)
    for copy in copies:
        copy.wait()


def kernel(
    x_hbm, base_hbm, frac_hbm, slots_hbm, out_ref, row_add, col_add,
    deep, base_ref, frac_ref, slots_ref, emf, lanes, mix, cols_mix, rows_mix, rows_split, band, onehot, owner, turned,
    blocks, table, idx_out, idx_in, rest_rows, picked, picked_rows, got_cols, got_rows, row_out, row_in, col_own, col_out, col_in,
    row_halo, col_halo,
    in_sem, idx_send, idx_recv, a_send, a_recv, s_send, b_send, b_recv, l_send, l_recv, r_send, r_recv, c_send, c_recv,
):
    panel, lon, col = lax.axis_index("panel"), lax.axis_index("lon"), lax.axis_index("colat")
    n_lon, n_col = lax.axis_size("lon"), lax.axis_size("colat")
    core, mine = lon & 1, lon >> 1
    member = core * n_col + col
    other = 1 - panel
    lon_up, lon_down = lax.rem(lon + 1, n_lon), lax.rem(lon + n_lon - 1, n_lon)
    col_up, col_down = lax.rem(col + 1, n_col), lax.rem(col + n_col - 1, n_col)
    outer = lax.rem(lon + 2 * core - 1 + n_lon, n_lon)
    col_edge = jnp.logical_or(col == 0, col == n_col - 1)

    sibling = (panel, lon + 1 - 2 * core, col)
    origin = core * GROUPS + mine

    def row_device(step, half):
        return (panel, 2 * mine + half, (col + step) & (n_col - 1))

    def target_device(target):
        return (other, 2 * (target & (GROUPS - 1)) + (target >> 3), col)

    def remote(src, dst, send, recv, device):
        return pltpu.make_async_remote_copy(
            src_ref=src, dst_ref=dst, send_sem=send, recv_sem=recv, device_id=device, device_id_type=MESH
        )

    frame = deep.reshape(2, FLAT * STRIDE, COL)
    copies = [
        pltpu.make_async_copy(src, dst, in_sem.at[i])
        for i, (src, dst) in enumerate(
            (
                (frac_hbm, frac_ref),
                (base_hbm, base_ref),
                (slots_hbm, slots_ref),
                (x_hbm, deep.at[0, :, pl.ds(8, LON), :]),
            )
        )
    ]
    for copy in copies:
        copy.start()

    barrier = pltpu.get_barrier_semaphore()
    for step in AROUND:
        for half in range(2):
            pl.semaphore_signal(barrier, inc=1, device_id=row_device(step, half), device_id_type=MESH)
    pl.semaphore_signal(barrier, inc=1, device_id=sibling, device_id_type=MESH)
    for target in range(TARGETS):
        pl.semaphore_signal(barrier, inc=1, device_id=target_device(target), device_id_type=MESH)
    pl.semaphore_signal(barrier, inc=1, device_id=(panel, outer, col), device_id_type=MESH)

    copies[0].wait()
    copies[1].wait()
    base = jnp.concatenate([base_ref[...], jnp.zeros((1, SLOTS - OUT), I32)], axis=1)
    base_row, base_col = lax.div(base, COL), lax.rem(base, COL)
    share = jnp.concatenate([frac_ref[...], jnp.zeros((2, SLOTS - OUT), F32)], axis=1)
    along, across = share[0:1, :], share[1:2, :]
    cells = iota((COL, SLOTS), 0)
    weight = jnp.where(cells == base_col, 1.0 - across, 0.0) + jnp.where(cells == base_col + 1, across, 0.0)
    weight_high, weight_low = split(weight)
    cols_mix[...] = weight
    mix[0:COL, :] = weight_high
    mix[COL : 2 * COL, :] = weight_high
    mix[2 * COL : 3 * COL, :] = weight_low
    cells = iota((LON, SLOTS), 0)
    weight = jnp.where(cells == base_row, 1.0 - along, 0.0) + jnp.where(cells == base_row + 1, along, 0.0)
    rows_mix[...] = weight
    place = (col * COL + iota((1, COL), 1)).astype(F32)
    scale = 1.0 / jnp.sin(math.pi / 4.0 + (place + 0.5) * (math.pi / 2.0 / (COL * n_col)))
    copies[3].wait()

    def message_tables():
        copies[2].wait()
        spot = iota((1, SLOTS), 1)
        sides = jnp.where(spot < SIDE, jnp.maximum(slots_ref[:, 0:SLOTS], slots_ref[:, SIDE : SIDE + SLOTS]) + 1, 0)
        digits = jnp.concatenate([lax.div(sides, COL), lax.rem(sides, COL), jnp.zeros((6, SLOTS), I32)], axis=0)
        source, target = iota((SLOTS, SLOTS), 0), iota((SLOTS, SLOTS), 1)
        layer = jnp.where(target >= LON, 1, 0) + jnp.where(target >= 2 * LON, 1, 0)
        order = jnp.logical_and(target < SIDE, source == HALO * (target - LON * layer) + layer)
        digits = dot(digits.astype(F32).astype(BF16), jnp.where(order, 1.0, 0.0).astype(BF16)).astype(I32)
        sides = digits[0:1, :] * COL + digits[1:2, :] - 1
        idx_out[0:1, :] = sides[:, 0:COL]
        idx_out[1:2, :] = sides[:, COL : 2 * COL]
        for h in range(HALO):
            at = 2 * SIDE + h * COL
            idx_out[2 + h : 3 + h, :] = jnp.maximum(
                slots_ref[:, at : at + COL], slots_ref[:, at + HALO * COL : at + HALO * COL + COL]
            )
        idx_out[5:8, :] = jnp.full((3, COL), -1, I32)

    def other_tables():
        zero_rows = jnp.zeros((8, COL), F32)
        for f in range(FLAT):
            for part in range(2):
                frame[part, f * STRIDE : f * STRIDE + 8, :] = zero_rows
                frame[part, f * STRIDE + 8 + LON : (f + 1) * STRIDE, :] = zero_rows
        for f in range(3 * SHELLS):
            emf[f * STRIDE : f * STRIDE + 8, :] = zero_rows
            emf[f * STRIDE + 8 + LON : (f + 1) * STRIDE, :] = zero_rows

        for half in range(2):
            turned[half, :, :] = jnp.zeros((COL, COL), F32)

        apart = iota((COL, COL), 0) - iota((COL, COL), 1)
        reach = jnp.abs(apart)
        first = jnp.where(reach == 1, 45.0, jnp.where(reach == 2, -9.0, jnp.where(reach == 3, 1.0, 0.0)))
        first = jnp.where(apart < 0, -first, first).astype(BF16)
        second = jnp.where(
            reach == 0, -490.0, jnp.where(reach == 1, 270.0, jnp.where(reach == 2, -27.0, jnp.where(reach == 3, 2.0, 0.0)))
        ).astype(BF16)
        for part in range(2):
            band[part * COL : (part + 1) * COL, 0:COL] = first
            band[part * COL : (part + 1) * COL, COL : 2 * COL] = second
        weight_high, weight_low = split(jnp.concatenate([rows_mix[...], jnp.zeros((COL - LON, SLOTS), F32)], axis=0))
        rows_split[0:COL, :] = weight_high
        rows_split[COL : 2 * COL, :] = weight_high
        rows_split[2 * COL : 3 * COL, :] = weight_low

    def load_split(part, pair):
        block = jnp.concatenate(
            [frame[part, pl.ds(pl.multiple_of((8 * pair + q) * STRIDE + 8, 8), LON), :] for q in range(8)], axis=0
        )
        return split(block)

    def interpolate(part, half):
        for pair in range(PART // 8):
            high, low = load_split(part, 2 * half + pair)
            value = dot(jnp.concatenate([high, low, high], axis=1), mix[...])
            value = jnp.sum(value.reshape(8, LON, SLOTS) * rows_mix[...][None], axis=1)
            blocks[part, half, 8 * pair : 8 * pair + 8, :] = value

    def send(part, half):
        for step in AROUND:
            a_copy(part, step, half).start()

        @pl.when(core != half)
        def _():
            s_copy(part, half).start()

        @pl.when(core == half)
        def _():
            table[part, member] = blocks[part, half]

    def lane_pass(part):
        def body(pair, carry):
            high, low = load_split(part, pair)
            both = jnp.concatenate([high, low], axis=1)
            lanes[pl.ds(pl.multiple_of(8 * LON * pair, 8), 8 * LON), :] = dot(both, band[...])
            return carry

        lax.fori_loop(0, FLAT // 8, body, 0)

    def cols_of(part):
        lane = iota((LON, COL), 1)
        for half in range(2):
            edge = jnp.zeros((LON, COL), F32)
            for g in range(FLAT // 2):
                at = (half * (FLAT // 2) + g) * STRIDE + 8
                moved = pltpu.roll(frame[part, at : at + LON, :], 8 * g + HALO, 1)
                edge = jnp.where(jnp.logical_and(lane >= 8 * g, lane < 8 * g + 2 * HALO), moved, edge)
            turned[half, :, 0:LON] = jnp.transpose(edge)
        for side in range(2):
            for j in range(HALO):
                first = (1 - side) * HALO + j
                for half in range(2):
                    col_own[part, side, j, half * (FLAT // 2) : (half + 1) * (FLAT // 2), :] = turned[
                        half, pl.ds(first, FLAT // 2, stride=8), :
                    ]
            col_out[part, side, 0] = jnp.where(
                iota((FLAT, COL), 1) < COL // 2, col_own[part, side, 0], pltpu.roll(col_own[part, side, 1], COL // 2, 1)
            )
            col_out[part, side, 1] = col_own[part, side, 2]

    def emf_pass(part):
        for r in range(SHELLS):
            def field(q):
                at = (q * SHELLS + r) * STRIDE + 8
                return frame[part, at : at + LON, :]

            m, b = [field(MR + i) for i in range(3)], [field(BR + i) for i in range(3)]
            for i, form in enumerate((cross_radial, cross_polar, cross_azimuthal)):
                at = (i * SHELLS + r) * STRIDE + 8
                emf[at : at + LON, :] = form(m, b)
        for i, at in ((0, FLAT), (2, FLAT + SHELLS)):
            block = jnp.concatenate(
                [emf[(i * SHELLS + r) * STRIDE + 8 : (i * SHELLS + r) * STRIDE + 8 + LON, :] for r in range(SHELLS)],
                axis=0,
            )
            high, low = split(block)
            lanes[at * LON : (at + SHELLS) * LON, 0:COL] = dot(
                jnp.concatenate([high, low], axis=1), band[:, 0:COL]
            )

    def main_pass(part, start, stop):
        def body(block, carry):
            here = pl.multiple_of(8 * block, 8)

            def near(f, apart):
                return frame[part, pl.ds(f * STRIDE + 8 + here + apart, 8), :]

            def near_emf(f, apart):
                return emf[pl.ds(f * STRIDE + 8 + here + apart, 8), :]

            def lane_first(f):
                return lanes[pl.ds(f * LON + here, 8), 0:COL]

            def lane_second(f):
                return lanes[pl.ds(f * LON + here, 8), COL : 2 * COL]

            def row_first(at):
                return 45.0 * (at[1] - at[-1]) - 9.0 * (at[2] - at[-2]) + (at[3] - at[-3])

            def row_second(at, centre):
                return (
                    270.0 * (at[1] + at[-1]) - 27.0 * (at[2] + at[-2]) + 2.0 * (at[3] + at[-3]) - 490.0 * centre
                )

            centre = [[near(q * SHELLS + r, 0) for r in range(SHELLS)] for q in range(QUANTITIES)]
            radial = [shell_first(x) for x in centre]
            radial_second = [None if q == S else shell_second(centre[q]) for q in range(QUANTITIES)]
            emf_centre = [[near_emf(i * SHELLS + r, 0) for r in range(SHELLS)] for i in range(3)]
            emf_radial = [None, shell_first(emf_centre[1]), shell_first(emf_centre[2])]
            for r in range(SHELLS):
                own = [centre[q][r] for q in range(QUANTITIES)]
                g, lap = [], []
                for q in range(QUANTITIES):
                    f = q * SHELLS + r
                    at = {d: near(f, d) for d in (-3, -2, -1, 1, 2, 3)}
                    g.append((radial[q][r], lane_first(f), scale * row_first(at)))
                    if q == S:
                        lap.append(None)
                    else:
                        lap.append(
                            radial_second[q][r] + lane_second(f) + (scale * scale) * row_second(at, own[q])
                        )
                m, b = own[MR:BR], own[BR:WARM]

                def advect(q):
                    return m[0] * g[q][0] + m[1] * g[q][1] + m[2] * g[q][2]

                div = g[MR][0] + g[MT][1] + g[MP][2]
                current = (g[BP][1] - g[BT][2], g[BR][2] - g[BP][0], g[BT][0] - g[BR][1])
                lorentz = (
                    current[1] * b[2] - current[2] * b[1],
                    current[2] * b[0] - current[0] * b[2],
                    current[0] * b[1] - current[1] * b[0],
                )
                grow, thin = jnp.exp(own[WARM]), jnp.exp(-own[S])
                emf_rows = {}
                for i in (0, 1):
                    f = i * SHELLS + r
                    emf_rows[i] = scale * row_first({d: near_emf(f, d) for d in (-3, -2, -1, 1, 2, 3)})
                turn = (
                    lane_first(FLAT + SHELLS + r) - emf_rows[1],
                    emf_rows[0] - emf_radial[2][r],
                    emf_radial[1][r] - lane_first(FLAT + r),
                )
                result = [-advect(S) - div]
                for i in range(3):
                    result.append(
                        -advect(MR + i) - grow * (g[S][i] + g[WARM][i]) + thin * lorentz[i] + SPREAD * lap[MR + i]
                    )
                for i in range(3):
                    result.append(turn[i] + SPREAD * lap[BR + i])
                result.append(-advect(WARM) - (2.0 / 3.0) * div + SPREAD * lap[WARM])
                for q in range(QUANTITIES):
                    f = q * SHELLS + r
                    value = own[q] + (TIME_STEP / 60.0) * result[q]
                    if part == 0:
                        frame[1, pl.ds(f * STRIDE + 8 + here, 8), :] = value
                    else:
                        start = frame[0, pl.ds(f * STRIDE + 8 + here, 8), :]
                        out_ref[pl.ds(f * LON + here, 8), :] = 0.5 * (start + value)
            return carry

        lax.fori_loop(start, stop, body, 0)

    def rows_of(part):
        for h in range(HALO):
            row_out[part, 0, h] = frame[part, pl.ds(8 + h, FLAT, stride=STRIDE), :]
            row_out[part, 1, h] = frame[part, pl.ds(8 + LON - HALO + h, FLAT, stride=STRIDE), :]

    def prepare_picks():
        for tile in range(2 * TILES):
            if tile < TARGETS:
                slot = idx_in[tile, 0:1, :]
            elif tile < TARGETS + 2:
                first = (tile - TARGETS) * GROUPS
                slot = idx_in[first, 1:2, :]
                for q in range(1, GROUPS):
                    slot = jnp.maximum(slot, pltpu.roll(idx_in[first + q], SPARE * q, 1)[1:2, :])
            else:
                side, h = divmod(tile - TARGETS - 2, HALO)
                slot = idx_in[side * (TARGETS - 1), 2 + h : 3 + h, :]
            slot = slot - mine * (GROUP * OUT)
            who = jnp.zeros_like(slot)
            for q in range(1, GROUP):
                who = who + jnp.where(slot >= q * OUT, 1, 0)
            cell = slot - who * OUT
            who = jnp.where(jnp.logical_and(slot >= 0, slot < GROUP * OUT), who, -1)
            at = (tile % 2) * COL
            owner[tile // 2, :, at : at + COL] = jnp.broadcast_to(who, (8, COL))
            hot = jnp.where(iota((SLOTS, COL), 0) == cell, 1.0, 0.0).astype(BF16)
            onehot[tile // 2, :, at : at + COL] = hot

    def table_split(part):
        high, low = split(table[part].reshape(GROUP * PART, SLOTS))
        return jnp.concatenate([high, low], axis=0)

    def product(both, tile):
        return dot(both, onehot[tile])

    def chosen(value, tile):
        value = value[0 : GROUP * PART] + value[GROUP * PART :]
        who = jnp.broadcast_to(owner[tile, 0:1, :], (PART, SLOTS))
        total = jnp.zeros((PART, SLOTS), F32)
        for q in range(GROUP):
            total = jnp.where(who == q, value[q * PART : (q + 1) * PART, :], total)
        return total[:, 0:COL], total[:, COL : 2 * COL]

    def fold(rests):
        turn = (lax.div(iota((8, COL), 1), SPARE) - iota((8, COL), 0)) & 7
        for half, rest in enumerate(rests):
            for s in range(FOLD):
                total = jnp.zeros((8, COL), F32)
                for d in range(8):
                    moved = rest[8 * s : 8 * s + 8, :]
                    if d:
                        moved = pltpu.roll(pltpu.roll(moved, SPARE * d, 1), 8 - d, 0)
                    total = jnp.where(turn == d, moved, total)
                rest_rows[half, s] = total

    def pick_all(part, both):
        sides = [(step + mine) & (TARGETS // 2 - 1) for step in range(TARGETS // 2)]
        extra = list(range(TARGETS // 2 + 1, TILES))
        ends, value = [], product(both, extra[0])
        for tile, after in zip(extra, extra[1:] + [None]):
            now = value
            if after is not None:
                value = product(both, after)
            ends += chosen(now, tile)
        for side in range(2):
            for h in range(HALO):
                picked_rows[part, side, h] = ends[side * HALO + h]
        for side in range(2):
            l_copy(part, side).start()

        @pl.when(col_edge)
        def _():
            now, value = product(both, TARGETS // 2), product(both, sides[0])
            fold(chosen(now, TARGETS // 2))
            for step, tile in enumerate(sides):
                now = value
                if step + 1 < len(sides):
                    value = product(both, sides[step + 1])
                for i, end in enumerate(chosen(now, tile)):
                    target = 2 * tile + i
                    picked[part, target, 0:PART, :] = end
                    for s in range(FOLD):
                        picked[part, target, PART + s : PART + s + 1, :] = rest_rows[
                            tile >> 2, s, pl.ds(target & (GROUPS - 1), 1), :
                        ]
                for i in range(2):
                    b_copy(part, 2 * tile + i).start()

    def corrections(part, side, along_lanes):
        halo_ref, own_ref, add_ref = (col_halo, col_own, col_add) if along_lanes else (row_halo, row_out, row_add)

        def scaled(value, power):
            for _ in range(0 if along_lanes else power):
                value = scale * value
            return value

        halo = [[halo_ref[side, h, q * SHELLS : (q + 1) * SHELLS, :] for q in range(QUANTITIES)] for h in range(HALO)]
        form = cross_azimuthal if along_lanes else cross_polar
        halo_emf = [(cross_radial(x[MR:BR], x[BR:WARM]), form(x[MR:BR], x[BR:WARM])) for x in halo]
        sign = -1.0 if side == 0 else 1.0
        firsts, seconds = (45.0 * sign, -9.0 * sign, sign), (270.0, -27.0, 2.0)
        for j in range(HALO):
            own = [own_ref[part, side, j, q * SHELLS : (q + 1) * SHELLS, :] for q in range(QUANTITIES)]

            def total(weights, of):
                result = None
                for m in (1, 2, 3):
                    h = j + 3 - m if side == 0 else m - 3 + j
                    if 0 <= h < HALO:
                        term = weights[m - 1] * of(h)
                        result = term if result is None else result + term
                return result

            d = [scaled(total(firsts, lambda h, q=q: halo[h][q]), 1) for q in range(QUANTITIES)]
            lap = [
                None if q == S else scaled(total(seconds, lambda h, q=q: halo[h][q]), 2) for q in range(QUANTITIES)
            ]
            radial = scaled(total(firsts, lambda h: halo_emf[h][0]), 1)
            second = scaled(total(firsts, lambda h: halo_emf[h][1]), 1)
            result = edge_rates(own, d, lap, second, radial, along_lanes)
            for q in range(QUANTITIES):
                add_ref[side, j, q * SHELLS : (q + 1) * SHELLS, :] = (TIME_STEP / 60.0 / (1 + part)) * result[q]

    def contribute(side, along_lanes):
        add_ref = col_add if along_lanes else row_add
        value = jnp.concatenate([add_ref[side, j] for j in range(HALO)], axis=0)
        if along_lanes:
            value = jnp.where(iota((HALO * FLAT, COL), 1) < LON, value, 0.0)
        high, low = split(value)
        value = dot(jnp.concatenate([high, low, high], axis=1), rows_split[...] if along_lanes else mix[...])
        total = jnp.zeros((FLAT, SLOTS), F32)
        for j in range(HALO):
            if along_lanes:
                at = j if side == 0 else COL - HALO + j
                weight = cols_mix[at : at + 1, :]
            else:
                at = j if side == 0 else LON - HALO + j
                weight = rows_mix[at : at + 1, :]
            total = total + weight * value[j * FLAT : (j + 1) * FLAT, :]
        for half in range(2):
            blocks[1, half] = blocks[1, half] + total[half * PART : (half + 1) * PART, :]

    def apply_edges():
        for side in range(2):
            for j in range(HALO):
                rows = pl.ds(8 + (j if side == 0 else LON - HALO + j), FLAT, stride=STRIDE)
                frame[1, rows, :] = frame[1, rows, :] + row_add[side, j]
        turn_edges(col_add, turned)
        for half in range(2):
            edge = jnp.transpose(turned[half])[0:LON, :]
            for g in range(FLAT // 2):
                at = (half * (FLAT // 2) + g) * STRIDE + 8
                frame[1, at : at + LON, :] = frame[1, at : at + LON, :] + field_edge(edge, g)

    def a_copy(part, step, half):
        return remote(
            blocks.at[part, half], table.at[part, member], a_send.at[part, half, step], a_recv.at[part, member],
            row_device(step, half),
        )

    def s_copy(part, half):
        return remote(
            blocks.at[part, half], table.at[part, member], s_send.at[part], a_recv.at[part, member], sibling
        )

    def a_arrival(part, step):
        there = (member + step) & (GROUP - 1)
        return remote(blocks.at[part, 0], table.at[part, there], s_send.at[part], a_recv.at[part, there], sibling)

    def b_copy(part, target):
        return remote(
            picked.at[part, target], got_cols.at[part, origin], b_send.at[part, target], b_recv.at[part, origin],
            target_device(target),
        )

    def b_arrival(part, source):
        return remote(
            picked.at[part, 0], got_cols.at[part, source], b_send.at[part, 0], b_recv.at[part, source],
            (other, lon, col),
        )

    def l_copy(part, side):
        return remote(
            picked_rows.at[part, side], got_rows.at[part, origin], l_send.at[part, side], l_recv.at[part, origin],
            target_device(side * (TARGETS - 1)),
        )

    def l_arrival(part, source):
        return remote(
            picked_rows.at[part, 0], got_rows.at[part, source], l_send.at[part, 0], l_recv.at[part, source],
            (other, lon, col),
        )

    def row_copy(part, side):
        return remote(
            row_out.at[part, 1 - side], row_in.at[part, side], r_send.at[part, side], r_recv.at[part, side],
            (panel, lon_up if side == 0 else lon_down, col),
        )

    def col_copy(part, side):
        return remote(
            col_out.at[part, 1 - side], col_in.at[part, side], c_send.at[part, side], c_recv.at[part, side],
            (panel, lon, col_up if side == 0 else col_down),
        )

    def idx_copy(target):
        return remote(
            idx_out, idx_in.at[origin], idx_send.at[target], idx_recv.at[origin], target_device(target)
        )

    def idx_arrival(source):
        return remote(idx_out, idx_in.at[source], idx_send.at[0], idx_recv.at[source], (other, lon, col))

    def inner_sides(part):
        for side in range(2):
            row_copy(part, side).wait_recv()

            @pl.when(lon != (0 if side == 0 else n_lon - 1))
            def _():
                row_halo[side] = row_in[part, side]
                corrections(part, side, False)
                if part == 0:
                    contribute(side, False)

            col_copy(part, side).wait_recv()

            @pl.when(col != (0 if side == 0 else n_col - 1))
            def _():
                pair = col_in[part, side, 0]
                col_halo[side, 0] = pair
                col_halo[side, 1] = pltpu.roll(pair, COL // 2, 1)
                col_halo[side, 2] = col_in[part, side, 1]
                corrections(part, side, True)
                if part == 0:
                    contribute(side, True)

    def outer_sides(part):
        for side in range(2):

            @pl.when(col == (0 if side == 0 else n_col - 1))
            def _():
                for source in range(TARGETS):
                    b_arrival(part, source).wait_recv()
                for half in range(2):
                    total = got_cols[part, half * GROUPS]
                    for group in range(1, GROUPS):
                        total = total + got_cols[part, half * GROUPS + group]
                    main = total[0:PART]
                    rows = slice(half * PART, (half + 1) * PART)
                    col_halo[side, 0, rows, :] = main
                    col_halo[side, 1, rows, :] = pltpu.roll(main, COL - LON, 1)
                    main = pltpu.roll(main, COL - 2 * LON, 1)
                    row, lane = iota((8, COL), 0), iota((8, COL), 1)
                    for s in range(FOLD):
                        value = main[8 * s : 8 * s + 8, :]
                        rest = jnp.broadcast_to(total[PART + s : PART + s + 1], (8, COL))
                        for q in range(8):
                            moved = pltpu.roll(rest, (2 * COL - 2 * LON - SPARE * q) % COL, 1)
                            value = jnp.where(jnp.logical_and(row == q, lane >= COL - 2 * LON), moved, value)
                        at = half * PART + 8 * s
                        col_halo[side, 2, at : at + 8, :] = value
                corrections(part, side, True)
                if part == 0:
                    contribute(side, True)

            @pl.when(lon == (0 if side == 0 else n_lon - 1))
            def _():
                for source in range(TARGETS):
                    l_arrival(part, source).wait_recv()
                for half in range(2):
                    total = got_rows[part, half * GROUPS]
                    for group in range(1, GROUPS):
                        total = total + got_rows[part, half * GROUPS + group]
                    row_halo[side, :, half * PART : (half + 1) * PART, :] = total
                corrections(part, side, False)
                if part == 0:
                    contribute(side, False)

    for part in range(2):
        if part == 0:
            interpolate(0, 0)
            pl.semaphore_wait(barrier, 2 * len(AROUND) + 2 + TARGETS)
            send(0, 0)
            interpolate(0, 1)
            send(0, 1)
            message_tables()
            for target in range(TARGETS):
                idx_copy(target).start()
            other_tables()
        else:
            send(1, 0)
            send(1, 1)
            apply_edges()
        rows_of(part)
        for side in range(2):
            row_copy(part, side).start()
        cols_of(part)
        for side in range(2):
            col_copy(part, side).start()
        if part == 0:
            for source in range(TARGETS):
                idx_arrival(source).wait_recv()
            prepare_picks()
        lane_pass(part)
        emf_pass(part)
        for step in range(1, GROUP):
            a_arrival(part, step).wait_recv()
        both = table_split(part)
        pick_all(part, both)
        main_pass(part, 0, 6)
        if part == 0:
            interpolate(1, 0)
            interpolate(1, 1)
        inner_sides(part)
        outer_sides(part)

    for target in range(TARGETS):
        idx_copy(target).wait_send()
    for part in range(2):
        for half in range(2):
            for step in AROUND:
                a_copy(part, step, half).wait_send()
        s_copy(part, 0).wait_send()
        for side in range(2):
            row_copy(part, side).wait_send()
            col_copy(part, side).wait_send()
            l_copy(part, side).wait_send()

        @pl.when(col_edge)
        def _():
            for target in range(TARGETS):
                b_copy(part, target).wait_send()


def shards(state, send_base, send_frac, recv_slots):
    rows = FLAT * LON
    dma = pltpu.SemaphoreType.DMA
    vmem = pltpu.VMEM
    scratch = [
        vmem((2, FLAT, STRIDE, COL), F32),
        vmem((1, OUT), I32),
        vmem((2, OUT), F32),
        vmem((1, recv_slots.shape[-1]), I32),
        vmem((3 * SHELLS * STRIDE, COL), F32),
        vmem(((FLAT + 2 * SHELLS) * LON, 2 * COL), F32),
        vmem((3 * COL, SLOTS), BF16),
        vmem((COL, SLOTS), F32),
        vmem((LON, SLOTS), F32),
        vmem((3 * COL, SLOTS), BF16),
        vmem((2 * COL, 2 * COL), BF16),
        vmem((TILES, SLOTS, 2 * COL), BF16),
        vmem((TILES, 8, 2 * COL), I32),
        vmem((2, COL, COL), F32),
        vmem((2, 2, PART, SLOTS), F32),
        vmem((2, GROUP, PART, SLOTS), F32),
        vmem((8, COL), I32),
        vmem((TARGETS, 8, COL), I32),
        vmem((2, FOLD, 8, COL), F32),
        vmem((2, TARGETS, PART + FOLD, COL), F32),
        vmem((2, 2, HALO, PART, COL), F32),
        vmem((2, TARGETS, PART + FOLD, COL), F32),
        vmem((2, TARGETS, HALO, PART, COL), F32),
        vmem((2, 2, HALO, FLAT, COL), F32),
        vmem((2, 2, HALO, FLAT, COL), F32),
        vmem((2, 2, HALO, FLAT, COL), F32),
        vmem((2, 2, 2, FLAT, COL), F32),
        vmem((2, 2, 2, FLAT, COL), F32),
        vmem((2, HALO, FLAT, COL), F32),
        vmem((2, HALO, FLAT, COL), F32),
        dma((4,)),
        dma((TARGETS,)),
        dma((TARGETS,)),
        dma((2, 2, RING)),
        dma((2, GROUP)),
        dma((2,)),
        dma((2, TARGETS)),
        dma((2, TARGETS)),
        dma((2, 2)),
        dma((2, TARGETS)),
        dma((2, 2)),
        dma((2, 2)),
        dma((2, 2)),
        dma((2, 2)),
    ]
    edges = jax.ShapeDtypeStruct((2, HALO, FLAT, COL), F32)
    value, row_add, col_add = pl.pallas_call(
        kernel,
        out_shape=(jax.ShapeDtypeStruct((rows, COL), F32), edges, edges),
        in_specs=[pl.BlockSpec(memory_space=pltpu.HBM)] * 4,
        out_specs=[pl.BlockSpec(memory_space=pltpu.VMEM)] * 3,
        scratch_shapes=scratch,
        compiler_params=pltpu.CompilerParams(
            collective_id=0, has_side_effects=True, vmem_limit_bytes=40 * 1024 * 1024
        ),
    )(*(
        pltpu.with_memory_space_constraint(x, pltpu.HBM)
        for x in (state.reshape(FLAT, LON, COL), send_base[0], send_frac[0, 0], recv_slots[0])
    ))
    result = pl.pallas_call(
        closing,
        out_shape=jax.ShapeDtypeStruct((rows, COL), F32),
        in_specs=[pl.BlockSpec(memory_space=pltpu.VMEM)] * 3,
        out_specs=pl.BlockSpec(memory_space=pltpu.HBM),
        scratch_shapes=[vmem((2, COL, COL), F32), vmem((rows, COL), F32), dma((4,))],
        compiler_params=pltpu.CompilerParams(vmem_limit_bytes=16 * 1024 * 1024),
    )(value, row_add, col_add)
    return result.reshape(state.shape)


def solution(mesh):
    placed = (
        P("panel", None, None, "lon", "colat"),
        P("panel", ("lon", "colat"), None),
        P("panel", ("lon", "colat"), None, None),
        P("panel", ("lon", "colat"), None),
    )
    return jax.shard_map(
        shards,
        mesh=mesh,
        in_specs=placed,
        out_specs=P("panel", None, None, "lon", "colat"),
        check_vma=False,
    )
```

```python
import math

import jax
import jax.numpy as jnp
from jax import lax
from jax.experimental import pallas as pl
from jax.experimental.pallas import tpu as pltpu
from jax.sharding import PartitionSpec as P

MESH = pl.DeviceIdType.MESH
F32, BF16, I32 = jnp.float32, jnp.bfloat16, jnp.int32

QUANTITIES = 8
SHELLS = 4
FLAT = QUANTITIES * SHELLS
LON = 48
COL = 128
HALO = 3
OUT = 240
SIDE = HALO * LON
SLOTS = 256
GROUP = 8
GROUPS = 8
AROUND = (1, 3, 2)
SPARE = SIDE - COL
PART = FLAT // 2
TARGETS = 2 * GROUPS
TILES = 12
RING = 4
FOLD = PART // 8
STRIDE = LON + 16
TIME_STEP = 0.25
SPREAD = 0.1 / 3.0
S, MR, MT, MP, BR, BT, BP, WARM = range(QUANTITIES)


def dot(left, right):
    return jnp.dot(left, right, preferred_element_type=F32)


def split(value):
    high = value.astype(BF16)
    return high, (value - high.astype(F32)).astype(BF16)


def iota(shape, dim):
    return lax.broadcasted_iota(I32, shape, dim)


def cross_radial(m, b):
    return m[1] * b[2] - m[2] * b[1]


def cross_polar(m, b):
    return m[2] * b[0] - m[0] * b[2]


def cross_azimuthal(m, b):
    return m[0] * b[1] - m[1] * b[0]


def edge_rates(own, d, lap, emf_first, emf_second, along_lanes):
    grow, thin = jnp.exp(own[WARM]), jnp.exp(-own[S])
    b = own[BR:WARM]
    if along_lanes:
        vel, out = own[MT], MT
        lorentz = (d[BR] * b[1], -d[BR] * b[0] - d[BP] * b[2], d[BP] * b[1])
        turn = (emf_first, None, -emf_second)
    else:
        vel, out = own[MP], MP
        lorentz = (d[BR] * b[2], d[BT] * b[2], -d[BT] * b[1] - d[BR] * b[0])
        turn = (-emf_first, emf_second, None)
    result = [-vel * d[S] - d[out]]
    for i in range(3):
        rate = -vel * d[MR + i] + thin * lorentz[i] + SPREAD * lap[MR + i]
        if MR + i == out:
            rate = rate - grow * (d[S] + d[WARM])
        result.append(rate)
    for i in range(3):
        rate = SPREAD * lap[BR + i]
        result.append(rate if turn[i] is None else rate + turn[i])
    result.append(-vel * d[WARM] - (2.0 / 3.0) * d[out] + SPREAD * lap[WARM])
    return result


def shell_first(x):
    a, b = 8.0 * (x[3] - x[0]), 45.0
    return (
        b * (x[1] - x[0]) - 9.0 * (x[2] - x[0]) + (x[3] - x[0]),
        b * (x[2] - x[0]) - a,
        b * (x[3] - x[1]) - a,
        b * (x[3] - x[2]) - 9.0 * (x[3] - x[1]) + (x[3] - x[0]),
    )


def shell_second(x):
    return (
        2.0 * x[3] - 27.0 * x[2] + 270.0 * x[1] - 245.0 * x[0],
        245.0 * x[0] - 490.0 * x[1] + 270.0 * x[2] - 25.0 * x[3],
        245.0 * x[3] - 490.0 * x[2] + 270.0 * x[1] - 25.0 * x[0],
        2.0 * x[0] - 27.0 * x[1] + 270.0 * x[2] - 245.0 * x[3],
    )


def turn_edges(col_add, turned):
    for side in range(2):
        for j in range(HALO):
            for half in range(2):
                turned[half, pl.ds((1 - side) * HALO + j, FLAT // 2, stride=8), :] = col_add[
                    side, j, half * (FLAT // 2) : (half + 1) * (FLAT // 2), :
                ]


def field_edge(edge, g):
    lane = iota((LON, COL), 1)
    border = jnp.logical_or(lane < HALO, lane >= COL - HALO)
    return jnp.where(border, pltpu.roll(edge, COL - 8 * g - HALO, 1), 0.0)


def closing(value_ref, row_add, col_add, out_hbm, turned, ready, sem):
    turn_edges(col_add, turned)
    copies = []
    for half in range(2):
        edge = jnp.transpose(turned[half])[0:LON, :]
        for chunk in range(2):
            first = half * (FLAT // 2) + 8 * chunk
            for q in range(8):
                at = (first + q) * LON
                ready[at : at + LON, :] = value_ref[at : at + LON, :] + field_edge(edge, 8 * chunk + q)
            for side in range(2):
                for j in range(HALO):
                    rows = pl.ds(first * LON + (j if side == 0 else LON - HALO + j), 8, stride=LON)
                    ready[rows, :] = ready[rows, :] + row_add[side, j, first : first + 8, :]
            rows = pl.ds(first * LON, 8 * LON)
            copy = pltpu.make_async_copy(ready.at[rows, :], out_hbm.at[rows, :], sem.at[2 * half + chunk])
            copy.start()
            copies.append(copy)
    for copy in copies:
        copy.wait()


def kernel(
    x_hbm, base_hbm, frac_hbm, slots_hbm, out_ref, row_add, col_add,
    deep, base_ref, frac_ref, slots_ref, emf, lanes, mix, cols_mix, rows_mix, rows_split, band, onehot, owner, turned,
    blocks, table, idx_out, idx_in, rest_rows, picked, picked_rows, got_cols, got_rows, row_out, row_in, col_own, col_out, col_in,
    row_halo, col_halo,
    in_sem, idx_send, idx_recv, a_send, a_recv, s_send, b_send, b_recv, l_send, l_recv, r_send, r_recv, c_send, c_recv,
):
    panel, lon, col = lax.axis_index("panel"), lax.axis_index("lon"), lax.axis_index("colat")
    n_lon, n_col = lax.axis_size("lon"), lax.axis_size("colat")
    core, mine = lon & 1, lon >> 1
    member = core * n_col + col
    other = 1 - panel
    lon_up, lon_down = lax.rem(lon + 1, n_lon), lax.rem(lon + n_lon - 1, n_lon)
    col_up, col_down = lax.rem(col + 1, n_col), lax.rem(col + n_col - 1, n_col)
    outer = lax.rem(lon + 2 * core - 1 + n_lon, n_lon)
    sends_rows = (lon < n_lon - 1, lon > 0)
    sends_cols = (col < n_col - 1, col > 0)
    col_edge = jnp.logical_or(col == 0, col == n_col - 1)

    sibling = (panel, lon + 1 - 2 * core, col)
    origin = core * GROUPS + mine

    def row_device(step, half):
        return (panel, 2 * mine + half, (col + step) & (n_col - 1))

    def target_device(target):
        return (other, 2 * (target & (GROUPS - 1)) + (target >> 3), col)

    def remote(src, dst, send, recv, device):
        return pltpu.make_async_remote_copy(
            src_ref=src, dst_ref=dst, send_sem=send, recv_sem=recv, device_id=device, device_id_type=MESH
        )

    frame = deep.reshape(2, FLAT * STRIDE, COL)
    copies = [
        pltpu.make_async_copy(src, dst, in_sem.at[i])
        for i, (src, dst) in enumerate(
            (
                (frac_hbm, frac_ref),
                (base_hbm, base_ref),
                (slots_hbm, slots_ref),
                (x_hbm, deep.at[0, :, pl.ds(8, LON), :]),
            )
        )
    ]
    for copy in copies:
        copy.start()

    barrier = pltpu.get_barrier_semaphore()
    for step in AROUND:
        for half in range(2):
            pl.semaphore_signal(barrier, inc=1, device_id=row_device(step, half), device_id_type=MESH)
    pl.semaphore_signal(barrier, inc=1, device_id=sibling, device_id_type=MESH)
    for target in range(TARGETS):
        pl.semaphore_signal(barrier, inc=1, device_id=target_device(target), device_id_type=MESH)
    pl.semaphore_signal(barrier, inc=1, device_id=(panel, outer, col), device_id_type=MESH)

    copies[0].wait()
    copies[1].wait()
    base = jnp.concatenate([base_ref[...], jnp.zeros((1, SLOTS - OUT), I32)], axis=1)
    base_row, base_col = lax.div(base, COL), lax.rem(base, COL)
    share = jnp.concatenate([frac_ref[...], jnp.zeros((2, SLOTS - OUT), F32)], axis=1)
    along, across = share[0:1, :], share[1:2, :]
    cells = iota((COL, SLOTS), 0)
    weight = jnp.where(cells == base_col, 1.0 - across, 0.0) + jnp.where(cells == base_col + 1, across, 0.0)
    weight_high, weight_low = split(weight)
    cols_mix[...] = weight
    mix[0:COL, :] = weight_high
    mix[COL : 2 * COL, :] = weight_high
    mix[2 * COL : 3 * COL, :] = weight_low
    cells = iota((LON, SLOTS), 0)
    weight = jnp.where(cells == base_row, 1.0 - along, 0.0) + jnp.where(cells == base_row + 1, along, 0.0)
    rows_mix[...] = weight
    place = (col * COL + iota((1, COL), 1)).astype(F32)
    scale = 1.0 / jnp.sin(math.pi / 4.0 + (place + 0.5) * (math.pi / 2.0 / (COL * n_col)))
    copies[3].wait()

    def message_tables():
        copies[2].wait()
        spot = iota((1, SLOTS), 1)
        sides = jnp.where(spot < SIDE, jnp.maximum(slots_ref[:, 0:SLOTS], slots_ref[:, SIDE : SIDE + SLOTS]) + 1, 0)
        digits = jnp.concatenate([lax.div(sides, COL), lax.rem(sides, COL), jnp.zeros((6, SLOTS), I32)], axis=0)
        source, target = iota((SLOTS, SLOTS), 0), iota((SLOTS, SLOTS), 1)
        layer = jnp.where(target >= LON, 1, 0) + jnp.where(target >= 2 * LON, 1, 0)
        order = jnp.logical_and(target < SIDE, source == HALO * (target - LON * layer) + layer)
        digits = dot(digits.astype(F32).astype(BF16), jnp.where(order, 1.0, 0.0).astype(BF16)).astype(I32)
        sides = digits[0:1, :] * COL + digits[1:2, :] - 1
        idx_out[0:1, :] = sides[:, 0:COL]
        idx_out[1:2, :] = sides[:, COL : 2 * COL]
        for h in range(HALO):
            at = 2 * SIDE + h * COL
            idx_out[2 + h : 3 + h, :] = jnp.maximum(
                slots_ref[:, at : at + COL], slots_ref[:, at + HALO * COL : at + HALO * COL + COL]
            )
        idx_out[5:8, :] = jnp.full((3, COL), -1, I32)

    def other_tables():
        zero_rows = jnp.zeros((8, COL), F32)
        for f in range(FLAT):
            for part in range(2):
                frame[part, f * STRIDE : f * STRIDE + 8, :] = zero_rows
                frame[part, f * STRIDE + 8 + LON : (f + 1) * STRIDE, :] = zero_rows
        for f in range(3 * SHELLS):
            emf[f * STRIDE : f * STRIDE + 8, :] = zero_rows
            emf[f * STRIDE + 8 + LON : (f + 1) * STRIDE, :] = zero_rows

        for half in range(2):
            turned[half, :, :] = jnp.zeros((COL, COL), F32)

        apart = iota((COL, COL), 0) - iota((COL, COL), 1)
        reach = jnp.abs(apart)
        first = jnp.where(reach == 1, 45.0, jnp.where(reach == 2, -9.0, jnp.where(reach == 3, 1.0, 0.0)))
        first = jnp.where(apart < 0, -first, first).astype(BF16)
        second = jnp.where(
            reach == 0, -490.0, jnp.where(reach == 1, 270.0, jnp.where(reach == 2, -27.0, jnp.where(reach == 3, 2.0, 0.0)))
        ).astype(BF16)
        for part in range(2):
            band[part * COL : (part + 1) * COL, 0:COL] = first
            band[part * COL : (part + 1) * COL, COL : 2 * COL] = second
        weight_high, weight_low = split(jnp.concatenate([rows_mix[...], jnp.zeros((COL - LON, SLOTS), F32)], axis=0))
        rows_split[0:COL, :] = weight_high
        rows_split[COL : 2 * COL, :] = weight_high
        rows_split[2 * COL : 3 * COL, :] = weight_low

    def load_split(part, pair):
        block = jnp.concatenate(
            [frame[part, pl.ds(pl.multiple_of((8 * pair + q) * STRIDE + 8, 8), LON), :] for q in range(8)], axis=0
        )
        return split(block)

    def interpolate(part, half):
        for pair in range(PART // 8):
            high, low = load_split(part, 2 * half + pair)
            value = dot(jnp.concatenate([high, low, high], axis=1), mix[...])
            value = jnp.sum(value.reshape(8, LON, SLOTS) * rows_mix[...][None], axis=1)
            blocks[part, half, 8 * pair : 8 * pair + 8, :] = value

    def send(part, half):
        for step in AROUND:
            a_copy(part, step, half).start()

        @pl.when(core != half)
        def _():
            s_copy(part, half).start()

        @pl.when(core == half)
        def _():
            table[part, member] = blocks[part, half]

    def lane_pass(part):
        def body(pair, carry):
            high, low = load_split(part, pair)
            both = jnp.concatenate([high, low], axis=1)
            lanes[pl.ds(pl.multiple_of(8 * LON * pair, 8), 8 * LON), :] = dot(both, band[...])
            return carry

        lax.fori_loop(0, FLAT // 8, body, 0)

    def cols_of(part):
        lane = iota((LON, COL), 1)
        for half in range(2):
            edge = jnp.zeros((LON, COL), F32)
            for g in range(FLAT // 2):
                at = (half * (FLAT // 2) + g) * STRIDE + 8
                moved = pltpu.roll(frame[part, at : at + LON, :], 8 * g + HALO, 1)
                edge = jnp.where(jnp.logical_and(lane >= 8 * g, lane < 8 * g + 2 * HALO), moved, edge)
            turned[half, :, 0:LON] = jnp.transpose(edge)
        for side in range(2):
            for j in range(HALO):
                first = (1 - side) * HALO + j
                for half in range(2):
                    col_own[part, side, j, half * (FLAT // 2) : (half + 1) * (FLAT // 2), :] = turned[
                        half, pl.ds(first, FLAT // 2, stride=8), :
                    ]
            col_out[part, side, 0] = jnp.where(
                iota((FLAT, COL), 1) < COL // 2, col_own[part, side, 0], pltpu.roll(col_own[part, side, 1], COL // 2, 1)
            )
            col_out[part, side, 1] = col_own[part, side, 2]

    def emf_pass(part):
        for r in range(SHELLS):
            def field(q):
                at = (q * SHELLS + r) * STRIDE + 8
                return frame[part, at : at + LON, :]

            m, b = [field(MR + i) for i in range(3)], [field(BR + i) for i in range(3)]
            for i, form in enumerate((cross_radial, cross_polar, cross_azimuthal)):
                at = (i * SHELLS + r) * STRIDE + 8
                emf[at : at + LON, :] = form(m, b)
        for i, at in ((0, FLAT), (2, FLAT + SHELLS)):
            block = jnp.concatenate(
                [emf[(i * SHELLS + r) * STRIDE + 8 : (i * SHELLS + r) * STRIDE + 8 + LON, :] for r in range(SHELLS)],
                axis=0,
            )
            high, low = split(block)
            lanes[at * LON : (at + SHELLS) * LON, 0:COL] = dot(
                jnp.concatenate([high, low], axis=1), band[:, 0:COL]
            )

    def main_pass(part, start, stop):
        def body(block, carry):
            here = pl.multiple_of(8 * block, 8)

            def near(f, apart):
                return frame[part, pl.ds(f * STRIDE + 8 + here + apart, 8), :]

            def near_emf(f, apart):
                return emf[pl.ds(f * STRIDE + 8 + here + apart, 8), :]

            def lane_first(f):
                return lanes[pl.ds(f * LON + here, 8), 0:COL]

            def lane_second(f):
                return lanes[pl.ds(f * LON + here, 8), COL : 2 * COL]

            def row_first(at):
                return 45.0 * (at[1] - at[-1]) - 9.0 * (at[2] - at[-2]) + (at[3] - at[-3])

            def row_second(at, centre):
                return (
                    270.0 * (at[1] + at[-1]) - 27.0 * (at[2] + at[-2]) + 2.0 * (at[3] + at[-3]) - 490.0 * centre
                )

            centre = [[near(q * SHELLS + r, 0) for r in range(SHELLS)] for q in range(QUANTITIES)]
            radial = [shell_first(x) for x in centre]
            radial_second = [None if q == S else shell_second(centre[q]) for q in range(QUANTITIES)]
            emf_centre = [[near_emf(i * SHELLS + r, 0) for r in range(SHELLS)] for i in range(3)]
            emf_radial = [None, shell_first(emf_centre[1]), shell_first(emf_centre[2])]
            for r in range(SHELLS):
                own = [centre[q][r] for q in range(QUANTITIES)]
                g, lap = [], []
                for q in range(QUANTITIES):
                    f = q * SHELLS + r
                    at = {d: near(f, d) for d in (-3, -2, -1, 1, 2, 3)}
                    g.append((radial[q][r], lane_first(f), scale * row_first(at)))
                    if q == S:
                        lap.append(None)
                    else:
                        lap.append(
                            radial_second[q][r] + lane_second(f) + (scale * scale) * row_second(at, own[q])
                        )
                m, b = own[MR:BR], own[BR:WARM]

                def advect(q):
                    return m[0] * g[q][0] + m[1] * g[q][1] + m[2] * g[q][2]

                div = g[MR][0] + g[MT][1] + g[MP][2]
                current = (g[BP][1] - g[BT][2], g[BR][2] - g[BP][0], g[BT][0] - g[BR][1])
                lorentz = (
                    current[1] * b[2] - current[2] * b[1],
                    current[2] * b[0] - current[0] * b[2],
                    current[0] * b[1] - current[1] * b[0],
                )
                grow, thin = jnp.exp(own[WARM]), jnp.exp(-own[S])
                emf_rows = {}
                for i in (0, 1):
                    f = i * SHELLS + r
                    emf_rows[i] = scale * row_first({d: near_emf(f, d) for d in (-3, -2, -1, 1, 2, 3)})
                turn = (
                    lane_first(FLAT + SHELLS + r) - emf_rows[1],
                    emf_rows[0] - emf_radial[2][r],
                    emf_radial[1][r] - lane_first(FLAT + r),
                )
                result = [-advect(S) - div]
                for i in range(3):
                    result.append(
                        -advect(MR + i) - grow * (g[S][i] + g[WARM][i]) + thin * lorentz[i] + SPREAD * lap[MR + i]
                    )
                for i in range(3):
                    result.append(turn[i] + SPREAD * lap[BR + i])
                result.append(-advect(WARM) - (2.0 / 3.0) * div + SPREAD * lap[WARM])
                for q in range(QUANTITIES):
                    f = q * SHELLS + r
                    value = own[q] + (TIME_STEP / 60.0) * result[q]
                    if part == 0:
                        frame[1, pl.ds(f * STRIDE + 8 + here, 8), :] = value
                    else:
                        start = frame[0, pl.ds(f * STRIDE + 8 + here, 8), :]
                        out_ref[pl.ds(f * LON + here, 8), :] = 0.5 * (start + value)
            return carry

        lax.fori_loop(start, stop, body, 0)

    def rows_of(part):
        for h in range(HALO):
            row_out[part, 0, h] = frame[part, pl.ds(8 + h, FLAT, stride=STRIDE), :]
            row_out[part, 1, h] = frame[part, pl.ds(8 + LON - HALO + h, FLAT, stride=STRIDE), :]

    def prepare_picks():
        for tile in range(2 * TILES):
            if tile < TARGETS:
                slot = idx_in[tile, 0:1, :]
            elif tile < TARGETS + 2:
                first = (tile - TARGETS) * GROUPS
                slot = idx_in[first, 1:2, :]
                for q in range(1, GROUPS):
                    slot = jnp.maximum(slot, pltpu.roll(idx_in[first + q], SPARE * q, 1)[1:2, :])
            else:
                side, h = divmod(tile - TARGETS - 2, HALO)
                slot = idx_in[side * (TARGETS - 1), 2 + h : 3 + h, :]
            slot = slot - mine * (GROUP * OUT)
            who = jnp.zeros_like(slot)
            for q in range(1, GROUP):
                who = who + jnp.where(slot >= q * OUT, 1, 0)
            cell = slot - who * OUT
            who = jnp.where(jnp.logical_and(slot >= 0, slot < GROUP * OUT), who, -1)
            at = (tile % 2) * COL
            owner[tile // 2, :, at : at + COL] = jnp.broadcast_to(who, (8, COL))
            hot = jnp.where(iota((SLOTS, COL), 0) == cell, 1.0, 0.0).astype(BF16)
            onehot[tile // 2, :, at : at + COL] = hot

    def table_split(part):
        high, low = split(table[part].reshape(GROUP * PART, SLOTS))
        return jnp.concatenate([high, low], axis=0)

    def product(both, tile):
        return dot(both, onehot[tile])

    def chosen(value, tile):
        value = value[0 : GROUP * PART] + value[GROUP * PART :]
        who = jnp.broadcast_to(owner[tile, 0:1, :], (PART, SLOTS))
        total = jnp.zeros((PART, SLOTS), F32)
        for q in range(GROUP):
            total = jnp.where(who == q, value[q * PART : (q + 1) * PART, :], total)
        return total[:, 0:COL], total[:, COL : 2 * COL]

    def fold(rests):
        turn = (lax.div(iota((8, COL), 1), SPARE) - iota((8, COL), 0)) & 7
        for half, rest in enumerate(rests):
            for s in range(FOLD):
                total = jnp.zeros((8, COL), F32)
                for d in range(8):
                    moved = rest[8 * s : 8 * s + 8, :]
                    if d:
                        moved = pltpu.roll(pltpu.roll(moved, SPARE * d, 1), 8 - d, 0)
                    total = jnp.where(turn == d, moved, total)
                rest_rows[half, s] = total

    def pick_all(part, both):
        sides = [(step + mine) & (TARGETS // 2 - 1) for step in range(TARGETS // 2)]
        extra = list(range(TARGETS // 2 + 1, TILES))
        ends, value = [], product(both, extra[0])
        for tile, after in zip(extra, extra[1:] + [None]):
            now = value
            if after is not None:
                value = product(both, after)
            ends += chosen(now, tile)
        for side in range(2):
            for h in range(HALO):
                picked_rows[part, side, h] = ends[side * HALO + h]
        for side in range(2):
            l_copy(part, side).start()

        @pl.when(col_edge)
        def _():
            now, value = product(both, TARGETS // 2), product(both, sides[0])
            fold(chosen(now, TARGETS // 2))
            for step, tile in enumerate(sides):
                now = value
                if step + 1 < len(sides):
                    value = product(both, sides[step + 1])
                for i, end in enumerate(chosen(now, tile)):
                    target = 2 * tile + i
                    picked[part, target, 0:PART, :] = end
                    for s in range(FOLD):
                        picked[part, target, PART + s : PART + s + 1, :] = rest_rows[
                            tile >> 2, s, pl.ds(target & (GROUPS - 1), 1), :
                        ]
                for i in range(2):
                    b_copy(part, 2 * tile + i).start()

    def corrections(part, side, along_lanes):
        halo_ref, own_ref, add_ref = (col_halo, col_own, col_add) if along_lanes else (row_halo, row_out, row_add)

        def scaled(value, power):
            for _ in range(0 if along_lanes else power):
                value = scale * value
            return value

        halo = [[halo_ref[side, h, q * SHELLS : (q + 1) * SHELLS, :] for q in range(QUANTITIES)] for h in range(HALO)]
        form = cross_azimuthal if along_lanes else cross_polar
        halo_emf = [(cross_radial(x[MR:BR], x[BR:WARM]), form(x[MR:BR], x[BR:WARM])) for x in halo]
        sign = -1.0 if side == 0 else 1.0
        firsts, seconds = (45.0 * sign, -9.0 * sign, sign), (270.0, -27.0, 2.0)
        for j in range(HALO):
            own = [own_ref[part, side, j, q * SHELLS : (q + 1) * SHELLS, :] for q in range(QUANTITIES)]

            def total(weights, of):
                result = None
                for m in (1, 2, 3):
                    h = j + 3 - m if side == 0 else m - 3 + j
                    if 0 <= h < HALO:
                        term = weights[m - 1] * of(h)
                        result = term if result is None else result + term
                return result

            d = [scaled(total(firsts, lambda h, q=q: halo[h][q]), 1) for q in range(QUANTITIES)]
            lap = [
                None if q == S else scaled(total(seconds, lambda h, q=q: halo[h][q]), 2) for q in range(QUANTITIES)
            ]
            radial = scaled(total(firsts, lambda h: halo_emf[h][0]), 1)
            second = scaled(total(firsts, lambda h: halo_emf[h][1]), 1)
            result = edge_rates(own, d, lap, second, radial, along_lanes)
            for q in range(QUANTITIES):
                add_ref[side, j, q * SHELLS : (q + 1) * SHELLS, :] = (TIME_STEP / 60.0 / (1 + part)) * result[q]

    def contribute(side, along_lanes):
        add_ref = col_add if along_lanes else row_add
        value = jnp.concatenate([add_ref[side, j] for j in range(HALO)], axis=0)
        if along_lanes:
            value = jnp.where(iota((HALO * FLAT, COL), 1) < LON, value, 0.0)
        high, low = split(value)
        value = dot(jnp.concatenate([high, low, high], axis=1), rows_split[...] if along_lanes else mix[...])
        total = jnp.zeros((FLAT, SLOTS), F32)
        for j in range(HALO):
            if along_lanes:
                at = j if side == 0 else COL - HALO + j
                weight = cols_mix[at : at + 1, :]
            else:
                at = j if side == 0 else LON - HALO + j
                weight = rows_mix[at : at + 1, :]
            total = total + weight * value[j * FLAT : (j + 1) * FLAT, :]
        for half in range(2):
            blocks[1, half] = blocks[1, half] + total[half * PART : (half + 1) * PART, :]

    def apply_edges():
        for side in range(2):
            for j in range(HALO):
                rows = pl.ds(8 + (j if side == 0 else LON - HALO + j), FLAT, stride=STRIDE)
                frame[1, rows, :] = frame[1, rows, :] + row_add[side, j]
        turn_edges(col_add, turned)
        for half in range(2):
            edge = jnp.transpose(turned[half])[0:LON, :]
            for g in range(FLAT // 2):
                at = (half * (FLAT // 2) + g) * STRIDE + 8
                frame[1, at : at + LON, :] = frame[1, at : at + LON, :] + field_edge(edge, g)

    def a_copy(part, step, half):
        return remote(
            blocks.at[part, half], table.at[part, member], a_send.at[part, half, step], a_recv.at[part, member],
            row_device(step, half),
        )

    def s_copy(part, half):
        return remote(
            blocks.at[part, half], table.at[part, member], s_send.at[part], a_recv.at[part, member], sibling
        )

    def a_arrival(part, step):
        there = (member + step) & (GROUP - 1)
        return remote(blocks.at[part, 0], table.at[part, there], s_send.at[part], a_recv.at[part, there], sibling)

    def b_copy(part, target):
        return remote(
            picked.at[part, target], got_cols.at[part, origin], b_send.at[part, target], b_recv.at[part, origin],
            target_device(target),
        )

    def b_arrival(part, source):
        return remote(
            picked.at[part, 0], got_cols.at[part, source], b_send.at[part, 0], b_recv.at[part, source],
            (other, lon, col),
        )

    def l_copy(part, side):
        return remote(
            picked_rows.at[part, side], got_rows.at[part, origin], l_send.at[part, side], l_recv.at[part, origin],
            target_device(side * (TARGETS - 1)),
        )

    def l_arrival(part, source):
        return remote(
            picked_rows.at[part, 0], got_rows.at[part, source], l_send.at[part, 0], l_recv.at[part, source],
            (other, lon, col),
        )

    def row_copy(part, side):
        return remote(
            row_out.at[part, 1 - side], row_in.at[part, side], r_send.at[part, side], r_recv.at[part, side],
            (panel, lon_up if side == 0 else lon_down, col),
        )

    def col_copy(part, side):
        return remote(
            col_out.at[part, 1 - side], col_in.at[part, side], c_send.at[part, side], c_recv.at[part, side],
            (panel, lon, col_up if side == 0 else col_down),
        )

    def idx_copy(target):
        return remote(
            idx_out, idx_in.at[origin], idx_send.at[target], idx_recv.at[origin], target_device(target)
        )

    def idx_arrival(source):
        return remote(idx_out, idx_in.at[source], idx_send.at[0], idx_recv.at[source], (other, lon, col))

    def inner_sides(part):
        for side in range(2):
            @pl.when(lon != (0 if side == 0 else n_lon - 1))
            def _():
                row_copy(part, side).wait_recv()
                row_halo[side] = row_in[part, side]
                corrections(part, side, False)
                if part == 0:
                    contribute(side, False)

            @pl.when(col != (0 if side == 0 else n_col - 1))
            def _():
                col_copy(part, side).wait_recv()
                pair = col_in[part, side, 0]
                col_halo[side, 0] = pair
                col_halo[side, 1] = pltpu.roll(pair, COL // 2, 1)
                col_halo[side, 2] = col_in[part, side, 1]
                corrections(part, side, True)
                if part == 0:
                    contribute(side, True)

    def outer_sides(part):
        for side in range(2):

            @pl.when(col == (0 if side == 0 else n_col - 1))
            def _():
                for source in range(TARGETS):
                    b_arrival(part, source).wait_recv()
                for half in range(2):
                    total = got_cols[part, half * GROUPS]
                    for group in range(1, GROUPS):
                        total = total + got_cols[part, half * GROUPS + group]
                    main = total[0:PART]
                    rows = slice(half * PART, (half + 1) * PART)
                    col_halo[side, 0, rows, :] = main
                    col_halo[side, 1, rows, :] = pltpu.roll(main, COL - LON, 1)
                    main = pltpu.roll(main, COL - 2 * LON, 1)
                    row, lane = iota((8, COL), 0), iota((8, COL), 1)
                    for s in range(FOLD):
                        value = main[8 * s : 8 * s + 8, :]
                        rest = jnp.broadcast_to(total[PART + s : PART + s + 1], (8, COL))
                        for q in range(8):
                            moved = pltpu.roll(rest, (2 * COL - 2 * LON - SPARE * q) % COL, 1)
                            value = jnp.where(jnp.logical_and(row == q, lane >= COL - 2 * LON), moved, value)
                        at = half * PART + 8 * s
                        col_halo[side, 2, at : at + 8, :] = value
                corrections(part, side, True)
                if part == 0:
                    contribute(side, True)

            @pl.when(lon == (0 if side == 0 else n_lon - 1))
            def _():
                for source in range(TARGETS):
                    l_arrival(part, source).wait_recv()
                for half in range(2):
                    total = got_rows[part, half * GROUPS]
                    for group in range(1, GROUPS):
                        total = total + got_rows[part, half * GROUPS + group]
                    row_halo[side, :, half * PART : (half + 1) * PART, :] = total
                corrections(part, side, False)
                if part == 0:
                    contribute(side, False)

    for part in range(2):
        if part == 0:
            interpolate(0, 0)
            pl.semaphore_wait(barrier, 2 * len(AROUND) + 2 + TARGETS)
            send(0, 0)
            interpolate(0, 1)
            send(0, 1)
            message_tables()
            for target in range(TARGETS):
                idx_copy(target).start()
            other_tables()
        else:
            send(1, 0)
            send(1, 1)
            apply_edges()
        rows_of(part)
        cols_of(part)
        if part == 0:
            for source in range(TARGETS):
                idx_arrival(source).wait_recv()
            prepare_picks()
        lane_pass(part)
        emf_pass(part)
        for step in range(1, GROUP):
            a_arrival(part, step).wait_recv()
        both = table_split(part)
        pick_all(part, both)
        for side in range(2):

            @pl.when(sends_rows[side])
            def _():
                row_copy(part, side).start()

            @pl.when(sends_cols[side])
            def _():
                col_copy(part, side).start()

        main_pass(part, 0, 6)
        if part == 0:
            interpolate(1, 0)
            interpolate(1, 1)
        inner_sides(part)
        outer_sides(part)

    for target in range(TARGETS):
        idx_copy(target).wait_send()
    for part in range(2):
        for half in range(2):
            for step in AROUND:
                a_copy(part, step, half).wait_send()
        s_copy(part, 0).wait_send()
        for side in range(2):
            l_copy(part, side).wait_send()

            @pl.when(sends_rows[side])
            def _():
                row_copy(part, side).wait_send()

            @pl.when(sends_cols[side])
            def _():
                col_copy(part, side).wait_send()


        @pl.when(col_edge)
        def _():
            for target in range(TARGETS):
                b_copy(part, target).wait_send()


def shards(state, send_base, send_frac, recv_slots):
    rows = FLAT * LON
    dma = pltpu.SemaphoreType.DMA
    vmem = pltpu.VMEM
    scratch = [
        vmem((2, FLAT, STRIDE, COL), F32),
        vmem((1, OUT), I32),
        vmem((2, OUT), F32),
        vmem((1, recv_slots.shape[-1]), I32),
        vmem((3 * SHELLS * STRIDE, COL), F32),
        vmem(((FLAT + 2 * SHELLS) * LON, 2 * COL), F32),
        vmem((3 * COL, SLOTS), BF16),
        vmem((COL, SLOTS), F32),
        vmem((LON, SLOTS), F32),
        vmem((3 * COL, SLOTS), BF16),
        vmem((2 * COL, 2 * COL), BF16),
        vmem((TILES, SLOTS, 2 * COL), BF16),
        vmem((TILES, 8, 2 * COL), I32),
        vmem((2, COL, COL), F32),
        vmem((2, 2, PART, SLOTS), F32),
        vmem((2, GROUP, PART, SLOTS), F32),
        vmem((8, COL), I32),
        vmem((TARGETS, 8, COL), I32),
        vmem((2, FOLD, 8, COL), F32),
        vmem((2, TARGETS, PART + FOLD, COL), F32),
        vmem((2, 2, HALO, PART, COL), F32),
        vmem((2, TARGETS, PART + FOLD, COL), F32),
        vmem((2, TARGETS, HALO, PART, COL), F32),
        vmem((2, 2, HALO, FLAT, COL), F32),
        vmem((2, 2, HALO, FLAT, COL), F32),
        vmem((2, 2, HALO, FLAT, COL), F32),
        vmem((2, 2, 2, FLAT, COL), F32),
        vmem((2, 2, 2, FLAT, COL), F32),
        vmem((2, HALO, FLAT, COL), F32),
        vmem((2, HALO, FLAT, COL), F32),
        dma((4,)),
        dma((TARGETS,)),
        dma((TARGETS,)),
        dma((2, 2, RING)),
        dma((2, GROUP)),
        dma((2,)),
        dma((2, TARGETS)),
        dma((2, TARGETS)),
        dma((2, 2)),
        dma((2, TARGETS)),
        dma((2, 2)),
        dma((2, 2)),
        dma((2, 2)),
        dma((2, 2)),
    ]
    edges = jax.ShapeDtypeStruct((2, HALO, FLAT, COL), F32)
    value, row_add, col_add = pl.pallas_call(
        kernel,
        out_shape=(jax.ShapeDtypeStruct((rows, COL), F32), edges, edges),
        in_specs=[pl.BlockSpec(memory_space=pltpu.HBM)] * 4,
        out_specs=[pl.BlockSpec(memory_space=pltpu.VMEM)] * 3,
        scratch_shapes=scratch,
        compiler_params=pltpu.CompilerParams(
            collective_id=0, has_side_effects=True, vmem_limit_bytes=40 * 1024 * 1024
        ),
    )(*(
        pltpu.with_memory_space_constraint(x, pltpu.HBM)
        for x in (state.reshape(FLAT, LON, COL), send_base[0], send_frac[0, 0], recv_slots[0])
    ))
    result = pl.pallas_call(
        closing,
        out_shape=jax.ShapeDtypeStruct((rows, COL), F32),
        in_specs=[pl.BlockSpec(memory_space=pltpu.VMEM)] * 3,
        out_specs=pl.BlockSpec(memory_space=pltpu.HBM),
        scratch_shapes=[vmem((2, COL, COL), F32), vmem((rows, COL), F32), dma((4,))],
        compiler_params=pltpu.CompilerParams(vmem_limit_bytes=16 * 1024 * 1024),
    )(value, row_add, col_add)
    return result.reshape(state.shape)


def solution(mesh):
    placed = (
        P("panel", None, None, "lon", "colat"),
        P("panel", ("lon", "colat"), None),
        P("panel", ("lon", "colat"), None, None),
        P("panel", ("lon", "colat"), None),
    )
    return jax.shard_map(
        shards,
        mesh=mesh,
        in_specs=placed,
        out_specs=P("panel", None, None, "lon", "colat"),
        check_vma=False,
    )
```

```python
import math

import jax
import jax.numpy as jnp
from jax import lax
from jax.experimental import pallas as pl
from jax.experimental.pallas import tpu as pltpu
from jax.sharding import PartitionSpec as P

MESH = pl.DeviceIdType.MESH
F32, BF16, I32 = jnp.float32, jnp.bfloat16, jnp.int32

QUANTITIES = 8
SHELLS = 4
FLAT = QUANTITIES * SHELLS
LON = 48
COL = 128
HALO = 3
OUT = 240
SIDE = HALO * LON
SLOTS = 256
GROUP = 8
GROUPS = 8
AROUND = (1, 3, 2)
SPARE = SIDE - COL
PART = FLAT // 2
TARGETS = 2 * GROUPS
TILES = 12
RING = 4
FOLD = PART // 8
STRIDE = LON + 16
TIME_STEP = 0.25
SPREAD = 0.1 / 3.0
S, MR, MT, MP, BR, BT, BP, WARM = range(QUANTITIES)


def dot(left, right):
    return jnp.dot(left, right, preferred_element_type=F32)


def split(value):
    high = value.astype(BF16)
    return high, (value - high.astype(F32)).astype(BF16)


def iota(shape, dim):
    return lax.broadcasted_iota(I32, shape, dim)


def cross_radial(m, b):
    return m[1] * b[2] - m[2] * b[1]


def cross_polar(m, b):
    return m[2] * b[0] - m[0] * b[2]


def cross_azimuthal(m, b):
    return m[0] * b[1] - m[1] * b[0]


def edge_rates(own, d, lap, emf_first, emf_second, along_lanes):
    grow, thin = jnp.exp(own[WARM]), jnp.exp(-own[S])
    b = own[BR:WARM]
    if along_lanes:
        vel, out = own[MT], MT
        lorentz = (d[BR] * b[1], -d[BR] * b[0] - d[BP] * b[2], d[BP] * b[1])
        turn = (emf_first, None, -emf_second)
    else:
        vel, out = own[MP], MP
        lorentz = (d[BR] * b[2], d[BT] * b[2], -d[BT] * b[1] - d[BR] * b[0])
        turn = (-emf_first, emf_second, None)
    result = [-vel * d[S] - d[out]]
    for i in range(3):
        rate = -vel * d[MR + i] + thin * lorentz[i] + SPREAD * lap[MR + i]
        if MR + i == out:
            rate = rate - grow * (d[S] + d[WARM])
        result.append(rate)
    for i in range(3):
        rate = SPREAD * lap[BR + i]
        result.append(rate if turn[i] is None else rate + turn[i])
    result.append(-vel * d[WARM] - (2.0 / 3.0) * d[out] + SPREAD * lap[WARM])
    return result


def shell_first(x):
    a, b = 8.0 * (x[3] - x[0]), 45.0
    return (
        b * (x[1] - x[0]) - 9.0 * (x[2] - x[0]) + (x[3] - x[0]),
        b * (x[2] - x[0]) - a,
        b * (x[3] - x[1]) - a,
        b * (x[3] - x[2]) - 9.0 * (x[3] - x[1]) + (x[3] - x[0]),
    )


def shell_second(x):
    return (
        2.0 * x[3] - 27.0 * x[2] + 270.0 * x[1] - 245.0 * x[0],
        245.0 * x[0] - 490.0 * x[1] + 270.0 * x[2] - 25.0 * x[3],
        245.0 * x[3] - 490.0 * x[2] + 270.0 * x[1] - 25.0 * x[0],
        2.0 * x[0] - 27.0 * x[1] + 270.0 * x[2] - 245.0 * x[3],
    )


def turn_edges(col_add, turned):
    for side in range(2):
        for j in range(HALO):
            for half in range(2):
                turned[half, pl.ds((1 - side) * HALO + j, FLAT // 2, stride=8), :] = col_add[
                    side, j, half * (FLAT // 2) : (half + 1) * (FLAT // 2), :
                ]


def field_edge(edge, g):
    lane = iota((LON, COL), 1)
    border = jnp.logical_or(lane < HALO, lane >= COL - HALO)
    return jnp.where(border, pltpu.roll(edge, COL - 8 * g - HALO, 1), 0.0)


def closing(value_ref, row_add, col_add, out_hbm, turned, ready, sem):
    turn_edges(col_add, turned)
    copies = []
    for half in range(2):
        edge = jnp.transpose(turned[half])[0:LON, :]
        for chunk in range(2):
            first = half * (FLAT // 2) + 8 * chunk
            for q in range(8):
                at = (first + q) * LON
                ready[at : at + LON, :] = value_ref[at : at + LON, :] + field_edge(edge, 8 * chunk + q)
            for side in range(2):
                for j in range(HALO):
                    rows = pl.ds(first * LON + (j if side == 0 else LON - HALO + j), 8, stride=LON)
                    ready[rows, :] = ready[rows, :] + row_add[side, j, first : first + 8, :]
            rows = pl.ds(first * LON, 8 * LON)
            copy = pltpu.make_async_copy(ready.at[rows, :], out_hbm.at[rows, :], sem.at[2 * half + chunk])
            copy.start()
            copies.append(copy)
    for copy in copies:
        copy.wait()


def kernel(
    x_hbm, base_hbm, frac_hbm, slots_hbm, out_ref, row_add, col_add,
    deep, base_ref, frac_ref, slots_ref, emf, lanes, mix, cols_mix, rows_mix, rows_split, band, onehot, owner, turned,
    blocks, table, idx_out, idx_in, rest_rows, picked, picked_rows, got_cols, got_rows, row_out, row_in, col_own, col_out, col_in,
    row_halo, col_halo,
    in_sem, idx_send, idx_recv, a_send, a_recv, s_send, b_send, b_recv, l_send, l_recv, r_send, r_recv, c_send, c_recv,
):
    panel, lon, col = lax.axis_index("panel"), lax.axis_index("lon"), lax.axis_index("colat")
    n_lon, n_col = lax.axis_size("lon"), lax.axis_size("colat")
    core, mine = lon & 1, lon >> 1
    member = core * n_col + col
    other = 1 - panel
    lon_up, lon_down = lax.rem(lon + 1, n_lon), lax.rem(lon + n_lon - 1, n_lon)
    col_up, col_down = lax.rem(col + 1, n_col), lax.rem(col + n_col - 1, n_col)
    outer = lax.rem(lon + 2 * core - 1 + n_lon, n_lon)
    sends_rows = (lon < n_lon - 1, lon > 0)
    sends_cols = (col < n_col - 1, col > 0)
    col_edge = jnp.logical_or(col == 0, col == n_col - 1)

    sibling = (panel, lon + 1 - 2 * core, col)
    origin = core * GROUPS + mine

    def row_device(step, half):
        return (panel, 2 * mine + half, (col + step) & (n_col - 1))

    def target_device(target):
        return (other, 2 * (target & (GROUPS - 1)) + (target >> 3), col)

    def remote(src, dst, send, recv, device):
        return pltpu.make_async_remote_copy(
            src_ref=src, dst_ref=dst, send_sem=send, recv_sem=recv, device_id=device, device_id_type=MESH
        )

    frame = deep.reshape(2, FLAT * STRIDE, COL)
    copies = [
        pltpu.make_async_copy(src, dst, in_sem.at[i])
        for i, (src, dst) in enumerate(
            (
                (frac_hbm, frac_ref),
                (base_hbm, base_ref),
                (slots_hbm, slots_ref),
                (x_hbm, deep.at[0, :, pl.ds(8, LON), :]),
            )
        )
    ]
    for copy in copies:
        copy.start()

    barrier = pltpu.get_barrier_semaphore()
    for step in AROUND:
        for half in range(2):
            pl.semaphore_signal(barrier, inc=1, device_id=row_device(step, half), device_id_type=MESH)
    pl.semaphore_signal(barrier, inc=1, device_id=sibling, device_id_type=MESH)
    for target in range(TARGETS):
        pl.semaphore_signal(barrier, inc=1, device_id=target_device(target), device_id_type=MESH)
    pl.semaphore_signal(barrier, inc=1, device_id=(panel, outer, col), device_id_type=MESH)

    copies[0].wait()
    copies[1].wait()
    base = jnp.concatenate([base_ref[...], jnp.zeros((1, SLOTS - OUT), I32)], axis=1)
    base_row, base_col = lax.div(base, COL), lax.rem(base, COL)
    share = jnp.concatenate([frac_ref[...], jnp.zeros((2, SLOTS - OUT), F32)], axis=1)
    along, across = share[0:1, :], share[1:2, :]
    cells = iota((COL, SLOTS), 0)
    weight = jnp.where(cells == base_col, 1.0 - across, 0.0) + jnp.where(cells == base_col + 1, across, 0.0)
    weight_high, weight_low = split(weight)
    cols_mix[...] = weight
    mix[0:COL, :] = weight_high
    mix[COL : 2 * COL, :] = weight_high
    mix[2 * COL : 3 * COL, :] = weight_low
    cells = iota((LON, SLOTS), 0)
    weight = jnp.where(cells == base_row, 1.0 - along, 0.0) + jnp.where(cells == base_row + 1, along, 0.0)
    rows_mix[...] = weight
    place = (col * COL + iota((1, COL), 1)).astype(F32)
    scale = 1.0 / jnp.sin(math.pi / 4.0 + (place + 0.5) * (math.pi / 2.0 / (COL * n_col)))

    def message_tables():
        copies[2].wait()
        spot = iota((1, SLOTS), 1)
        sides = jnp.where(spot < SIDE, jnp.maximum(slots_ref[:, 0:SLOTS], slots_ref[:, SIDE : SIDE + SLOTS]) + 1, 0)
        digits = jnp.concatenate([lax.div(sides, COL), lax.rem(sides, COL), jnp.zeros((6, SLOTS), I32)], axis=0)
        source, target = iota((SLOTS, SLOTS), 0), iota((SLOTS, SLOTS), 1)
        layer = jnp.where(target >= LON, 1, 0) + jnp.where(target >= 2 * LON, 1, 0)
        order = jnp.logical_and(target < SIDE, source == HALO * (target - LON * layer) + layer)
        digits = dot(digits.astype(F32).astype(BF16), jnp.where(order, 1.0, 0.0).astype(BF16)).astype(I32)
        sides = digits[0:1, :] * COL + digits[1:2, :] - 1
        idx_out[0:1, :] = sides[:, 0:COL]
        idx_out[1:2, :] = sides[:, COL : 2 * COL]
        for h in range(HALO):
            at = 2 * SIDE + h * COL
            idx_out[2 + h : 3 + h, :] = jnp.maximum(
                slots_ref[:, at : at + COL], slots_ref[:, at + HALO * COL : at + HALO * COL + COL]
            )
        idx_out[5:8, :] = jnp.full((3, COL), -1, I32)

    def other_tables():
        zero_rows = jnp.zeros((8, COL), F32)
        for f in range(FLAT):
            for part in range(2):
                frame[part, f * STRIDE : f * STRIDE + 8, :] = zero_rows
                frame[part, f * STRIDE + 8 + LON : (f + 1) * STRIDE, :] = zero_rows
        for f in range(3 * SHELLS):
            emf[f * STRIDE : f * STRIDE + 8, :] = zero_rows
            emf[f * STRIDE + 8 + LON : (f + 1) * STRIDE, :] = zero_rows

        for half in range(2):
            turned[half, :, :] = jnp.zeros((COL, COL), F32)

        apart = iota((COL, COL), 0) - iota((COL, COL), 1)
        reach = jnp.abs(apart)
        first = jnp.where(reach == 1, 45.0, jnp.where(reach == 2, -9.0, jnp.where(reach == 3, 1.0, 0.0)))
        first = jnp.where(apart < 0, -first, first).astype(BF16)
        second = jnp.where(
            reach == 0, -490.0, jnp.where(reach == 1, 270.0, jnp.where(reach == 2, -27.0, jnp.where(reach == 3, 2.0, 0.0)))
        ).astype(BF16)
        for part in range(2):
            band[part * COL : (part + 1) * COL, 0:COL] = first
            band[part * COL : (part + 1) * COL, COL : 2 * COL] = second
        weight_high, weight_low = split(jnp.concatenate([rows_mix[...], jnp.zeros((COL - LON, SLOTS), F32)], axis=0))
        rows_split[0:COL, :] = weight_high
        rows_split[COL : 2 * COL, :] = weight_high
        rows_split[2 * COL : 3 * COL, :] = weight_low

    def load_split(part, pair):
        block = jnp.concatenate(
            [frame[part, pl.ds(pl.multiple_of((8 * pair + q) * STRIDE + 8, 8), LON), :] for q in range(8)], axis=0
        )
        return split(block)

    def interpolate(part, half):
        for pair in range(PART // 8):
            high, low = load_split(part, 2 * half + pair)
            value = dot(jnp.concatenate([high, low, high], axis=1), mix[...])
            value = jnp.sum(value.reshape(8, LON, SLOTS) * rows_mix[...][None], axis=1)
            blocks[part, half, 8 * pair : 8 * pair + 8, :] = value

    def send(part, half):
        for step in AROUND:
            a_copy(part, step, half).start()

        @pl.when(core != half)
        def _():
            s_copy(part, half).start()

        @pl.when(core == half)
        def _():
            table[part, member] = blocks[part, half]

    def lane_pass(part):
        def body(pair, carry):
            high, low = load_split(part, pair)
            both = jnp.concatenate([high, low], axis=1)
            lanes[pl.ds(pl.multiple_of(8 * LON * pair, 8), 8 * LON), :] = dot(both, band[...])
            return carry

        lax.fori_loop(0, FLAT // 8, body, 0)

    def cols_of(part):
        lane = iota((LON, COL), 1)
        for half in range(2):
            edge = jnp.zeros((LON, COL), F32)
            for g in range(FLAT // 2):
                at = (half * (FLAT // 2) + g) * STRIDE + 8
                moved = pltpu.roll(frame[part, at : at + LON, :], 8 * g + HALO, 1)
                edge = jnp.where(jnp.logical_and(lane >= 8 * g, lane < 8 * g + 2 * HALO), moved, edge)
            turned[half, :, 0:LON] = jnp.transpose(edge)
        for side in range(2):
            for j in range(HALO):
                first = (1 - side) * HALO + j
                for half in range(2):
                    col_own[part, side, j, half * (FLAT // 2) : (half + 1) * (FLAT // 2), :] = turned[
                        half, pl.ds(first, FLAT // 2, stride=8), :
                    ]
            col_out[part, side, 0] = jnp.where(
                iota((FLAT, COL), 1) < COL // 2, col_own[part, side, 0], pltpu.roll(col_own[part, side, 1], COL // 2, 1)
            )
            col_out[part, side, 1] = col_own[part, side, 2]

    def emf_pass(part):
        for r in range(SHELLS):
            def field(q):
                at = (q * SHELLS + r) * STRIDE + 8
                return frame[part, at : at + LON, :]

            m, b = [field(MR + i) for i in range(3)], [field(BR + i) for i in range(3)]
            for i, form in enumerate((cross_radial, cross_polar, cross_azimuthal)):
                at = (i * SHELLS + r) * STRIDE + 8
                emf[at : at + LON, :] = form(m, b)
        for i, at in ((0, FLAT), (2, FLAT + SHELLS)):
            block = jnp.concatenate(
                [emf[(i * SHELLS + r) * STRIDE + 8 : (i * SHELLS + r) * STRIDE + 8 + LON, :] for r in range(SHELLS)],
                axis=0,
            )
            high, low = split(block)
            lanes[at * LON : (at + SHELLS) * LON, 0:COL] = dot(
                jnp.concatenate([high, low], axis=1), band[:, 0:COL]
            )

    def main_pass(part, start, stop):
        def body(block, carry):
            here = pl.multiple_of(8 * block, 8)

            def near(f, apart):
                return frame[part, pl.ds(f * STRIDE + 8 + here + apart, 8), :]

            def near_emf(f, apart):
                return emf[pl.ds(f * STRIDE + 8 + here + apart, 8), :]

            def lane_first(f):
                return lanes[pl.ds(f * LON + here, 8), 0:COL]

            def lane_second(f):
                return lanes[pl.ds(f * LON + here, 8), COL : 2 * COL]

            def row_first(at):
                return 45.0 * (at[1] - at[-1]) - 9.0 * (at[2] - at[-2]) + (at[3] - at[-3])

            def row_second(at, centre):
                return (
                    270.0 * (at[1] + at[-1]) - 27.0 * (at[2] + at[-2]) + 2.0 * (at[3] + at[-3]) - 490.0 * centre
                )

            centre = [[near(q * SHELLS + r, 0) for r in range(SHELLS)] for q in range(QUANTITIES)]
            radial = [shell_first(x) for x in centre]
            radial_second = [None if q == S else shell_second(centre[q]) for q in range(QUANTITIES)]
            emf_centre = [[near_emf(i * SHELLS + r, 0) for r in range(SHELLS)] for i in range(3)]
            emf_radial = [None, shell_first(emf_centre[1]), shell_first(emf_centre[2])]
            for r in range(SHELLS):
                own = [centre[q][r] for q in range(QUANTITIES)]
                g, lap = [], []
                for q in range(QUANTITIES):
                    f = q * SHELLS + r
                    at = {d: near(f, d) for d in (-3, -2, -1, 1, 2, 3)}
                    g.append((radial[q][r], lane_first(f), scale * row_first(at)))
                    if q == S:
                        lap.append(None)
                    else:
                        lap.append(
                            radial_second[q][r] + lane_second(f) + (scale * scale) * row_second(at, own[q])
                        )
                m, b = own[MR:BR], own[BR:WARM]

                def advect(q):
                    return m[0] * g[q][0] + m[1] * g[q][1] + m[2] * g[q][2]

                div = g[MR][0] + g[MT][1] + g[MP][2]
                current = (g[BP][1] - g[BT][2], g[BR][2] - g[BP][0], g[BT][0] - g[BR][1])
                lorentz = (
                    current[1] * b[2] - current[2] * b[1],
                    current[2] * b[0] - current[0] * b[2],
                    current[0] * b[1] - current[1] * b[0],
                )
                grow, thin = jnp.exp(own[WARM]), jnp.exp(-own[S])
                emf_rows = {}
                for i in (0, 1):
                    f = i * SHELLS + r
                    emf_rows[i] = scale * row_first({d: near_emf(f, d) for d in (-3, -2, -1, 1, 2, 3)})
                turn = (
                    lane_first(FLAT + SHELLS + r) - emf_rows[1],
                    emf_rows[0] - emf_radial[2][r],
                    emf_radial[1][r] - lane_first(FLAT + r),
                )
                result = [-advect(S) - div]
                for i in range(3):
                    result.append(
                        -advect(MR + i) - grow * (g[S][i] + g[WARM][i]) + thin * lorentz[i] + SPREAD * lap[MR + i]
                    )
                for i in range(3):
                    result.append(turn[i] + SPREAD * lap[BR + i])
                result.append(-advect(WARM) - (2.0 / 3.0) * div + SPREAD * lap[WARM])
                for q in range(QUANTITIES):
                    f = q * SHELLS + r
                    value = own[q] + (TIME_STEP / 60.0) * result[q]
                    if part == 0:
                        frame[1, pl.ds(f * STRIDE + 8 + here, 8), :] = value
                    else:
                        start = frame[0, pl.ds(f * STRIDE + 8 + here, 8), :]
                        out_ref[pl.ds(f * LON + here, 8), :] = 0.5 * (start + value)
            return carry

        lax.fori_loop(start, stop, body, 0)

    def rows_of(part):
        for h in range(HALO):
            row_out[part, 0, h] = frame[part, pl.ds(8 + h, FLAT, stride=STRIDE), :]
            row_out[part, 1, h] = frame[part, pl.ds(8 + LON - HALO + h, FLAT, stride=STRIDE), :]

    def prepare_picks():
        for tile in range(2 * TILES):
            if tile < TARGETS:
                slot = idx_in[tile, 0:1, :]
            elif tile < TARGETS + 2:
                first = (tile - TARGETS) * GROUPS
                slot = idx_in[first, 1:2, :]
                for q in range(1, GROUPS):
                    slot = jnp.maximum(slot, pltpu.roll(idx_in[first + q], SPARE * q, 1)[1:2, :])
            else:
                side, h = divmod(tile - TARGETS - 2, HALO)
                slot = idx_in[side * (TARGETS - 1), 2 + h : 3 + h, :]
            slot = slot - mine * (GROUP * OUT)
            who = jnp.zeros_like(slot)
            for q in range(1, GROUP):
                who = who + jnp.where(slot >= q * OUT, 1, 0)
            cell = slot - who * OUT
            who = jnp.where(jnp.logical_and(slot >= 0, slot < GROUP * OUT), who, -1)
            at = (tile % 2) * COL
            owner[tile // 2, :, at : at + COL] = jnp.broadcast_to(who, (8, COL))
            hot = jnp.where(iota((SLOTS, COL), 0) == cell, 1.0, 0.0).astype(BF16)
            onehot[tile // 2, :, at : at + COL] = hot

    def table_split(part):
        high, low = split(table[part].reshape(GROUP * PART, SLOTS))
        return jnp.concatenate([high, low], axis=0)

    def product(both, tile):
        return dot(both, onehot[tile])

    def chosen(value, tile):
        value = value[0 : GROUP * PART] + value[GROUP * PART :]
        who = jnp.broadcast_to(owner[tile, 0:1, :], (PART, SLOTS))
        total = jnp.zeros((PART, SLOTS), F32)
        for q in range(GROUP):
            total = jnp.where(who == q, value[q * PART : (q + 1) * PART, :], total)
        return total[:, 0:COL], total[:, COL : 2 * COL]

    def fold(rests):
        turn = (lax.div(iota((8, COL), 1), SPARE) - iota((8, COL), 0)) & 7
        for half, rest in enumerate(rests):
            for s in range(FOLD):
                total = jnp.zeros((8, COL), F32)
                for d in range(8):
                    moved = rest[8 * s : 8 * s + 8, :]
                    if d:
                        moved = pltpu.roll(pltpu.roll(moved, SPARE * d, 1), 8 - d, 0)
                    total = jnp.where(turn == d, moved, total)
                rest_rows[half, s] = total

    def pick_all(part, both):
        sides = [(step + mine) & (TARGETS // 2 - 1) for step in range(TARGETS // 2)]
        extra = list(range(TARGETS // 2 + 1, TILES))
        ends, value = [], product(both, extra[0])
        for tile, after in zip(extra, extra[1:] + [None]):
            now = value
            if after is not None:
                value = product(both, after)
            ends += chosen(now, tile)
        for side in range(2):
            for h in range(HALO):
                picked_rows[part, side, h] = ends[side * HALO + h]
        for side in range(2):
            l_copy(part, side).start()

        @pl.when(col_edge)
        def _():
            now, value = product(both, TARGETS // 2), product(both, sides[0])
            fold(chosen(now, TARGETS // 2))
            for step, tile in enumerate(sides):
                now = value
                if step + 1 < len(sides):
                    value = product(both, sides[step + 1])
                for i, end in enumerate(chosen(now, tile)):
                    target = 2 * tile + i
                    picked[part, target, 0:PART, :] = end
                    for s in range(FOLD):
                        picked[part, target, PART + s : PART + s + 1, :] = rest_rows[
                            tile >> 2, s, pl.ds(target & (GROUPS - 1), 1), :
                        ]
                for i in range(2):
                    b_copy(part, 2 * tile + i).start()

    def corrections(part, side, along_lanes):
        halo_ref, own_ref, add_ref = (col_halo, col_own, col_add) if along_lanes else (row_halo, row_out, row_add)

        def scaled(value, power):
            for _ in range(0 if along_lanes else power):
                value = scale * value
            return value

        halo = [[halo_ref[side, h, q * SHELLS : (q + 1) * SHELLS, :] for q in range(QUANTITIES)] for h in range(HALO)]
        form = cross_azimuthal if along_lanes else cross_polar
        halo_emf = [(cross_radial(x[MR:BR], x[BR:WARM]), form(x[MR:BR], x[BR:WARM])) for x in halo]
        sign = -1.0 if side == 0 else 1.0
        firsts, seconds = (45.0 * sign, -9.0 * sign, sign), (270.0, -27.0, 2.0)
        for j in range(HALO):
            own = [own_ref[part, side, j, q * SHELLS : (q + 1) * SHELLS, :] for q in range(QUANTITIES)]

            def total(weights, of):
                result = None
                for m in (1, 2, 3):
                    h = j + 3 - m if side == 0 else m - 3 + j
                    if 0 <= h < HALO:
                        term = weights[m - 1] * of(h)
                        result = term if result is None else result + term
                return result

            d = [scaled(total(firsts, lambda h, q=q: halo[h][q]), 1) for q in range(QUANTITIES)]
            lap = [
                None if q == S else scaled(total(seconds, lambda h, q=q: halo[h][q]), 2) for q in range(QUANTITIES)
            ]
            radial = scaled(total(firsts, lambda h: halo_emf[h][0]), 1)
            second = scaled(total(firsts, lambda h: halo_emf[h][1]), 1)
            result = edge_rates(own, d, lap, second, radial, along_lanes)
            for q in range(QUANTITIES):
                add_ref[side, j, q * SHELLS : (q + 1) * SHELLS, :] = (TIME_STEP / 60.0 / (1 + part)) * result[q]

    def contribute(side, along_lanes):
        add_ref = col_add if along_lanes else row_add
        value = jnp.concatenate([add_ref[side, j] for j in range(HALO)], axis=0)
        if along_lanes:
            value = jnp.where(iota((HALO * FLAT, COL), 1) < LON, value, 0.0)
        high, low = split(value)
        value = dot(jnp.concatenate([high, low, high], axis=1), rows_split[...] if along_lanes else mix[...])
        total = jnp.zeros((FLAT, SLOTS), F32)
        for j in range(HALO):
            if along_lanes:
                at = j if side == 0 else COL - HALO + j
                weight = cols_mix[at : at + 1, :]
            else:
                at = j if side == 0 else LON - HALO + j
                weight = rows_mix[at : at + 1, :]
            total = total + weight * value[j * FLAT : (j + 1) * FLAT, :]
        for half in range(2):
            blocks[1, half] = blocks[1, half] + total[half * PART : (half + 1) * PART, :]

    def apply_edges():
        for side in range(2):
            for j in range(HALO):
                rows = pl.ds(8 + (j if side == 0 else LON - HALO + j), FLAT, stride=STRIDE)
                frame[1, rows, :] = frame[1, rows, :] + row_add[side, j]
        turn_edges(col_add, turned)
        for half in range(2):
            edge = jnp.transpose(turned[half])[0:LON, :]
            for g in range(FLAT // 2):
                at = (half * (FLAT // 2) + g) * STRIDE + 8
                frame[1, at : at + LON, :] = frame[1, at : at + LON, :] + field_edge(edge, g)

    def a_copy(part, step, half):
        return remote(
            blocks.at[part, half], table.at[part, member], a_send.at[part, half, step], a_recv.at[part, member],
            row_device(step, half),
        )

    def s_copy(part, half):
        return remote(
            blocks.at[part, half], table.at[part, member], s_send.at[part], a_recv.at[part, member], sibling
        )

    def a_arrival(part, step):
        there = (member + step) & (GROUP - 1)
        return remote(blocks.at[part, 0], table.at[part, there], s_send.at[part], a_recv.at[part, there], sibling)

    def b_copy(part, target):
        return remote(
            picked.at[part, target], got_cols.at[part, origin], b_send.at[part, target], b_recv.at[part, origin],
            target_device(target),
        )

    def b_arrival(part, source):
        return remote(
            picked.at[part, 0], got_cols.at[part, source], b_send.at[part, 0], b_recv.at[part, source],
            (other, lon, col),
        )

    def l_copy(part, side):
        return remote(
            picked_rows.at[part, side], got_rows.at[part, origin], l_send.at[part, side], l_recv.at[part, origin],
            target_device(side * (TARGETS - 1)),
        )

    def l_arrival(part, source):
        return remote(
            picked_rows.at[part, 0], got_rows.at[part, source], l_send.at[part, 0], l_recv.at[part, source],
            (other, lon, col),
        )

    def row_copy(part, side):
        return remote(
            row_out.at[part, 1 - side], row_in.at[part, side], r_send.at[part, side], r_recv.at[part, side],
            (panel, lon_up if side == 0 else lon_down, col),
        )

    def col_copy(part, side):
        return remote(
            col_out.at[part, 1 - side], col_in.at[part, side], c_send.at[part, side], c_recv.at[part, side],
            (panel, lon, col_up if side == 0 else col_down),
        )

    def idx_copy(target):
        return remote(
            idx_out, idx_in.at[origin], idx_send.at[target], idx_recv.at[origin], target_device(target)
        )

    def idx_arrival(source):
        return remote(idx_out, idx_in.at[source], idx_send.at[0], idx_recv.at[source], (other, lon, col))

    def inner_sides(part):
        for side in range(2):
            @pl.when(lon != (0 if side == 0 else n_lon - 1))
            def _():
                row_copy(part, side).wait_recv()
                row_halo[side] = row_in[part, side]
                corrections(part, side, False)
                if part == 0:
                    contribute(side, False)

            @pl.when(col != (0 if side == 0 else n_col - 1))
            def _():
                col_copy(part, side).wait_recv()
                pair = col_in[part, side, 0]
                col_halo[side, 0] = pair
                col_halo[side, 1] = pltpu.roll(pair, COL // 2, 1)
                col_halo[side, 2] = col_in[part, side, 1]
                corrections(part, side, True)
                if part == 0:
                    contribute(side, True)

    def outer_sides(part):
        for side in range(2):

            @pl.when(col == (0 if side == 0 else n_col - 1))
            def _():
                for source in range(TARGETS):
                    b_arrival(part, source).wait_recv()
                for half in range(2):
                    total = got_cols[part, half * GROUPS]
                    for group in range(1, GROUPS):
                        total = total + got_cols[part, half * GROUPS + group]
                    main = total[0:PART]
                    rows = slice(half * PART, (half + 1) * PART)
                    col_halo[side, 0, rows, :] = main
                    col_halo[side, 1, rows, :] = pltpu.roll(main, COL - LON, 1)
                    main = pltpu.roll(main, COL - 2 * LON, 1)
                    row, lane = iota((8, COL), 0), iota((8, COL), 1)
                    for s in range(FOLD):
                        value = main[8 * s : 8 * s + 8, :]
                        rest = jnp.broadcast_to(total[PART + s : PART + s + 1], (8, COL))
                        for q in range(8):
                            moved = pltpu.roll(rest, (2 * COL - 2 * LON - SPARE * q) % COL, 1)
                            value = jnp.where(jnp.logical_and(row == q, lane >= COL - 2 * LON), moved, value)
                        at = half * PART + 8 * s
                        col_halo[side, 2, at : at + 8, :] = value
                corrections(part, side, True)
                if part == 0:
                    contribute(side, True)

            @pl.when(lon == (0 if side == 0 else n_lon - 1))
            def _():
                for source in range(TARGETS):
                    l_arrival(part, source).wait_recv()
                for half in range(2):
                    total = got_rows[part, half * GROUPS]
                    for group in range(1, GROUPS):
                        total = total + got_rows[part, half * GROUPS + group]
                    row_halo[side, :, half * PART : (half + 1) * PART, :] = total
                corrections(part, side, False)
                if part == 0:
                    contribute(side, False)

    for part in range(2):
        if part == 0:
            message_tables()
            pl.semaphore_wait(barrier, 2 * len(AROUND) + 2 + TARGETS)
            for target in range(TARGETS):
                idx_copy(target).start()
            copies[3].wait()
            interpolate(0, 0)
            send(0, 0)
            interpolate(0, 1)
            send(0, 1)
            other_tables()
        else:
            send(1, 0)
            send(1, 1)
            apply_edges()
        rows_of(part)
        for side in range(2):

            @pl.when(sends_rows[side])
            def _():
                row_copy(part, side).start()

        cols_of(part)
        for side in range(2):

            @pl.when(sends_cols[side])
            def _():
                col_copy(part, side).start()

        lane_pass(part)
        emf_pass(part)
        if part == 0:
            for source in range(TARGETS):
                idx_arrival(source).wait_recv()
            prepare_picks()
        for step in range(1, GROUP):
            a_arrival(part, step).wait_recv()
        both = table_split(part)
        pick_all(part, both)
        main_pass(part, 0, 6)
        if part == 0:
            interpolate(1, 0)
            interpolate(1, 1)
        inner_sides(part)
        outer_sides(part)

    for target in range(TARGETS):
        idx_copy(target).wait_send()
    for part in range(2):
        for half in range(2):
            for step in AROUND:
                a_copy(part, step, half).wait_send()
        s_copy(part, 0).wait_send()
        for side in range(2):
            l_copy(part, side).wait_send()

            @pl.when(sends_rows[side])
            def _():
                row_copy(part, side).wait_send()

            @pl.when(sends_cols[side])
            def _():
                col_copy(part, side).wait_send()


        @pl.when(col_edge)
        def _():
            for target in range(TARGETS):
                b_copy(part, target).wait_send()


def shards(state, send_base, send_frac, recv_slots):
    rows = FLAT * LON
    dma = pltpu.SemaphoreType.DMA
    vmem = pltpu.VMEM
    scratch = [
        vmem((2, FLAT, STRIDE, COL), F32),
        vmem((1, OUT), I32),
        vmem((2, OUT), F32),
        vmem((1, recv_slots.shape[-1]), I32),
        vmem((3 * SHELLS * STRIDE, COL), F32),
        vmem(((FLAT + 2 * SHELLS) * LON, 2 * COL), F32),
        vmem((3 * COL, SLOTS), BF16),
        vmem((COL, SLOTS), F32),
        vmem((LON, SLOTS), F32),
        vmem((3 * COL, SLOTS), BF16),
        vmem((2 * COL, 2 * COL), BF16),
        vmem((TILES, SLOTS, 2 * COL), BF16),
        vmem((TILES, 8, 2 * COL), I32),
        vmem((2, COL, COL), F32),
        vmem((2, 2, PART, SLOTS), F32),
        vmem((2, GROUP, PART, SLOTS), F32),
        vmem((8, COL), I32),
        vmem((TARGETS, 8, COL), I32),
        vmem((2, FOLD, 8, COL), F32),
        vmem((2, TARGETS, PART + FOLD, COL), F32),
        vmem((2, 2, HALO, PART, COL), F32),
        vmem((2, TARGETS, PART + FOLD, COL), F32),
        vmem((2, TARGETS, HALO, PART, COL), F32),
        vmem((2, 2, HALO, FLAT, COL), F32),
        vmem((2, 2, HALO, FLAT, COL), F32),
        vmem((2, 2, HALO, FLAT, COL), F32),
        vmem((2, 2, 2, FLAT, COL), F32),
        vmem((2, 2, 2, FLAT, COL), F32),
        vmem((2, HALO, FLAT, COL), F32),
        vmem((2, HALO, FLAT, COL), F32),
        dma((4,)),
        dma((TARGETS,)),
        dma((TARGETS,)),
        dma((2, 2, RING)),
        dma((2, GROUP)),
        dma((2,)),
        dma((2, TARGETS)),
        dma((2, TARGETS)),
        dma((2, 2)),
        dma((2, TARGETS)),
        dma((2, 2)),
        dma((2, 2)),
        dma((2, 2)),
        dma((2, 2)),
    ]
    edges = jax.ShapeDtypeStruct((2, HALO, FLAT, COL), F32)
    value, row_add, col_add = pl.pallas_call(
        kernel,
        out_shape=(jax.ShapeDtypeStruct((rows, COL), F32), edges, edges),
        in_specs=[pl.BlockSpec(memory_space=pltpu.HBM)] * 4,
        out_specs=[pl.BlockSpec(memory_space=pltpu.VMEM)] * 3,
        scratch_shapes=scratch,
        compiler_params=pltpu.CompilerParams(
            collective_id=0, has_side_effects=True, vmem_limit_bytes=40 * 1024 * 1024
        ),
    )(*(
        pltpu.with_memory_space_constraint(x, pltpu.HBM)
        for x in (state.reshape(FLAT, LON, COL), send_base[0], send_frac[0, 0], recv_slots[0])
    ))
    result = pl.pallas_call(
        closing,
        out_shape=jax.ShapeDtypeStruct((rows, COL), F32),
        in_specs=[pl.BlockSpec(memory_space=pltpu.VMEM)] * 3,
        out_specs=pl.BlockSpec(memory_space=pltpu.HBM),
        scratch_shapes=[vmem((2, COL, COL), F32), vmem((rows, COL), F32), dma((4,))],
        compiler_params=pltpu.CompilerParams(vmem_limit_bytes=16 * 1024 * 1024),
    )(value, row_add, col_add)
    return result.reshape(state.shape)


def solution(mesh):
    placed = (
        P("panel", None, None, "lon", "colat"),
        P("panel", ("lon", "colat"), None),
        P("panel", ("lon", "colat"), None, None),
        P("panel", ("lon", "colat"), None),
    )
    return jax.shard_map(
        shards,
        mesh=mesh,
        in_specs=placed,
        out_specs=P("panel", None, None, "lon", "colat"),
        check_vma=False,
    )
```

```python
import math

import jax
import jax.numpy as jnp
from jax import lax
from jax.experimental import pallas as pl
from jax.experimental.pallas import tpu as pltpu
from jax.sharding import PartitionSpec as P

MESH = pl.DeviceIdType.MESH
F32, BF16, I32 = jnp.float32, jnp.bfloat16, jnp.int32

QUANTITIES = 8
SHELLS = 4
FLAT = QUANTITIES * SHELLS
LON = 48
COL = 128
HALO = 3
OUT = 240
SIDE = HALO * LON
SLOTS = 256
GROUP = 8
GROUPS = 8
AROUND = (1, 3, 2)
SPARE = SIDE - COL
PART = FLAT // 2
TARGETS = 2 * GROUPS
TILES = 12
RING = 4
FOLD = PART // 8
STRIDE = LON + 16
TIME_STEP = 0.25
SPREAD = 0.1 / 3.0
S, MR, MT, MP, BR, BT, BP, WARM = range(QUANTITIES)


def dot(left, right):
    return jnp.dot(left, right, preferred_element_type=F32)


def split(value):
    high = value.astype(BF16)
    return high, (value - high.astype(F32)).astype(BF16)


def iota(shape, dim):
    return lax.broadcasted_iota(I32, shape, dim)


def cross_radial(m, b):
    return m[1] * b[2] - m[2] * b[1]


def cross_polar(m, b):
    return m[2] * b[0] - m[0] * b[2]


def cross_azimuthal(m, b):
    return m[0] * b[1] - m[1] * b[0]


def edge_rates(own, d, lap, emf_first, emf_second, along_lanes):
    grow, thin = jnp.exp(own[WARM]), jnp.exp(-own[S])
    b = own[BR:WARM]
    if along_lanes:
        vel, out = own[MT], MT
        lorentz = (d[BR] * b[1], -d[BR] * b[0] - d[BP] * b[2], d[BP] * b[1])
        turn = (emf_first, None, -emf_second)
    else:
        vel, out = own[MP], MP
        lorentz = (d[BR] * b[2], d[BT] * b[2], -d[BT] * b[1] - d[BR] * b[0])
        turn = (-emf_first, emf_second, None)
    result = [-vel * d[S] - d[out]]
    for i in range(3):
        rate = -vel * d[MR + i] + thin * lorentz[i] + SPREAD * lap[MR + i]
        if MR + i == out:
            rate = rate - grow * (d[S] + d[WARM])
        result.append(rate)
    for i in range(3):
        rate = SPREAD * lap[BR + i]
        result.append(rate if turn[i] is None else rate + turn[i])
    result.append(-vel * d[WARM] - (2.0 / 3.0) * d[out] + SPREAD * lap[WARM])
    return result


def shell_first(x):
    a, b = 8.0 * (x[3] - x[0]), 45.0
    return (
        b * (x[1] - x[0]) - 9.0 * (x[2] - x[0]) + (x[3] - x[0]),
        b * (x[2] - x[0]) - a,
        b * (x[3] - x[1]) - a,
        b * (x[3] - x[2]) - 9.0 * (x[3] - x[1]) + (x[3] - x[0]),
    )


def shell_second(x):
    return (
        2.0 * x[3] - 27.0 * x[2] + 270.0 * x[1] - 245.0 * x[0],
        245.0 * x[0] - 490.0 * x[1] + 270.0 * x[2] - 25.0 * x[3],
        245.0 * x[3] - 490.0 * x[2] + 270.0 * x[1] - 25.0 * x[0],
        2.0 * x[0] - 27.0 * x[1] + 270.0 * x[2] - 245.0 * x[3],
    )


def turn_edges(col_add, turned):
    for side in range(2):
        for j in range(HALO):
            for half in range(2):
                turned[half, pl.ds((1 - side) * HALO + j, FLAT // 2, stride=8), :] = col_add[
                    side, j, half * (FLAT // 2) : (half + 1) * (FLAT // 2), :
                ]


def field_edge(edge, g):
    lane = iota((LON, COL), 1)
    border = jnp.logical_or(lane < HALO, lane >= COL - HALO)
    return jnp.where(border, pltpu.roll(edge, COL - 8 * g - HALO, 1), 0.0)


def closing(value_ref, row_add, col_add, out_hbm, turned, ready, sem):
    turn_edges(col_add, turned)
    copies = []
    for half in range(2):
        edge = jnp.transpose(turned[half])[0:LON, :]
        for chunk in range(2):
            first = half * (FLAT // 2) + 8 * chunk
            for q in range(8):
                at = (first + q) * LON
                ready[at : at + LON, :] = value_ref[at : at + LON, :] + field_edge(edge, 8 * chunk + q)
            for side in range(2):
                for j in range(HALO):
                    rows = pl.ds(first * LON + (j if side == 0 else LON - HALO + j), 8, stride=LON)
                    ready[rows, :] = ready[rows, :] + row_add[side, j, first : first + 8, :]
            rows = pl.ds(first * LON, 8 * LON)
            copy = pltpu.make_async_copy(ready.at[rows, :], out_hbm.at[rows, :], sem.at[2 * half + chunk])
            copy.start()
            copies.append(copy)
    for copy in copies:
        copy.wait()


def kernel(
    x_hbm, base_hbm, frac_hbm, slots_hbm, out_ref, row_add, col_add,
    deep, base_ref, frac_ref, slots_ref, emf, lanes, mix, cols_mix, rows_mix, rows_split, band, onehot, owner, turned,
    blocks, table, idx_out, idx_in, rest_rows, picked, picked_rows, got_cols, got_rows, row_out, row_in, col_own, col_out, col_in,
    row_halo, col_halo,
    in_sem, idx_send, idx_recv, a_send, a_recv, s_send, b_send, b_recv, l_send, l_recv, r_send, r_recv, c_send, c_recv,
):
    panel, lon, col = lax.axis_index("panel"), lax.axis_index("lon"), lax.axis_index("colat")
    n_lon, n_col = lax.axis_size("lon"), lax.axis_size("colat")
    core, mine = lon & 1, lon >> 1
    member = core * n_col + col
    other = 1 - panel
    lon_up, lon_down = lax.rem(lon + 1, n_lon), lax.rem(lon + n_lon - 1, n_lon)
    col_up, col_down = lax.rem(col + 1, n_col), lax.rem(col + n_col - 1, n_col)
    outer = lax.rem(lon + 2 * core - 1 + n_lon, n_lon)
    sends_rows = (lon < n_lon - 1, lon > 0)
    sends_cols = (col < n_col - 1, col > 0)
    col_edge = jnp.logical_or(col == 0, col == n_col - 1)

    sibling = (panel, lon + 1 - 2 * core, col)
    origin = core * GROUPS + mine

    def row_device(step, half):
        return (panel, 2 * mine + half, (col + step) & (n_col - 1))

    def target_device(target):
        return (other, 2 * (target & (GROUPS - 1)) + (target >> 3), col)

    def remote(src, dst, send, recv, device):
        return pltpu.make_async_remote_copy(
            src_ref=src, dst_ref=dst, send_sem=send, recv_sem=recv, device_id=device, device_id_type=MESH
        )

    frame = deep.reshape(2, FLAT * STRIDE, COL)
    copies = [
        pltpu.make_async_copy(src, dst, in_sem.at[i])
        for i, (src, dst) in enumerate(
            (
                (frac_hbm, frac_ref),
                (base_hbm, base_ref),
                (slots_hbm, slots_ref),
                (x_hbm.at[pl.ds(0, PART)], deep.at[0, pl.ds(0, PART), pl.ds(8, LON), :]),
                (x_hbm.at[pl.ds(PART, PART)], deep.at[0, pl.ds(PART, PART), pl.ds(8, LON), :]),
            )
        )
    ]
    for copy in copies:
        copy.start()

    barrier = pltpu.get_barrier_semaphore()
    for step in AROUND:
        for half in range(2):
            pl.semaphore_signal(barrier, inc=1, device_id=row_device(step, half), device_id_type=MESH)
    pl.semaphore_signal(barrier, inc=1, device_id=sibling, device_id_type=MESH)
    for target in range(TARGETS):
        pl.semaphore_signal(barrier, inc=1, device_id=target_device(target), device_id_type=MESH)
    pl.semaphore_signal(barrier, inc=1, device_id=(panel, outer, col), device_id_type=MESH)

    copies[0].wait()
    copies[1].wait()
    base = jnp.concatenate([base_ref[...], jnp.zeros((1, SLOTS - OUT), I32)], axis=1)
    base_row, base_col = lax.div(base, COL), lax.rem(base, COL)
    share = jnp.concatenate([frac_ref[...], jnp.zeros((2, SLOTS - OUT), F32)], axis=1)
    along, across = share[0:1, :], share[1:2, :]
    cells = iota((COL, SLOTS), 0)
    weight = jnp.where(cells == base_col, 1.0 - across, 0.0) + jnp.where(cells == base_col + 1, across, 0.0)
    weight_high, weight_low = split(weight)
    cols_mix[...] = weight
    mix[0:COL, :] = weight_high
    mix[COL : 2 * COL, :] = weight_high
    mix[2 * COL : 3 * COL, :] = weight_low
    cells = iota((LON, SLOTS), 0)
    weight = jnp.where(cells == base_row, 1.0 - along, 0.0) + jnp.where(cells == base_row + 1, along, 0.0)
    rows_mix[...] = weight
    place = (col * COL + iota((1, COL), 1)).astype(F32)
    scale = 1.0 / jnp.sin(math.pi / 4.0 + (place + 0.5) * (math.pi / 2.0 / (COL * n_col)))

    def message_tables():
        copies[2].wait()
        spot = iota((1, SLOTS), 1)
        sides = jnp.where(spot < SIDE, jnp.maximum(slots_ref[:, 0:SLOTS], slots_ref[:, SIDE : SIDE + SLOTS]) + 1, 0)
        digits = jnp.concatenate([lax.div(sides, COL), lax.rem(sides, COL), jnp.zeros((6, SLOTS), I32)], axis=0)
        source, target = iota((SLOTS, SLOTS), 0), iota((SLOTS, SLOTS), 1)
        layer = jnp.where(target >= LON, 1, 0) + jnp.where(target >= 2 * LON, 1, 0)
        order = jnp.logical_and(target < SIDE, source == HALO * (target - LON * layer) + layer)
        digits = dot(digits.astype(F32).astype(BF16), jnp.where(order, 1.0, 0.0).astype(BF16)).astype(I32)
        sides = digits[0:1, :] * COL + digits[1:2, :] - 1
        idx_out[0:1, :] = sides[:, 0:COL]
        idx_out[1:2, :] = sides[:, COL : 2 * COL]
        for h in range(HALO):
            at = 2 * SIDE + h * COL
            idx_out[2 + h : 3 + h, :] = jnp.maximum(
                slots_ref[:, at : at + COL], slots_ref[:, at + HALO * COL : at + HALO * COL + COL]
            )
        idx_out[5:8, :] = jnp.full((3, COL), -1, I32)

    def other_tables():
        zero_rows = jnp.zeros((8, COL), F32)
        for f in range(FLAT):
            for part in range(2):
                frame[part, f * STRIDE : f * STRIDE + 8, :] = zero_rows
                frame[part, f * STRIDE + 8 + LON : (f + 1) * STRIDE, :] = zero_rows
        for f in range(3 * SHELLS):
            emf[f * STRIDE : f * STRIDE + 8, :] = zero_rows
            emf[f * STRIDE + 8 + LON : (f + 1) * STRIDE, :] = zero_rows

        for half in range(2):
            turned[half, :, :] = jnp.zeros((COL, COL), F32)

        apart = iota((COL, COL), 0) - iota((COL, COL), 1)
        reach = jnp.abs(apart)
        first = jnp.where(reach == 1, 45.0, jnp.where(reach == 2, -9.0, jnp.where(reach == 3, 1.0, 0.0)))
        first = jnp.where(apart < 0, -first, first).astype(BF16)
        second = jnp.where(
            reach == 0, -490.0, jnp.where(reach == 1, 270.0, jnp.where(reach == 2, -27.0, jnp.where(reach == 3, 2.0, 0.0)))
        ).astype(BF16)
        for part in range(2):
            band[part * COL : (part + 1) * COL, 0:COL] = first
            band[part * COL : (part + 1) * COL, COL : 2 * COL] = second
        weight_high, weight_low = split(jnp.concatenate([rows_mix[...], jnp.zeros((COL - LON, SLOTS), F32)], axis=0))
        rows_split[0:COL, :] = weight_high
        rows_split[COL : 2 * COL, :] = weight_high
        rows_split[2 * COL : 3 * COL, :] = weight_low

    def load_split(part, pair):
        block = jnp.concatenate(
            [frame[part, pl.ds(pl.multiple_of((8 * pair + q) * STRIDE + 8, 8), LON), :] for q in range(8)], axis=0
        )
        return split(block)

    def interpolate(part, half):
        for pair in range(PART // 8):
            high, low = load_split(part, 2 * half + pair)
            value = dot(jnp.concatenate([high, low, high], axis=1), mix[...])
            value = jnp.sum(value.reshape(8, LON, SLOTS) * rows_mix[...][None], axis=1)
            blocks[part, half, 8 * pair : 8 * pair + 8, :] = value

    def send(part, half):
        for step in AROUND:
            a_copy(part, step, half).start()

        @pl.when(core != half)
        def _():
            s_copy(part, half).start()

        @pl.when(core == half)
        def _():
            table[part, member] = blocks[part, half]

    def lane_pass(part):
        def body(pair, carry):
            high, low = load_split(part, pair)
            both = jnp.concatenate([high, low], axis=1)
            lanes[pl.ds(pl.multiple_of(8 * LON * pair, 8), 8 * LON), :] = dot(both, band[...])
            return carry

        lax.fori_loop(0, FLAT // 8, body, 0)

    def cols_of(part):
        lane = iota((LON, COL), 1)
        for half in range(2):
            edge = jnp.zeros((LON, COL), F32)
            for g in range(FLAT // 2):
                at = (half * (FLAT // 2) + g) * STRIDE + 8
                moved = pltpu.roll(frame[part, at : at + LON, :], 8 * g + HALO, 1)
                edge = jnp.where(jnp.logical_and(lane >= 8 * g, lane < 8 * g + 2 * HALO), moved, edge)
            turned[half, :, 0:LON] = jnp.transpose(edge)
        for side in range(2):
            for j in range(HALO):
                first = (1 - side) * HALO + j
                for half in range(2):
                    col_own[part, side, j, half * (FLAT // 2) : (half + 1) * (FLAT // 2), :] = turned[
                        half, pl.ds(first, FLAT // 2, stride=8), :
                    ]
            col_out[part, side, 0] = jnp.where(
                iota((FLAT, COL), 1) < COL // 2, col_own[part, side, 0], pltpu.roll(col_own[part, side, 1], COL // 2, 1)
            )
            col_out[part, side, 1] = col_own[part, side, 2]

    def emf_pass(part):
        for r in range(SHELLS):
            def field(q):
                at = (q * SHELLS + r) * STRIDE + 8
                return frame[part, at : at + LON, :]

            m, b = [field(MR + i) for i in range(3)], [field(BR + i) for i in range(3)]
            for i, form in enumerate((cross_radial, cross_polar, cross_azimuthal)):
                at = (i * SHELLS + r) * STRIDE + 8
                emf[at : at + LON, :] = form(m, b)
        for i, at in ((0, FLAT), (2, FLAT + SHELLS)):
            block = jnp.concatenate(
                [emf[(i * SHELLS + r) * STRIDE + 8 : (i * SHELLS + r) * STRIDE + 8 + LON, :] for r in range(SHELLS)],
                axis=0,
            )
            high, low = split(block)
            lanes[at * LON : (at + SHELLS) * LON, 0:COL] = dot(
                jnp.concatenate([high, low], axis=1), band[:, 0:COL]
            )

    def main_pass(part, start, stop):
        def body(block, carry):
            here = pl.multiple_of(8 * block, 8)

            def near(f, apart):
                return frame[part, pl.ds(f * STRIDE + 8 + here + apart, 8), :]

            def near_emf(f, apart):
                return emf[pl.ds(f * STRIDE + 8 + here + apart, 8), :]

            def lane_first(f):
                return lanes[pl.ds(f * LON + here, 8), 0:COL]

            def lane_second(f):
                return lanes[pl.ds(f * LON + here, 8), COL : 2 * COL]

            def row_first(at):
                return 45.0 * (at[1] - at[-1]) - 9.0 * (at[2] - at[-2]) + (at[3] - at[-3])

            def row_second(at, centre):
                return (
                    270.0 * (at[1] + at[-1]) - 27.0 * (at[2] + at[-2]) + 2.0 * (at[3] + at[-3]) - 490.0 * centre
                )

            centre = [[near(q * SHELLS + r, 0) for r in range(SHELLS)] for q in range(QUANTITIES)]
            radial = [shell_first(x) for x in centre]
            radial_second = [None if q == S else shell_second(centre[q]) for q in range(QUANTITIES)]
            emf_centre = [[near_emf(i * SHELLS + r, 0) for r in range(SHELLS)] for i in range(3)]
            emf_radial = [None, shell_first(emf_centre[1]), shell_first(emf_centre[2])]
            for r in range(SHELLS):
                own = [centre[q][r] for q in range(QUANTITIES)]
                g, lap = [], []
                for q in range(QUANTITIES):
                    f = q * SHELLS + r
                    at = {d: near(f, d) for d in (-3, -2, -1, 1, 2, 3)}
                    g.append((radial[q][r], lane_first(f), scale * row_first(at)))
                    if q == S:
                        lap.append(None)
                    else:
                        lap.append(
                            radial_second[q][r] + lane_second(f) + (scale * scale) * row_second(at, own[q])
                        )
                m, b = own[MR:BR], own[BR:WARM]

                def advect(q):
                    return m[0] * g[q][0] + m[1] * g[q][1] + m[2] * g[q][2]

                div = g[MR][0] + g[MT][1] + g[MP][2]
                current = (g[BP][1] - g[BT][2], g[BR][2] - g[BP][0], g[BT][0] - g[BR][1])
                lorentz = (
                    current[1] * b[2] - current[2] * b[1],
                    current[2] * b[0] - current[0] * b[2],
                    current[0] * b[1] - current[1] * b[0],
                )
                grow, thin = jnp.exp(own[WARM]), jnp.exp(-own[S])
                emf_rows = {}
                for i in (0, 1):
                    f = i * SHELLS + r
                    emf_rows[i] = scale * row_first({d: near_emf(f, d) for d in (-3, -2, -1, 1, 2, 3)})
                turn = (
                    lane_first(FLAT + SHELLS + r) - emf_rows[1],
                    emf_rows[0] - emf_radial[2][r],
                    emf_radial[1][r] - lane_first(FLAT + r),
                )
                result = [-advect(S) - div]
                for i in range(3):
                    result.append(
                        -advect(MR + i) - grow * (g[S][i] + g[WARM][i]) + thin * lorentz[i] + SPREAD * lap[MR + i]
                    )
                for i in range(3):
                    result.append(turn[i] + SPREAD * lap[BR + i])
                result.append(-advect(WARM) - (2.0 / 3.0) * div + SPREAD * lap[WARM])
                for q in range(QUANTITIES):
                    f = q * SHELLS + r
                    value = own[q] + (TIME_STEP / 60.0) * result[q]
                    if part == 0:
                        frame[1, pl.ds(f * STRIDE + 8 + here, 8), :] = value
                    else:
                        start = frame[0, pl.ds(f * STRIDE + 8 + here, 8), :]
                        out_ref[pl.ds(f * LON + here, 8), :] = 0.5 * (start + value)
            return carry

        lax.fori_loop(start, stop, body, 0)

    def rows_of(part):
        for h in range(HALO):
            row_out[part, 0, h] = frame[part, pl.ds(8 + h, FLAT, stride=STRIDE), :]
            row_out[part, 1, h] = frame[part, pl.ds(8 + LON - HALO + h, FLAT, stride=STRIDE), :]

    def prepare_picks():
        for tile in range(2 * TILES):
            if tile < TARGETS:
                slot = idx_in[tile, 0:1, :]
            elif tile < TARGETS + 2:
                first = (tile - TARGETS) * GROUPS
                slot = idx_in[first, 1:2, :]
                for q in range(1, GROUPS):
                    slot = jnp.maximum(slot, pltpu.roll(idx_in[first + q], SPARE * q, 1)[1:2, :])
            else:
                side, h = divmod(tile - TARGETS - 2, HALO)
                slot = idx_in[side * (TARGETS - 1), 2 + h : 3 + h, :]
            slot = slot - mine * (GROUP * OUT)
            who = jnp.zeros_like(slot)
            for q in range(1, GROUP):
                who = who + jnp.where(slot >= q * OUT, 1, 0)
            cell = slot - who * OUT
            who = jnp.where(jnp.logical_and(slot >= 0, slot < GROUP * OUT), who, -1)
            at = (tile % 2) * COL
            owner[tile // 2, :, at : at + COL] = jnp.broadcast_to(who, (8, COL))
            hot = jnp.where(iota((SLOTS, COL), 0) == cell, 1.0, 0.0).astype(BF16)
            onehot[tile // 2, :, at : at + COL] = hot

    def table_split(part):
        high, low = split(table[part].reshape(GROUP * PART, SLOTS))
        return jnp.concatenate([high, low], axis=0)

    def product(both, tile):
        return dot(both, onehot[tile])

    def chosen(value, tile):
        value = value[0 : GROUP * PART] + value[GROUP * PART :]
        who = jnp.broadcast_to(owner[tile, 0:1, :], (PART, SLOTS))
        total = jnp.zeros((PART, SLOTS), F32)
        for q in range(GROUP):
            total = jnp.where(who == q, value[q * PART : (q + 1) * PART, :], total)
        return total[:, 0:COL], total[:, COL : 2 * COL]

    def fold(rests):
        turn = (lax.div(iota((8, COL), 1), SPARE) - iota((8, COL), 0)) & 7
        for half, rest in enumerate(rests):
            for s in range(FOLD):
                total = jnp.zeros((8, COL), F32)
                for d in range(8):
                    moved = rest[8 * s : 8 * s + 8, :]
                    if d:
                        moved = pltpu.roll(pltpu.roll(moved, SPARE * d, 1), 8 - d, 0)
                    total = jnp.where(turn == d, moved, total)
                rest_rows[half, s] = total

    def pick_all(part, both):
        sides = [(step + mine) & (TARGETS // 2 - 1) for step in range(TARGETS // 2)]
        extra = list(range(TARGETS // 2 + 1, TILES))
        ends, value = [], product(both, extra[0])
        for tile, after in zip(extra, extra[1:] + [None]):
            now = value
            if after is not None:
                value = product(both, after)
            ends += chosen(now, tile)
        for side in range(2):
            for h in range(HALO):
                picked_rows[part, side, h] = ends[side * HALO + h]
        for side in range(2):
            l_copy(part, side).start()

        @pl.when(col_edge)
        def _():
            now, value = product(both, TARGETS // 2), product(both, sides[0])
            fold(chosen(now, TARGETS // 2))
            for step, tile in enumerate(sides):
                now = value
                if step + 1 < len(sides):
                    value = product(both, sides[step + 1])
                for i, end in enumerate(chosen(now, tile)):
                    target = 2 * tile + i
                    picked[part, target, 0:PART, :] = end
                    for s in range(FOLD):
                        picked[part, target, PART + s : PART + s + 1, :] = rest_rows[
                            tile >> 2, s, pl.ds(target & (GROUPS - 1), 1), :
                        ]
                for i in range(2):
                    b_copy(part, 2 * tile + i).start()

    def corrections(part, side, along_lanes):
        halo_ref, own_ref, add_ref = (col_halo, col_own, col_add) if along_lanes else (row_halo, row_out, row_add)

        def scaled(value, power):
            for _ in range(0 if along_lanes else power):
                value = scale * value
            return value

        halo = [[halo_ref[side, h, q * SHELLS : (q + 1) * SHELLS, :] for q in range(QUANTITIES)] for h in range(HALO)]
        form = cross_azimuthal if along_lanes else cross_polar
        halo_emf = [(cross_radial(x[MR:BR], x[BR:WARM]), form(x[MR:BR], x[BR:WARM])) for x in halo]
        sign = -1.0 if side == 0 else 1.0
        firsts, seconds = (45.0 * sign, -9.0 * sign, sign), (270.0, -27.0, 2.0)
        for j in range(HALO):
            own = [own_ref[part, side, j, q * SHELLS : (q + 1) * SHELLS, :] for q in range(QUANTITIES)]

            def total(weights, of):
                result = None
                for m in (1, 2, 3):
                    h = j + 3 - m if side == 0 else m - 3 + j
                    if 0 <= h < HALO:
                        term = weights[m - 1] * of(h)
                        result = term if result is None else result + term
                return result

            d = [scaled(total(firsts, lambda h, q=q: halo[h][q]), 1) for q in range(QUANTITIES)]
            lap = [
                None if q == S else scaled(total(seconds, lambda h, q=q: halo[h][q]), 2) for q in range(QUANTITIES)
            ]
            radial = scaled(total(firsts, lambda h: halo_emf[h][0]), 1)
            second = scaled(total(firsts, lambda h: halo_emf[h][1]), 1)
            result = edge_rates(own, d, lap, second, radial, along_lanes)
            for q in range(QUANTITIES):
                add_ref[side, j, q * SHELLS : (q + 1) * SHELLS, :] = (TIME_STEP / 60.0 / (1 + part)) * result[q]

    def contribute(side, along_lanes):
        add_ref = col_add if along_lanes else row_add
        value = jnp.concatenate([add_ref[side, j] for j in range(HALO)], axis=0)
        if along_lanes:
            value = jnp.where(iota((HALO * FLAT, COL), 1) < LON, value, 0.0)
        high, low = split(value)
        value = dot(jnp.concatenate([high, low, high], axis=1), rows_split[...] if along_lanes else mix[...])
        total = jnp.zeros((FLAT, SLOTS), F32)
        for j in range(HALO):
            if along_lanes:
                at = j if side == 0 else COL - HALO + j
                weight = cols_mix[at : at + 1, :]
            else:
                at = j if side == 0 else LON - HALO + j
                weight = rows_mix[at : at + 1, :]
            total = total + weight * value[j * FLAT : (j + 1) * FLAT, :]
        for half in range(2):
            blocks[1, half] = blocks[1, half] + total[half * PART : (half + 1) * PART, :]

    def apply_edges():
        for side in range(2):
            for j in range(HALO):
                rows = pl.ds(8 + (j if side == 0 else LON - HALO + j), FLAT, stride=STRIDE)
                frame[1, rows, :] = frame[1, rows, :] + row_add[side, j]
        turn_edges(col_add, turned)
        for half in range(2):
            edge = jnp.transpose(turned[half])[0:LON, :]
            for g in range(FLAT // 2):
                at = (half * (FLAT // 2) + g) * STRIDE + 8
                frame[1, at : at + LON, :] = frame[1, at : at + LON, :] + field_edge(edge, g)

    def a_copy(part, step, half):
        return remote(
            blocks.at[part, half], table.at[part, member], a_send.at[part, half, step], a_recv.at[part, member],
            row_device(step, half),
        )

    def s_copy(part, half):
        return remote(
            blocks.at[part, half], table.at[part, member], s_send.at[part], a_recv.at[part, member], sibling
        )

    def a_arrival(part, step):
        there = (member + step) & (GROUP - 1)
        return remote(blocks.at[part, 0], table.at[part, there], s_send.at[part], a_recv.at[part, there], sibling)

    def b_copy(part, target):
        return remote(
            picked.at[part, target], got_cols.at[part, origin], b_send.at[part, target], b_recv.at[part, origin],
            target_device(target),
        )

    def b_arrival(part, source):
        return remote(
            picked.at[part, 0], got_cols.at[part, source], b_send.at[part, 0], b_recv.at[part, source],
            (other, lon, col),
        )

    def l_copy(part, side):
        return remote(
            picked_rows.at[part, side], got_rows.at[part, origin], l_send.at[part, side], l_recv.at[part, origin],
            target_device(side * (TARGETS - 1)),
        )

    def l_arrival(part, source):
        return remote(
            picked_rows.at[part, 0], got_rows.at[part, source], l_send.at[part, 0], l_recv.at[part, source],
            (other, lon, col),
        )

    def row_copy(part, side):
        return remote(
            row_out.at[part, 1 - side], row_in.at[part, side], r_send.at[part, side], r_recv.at[part, side],
            (panel, lon_up if side == 0 else lon_down, col),
        )

    def col_copy(part, side):
        return remote(
            col_out.at[part, 1 - side], col_in.at[part, side], c_send.at[part, side], c_recv.at[part, side],
            (panel, lon, col_up if side == 0 else col_down),
        )

    def idx_copy(target):
        return remote(
            idx_out, idx_in.at[origin], idx_send.at[target], idx_recv.at[origin], target_device(target)
        )

    def idx_arrival(source):
        return remote(idx_out, idx_in.at[source], idx_send.at[0], idx_recv.at[source], (other, lon, col))

    def inner_sides(part):
        for side in range(2):
            @pl.when(lon != (0 if side == 0 else n_lon - 1))
            def _():
                row_copy(part, side).wait_recv()
                row_halo[side] = row_in[part, side]
                corrections(part, side, False)
                if part == 0:
                    contribute(side, False)

            @pl.when(col != (0 if side == 0 else n_col - 1))
            def _():
                col_copy(part, side).wait_recv()
                pair = col_in[part, side, 0]
                col_halo[side, 0] = pair
                col_halo[side, 1] = pltpu.roll(pair, COL // 2, 1)
                col_halo[side, 2] = col_in[part, side, 1]
                corrections(part, side, True)
                if part == 0:
                    contribute(side, True)

    def outer_sides(part):
        for side in range(2):

            @pl.when(col == (0 if side == 0 else n_col - 1))
            def _():
                for source in range(TARGETS):
                    b_arrival(part, source).wait_recv()
                for half in range(2):
                    total = got_cols[part, half * GROUPS]
                    for group in range(1, GROUPS):
                        total = total + got_cols[part, half * GROUPS + group]
                    main = total[0:PART]
                    rows = slice(half * PART, (half + 1) * PART)
                    col_halo[side, 0, rows, :] = main
                    col_halo[side, 1, rows, :] = pltpu.roll(main, COL - LON, 1)
                    main = pltpu.roll(main, COL - 2 * LON, 1)
                    row, lane = iota((8, COL), 0), iota((8, COL), 1)
                    for s in range(FOLD):
                        value = main[8 * s : 8 * s + 8, :]
                        rest = jnp.broadcast_to(total[PART + s : PART + s + 1], (8, COL))
                        for q in range(8):
                            moved = pltpu.roll(rest, (2 * COL - 2 * LON - SPARE * q) % COL, 1)
                            value = jnp.where(jnp.logical_and(row == q, lane >= COL - 2 * LON), moved, value)
                        at = half * PART + 8 * s
                        col_halo[side, 2, at : at + 8, :] = value
                corrections(part, side, True)
                if part == 0:
                    contribute(side, True)

            @pl.when(lon == (0 if side == 0 else n_lon - 1))
            def _():
                for source in range(TARGETS):
                    l_arrival(part, source).wait_recv()
                for half in range(2):
                    total = got_rows[part, half * GROUPS]
                    for group in range(1, GROUPS):
                        total = total + got_rows[part, half * GROUPS + group]
                    row_halo[side, :, half * PART : (half + 1) * PART, :] = total
                corrections(part, side, False)
                if part == 0:
                    contribute(side, False)

    for part in range(2):
        if part == 0:
            message_tables()
            copies[3].wait()
            interpolate(0, 0)
            pl.semaphore_wait(barrier, 2 * len(AROUND) + 2 + TARGETS)
            for target in range(TARGETS):
                idx_copy(target).start()
            send(0, 0)
            copies[4].wait()
            interpolate(0, 1)
            send(0, 1)
            other_tables()
        else:
            send(1, 0)
            send(1, 1)
            apply_edges()
        rows_of(part)
        for side in range(2):

            @pl.when(sends_rows[side])
            def _():
                row_copy(part, side).start()

        cols_of(part)
        for side in range(2):

            @pl.when(sends_cols[side])
            def _():
                col_copy(part, side).start()

        lane_pass(part)
        emf_pass(part)
        if part == 0:
            for source in range(TARGETS):
                idx_arrival(source).wait_recv()
            prepare_picks()
        for step in range(1, GROUP):
            a_arrival(part, step).wait_recv()
        both = table_split(part)
        pick_all(part, both)
        main_pass(part, 0, 6)
        if part == 0:
            interpolate(1, 0)
            interpolate(1, 1)
        inner_sides(part)
        outer_sides(part)

    for target in range(TARGETS):
        idx_copy(target).wait_send()
    for part in range(2):
        for half in range(2):
            for step in AROUND:
                a_copy(part, step, half).wait_send()
        s_copy(part, 0).wait_send()
        for side in range(2):
            l_copy(part, side).wait_send()

            @pl.when(sends_rows[side])
            def _():
                row_copy(part, side).wait_send()

            @pl.when(sends_cols[side])
            def _():
                col_copy(part, side).wait_send()


        @pl.when(col_edge)
        def _():
            for target in range(TARGETS):
                b_copy(part, target).wait_send()


def shards(state, send_base, send_frac, recv_slots):
    rows = FLAT * LON
    dma = pltpu.SemaphoreType.DMA
    vmem = pltpu.VMEM
    scratch = [
        vmem((2, FLAT, STRIDE, COL), F32),
        vmem((1, OUT), I32),
        vmem((2, OUT), F32),
        vmem((1, recv_slots.shape[-1]), I32),
        vmem((3 * SHELLS * STRIDE, COL), F32),
        vmem(((FLAT + 2 * SHELLS) * LON, 2 * COL), F32),
        vmem((3 * COL, SLOTS), BF16),
        vmem((COL, SLOTS), F32),
        vmem((LON, SLOTS), F32),
        vmem((3 * COL, SLOTS), BF16),
        vmem((2 * COL, 2 * COL), BF16),
        vmem((TILES, SLOTS, 2 * COL), BF16),
        vmem((TILES, 8, 2 * COL), I32),
        vmem((2, COL, COL), F32),
        vmem((2, 2, PART, SLOTS), F32),
        vmem((2, GROUP, PART, SLOTS), F32),
        vmem((8, COL), I32),
        vmem((TARGETS, 8, COL), I32),
        vmem((2, FOLD, 8, COL), F32),
        vmem((2, TARGETS, PART + FOLD, COL), F32),
        vmem((2, 2, HALO, PART, COL), F32),
        vmem((2, TARGETS, PART + FOLD, COL), F32),
        vmem((2, TARGETS, HALO, PART, COL), F32),
        vmem((2, 2, HALO, FLAT, COL), F32),
        vmem((2, 2, HALO, FLAT, COL), F32),
        vmem((2, 2, HALO, FLAT, COL), F32),
        vmem((2, 2, 2, FLAT, COL), F32),
        vmem((2, 2, 2, FLAT, COL), F32),
        vmem((2, HALO, FLAT, COL), F32),
        vmem((2, HALO, FLAT, COL), F32),
        dma((5,)),
        dma((TARGETS,)),
        dma((TARGETS,)),
        dma((2, 2, RING)),
        dma((2, GROUP)),
        dma((2,)),
        dma((2, TARGETS)),
        dma((2, TARGETS)),
        dma((2, 2)),
        dma((2, TARGETS)),
        dma((2, 2)),
        dma((2, 2)),
        dma((2, 2)),
        dma((2, 2)),
    ]
    edges = jax.ShapeDtypeStruct((2, HALO, FLAT, COL), F32)
    value, row_add, col_add = pl.pallas_call(
        kernel,
        out_shape=(jax.ShapeDtypeStruct((rows, COL), F32), edges, edges),
        in_specs=[pl.BlockSpec(memory_space=pltpu.HBM)] * 4,
        out_specs=[pl.BlockSpec(memory_space=pltpu.VMEM)] * 3,
        scratch_shapes=scratch,
        compiler_params=pltpu.CompilerParams(
            collective_id=0, has_side_effects=True, vmem_limit_bytes=40 * 1024 * 1024
        ),
    )(*(
        pltpu.with_memory_space_constraint(x, pltpu.HBM)
        for x in (state.reshape(FLAT, LON, COL), send_base[0], send_frac[0, 0], recv_slots[0])
    ))
    result = pl.pallas_call(
        closing,
        out_shape=jax.ShapeDtypeStruct((rows, COL), F32),
        in_specs=[pl.BlockSpec(memory_space=pltpu.VMEM)] * 3,
        out_specs=pl.BlockSpec(memory_space=pltpu.HBM),
        scratch_shapes=[vmem((2, COL, COL), F32), vmem((rows, COL), F32), dma((4,))],
        compiler_params=pltpu.CompilerParams(vmem_limit_bytes=16 * 1024 * 1024),
    )(value, row_add, col_add)
    return result.reshape(state.shape)


def solution(mesh):
    placed = (
        P("panel", None, None, "lon", "colat"),
        P("panel", ("lon", "colat"), None),
        P("panel", ("lon", "colat"), None, None),
        P("panel", ("lon", "colat"), None),
    )
    return jax.shard_map(
        shards,
        mesh=mesh,
        in_specs=placed,
        out_specs=P("panel", None, None, "lon", "colat"),
        check_vma=False,
    )
```

```python
import math

import jax
import jax.numpy as jnp
from jax import lax
from jax.experimental import pallas as pl
from jax.experimental.pallas import tpu as pltpu
from jax.sharding import PartitionSpec as P

MESH = pl.DeviceIdType.MESH
F32, BF16, I32 = jnp.float32, jnp.bfloat16, jnp.int32

QUANTITIES = 8
SHELLS = 4
FLAT = QUANTITIES * SHELLS
LON = 48
COL = 128
HALO = 3
OUT = 240
SIDE = HALO * LON
SLOTS = 256
GROUP = 8
GROUPS = 8
AROUND = (1, 3, 2)
SPARE = SIDE - COL
PART = FLAT // 2
TARGETS = 2 * GROUPS
TILES = 12
RING = 4
FOLD = PART // 8
STRIDE = LON + 16
TIME_STEP = 0.25
SPREAD = 0.1 / 3.0
S, MR, MT, MP, BR, BT, BP, WARM = range(QUANTITIES)


def dot(left, right):
    return jnp.dot(left, right, preferred_element_type=F32)


def split(value):
    high = value.astype(BF16)
    return high, (value - high.astype(F32)).astype(BF16)


def iota(shape, dim):
    return lax.broadcasted_iota(I32, shape, dim)


def cross_radial(m, b):
    return m[1] * b[2] - m[2] * b[1]


def cross_polar(m, b):
    return m[2] * b[0] - m[0] * b[2]


def cross_azimuthal(m, b):
    return m[0] * b[1] - m[1] * b[0]


def edge_rates(own, d, lap, emf_first, emf_second, along_lanes):
    grow, thin = jnp.exp(own[WARM]), jnp.exp(-own[S])
    b = own[BR:WARM]
    if along_lanes:
        vel, out = own[MT], MT
        lorentz = (d[BR] * b[1], -d[BR] * b[0] - d[BP] * b[2], d[BP] * b[1])
        turn = (emf_first, None, -emf_second)
    else:
        vel, out = own[MP], MP
        lorentz = (d[BR] * b[2], d[BT] * b[2], -d[BT] * b[1] - d[BR] * b[0])
        turn = (-emf_first, emf_second, None)
    result = [-vel * d[S] - d[out]]
    for i in range(3):
        rate = -vel * d[MR + i] + thin * lorentz[i] + SPREAD * lap[MR + i]
        if MR + i == out:
            rate = rate - grow * (d[S] + d[WARM])
        result.append(rate)
    for i in range(3):
        rate = SPREAD * lap[BR + i]
        result.append(rate if turn[i] is None else rate + turn[i])
    result.append(-vel * d[WARM] - (2.0 / 3.0) * d[out] + SPREAD * lap[WARM])
    return result


def shell_first(x):
    a, b = 8.0 * (x[3] - x[0]), 45.0
    return (
        b * (x[1] - x[0]) - 9.0 * (x[2] - x[0]) + (x[3] - x[0]),
        b * (x[2] - x[0]) - a,
        b * (x[3] - x[1]) - a,
        b * (x[3] - x[2]) - 9.0 * (x[3] - x[1]) + (x[3] - x[0]),
    )


def shell_second(x):
    return (
        2.0 * x[3] - 27.0 * x[2] + 270.0 * x[1] - 245.0 * x[0],
        245.0 * x[0] - 490.0 * x[1] + 270.0 * x[2] - 25.0 * x[3],
        245.0 * x[3] - 490.0 * x[2] + 270.0 * x[1] - 25.0 * x[0],
        2.0 * x[0] - 27.0 * x[1] + 270.0 * x[2] - 245.0 * x[3],
    )


def turn_edges(col_add, turned):
    for side in range(2):
        for j in range(HALO):
            for half in range(2):
                turned[half, pl.ds((1 - side) * HALO + j, FLAT // 2, stride=8), :] = col_add[
                    side, j, half * (FLAT // 2) : (half + 1) * (FLAT // 2), :
                ]


def field_edge(edge, g):
    lane = iota((LON, COL), 1)
    border = jnp.logical_or(lane < HALO, lane >= COL - HALO)
    return jnp.where(border, pltpu.roll(edge, COL - 8 * g - HALO, 1), 0.0)


def closing(value_ref, row_add, col_add, out_hbm, turned, ready, sem):
    turn_edges(col_add, turned)
    copies = []
    for half in range(2):
        edge = jnp.transpose(turned[half])[0:LON, :]
        for chunk in range(2):
            first = half * (FLAT // 2) + 8 * chunk
            for q in range(8):
                at = (first + q) * LON
                ready[at : at + LON, :] = value_ref[at : at + LON, :] + field_edge(edge, 8 * chunk + q)
            for side in range(2):
                for j in range(HALO):
                    rows = pl.ds(first * LON + (j if side == 0 else LON - HALO + j), 8, stride=LON)
                    ready[rows, :] = ready[rows, :] + row_add[side, j, first : first + 8, :]
            rows = pl.ds(first * LON, 8 * LON)
            copy = pltpu.make_async_copy(ready.at[rows, :], out_hbm.at[rows, :], sem.at[2 * half + chunk])
            copy.start()
            copies.append(copy)
    for copy in copies:
        copy.wait()


def kernel(
    x_hbm, base_hbm, frac_hbm, slots_hbm, out_ref, row_add, col_add,
    deep, base_ref, frac_ref, slots_ref, emf, lanes, mix, cols_mix, rows_mix, rows_split, band, onehot, owner, turned,
    blocks, table, idx_out, idx_in, rest_rows, picked, picked_rows, got_cols, got_rows, row_out, row_in, col_own, col_out, col_in,
    row_halo, col_halo,
    in_sem, idx_send, idx_recv, a_send, a_recv, s_send, b_send, b_recv, l_send, l_recv, r_send, r_recv, c_send, c_recv,
):
    panel, lon, col = lax.axis_index("panel"), lax.axis_index("lon"), lax.axis_index("colat")
    n_lon, n_col = lax.axis_size("lon"), lax.axis_size("colat")
    core, mine = lon & 1, lon >> 1
    member = core * n_col + col
    other = 1 - panel
    lon_up, lon_down = lax.rem(lon + 1, n_lon), lax.rem(lon + n_lon - 1, n_lon)
    col_up, col_down = lax.rem(col + 1, n_col), lax.rem(col + n_col - 1, n_col)
    outer = lax.rem(lon + 2 * core - 1 + n_lon, n_lon)
    sends_rows = (lon < n_lon - 1, lon > 0)
    sends_cols = (col < n_col - 1, col > 0)
    col_edge = jnp.logical_or(col == 0, col == n_col - 1)

    sibling = (panel, lon + 1 - 2 * core, col)
    origin = core * GROUPS + mine

    def row_device(step, half):
        return (panel, 2 * mine + half, (col + step) & (n_col - 1))

    def target_device(target):
        return (other, 2 * (target & (GROUPS - 1)) + (target >> 3), col)

    def remote(src, dst, send, recv, device):
        return pltpu.make_async_remote_copy(
            src_ref=src, dst_ref=dst, send_sem=send, recv_sem=recv, device_id=device, device_id_type=MESH
        )

    frame = deep.reshape(2, FLAT * STRIDE, COL)
    copies = [
        pltpu.make_async_copy(src, dst, in_sem.at[i])
        for i, (src, dst) in enumerate(
            (
                (frac_hbm, frac_ref),
                (base_hbm, base_ref),
                (slots_hbm, slots_ref),
                (x_hbm.at[pl.ds(0, PART)], deep.at[0, pl.ds(0, PART), pl.ds(8, LON), :]),
                (x_hbm.at[pl.ds(PART, PART)], deep.at[0, pl.ds(PART, PART), pl.ds(8, LON), :]),
            )
        )
    ]
    for copy in copies:
        copy.start()

    barrier = pltpu.get_barrier_semaphore()
    for step in AROUND:
        for half in range(2):
            pl.semaphore_signal(barrier, inc=1, device_id=row_device(step, half), device_id_type=MESH)
    pl.semaphore_signal(barrier, inc=1, device_id=sibling, device_id_type=MESH)
    for target in range(TARGETS):
        pl.semaphore_signal(barrier, inc=1, device_id=target_device(target), device_id_type=MESH)
    pl.semaphore_signal(barrier, inc=1, device_id=(panel, outer, col), device_id_type=MESH)

    copies[0].wait()
    copies[1].wait()
    base = jnp.concatenate([base_ref[...], jnp.zeros((1, SLOTS - OUT), I32)], axis=1)
    base_row, base_col = lax.div(base, COL), lax.rem(base, COL)
    share = jnp.concatenate([frac_ref[...], jnp.zeros((2, SLOTS - OUT), F32)], axis=1)
    along, across = share[0:1, :], share[1:2, :]
    cells = iota((COL, SLOTS), 0)
    weight = jnp.where(cells == base_col, 1.0 - across, 0.0) + jnp.where(cells == base_col + 1, across, 0.0)
    weight_high, weight_low = split(weight)
    cols_mix[...] = weight
    mix[0:COL, :] = weight_high
    mix[COL : 2 * COL, :] = weight_high
    mix[2 * COL : 3 * COL, :] = weight_low
    cells = iota((LON, SLOTS), 0)
    weight = jnp.where(cells == base_row, 1.0 - along, 0.0) + jnp.where(cells == base_row + 1, along, 0.0)
    rows_mix[...] = weight
    place = (col * COL + iota((1, COL), 1)).astype(F32)
    scale = 1.0 / jnp.sin(math.pi / 4.0 + (place + 0.5) * (math.pi / 2.0 / (COL * n_col)))

    def message_tables():
        copies[2].wait()
        spot = iota((1, SLOTS), 1)
        sides = jnp.where(spot < SIDE, jnp.maximum(slots_ref[:, 0:SLOTS], slots_ref[:, SIDE : SIDE + SLOTS]) + 1, 0)
        digits = jnp.concatenate([lax.div(sides, COL), lax.rem(sides, COL), jnp.zeros((6, SLOTS), I32)], axis=0)
        source, target = iota((SLOTS, SLOTS), 0), iota((SLOTS, SLOTS), 1)
        layer = jnp.where(target >= LON, 1, 0) + jnp.where(target >= 2 * LON, 1, 0)
        order = jnp.logical_and(target < SIDE, source == HALO * (target - LON * layer) + layer)
        digits = dot(digits.astype(F32).astype(BF16), jnp.where(order, 1.0, 0.0).astype(BF16)).astype(I32)
        sides = digits[0:1, :] * COL + digits[1:2, :] - 1
        idx_out[0:1, :] = sides[:, 0:COL]
        idx_out[1:2, :] = sides[:, COL : 2 * COL]
        for h in range(HALO):
            at = 2 * SIDE + h * COL
            idx_out[2 + h : 3 + h, :] = jnp.maximum(
                slots_ref[:, at : at + COL], slots_ref[:, at + HALO * COL : at + HALO * COL + COL]
            )
        idx_out[5:8, :] = jnp.full((3, COL), -1, I32)

    def other_tables():
        zero_rows = jnp.zeros((8, COL), F32)
        for f in range(FLAT):
            for part in range(2):
                frame[part, f * STRIDE : f * STRIDE + 8, :] = zero_rows
                frame[part, f * STRIDE + 8 + LON : (f + 1) * STRIDE, :] = zero_rows
        for f in range(3 * SHELLS):
            emf[f * STRIDE : f * STRIDE + 8, :] = zero_rows
            emf[f * STRIDE + 8 + LON : (f + 1) * STRIDE, :] = zero_rows

        for half in range(2):
            turned[half, :, :] = jnp.zeros((COL, COL), F32)

        apart = iota((COL, COL), 0) - iota((COL, COL), 1)
        reach = jnp.abs(apart)
        first = jnp.where(reach == 1, 45.0, jnp.where(reach == 2, -9.0, jnp.where(reach == 3, 1.0, 0.0)))
        first = jnp.where(apart < 0, -first, first).astype(BF16)
        second = jnp.where(
            reach == 0, -490.0, jnp.where(reach == 1, 270.0, jnp.where(reach == 2, -27.0, jnp.where(reach == 3, 2.0, 0.0)))
        ).astype(BF16)
        for part in range(2):
            band[part * COL : (part + 1) * COL, 0:COL] = first
            band[part * COL : (part + 1) * COL, COL : 2 * COL] = second
        weight_high, weight_low = split(jnp.concatenate([rows_mix[...], jnp.zeros((COL - LON, SLOTS), F32)], axis=0))
        rows_split[0:COL, :] = weight_high
        rows_split[COL : 2 * COL, :] = weight_high
        rows_split[2 * COL : 3 * COL, :] = weight_low

    def load_split(part, pair):
        block = jnp.concatenate(
            [frame[part, pl.ds(pl.multiple_of((8 * pair + q) * STRIDE + 8, 8), LON), :] for q in range(8)], axis=0
        )
        return split(block)

    def interpolate(part, half):
        for pair in range(PART // 8):
            high, low = load_split(part, 2 * half + pair)
            value = dot(jnp.concatenate([high, low, high], axis=1), mix[...])
            value = jnp.sum(value.reshape(8, LON, SLOTS) * rows_mix[...][None], axis=1)
            blocks[part, half, 8 * pair : 8 * pair + 8, :] = value

    def send(part, half):
        for step in AROUND:
            a_copy(part, step, half).start()

        @pl.when(core != half)
        def _():
            s_copy(part, half).start()

        @pl.when(core == half)
        def _():
            table[part, member] = blocks[part, half]

    def lane_pass(part):
        def body(pair, carry):
            high, low = load_split(part, pair)
            both = jnp.concatenate([high, low], axis=1)
            lanes[pl.ds(pl.multiple_of(8 * LON * pair, 8), 8 * LON), :] = dot(both, band[...])
            return carry

        lax.fori_loop(0, FLAT // 8, body, 0)

    def cols_of(part):
        lane = iota((LON, COL), 1)
        for half in range(2):
            edge = jnp.zeros((LON, COL), F32)
            for g in range(FLAT // 2):
                at = (half * (FLAT // 2) + g) * STRIDE + 8
                moved = pltpu.roll(frame[part, at : at + LON, :], 8 * g + HALO, 1)
                edge = jnp.where(jnp.logical_and(lane >= 8 * g, lane < 8 * g + 2 * HALO), moved, edge)
            turned[half, :, 0:LON] = jnp.transpose(edge)
        for side in range(2):
            for j in range(HALO):
                first = (1 - side) * HALO + j
                for half in range(2):
                    col_own[part, side, j, half * (FLAT // 2) : (half + 1) * (FLAT // 2), :] = turned[
                        half, pl.ds(first, FLAT // 2, stride=8), :
                    ]
            col_out[part, side, 0] = jnp.where(
                iota((FLAT, COL), 1) < COL // 2, col_own[part, side, 0], pltpu.roll(col_own[part, side, 1], COL // 2, 1)
            )
            col_out[part, side, 1] = col_own[part, side, 2]

    def emf_pass(part):
        for r in range(SHELLS):
            def field(q):
                at = (q * SHELLS + r) * STRIDE + 8
                return frame[part, at : at + LON, :]

            m, b = [field(MR + i) for i in range(3)], [field(BR + i) for i in range(3)]
            for i, form in enumerate((cross_radial, cross_polar, cross_azimuthal)):
                at = (i * SHELLS + r) * STRIDE + 8
                emf[at : at + LON, :] = form(m, b)
        for i, at in ((0, FLAT), (2, FLAT + SHELLS)):
            block = jnp.concatenate(
                [emf[(i * SHELLS + r) * STRIDE + 8 : (i * SHELLS + r) * STRIDE + 8 + LON, :] for r in range(SHELLS)],
                axis=0,
            )
            high, low = split(block)
            lanes[at * LON : (at + SHELLS) * LON, 0:COL] = dot(
                jnp.concatenate([high, low], axis=1), band[:, 0:COL]
            )

    def main_pass(part, start, stop):
        def body(block, carry):
            here = pl.multiple_of(8 * block, 8)

            def near(f, apart):
                return frame[part, pl.ds(f * STRIDE + 8 + here + apart, 8), :]

            def near_emf(f, apart):
                return emf[pl.ds(f * STRIDE + 8 + here + apart, 8), :]

            def lane_first(f):
                return lanes[pl.ds(f * LON + here, 8), 0:COL]

            def lane_second(f):
                return lanes[pl.ds(f * LON + here, 8), COL : 2 * COL]

            def row_first(at):
                return 45.0 * (at[1] - at[-1]) - 9.0 * (at[2] - at[-2]) + (at[3] - at[-3])

            def row_second(at, centre):
                return (
                    270.0 * (at[1] + at[-1]) - 27.0 * (at[2] + at[-2]) + 2.0 * (at[3] + at[-3]) - 490.0 * centre
                )

            centre = [[near(q * SHELLS + r, 0) for r in range(SHELLS)] for q in range(QUANTITIES)]
            radial = [shell_first(x) for x in centre]
            radial_second = [None if q == S else shell_second(centre[q]) for q in range(QUANTITIES)]
            emf_centre = [[near_emf(i * SHELLS + r, 0) for r in range(SHELLS)] for i in range(3)]
            emf_radial = [None, shell_first(emf_centre[1]), shell_first(emf_centre[2])]
            for r in range(SHELLS):
                own = [centre[q][r] for q in range(QUANTITIES)]
                g, lap = [], []
                for q in range(QUANTITIES):
                    f = q * SHELLS + r
                    at = {d: near(f, d) for d in (-3, -2, -1, 1, 2, 3)}
                    g.append((radial[q][r], lane_first(f), scale * row_first(at)))
                    if q == S:
                        lap.append(None)
                    else:
                        lap.append(
                            radial_second[q][r] + lane_second(f) + (scale * scale) * row_second(at, own[q])
                        )
                m, b = own[MR:BR], own[BR:WARM]

                def advect(q):
                    return m[0] * g[q][0] + m[1] * g[q][1] + m[2] * g[q][2]

                div = g[MR][0] + g[MT][1] + g[MP][2]
                current = (g[BP][1] - g[BT][2], g[BR][2] - g[BP][0], g[BT][0] - g[BR][1])
                lorentz = (
                    current[1] * b[2] - current[2] * b[1],
                    current[2] * b[0] - current[0] * b[2],
                    current[0] * b[1] - current[1] * b[0],
                )
                grow, thin = jnp.exp(own[WARM]), jnp.exp(-own[S])
                emf_rows = {}
                for i in (0, 1):
                    f = i * SHELLS + r
                    emf_rows[i] = scale * row_first({d: near_emf(f, d) for d in (-3, -2, -1, 1, 2, 3)})
                turn = (
                    lane_first(FLAT + SHELLS + r) - emf_rows[1],
                    emf_rows[0] - emf_radial[2][r],
                    emf_radial[1][r] - lane_first(FLAT + r),
                )
                result = [-advect(S) - div]
                for i in range(3):
                    result.append(
                        -advect(MR + i) - grow * (g[S][i] + g[WARM][i]) + thin * lorentz[i] + SPREAD * lap[MR + i]
                    )
                for i in range(3):
                    result.append(turn[i] + SPREAD * lap[BR + i])
                result.append(-advect(WARM) - (2.0 / 3.0) * div + SPREAD * lap[WARM])
                for q in range(QUANTITIES):
                    f = q * SHELLS + r
                    value = own[q] + (TIME_STEP / 60.0) * result[q]
                    if part == 0:
                        frame[1, pl.ds(f * STRIDE + 8 + here, 8), :] = value
                    else:
                        start = frame[0, pl.ds(f * STRIDE + 8 + here, 8), :]
                        out_ref[pl.ds(f * LON + here, 8), :] = 0.5 * (start + value)
            return carry

        lax.fori_loop(start, stop, body, 0)

    def rows_of(part):
        for h in range(HALO):
            row_out[part, 0, h] = frame[part, pl.ds(8 + h, FLAT, stride=STRIDE), :]
            row_out[part, 1, h] = frame[part, pl.ds(8 + LON - HALO + h, FLAT, stride=STRIDE), :]

    def prepare_picks():
        for tile in range(2 * TILES):
            if tile < TARGETS:
                slot = idx_in[tile, 0:1, :]
            elif tile < TARGETS + 2:
                first = (tile - TARGETS) * GROUPS
                slot = idx_in[first, 1:2, :]
                for q in range(1, GROUPS):
                    slot = jnp.maximum(slot, pltpu.roll(idx_in[first + q], SPARE * q, 1)[1:2, :])
            else:
                side, h = divmod(tile - TARGETS - 2, HALO)
                slot = idx_in[side * (TARGETS - 1), 2 + h : 3 + h, :]
            slot = slot - mine * (GROUP * OUT)
            who = jnp.zeros_like(slot)
            for q in range(1, GROUP):
                who = who + jnp.where(slot >= q * OUT, 1, 0)
            cell = slot - who * OUT
            who = jnp.where(jnp.logical_and(slot >= 0, slot < GROUP * OUT), who, -1)
            at = (tile % 2) * COL
            owner[tile // 2, :, at : at + COL] = jnp.broadcast_to(who, (8, COL))
            hot = jnp.where(iota((SLOTS, COL), 0) == cell, 1.0, 0.0).astype(BF16)
            onehot[tile // 2, :, at : at + COL] = hot

    def table_split(part):
        high, low = split(table[part].reshape(GROUP * PART, SLOTS))
        return jnp.concatenate([high, low], axis=0)

    def product(both, tile):
        return dot(both, onehot[tile])

    def chosen(value, tile):
        value = value[0 : GROUP * PART] + value[GROUP * PART :]
        who = jnp.broadcast_to(owner[tile, 0:1, :], (PART, SLOTS))
        total = jnp.zeros((PART, SLOTS), F32)
        for q in range(GROUP):
            total = jnp.where(who == q, value[q * PART : (q + 1) * PART, :], total)
        return total[:, 0:COL], total[:, COL : 2 * COL]

    def fold(rests):
        turn = (lax.div(iota((8, COL), 1), SPARE) - iota((8, COL), 0)) & 7
        for half, rest in enumerate(rests):
            for s in range(FOLD):
                total = jnp.zeros((8, COL), F32)
                for d in range(8):
                    moved = rest[8 * s : 8 * s + 8, :]
                    if d:
                        moved = pltpu.roll(pltpu.roll(moved, SPARE * d, 1), 8 - d, 0)
                    total = jnp.where(turn == d, moved, total)
                rest_rows[half, s] = total

    def pick_all(part, both):
        sides = [(step + mine) & (TARGETS // 2 - 1) for step in range(TARGETS // 2)]
        extra = list(range(TARGETS // 2 + 1, TILES))
        ends, value = [], product(both, extra[0])
        for tile, after in zip(extra, extra[1:] + [None]):
            now = value
            if after is not None:
                value = product(both, after)
            ends += chosen(now, tile)
        for side in range(2):
            for h in range(HALO):
                picked_rows[part, side, h] = ends[side * HALO + h]
        for side in range(2):
            l_copy(part, side).start()

        @pl.when(col_edge)
        def _():
            now, value = product(both, TARGETS // 2), product(both, sides[0])
            fold(chosen(now, TARGETS // 2))
            for step, tile in enumerate(sides):
                now = value
                if step + 1 < len(sides):
                    value = product(both, sides[step + 1])
                for i, end in enumerate(chosen(now, tile)):
                    target = 2 * tile + i
                    picked[part, target, 0:PART, :] = end
                    for s in range(FOLD):
                        picked[part, target, PART + s : PART + s + 1, :] = rest_rows[
                            tile >> 2, s, pl.ds(target & (GROUPS - 1), 1), :
                        ]
                for i in range(2):
                    b_copy(part, 2 * tile + i).start()

    def corrections(part, side, along_lanes):
        halo_ref, own_ref, add_ref = (col_halo, col_own, col_add) if along_lanes else (row_halo, row_out, row_add)

        def scaled(value, power):
            for _ in range(0 if along_lanes else power):
                value = scale * value
            return value

        halo = [[halo_ref[side, h, q * SHELLS : (q + 1) * SHELLS, :] for q in range(QUANTITIES)] for h in range(HALO)]
        form = cross_azimuthal if along_lanes else cross_polar
        halo_emf = [(cross_radial(x[MR:BR], x[BR:WARM]), form(x[MR:BR], x[BR:WARM])) for x in halo]
        sign = -1.0 if side == 0 else 1.0
        firsts, seconds = (45.0 * sign, -9.0 * sign, sign), (270.0, -27.0, 2.0)
        for j in range(HALO):
            own = [own_ref[part, side, j, q * SHELLS : (q + 1) * SHELLS, :] for q in range(QUANTITIES)]

            def total(weights, of):
                result = None
                for m in (1, 2, 3):
                    h = j + 3 - m if side == 0 else m - 3 + j
                    if 0 <= h < HALO:
                        term = weights[m - 1] * of(h)
                        result = term if result is None else result + term
                return result

            d = [scaled(total(firsts, lambda h, q=q: halo[h][q]), 1) for q in range(QUANTITIES)]
            lap = [
                None if q == S else scaled(total(seconds, lambda h, q=q: halo[h][q]), 2) for q in range(QUANTITIES)
            ]
            radial = scaled(total(firsts, lambda h: halo_emf[h][0]), 1)
            second = scaled(total(firsts, lambda h: halo_emf[h][1]), 1)
            result = edge_rates(own, d, lap, second, radial, along_lanes)
            for q in range(QUANTITIES):
                add_ref[side, j, q * SHELLS : (q + 1) * SHELLS, :] = (TIME_STEP / 60.0 / (1 + part)) * result[q]

    def contribute(side, along_lanes):
        add_ref = col_add if along_lanes else row_add
        value = jnp.concatenate([add_ref[side, j] for j in range(HALO)], axis=0)
        if along_lanes:
            value = jnp.where(iota((HALO * FLAT, COL), 1) < LON, value, 0.0)
        high, low = split(value)
        value = dot(jnp.concatenate([high, low, high], axis=1), rows_split[...] if along_lanes else mix[...])
        total = jnp.zeros((FLAT, SLOTS), F32)
        for j in range(HALO):
            if along_lanes:
                at = j if side == 0 else COL - HALO + j
                weight = cols_mix[at : at + 1, :]
            else:
                at = j if side == 0 else LON - HALO + j
                weight = rows_mix[at : at + 1, :]
            total = total + weight * value[j * FLAT : (j + 1) * FLAT, :]
        for half in range(2):
            blocks[1, half] = blocks[1, half] + total[half * PART : (half + 1) * PART, :]

    def apply_edges():
        for side in range(2):
            for j in range(HALO):
                rows = pl.ds(8 + (j if side == 0 else LON - HALO + j), FLAT, stride=STRIDE)
                frame[1, rows, :] = frame[1, rows, :] + row_add[side, j]
        turn_edges(col_add, turned)
        for half in range(2):
            edge = jnp.transpose(turned[half])[0:LON, :]
            for g in range(FLAT // 2):
                at = (half * (FLAT // 2) + g) * STRIDE + 8
                frame[1, at : at + LON, :] = frame[1, at : at + LON, :] + field_edge(edge, g)

    def a_copy(part, step, half):
        return remote(
            blocks.at[part, half], table.at[part, member], a_send.at[part, half, step], a_recv.at[part, member],
            row_device(step, half),
        )

    def s_copy(part, half):
        return remote(
            blocks.at[part, half], table.at[part, member], s_send.at[part], a_recv.at[part, member], sibling
        )

    def a_arrival(part, step):
        there = (member + step) & (GROUP - 1)
        return remote(blocks.at[part, 0], table.at[part, there], s_send.at[part], a_recv.at[part, there], sibling)

    def b_copy(part, target):
        return remote(
            picked.at[part, target], got_cols.at[part, origin], b_send.at[part, target], b_recv.at[part, origin],
            target_device(target),
        )

    def b_arrival(part, source):
        return remote(
            picked.at[part, 0], got_cols.at[part, source], b_send.at[part, 0], b_recv.at[part, source],
            (other, lon, col),
        )

    def l_copy(part, side):
        return remote(
            picked_rows.at[part, side], got_rows.at[part, origin], l_send.at[part, side], l_recv.at[part, origin],
            target_device(side * (TARGETS - 1)),
        )

    def l_arrival(part, source):
        return remote(
            picked_rows.at[part, 0], got_rows.at[part, source], l_send.at[part, 0], l_recv.at[part, source],
            (other, lon, col),
        )

    def row_copy(part, side):
        return remote(
            row_out.at[part, 1 - side], row_in.at[part, side], r_send.at[part, side], r_recv.at[part, side],
            (panel, lon_up if side == 0 else lon_down, col),
        )

    def col_copy(part, side):
        return remote(
            col_out.at[part, 1 - side], col_in.at[part, side], c_send.at[part, side], c_recv.at[part, side],
            (panel, lon, col_up if side == 0 else col_down),
        )

    def idx_copy(target):
        return remote(
            idx_out, idx_in.at[origin], idx_send.at[target], idx_recv.at[origin], target_device(target)
        )

    def idx_arrival(source):
        return remote(idx_out, idx_in.at[source], idx_send.at[0], idx_recv.at[source], (other, lon, col))

    def inner_sides(part):
        for side in range(2):
            @pl.when(lon != (0 if side == 0 else n_lon - 1))
            def _():
                row_copy(part, side).wait_recv()
                row_halo[side] = row_in[part, side]
                corrections(part, side, False)
                if part == 0:
                    contribute(side, False)

            @pl.when(col != (0 if side == 0 else n_col - 1))
            def _():
                col_copy(part, side).wait_recv()
                pair = col_in[part, side, 0]
                col_halo[side, 0] = pair
                col_halo[side, 1] = pltpu.roll(pair, COL // 2, 1)
                col_halo[side, 2] = col_in[part, side, 1]
                corrections(part, side, True)
                if part == 0:
                    contribute(side, True)

    def outer_sides(part):
        for side in range(2):

            @pl.when(col == (0 if side == 0 else n_col - 1))
            def _():
                for source in range(TARGETS):
                    b_arrival(part, source).wait_recv()
                for half in range(2):
                    total = got_cols[part, half * GROUPS]
                    for group in range(1, GROUPS):
                        total = total + got_cols[part, half * GROUPS + group]
                    main = total[0:PART]
                    rows = slice(half * PART, (half + 1) * PART)
                    col_halo[side, 0, rows, :] = main
                    col_halo[side, 1, rows, :] = pltpu.roll(main, COL - LON, 1)
                    main = pltpu.roll(main, COL - 2 * LON, 1)
                    row, lane = iota((8, COL), 0), iota((8, COL), 1)
                    for s in range(FOLD):
                        value = main[8 * s : 8 * s + 8, :]
                        rest = jnp.broadcast_to(total[PART + s : PART + s + 1], (8, COL))
                        for q in range(8):
                            moved = pltpu.roll(rest, (2 * COL - 2 * LON - SPARE * q) % COL, 1)
                            value = jnp.where(jnp.logical_and(row == q, lane >= COL - 2 * LON), moved, value)
                        at = half * PART + 8 * s
                        col_halo[side, 2, at : at + 8, :] = value
                corrections(part, side, True)
                if part == 0:
                    contribute(side, True)

            @pl.when(lon == (0 if side == 0 else n_lon - 1))
            def _():
                for source in range(TARGETS):
                    l_arrival(part, source).wait_recv()
                for half in range(2):
                    total = got_rows[part, half * GROUPS]
                    for group in range(1, GROUPS):
                        total = total + got_rows[part, half * GROUPS + group]
                    row_halo[side, :, half * PART : (half + 1) * PART, :] = total
                corrections(part, side, False)
                if part == 0:
                    contribute(side, False)

    for part in range(2):
        if part == 0:
            message_tables()
            copies[3].wait()
            interpolate(0, 0)
            pl.semaphore_wait(barrier, 2 * len(AROUND) + 2 + TARGETS)
            for target in range(TARGETS):
                idx_copy(target).start()
            send(0, 0)
            copies[4].wait()
            interpolate(0, 1)
            send(0, 1)
            other_tables()
        else:
            send(1, 0)
            send(1, 1)
            apply_edges()
        rows_of(part)
        for side in range(2):

            @pl.when(sends_rows[side])
            def _():
                row_copy(part, side).start()

        cols_of(part)
        for side in range(2):

            @pl.when(sends_cols[side])
            def _():
                col_copy(part, side).start()

        if part == 0:
            for source in range(TARGETS):
                idx_arrival(source).wait_recv()
            prepare_picks()
        for step in range(1, GROUP):
            a_arrival(part, step).wait_recv()
        both = table_split(part)
        pick_all(part, both)
        lane_pass(part)
        emf_pass(part)
        main_pass(part, 0, 6)
        if part == 0:
            interpolate(1, 0)
            interpolate(1, 1)
        inner_sides(part)
        outer_sides(part)

    for target in range(TARGETS):
        idx_copy(target).wait_send()
    for part in range(2):
        for half in range(2):
            for step in AROUND:
                a_copy(part, step, half).wait_send()
        s_copy(part, 0).wait_send()
        for side in range(2):
            l_copy(part, side).wait_send()

            @pl.when(sends_rows[side])
            def _():
                row_copy(part, side).wait_send()

            @pl.when(sends_cols[side])
            def _():
                col_copy(part, side).wait_send()


        @pl.when(col_edge)
        def _():
            for target in range(TARGETS):
                b_copy(part, target).wait_send()


def shards(state, send_base, send_frac, recv_slots):
    rows = FLAT * LON
    dma = pltpu.SemaphoreType.DMA
    vmem = pltpu.VMEM
    scratch = [
        vmem((2, FLAT, STRIDE, COL), F32),
        vmem((1, OUT), I32),
        vmem((2, OUT), F32),
        vmem((1, recv_slots.shape[-1]), I32),
        vmem((3 * SHELLS * STRIDE, COL), F32),
        vmem(((FLAT + 2 * SHELLS) * LON, 2 * COL), F32),
        vmem((3 * COL, SLOTS), BF16),
        vmem((COL, SLOTS), F32),
        vmem((LON, SLOTS), F32),
        vmem((3 * COL, SLOTS), BF16),
        vmem((2 * COL, 2 * COL), BF16),
        vmem((TILES, SLOTS, 2 * COL), BF16),
        vmem((TILES, 8, 2 * COL), I32),
        vmem((2, COL, COL), F32),
        vmem((2, 2, PART, SLOTS), F32),
        vmem((2, GROUP, PART, SLOTS), F32),
        vmem((8, COL), I32),
        vmem((TARGETS, 8, COL), I32),
        vmem((2, FOLD, 8, COL), F32),
        vmem((2, TARGETS, PART + FOLD, COL), F32),
        vmem((2, 2, HALO, PART, COL), F32),
        vmem((2, TARGETS, PART + FOLD, COL), F32),
        vmem((2, TARGETS, HALO, PART, COL), F32),
        vmem((2, 2, HALO, FLAT, COL), F32),
        vmem((2, 2, HALO, FLAT, COL), F32),
        vmem((2, 2, HALO, FLAT, COL), F32),
        vmem((2, 2, 2, FLAT, COL), F32),
        vmem((2, 2, 2, FLAT, COL), F32),
        vmem((2, HALO, FLAT, COL), F32),
        vmem((2, HALO, FLAT, COL), F32),
        dma((5,)),
        dma((TARGETS,)),
        dma((TARGETS,)),
        dma((2, 2, RING)),
        dma((2, GROUP)),
        dma((2,)),
        dma((2, TARGETS)),
        dma((2, TARGETS)),
        dma((2, 2)),
        dma((2, TARGETS)),
        dma((2, 2)),
        dma((2, 2)),
        dma((2, 2)),
        dma((2, 2)),
    ]
    edges = jax.ShapeDtypeStruct((2, HALO, FLAT, COL), F32)
    value, row_add, col_add = pl.pallas_call(
        kernel,
        out_shape=(jax.ShapeDtypeStruct((rows, COL), F32), edges, edges),
        in_specs=[pl.BlockSpec(memory_space=pltpu.HBM)] * 4,
        out_specs=[pl.BlockSpec(memory_space=pltpu.VMEM)] * 3,
        scratch_shapes=scratch,
        compiler_params=pltpu.CompilerParams(
            collective_id=0, has_side_effects=True, vmem_limit_bytes=40 * 1024 * 1024
        ),
    )(*(
        pltpu.with_memory_space_constraint(x, pltpu.HBM)
        for x in (state.reshape(FLAT, LON, COL), send_base[0], send_frac[0, 0], recv_slots[0])
    ))
    result = pl.pallas_call(
        closing,
        out_shape=jax.ShapeDtypeStruct((rows, COL), F32),
        in_specs=[pl.BlockSpec(memory_space=pltpu.VMEM)] * 3,
        out_specs=pl.BlockSpec(memory_space=pltpu.HBM),
        scratch_shapes=[vmem((2, COL, COL), F32), vmem((rows, COL), F32), dma((4,))],
        compiler_params=pltpu.CompilerParams(vmem_limit_bytes=16 * 1024 * 1024),
    )(value, row_add, col_add)
    return result.reshape(state.shape)


def solution(mesh):
    placed = (
        P("panel", None, None, "lon", "colat"),
        P("panel", ("lon", "colat"), None),
        P("panel", ("lon", "colat"), None, None),
        P("panel", ("lon", "colat"), None),
    )
    return jax.shard_map(
        shards,
        mesh=mesh,
        in_specs=placed,
        out_specs=P("panel", None, None, "lon", "colat"),
        check_vma=False,
    )
```

```python
import math

import jax
import jax.numpy as jnp
from jax import lax
from jax.experimental import pallas as pl
from jax.experimental.pallas import tpu as pltpu
from jax.sharding import PartitionSpec as P

MESH = pl.DeviceIdType.MESH
F32, BF16, I32 = jnp.float32, jnp.bfloat16, jnp.int32

QUANTITIES = 8
SHELLS = 4
FLAT = QUANTITIES * SHELLS
LON = 48
COL = 128
HALO = 3
OUT = 240
SIDE = HALO * LON
SLOTS = 256
GROUP = 8
GROUPS = 8
AROUND = (1, 3, 2)
SPARE = SIDE - COL
PART = FLAT // 2
TARGETS = 2 * GROUPS
TILES = 12
RING = 4
FOLD = PART // 8
STRIDE = LON + 16
TIME_STEP = 0.25
SPREAD = 0.1 / 3.0
S, MR, MT, MP, BR, BT, BP, WARM = range(QUANTITIES)


def dot(left, right):
    return jnp.dot(left, right, preferred_element_type=F32)


def split(value):
    high = value.astype(BF16)
    return high, (value - high.astype(F32)).astype(BF16)


def iota(shape, dim):
    return lax.broadcasted_iota(I32, shape, dim)


def cross_radial(m, b):
    return m[1] * b[2] - m[2] * b[1]


def cross_polar(m, b):
    return m[2] * b[0] - m[0] * b[2]


def cross_azimuthal(m, b):
    return m[0] * b[1] - m[1] * b[0]


def edge_rates(own, d, lap, emf_first, emf_second, along_lanes):
    grow, thin = jnp.exp(own[WARM]), jnp.exp(-own[S])
    b = own[BR:WARM]
    if along_lanes:
        vel, out = own[MT], MT
        lorentz = (d[BR] * b[1], -d[BR] * b[0] - d[BP] * b[2], d[BP] * b[1])
        turn = (emf_first, None, -emf_second)
    else:
        vel, out = own[MP], MP
        lorentz = (d[BR] * b[2], d[BT] * b[2], -d[BT] * b[1] - d[BR] * b[0])
        turn = (-emf_first, emf_second, None)
    result = [-vel * d[S] - d[out]]
    for i in range(3):
        rate = -vel * d[MR + i] + thin * lorentz[i] + SPREAD * lap[MR + i]
        if MR + i == out:
            rate = rate - grow * (d[S] + d[WARM])
        result.append(rate)
    for i in range(3):
        rate = SPREAD * lap[BR + i]
        result.append(rate if turn[i] is None else rate + turn[i])
    result.append(-vel * d[WARM] - (2.0 / 3.0) * d[out] + SPREAD * lap[WARM])
    return result


def shell_steps(x):
    a, b, c = x[1] - x[0], x[2] - x[0], x[3] - x[0]
    p, q, r = 45.0 * a, 45.0 * b, 37.0 * c
    first = (p - 9.0 * b + c, q - 8.0 * c, r - p, r - q + 9.0 * a)
    p, q, r = 270.0 * a, 270.0 * b, 245.0 * c
    second = (p - 27.0 * b + 2.0 * c, q - 490.0 * a - 25.0 * c, p - 490.0 * b + r, q - 27.0 * a - r)
    return first, second


def turn_edges(col_add, turned):
    for side in range(2):
        for j in range(HALO):
            for half in range(2):
                turned[half, pl.ds((1 - side) * HALO + j, FLAT // 2, stride=8), :] = col_add[
                    side, j, half * (FLAT // 2) : (half + 1) * (FLAT // 2), :
                ]


def field_edge(edge, g):
    lane = iota((LON, COL), 1)
    border = jnp.logical_or(lane < HALO, lane >= COL - HALO)
    return jnp.where(border, pltpu.roll(edge, COL - 8 * g - HALO, 1), 0.0)


def closing(value_ref, row_add, col_add, out_hbm, turned, ready, sem):
    turn_edges(col_add, turned)
    copies = []
    for half in range(2):
        edge = jnp.transpose(turned[half])[0:LON, :]
        for chunk in range(2):
            first = half * (FLAT // 2) + 8 * chunk
            for q in range(8):
                at = (first + q) * LON
                ready[at : at + LON, :] = value_ref[at : at + LON, :] + field_edge(edge, 8 * chunk + q)
            for side in range(2):
                for j in range(HALO):
                    rows = pl.ds(first * LON + (j if side == 0 else LON - HALO + j), 8, stride=LON)
                    ready[rows, :] = ready[rows, :] + row_add[side, j, first : first + 8, :]
            rows = pl.ds(first * LON, 8 * LON)
            copy = pltpu.make_async_copy(ready.at[rows, :], out_hbm.at[rows, :], sem.at[2 * half + chunk])
            copy.start()
            copies.append(copy)
    for copy in copies:
        copy.wait()


def kernel(
    x_hbm, base_hbm, frac_hbm, slots_hbm, out_ref, row_add, col_add,
    deep, base_ref, frac_ref, slots_ref, emf, lanes, mix, cols_mix, rows_mix, rows_split, band, onehot, owner, turned,
    blocks, table, idx_out, idx_in, rest_rows, picked, picked_rows, got_cols, got_rows, row_out, row_in, col_own, col_out, col_in,
    row_halo, col_halo,
    in_sem, idx_send, idx_recv, a_send, a_recv, s_send, b_send, b_recv, l_send, l_recv, r_send, r_recv, c_send, c_recv,
):
    panel, lon, col = lax.axis_index("panel"), lax.axis_index("lon"), lax.axis_index("colat")
    n_lon, n_col = lax.axis_size("lon"), lax.axis_size("colat")
    core, mine = lon & 1, lon >> 1
    member = core * n_col + col
    other = 1 - panel
    lon_up, lon_down = lax.rem(lon + 1, n_lon), lax.rem(lon + n_lon - 1, n_lon)
    col_up, col_down = lax.rem(col + 1, n_col), lax.rem(col + n_col - 1, n_col)
    outer = lax.rem(lon + 2 * core - 1 + n_lon, n_lon)
    sends_rows = (lon < n_lon - 1, lon > 0)
    sends_cols = (col < n_col - 1, col > 0)
    col_edge = jnp.logical_or(col == 0, col == n_col - 1)

    sibling = (panel, lon + 1 - 2 * core, col)
    origin = core * GROUPS + mine

    def row_device(step, half):
        return (panel, 2 * mine + half, (col + step) & (n_col - 1))

    def target_device(target):
        return (other, 2 * (target & (GROUPS - 1)) + (target >> 3), col)

    def remote(src, dst, send, recv, device):
        return pltpu.make_async_remote_copy(
            src_ref=src, dst_ref=dst, send_sem=send, recv_sem=recv, device_id=device, device_id_type=MESH
        )

    frame = deep.reshape(2, FLAT * STRIDE, COL)
    copies = [
        pltpu.make_async_copy(src, dst, in_sem.at[i])
        for i, (src, dst) in enumerate(
            (
                (frac_hbm, frac_ref),
                (base_hbm, base_ref),
                (slots_hbm, slots_ref),
                (x_hbm.at[pl.ds(0, PART)], deep.at[0, pl.ds(0, PART), pl.ds(8, LON), :]),
                (x_hbm.at[pl.ds(PART, PART)], deep.at[0, pl.ds(PART, PART), pl.ds(8, LON), :]),
            )
        )
    ]
    for copy in copies:
        copy.start()

    barrier = pltpu.get_barrier_semaphore()
    for step in AROUND:
        for half in range(2):
            pl.semaphore_signal(barrier, inc=1, device_id=row_device(step, half), device_id_type=MESH)
    pl.semaphore_signal(barrier, inc=1, device_id=sibling, device_id_type=MESH)
    for target in range(TARGETS):
        pl.semaphore_signal(barrier, inc=1, device_id=target_device(target), device_id_type=MESH)
    pl.semaphore_signal(barrier, inc=1, device_id=(panel, outer, col), device_id_type=MESH)

    copies[0].wait()
    copies[1].wait()
    base = jnp.concatenate([base_ref[...], jnp.zeros((1, SLOTS - OUT), I32)], axis=1)
    base_row, base_col = lax.div(base, COL), lax.rem(base, COL)
    share = jnp.concatenate([frac_ref[...], jnp.zeros((2, SLOTS - OUT), F32)], axis=1)
    along, across = share[0:1, :], share[1:2, :]
    cells = iota((COL, SLOTS), 0)
    weight = jnp.where(cells == base_col, 1.0 - across, 0.0) + jnp.where(cells == base_col + 1, across, 0.0)
    weight_high, weight_low = split(weight)
    cols_mix[...] = weight
    mix[0:COL, :] = weight_high
    mix[COL : 2 * COL, :] = weight_high
    mix[2 * COL : 3 * COL, :] = weight_low
    cells = iota((LON, SLOTS), 0)
    weight = jnp.where(cells == base_row, 1.0 - along, 0.0) + jnp.where(cells == base_row + 1, along, 0.0)
    rows_mix[...] = weight
    place = (col * COL + iota((1, COL), 1)).astype(F32)
    scale = 1.0 / jnp.sin(math.pi / 4.0 + (place + 0.5) * (math.pi / 2.0 / (COL * n_col)))

    def message_tables():
        copies[2].wait()
        spot = iota((1, SLOTS), 1)
        sides = jnp.where(spot < SIDE, jnp.maximum(slots_ref[:, 0:SLOTS], slots_ref[:, SIDE : SIDE + SLOTS]) + 1, 0)
        digits = jnp.concatenate([lax.div(sides, COL), lax.rem(sides, COL), jnp.zeros((6, SLOTS), I32)], axis=0)
        source, target = iota((SLOTS, SLOTS), 0), iota((SLOTS, SLOTS), 1)
        layer = jnp.where(target >= LON, 1, 0) + jnp.where(target >= 2 * LON, 1, 0)
        order = jnp.logical_and(target < SIDE, source == HALO * (target - LON * layer) + layer)
        digits = dot(digits.astype(F32).astype(BF16), jnp.where(order, 1.0, 0.0).astype(BF16)).astype(I32)
        sides = digits[0:1, :] * COL + digits[1:2, :] - 1
        idx_out[0:1, :] = sides[:, 0:COL]
        idx_out[1:2, :] = sides[:, COL : 2 * COL]
        for h in range(HALO):
            at = 2 * SIDE + h * COL
            idx_out[2 + h : 3 + h, :] = jnp.maximum(
                slots_ref[:, at : at + COL], slots_ref[:, at + HALO * COL : at + HALO * COL + COL]
            )
        idx_out[5:8, :] = jnp.full((3, COL), -1, I32)

    def other_tables():
        zero_rows = jnp.zeros((8, COL), F32)
        for f in range(FLAT):
            for part in range(2):
                frame[part, f * STRIDE : f * STRIDE + 8, :] = zero_rows
                frame[part, f * STRIDE + 8 + LON : (f + 1) * STRIDE, :] = zero_rows
        for f in range(3 * SHELLS):
            emf[f * STRIDE : f * STRIDE + 8, :] = zero_rows
            emf[f * STRIDE + 8 + LON : (f + 1) * STRIDE, :] = zero_rows

        for half in range(2):
            turned[half, :, :] = jnp.zeros((COL, COL), F32)

        apart = iota((COL, COL), 0) - iota((COL, COL), 1)
        reach = jnp.abs(apart)
        first = jnp.where(reach == 1, 45.0, jnp.where(reach == 2, -9.0, jnp.where(reach == 3, 1.0, 0.0)))
        first = jnp.where(apart < 0, -first, first).astype(BF16)
        second = jnp.where(
            reach == 0, -490.0, jnp.where(reach == 1, 270.0, jnp.where(reach == 2, -27.0, jnp.where(reach == 3, 2.0, 0.0)))
        ).astype(BF16)
        for part in range(2):
            band[part * COL : (part + 1) * COL, 0:COL] = first
            band[part * COL : (part + 1) * COL, COL : 2 * COL] = second
        weight_high, weight_low = split(jnp.concatenate([rows_mix[...], jnp.zeros((COL - LON, SLOTS), F32)], axis=0))
        rows_split[0:COL, :] = weight_high
        rows_split[COL : 2 * COL, :] = weight_high
        rows_split[2 * COL : 3 * COL, :] = weight_low

    def load_split(part, pair):
        block = jnp.concatenate(
            [frame[part, pl.ds(pl.multiple_of((8 * pair + q) * STRIDE + 8, 8), LON), :] for q in range(8)], axis=0
        )
        return split(block)

    def interpolate(part, half):
        for pair in range(PART // 8):
            high, low = load_split(part, 2 * half + pair)
            value = dot(jnp.concatenate([high, low], axis=1), mix[0 : 2 * COL, :])
            value = jnp.sum(value.reshape(8, LON, SLOTS) * rows_mix[...][None], axis=1)
            blocks[part, half, 8 * pair : 8 * pair + 8, :] = value

    def send(part, half):
        for step in AROUND:
            a_copy(part, step, half).start()

        @pl.when(core != half)
        def _():
            s_copy(part, half).start()

        @pl.when(core == half)
        def _():
            table[part, member] = blocks[part, half]

    def lane_pass(part):
        for pair in range(FLAT // 8):
            high, low = load_split(part, pair)
            both = jnp.concatenate([high, low], axis=1)
            lanes[8 * LON * pair : 8 * LON * (pair + 1), :] = dot(both, band[...])

    def cols_of(part):
        lane = iota((LON, COL), 1)
        for half in range(2):
            edge = jnp.zeros((LON, COL), F32)
            for g in range(FLAT // 2):
                at = (half * (FLAT // 2) + g) * STRIDE + 8
                moved = pltpu.roll(frame[part, at : at + LON, :], 8 * g + HALO, 1)
                edge = jnp.where(jnp.logical_and(lane >= 8 * g, lane < 8 * g + 2 * HALO), moved, edge)
            turned[half, :, 0:LON] = jnp.transpose(edge)
        for side in range(2):
            for j in range(HALO):
                first = (1 - side) * HALO + j
                for half in range(2):
                    col_own[part, side, j, half * (FLAT // 2) : (half + 1) * (FLAT // 2), :] = turned[
                        half, pl.ds(first, FLAT // 2, stride=8), :
                    ]
            col_out[part, side, 0] = jnp.where(
                iota((FLAT, COL), 1) < COL // 2, col_own[part, side, 0], pltpu.roll(col_own[part, side, 1], COL // 2, 1)
            )
            col_out[part, side, 1] = col_own[part, side, 2]

    def emf_pass(part):
        for r in range(SHELLS):
            def field(q):
                at = (q * SHELLS + r) * STRIDE + 8
                return frame[part, at : at + LON, :]

            m, b = [field(MR + i) for i in range(3)], [field(BR + i) for i in range(3)]
            for i, form in enumerate((cross_radial, cross_polar, cross_azimuthal)):
                at = (i * SHELLS + r) * STRIDE + 8
                emf[at : at + LON, :] = form(m, b)
        for i, at in ((0, FLAT), (2, FLAT + SHELLS)):
            block = jnp.concatenate(
                [emf[(i * SHELLS + r) * STRIDE + 8 : (i * SHELLS + r) * STRIDE + 8 + LON, :] for r in range(SHELLS)],
                axis=0,
            )
            high, low = split(block)
            lanes[at * LON : (at + SHELLS) * LON, 0:COL] = dot(
                jnp.concatenate([high, low], axis=1), band[:, 0:COL]
            )

    def main_pass(part, start, stop):
        def body(block, carry):
            here = pl.multiple_of(8 * block, 8)

            def near(f, apart):
                return frame[part, pl.ds(f * STRIDE + 8 + here + apart, 8), :]

            def near_emf(f, apart):
                return emf[pl.ds(f * STRIDE + 8 + here + apart, 8), :]

            def lane_first(f):
                return lanes[pl.ds(f * LON + here, 8), 0:COL]

            def lane_second(f):
                return lanes[pl.ds(f * LON + here, 8), COL : 2 * COL]

            def row_first(at):
                return 45.0 * (at[1] - at[-1]) - 9.0 * (at[2] - at[-2]) + (at[3] - at[-3])

            def row_second(at, centre):
                return (
                    270.0 * (at[1] + at[-1]) - 27.0 * (at[2] + at[-2]) + 2.0 * (at[3] + at[-3]) - 490.0 * centre
                )

            centre = [[near(q * SHELLS + r, 0) for r in range(SHELLS)] for q in range(QUANTITIES)]
            steps = [shell_steps(x) for x in centre]
            radial, radial_second = [x[0] for x in steps], [x[1] for x in steps]
            emf_centre = [[near_emf(i * SHELLS + r, 0) for r in range(SHELLS)] for i in range(3)]
            emf_radial = [None, shell_steps(emf_centre[1])[0], shell_steps(emf_centre[2])[0]]
            for r in range(SHELLS):
                own = [centre[q][r] for q in range(QUANTITIES)]
                g, lap = [], []
                for q in range(QUANTITIES):
                    f = q * SHELLS + r
                    at = {d: near(f, d) for d in (-3, -2, -1, 1, 2, 3)}
                    g.append((radial[q][r], lane_first(f), scale * row_first(at)))
                    if q == S:
                        lap.append(None)
                    else:
                        lap.append(
                            radial_second[q][r] + lane_second(f) + (scale * scale) * row_second(at, own[q])
                        )
                m, b = own[MR:BR], own[BR:WARM]

                def advect(q):
                    return m[0] * g[q][0] + m[1] * g[q][1] + m[2] * g[q][2]

                div = g[MR][0] + g[MT][1] + g[MP][2]
                current = (g[BP][1] - g[BT][2], g[BR][2] - g[BP][0], g[BT][0] - g[BR][1])
                lorentz = (
                    current[1] * b[2] - current[2] * b[1],
                    current[2] * b[0] - current[0] * b[2],
                    current[0] * b[1] - current[1] * b[0],
                )
                grow, thin = jnp.exp(own[WARM]), jnp.exp(-own[S])
                emf_rows = {}
                for i in (0, 1):
                    f = i * SHELLS + r
                    emf_rows[i] = scale * row_first({d: near_emf(f, d) for d in (-3, -2, -1, 1, 2, 3)})
                turn = (
                    lane_first(FLAT + SHELLS + r) - emf_rows[1],
                    emf_rows[0] - emf_radial[2][r],
                    emf_radial[1][r] - lane_first(FLAT + r),
                )
                result = [-advect(S) - div]
                for i in range(3):
                    result.append(
                        -advect(MR + i) - grow * (g[S][i] + g[WARM][i]) + thin * lorentz[i] + SPREAD * lap[MR + i]
                    )
                for i in range(3):
                    result.append(turn[i] + SPREAD * lap[BR + i])
                result.append(-advect(WARM) - (2.0 / 3.0) * div + SPREAD * lap[WARM])
                for q in range(QUANTITIES):
                    f = q * SHELLS + r
                    value = own[q] + (TIME_STEP / 60.0) * result[q]
                    if part == 0:
                        frame[1, pl.ds(f * STRIDE + 8 + here, 8), :] = value
                    else:
                        start = frame[0, pl.ds(f * STRIDE + 8 + here, 8), :]
                        out_ref[pl.ds(f * LON + here, 8), :] = 0.5 * (start + value)
            return carry

        lax.fori_loop(start, stop, body, 0)

    def rows_of(part):
        for h in range(HALO):
            row_out[part, 0, h] = frame[part, pl.ds(8 + h, FLAT, stride=STRIDE), :]
            row_out[part, 1, h] = frame[part, pl.ds(8 + LON - HALO + h, FLAT, stride=STRIDE), :]

    def prepare_picks():
        for tile in range(2 * TILES):
            if tile < TARGETS:
                slot = idx_in[tile, 0:1, :]
            elif tile < TARGETS + 2:
                first = (tile - TARGETS) * GROUPS
                slot = idx_in[first, 1:2, :]
                for q in range(1, GROUPS):
                    slot = jnp.maximum(slot, pltpu.roll(idx_in[first + q], SPARE * q, 1)[1:2, :])
            else:
                side, h = divmod(tile - TARGETS - 2, HALO)
                slot = idx_in[side * (TARGETS - 1), 2 + h : 3 + h, :]
            slot = slot - mine * (GROUP * OUT)
            who = jnp.zeros_like(slot)
            for q in range(1, GROUP):
                who = who + jnp.where(slot >= q * OUT, 1, 0)
            cell = slot - who * OUT
            who = jnp.where(jnp.logical_and(slot >= 0, slot < GROUP * OUT), who, -1)
            at = (tile % 2) * COL
            owner[tile // 2, :, at : at + COL] = jnp.broadcast_to(who, (8, COL))
            hot = jnp.where(iota((SLOTS, COL), 0) == cell, 1.0, 0.0).astype(BF16)
            onehot[tile // 2, :, at : at + COL] = hot

    def rounded_table(part):
        return table[part].reshape(GROUP * PART, SLOTS).astype(BF16)

    def product(both, tile):
        return dot(both, onehot[tile])

    def chosen(value, tile):
        who = jnp.broadcast_to(owner[tile, 0:1, :], (PART, SLOTS))
        total = jnp.zeros((PART, SLOTS), F32)
        for q in range(GROUP):
            total = jnp.where(who == q, value[q * PART : (q + 1) * PART, :], total)
        return total[:, 0:COL], total[:, COL : 2 * COL]

    def fold(rests):
        turn = (lax.div(iota((8, COL), 1), SPARE) - iota((8, COL), 0)) & 7
        for half, rest in enumerate(rests):
            for s in range(FOLD):
                total = jnp.zeros((8, COL), F32)
                for d in range(8):
                    moved = rest[8 * s : 8 * s + 8, :]
                    if d:
                        moved = pltpu.roll(pltpu.roll(moved, SPARE * d, 1), 8 - d, 0)
                    total = jnp.where(turn == d, moved, total)
                rest_rows[half, s] = total

    def pick_all(part, both):
        sides = [(step + mine) & (TARGETS // 2 - 1) for step in range(TARGETS // 2)]
        extra = list(range(TARGETS // 2 + 1, TILES))
        ends, value = [], product(both, extra[0])
        for tile, after in zip(extra, extra[1:] + [None]):
            now = value
            if after is not None:
                value = product(both, after)
            ends += chosen(now, tile)
        for side in range(2):
            for h in range(HALO):
                picked_rows[part, side, h] = ends[side * HALO + h]
        for side in range(2):
            l_copy(part, side).start()

        @pl.when(col_edge)
        def _():
            now, value = product(both, TARGETS // 2), product(both, sides[0])
            fold(chosen(now, TARGETS // 2))
            for step, tile in enumerate(sides):
                now = value
                if step + 1 < len(sides):
                    value = product(both, sides[step + 1])
                for i, end in enumerate(chosen(now, tile)):
                    target = 2 * tile + i
                    picked[part, target, 0:PART, :] = end
                    for s in range(FOLD):
                        picked[part, target, PART + s : PART + s + 1, :] = rest_rows[
                            tile >> 2, s, pl.ds(target & (GROUPS - 1), 1), :
                        ]
                for i in range(2):
                    b_copy(part, 2 * tile + i).start()

    def corrections(part, side, along_lanes):
        halo_ref, own_ref, add_ref = (col_halo, col_own, col_add) if along_lanes else (row_halo, row_out, row_add)

        def scaled(value, power):
            for _ in range(0 if along_lanes else power):
                value = scale * value
            return value

        halo = [[halo_ref[side, h, q * SHELLS : (q + 1) * SHELLS, :] for q in range(QUANTITIES)] for h in range(HALO)]
        form = cross_azimuthal if along_lanes else cross_polar
        halo_emf = [(cross_radial(x[MR:BR], x[BR:WARM]), form(x[MR:BR], x[BR:WARM])) for x in halo]
        sign = -1.0 if side == 0 else 1.0
        firsts, seconds = (45.0 * sign, -9.0 * sign, sign), (270.0, -27.0, 2.0)
        for j in range(HALO):
            own = [own_ref[part, side, j, q * SHELLS : (q + 1) * SHELLS, :] for q in range(QUANTITIES)]

            def total(weights, of):
                result = None
                for m in (1, 2, 3):
                    h = j + 3 - m if side == 0 else m - 3 + j
                    if 0 <= h < HALO:
                        term = weights[m - 1] * of(h)
                        result = term if result is None else result + term
                return result

            d = [scaled(total(firsts, lambda h, q=q: halo[h][q]), 1) for q in range(QUANTITIES)]
            lap = [
                None if q == S else scaled(total(seconds, lambda h, q=q: halo[h][q]), 2) for q in range(QUANTITIES)
            ]
            radial = scaled(total(firsts, lambda h: halo_emf[h][0]), 1)
            second = scaled(total(firsts, lambda h: halo_emf[h][1]), 1)
            result = edge_rates(own, d, lap, second, radial, along_lanes)
            for q in range(QUANTITIES):
                add_ref[side, j, q * SHELLS : (q + 1) * SHELLS, :] = (TIME_STEP / 60.0 / (1 + part)) * result[q]

    def contribute(side, along_lanes):
        add_ref = col_add if along_lanes else row_add
        value = jnp.concatenate([add_ref[side, j] for j in range(HALO)], axis=0)
        if along_lanes:
            value = jnp.where(iota((HALO * FLAT, COL), 1) < LON, value, 0.0)
        high, low = split(value)
        value = dot(jnp.concatenate([high, low, high], axis=1), rows_split[...] if along_lanes else mix[...])
        total = jnp.zeros((FLAT, SLOTS), F32)
        for j in range(HALO):
            if along_lanes:
                at = j if side == 0 else COL - HALO + j
                weight = cols_mix[at : at + 1, :]
            else:
                at = j if side == 0 else LON - HALO + j
                weight = rows_mix[at : at + 1, :]
            total = total + weight * value[j * FLAT : (j + 1) * FLAT, :]
        for half in range(2):
            blocks[1, half] = blocks[1, half] + total[half * PART : (half + 1) * PART, :]

    def apply_edges():
        for side in range(2):
            for j in range(HALO):
                rows = pl.ds(8 + (j if side == 0 else LON - HALO + j), FLAT, stride=STRIDE)
                frame[1, rows, :] = frame[1, rows, :] + row_add[side, j]
        turn_edges(col_add, turned)
        for half in range(2):
            edge = jnp.transpose(turned[half])[0:LON, :]
            for g in range(FLAT // 2):
                at = (half * (FLAT // 2) + g) * STRIDE + 8
                frame[1, at : at + LON, :] = frame[1, at : at + LON, :] + field_edge(edge, g)

    def a_copy(part, step, half):
        return remote(
            blocks.at[part, half], table.at[part, member], a_send.at[part, half, step], a_recv.at[part, member],
            row_device(step, half),
        )

    def s_copy(part, half):
        return remote(
            blocks.at[part, half], table.at[part, member], s_send.at[part], a_recv.at[part, member], sibling
        )

    def a_arrival(part, step):
        there = (member + step) & (GROUP - 1)
        return remote(blocks.at[part, 0], table.at[part, there], s_send.at[part], a_recv.at[part, there], sibling)

    def b_copy(part, target):
        return remote(
            picked.at[part, target], got_cols.at[part, origin], b_send.at[part, target], b_recv.at[part, origin],
            target_device(target),
        )

    def b_arrival(part, source):
        return remote(
            picked.at[part, 0], got_cols.at[part, source], b_send.at[part, 0], b_recv.at[part, source],
            (other, lon, col),
        )

    def l_copy(part, side):
        return remote(
            picked_rows.at[part, side], got_rows.at[part, origin], l_send.at[part, side], l_recv.at[part, origin],
            target_device(side * (TARGETS - 1)),
        )

    def l_arrival(part, source):
        return remote(
            picked_rows.at[part, 0], got_rows.at[part, source], l_send.at[part, 0], l_recv.at[part, source],
            (other, lon, col),
        )

    def row_copy(part, side):
        return remote(
            row_out.at[part, 1 - side], row_in.at[part, side], r_send.at[part, side], r_recv.at[part, side],
            (panel, lon_up if side == 0 else lon_down, col),
        )

    def col_copy(part, side):
        return remote(
            col_out.at[part, 1 - side], col_in.at[part, side], c_send.at[part, side], c_recv.at[part, side],
            (panel, lon, col_up if side == 0 else col_down),
        )

    def idx_copy(target):
        return remote(
            idx_out, idx_in.at[origin], idx_send.at[target], idx_recv.at[origin], target_device(target)
        )

    def idx_arrival(source):
        return remote(idx_out, idx_in.at[source], idx_send.at[0], idx_recv.at[source], (other, lon, col))

    def inner_sides(part):
        for side in range(2):
            @pl.when(lon != (0 if side == 0 else n_lon - 1))
            def _():
                row_copy(part, side).wait_recv()
                row_halo[side] = row_in[part, side]
                corrections(part, side, False)
                if part == 0:
                    contribute(side, False)

            @pl.when(col != (0 if side == 0 else n_col - 1))
            def _():
                col_copy(part, side).wait_recv()
                pair = col_in[part, side, 0]
                col_halo[side, 0] = pair
                col_halo[side, 1] = pltpu.roll(pair, COL // 2, 1)
                col_halo[side, 2] = col_in[part, side, 1]
                corrections(part, side, True)
                if part == 0:
                    contribute(side, True)

    def outer_sides(part):
        for side in range(2):

            @pl.when(col == (0 if side == 0 else n_col - 1))
            def _():
                for source in range(TARGETS):
                    b_arrival(part, source).wait_recv()
                for half in range(2):
                    total = got_cols[part, half * GROUPS]
                    for group in range(1, GROUPS):
                        total = total + got_cols[part, half * GROUPS + group]
                    main = total[0:PART]
                    rows = slice(half * PART, (half + 1) * PART)
                    col_halo[side, 0, rows, :] = main
                    col_halo[side, 1, rows, :] = pltpu.roll(main, COL - LON, 1)
                    main = pltpu.roll(main, COL - 2 * LON, 1)
                    row, lane = iota((8, COL), 0), iota((8, COL), 1)
                    for s in range(FOLD):
                        value = main[8 * s : 8 * s + 8, :]
                        rest = jnp.broadcast_to(total[PART + s : PART + s + 1], (8, COL))
                        for q in range(8):
                            moved = pltpu.roll(rest, (2 * COL - 2 * LON - SPARE * q) % COL, 1)
                            value = jnp.where(jnp.logical_and(row == q, lane >= COL - 2 * LON), moved, value)
                        at = half * PART + 8 * s
                        col_halo[side, 2, at : at + 8, :] = value
                corrections(part, side, True)
                if part == 0:
                    contribute(side, True)

            @pl.when(lon == (0 if side == 0 else n_lon - 1))
            def _():
                for source in range(TARGETS):
                    l_arrival(part, source).wait_recv()
                for half in range(2):
                    total = got_rows[part, half * GROUPS]
                    for group in range(1, GROUPS):
                        total = total + got_rows[part, half * GROUPS + group]
                    row_halo[side, :, half * PART : (half + 1) * PART, :] = total
                corrections(part, side, False)
                if part == 0:
                    contribute(side, False)

    for part in range(2):
        if part == 0:
            message_tables()
            copies[3].wait()
            interpolate(0, 0)
            pl.semaphore_wait(barrier, 2 * len(AROUND) + 2 + TARGETS)
            for target in range(TARGETS):
                idx_copy(target).start()
            send(0, 0)
            copies[4].wait()
            interpolate(0, 1)
            send(0, 1)
            other_tables()
        else:
            send(1, 0)
            send(1, 1)
            apply_edges()
        rows_of(part)
        for side in range(2):

            @pl.when(sends_rows[side])
            def _():
                row_copy(part, side).start()

        cols_of(part)
        for side in range(2):

            @pl.when(sends_cols[side])
            def _():
                col_copy(part, side).start()

        lane_pass(part)
        emf_pass(part)
        if part == 0:
            for source in range(TARGETS):
                idx_arrival(source).wait_recv()
            prepare_picks()
        for step in range(1, GROUP):
            a_arrival(part, step).wait_recv()
        both = rounded_table(part)
        pick_all(part, both)
        main_pass(part, 0, 6)
        if part == 0:
            interpolate(1, 0)
            interpolate(1, 1)
        inner_sides(part)
        outer_sides(part)

    for target in range(TARGETS):
        idx_copy(target).wait_send()
    for part in range(2):
        for half in range(2):
            for step in AROUND:
                a_copy(part, step, half).wait_send()
        s_copy(part, 0).wait_send()
        for side in range(2):
            l_copy(part, side).wait_send()

            @pl.when(sends_rows[side])
            def _():
                row_copy(part, side).wait_send()

            @pl.when(sends_cols[side])
            def _():
                col_copy(part, side).wait_send()


        @pl.when(col_edge)
        def _():
            for target in range(TARGETS):
                b_copy(part, target).wait_send()


def shards(state, send_base, send_frac, recv_slots):
    rows = FLAT * LON
    dma = pltpu.SemaphoreType.DMA
    vmem = pltpu.VMEM
    scratch = [
        vmem((2, FLAT, STRIDE, COL), F32),
        vmem((1, OUT), I32),
        vmem((2, OUT), F32),
        vmem((1, recv_slots.shape[-1]), I32),
        vmem((3 * SHELLS * STRIDE, COL), F32),
        vmem(((FLAT + 2 * SHELLS) * LON, 2 * COL), F32),
        vmem((3 * COL, SLOTS), BF16),
        vmem((COL, SLOTS), F32),
        vmem((LON, SLOTS), F32),
        vmem((3 * COL, SLOTS), BF16),
        vmem((2 * COL, 2 * COL), BF16),
        vmem((TILES, SLOTS, 2 * COL), BF16),
        vmem((TILES, 8, 2 * COL), I32),
        vmem((2, COL, COL), F32),
        vmem((2, 2, PART, SLOTS), F32),
        vmem((2, GROUP, PART, SLOTS), F32),
        vmem((8, COL), I32),
        vmem((TARGETS, 8, COL), I32),
        vmem((2, FOLD, 8, COL), F32),
        vmem((2, TARGETS, PART + FOLD, COL), F32),
        vmem((2, 2, HALO, PART, COL), F32),
        vmem((2, TARGETS, PART + FOLD, COL), F32),
        vmem((2, TARGETS, HALO, PART, COL), F32),
        vmem((2, 2, HALO, FLAT, COL), F32),
        vmem((2, 2, HALO, FLAT, COL), F32),
        vmem((2, 2, HALO, FLAT, COL), F32),
        vmem((2, 2, 2, FLAT, COL), F32),
        vmem((2, 2, 2, FLAT, COL), F32),
        vmem((2, HALO, FLAT, COL), F32),
        vmem((2, HALO, FLAT, COL), F32),
        dma((5,)),
        dma((TARGETS,)),
        dma((TARGETS,)),
        dma((2, 2, RING)),
        dma((2, GROUP)),
        dma((2,)),
        dma((2, TARGETS)),
        dma((2, TARGETS)),
        dma((2, 2)),
        dma((2, TARGETS)),
        dma((2, 2)),
        dma((2, 2)),
        dma((2, 2)),
        dma((2, 2)),
    ]
    edges = jax.ShapeDtypeStruct((2, HALO, FLAT, COL), F32)
    value, row_add, col_add = pl.pallas_call(
        kernel,
        out_shape=(jax.ShapeDtypeStruct((rows, COL), F32), edges, edges),
        in_specs=[pl.BlockSpec(memory_space=pltpu.HBM)] * 4,
        out_specs=[pl.BlockSpec(memory_space=pltpu.VMEM)] * 3,
        scratch_shapes=scratch,
        compiler_params=pltpu.CompilerParams(
            collective_id=0, has_side_effects=True, vmem_limit_bytes=40 * 1024 * 1024
        ),
    )(*(
        pltpu.with_memory_space_constraint(x, pltpu.HBM)
        for x in (state.reshape(FLAT, LON, COL), send_base[0], send_frac[0, 0], recv_slots[0])
    ))
    result = pl.pallas_call(
        closing,
        out_shape=jax.ShapeDtypeStruct((rows, COL), F32),
        in_specs=[pl.BlockSpec(memory_space=pltpu.VMEM)] * 3,
        out_specs=pl.BlockSpec(memory_space=pltpu.HBM),
        scratch_shapes=[vmem((2, COL, COL), F32), vmem((rows, COL), F32), dma((4,))],
        compiler_params=pltpu.CompilerParams(vmem_limit_bytes=16 * 1024 * 1024),
    )(value, row_add, col_add)
    return result.reshape(state.shape)


def solution(mesh):
    placed = (
        P("panel", None, None, "lon", "colat"),
        P("panel", ("lon", "colat"), None),
        P("panel", ("lon", "colat"), None, None),
        P("panel", ("lon", "colat"), None),
    )
    return jax.shard_map(
        shards,
        mesh=mesh,
        in_specs=placed,
        out_specs=P("panel", None, None, "lon", "colat"),
        check_vma=False,
    )
```

```python
import math

import jax
import jax.numpy as jnp
from jax import lax
from jax.experimental import pallas as pl
from jax.experimental.pallas import tpu as pltpu
from jax.sharding import PartitionSpec as P

MESH = pl.DeviceIdType.MESH
F32, BF16, I32 = jnp.float32, jnp.bfloat16, jnp.int32

QUANTITIES = 8
SHELLS = 4
FLAT = QUANTITIES * SHELLS
LON = 48
COL = 128
HALO = 3
OUT = 240
SIDE = HALO * LON
SLOTS = 256
GROUP = 8
GROUPS = 8
AROUND = (1, 3, 2)
SPARE = SIDE - COL
PART = FLAT // 2
TARGETS = 2 * GROUPS
TILES = 12
RING = 4
CHUNKS = 2
ROWS = PART // CHUNKS
STRIDE = LON + 16
TIME_STEP = 0.25
SPREAD = 0.1 / 3.0
S, MR, MT, MP, BR, BT, BP, WARM = range(QUANTITIES)


def dot(left, right):
    return jnp.dot(left, right, preferred_element_type=F32)


def split(value):
    high = value.astype(BF16)
    return high, (value - high.astype(F32)).astype(BF16)


def iota(shape, dim):
    return lax.broadcasted_iota(I32, shape, dim)


def cross_radial(m, b):
    return m[1] * b[2] - m[2] * b[1]


def cross_polar(m, b):
    return m[2] * b[0] - m[0] * b[2]


def cross_azimuthal(m, b):
    return m[0] * b[1] - m[1] * b[0]


def edge_rates(own, d, lap, emf_first, emf_second, along_lanes):
    grow, thin = jnp.exp(own[WARM]), jnp.exp(-own[S])
    b = own[BR:WARM]
    if along_lanes:
        vel, out = own[MT], MT
        lorentz = (d[BR] * b[1], -d[BR] * b[0] - d[BP] * b[2], d[BP] * b[1])
        turn = (emf_first, None, -emf_second)
    else:
        vel, out = own[MP], MP
        lorentz = (d[BR] * b[2], d[BT] * b[2], -d[BT] * b[1] - d[BR] * b[0])
        turn = (-emf_first, emf_second, None)
    result = [-vel * d[S] - d[out]]
    for i in range(3):
        rate = -vel * d[MR + i] + thin * lorentz[i] + SPREAD * lap[MR + i]
        if MR + i == out:
            rate = rate - grow * (d[S] + d[WARM])
        result.append(rate)
    for i in range(3):
        rate = SPREAD * lap[BR + i]
        result.append(rate if turn[i] is None else rate + turn[i])
    result.append(-vel * d[WARM] - (2.0 / 3.0) * d[out] + SPREAD * lap[WARM])
    return result


def shell_steps(x):
    a, b, c = x[1] - x[0], x[2] - x[0], x[3] - x[0]
    p, q, r = 45.0 * a, 45.0 * b, 37.0 * c
    first = (p - 9.0 * b + c, q - 8.0 * c, r - p, r - q + 9.0 * a)
    p, q, r = 270.0 * a, 270.0 * b, 245.0 * c
    second = (p - 27.0 * b + 2.0 * c, q - 490.0 * a - 25.0 * c, p - 490.0 * b + r, q - 27.0 * a - r)
    return first, second


def turn_edges(col_add, turned):
    for side in range(2):
        for j in range(HALO):
            for half in range(2):
                turned[half, pl.ds((1 - side) * HALO + j, FLAT // 2, stride=8), :] = col_add[
                    side, j, half * (FLAT // 2) : (half + 1) * (FLAT // 2), :
                ]


def field_edge(edge, g):
    lane = iota((LON, COL), 1)
    border = jnp.logical_or(lane < HALO, lane >= COL - HALO)
    return jnp.where(border, pltpu.roll(edge, COL - 8 * g - HALO, 1), 0.0)


def closing(value_ref, row_add, col_add, out_hbm, turned, ready, sem):
    turn_edges(col_add, turned)
    copies = []
    for half in range(2):
        edge = jnp.transpose(turned[half])[0:LON, :]
        for chunk in range(2):
            first = half * (FLAT // 2) + 8 * chunk
            for q in range(8):
                at = (first + q) * LON
                ready[at : at + LON, :] = value_ref[at : at + LON, :] + field_edge(edge, 8 * chunk + q)
            for side in range(2):
                for j in range(HALO):
                    rows = pl.ds(first * LON + (j if side == 0 else LON - HALO + j), 8, stride=LON)
                    ready[rows, :] = ready[rows, :] + row_add[side, j, first : first + 8, :]
            rows = pl.ds(first * LON, 8 * LON)
            copy = pltpu.make_async_copy(ready.at[rows, :], out_hbm.at[rows, :], sem.at[2 * half + chunk])
            copy.start()
            copies.append(copy)
    for copy in copies:
        copy.wait()


def kernel(
    x_hbm, base_hbm, frac_hbm, slots_hbm, out_ref, row_add, col_add,
    deep, base_ref, frac_ref, slots_ref, emf, lanes, mix, cols_mix, rows_mix, rows_split, band, onehot, owner, turned,
    blocks, table, idx_out, idx_in, rest_rows, picked, picked_rows, got_cols, got_rows, row_out, row_in, col_own, col_out, col_in,
    row_halo, col_halo,
    in_sem, idx_send, idx_recv, a_send, a_recv, s_send, b_send, b_recv, l_send, l_recv, r_send, r_recv, c_send, c_recv,
):
    panel, lon, col = lax.axis_index("panel"), lax.axis_index("lon"), lax.axis_index("colat")
    n_lon, n_col = lax.axis_size("lon"), lax.axis_size("colat")
    core, mine = lon & 1, lon >> 1
    member = core * n_col + col
    other = 1 - panel
    lon_up, lon_down = lax.rem(lon + 1, n_lon), lax.rem(lon + n_lon - 1, n_lon)
    col_up, col_down = lax.rem(col + 1, n_col), lax.rem(col + n_col - 1, n_col)
    outer = lax.rem(lon + 2 * core - 1 + n_lon, n_lon)
    sends_rows = (lon < n_lon - 1, lon > 0)
    sends_cols = (col < n_col - 1, col > 0)
    col_edge = jnp.logical_or(col == 0, col == n_col - 1)

    sibling = (panel, lon + 1 - 2 * core, col)
    origin = core * GROUPS + mine

    def row_device(step, half):
        return (panel, 2 * mine + half, (col + step) & (n_col - 1))

    def target_device(target):
        return (other, 2 * (target & (GROUPS - 1)) + (target >> 3), col)

    def remote(src, dst, send, recv, device):
        return pltpu.make_async_remote_copy(
            src_ref=src, dst_ref=dst, send_sem=send, recv_sem=recv, device_id=device, device_id_type=MESH
        )

    frame = deep.reshape(2, FLAT * STRIDE, COL)
    copies = [
        pltpu.make_async_copy(src, dst, in_sem.at[i])
        for i, (src, dst) in enumerate(
            (
                (frac_hbm, frac_ref),
                (base_hbm, base_ref),
                (slots_hbm, slots_ref),
                (x_hbm.at[pl.ds(0, PART)], deep.at[0, pl.ds(0, PART), pl.ds(8, LON), :]),
                (x_hbm.at[pl.ds(PART, PART)], deep.at[0, pl.ds(PART, PART), pl.ds(8, LON), :]),
            )
        )
    ]
    for copy in copies:
        copy.start()

    barrier = pltpu.get_barrier_semaphore()
    for step in AROUND:
        for half in range(2):
            pl.semaphore_signal(barrier, inc=1, device_id=row_device(step, half), device_id_type=MESH)
    pl.semaphore_signal(barrier, inc=1, device_id=sibling, device_id_type=MESH)
    for target in range(TARGETS):
        pl.semaphore_signal(barrier, inc=1, device_id=target_device(target), device_id_type=MESH)
    pl.semaphore_signal(barrier, inc=1, device_id=(panel, outer, col), device_id_type=MESH)

    copies[0].wait()
    copies[1].wait()
    base = jnp.concatenate([base_ref[...], jnp.zeros((1, SLOTS - OUT), I32)], axis=1)
    base_row, base_col = lax.div(base, COL), lax.rem(base, COL)
    share = jnp.concatenate([frac_ref[...], jnp.zeros((2, SLOTS - OUT), F32)], axis=1)
    along, across = share[0:1, :], share[1:2, :]
    cells = iota((COL, SLOTS), 0)
    weight = jnp.where(cells == base_col, 1.0 - across, 0.0) + jnp.where(cells == base_col + 1, across, 0.0)
    weight_high, weight_low = split(weight)
    cols_mix[...] = weight
    mix[0:COL, :] = weight_high
    mix[COL : 2 * COL, :] = weight_high
    mix[2 * COL : 3 * COL, :] = weight_low
    cells = iota((LON, SLOTS), 0)
    weight = jnp.where(cells == base_row, 1.0 - along, 0.0) + jnp.where(cells == base_row + 1, along, 0.0)
    rows_mix[...] = weight
    place = (col * COL + iota((1, COL), 1)).astype(F32)
    scale = 1.0 / jnp.sin(math.pi / 4.0 + (place + 0.5) * (math.pi / 2.0 / (COL * n_col)))

    def message_tables():
        copies[2].wait()
        spot = iota((1, SLOTS), 1)
        sides = jnp.where(spot < SIDE, jnp.maximum(slots_ref[:, 0:SLOTS], slots_ref[:, SIDE : SIDE + SLOTS]) + 1, 0)
        digits = jnp.concatenate([lax.div(sides, COL), lax.rem(sides, COL), jnp.zeros((6, SLOTS), I32)], axis=0)
        source, target = iota((SLOTS, SLOTS), 0), iota((SLOTS, SLOTS), 1)
        layer = jnp.where(target >= LON, 1, 0) + jnp.where(target >= 2 * LON, 1, 0)
        order = jnp.logical_and(target < SIDE, source == HALO * (target - LON * layer) + layer)
        digits = dot(digits.astype(F32).astype(BF16), jnp.where(order, 1.0, 0.0).astype(BF16)).astype(I32)
        sides = digits[0:1, :] * COL + digits[1:2, :] - 1
        idx_out[0:1, :] = sides[:, 0:COL]
        idx_out[1:2, :] = sides[:, COL : 2 * COL]
        for h in range(HALO):
            at = 2 * SIDE + h * COL
            idx_out[2 + h : 3 + h, :] = jnp.maximum(
                slots_ref[:, at : at + COL], slots_ref[:, at + HALO * COL : at + HALO * COL + COL]
            )
        idx_out[5:8, :] = jnp.full((3, COL), -1, I32)

    def other_tables():
        zero_rows = jnp.zeros((8, COL), F32)
        for f in range(FLAT):
            for part in range(2):
                frame[part, f * STRIDE : f * STRIDE + 8, :] = zero_rows
                frame[part, f * STRIDE + 8 + LON : (f + 1) * STRIDE, :] = zero_rows
        for f in range(3 * SHELLS):
            emf[f * STRIDE : f * STRIDE + 8, :] = zero_rows
            emf[f * STRIDE + 8 + LON : (f + 1) * STRIDE, :] = zero_rows

        for half in range(2):
            turned[half, :, :] = jnp.zeros((COL, COL), F32)

        apart = iota((COL, COL), 0) - iota((COL, COL), 1)
        reach = jnp.abs(apart)
        first = jnp.where(reach == 1, 45.0, jnp.where(reach == 2, -9.0, jnp.where(reach == 3, 1.0, 0.0)))
        first = jnp.where(apart < 0, -first, first).astype(BF16)
        second = jnp.where(
            reach == 0, -490.0, jnp.where(reach == 1, 270.0, jnp.where(reach == 2, -27.0, jnp.where(reach == 3, 2.0, 0.0)))
        ).astype(BF16)
        for part in range(2):
            band[part * COL : (part + 1) * COL, 0:COL] = first
            band[part * COL : (part + 1) * COL, COL : 2 * COL] = second
        weight_high, weight_low = split(jnp.concatenate([rows_mix[...], jnp.zeros((COL - LON, SLOTS), F32)], axis=0))
        rows_split[0:COL, :] = weight_high
        rows_split[COL : 2 * COL, :] = weight_high
        rows_split[2 * COL : 3 * COL, :] = weight_low

    def load_split(part, pair):
        block = jnp.concatenate(
            [frame[part, pl.ds(pl.multiple_of((8 * pair + q) * STRIDE + 8, 8), LON), :] for q in range(8)], axis=0
        )
        return split(block)

    def interpolate(part, half, chunk):
        high, low = load_split(part, CHUNKS * half + chunk)
        value = dot(jnp.concatenate([high, low, high], axis=1), mix[...])
        blocks[part, half, chunk] = jnp.sum(value.reshape(ROWS, LON, SLOTS) * rows_mix[...][None], axis=1)

    def send(part, half, chunk):
        for step in AROUND:
            a_copy(part, half, chunk, step).start()

        @pl.when(core != half)
        def _():
            s_copy(part, half, chunk).start()

        @pl.when(core == half)
        def _():
            table[part, chunk, member] = blocks[part, half, chunk]

    def lane_pass(part):
        for pair in range(FLAT // 8):
            high, low = load_split(part, pair)
            both = jnp.concatenate([high, low], axis=1)
            lanes[8 * LON * pair : 8 * LON * (pair + 1), :] = dot(both, band[...])

    def cols_of(part):
        lane = iota((LON, COL), 1)
        for half in range(2):
            edge = jnp.zeros((LON, COL), F32)
            for g in range(FLAT // 2):
                at = (half * (FLAT // 2) + g) * STRIDE + 8
                moved = pltpu.roll(frame[part, at : at + LON, :], 8 * g + HALO, 1)
                edge = jnp.where(jnp.logical_and(lane >= 8 * g, lane < 8 * g + 2 * HALO), moved, edge)
            turned[half, :, 0:LON] = jnp.transpose(edge)
        for side in range(2):
            for j in range(HALO):
                first = (1 - side) * HALO + j
                for half in range(2):
                    col_own[part, side, j, half * (FLAT // 2) : (half + 1) * (FLAT // 2), :] = turned[
                        half, pl.ds(first, FLAT // 2, stride=8), :
                    ]
            col_out[part, side, 0] = jnp.where(
                iota((FLAT, COL), 1) < COL // 2, col_own[part, side, 0], pltpu.roll(col_own[part, side, 1], COL // 2, 1)
            )
            col_out[part, side, 1] = col_own[part, side, 2]

    def emf_pass(part):
        for r in range(SHELLS):
            def field(q):
                at = (q * SHELLS + r) * STRIDE + 8
                return frame[part, at : at + LON, :]

            m, b = [field(MR + i) for i in range(3)], [field(BR + i) for i in range(3)]
            for i, form in enumerate((cross_radial, cross_polar, cross_azimuthal)):
                at = (i * SHELLS + r) * STRIDE + 8
                emf[at : at + LON, :] = form(m, b)
        for i, at in ((0, FLAT), (2, FLAT + SHELLS)):
            block = jnp.concatenate(
                [emf[(i * SHELLS + r) * STRIDE + 8 : (i * SHELLS + r) * STRIDE + 8 + LON, :] for r in range(SHELLS)],
                axis=0,
            )
            high, low = split(block)
            lanes[at * LON : (at + SHELLS) * LON, 0:COL] = dot(
                jnp.concatenate([high, low], axis=1), band[:, 0:COL]
            )

    def main_pass(part, start, stop):
        def body(block, carry):
            here = pl.multiple_of(8 * block, 8)

            def near(f, apart):
                return frame[part, pl.ds(f * STRIDE + 8 + here + apart, 8), :]

            def near_emf(f, apart):
                return emf[pl.ds(f * STRIDE + 8 + here + apart, 8), :]

            def lane_first(f):
                return lanes[pl.ds(f * LON + here, 8), 0:COL]

            def lane_second(f):
                return lanes[pl.ds(f * LON + here, 8), COL : 2 * COL]

            def row_first(at):
                return 45.0 * (at[1] - at[-1]) - 9.0 * (at[2] - at[-2]) + (at[3] - at[-3])

            def row_second(at, centre):
                return (
                    270.0 * (at[1] + at[-1]) - 27.0 * (at[2] + at[-2]) + 2.0 * (at[3] + at[-3]) - 490.0 * centre
                )

            centre = [[near(q * SHELLS + r, 0) for r in range(SHELLS)] for q in range(QUANTITIES)]
            steps = [shell_steps(x) for x in centre]
            radial, radial_second = [x[0] for x in steps], [x[1] for x in steps]
            emf_centre = [[near_emf(i * SHELLS + r, 0) for r in range(SHELLS)] for i in range(3)]
            emf_radial = [None, shell_steps(emf_centre[1])[0], shell_steps(emf_centre[2])[0]]
            for r in range(SHELLS):
                own = [centre[q][r] for q in range(QUANTITIES)]
                g, lap = [], []
                for q in range(QUANTITIES):
                    f = q * SHELLS + r
                    at = {d: near(f, d) for d in (-3, -2, -1, 1, 2, 3)}
                    g.append((radial[q][r], lane_first(f), scale * row_first(at)))
                    if q == S:
                        lap.append(None)
                    else:
                        lap.append(
                            radial_second[q][r] + lane_second(f) + (scale * scale) * row_second(at, own[q])
                        )
                m, b = own[MR:BR], own[BR:WARM]

                def advect(q):
                    return m[0] * g[q][0] + m[1] * g[q][1] + m[2] * g[q][2]

                div = g[MR][0] + g[MT][1] + g[MP][2]
                current = (g[BP][1] - g[BT][2], g[BR][2] - g[BP][0], g[BT][0] - g[BR][1])
                lorentz = (
                    current[1] * b[2] - current[2] * b[1],
                    current[2] * b[0] - current[0] * b[2],
                    current[0] * b[1] - current[1] * b[0],
                )
                grow, thin = jnp.exp(own[WARM]), jnp.exp(-own[S])
                emf_rows = {}
                for i in (0, 1):
                    f = i * SHELLS + r
                    emf_rows[i] = scale * row_first({d: near_emf(f, d) for d in (-3, -2, -1, 1, 2, 3)})
                turn = (
                    lane_first(FLAT + SHELLS + r) - emf_rows[1],
                    emf_rows[0] - emf_radial[2][r],
                    emf_radial[1][r] - lane_first(FLAT + r),
                )
                result = [-advect(S) - div]
                for i in range(3):
                    result.append(
                        -advect(MR + i) - grow * (g[S][i] + g[WARM][i]) + thin * lorentz[i] + SPREAD * lap[MR + i]
                    )
                for i in range(3):
                    result.append(turn[i] + SPREAD * lap[BR + i])
                result.append(-advect(WARM) - (2.0 / 3.0) * div + SPREAD * lap[WARM])
                for q in range(QUANTITIES):
                    f = q * SHELLS + r
                    value = own[q] + (TIME_STEP / 60.0) * result[q]
                    if part == 0:
                        frame[1, pl.ds(f * STRIDE + 8 + here, 8), :] = value
                    else:
                        start = frame[0, pl.ds(f * STRIDE + 8 + here, 8), :]
                        out_ref[pl.ds(f * LON + here, 8), :] = 0.5 * (start + value)
            return carry

        lax.fori_loop(start, stop, body, 0)

    def rows_of(part):
        for h in range(HALO):
            row_out[part, 0, h] = frame[part, pl.ds(8 + h, FLAT, stride=STRIDE), :]
            row_out[part, 1, h] = frame[part, pl.ds(8 + LON - HALO + h, FLAT, stride=STRIDE), :]

    def prepare_picks():
        for tile in range(2 * TILES):
            if tile < TARGETS:
                slot = idx_in[tile, 0:1, :]
            elif tile < TARGETS + 2:
                first = (tile - TARGETS) * GROUPS
                slot = idx_in[first, 1:2, :]
                for q in range(1, GROUPS):
                    slot = jnp.maximum(slot, pltpu.roll(idx_in[first + q], SPARE * q, 1)[1:2, :])
            else:
                side, h = divmod(tile - TARGETS - 2, HALO)
                slot = idx_in[side * (TARGETS - 1), 2 + h : 3 + h, :]
            slot = slot - mine * (GROUP * OUT)
            who = jnp.zeros_like(slot)
            for q in range(1, GROUP):
                who = who + jnp.where(slot >= q * OUT, 1, 0)
            cell = slot - who * OUT
            who = jnp.where(jnp.logical_and(slot >= 0, slot < GROUP * OUT), who, -1)
            at = (tile % 2) * COL
            owner[tile // 2, :, at : at + COL] = jnp.broadcast_to(who, (8, COL))
            hot = jnp.where(iota((SLOTS, COL), 0) == cell, 1.0, 0.0).astype(BF16)
            onehot[tile // 2, :, at : at + COL] = hot

    def split_table(part, chunk):
        high, low = split(table[part, chunk].reshape(GROUP * ROWS, SLOTS))
        return jnp.concatenate([high, low], axis=0)

    def product(both, tile):
        return dot(both, onehot[tile])

    def chosen(value, tile):
        value = value[0 : GROUP * ROWS] + value[GROUP * ROWS :]
        who = jnp.broadcast_to(owner[tile, 0:1, :], (ROWS, SLOTS))
        total = jnp.zeros((ROWS, SLOTS), F32)
        for q in range(GROUP):
            total = jnp.where(who == q, value[q * ROWS : (q + 1) * ROWS, :], total)
        return total[:, 0:COL], total[:, COL : 2 * COL]

    def fold(rests):
        turn = (lax.div(iota((8, COL), 1), SPARE) - iota((8, COL), 0)) & 7
        for half, rest in enumerate(rests):
            total = jnp.zeros((8, COL), F32)
            for d in range(8):
                moved = pltpu.roll(pltpu.roll(rest, SPARE * d, 1), 8 - d, 0) if d else rest
                total = jnp.where(turn == d, moved, total)
            rest_rows[half] = total

    def pick_all(part, chunk):
        both = split_table(part, chunk)
        sides = [(step + mine) & (TARGETS // 2 - 1) for step in range(TARGETS // 2)]
        extra = list(range(TARGETS // 2 + 1, TILES))
        ends, value = [], product(both, extra[0])
        for tile, after in zip(extra, extra[1:] + [None]):
            now = value
            if after is not None:
                value = product(both, after)
            ends += chosen(now, tile)
        for side in range(2):
            for h in range(HALO):
                picked_rows[part, chunk, side, h] = ends[side * HALO + h]
        for side in range(2):
            l_copy(part, chunk, side).start()

        @pl.when(col_edge)
        def _():
            now, value = product(both, TARGETS // 2), product(both, sides[0])
            fold(chosen(now, TARGETS // 2))
            for step, tile in enumerate(sides):
                now = value
                if step + 1 < len(sides):
                    value = product(both, sides[step + 1])
                for i, end in enumerate(chosen(now, tile)):
                    target = 2 * tile + i
                    picked[part, chunk, target, 0:ROWS, :] = end
                    picked[part, chunk, target, ROWS : ROWS + 1, :] = rest_rows[
                        tile >> 2, pl.ds(target & (GROUPS - 1), 1), :
                    ]
                for i in range(2):
                    b_copy(part, chunk, 2 * tile + i).start()

    def corrections(part, side, along_lanes):
        halo_ref, own_ref, add_ref = (col_halo, col_own, col_add) if along_lanes else (row_halo, row_out, row_add)

        def scaled(value, power):
            for _ in range(0 if along_lanes else power):
                value = scale * value
            return value

        halo = [[halo_ref[side, h, q * SHELLS : (q + 1) * SHELLS, :] for q in range(QUANTITIES)] for h in range(HALO)]
        form = cross_azimuthal if along_lanes else cross_polar
        halo_emf = [(cross_radial(x[MR:BR], x[BR:WARM]), form(x[MR:BR], x[BR:WARM])) for x in halo]
        sign = -1.0 if side == 0 else 1.0
        firsts, seconds = (45.0 * sign, -9.0 * sign, sign), (270.0, -27.0, 2.0)
        for j in range(HALO):
            own = [own_ref[part, side, j, q * SHELLS : (q + 1) * SHELLS, :] for q in range(QUANTITIES)]

            def total(weights, of):
                result = None
                for m in (1, 2, 3):
                    h = j + 3 - m if side == 0 else m - 3 + j
                    if 0 <= h < HALO:
                        term = weights[m - 1] * of(h)
                        result = term if result is None else result + term
                return result

            d = [scaled(total(firsts, lambda h, q=q: halo[h][q]), 1) for q in range(QUANTITIES)]
            lap = [
                None if q == S else scaled(total(seconds, lambda h, q=q: halo[h][q]), 2) for q in range(QUANTITIES)
            ]
            radial = scaled(total(firsts, lambda h: halo_emf[h][0]), 1)
            second = scaled(total(firsts, lambda h: halo_emf[h][1]), 1)
            result = edge_rates(own, d, lap, second, radial, along_lanes)
            for q in range(QUANTITIES):
                add_ref[side, j, q * SHELLS : (q + 1) * SHELLS, :] = (TIME_STEP / 60.0 / (1 + part)) * result[q]

    def contribute(side, along_lanes):
        add_ref = col_add if along_lanes else row_add
        value = jnp.concatenate([add_ref[side, j] for j in range(HALO)], axis=0)
        if along_lanes:
            value = jnp.where(iota((HALO * FLAT, COL), 1) < LON, value, 0.0)
        high, low = split(value)
        value = dot(jnp.concatenate([high, low, high], axis=1), rows_split[...] if along_lanes else mix[...])
        total = jnp.zeros((FLAT, SLOTS), F32)
        for j in range(HALO):
            if along_lanes:
                at = j if side == 0 else COL - HALO + j
                weight = cols_mix[at : at + 1, :]
            else:
                at = j if side == 0 else LON - HALO + j
                weight = rows_mix[at : at + 1, :]
            total = total + weight * value[j * FLAT : (j + 1) * FLAT, :]
        for half in range(2):
            for chunk in range(CHUNKS):
                at = half * PART + ROWS * chunk
                blocks[1, half, chunk] = blocks[1, half, chunk] + total[at : at + ROWS, :]

    def apply_edges():
        for side in range(2):
            for j in range(HALO):
                rows = pl.ds(8 + (j if side == 0 else LON - HALO + j), FLAT, stride=STRIDE)
                frame[1, rows, :] = frame[1, rows, :] + row_add[side, j]
        turn_edges(col_add, turned)
        for half in range(2):
            edge = jnp.transpose(turned[half])[0:LON, :]
            for g in range(FLAT // 2):
                at = (half * (FLAT // 2) + g) * STRIDE + 8
                frame[1, at : at + LON, :] = frame[1, at : at + LON, :] + field_edge(edge, g)

    def a_copy(part, half, chunk, step):
        return remote(
            blocks.at[part, half, chunk], table.at[part, chunk, member], a_send.at[part, half, chunk, step],
            a_recv.at[part, chunk, member], row_device(step, half),
        )

    def s_copy(part, half, chunk):
        return remote(
            blocks.at[part, half, chunk], table.at[part, chunk, member], s_send.at[part, chunk],
            a_recv.at[part, chunk, member], sibling,
        )

    def a_arrival(part, chunk, step):
        there = (member + step) & (GROUP - 1)
        return remote(
            blocks.at[part, 0, chunk], table.at[part, chunk, there], s_send.at[part, chunk],
            a_recv.at[part, chunk, there], sibling,
        )

    def b_copy(part, chunk, target):
        return remote(
            picked.at[part, chunk, target], got_cols.at[part, chunk, origin], b_send.at[part, chunk, target],
            b_recv.at[part, chunk, origin], target_device(target),
        )

    def b_arrival(part, chunk, source):
        return remote(
            picked.at[part, chunk, 0], got_cols.at[part, chunk, source], b_send.at[part, chunk, 0],
            b_recv.at[part, chunk, source], (other, lon, col),
        )

    def l_copy(part, chunk, side):
        return remote(
            picked_rows.at[part, chunk, side], got_rows.at[part, chunk, origin], l_send.at[part, chunk, side],
            l_recv.at[part, chunk, origin], target_device(side * (TARGETS - 1)),
        )

    def l_arrival(part, chunk, source):
        return remote(
            picked_rows.at[part, chunk, 0], got_rows.at[part, chunk, source], l_send.at[part, chunk, 0],
            l_recv.at[part, chunk, source], (other, lon, col),
        )

    def row_copy(part, side):
        return remote(
            row_out.at[part, 1 - side], row_in.at[part, side], r_send.at[part, side], r_recv.at[part, side],
            (panel, lon_up if side == 0 else lon_down, col),
        )

    def col_copy(part, side):
        return remote(
            col_out.at[part, 1 - side], col_in.at[part, side], c_send.at[part, side], c_recv.at[part, side],
            (panel, lon, col_up if side == 0 else col_down),
        )

    def idx_copy(target):
        return remote(
            idx_out, idx_in.at[origin], idx_send.at[target], idx_recv.at[origin], target_device(target)
        )

    def idx_arrival(source):
        return remote(idx_out, idx_in.at[source], idx_send.at[0], idx_recv.at[source], (other, lon, col))

    def inner_sides(part):
        for side in range(2):
            @pl.when(lon != (0 if side == 0 else n_lon - 1))
            def _():
                row_copy(part, side).wait_recv()
                row_halo[side] = row_in[part, side]
                corrections(part, side, False)
                if part == 0:
                    contribute(side, False)

            @pl.when(col != (0 if side == 0 else n_col - 1))
            def _():
                col_copy(part, side).wait_recv()
                pair = col_in[part, side, 0]
                col_halo[side, 0] = pair
                col_halo[side, 1] = pltpu.roll(pair, COL // 2, 1)
                col_halo[side, 2] = col_in[part, side, 1]
                corrections(part, side, True)
                if part == 0:
                    contribute(side, True)

    def outer_sides(part):
        for side in range(2):

            @pl.when(col == (0 if side == 0 else n_col - 1))
            def _():
                row, lane = iota((8, COL), 0), iota((8, COL), 1)
                for chunk in range(CHUNKS):
                    for source in range(TARGETS):
                        b_arrival(part, chunk, source).wait_recv()
                    for half in range(2):
                        total = got_cols[part, chunk, half * GROUPS]
                        for group in range(1, GROUPS):
                            total = total + got_cols[part, chunk, half * GROUPS + group]
                        main = total[0:ROWS]
                        at = half * PART + ROWS * chunk
                        col_halo[side, 0, at : at + ROWS, :] = main
                        col_halo[side, 1, at : at + ROWS, :] = pltpu.roll(main, COL - LON, 1)
                        value = pltpu.roll(main, COL - 2 * LON, 1)
                        rest = jnp.broadcast_to(total[ROWS : ROWS + 1], (ROWS, COL))
                        for q in range(ROWS):
                            moved = pltpu.roll(rest, (2 * COL - 2 * LON - SPARE * q) % COL, 1)
                            value = jnp.where(jnp.logical_and(row == q, lane >= COL - 2 * LON), moved, value)
                        col_halo[side, 2, at : at + ROWS, :] = value
                corrections(part, side, True)
                if part == 0:
                    contribute(side, True)

            @pl.when(lon == (0 if side == 0 else n_lon - 1))
            def _():
                for chunk in range(CHUNKS):
                    for source in range(TARGETS):
                        l_arrival(part, chunk, source).wait_recv()
                    for half in range(2):
                        total = got_rows[part, chunk, half * GROUPS]
                        for group in range(1, GROUPS):
                            total = total + got_rows[part, chunk, half * GROUPS + group]
                        at = half * PART + ROWS * chunk
                        row_halo[side, :, at : at + ROWS, :] = total
                corrections(part, side, False)
                if part == 0:
                    contribute(side, False)

    for part in range(2):
        if part == 0:
            message_tables()
            copies[3].wait()
            interpolate(0, 0, 0)
            pl.semaphore_wait(barrier, 2 * len(AROUND) + 2 + TARGETS)
            for target in range(TARGETS):
                idx_copy(target).start()
            send(0, 0, 0)
            copies[4].wait()
            for half, chunk in ((1, 0), (0, 1), (1, 1)):
                interpolate(0, half, chunk)
                send(0, half, chunk)
            other_tables()
        else:
            for chunk in range(CHUNKS):
                for half in range(2):
                    send(1, half, chunk)
            apply_edges()
        rows_of(part)
        for side in range(2):

            @pl.when(sends_rows[side])
            def _():
                row_copy(part, side).start()

        cols_of(part)
        for side in range(2):

            @pl.when(sends_cols[side])
            def _():
                col_copy(part, side).start()

        lane_pass(part)
        emf_pass(part)
        if part == 0:
            for source in range(TARGETS):
                idx_arrival(source).wait_recv()
            prepare_picks()
        for chunk in range(CHUNKS):
            for step in range(1, GROUP):
                a_arrival(part, chunk, step).wait_recv()
            pick_all(part, chunk)
        main_pass(part, 0, 6)
        if part == 0:
            for half in range(2):
                for chunk in range(CHUNKS):
                    interpolate(1, half, chunk)
        inner_sides(part)
        outer_sides(part)

    for target in range(TARGETS):
        idx_copy(target).wait_send()
    for part in range(2):
        for chunk in range(CHUNKS):
            for half in range(2):
                for step in AROUND:
                    a_copy(part, half, chunk, step).wait_send()
            s_copy(part, 0, chunk).wait_send()
            for side in range(2):
                l_copy(part, chunk, side).wait_send()

            @pl.when(col_edge)
            def _():
                for target in range(TARGETS):
                    b_copy(part, chunk, target).wait_send()

        for side in range(2):

            @pl.when(sends_rows[side])
            def _():
                row_copy(part, side).wait_send()

            @pl.when(sends_cols[side])
            def _():
                col_copy(part, side).wait_send()


def shards(state, send_base, send_frac, recv_slots):
    rows = FLAT * LON
    dma = pltpu.SemaphoreType.DMA
    vmem = pltpu.VMEM
    scratch = [
        vmem((2, FLAT, STRIDE, COL), F32),
        vmem((1, OUT), I32),
        vmem((2, OUT), F32),
        vmem((1, recv_slots.shape[-1]), I32),
        vmem((3 * SHELLS * STRIDE, COL), F32),
        vmem(((FLAT + 2 * SHELLS) * LON, 2 * COL), F32),
        vmem((3 * COL, SLOTS), BF16),
        vmem((COL, SLOTS), F32),
        vmem((LON, SLOTS), F32),
        vmem((3 * COL, SLOTS), BF16),
        vmem((2 * COL, 2 * COL), BF16),
        vmem((TILES, SLOTS, 2 * COL), BF16),
        vmem((TILES, 8, 2 * COL), I32),
        vmem((2, COL, COL), F32),
        vmem((2, 2, CHUNKS, ROWS, SLOTS), F32),
        vmem((2, CHUNKS, GROUP, ROWS, SLOTS), F32),
        vmem((8, COL), I32),
        vmem((TARGETS, 8, COL), I32),
        vmem((2, ROWS, COL), F32),
        vmem((2, CHUNKS, TARGETS, ROWS + 1, COL), F32),
        vmem((2, CHUNKS, 2, HALO, ROWS, COL), F32),
        vmem((2, CHUNKS, TARGETS, ROWS + 1, COL), F32),
        vmem((2, CHUNKS, TARGETS, HALO, ROWS, COL), F32),
        vmem((2, 2, HALO, FLAT, COL), F32),
        vmem((2, 2, HALO, FLAT, COL), F32),
        vmem((2, 2, HALO, FLAT, COL), F32),
        vmem((2, 2, 2, FLAT, COL), F32),
        vmem((2, 2, 2, FLAT, COL), F32),
        vmem((2, HALO, FLAT, COL), F32),
        vmem((2, HALO, FLAT, COL), F32),
        dma((5,)),
        dma((TARGETS,)),
        dma((TARGETS,)),
        dma((2, 2, CHUNKS, RING)),
        dma((2, CHUNKS, GROUP)),
        dma((2, CHUNKS)),
        dma((2, CHUNKS, TARGETS)),
        dma((2, CHUNKS, TARGETS)),
        dma((2, CHUNKS, 2)),
        dma((2, CHUNKS, TARGETS)),
        dma((2, 2)),
        dma((2, 2)),
        dma((2, 2)),
        dma((2, 2)),
    ]
    edges = jax.ShapeDtypeStruct((2, HALO, FLAT, COL), F32)
    value, row_add, col_add = pl.pallas_call(
        kernel,
        out_shape=(jax.ShapeDtypeStruct((rows, COL), F32), edges, edges),
        in_specs=[pl.BlockSpec(memory_space=pltpu.HBM)] * 4,
        out_specs=[pl.BlockSpec(memory_space=pltpu.VMEM)] * 3,
        scratch_shapes=scratch,
        compiler_params=pltpu.CompilerParams(
            collective_id=0, has_side_effects=True, vmem_limit_bytes=40 * 1024 * 1024
        ),
    )(*(
        pltpu.with_memory_space_constraint(x, pltpu.HBM)
        for x in (state.reshape(FLAT, LON, COL), send_base[0], send_frac[0, 0], recv_slots[0])
    ))
    result = pl.pallas_call(
        closing,
        out_shape=jax.ShapeDtypeStruct((rows, COL), F32),
        in_specs=[pl.BlockSpec(memory_space=pltpu.VMEM)] * 3,
        out_specs=pl.BlockSpec(memory_space=pltpu.HBM),
        scratch_shapes=[vmem((2, COL, COL), F32), vmem((rows, COL), F32), dma((4,))],
        compiler_params=pltpu.CompilerParams(vmem_limit_bytes=16 * 1024 * 1024),
    )(value, row_add, col_add)
    return result.reshape(state.shape)


def solution(mesh):
    placed = (
        P("panel", None, None, "lon", "colat"),
        P("panel", ("lon", "colat"), None),
        P("panel", ("lon", "colat"), None, None),
        P("panel", ("lon", "colat"), None),
    )
    return jax.shard_map(
        shards,
        mesh=mesh,
        in_specs=placed,
        out_specs=P("panel", None, None, "lon", "colat"),
        check_vma=False,
    )
```

```python
import math

import jax
import jax.numpy as jnp
from jax import lax
from jax.experimental import pallas as pl
from jax.experimental.pallas import tpu as pltpu
from jax.sharding import PartitionSpec as P

MESH = pl.DeviceIdType.MESH
F32, BF16, I32 = jnp.float32, jnp.bfloat16, jnp.int32

QUANTITIES = 8
SHELLS = 4
FLAT = QUANTITIES * SHELLS
LON = 48
COL = 128
HALO = 3
OUT = 240
SIDE = HALO * LON
SLOTS = 256
GROUP = 8
GROUPS = 8
AROUND = (1, 3, 2)
SPARE = SIDE - COL
PART = FLAT // 2
TARGETS = 2 * GROUPS
TILES = 12
RING = 4
FOLD = PART // 8
STRIDE = LON + 16
TIME_STEP = 0.25
SPREAD = 0.1 / 3.0
S, MR, MT, MP, BR, BT, BP, WARM = range(QUANTITIES)


def dot(left, right):
    return jnp.dot(left, right, preferred_element_type=F32)


def split(value):
    high = value.astype(BF16)
    return high, (value - high.astype(F32)).astype(BF16)


def iota(shape, dim):
    return lax.broadcasted_iota(I32, shape, dim)


def cross_radial(m, b):
    return m[1] * b[2] - m[2] * b[1]


def cross_polar(m, b):
    return m[2] * b[0] - m[0] * b[2]


def cross_azimuthal(m, b):
    return m[0] * b[1] - m[1] * b[0]


def edge_rates(own, d, lap, emf_first, emf_second, along_lanes):
    grow, thin = jnp.exp(own[WARM]), jnp.exp(-own[S])
    b = own[BR:WARM]
    if along_lanes:
        vel, out = own[MT], MT
        lorentz = (d[BR] * b[1], -d[BR] * b[0] - d[BP] * b[2], d[BP] * b[1])
        turn = (emf_first, None, -emf_second)
    else:
        vel, out = own[MP], MP
        lorentz = (d[BR] * b[2], d[BT] * b[2], -d[BT] * b[1] - d[BR] * b[0])
        turn = (-emf_first, emf_second, None)
    result = [-vel * d[S] - d[out]]
    for i in range(3):
        rate = -vel * d[MR + i] + thin * lorentz[i] + SPREAD * lap[MR + i]
        if MR + i == out:
            rate = rate - grow * (d[S] + d[WARM])
        result.append(rate)
    for i in range(3):
        rate = SPREAD * lap[BR + i]
        result.append(rate if turn[i] is None else rate + turn[i])
    result.append(-vel * d[WARM] - (2.0 / 3.0) * d[out] + SPREAD * lap[WARM])
    return result


def shell_steps(x):
    a, b, c = x[1] - x[0], x[2] - x[0], x[3] - x[0]
    p, q, r = 45.0 * a, 45.0 * b, 37.0 * c
    first = (p - 9.0 * b + c, q - 8.0 * c, r - p, r - q + 9.0 * a)
    p, q, r = 270.0 * a, 270.0 * b, 245.0 * c
    second = (p - 27.0 * b + 2.0 * c, q - 490.0 * a - 25.0 * c, p - 490.0 * b + r, q - 27.0 * a - r)
    return first, second


def turn_edges(col_add, turned):
    for side in range(2):
        for j in range(HALO):
            for half in range(2):
                turned[half, pl.ds((1 - side) * HALO + j, FLAT // 2, stride=8), :] = col_add[
                    side, j, half * (FLAT // 2) : (half + 1) * (FLAT // 2), :
                ]


def field_edge(edge, g):
    lane = iota((LON, COL), 1)
    border = jnp.logical_or(lane < HALO, lane >= COL - HALO)
    return jnp.where(border, pltpu.roll(edge, COL - 8 * g - HALO, 1), 0.0)


def closing(value_ref, row_add, col_add, out_hbm, turned, ready, sem):
    turn_edges(col_add, turned)
    copies = []
    for half in range(2):
        edge = jnp.transpose(turned[half])[0:LON, :]
        for chunk in range(4):
            first = half * (FLAT // 2) + 4 * chunk
            for q in range(4):
                at = (first + q) * LON
                ready[at : at + LON, :] = value_ref[at : at + LON, :] + field_edge(edge, 4 * chunk + q)
            for side in range(2):
                for j in range(HALO):
                    rows = pl.ds(first * LON + (j if side == 0 else LON - HALO + j), 4, stride=LON)
                    ready[rows, :] = ready[rows, :] + row_add[side, j, first : first + 4, :]
            rows = pl.ds(first * LON, 4 * LON)
            copy = pltpu.make_async_copy(ready.at[rows, :], out_hbm.at[rows, :], sem.at[4 * half + chunk])
            copy.start()
            copies.append(copy)
    for copy in copies:
        copy.wait()


def kernel(
    x_hbm, base_hbm, frac_hbm, slots_hbm, out_ref, row_add, col_add,
    deep, base_ref, frac_ref, slots_ref, emf, lanes, mix, cols_mix, rows_mix, rows_split, band, onehot, owner, turned,
    blocks, table, idx_out, idx_in, rest_rows, picked, picked_rows, got_cols, got_rows, row_out, row_in, col_own, col_out, col_in,
    row_halo, col_halo,
    in_sem, idx_send, idx_recv, a_send, a_recv, s_send, b_send, b_recv, l_send, l_recv, r_send, r_recv, c_send, c_recv,
):
    panel, lon, col = lax.axis_index("panel"), lax.axis_index("lon"), lax.axis_index("colat")
    n_lon, n_col = lax.axis_size("lon"), lax.axis_size("colat")
    core, mine = lon & 1, lon >> 1
    member = core * n_col + col
    other = 1 - panel
    lon_up, lon_down = lax.rem(lon + 1, n_lon), lax.rem(lon + n_lon - 1, n_lon)
    col_up, col_down = lax.rem(col + 1, n_col), lax.rem(col + n_col - 1, n_col)
    outer = lax.rem(lon + 2 * core - 1 + n_lon, n_lon)
    sends_rows = (lon < n_lon - 1, lon > 0)
    sends_cols = (col < n_col - 1, col > 0)
    col_edge = jnp.logical_or(col == 0, col == n_col - 1)

    sibling = (panel, lon + 1 - 2 * core, col)
    origin = core * GROUPS + mine

    def row_device(step, half):
        return (panel, 2 * mine + half, (col + step) & (n_col - 1))

    def target_device(target):
        return (other, 2 * (target & (GROUPS - 1)) + (target >> 3), col)

    def remote(src, dst, send, recv, device):
        return pltpu.make_async_remote_copy(
            src_ref=src, dst_ref=dst, send_sem=send, recv_sem=recv, device_id=device, device_id_type=MESH
        )

    frame = deep.reshape(2, FLAT * STRIDE, COL)
    copies = [
        pltpu.make_async_copy(src, dst, in_sem.at[i])
        for i, (src, dst) in enumerate(
            (
                (frac_hbm, frac_ref),
                (base_hbm, base_ref),
                (slots_hbm, slots_ref),
                (x_hbm.at[pl.ds(0, PART)], deep.at[0, pl.ds(0, PART), pl.ds(8, LON), :]),
                (x_hbm.at[pl.ds(PART, PART)], deep.at[0, pl.ds(PART, PART), pl.ds(8, LON), :]),
            )
        )
    ]
    for copy in copies:
        copy.start()

    barrier = pltpu.get_barrier_semaphore()
    for step in AROUND:
        for half in range(2):
            pl.semaphore_signal(barrier, inc=1, device_id=row_device(step, half), device_id_type=MESH)
    pl.semaphore_signal(barrier, inc=1, device_id=sibling, device_id_type=MESH)
    for target in range(TARGETS):
        pl.semaphore_signal(barrier, inc=1, device_id=target_device(target), device_id_type=MESH)
    pl.semaphore_signal(barrier, inc=1, device_id=(panel, outer, col), device_id_type=MESH)

    copies[0].wait()
    copies[1].wait()
    base = jnp.concatenate([base_ref[...], jnp.zeros((1, SLOTS - OUT), I32)], axis=1)
    base_row, base_col = lax.div(base, COL), lax.rem(base, COL)
    share = jnp.concatenate([frac_ref[...], jnp.zeros((2, SLOTS - OUT), F32)], axis=1)
    along, across = share[0:1, :], share[1:2, :]
    cells = iota((COL, SLOTS), 0)
    weight = jnp.where(cells == base_col, 1.0 - across, 0.0) + jnp.where(cells == base_col + 1, across, 0.0)
    weight_high, weight_low = split(weight)
    cols_mix[...] = weight
    mix[0:COL, :] = weight_high
    mix[COL : 2 * COL, :] = weight_high
    mix[2 * COL : 3 * COL, :] = weight_low
    cells = iota((LON, SLOTS), 0)
    weight = jnp.where(cells == base_row, 1.0 - along, 0.0) + jnp.where(cells == base_row + 1, along, 0.0)
    rows_mix[...] = weight
    place = (col * COL + iota((1, COL), 1)).astype(F32)
    scale = 1.0 / jnp.sin(math.pi / 4.0 + (place + 0.5) * (math.pi / 2.0 / (COL * n_col)))

    def message_tables():
        copies[2].wait()
        spot = iota((1, SLOTS), 1)
        sides = jnp.where(spot < SIDE, jnp.maximum(slots_ref[:, 0:SLOTS], slots_ref[:, SIDE : SIDE + SLOTS]) + 1, 0)
        digits = jnp.concatenate([lax.div(sides, COL), lax.rem(sides, COL), jnp.zeros((6, SLOTS), I32)], axis=0)
        source, target = iota((SLOTS, SLOTS), 0), iota((SLOTS, SLOTS), 1)
        layer = jnp.where(target >= LON, 1, 0) + jnp.where(target >= 2 * LON, 1, 0)
        order = jnp.logical_and(target < SIDE, source == HALO * (target - LON * layer) + layer)
        digits = dot(digits.astype(F32).astype(BF16), jnp.where(order, 1.0, 0.0).astype(BF16)).astype(I32)
        sides = digits[0:1, :] * COL + digits[1:2, :] - 1
        idx_out[0:1, :] = sides[:, 0:COL]
        idx_out[1:2, :] = sides[:, COL : 2 * COL]
        for h in range(HALO):
            at = 2 * SIDE + h * COL
            idx_out[2 + h : 3 + h, :] = jnp.maximum(
                slots_ref[:, at : at + COL], slots_ref[:, at + HALO * COL : at + HALO * COL + COL]
            )
        idx_out[5:8, :] = jnp.full((3, COL), -1, I32)

    def other_tables():
        zero_rows = jnp.zeros((8, COL), F32)
        for f in range(FLAT):
            for part in range(2):
                frame[part, f * STRIDE : f * STRIDE + 8, :] = zero_rows
                frame[part, f * STRIDE + 8 + LON : (f + 1) * STRIDE, :] = zero_rows
        for f in range(3 * SHELLS):
            emf[f * STRIDE : f * STRIDE + 8, :] = zero_rows
            emf[f * STRIDE + 8 + LON : (f + 1) * STRIDE, :] = zero_rows

        for half in range(2):
            turned[half, :, :] = jnp.zeros((COL, COL), F32)

        apart = iota((COL, COL), 0) - iota((COL, COL), 1)
        reach = jnp.abs(apart)
        first = jnp.where(reach == 1, 45.0, jnp.where(reach == 2, -9.0, jnp.where(reach == 3, 1.0, 0.0)))
        first = jnp.where(apart < 0, -first, first).astype(BF16)
        second = jnp.where(
            reach == 0, -490.0, jnp.where(reach == 1, 270.0, jnp.where(reach == 2, -27.0, jnp.where(reach == 3, 2.0, 0.0)))
        ).astype(BF16)
        for part in range(2):
            band[part * COL : (part + 1) * COL, 0:COL] = first
            band[part * COL : (part + 1) * COL, COL : 2 * COL] = second
        weight_high, weight_low = split(jnp.concatenate([rows_mix[...], jnp.zeros((COL - LON, SLOTS), F32)], axis=0))
        rows_split[0:COL, :] = weight_high
        rows_split[COL : 2 * COL, :] = weight_high
        rows_split[2 * COL : 3 * COL, :] = weight_low

    def load_split(part, pair):
        block = jnp.concatenate(
            [frame[part, pl.ds(pl.multiple_of((8 * pair + q) * STRIDE + 8, 8), LON), :] for q in range(8)], axis=0
        )
        return split(block)

    def interpolate(part, half):
        for pair in range(PART // 8):
            high, low = load_split(part, 2 * half + pair)
            value = dot(jnp.concatenate([high, low, high], axis=1), mix[...])
            value = jnp.sum(value.reshape(8, LON, SLOTS) * rows_mix[...][None], axis=1)
            blocks[part, half, 8 * pair : 8 * pair + 8, :] = value

    def send(part, half):
        for step in AROUND:
            a_copy(part, step, half).start()

        @pl.when(core != half)
        def _():
            s_copy(part, half).start()

        @pl.when(core == half)
        def _():
            table[part, member] = blocks[part, half]

    def lane_pass(part):
        for pair in range(FLAT // 8):
            high, low = load_split(part, pair)
            both = jnp.concatenate([high, low], axis=1)
            lanes[8 * LON * pair : 8 * LON * (pair + 1), :] = dot(both, band[...])

    def cols_of(part):
        lane = iota((LON, COL), 1)
        for half in range(2):
            edge = jnp.zeros((LON, COL), F32)
            for g in range(FLAT // 2):
                at = (half * (FLAT // 2) + g) * STRIDE + 8
                moved = pltpu.roll(frame[part, at : at + LON, :], 8 * g + HALO, 1)
                edge = jnp.where(jnp.logical_and(lane >= 8 * g, lane < 8 * g + 2 * HALO), moved, edge)
            turned[half, :, 0:LON] = jnp.transpose(edge)
        for side in range(2):
            for j in range(HALO):
                first = (1 - side) * HALO + j
                for half in range(2):
                    col_own[part, side, j, half * (FLAT // 2) : (half + 1) * (FLAT // 2), :] = turned[
                        half, pl.ds(first, FLAT // 2, stride=8), :
                    ]
            col_out[part, side, 0] = jnp.where(
                iota((FLAT, COL), 1) < COL // 2, col_own[part, side, 0], pltpu.roll(col_own[part, side, 1], COL // 2, 1)
            )
            col_out[part, side, 1] = col_own[part, side, 2]

    def emf_pass(part):
        for r in range(SHELLS):
            def field(q):
                at = (q * SHELLS + r) * STRIDE + 8
                return frame[part, at : at + LON, :]

            m, b = [field(MR + i) for i in range(3)], [field(BR + i) for i in range(3)]
            for i, form in enumerate((cross_radial, cross_polar, cross_azimuthal)):
                at = (i * SHELLS + r) * STRIDE + 8
                emf[at : at + LON, :] = form(m, b)
        for i, at in ((0, FLAT), (2, FLAT + SHELLS)):
            block = jnp.concatenate(
                [emf[(i * SHELLS + r) * STRIDE + 8 : (i * SHELLS + r) * STRIDE + 8 + LON, :] for r in range(SHELLS)],
                axis=0,
            )
            high, low = split(block)
            lanes[at * LON : (at + SHELLS) * LON, 0:COL] = dot(
                jnp.concatenate([high, low], axis=1), band[:, 0:COL]
            )

    def main_pass(part, start, stop):
        def body(block, carry):
            here = pl.multiple_of(8 * block, 8)

            def near(f, apart):
                return frame[part, pl.ds(f * STRIDE + 8 + here + apart, 8), :]

            def near_emf(f, apart):
                return emf[pl.ds(f * STRIDE + 8 + here + apart, 8), :]

            def lane_first(f):
                return lanes[pl.ds(f * LON + here, 8), 0:COL]

            def lane_second(f):
                return lanes[pl.ds(f * LON + here, 8), COL : 2 * COL]

            def row_first(at):
                return 45.0 * (at[1] - at[-1]) - 9.0 * (at[2] - at[-2]) + (at[3] - at[-3])

            def row_second(at, centre):
                return (
                    270.0 * (at[1] + at[-1]) - 27.0 * (at[2] + at[-2]) + 2.0 * (at[3] + at[-3]) - 490.0 * centre
                )

            centre = [[near(q * SHELLS + r, 0) for r in range(SHELLS)] for q in range(QUANTITIES)]
            steps = [shell_steps(x) for x in centre]
            radial, radial_second = [x[0] for x in steps], [x[1] for x in steps]
            emf_centre = [[near_emf(i * SHELLS + r, 0) for r in range(SHELLS)] for i in range(3)]
            emf_radial = [None, shell_steps(emf_centre[1])[0], shell_steps(emf_centre[2])[0]]
            for r in range(SHELLS):
                own = [centre[q][r] for q in range(QUANTITIES)]
                g, lap = [], []
                for q in range(QUANTITIES):
                    f = q * SHELLS + r
                    at = {d: near(f, d) for d in (-3, -2, -1, 1, 2, 3)}
                    g.append((radial[q][r], lane_first(f), scale * row_first(at)))
                    if q == S:
                        lap.append(None)
                    else:
                        lap.append(
                            radial_second[q][r] + lane_second(f) + (scale * scale) * row_second(at, own[q])
                        )
                m, b = own[MR:BR], own[BR:WARM]

                def advect(q):
                    return m[0] * g[q][0] + m[1] * g[q][1] + m[2] * g[q][2]

                div = g[MR][0] + g[MT][1] + g[MP][2]
                current = (g[BP][1] - g[BT][2], g[BR][2] - g[BP][0], g[BT][0] - g[BR][1])
                lorentz = (
                    current[1] * b[2] - current[2] * b[1],
                    current[2] * b[0] - current[0] * b[2],
                    current[0] * b[1] - current[1] * b[0],
                )
                grow, thin = jnp.exp(own[WARM]), jnp.exp(-own[S])
                emf_rows = {}
                for i in (0, 1):
                    f = i * SHELLS + r
                    emf_rows[i] = scale * row_first({d: near_emf(f, d) for d in (-3, -2, -1, 1, 2, 3)})
                turn = (
                    lane_first(FLAT + SHELLS + r) - emf_rows[1],
                    emf_rows[0] - emf_radial[2][r],
                    emf_radial[1][r] - lane_first(FLAT + r),
                )
                result = [-advect(S) - div]
                for i in range(3):
                    result.append(
                        -advect(MR + i) - grow * (g[S][i] + g[WARM][i]) + thin * lorentz[i] + SPREAD * lap[MR + i]
                    )
                for i in range(3):
                    result.append(turn[i] + SPREAD * lap[BR + i])
                result.append(-advect(WARM) - (2.0 / 3.0) * div + SPREAD * lap[WARM])
                for q in range(QUANTITIES):
                    f = q * SHELLS + r
                    value = own[q] + (TIME_STEP / 60.0) * result[q]
                    if part == 0:
                        frame[1, pl.ds(f * STRIDE + 8 + here, 8), :] = value
                    else:
                        start = frame[0, pl.ds(f * STRIDE + 8 + here, 8), :]
                        out_ref[pl.ds(f * LON + here, 8), :] = 0.5 * (start + value)
            return carry

        lax.fori_loop(start, stop, body, 0)

    def rows_of(part):
        for h in range(HALO):
            row_out[part, 0, h] = frame[part, pl.ds(8 + h, FLAT, stride=STRIDE), :]
            row_out[part, 1, h] = frame[part, pl.ds(8 + LON - HALO + h, FLAT, stride=STRIDE), :]

    def prepare_picks():
        for tile in range(2 * TILES):
            if tile < TARGETS:
                slot = idx_in[tile, 0:1, :]
            elif tile < TARGETS + 2:
                first = (tile - TARGETS) * GROUPS
                slot = idx_in[first, 1:2, :]
                for q in range(1, GROUPS):
                    slot = jnp.maximum(slot, pltpu.roll(idx_in[first + q], SPARE * q, 1)[1:2, :])
            else:
                side, h = divmod(tile - TARGETS - 2, HALO)
                slot = idx_in[side * (TARGETS - 1), 2 + h : 3 + h, :]
            slot = slot - mine * (GROUP * OUT)
            who = jnp.zeros_like(slot)
            for q in range(1, GROUP):
                who = who + jnp.where(slot >= q * OUT, 1, 0)
            cell = slot - who * OUT
            who = jnp.where(jnp.logical_and(slot >= 0, slot < GROUP * OUT), who, -1)
            at = (tile % 2) * COL
            owner[tile // 2, :, at : at + COL] = jnp.broadcast_to(who, (8, COL))
            hot = jnp.where(iota((SLOTS, COL), 0) == cell, 1.0, 0.0).astype(BF16)
            onehot[tile // 2, :, at : at + COL] = hot

    def table_split(part):
        high, low = split(table[part].reshape(GROUP * PART, SLOTS))
        return jnp.concatenate([high, low], axis=0)

    def product(both, tile):
        return dot(both, onehot[tile])

    def chosen(value, tile):
        value = value[0 : GROUP * PART] + value[GROUP * PART :]
        who = jnp.broadcast_to(owner[tile, 0:1, :], (PART, SLOTS))
        total = jnp.zeros((PART, SLOTS), F32)
        for q in range(GROUP):
            total = jnp.where(who == q, value[q * PART : (q + 1) * PART, :], total)
        return total[:, 0:COL], total[:, COL : 2 * COL]

    def fold(rests):
        turn = (lax.div(iota((8, COL), 1), SPARE) - iota((8, COL), 0)) & 7
        for half, rest in enumerate(rests):
            for s in range(FOLD):
                total = jnp.zeros((8, COL), F32)
                for d in range(8):
                    moved = rest[8 * s : 8 * s + 8, :]
                    if d:
                        moved = pltpu.roll(pltpu.roll(moved, SPARE * d, 1), 8 - d, 0)
                    total = jnp.where(turn == d, moved, total)
                rest_rows[half, s] = total

    def pick_all(part, both):
        sides = [(step + mine) & (TARGETS // 2 - 1) for step in range(TARGETS // 2)]
        extra = list(range(TARGETS // 2 + 1, TILES))
        ends, value = [], product(both, extra[0])
        for tile, after in zip(extra, extra[1:] + [None]):
            now = value
            if after is not None:
                value = product(both, after)
            ends += chosen(now, tile)
        for side in range(2):
            for h in range(HALO):
                picked_rows[part, side, h] = ends[side * HALO + h]
        for side in range(2):
            l_copy(part, side).start()

        @pl.when(col_edge)
        def _():
            now, value = product(both, TARGETS // 2), product(both, sides[0])
            fold(chosen(now, TARGETS // 2))
            for step, tile in enumerate(sides):
                now = value
                if step + 1 < len(sides):
                    value = product(both, sides[step + 1])
                for i, end in enumerate(chosen(now, tile)):
                    target = 2 * tile + i
                    picked[part, target, 0:PART, :] = end
                    for s in range(FOLD):
                        picked[part, target, PART + s : PART + s + 1, :] = rest_rows[
                            tile >> 2, s, pl.ds(target & (GROUPS - 1), 1), :
                        ]
                for i in range(2):
                    b_copy(part, 2 * tile + i).start()

    def corrections(part, side, along_lanes):
        halo_ref, own_ref, add_ref = (col_halo, col_own, col_add) if along_lanes else (row_halo, row_out, row_add)

        def scaled(value, power):
            for _ in range(0 if along_lanes else power):
                value = scale * value
            return value

        halo = [[halo_ref[side, h, q * SHELLS : (q + 1) * SHELLS, :] for q in range(QUANTITIES)] for h in range(HALO)]
        form = cross_azimuthal if along_lanes else cross_polar
        halo_emf = [(cross_radial(x[MR:BR], x[BR:WARM]), form(x[MR:BR], x[BR:WARM])) for x in halo]
        sign = -1.0 if side == 0 else 1.0
        firsts, seconds = (45.0 * sign, -9.0 * sign, sign), (270.0, -27.0, 2.0)
        for j in range(HALO):
            own = [own_ref[part, side, j, q * SHELLS : (q + 1) * SHELLS, :] for q in range(QUANTITIES)]

            def total(weights, of):
                result = None
                for m in (1, 2, 3):
                    h = j + 3 - m if side == 0 else m - 3 + j
                    if 0 <= h < HALO:
                        term = weights[m - 1] * of(h)
                        result = term if result is None else result + term
                return result

            d = [scaled(total(firsts, lambda h, q=q: halo[h][q]), 1) for q in range(QUANTITIES)]
            lap = [
                None if q == S else scaled(total(seconds, lambda h, q=q: halo[h][q]), 2) for q in range(QUANTITIES)
            ]
            radial = scaled(total(firsts, lambda h: halo_emf[h][0]), 1)
            second = scaled(total(firsts, lambda h: halo_emf[h][1]), 1)
            result = edge_rates(own, d, lap, second, radial, along_lanes)
            for q in range(QUANTITIES):
                add_ref[side, j, q * SHELLS : (q + 1) * SHELLS, :] = (TIME_STEP / 60.0 / (1 + part)) * result[q]

    def contribute(side, along_lanes):
        add_ref = col_add if along_lanes else row_add
        value = jnp.concatenate([add_ref[side, j] for j in range(HALO)], axis=0)
        if along_lanes:
            value = jnp.where(iota((HALO * FLAT, COL), 1) < LON, value, 0.0)
        high, low = split(value)
        value = dot(jnp.concatenate([high, low, high], axis=1), rows_split[...] if along_lanes else mix[...])
        total = jnp.zeros((FLAT, SLOTS), F32)
        for j in range(HALO):
            if along_lanes:
                at = j if side == 0 else COL - HALO + j
                weight = cols_mix[at : at + 1, :]
            else:
                at = j if side == 0 else LON - HALO + j
                weight = rows_mix[at : at + 1, :]
            total = total + weight * value[j * FLAT : (j + 1) * FLAT, :]
        for half in range(2):
            blocks[1, half] = blocks[1, half] + total[half * PART : (half + 1) * PART, :]

    def apply_edges():
        for side in range(2):
            for j in range(HALO):
                rows = pl.ds(8 + (j if side == 0 else LON - HALO + j), FLAT, stride=STRIDE)
                frame[1, rows, :] = frame[1, rows, :] + row_add[side, j]
        turn_edges(col_add, turned)
        for half in range(2):
            edge = jnp.transpose(turned[half])[0:LON, :]
            for g in range(FLAT // 2):
                at = (half * (FLAT // 2) + g) * STRIDE + 8
                frame[1, at : at + LON, :] = frame[1, at : at + LON, :] + field_edge(edge, g)

    def a_copy(part, step, half):
        return remote(
            blocks.at[part, half], table.at[part, member], a_send.at[part, half, step], a_recv.at[part, member],
            row_device(step, half),
        )

    def s_copy(part, half):
        return remote(
            blocks.at[part, half], table.at[part, member], s_send.at[part], a_recv.at[part, member], sibling
        )

    def a_arrival(part, step):
        there = (member + step) & (GROUP - 1)
        return remote(blocks.at[part, 0], table.at[part, there], s_send.at[part], a_recv.at[part, there], sibling)

    def b_copy(part, target):
        return remote(
            picked.at[part, target], got_cols.at[part, origin], b_send.at[part, target], b_recv.at[part, origin],
            target_device(target),
        )

    def b_arrival(part, source):
        return remote(
            picked.at[part, 0], got_cols.at[part, source], b_send.at[part, 0], b_recv.at[part, source],
            (other, lon, col),
        )

    def l_copy(part, side):
        return remote(
            picked_rows.at[part, side], got_rows.at[part, origin], l_send.at[part, side], l_recv.at[part, origin],
            target_device(side * (TARGETS - 1)),
        )

    def l_arrival(part, source):
        return remote(
            picked_rows.at[part, 0], got_rows.at[part, source], l_send.at[part, 0], l_recv.at[part, source],
            (other, lon, col),
        )

    def row_copy(part, side):
        return remote(
            row_out.at[part, 1 - side], row_in.at[part, side], r_send.at[part, side], r_recv.at[part, side],
            (panel, lon_up if side == 0 else lon_down, col),
        )

    def col_copy(part, side):
        return remote(
            col_out.at[part, 1 - side], col_in.at[part, side], c_send.at[part, side], c_recv.at[part, side],
            (panel, lon, col_up if side == 0 else col_down),
        )

    def idx_copy(target):
        return remote(
            idx_out, idx_in.at[origin], idx_send.at[target], idx_recv.at[origin], target_device(target)
        )

    def idx_arrival(source):
        return remote(idx_out, idx_in.at[source], idx_send.at[0], idx_recv.at[source], (other, lon, col))

    def inner_sides(part):
        for side in range(2):
            @pl.when(lon != (0 if side == 0 else n_lon - 1))
            def _():
                row_copy(part, side).wait_recv()
                row_halo[side] = row_in[part, side]
                corrections(part, side, False)
                if part == 0:
                    contribute(side, False)

            @pl.when(col != (0 if side == 0 else n_col - 1))
            def _():
                col_copy(part, side).wait_recv()
                pair = col_in[part, side, 0]
                col_halo[side, 0] = pair
                col_halo[side, 1] = pltpu.roll(pair, COL // 2, 1)
                col_halo[side, 2] = col_in[part, side, 1]
                corrections(part, side, True)
                if part == 0:
                    contribute(side, True)

    def outer_sides(part):
        for side in range(2):

            @pl.when(col == (0 if side == 0 else n_col - 1))
            def _():
                for source in range(TARGETS):
                    b_arrival(part, source).wait_recv()
                for half in range(2):
                    total = got_cols[part, half * GROUPS]
                    for group in range(1, GROUPS):
                        total = total + got_cols[part, half * GROUPS + group]
                    main = total[0:PART]
                    rows = slice(half * PART, (half + 1) * PART)
                    col_halo[side, 0, rows, :] = main
                    col_halo[side, 1, rows, :] = pltpu.roll(main, COL - LON, 1)
                    main = pltpu.roll(main, COL - 2 * LON, 1)
                    row, lane = iota((8, COL), 0), iota((8, COL), 1)
                    for s in range(FOLD):
                        value = main[8 * s : 8 * s + 8, :]
                        rest = jnp.broadcast_to(total[PART + s : PART + s + 1], (8, COL))
                        for q in range(8):
                            moved = pltpu.roll(rest, (2 * COL - 2 * LON - SPARE * q) % COL, 1)
                            value = jnp.where(jnp.logical_and(row == q, lane >= COL - 2 * LON), moved, value)
                        at = half * PART + 8 * s
                        col_halo[side, 2, at : at + 8, :] = value
                corrections(part, side, True)
                if part == 0:
                    contribute(side, True)

            @pl.when(lon == (0 if side == 0 else n_lon - 1))
            def _():
                for source in range(TARGETS):
                    l_arrival(part, source).wait_recv()
                for half in range(2):
                    total = got_rows[part, half * GROUPS]
                    for group in range(1, GROUPS):
                        total = total + got_rows[part, half * GROUPS + group]
                    row_halo[side, :, half * PART : (half + 1) * PART, :] = total
                corrections(part, side, False)
                if part == 0:
                    contribute(side, False)

    for part in range(2):
        if part == 0:
            message_tables()
            copies[3].wait()
            interpolate(0, 0)
            copies[4].wait()
            interpolate(0, 1)
            pl.semaphore_wait(barrier, 2 * len(AROUND) + 2 + TARGETS)
            send(0, 0)
            send(0, 1)
            for target in range(TARGETS):
                idx_copy(target).start()
            other_tables()
        else:
            send(1, 0)
            send(1, 1)
            apply_edges()
        rows_of(part)
        for side in range(2):

            @pl.when(sends_rows[side])
            def _():
                row_copy(part, side).start()

        cols_of(part)
        for side in range(2):

            @pl.when(sends_cols[side])
            def _():
                col_copy(part, side).start()

        lane_pass(part)
        emf_pass(part)
        if part == 0:
            for source in range(TARGETS):
                idx_arrival(source).wait_recv()
            prepare_picks()
        for step in range(1, GROUP):
            a_arrival(part, step).wait_recv()
        both = table_split(part)
        pick_all(part, both)
        main_pass(part, 0, 6)
        if part == 0:
            interpolate(1, 0)
            interpolate(1, 1)
        inner_sides(part)
        outer_sides(part)

    for target in range(TARGETS):
        idx_copy(target).wait_send()
    for part in range(2):
        for half in range(2):
            for step in AROUND:
                a_copy(part, step, half).wait_send()
        s_copy(part, 0).wait_send()
        for side in range(2):
            l_copy(part, side).wait_send()

            @pl.when(sends_rows[side])
            def _():
                row_copy(part, side).wait_send()

            @pl.when(sends_cols[side])
            def _():
                col_copy(part, side).wait_send()


        @pl.when(col_edge)
        def _():
            for target in range(TARGETS):
                b_copy(part, target).wait_send()


def shards(state, send_base, send_frac, recv_slots):
    rows = FLAT * LON
    dma = pltpu.SemaphoreType.DMA
    vmem = pltpu.VMEM
    scratch = [
        vmem((2, FLAT, STRIDE, COL), F32),
        vmem((1, OUT), I32),
        vmem((2, OUT), F32),
        vmem((1, recv_slots.shape[-1]), I32),
        vmem((3 * SHELLS * STRIDE, COL), F32),
        vmem(((FLAT + 2 * SHELLS) * LON, 2 * COL), F32),
        vmem((3 * COL, SLOTS), BF16),
        vmem((COL, SLOTS), F32),
        vmem((LON, SLOTS), F32),
        vmem((3 * COL, SLOTS), BF16),
        vmem((2 * COL, 2 * COL), BF16),
        vmem((TILES, SLOTS, 2 * COL), BF16),
        vmem((TILES, 8, 2 * COL), I32),
        vmem((2, COL, COL), F32),
        vmem((2, 2, PART, SLOTS), F32),
        vmem((2, GROUP, PART, SLOTS), F32),
        vmem((8, COL), I32),
        vmem((TARGETS, 8, COL), I32),
        vmem((2, FOLD, 8, COL), F32),
        vmem((2, TARGETS, PART + FOLD, COL), F32),
        vmem((2, 2, HALO, PART, COL), F32),
        vmem((2, TARGETS, PART + FOLD, COL), F32),
        vmem((2, TARGETS, HALO, PART, COL), F32),
        vmem((2, 2, HALO, FLAT, COL), F32),
        vmem((2, 2, HALO, FLAT, COL), F32),
        vmem((2, 2, HALO, FLAT, COL), F32),
        vmem((2, 2, 2, FLAT, COL), F32),
        vmem((2, 2, 2, FLAT, COL), F32),
        vmem((2, HALO, FLAT, COL), F32),
        vmem((2, HALO, FLAT, COL), F32),
        dma((5,)),
        dma((TARGETS,)),
        dma((TARGETS,)),
        dma((2, 2, RING)),
        dma((2, GROUP)),
        dma((2,)),
        dma((2, TARGETS)),
        dma((2, TARGETS)),
        dma((2, 2)),
        dma((2, TARGETS)),
        dma((2, 2)),
        dma((2, 2)),
        dma((2, 2)),
        dma((2, 2)),
    ]
    edges = jax.ShapeDtypeStruct((2, HALO, FLAT, COL), F32)
    value, row_add, col_add = pl.pallas_call(
        kernel,
        out_shape=(jax.ShapeDtypeStruct((rows, COL), F32), edges, edges),
        in_specs=[pl.BlockSpec(memory_space=pltpu.HBM)] * 4,
        out_specs=[pl.BlockSpec(memory_space=pltpu.VMEM)] * 3,
        scratch_shapes=scratch,
        compiler_params=pltpu.CompilerParams(
            collective_id=0, has_side_effects=True, vmem_limit_bytes=40 * 1024 * 1024
        ),
    )(*(
        pltpu.with_memory_space_constraint(x, pltpu.HBM)
        for x in (state.reshape(FLAT, LON, COL), send_base[0], send_frac[0, 0], recv_slots[0])
    ))
    result = pl.pallas_call(
        closing,
        out_shape=jax.ShapeDtypeStruct((rows, COL), F32),
        in_specs=[pl.BlockSpec(memory_space=pltpu.VMEM)] * 3,
        out_specs=pl.BlockSpec(memory_space=pltpu.HBM),
        scratch_shapes=[vmem((2, COL, COL), F32), vmem((rows, COL), F32), dma((8,))],
        compiler_params=pltpu.CompilerParams(vmem_limit_bytes=16 * 1024 * 1024),
    )(value, row_add, col_add)
    return result.reshape(state.shape)


def solution(mesh):
    placed = (
        P("panel", None, None, "lon", "colat"),
        P("panel", ("lon", "colat"), None),
        P("panel", ("lon", "colat"), None, None),
        P("panel", ("lon", "colat"), None),
    )
    return jax.shard_map(
        shards,
        mesh=mesh,
        in_specs=placed,
        out_specs=P("panel", None, None, "lon", "colat"),
        check_vma=False,
    )
```

```python
import math

import jax
import jax.numpy as jnp
from jax import lax
from jax.experimental import pallas as pl
from jax.experimental.pallas import tpu as pltpu
from jax.sharding import PartitionSpec as P

MESH = pl.DeviceIdType.MESH
F32, BF16, I32 = jnp.float32, jnp.bfloat16, jnp.int32

QUANTITIES = 8
SHELLS = 4
FLAT = QUANTITIES * SHELLS
LON = 48
COL = 128
HALO = 3
OUT = 240
SIDE = HALO * LON
SLOTS = 256
GROUP = 8
GROUPS = 8
AROUND = (1, 3, 2)
SPARE = SIDE - COL
PART = FLAT // 2
TARGETS = 2 * GROUPS
TILES = 8
RING = 4
FOLD = PART // 8
STRIDE = LON + 16
TIME_STEP = 0.25
SPREAD = 0.1 / 3.0
S, MR, MT, MP, BR, BT, BP, WARM = range(QUANTITIES)


def dot(left, right):
    return jnp.dot(left, right, preferred_element_type=F32)


def split(value):
    high = value.astype(BF16)
    return high, (value - high.astype(F32)).astype(BF16)


def iota(shape, dim):
    return lax.broadcasted_iota(I32, shape, dim)


def cross_radial(m, b):
    return m[1] * b[2] - m[2] * b[1]


def cross_polar(m, b):
    return m[2] * b[0] - m[0] * b[2]


def cross_azimuthal(m, b):
    return m[0] * b[1] - m[1] * b[0]


def edge_rates(own, d, lap, emf_first, emf_second, along_lanes):
    grow, thin = jnp.exp(own[WARM]), jnp.exp(-own[S])
    b = own[BR:WARM]
    if along_lanes:
        vel, out = own[MT], MT
        lorentz = (d[BR] * b[1], -d[BR] * b[0] - d[BP] * b[2], d[BP] * b[1])
        turn = (emf_first, None, -emf_second)
    else:
        vel, out = own[MP], MP
        lorentz = (d[BR] * b[2], d[BT] * b[2], -d[BT] * b[1] - d[BR] * b[0])
        turn = (-emf_first, emf_second, None)
    result = [-vel * d[S] - d[out]]
    for i in range(3):
        rate = -vel * d[MR + i] + thin * lorentz[i] + SPREAD * lap[MR + i]
        if MR + i == out:
            rate = rate - grow * (d[S] + d[WARM])
        result.append(rate)
    for i in range(3):
        rate = SPREAD * lap[BR + i]
        result.append(rate if turn[i] is None else rate + turn[i])
    result.append(-vel * d[WARM] - (2.0 / 3.0) * d[out] + SPREAD * lap[WARM])
    return result


def shell_steps(x):
    a, b, c = x[1] - x[0], x[2] - x[0], x[3] - x[0]
    p, q, r = 45.0 * a, 45.0 * b, 37.0 * c
    first = (p - 9.0 * b + c, q - 8.0 * c, r - p, r - q + 9.0 * a)
    p, q, r = 270.0 * a, 270.0 * b, 245.0 * c
    second = (p - 27.0 * b + 2.0 * c, q - 490.0 * a - 25.0 * c, p - 490.0 * b + r, q - 27.0 * a - r)
    return first, second


def turn_edges(col_add, turned):
    for side in range(2):
        for j in range(HALO):
            for half in range(2):
                turned[half, pl.ds((1 - side) * HALO + j, FLAT // 2, stride=8), :] = col_add[
                    side, j, half * (FLAT // 2) : (half + 1) * (FLAT // 2), :
                ]


def field_edge(edge, g):
    lane = iota((LON, COL), 1)
    border = jnp.logical_or(lane < HALO, lane >= COL - HALO)
    return jnp.where(border, pltpu.roll(edge, COL - 8 * g - HALO, 1), 0.0)


def closing(value_ref, row_add, col_add, out_hbm, turned, ready, sem):
    turn_edges(col_add, turned)
    copies = []
    for half in range(2):
        edge = jnp.transpose(turned[half])[0:LON, :]
        for chunk in range(4):
            first = half * (FLAT // 2) + 4 * chunk
            for q in range(4):
                at = (first + q) * LON
                ready[at : at + LON, :] = value_ref[at : at + LON, :] + field_edge(edge, 4 * chunk + q)
            for side in range(2):
                for j in range(HALO):
                    rows = pl.ds(first * LON + (j if side == 0 else LON - HALO + j), 4, stride=LON)
                    ready[rows, :] = ready[rows, :] + row_add[side, j, first : first + 4, :]
            rows = pl.ds(first * LON, 4 * LON)
            copy = pltpu.make_async_copy(ready.at[rows, :], out_hbm.at[rows, :], sem.at[4 * half + chunk])
            copy.start()
            copies.append(copy)
    for copy in copies:
        copy.wait()


def kernel(
    x_hbm, base_hbm, frac_hbm, slots_hbm, out_ref, row_add, col_add,
    deep, base_ref, frac_ref, slots_ref, emf, lanes, mix, cols_mix, rows_mix, rows_split, band, onehot, owner, turned,
    blocks, table, idx_out, idx_in, idx_ends, rest_rows, picked, picked_rows, got_cols, got_rows, row_out, row_in, col_own, col_out, col_in,
    row_halo, col_halo,
    in_sem, idx_send, idx_recv, e_send, e_recv, a_send, a_recv, s_send, b_send, b_recv, l_send, l_recv, r_send, r_recv, c_send, c_recv,
):
    panel, lon, col = lax.axis_index("panel"), lax.axis_index("lon"), lax.axis_index("colat")
    n_lon, n_col = lax.axis_size("lon"), lax.axis_size("colat")
    core, mine = lon & 1, lon >> 1
    member = core * n_col + col
    other = 1 - panel
    lon_up, lon_down = lax.rem(lon + 1, n_lon), lax.rem(lon + n_lon - 1, n_lon)
    col_up, col_down = lax.rem(col + 1, n_col), lax.rem(col + n_col - 1, n_col)
    outer = lax.rem(lon + 2 * core - 1 + n_lon, n_lon)
    sends_rows = (lon < n_lon - 1, lon > 0)
    sends_cols = (col < n_col - 1, col > 0)
    col_edge = jnp.logical_or(col == 0, col == n_col - 1)

    sibling = (panel, lon + 1 - 2 * core, col)
    origin = core * GROUPS + mine
    lon_edge = jnp.logical_or(lon == 0, lon == n_lon - 1)
    target_col, target_core = (col >> 1) * (n_col - 1), (col ^ (col >> 1)) & 1
    source_col = col ^ core

    def row_device(step, half):
        return (panel, 2 * mine + half, (col + step) & (n_col - 1))

    def side_device(target):
        return (other, 2 * target + target_core, target_col)

    def end_device(side):
        return (other, side * (n_lon - 1), col)

    def side_source(source):
        return (other, 2 * (source % GROUPS) + source // GROUPS, source_col)

    def end_source(source):
        return (other, 2 * (source % GROUPS) + source // GROUPS, col)

    def remote(src, dst, send, recv, device):
        return pltpu.make_async_remote_copy(
            src_ref=src, dst_ref=dst, send_sem=send, recv_sem=recv, device_id=device, device_id_type=MESH
        )

    frame = deep.reshape(2, FLAT * STRIDE, COL)
    copies = [
        pltpu.make_async_copy(src, dst, in_sem.at[i])
        for i, (src, dst) in enumerate(
            (
                (frac_hbm, frac_ref),
                (base_hbm, base_ref),
                (slots_hbm, slots_ref),
                (x_hbm.at[pl.ds(0, PART)], deep.at[0, pl.ds(0, PART), pl.ds(8, LON), :]),
                (x_hbm.at[pl.ds(PART, PART)], deep.at[0, pl.ds(PART, PART), pl.ds(8, LON), :]),
            )
        )
    ]
    for copy in copies:
        copy.start()

    barrier = pltpu.get_barrier_semaphore()
    for step in AROUND:
        for half in range(2):
            pl.semaphore_signal(barrier, inc=1, device_id=row_device(step, half), device_id_type=MESH)
    pl.semaphore_signal(barrier, inc=1, device_id=sibling, device_id_type=MESH)
    for target in range(GROUPS):
        pl.semaphore_signal(barrier, inc=1, device_id=side_device(target), device_id_type=MESH)
    for side in range(2):
        pl.semaphore_signal(barrier, inc=1, device_id=end_device(side), device_id_type=MESH)

    @pl.when(col_edge)
    def _():
        for source in range(TARGETS):
            pl.semaphore_signal(barrier, inc=1, device_id=side_source(source), device_id_type=MESH)

    @pl.when(lon_edge)
    def _():
        for source in range(TARGETS):
            pl.semaphore_signal(barrier, inc=1, device_id=end_source(source), device_id_type=MESH)

    pl.semaphore_signal(barrier, inc=1, device_id=(panel, outer, col), device_id_type=MESH)

    copies[0].wait()
    copies[1].wait()
    base = jnp.concatenate([base_ref[...], jnp.zeros((1, SLOTS - OUT), I32)], axis=1)
    base_row, base_col = lax.div(base, COL), lax.rem(base, COL)
    share = jnp.concatenate([frac_ref[...], jnp.zeros((2, SLOTS - OUT), F32)], axis=1)
    along, across = share[0:1, :], share[1:2, :]
    cells = iota((COL, SLOTS), 0)
    weight = jnp.where(cells == base_col, 1.0 - across, 0.0) + jnp.where(cells == base_col + 1, across, 0.0)
    weight_high, weight_low = split(weight)
    cols_mix[...] = weight
    mix[0:COL, :] = weight_high
    mix[COL : 2 * COL, :] = weight_high
    mix[2 * COL : 3 * COL, :] = weight_low
    cells = iota((LON, SLOTS), 0)
    weight = jnp.where(cells == base_row, 1.0 - along, 0.0) + jnp.where(cells == base_row + 1, along, 0.0)
    rows_mix[...] = weight
    place = (col * COL + iota((1, COL), 1)).astype(F32)
    scale = 1.0 / jnp.sin(math.pi / 4.0 + (place + 0.5) * (math.pi / 2.0 / (COL * n_col)))

    def message_tables():
        copies[2].wait()
        spot = iota((1, SLOTS), 1)
        sides = jnp.where(spot < SIDE, jnp.maximum(slots_ref[:, 0:SLOTS], slots_ref[:, SIDE : SIDE + SLOTS]) + 1, 0)
        digits = jnp.concatenate([lax.div(sides, COL), lax.rem(sides, COL), jnp.zeros((6, SLOTS), I32)], axis=0)
        source, target = iota((SLOTS, SLOTS), 0), iota((SLOTS, SLOTS), 1)
        layer = jnp.where(target >= LON, 1, 0) + jnp.where(target >= 2 * LON, 1, 0)
        order = jnp.logical_and(target < SIDE, source == HALO * (target - LON * layer) + layer)
        digits = dot(digits.astype(F32).astype(BF16), jnp.where(order, 1.0, 0.0).astype(BF16)).astype(I32)
        sides = digits[0:1, :] * COL + digits[1:2, :] - 1
        idx_out[0:1, :] = sides[:, 0:COL]
        idx_out[1:2, :] = sides[:, COL : 2 * COL]
        for h in range(HALO):
            at = 2 * SIDE + h * COL
            idx_out[2 + h : 3 + h, :] = jnp.maximum(
                slots_ref[:, at : at + COL], slots_ref[:, at + HALO * COL : at + HALO * COL + COL]
            )
        idx_out[5:8, :] = jnp.full((3, COL), -1, I32)

    def other_tables():
        zero_rows = jnp.zeros((8, COL), F32)
        for f in range(FLAT):
            for part in range(2):
                frame[part, f * STRIDE : f * STRIDE + 8, :] = zero_rows
                frame[part, f * STRIDE + 8 + LON : (f + 1) * STRIDE, :] = zero_rows
        for f in range(3 * SHELLS):
            emf[f * STRIDE : f * STRIDE + 8, :] = zero_rows
            emf[f * STRIDE + 8 + LON : (f + 1) * STRIDE, :] = zero_rows

        for half in range(2):
            turned[half, :, :] = jnp.zeros((COL, COL), F32)

        apart = iota((COL, COL), 0) - iota((COL, COL), 1)
        reach = jnp.abs(apart)
        first = jnp.where(reach == 1, 45.0, jnp.where(reach == 2, -9.0, jnp.where(reach == 3, 1.0, 0.0)))
        first = jnp.where(apart < 0, -first, first).astype(BF16)
        second = jnp.where(
            reach == 0, -490.0, jnp.where(reach == 1, 270.0, jnp.where(reach == 2, -27.0, jnp.where(reach == 3, 2.0, 0.0)))
        ).astype(BF16)
        for part in range(2):
            band[part * COL : (part + 1) * COL, 0:COL] = first
            band[part * COL : (part + 1) * COL, COL : 2 * COL] = second
        weight_high, weight_low = split(jnp.concatenate([rows_mix[...], jnp.zeros((COL - LON, SLOTS), F32)], axis=0))
        rows_split[0:COL, :] = weight_high
        rows_split[COL : 2 * COL, :] = weight_high
        rows_split[2 * COL : 3 * COL, :] = weight_low

    def load_split(part, pair):
        block = jnp.concatenate(
            [frame[part, pl.ds(pl.multiple_of((8 * pair + q) * STRIDE + 8, 8), LON), :] for q in range(8)], axis=0
        )
        return split(block)

    def interpolate(part, half):
        for pair in range(PART // 8):
            high, low = load_split(part, 2 * half + pair)
            value = dot(jnp.concatenate([high, low, high], axis=1), mix[...])
            value = jnp.sum(value.reshape(8, LON, SLOTS) * rows_mix[...][None], axis=1)
            blocks[part, half, 8 * pair : 8 * pair + 8, :] = value

    def send(part, half):
        for step in AROUND:
            a_copy(part, step, half).start()

        @pl.when(core != half)
        def _():
            s_copy(part, half).start()

        @pl.when(core == half)
        def _():
            table[part, member] = blocks[part, half]

    def lane_pass(part):
        for pair in range(FLAT // 8):
            high, low = load_split(part, pair)
            both = jnp.concatenate([high, low], axis=1)
            lanes[8 * LON * pair : 8 * LON * (pair + 1), :] = dot(both, band[...])

    def cols_of(part):
        lane = iota((LON, COL), 1)
        for half in range(2):
            edge = jnp.zeros((LON, COL), F32)
            for g in range(FLAT // 2):
                at = (half * (FLAT // 2) + g) * STRIDE + 8
                moved = pltpu.roll(frame[part, at : at + LON, :], 8 * g + HALO, 1)
                edge = jnp.where(jnp.logical_and(lane >= 8 * g, lane < 8 * g + 2 * HALO), moved, edge)
            turned[half, :, 0:LON] = jnp.transpose(edge)
        for side in range(2):
            for j in range(HALO):
                first = (1 - side) * HALO + j
                for half in range(2):
                    col_own[part, side, j, half * (FLAT // 2) : (half + 1) * (FLAT // 2), :] = turned[
                        half, pl.ds(first, FLAT // 2, stride=8), :
                    ]
            col_out[part, side, 0] = jnp.where(
                iota((FLAT, COL), 1) < COL // 2, col_own[part, side, 0], pltpu.roll(col_own[part, side, 1], COL // 2, 1)
            )
            col_out[part, side, 1] = col_own[part, side, 2]

    def emf_pass(part):
        for r in range(SHELLS):
            def field(q):
                at = (q * SHELLS + r) * STRIDE + 8
                return frame[part, at : at + LON, :]

            m, b = [field(MR + i) for i in range(3)], [field(BR + i) for i in range(3)]
            for i, form in enumerate((cross_radial, cross_polar, cross_azimuthal)):
                at = (i * SHELLS + r) * STRIDE + 8
                emf[at : at + LON, :] = form(m, b)
        for i, at in ((0, FLAT), (2, FLAT + SHELLS)):
            block = jnp.concatenate(
                [emf[(i * SHELLS + r) * STRIDE + 8 : (i * SHELLS + r) * STRIDE + 8 + LON, :] for r in range(SHELLS)],
                axis=0,
            )
            high, low = split(block)
            lanes[at * LON : (at + SHELLS) * LON, 0:COL] = dot(
                jnp.concatenate([high, low], axis=1), band[:, 0:COL]
            )

    def main_pass(part, start, stop):
        def body(block, carry):
            here = pl.multiple_of(8 * block, 8)

            def near(f, apart):
                return frame[part, pl.ds(f * STRIDE + 8 + here + apart, 8), :]

            def near_emf(f, apart):
                return emf[pl.ds(f * STRIDE + 8 + here + apart, 8), :]

            def lane_first(f):
                return lanes[pl.ds(f * LON + here, 8), 0:COL]

            def lane_second(f):
                return lanes[pl.ds(f * LON + here, 8), COL : 2 * COL]

            def row_first(at):
                return 45.0 * (at[1] - at[-1]) - 9.0 * (at[2] - at[-2]) + (at[3] - at[-3])

            def row_second(at, centre):
                return (
                    270.0 * (at[1] + at[-1]) - 27.0 * (at[2] + at[-2]) + 2.0 * (at[3] + at[-3]) - 490.0 * centre
                )

            centre = [[near(q * SHELLS + r, 0) for r in range(SHELLS)] for q in range(QUANTITIES)]
            steps = [shell_steps(x) for x in centre]
            radial, radial_second = [x[0] for x in steps], [x[1] for x in steps]
            emf_centre = [[near_emf(i * SHELLS + r, 0) for r in range(SHELLS)] for i in range(3)]
            emf_radial = [None, shell_steps(emf_centre[1])[0], shell_steps(emf_centre[2])[0]]
            for r in range(SHELLS):
                own = [centre[q][r] for q in range(QUANTITIES)]
                g, lap = [], []
                for q in range(QUANTITIES):
                    f = q * SHELLS + r
                    at = {d: near(f, d) for d in (-3, -2, -1, 1, 2, 3)}
                    g.append((radial[q][r], lane_first(f), scale * row_first(at)))
                    if q == S:
                        lap.append(None)
                    else:
                        lap.append(
                            radial_second[q][r] + lane_second(f) + (scale * scale) * row_second(at, own[q])
                        )
                m, b = own[MR:BR], own[BR:WARM]

                def advect(q):
                    return m[0] * g[q][0] + m[1] * g[q][1] + m[2] * g[q][2]

                div = g[MR][0] + g[MT][1] + g[MP][2]
                current = (g[BP][1] - g[BT][2], g[BR][2] - g[BP][0], g[BT][0] - g[BR][1])
                lorentz = (
                    current[1] * b[2] - current[2] * b[1],
                    current[2] * b[0] - current[0] * b[2],
                    current[0] * b[1] - current[1] * b[0],
                )
                grow, thin = jnp.exp(own[WARM]), jnp.exp(-own[S])
                emf_rows = {}
                for i in (0, 1):
                    f = i * SHELLS + r
                    emf_rows[i] = scale * row_first({d: near_emf(f, d) for d in (-3, -2, -1, 1, 2, 3)})
                turn = (
                    lane_first(FLAT + SHELLS + r) - emf_rows[1],
                    emf_rows[0] - emf_radial[2][r],
                    emf_radial[1][r] - lane_first(FLAT + r),
                )
                result = [-advect(S) - div]
                for i in range(3):
                    result.append(
                        -advect(MR + i) - grow * (g[S][i] + g[WARM][i]) + thin * lorentz[i] + SPREAD * lap[MR + i]
                    )
                for i in range(3):
                    result.append(turn[i] + SPREAD * lap[BR + i])
                result.append(-advect(WARM) - (2.0 / 3.0) * div + SPREAD * lap[WARM])
                for q in range(QUANTITIES):
                    f = q * SHELLS + r
                    value = own[q] + (TIME_STEP / 60.0) * result[q]
                    if part == 0:
                        frame[1, pl.ds(f * STRIDE + 8 + here, 8), :] = value
                    else:
                        start = frame[0, pl.ds(f * STRIDE + 8 + here, 8), :]
                        out_ref[pl.ds(f * LON + here, 8), :] = 0.5 * (start + value)
            return carry

        lax.fori_loop(start, stop, body, 0)

    def rows_of(part):
        for h in range(HALO):
            row_out[part, 0, h] = frame[part, pl.ds(8 + h, FLAT, stride=STRIDE), :]
            row_out[part, 1, h] = frame[part, pl.ds(8 + LON - HALO + h, FLAT, stride=STRIDE), :]

    def prepare_picks():
        for tile in range(2 * TILES):
            if tile < GROUPS:
                slot = idx_in[tile, 0:1, :]
            elif tile == GROUPS:
                slot = idx_in[0, 1:2, :]
                for q in range(1, GROUPS):
                    slot = jnp.maximum(slot, pltpu.roll(idx_in[q], SPARE * q, 1)[1:2, :])
            elif tile <= GROUPS + 2 * HALO:
                side, h = divmod(tile - GROUPS - 1, HALO)
                slot = idx_ends[side, 2 + h : 3 + h, :]
            else:
                slot = jnp.full((1, COL), -1, I32)
            slot = slot - mine * (GROUP * OUT)
            who = jnp.zeros_like(slot)
            for q in range(1, GROUP):
                who = who + jnp.where(slot >= q * OUT, 1, 0)
            cell = slot - who * OUT
            who = jnp.where(jnp.logical_and(slot >= 0, slot < GROUP * OUT), who, -1)
            at = (tile % 2) * COL
            owner[tile // 2, :, at : at + COL] = jnp.broadcast_to(who, (8, COL))
            hot = jnp.where(iota((SLOTS, COL), 0) == cell, 1.0, 0.0).astype(BF16)
            onehot[tile // 2, :, at : at + COL] = hot

    def table_split(part):
        high, low = split(table[part].reshape(GROUP * PART, SLOTS))
        return jnp.concatenate([high, low], axis=0)

    def product(both, tile):
        return dot(both, onehot[tile])

    def chosen(value, tile):
        value = value[0 : GROUP * PART] + value[GROUP * PART :]
        who = jnp.broadcast_to(owner[tile, 0:1, :], (PART, SLOTS))
        total = jnp.zeros((PART, SLOTS), F32)
        for q in range(GROUP):
            total = jnp.where(who == q, value[q * PART : (q + 1) * PART, :], total)
        return total[:, 0:COL], total[:, COL : 2 * COL]

    def fold(rest):
        turn = (lax.div(iota((8, COL), 1), SPARE) - iota((8, COL), 0)) & 7
        for s in range(FOLD):
            total = jnp.zeros((8, COL), F32)
            for d in range(8):
                moved = rest[8 * s : 8 * s + 8, :]
                if d:
                    moved = pltpu.roll(pltpu.roll(moved, SPARE * d, 1), 8 - d, 0)
                total = jnp.where(turn == d, moved, total)
            rest_rows[s] = total

    def pick_all(part, both):
        order = list(range(GROUPS // 2, TILES)) + [(step + mine) & (GROUPS // 2 - 1) for step in range(GROUPS // 2)]
        ends, value = [], product(both, order[0])
        for place, tile in enumerate(order):
            now = value
            if place + 1 < len(order):
                value = product(both, order[place + 1])
            pair = chosen(now, tile)
            if place < TILES - GROUPS // 2:
                ends += pair
                if place == TILES - GROUPS // 2 - 1:
                    for side in range(2):
                        for h in range(HALO):
                            picked_rows[part, side, h] = ends[1 + side * HALO + h]
                        l_copy(part, side).start()
                    fold(ends[0])
            else:
                for i, end in enumerate(pair):
                    target = 2 * tile + i
                    picked[part, target, 0:PART, :] = end
                    for s in range(FOLD):
                        picked[part, target, PART + s : PART + s + 1, :] = rest_rows[s, pl.ds(target, 1), :]
                for i in range(2):
                    b_copy(part, 2 * tile + i).start()

    def corrections(part, side, along_lanes):
        halo_ref, own_ref, add_ref = (col_halo, col_own, col_add) if along_lanes else (row_halo, row_out, row_add)

        def scaled(value, power):
            for _ in range(0 if along_lanes else power):
                value = scale * value
            return value

        halo = [[halo_ref[side, h, q * SHELLS : (q + 1) * SHELLS, :] for q in range(QUANTITIES)] for h in range(HALO)]
        form = cross_azimuthal if along_lanes else cross_polar
        halo_emf = [(cross_radial(x[MR:BR], x[BR:WARM]), form(x[MR:BR], x[BR:WARM])) for x in halo]
        sign = -1.0 if side == 0 else 1.0
        firsts, seconds = (45.0 * sign, -9.0 * sign, sign), (270.0, -27.0, 2.0)
        for j in range(HALO):
            own = [own_ref[part, side, j, q * SHELLS : (q + 1) * SHELLS, :] for q in range(QUANTITIES)]

            def total(weights, of):
                result = None
                for m in (1, 2, 3):
                    h = j + 3 - m if side == 0 else m - 3 + j
                    if 0 <= h < HALO:
                        term = weights[m - 1] * of(h)
                        result = term if result is None else result + term
                return result

            d = [scaled(total(firsts, lambda h, q=q: halo[h][q]), 1) for q in range(QUANTITIES)]
            lap = [
                None if q == S else scaled(total(seconds, lambda h, q=q: halo[h][q]), 2) for q in range(QUANTITIES)
            ]
            radial = scaled(total(firsts, lambda h: halo_emf[h][0]), 1)
            second = scaled(total(firsts, lambda h: halo_emf[h][1]), 1)
            result = edge_rates(own, d, lap, second, radial, along_lanes)
            for q in range(QUANTITIES):
                add_ref[side, j, q * SHELLS : (q + 1) * SHELLS, :] = (TIME_STEP / 60.0 / (1 + part)) * result[q]

    def contribute(side, along_lanes):
        add_ref = col_add if along_lanes else row_add
        value = jnp.concatenate([add_ref[side, j] for j in range(HALO)], axis=0)
        if along_lanes:
            value = jnp.where(iota((HALO * FLAT, COL), 1) < LON, value, 0.0)
        high, low = split(value)
        value = dot(jnp.concatenate([high, low, high], axis=1), rows_split[...] if along_lanes else mix[...])
        total = jnp.zeros((FLAT, SLOTS), F32)
        for j in range(HALO):
            if along_lanes:
                at = j if side == 0 else COL - HALO + j
                weight = cols_mix[at : at + 1, :]
            else:
                at = j if side == 0 else LON - HALO + j
                weight = rows_mix[at : at + 1, :]
            total = total + weight * value[j * FLAT : (j + 1) * FLAT, :]
        for half in range(2):
            blocks[1, half] = blocks[1, half] + total[half * PART : (half + 1) * PART, :]

    def apply_edges():
        for side in range(2):
            for j in range(HALO):
                rows = pl.ds(8 + (j if side == 0 else LON - HALO + j), FLAT, stride=STRIDE)
                frame[1, rows, :] = frame[1, rows, :] + row_add[side, j]
        turn_edges(col_add, turned)
        for half in range(2):
            edge = jnp.transpose(turned[half])[0:LON, :]
            for g in range(FLAT // 2):
                at = (half * (FLAT // 2) + g) * STRIDE + 8
                frame[1, at : at + LON, :] = frame[1, at : at + LON, :] + field_edge(edge, g)

    def a_copy(part, step, half):
        return remote(
            blocks.at[part, half], table.at[part, member], a_send.at[part, half, step], a_recv.at[part, member],
            row_device(step, half),
        )

    def s_copy(part, half):
        return remote(
            blocks.at[part, half], table.at[part, member], s_send.at[part], a_recv.at[part, member], sibling
        )

    def a_arrival(part, step):
        there = (member + step) & (GROUP - 1)
        return remote(blocks.at[part, 0], table.at[part, there], s_send.at[part], a_recv.at[part, there], sibling)

    def b_copy(part, target):
        return remote(
            picked.at[part, target], got_cols.at[part, origin], b_send.at[part, target], b_recv.at[part, origin],
            side_device(target),
        )

    def b_arrival(part, source):
        return remote(
            picked.at[part, 0], got_cols.at[part, source], b_send.at[part, 0], b_recv.at[part, source],
            (other, lon, col),
        )

    def l_copy(part, side):
        return remote(
            picked_rows.at[part, side], got_rows.at[part, origin], l_send.at[part, side], l_recv.at[part, origin],
            end_device(side),
        )

    def l_arrival(part, source):
        return remote(
            picked_rows.at[part, 0], got_rows.at[part, source], l_send.at[part, 0], l_recv.at[part, source],
            (other, lon, col),
        )

    def row_copy(part, side):
        return remote(
            row_out.at[part, 1 - side], row_in.at[part, side], r_send.at[part, side], r_recv.at[part, side],
            (panel, lon_up if side == 0 else lon_down, col),
        )

    def col_copy(part, side):
        return remote(
            col_out.at[part, 1 - side], col_in.at[part, side], c_send.at[part, side], c_recv.at[part, side],
            (panel, lon, col_up if side == 0 else col_down),
        )

    def idx_copy(source):
        return remote(idx_out, idx_in.at[mine], idx_send.at[source], idx_recv.at[mine], side_source(source))

    def idx_arrival(target):
        return remote(idx_out, idx_in.at[target], idx_send.at[0], idx_recv.at[target], (other, lon, col))

    def end_copy(source):
        return remote(idx_out, idx_ends.at[core], e_send.at[source], e_recv.at[core], end_source(source))

    def end_arrival(side):
        return remote(idx_out, idx_ends.at[side], e_send.at[0], e_recv.at[side], (other, lon, col))

    def inner_sides(part):
        for side in range(2):
            @pl.when(lon != (0 if side == 0 else n_lon - 1))
            def _():
                row_copy(part, side).wait_recv()
                row_halo[side] = row_in[part, side]
                corrections(part, side, False)
                if part == 0:
                    contribute(side, False)

            @pl.when(col != (0 if side == 0 else n_col - 1))
            def _():
                col_copy(part, side).wait_recv()
                pair = col_in[part, side, 0]
                col_halo[side, 0] = pair
                col_halo[side, 1] = pltpu.roll(pair, COL // 2, 1)
                col_halo[side, 2] = col_in[part, side, 1]
                corrections(part, side, True)
                if part == 0:
                    contribute(side, True)

    def outer_sides(part):
        for side in range(2):

            @pl.when(col == (0 if side == 0 else n_col - 1))
            def _():
                for source in range(TARGETS):
                    b_arrival(part, source).wait_recv()
                for half in range(2):
                    total = got_cols[part, half * GROUPS]
                    for group in range(1, GROUPS):
                        total = total + got_cols[part, half * GROUPS + group]
                    main = total[0:PART]
                    rows = slice(half * PART, (half + 1) * PART)
                    col_halo[side, 0, rows, :] = main
                    col_halo[side, 1, rows, :] = pltpu.roll(main, COL - LON, 1)
                    main = pltpu.roll(main, COL - 2 * LON, 1)
                    row, lane = iota((8, COL), 0), iota((8, COL), 1)
                    for s in range(FOLD):
                        value = main[8 * s : 8 * s + 8, :]
                        rest = jnp.broadcast_to(total[PART + s : PART + s + 1], (8, COL))
                        for q in range(8):
                            moved = pltpu.roll(rest, (2 * COL - 2 * LON - SPARE * q) % COL, 1)
                            value = jnp.where(jnp.logical_and(row == q, lane >= COL - 2 * LON), moved, value)
                        at = half * PART + 8 * s
                        col_halo[side, 2, at : at + 8, :] = value
                corrections(part, side, True)
                if part == 0:
                    contribute(side, True)

            @pl.when(lon == (0 if side == 0 else n_lon - 1))
            def _():
                for source in range(TARGETS):
                    l_arrival(part, source).wait_recv()
                for half in range(2):
                    total = got_rows[part, half * GROUPS]
                    for group in range(1, GROUPS):
                        total = total + got_rows[part, half * GROUPS + group]
                    row_halo[side, :, half * PART : (half + 1) * PART, :] = total
                corrections(part, side, False)
                if part == 0:
                    contribute(side, False)

    for part in range(2):
        if part == 0:
            message_tables()
            copies[3].wait()
            interpolate(0, 0)
            copies[4].wait()
            interpolate(0, 1)
            greetings = 2 * len(AROUND) + 2 + GROUPS + 2
            greetings = greetings + jnp.where(col_edge, TARGETS, 0) + jnp.where(lon_edge, TARGETS, 0)
            pl.semaphore_wait(barrier, greetings)
            send(0, 0)
            send(0, 1)

            @pl.when(col_edge)
            def _():
                for source in range(TARGETS):
                    idx_copy(source).start()

            @pl.when(lon_edge)
            def _():
                for source in range(TARGETS):
                    end_copy(source).start()

            other_tables()
        else:
            send(1, 0)
            send(1, 1)
            apply_edges()
        rows_of(part)
        for side in range(2):

            @pl.when(sends_rows[side])
            def _():
                row_copy(part, side).start()

        cols_of(part)
        for side in range(2):

            @pl.when(sends_cols[side])
            def _():
                col_copy(part, side).start()

        lane_pass(part)
        emf_pass(part)
        if part == 0:
            for target in range(GROUPS):
                idx_arrival(target).wait_recv()
            for side in range(2):
                end_arrival(side).wait_recv()
            prepare_picks()
        for step in range(1, GROUP):
            a_arrival(part, step).wait_recv()
        both = table_split(part)
        pick_all(part, both)
        main_pass(part, 0, 6)
        if part == 0:
            interpolate(1, 0)
            interpolate(1, 1)
        inner_sides(part)
        outer_sides(part)

    @pl.when(col_edge)
    def _():
        for source in range(TARGETS):
            idx_copy(source).wait_send()

    @pl.when(lon_edge)
    def _():
        for source in range(TARGETS):
            end_copy(source).wait_send()

    for part in range(2):
        for half in range(2):
            for step in AROUND:
                a_copy(part, step, half).wait_send()
        s_copy(part, 0).wait_send()
        for side in range(2):
            l_copy(part, side).wait_send()

            @pl.when(sends_rows[side])
            def _():
                row_copy(part, side).wait_send()

            @pl.when(sends_cols[side])
            def _():
                col_copy(part, side).wait_send()

        for target in range(GROUPS):
            b_copy(part, target).wait_send()


def shards(state, send_base, send_frac, recv_slots):
    rows = FLAT * LON
    dma = pltpu.SemaphoreType.DMA
    vmem = pltpu.VMEM
    scratch = [
        vmem((2, FLAT, STRIDE, COL), F32),
        vmem((1, OUT), I32),
        vmem((2, OUT), F32),
        vmem((1, recv_slots.shape[-1]), I32),
        vmem((3 * SHELLS * STRIDE, COL), F32),
        vmem(((FLAT + 2 * SHELLS) * LON, 2 * COL), F32),
        vmem((3 * COL, SLOTS), BF16),
        vmem((COL, SLOTS), F32),
        vmem((LON, SLOTS), F32),
        vmem((3 * COL, SLOTS), BF16),
        vmem((2 * COL, 2 * COL), BF16),
        vmem((TILES, SLOTS, 2 * COL), BF16),
        vmem((TILES, 8, 2 * COL), I32),
        vmem((2, COL, COL), F32),
        vmem((2, 2, PART, SLOTS), F32),
        vmem((2, GROUP, PART, SLOTS), F32),
        vmem((8, COL), I32),
        vmem((GROUPS, 8, COL), I32),
        vmem((2, 8, COL), I32),
        vmem((FOLD, 8, COL), F32),
        vmem((2, GROUPS, PART + FOLD, COL), F32),
        vmem((2, 2, HALO, PART, COL), F32),
        vmem((2, TARGETS, PART + FOLD, COL), F32),
        vmem((2, TARGETS, HALO, PART, COL), F32),
        vmem((2, 2, HALO, FLAT, COL), F32),
        vmem((2, 2, HALO, FLAT, COL), F32),
        vmem((2, 2, HALO, FLAT, COL), F32),
        vmem((2, 2, 2, FLAT, COL), F32),
        vmem((2, 2, 2, FLAT, COL), F32),
        vmem((2, HALO, FLAT, COL), F32),
        vmem((2, HALO, FLAT, COL), F32),
        dma((5,)),
        dma((TARGETS,)),
        dma((GROUPS,)),
        dma((TARGETS,)),
        dma((2,)),
        dma((2, 2, RING)),
        dma((2, GROUP)),
        dma((2,)),
        dma((2, GROUPS)),
        dma((2, TARGETS)),
        dma((2, 2)),
        dma((2, TARGETS)),
        dma((2, 2)),
        dma((2, 2)),
        dma((2, 2)),
        dma((2, 2)),
    ]
    edges = jax.ShapeDtypeStruct((2, HALO, FLAT, COL), F32)
    value, row_add, col_add = pl.pallas_call(
        kernel,
        out_shape=(jax.ShapeDtypeStruct((rows, COL), F32), edges, edges),
        in_specs=[pl.BlockSpec(memory_space=pltpu.HBM)] * 4,
        out_specs=[pl.BlockSpec(memory_space=pltpu.VMEM)] * 3,
        scratch_shapes=scratch,
        compiler_params=pltpu.CompilerParams(
            collective_id=0, has_side_effects=True, vmem_limit_bytes=40 * 1024 * 1024
        ),
    )(*(
        pltpu.with_memory_space_constraint(x, pltpu.HBM)
        for x in (state.reshape(FLAT, LON, COL), send_base[0], send_frac[0, 0], recv_slots[0])
    ))
    result = pl.pallas_call(
        closing,
        out_shape=jax.ShapeDtypeStruct((rows, COL), F32),
        in_specs=[pl.BlockSpec(memory_space=pltpu.VMEM)] * 3,
        out_specs=pl.BlockSpec(memory_space=pltpu.HBM),
        scratch_shapes=[vmem((2, COL, COL), F32), vmem((rows, COL), F32), dma((8,))],
        compiler_params=pltpu.CompilerParams(vmem_limit_bytes=16 * 1024 * 1024),
    )(value, row_add, col_add)
    return result.reshape(state.shape)


def solution(mesh):
    placed = (
        P("panel", None, None, "lon", "colat"),
        P("panel", ("lon", "colat"), None),
        P("panel", ("lon", "colat"), None, None),
        P("panel", ("lon", "colat"), None),
    )
    return jax.shard_map(
        shards,
        mesh=mesh,
        in_specs=placed,
        out_specs=P("panel", None, None, "lon", "colat"),
        check_vma=False,
    )
```

```python
import math

import jax
import jax.numpy as jnp
from jax import lax
from jax.experimental import pallas as pl
from jax.experimental.pallas import tpu as pltpu
from jax.sharding import PartitionSpec as P

MESH = pl.DeviceIdType.MESH
F32, BF16, I32 = jnp.float32, jnp.bfloat16, jnp.int32

QUANTITIES = 8
SHELLS = 4
FLAT = QUANTITIES * SHELLS
LON = 48
COL = 128
HALO = 3
OUT = 240
SIDE = HALO * LON
SLOTS = 256
GROUP = 8
GROUPS = 8
AROUND = (2, 1, 3)
FAR_FIRST = (1, 3, 5, 7, 0, 2, 4, 6)
SPARE = SIDE - COL
PART = FLAT // 2
TARGETS = 2 * GROUPS
TILES = 12
RING = 4
FOLD = PART // 8
STRIDE = LON + 16
TIME_STEP = 0.25
SPREAD = 0.1 / 3.0
S, MR, MT, MP, BR, BT, BP, WARM = range(QUANTITIES)


def dot(left, right):
    return jnp.dot(left, right, preferred_element_type=F32)


def split(value):
    high = value.astype(BF16)
    return high, (value - high.astype(F32)).astype(BF16)


def iota(shape, dim):
    return lax.broadcasted_iota(I32, shape, dim)


def cross_radial(m, b):
    return m[1] * b[2] - m[2] * b[1]


def cross_polar(m, b):
    return m[2] * b[0] - m[0] * b[2]


def cross_azimuthal(m, b):
    return m[0] * b[1] - m[1] * b[0]


def edge_rates(own, d, lap, emf_first, emf_second, along_lanes):
    grow, thin = jnp.exp(own[WARM]), jnp.exp(-own[S])
    b = own[BR:WARM]
    if along_lanes:
        vel, out = own[MT], MT
        lorentz = (d[BR] * b[1], -d[BR] * b[0] - d[BP] * b[2], d[BP] * b[1])
        turn = (emf_first, None, -emf_second)
    else:
        vel, out = own[MP], MP
        lorentz = (d[BR] * b[2], d[BT] * b[2], -d[BT] * b[1] - d[BR] * b[0])
        turn = (-emf_first, emf_second, None)
    result = [-vel * d[S] - d[out]]
    for i in range(3):
        rate = -vel * d[MR + i] + thin * lorentz[i] + SPREAD * lap[MR + i]
        if MR + i == out:
            rate = rate - grow * (d[S] + d[WARM])
        result.append(rate)
    for i in range(3):
        rate = SPREAD * lap[BR + i]
        result.append(rate if turn[i] is None else rate + turn[i])
    result.append(-vel * d[WARM] - (2.0 / 3.0) * d[out] + SPREAD * lap[WARM])
    return result


def shell_steps(x):
    a, b, c = x[1] - x[0], x[2] - x[0], x[3] - x[0]
    p, q, r = 45.0 * a, 45.0 * b, 37.0 * c
    first = (p - 9.0 * b + c, q - 8.0 * c, r - p, r - q + 9.0 * a)
    p, q, r = 270.0 * a, 270.0 * b, 245.0 * c
    second = (p - 27.0 * b + 2.0 * c, q - 490.0 * a - 25.0 * c, p - 490.0 * b + r, q - 27.0 * a - r)
    return first, second


def turn_edges(col_add, turned):
    for side in range(2):
        for j in range(HALO):
            for half in range(2):
                turned[half, pl.ds((1 - side) * HALO + j, FLAT // 2, stride=8), :] = col_add[
                    side, j, half * (FLAT // 2) : (half + 1) * (FLAT // 2), :
                ]


def field_edge(edge, g):
    lane = iota((LON, COL), 1)
    border = jnp.logical_or(lane < HALO, lane >= COL - HALO)
    return jnp.where(border, pltpu.roll(edge, COL - 8 * g - HALO, 1), 0.0)


def closing(value_ref, row_add, col_add, out_hbm, turned, ready, sem):
    turn_edges(col_add, turned)
    copies = []
    for half in range(2):
        edge = jnp.transpose(turned[half])[0:LON, :]
        for chunk in range(4):
            first = half * (FLAT // 2) + 4 * chunk
            for q in range(4):
                at = (first + q) * LON
                ready[at : at + LON, :] = value_ref[at : at + LON, :] + field_edge(edge, 4 * chunk + q)
            for side in range(2):
                for j in range(HALO):
                    rows = pl.ds(first * LON + (j if side == 0 else LON - HALO + j), 4, stride=LON)
                    ready[rows, :] = ready[rows, :] + row_add[side, j, first : first + 4, :]
            rows = pl.ds(first * LON, 4 * LON)
            copy = pltpu.make_async_copy(ready.at[rows, :], out_hbm.at[rows, :], sem.at[4 * half + chunk])
            copy.start()
            copies.append(copy)
    for copy in copies:
        copy.wait()


def kernel(
    x_hbm, base_hbm, frac_hbm, slots_hbm, out_ref, row_add, col_add,
    deep, base_ref, frac_ref, slots_ref, emf, lanes, mix, cols_mix, rows_mix, rows_split, band, onehot, owner, turned,
    blocks, table, idx_out, idx_in, rest_rows, picked, picked_rows, got_cols, got_rows, row_out, row_in, col_own, col_out, col_in,
    row_halo, col_halo,
    in_sem, idx_send, idx_recv, a_send, a_recv, s_send, b_send, b_recv, l_send, l_recv, r_send, r_recv, c_send, c_recv,
):
    panel, lon, col = lax.axis_index("panel"), lax.axis_index("lon"), lax.axis_index("colat")
    n_lon, n_col = lax.axis_size("lon"), lax.axis_size("colat")
    core, mine = lon & 1, lon >> 1
    member = core * n_col + col
    other = 1 - panel
    lon_up, lon_down = lax.rem(lon + 1, n_lon), lax.rem(lon + n_lon - 1, n_lon)
    col_up, col_down = lax.rem(col + 1, n_col), lax.rem(col + n_col - 1, n_col)
    outer = lax.rem(lon + 2 * core - 1 + n_lon, n_lon)
    sends_rows = (lon < n_lon - 1, lon > 0)
    sends_cols = (col < n_col - 1, col > 0)
    col_edge = jnp.logical_or(col == 0, col == n_col - 1)

    sibling = (panel, lon + 1 - 2 * core, col)
    origin = core * GROUPS + mine

    def row_device(step, half):
        return (panel, 2 * mine + half, (col + step) & (n_col - 1))

    def target_device(target):
        return (other, 2 * (target & (GROUPS - 1)) + (target >> 3), col)

    def remote(src, dst, send, recv, device):
        return pltpu.make_async_remote_copy(
            src_ref=src, dst_ref=dst, send_sem=send, recv_sem=recv, device_id=device, device_id_type=MESH
        )

    frame = deep.reshape(2, FLAT * STRIDE, COL)
    copies = [
        pltpu.make_async_copy(src, dst, in_sem.at[i])
        for i, (src, dst) in enumerate(
            (
                (frac_hbm, frac_ref),
                (base_hbm, base_ref),
                (slots_hbm, slots_ref),
                (x_hbm.at[pl.ds(0, PART)], deep.at[0, pl.ds(0, PART), pl.ds(8, LON), :]),
                (x_hbm.at[pl.ds(PART, PART)], deep.at[0, pl.ds(PART, PART), pl.ds(8, LON), :]),
            )
        )
    ]
    for copy in copies:
        copy.start()

    barrier = pltpu.get_barrier_semaphore()
    for step in AROUND:
        for half in range(2):
            pl.semaphore_signal(barrier, inc=1, device_id=row_device(step, half), device_id_type=MESH)
    pl.semaphore_signal(barrier, inc=1, device_id=sibling, device_id_type=MESH)
    for target in range(TARGETS):
        pl.semaphore_signal(barrier, inc=1, device_id=target_device(target), device_id_type=MESH)
    pl.semaphore_signal(barrier, inc=1, device_id=(panel, outer, col), device_id_type=MESH)

    copies[0].wait()
    copies[1].wait()
    base = jnp.concatenate([base_ref[...], jnp.zeros((1, SLOTS - OUT), I32)], axis=1)
    base_row, base_col = lax.div(base, COL), lax.rem(base, COL)
    share = jnp.concatenate([frac_ref[...], jnp.zeros((2, SLOTS - OUT), F32)], axis=1)
    along, across = share[0:1, :], share[1:2, :]
    cells = iota((COL, SLOTS), 0)
    weight = jnp.where(cells == base_col, 1.0 - across, 0.0) + jnp.where(cells == base_col + 1, across, 0.0)
    weight_high, weight_low = split(weight)
    cols_mix[...] = weight
    mix[0:COL, :] = weight_high
    mix[COL : 2 * COL, :] = weight_high
    mix[2 * COL : 3 * COL, :] = weight_low
    cells = iota((LON, SLOTS), 0)
    weight = jnp.where(cells == base_row, 1.0 - along, 0.0) + jnp.where(cells == base_row + 1, along, 0.0)
    rows_mix[...] = weight
    place = (col * COL + iota((1, COL), 1)).astype(F32)
    scale = 1.0 / jnp.sin(math.pi / 4.0 + (place + 0.5) * (math.pi / 2.0 / (COL * n_col)))

    def message_tables():
        copies[2].wait()
        spot = iota((1, SLOTS), 1)
        sides = jnp.where(spot < SIDE, jnp.maximum(slots_ref[:, 0:SLOTS], slots_ref[:, SIDE : SIDE + SLOTS]) + 1, 0)
        digits = jnp.concatenate([lax.div(sides, COL), lax.rem(sides, COL), jnp.zeros((6, SLOTS), I32)], axis=0)
        source, target = iota((SLOTS, SLOTS), 0), iota((SLOTS, SLOTS), 1)
        layer = jnp.where(target >= LON, 1, 0) + jnp.where(target >= 2 * LON, 1, 0)
        order = jnp.logical_and(target < SIDE, source == HALO * (target - LON * layer) + layer)
        digits = dot(digits.astype(F32).astype(BF16), jnp.where(order, 1.0, 0.0).astype(BF16)).astype(I32)
        sides = digits[0:1, :] * COL + digits[1:2, :] - 1
        idx_out[0:1, :] = sides[:, 0:COL]
        idx_out[1:2, :] = sides[:, COL : 2 * COL]
        for h in range(HALO):
            at = 2 * SIDE + h * COL
            idx_out[2 + h : 3 + h, :] = jnp.maximum(
                slots_ref[:, at : at + COL], slots_ref[:, at + HALO * COL : at + HALO * COL + COL]
            )
        idx_out[5:8, :] = jnp.full((3, COL), -1, I32)

    def other_tables():
        zero_rows = jnp.zeros((8, COL), F32)
        for f in range(FLAT):
            for part in range(2):
                frame[part, f * STRIDE : f * STRIDE + 8, :] = zero_rows
                frame[part, f * STRIDE + 8 + LON : (f + 1) * STRIDE, :] = zero_rows
        for f in range(3 * SHELLS):
            emf[f * STRIDE : f * STRIDE + 8, :] = zero_rows
            emf[f * STRIDE + 8 + LON : (f + 1) * STRIDE, :] = zero_rows

        for half in range(2):
            turned[half, :, :] = jnp.zeros((COL, COL), F32)

        apart = iota((COL, COL), 0) - iota((COL, COL), 1)
        reach = jnp.abs(apart)
        first = jnp.where(reach == 1, 45.0, jnp.where(reach == 2, -9.0, jnp.where(reach == 3, 1.0, 0.0)))
        first = jnp.where(apart < 0, -first, first).astype(BF16)
        second = jnp.where(
            reach == 0, -490.0, jnp.where(reach == 1, 270.0, jnp.where(reach == 2, -27.0, jnp.where(reach == 3, 2.0, 0.0)))
        ).astype(BF16)
        for part in range(2):
            band[part * COL : (part + 1) * COL, 0:COL] = first
            band[part * COL : (part + 1) * COL, COL : 2 * COL] = second
        weight_high, weight_low = split(jnp.concatenate([rows_mix[...], jnp.zeros((COL - LON, SLOTS), F32)], axis=0))
        rows_split[0:COL, :] = weight_high
        rows_split[COL : 2 * COL, :] = weight_high
        rows_split[2 * COL : 3 * COL, :] = weight_low

    def load_split(part, pair):
        block = jnp.concatenate(
            [frame[part, pl.ds(pl.multiple_of((8 * pair + q) * STRIDE + 8, 8), LON), :] for q in range(8)], axis=0
        )
        return split(block)

    def interpolate(part, half):
        for pair in range(PART // 8):
            high, low = load_split(part, 2 * half + pair)
            value = dot(jnp.concatenate([high, low, high], axis=1), mix[...])
            value = jnp.sum(value.reshape(8, LON, SLOTS) * rows_mix[...][None], axis=1)
            blocks[part, half, 8 * pair : 8 * pair + 8, :] = value

    def send(part, half):
        for step in AROUND:
            a_copy(part, step, half).start()

        @pl.when(core != half)
        def _():
            s_copy(part, half).start()

        @pl.when(core == half)
        def _():
            table[part, member] = blocks[part, half]

    def lane_pass(part):
        for pair in range(FLAT // 8):
            high, low = load_split(part, pair)
            both = jnp.concatenate([high, low], axis=1)
            lanes[8 * LON * pair : 8 * LON * (pair + 1), :] = dot(both, band[...])

    def cols_of(part):
        lane = iota((LON, COL), 1)
        for half in range(2):
            edge = jnp.zeros((LON, COL), F32)
            for g in range(FLAT // 2):
                at = (half * (FLAT // 2) + g) * STRIDE + 8
                moved = pltpu.roll(frame[part, at : at + LON, :], 8 * g + HALO, 1)
                edge = jnp.where(jnp.logical_and(lane >= 8 * g, lane < 8 * g + 2 * HALO), moved, edge)
            turned[half, :, 0:LON] = jnp.transpose(edge)
        for side in range(2):
            for j in range(HALO):
                first = (1 - side) * HALO + j
                for half in range(2):
                    col_own[part, side, j, half * (FLAT // 2) : (half + 1) * (FLAT // 2), :] = turned[
                        half, pl.ds(first, FLAT // 2, stride=8), :
                    ]
            col_out[part, side, 0] = jnp.where(
                iota((FLAT, COL), 1) < COL // 2, col_own[part, side, 0], pltpu.roll(col_own[part, side, 1], COL // 2, 1)
            )
            col_out[part, side, 1] = col_own[part, side, 2]

    def emf_pass(part):
        for r in range(SHELLS):
            def field(q):
                at = (q * SHELLS + r) * STRIDE + 8
                return frame[part, at : at + LON, :]

            m, b = [field(MR + i) for i in range(3)], [field(BR + i) for i in range(3)]
            for i, form in enumerate((cross_radial, cross_polar, cross_azimuthal)):
                at = (i * SHELLS + r) * STRIDE + 8
                emf[at : at + LON, :] = form(m, b)
        for i, at in ((0, FLAT), (2, FLAT + SHELLS)):
            block = jnp.concatenate(
                [emf[(i * SHELLS + r) * STRIDE + 8 : (i * SHELLS + r) * STRIDE + 8 + LON, :] for r in range(SHELLS)],
                axis=0,
            )
            high, low = split(block)
            lanes[at * LON : (at + SHELLS) * LON, 0:COL] = dot(
                jnp.concatenate([high, low], axis=1), band[:, 0:COL]
            )

    def main_pass(part, start, stop):
        def body(block, carry):
            here = pl.multiple_of(8 * block, 8)

            def near(f, apart):
                return frame[part, pl.ds(f * STRIDE + 8 + here + apart, 8), :]

            def near_emf(f, apart):
                return emf[pl.ds(f * STRIDE + 8 + here + apart, 8), :]

            def lane_first(f):
                return lanes[pl.ds(f * LON + here, 8), 0:COL]

            def lane_second(f):
                return lanes[pl.ds(f * LON + here, 8), COL : 2 * COL]

            def row_first(at):
                return 45.0 * (at[1] - at[-1]) - 9.0 * (at[2] - at[-2]) + (at[3] - at[-3])

            def row_second(at, centre):
                return (
                    270.0 * (at[1] + at[-1]) - 27.0 * (at[2] + at[-2]) + 2.0 * (at[3] + at[-3]) - 490.0 * centre
                )

            centre = [[near(q * SHELLS + r, 0) for r in range(SHELLS)] for q in range(QUANTITIES)]
            steps = [shell_steps(x) for x in centre]
            radial, radial_second = [x[0] for x in steps], [x[1] for x in steps]
            emf_centre = [[near_emf(i * SHELLS + r, 0) for r in range(SHELLS)] for i in range(3)]
            emf_radial = [None, shell_steps(emf_centre[1])[0], shell_steps(emf_centre[2])[0]]
            for r in range(SHELLS):
                own = [centre[q][r] for q in range(QUANTITIES)]
                g, lap = [], []
                for q in range(QUANTITIES):
                    f = q * SHELLS + r
                    at = {d: near(f, d) for d in (-3, -2, -1, 1, 2, 3)}
                    g.append((radial[q][r], lane_first(f), scale * row_first(at)))
                    if q == S:
                        lap.append(None)
                    else:
                        lap.append(
                            radial_second[q][r] + lane_second(f) + (scale * scale) * row_second(at, own[q])
                        )
                m, b = own[MR:BR], own[BR:WARM]

                def advect(q):
                    return m[0] * g[q][0] + m[1] * g[q][1] + m[2] * g[q][2]

                div = g[MR][0] + g[MT][1] + g[MP][2]
                current = (g[BP][1] - g[BT][2], g[BR][2] - g[BP][0], g[BT][0] - g[BR][1])
                lorentz = (
                    current[1] * b[2] - current[2] * b[1],
                    current[2] * b[0] - current[0] * b[2],
                    current[0] * b[1] - current[1] * b[0],
                )
                grow, thin = jnp.exp(own[WARM]), jnp.exp(-own[S])
                emf_rows = {}
                for i in (0, 1):
                    f = i * SHELLS + r
                    emf_rows[i] = scale * row_first({d: near_emf(f, d) for d in (-3, -2, -1, 1, 2, 3)})
                turn = (
                    lane_first(FLAT + SHELLS + r) - emf_rows[1],
                    emf_rows[0] - emf_radial[2][r],
                    emf_radial[1][r] - lane_first(FLAT + r),
                )
                result = [-advect(S) - div]
                for i in range(3):
                    result.append(
                        -advect(MR + i) - grow * (g[S][i] + g[WARM][i]) + thin * lorentz[i] + SPREAD * lap[MR + i]
                    )
                for i in range(3):
                    result.append(turn[i] + SPREAD * lap[BR + i])
                result.append(-advect(WARM) - (2.0 / 3.0) * div + SPREAD * lap[WARM])
                for q in range(QUANTITIES):
                    f = q * SHELLS + r
                    value = own[q] + (TIME_STEP / 60.0) * result[q]
                    if part == 0:
                        frame[1, pl.ds(f * STRIDE + 8 + here, 8), :] = value
                    else:
                        start = frame[0, pl.ds(f * STRIDE + 8 + here, 8), :]
                        out_ref[pl.ds(f * LON + here, 8), :] = 0.5 * (start + value)
            return carry

        lax.fori_loop(start, stop, body, 0)

    def rows_of(part):
        for h in range(HALO):
            row_out[part, 0, h] = frame[part, pl.ds(8 + h, FLAT, stride=STRIDE), :]
            row_out[part, 1, h] = frame[part, pl.ds(8 + LON - HALO + h, FLAT, stride=STRIDE), :]

    def prepare_picks():
        for tile in range(2 * TILES):
            if tile < TARGETS:
                slot = idx_in[tile, 0:1, :]
            elif tile < TARGETS + 2:
                first = (tile - TARGETS) * GROUPS
                slot = idx_in[first, 1:2, :]
                for q in range(1, GROUPS):
                    slot = jnp.maximum(slot, pltpu.roll(idx_in[first + q], SPARE * q, 1)[1:2, :])
            else:
                side, h = divmod(tile - TARGETS - 2, HALO)
                slot = idx_in[side * (TARGETS - 1), 2 + h : 3 + h, :]
            slot = slot - mine * (GROUP * OUT)
            who = jnp.zeros_like(slot)
            for q in range(1, GROUP):
                who = who + jnp.where(slot >= q * OUT, 1, 0)
            cell = slot - who * OUT
            who = jnp.where(jnp.logical_and(slot >= 0, slot < GROUP * OUT), who, -1)
            at = (tile % 2) * COL
            owner[tile // 2, :, at : at + COL] = jnp.broadcast_to(who, (8, COL))
            hot = jnp.where(iota((SLOTS, COL), 0) == cell, 1.0, 0.0).astype(BF16)
            onehot[tile // 2, :, at : at + COL] = hot

    def table_split(part):
        high, low = split(table[part].reshape(GROUP * PART, SLOTS))
        return jnp.concatenate([high, low], axis=0)

    def product(both, tile):
        return dot(both, onehot[tile])

    def chosen(value, tile):
        value = value[0 : GROUP * PART] + value[GROUP * PART :]
        who = jnp.broadcast_to(owner[tile, 0:1, :], (PART, SLOTS))
        total = jnp.zeros((PART, SLOTS), F32)
        for q in range(GROUP):
            total = jnp.where(who == q, value[q * PART : (q + 1) * PART, :], total)
        return total[:, 0:COL], total[:, COL : 2 * COL]

    def fold(rests):
        turn = (lax.div(iota((8, COL), 1), SPARE) - iota((8, COL), 0)) & 7
        for half, rest in enumerate(rests):
            for s in range(FOLD):
                total = jnp.zeros((8, COL), F32)
                for d in range(8):
                    moved = rest[8 * s : 8 * s + 8, :]
                    if d:
                        moved = pltpu.roll(pltpu.roll(moved, SPARE * d, 1), 8 - d, 0)
                    total = jnp.where(turn == d, moved, total)
                rest_rows[half, s] = total

    def pick_all(part, both):
        sides = [(core * (GROUPS // 2) + (mine >> 1)) ^ place for place in FAR_FIRST]
        extra = list(range(TARGETS // 2 + 1, TILES))
        ends, value = [], product(both, extra[0])
        for tile, after in zip(extra, extra[1:] + [None]):
            now = value
            if after is not None:
                value = product(both, after)
            ends += chosen(now, tile)
        for side in range(2):
            for h in range(HALO):
                picked_rows[part, side, h] = ends[side * HALO + h]
        for side in range(2):
            l_copy(part, side).start()

        @pl.when(col_edge)
        def _():
            now, value = product(both, TARGETS // 2), product(both, sides[0])
            fold(chosen(now, TARGETS // 2))
            for step, tile in enumerate(sides):
                now = value
                if step + 1 < len(sides):
                    value = product(both, sides[step + 1])
                for i, end in enumerate(chosen(now, tile)):
                    target = 2 * tile + i
                    picked[part, target, 0:PART, :] = end
                    for s in range(FOLD):
                        picked[part, target, PART + s : PART + s + 1, :] = rest_rows[
                            tile >> 2, s, pl.ds(target & (GROUPS - 1), 1), :
                        ]
                for i in range(2):
                    b_copy(part, 2 * tile + i).start()

    def corrections(part, side, along_lanes):
        halo_ref, own_ref, add_ref = (col_halo, col_own, col_add) if along_lanes else (row_halo, row_out, row_add)

        def scaled(value, power):
            for _ in range(0 if along_lanes else power):
                value = scale * value
            return value

        halo = [[halo_ref[side, h, q * SHELLS : (q + 1) * SHELLS, :] for q in range(QUANTITIES)] for h in range(HALO)]
        form = cross_azimuthal if along_lanes else cross_polar
        halo_emf = [(cross_radial(x[MR:BR], x[BR:WARM]), form(x[MR:BR], x[BR:WARM])) for x in halo]
        sign = -1.0 if side == 0 else 1.0
        firsts, seconds = (45.0 * sign, -9.0 * sign, sign), (270.0, -27.0, 2.0)
        for j in range(HALO):
            own = [own_ref[part, side, j, q * SHELLS : (q + 1) * SHELLS, :] for q in range(QUANTITIES)]

            def total(weights, of):
                result = None
                for m in (1, 2, 3):
                    h = j + 3 - m if side == 0 else m - 3 + j
                    if 0 <= h < HALO:
                        term = weights[m - 1] * of(h)
                        result = term if result is None else result + term
                return result

            d = [scaled(total(firsts, lambda h, q=q: halo[h][q]), 1) for q in range(QUANTITIES)]
            lap = [
                None if q == S else scaled(total(seconds, lambda h, q=q: halo[h][q]), 2) for q in range(QUANTITIES)
            ]
            radial = scaled(total(firsts, lambda h: halo_emf[h][0]), 1)
            second = scaled(total(firsts, lambda h: halo_emf[h][1]), 1)
            result = edge_rates(own, d, lap, second, radial, along_lanes)
            for q in range(QUANTITIES):
                add_ref[side, j, q * SHELLS : (q + 1) * SHELLS, :] = (TIME_STEP / 60.0 / (1 + part)) * result[q]

    def contribute(side, along_lanes):
        add_ref = col_add if along_lanes else row_add
        value = jnp.concatenate([add_ref[side, j] for j in range(HALO)], axis=0)
        if along_lanes:
            value = jnp.where(iota((HALO * FLAT, COL), 1) < LON, value, 0.0)
        high, low = split(value)
        value = dot(jnp.concatenate([high, low, high], axis=1), rows_split[...] if along_lanes else mix[...])
        total = jnp.zeros((FLAT, SLOTS), F32)
        for j in range(HALO):
            if along_lanes:
                at = j if side == 0 else COL - HALO + j
                weight = cols_mix[at : at + 1, :]
            else:
                at = j if side == 0 else LON - HALO + j
                weight = rows_mix[at : at + 1, :]
            total = total + weight * value[j * FLAT : (j + 1) * FLAT, :]
        for half in range(2):
            blocks[1, half] = blocks[1, half] + total[half * PART : (half + 1) * PART, :]

    def apply_edges():
        for side in range(2):
            for j in range(HALO):
                rows = pl.ds(8 + (j if side == 0 else LON - HALO + j), FLAT, stride=STRIDE)
                frame[1, rows, :] = frame[1, rows, :] + row_add[side, j]
        turn_edges(col_add, turned)
        for half in range(2):
            edge = jnp.transpose(turned[half])[0:LON, :]
            for g in range(FLAT // 2):
                at = (half * (FLAT // 2) + g) * STRIDE + 8
                frame[1, at : at + LON, :] = frame[1, at : at + LON, :] + field_edge(edge, g)

    def a_copy(part, step, half):
        return remote(
            blocks.at[part, half], table.at[part, member], a_send.at[part, half, step], a_recv.at[part, member],
            row_device(step, half),
        )

    def s_copy(part, half):
        return remote(
            blocks.at[part, half], table.at[part, member], s_send.at[part], a_recv.at[part, member], sibling
        )

    def a_arrival(part, step):
        there = (member + step) & (GROUP - 1)
        return remote(blocks.at[part, 0], table.at[part, there], s_send.at[part], a_recv.at[part, there], sibling)

    def b_copy(part, target):
        return remote(
            picked.at[part, target], got_cols.at[part, origin], b_send.at[part, target], b_recv.at[part, origin],
            target_device(target),
        )

    def b_arrival(part, source):
        return remote(
            picked.at[part, 0], got_cols.at[part, source], b_send.at[part, 0], b_recv.at[part, source],
            (other, lon, col),
        )

    def l_copy(part, side):
        return remote(
            picked_rows.at[part, side], got_rows.at[part, origin], l_send.at[part, side], l_recv.at[part, origin],
            target_device(side * (TARGETS - 1)),
        )

    def l_arrival(part, source):
        return remote(
            picked_rows.at[part, 0], got_rows.at[part, source], l_send.at[part, 0], l_recv.at[part, source],
            (other, lon, col),
        )

    def row_copy(part, side):
        return remote(
            row_out.at[part, 1 - side], row_in.at[part, side], r_send.at[part, side], r_recv.at[part, side],
            (panel, lon_up if side == 0 else lon_down, col),
        )

    def col_copy(part, side):
        return remote(
            col_out.at[part, 1 - side], col_in.at[part, side], c_send.at[part, side], c_recv.at[part, side],
            (panel, lon, col_up if side == 0 else col_down),
        )

    def idx_copy(target):
        return remote(
            idx_out, idx_in.at[origin], idx_send.at[target], idx_recv.at[origin], target_device(target)
        )

    def idx_arrival(source):
        return remote(idx_out, idx_in.at[source], idx_send.at[0], idx_recv.at[source], (other, lon, col))

    def inner_sides(part):
        for side in range(2):
            @pl.when(lon != (0 if side == 0 else n_lon - 1))
            def _():
                row_copy(part, side).wait_recv()
                row_halo[side] = row_in[part, side]
                corrections(part, side, False)
                if part == 0:
                    contribute(side, False)

            @pl.when(col != (0 if side == 0 else n_col - 1))
            def _():
                col_copy(part, side).wait_recv()
                pair = col_in[part, side, 0]
                col_halo[side, 0] = pair
                col_halo[side, 1] = pltpu.roll(pair, COL // 2, 1)
                col_halo[side, 2] = col_in[part, side, 1]
                corrections(part, side, True)
                if part == 0:
                    contribute(side, True)

    def outer_sides(part):
        for side in range(2):

            @pl.when(col == (0 if side == 0 else n_col - 1))
            def _():
                for source in range(TARGETS):
                    b_arrival(part, source).wait_recv()
                for half in range(2):
                    total = got_cols[part, half * GROUPS]
                    for group in range(1, GROUPS):
                        total = total + got_cols[part, half * GROUPS + group]
                    main = total[0:PART]
                    rows = slice(half * PART, (half + 1) * PART)
                    col_halo[side, 0, rows, :] = main
                    col_halo[side, 1, rows, :] = pltpu.roll(main, COL - LON, 1)
                    main = pltpu.roll(main, COL - 2 * LON, 1)
                    row, lane = iota((8, COL), 0), iota((8, COL), 1)
                    for s in range(FOLD):
                        value = main[8 * s : 8 * s + 8, :]
                        rest = jnp.broadcast_to(total[PART + s : PART + s + 1], (8, COL))
                        for q in range(8):
                            moved = pltpu.roll(rest, (2 * COL - 2 * LON - SPARE * q) % COL, 1)
                            value = jnp.where(jnp.logical_and(row == q, lane >= COL - 2 * LON), moved, value)
                        at = half * PART + 8 * s
                        col_halo[side, 2, at : at + 8, :] = value
                corrections(part, side, True)
                if part == 0:
                    contribute(side, True)

            @pl.when(lon == (0 if side == 0 else n_lon - 1))
            def _():
                for source in range(TARGETS):
                    l_arrival(part, source).wait_recv()
                for half in range(2):
                    total = got_rows[part, half * GROUPS]
                    for group in range(1, GROUPS):
                        total = total + got_rows[part, half * GROUPS + group]
                    row_halo[side, :, half * PART : (half + 1) * PART, :] = total
                corrections(part, side, False)
                if part == 0:
                    contribute(side, False)

    for part in range(2):
        if part == 0:
            message_tables()
            copies[3].wait()
            interpolate(0, 0)
            copies[4].wait()
            interpolate(0, 1)
            pl.semaphore_wait(barrier, 2 * len(AROUND) + 2 + TARGETS)
            send(0, 0)
            send(0, 1)
            for target in range(TARGETS):
                idx_copy(target).start()
            other_tables()
        else:
            send(1, 0)
            send(1, 1)
            apply_edges()
        rows_of(part)
        for side in range(2):

            @pl.when(sends_rows[side])
            def _():
                row_copy(part, side).start()

        cols_of(part)
        for side in range(2):

            @pl.when(sends_cols[side])
            def _():
                col_copy(part, side).start()

        lane_pass(part)
        emf_pass(part)
        if part == 0:
            for source in range(TARGETS):
                idx_arrival(source).wait_recv()
            prepare_picks()
        for step in range(1, GROUP):
            a_arrival(part, step).wait_recv()
        both = table_split(part)
        pick_all(part, both)
        main_pass(part, 0, 6)
        if part == 0:
            interpolate(1, 0)
            interpolate(1, 1)
        inner_sides(part)
        outer_sides(part)

    for target in range(TARGETS):
        idx_copy(target).wait_send()
    for part in range(2):
        for half in range(2):
            for step in AROUND:
                a_copy(part, step, half).wait_send()
        s_copy(part, 0).wait_send()
        for side in range(2):
            l_copy(part, side).wait_send()

            @pl.when(sends_rows[side])
            def _():
                row_copy(part, side).wait_send()

            @pl.when(sends_cols[side])
            def _():
                col_copy(part, side).wait_send()


        @pl.when(col_edge)
        def _():
            for target in range(TARGETS):
                b_copy(part, target).wait_send()


def shards(state, send_base, send_frac, recv_slots):
    rows = FLAT * LON
    dma = pltpu.SemaphoreType.DMA
    vmem = pltpu.VMEM
    scratch = [
        vmem((2, FLAT, STRIDE, COL), F32),
        vmem((1, OUT), I32),
        vmem((2, OUT), F32),
        vmem((1, recv_slots.shape[-1]), I32),
        vmem((3 * SHELLS * STRIDE, COL), F32),
        vmem(((FLAT + 2 * SHELLS) * LON, 2 * COL), F32),
        vmem((3 * COL, SLOTS), BF16),
        vmem((COL, SLOTS), F32),
        vmem((LON, SLOTS), F32),
        vmem((3 * COL, SLOTS), BF16),
        vmem((2 * COL, 2 * COL), BF16),
        vmem((TILES, SLOTS, 2 * COL), BF16),
        vmem((TILES, 8, 2 * COL), I32),
        vmem((2, COL, COL), F32),
        vmem((2, 2, PART, SLOTS), F32),
        vmem((2, GROUP, PART, SLOTS), F32),
        vmem((8, COL), I32),
        vmem((TARGETS, 8, COL), I32),
        vmem((2, FOLD, 8, COL), F32),
        vmem((2, TARGETS, PART + FOLD, COL), F32),
        vmem((2, 2, HALO, PART, COL), F32),
        vmem((2, TARGETS, PART + FOLD, COL), F32),
        vmem((2, TARGETS, HALO, PART, COL), F32),
        vmem((2, 2, HALO, FLAT, COL), F32),
        vmem((2, 2, HALO, FLAT, COL), F32),
        vmem((2, 2, HALO, FLAT, COL), F32),
        vmem((2, 2, 2, FLAT, COL), F32),
        vmem((2, 2, 2, FLAT, COL), F32),
        vmem((2, HALO, FLAT, COL), F32),
        vmem((2, HALO, FLAT, COL), F32),
        dma((5,)),
        dma((TARGETS,)),
        dma((TARGETS,)),
        dma((2, 2, RING)),
        dma((2, GROUP)),
        dma((2,)),
        dma((2, TARGETS)),
        dma((2, TARGETS)),
        dma((2, 2)),
        dma((2, TARGETS)),
        dma((2, 2)),
        dma((2, 2)),
        dma((2, 2)),
        dma((2, 2)),
    ]
    edges = jax.ShapeDtypeStruct((2, HALO, FLAT, COL), F32)
    value, row_add, col_add = pl.pallas_call(
        kernel,
        out_shape=(jax.ShapeDtypeStruct((rows, COL), F32), edges, edges),
        in_specs=[pl.BlockSpec(memory_space=pltpu.HBM)] * 4,
        out_specs=[pl.BlockSpec(memory_space=pltpu.VMEM)] * 3,
        scratch_shapes=scratch,
        compiler_params=pltpu.CompilerParams(
            collective_id=0, has_side_effects=True, vmem_limit_bytes=40 * 1024 * 1024
        ),
    )(*(
        pltpu.with_memory_space_constraint(x, pltpu.HBM)
        for x in (state.reshape(FLAT, LON, COL), send_base[0], send_frac[0, 0], recv_slots[0])
    ))
    result = pl.pallas_call(
        closing,
        out_shape=jax.ShapeDtypeStruct((rows, COL), F32),
        in_specs=[pl.BlockSpec(memory_space=pltpu.VMEM)] * 3,
        out_specs=pl.BlockSpec(memory_space=pltpu.HBM),
        scratch_shapes=[vmem((2, COL, COL), F32), vmem((rows, COL), F32), dma((8,))],
        compiler_params=pltpu.CompilerParams(vmem_limit_bytes=16 * 1024 * 1024),
    )(value, row_add, col_add)
    return result.reshape(state.shape)


def solution(mesh):
    placed = (
        P("panel", None, None, "lon", "colat"),
        P("panel", ("lon", "colat"), None),
        P("panel", ("lon", "colat"), None, None),
        P("panel", ("lon", "colat"), None),
    )
    return jax.shard_map(
        shards,
        mesh=mesh,
        in_specs=placed,
        out_specs=P("panel", None, None, "lon", "colat"),
        check_vma=False,
    )
```

```python
import math

import jax
import jax.numpy as jnp
from jax import lax
from jax.experimental import pallas as pl
from jax.experimental.pallas import tpu as pltpu
from jax.sharding import PartitionSpec as P

MESH = pl.DeviceIdType.MESH
F32, BF16, I32 = jnp.float32, jnp.bfloat16, jnp.int32

QUANTITIES = 8
SHELLS = 4
FLAT = QUANTITIES * SHELLS
LON = 48
COL = 128
HALO = 3
OUT = 240
SIDE = HALO * LON
SLOTS = 256
GROUP = 8
GROUPS = 8
AROUND = (2, 1, 3)
FAR_FIRST = (1, 3, 5, 7, 0, 2, 4, 6)
CROSS_ORDER = (2, 6, 10, 14, 1, 5, 9, 13, 3, 7, 11, 15, 0, 4, 8, 12)
SPARE = SIDE - COL
PART = FLAT // 2
TARGETS = 2 * GROUPS
TILES = 12
RING = 4
FOLD = PART // 8
STRIDE = LON + 16
TIME_STEP = 0.25
SPREAD = 0.1 / 3.0
S, MR, MT, MP, BR, BT, BP, WARM = range(QUANTITIES)


def dot(left, right):
    return jnp.dot(left, right, preferred_element_type=F32)


def split(value):
    high = value.astype(BF16)
    return high, (value - high.astype(F32)).astype(BF16)


def iota(shape, dim):
    return lax.broadcasted_iota(I32, shape, dim)


def cross_radial(m, b):
    return m[1] * b[2] - m[2] * b[1]


def cross_polar(m, b):
    return m[2] * b[0] - m[0] * b[2]


def cross_azimuthal(m, b):
    return m[0] * b[1] - m[1] * b[0]


def edge_rates(own, d, lap, emf_first, emf_second, along_lanes):
    grow, thin = jnp.exp(own[WARM]), jnp.exp(-own[S])
    b = own[BR:WARM]
    if along_lanes:
        vel, out = own[MT], MT
        lorentz = (d[BR] * b[1], -d[BR] * b[0] - d[BP] * b[2], d[BP] * b[1])
        turn = (emf_first, None, -emf_second)
    else:
        vel, out = own[MP], MP
        lorentz = (d[BR] * b[2], d[BT] * b[2], -d[BT] * b[1] - d[BR] * b[0])
        turn = (-emf_first, emf_second, None)
    result = [-vel * d[S] - d[out]]
    for i in range(3):
        rate = -vel * d[MR + i] + thin * lorentz[i] + SPREAD * lap[MR + i]
        if MR + i == out:
            rate = rate - grow * (d[S] + d[WARM])
        result.append(rate)
    for i in range(3):
        rate = SPREAD * lap[BR + i]
        result.append(rate if turn[i] is None else rate + turn[i])
    result.append(-vel * d[WARM] - (2.0 / 3.0) * d[out] + SPREAD * lap[WARM])
    return result


def shell_steps(x):
    a, b, c = x[1] - x[0], x[2] - x[0], x[3] - x[0]
    p, q, r = 45.0 * a, 45.0 * b, 37.0 * c
    first = (p - 9.0 * b + c, q - 8.0 * c, r - p, r - q + 9.0 * a)
    p, q, r = 270.0 * a, 270.0 * b, 245.0 * c
    second = (p - 27.0 * b + 2.0 * c, q - 490.0 * a - 25.0 * c, p - 490.0 * b + r, q - 27.0 * a - r)
    return first, second


def turn_edges(col_add, turned):
    for side in range(2):
        for j in range(HALO):
            for half in range(2):
                turned[half, pl.ds((1 - side) * HALO + j, FLAT // 2, stride=8), :] = col_add[
                    side, j, half * (FLAT // 2) : (half + 1) * (FLAT // 2), :
                ]


def field_edge(edge, g):
    lane = iota((LON, COL), 1)
    border = jnp.logical_or(lane < HALO, lane >= COL - HALO)
    return jnp.where(border, pltpu.roll(edge, COL - 8 * g - HALO, 1), 0.0)


def closing(value_ref, row_add, col_add, out_hbm, turned, ready, sem):
    turn_edges(col_add, turned)
    copies = []
    for half in range(2):
        edge = jnp.transpose(turned[half])[0:LON, :]
        for chunk in range(4):
            first = half * (FLAT // 2) + 4 * chunk
            for q in range(4):
                at = (first + q) * LON
                ready[at : at + LON, :] = value_ref[at : at + LON, :] + field_edge(edge, 4 * chunk + q)
            for side in range(2):
                for j in range(HALO):
                    rows = pl.ds(first * LON + (j if side == 0 else LON - HALO + j), 4, stride=LON)
                    ready[rows, :] = ready[rows, :] + row_add[side, j, first : first + 4, :]
            rows = pl.ds(first * LON, 4 * LON)
            copy = pltpu.make_async_copy(ready.at[rows, :], out_hbm.at[rows, :], sem.at[4 * half + chunk])
            copy.start()
            copies.append(copy)
    for copy in copies:
        copy.wait()


def kernel(
    x_hbm, base_hbm, frac_hbm, slots_hbm, out_ref, row_add, col_add,
    deep, base_ref, frac_ref, slots_ref, emf, lanes, mix, cols_mix, rows_mix, rows_split, band, onehot, owner, turned,
    blocks, table, idx_out, idx_in, rest_rows, picked, picked_rows, got_cols, got_rows, row_out, row_in, col_own, col_out, col_in,
    row_halo, col_halo,
    in_sem, idx_send, idx_recv, a_send, a_recv, s_send, b_send, b_recv, l_send, l_recv, r_send, r_recv, c_send, c_recv,
):
    panel, lon, col = lax.axis_index("panel"), lax.axis_index("lon"), lax.axis_index("colat")
    n_lon, n_col = lax.axis_size("lon"), lax.axis_size("colat")
    core, mine = lon & 1, lon >> 1
    member = core * n_col + col
    other = 1 - panel
    lon_up, lon_down = lax.rem(lon + 1, n_lon), lax.rem(lon + n_lon - 1, n_lon)
    col_up, col_down = lax.rem(col + 1, n_col), lax.rem(col + n_col - 1, n_col)
    outer = lax.rem(lon + 2 * core - 1 + n_lon, n_lon)
    sends_rows = (lon < n_lon - 1, lon > 0)
    sends_cols = (col < n_col - 1, col > 0)
    col_edge = jnp.logical_or(col == 0, col == n_col - 1)

    sibling = (panel, lon + 1 - 2 * core, col)
    origin = core * GROUPS + mine

    def row_device(step, half):
        return (panel, 2 * mine + half, (col + step) & (n_col - 1))

    def target_device(target):
        return (other, 2 * (target & (GROUPS - 1)) + (target >> 3), col)

    def remote(src, dst, send, recv, device):
        return pltpu.make_async_remote_copy(
            src_ref=src, dst_ref=dst, send_sem=send, recv_sem=recv, device_id=device, device_id_type=MESH
        )

    frame = deep.reshape(2, FLAT * STRIDE, COL)
    copies = [
        pltpu.make_async_copy(src, dst, in_sem.at[i])
        for i, (src, dst) in enumerate(
            (
                (frac_hbm, frac_ref),
                (base_hbm, base_ref),
                (slots_hbm, slots_ref),
                (x_hbm.at[pl.ds(0, PART)], deep.at[0, pl.ds(0, PART), pl.ds(8, LON), :]),
                (x_hbm.at[pl.ds(PART, PART)], deep.at[0, pl.ds(PART, PART), pl.ds(8, LON), :]),
            )
        )
    ]
    for copy in copies:
        copy.start()

    barrier = pltpu.get_barrier_semaphore()
    for step in AROUND:
        for half in range(2):
            pl.semaphore_signal(barrier, inc=1, device_id=row_device(step, half), device_id_type=MESH)
    pl.semaphore_signal(barrier, inc=1, device_id=sibling, device_id_type=MESH)
    for place in CROSS_ORDER:
        pl.semaphore_signal(barrier, inc=1, device_id=target_device(origin ^ place), device_id_type=MESH)
    pl.semaphore_signal(barrier, inc=1, device_id=(panel, outer, col), device_id_type=MESH)

    copies[0].wait()
    copies[1].wait()
    base = jnp.concatenate([base_ref[...], jnp.zeros((1, SLOTS - OUT), I32)], axis=1)
    base_row, base_col = lax.div(base, COL), lax.rem(base, COL)
    share = jnp.concatenate([frac_ref[...], jnp.zeros((2, SLOTS - OUT), F32)], axis=1)
    along, across = share[0:1, :], share[1:2, :]
    cells = iota((COL, SLOTS), 0)
    weight = jnp.where(cells == base_col, 1.0 - across, 0.0) + jnp.where(cells == base_col + 1, across, 0.0)
    weight_high, weight_low = split(weight)
    cols_mix[...] = weight
    mix[0:COL, :] = weight_high
    mix[COL : 2 * COL, :] = weight_high
    mix[2 * COL : 3 * COL, :] = weight_low
    cells = iota((LON, SLOTS), 0)
    weight = jnp.where(cells == base_row, 1.0 - along, 0.0) + jnp.where(cells == base_row + 1, along, 0.0)
    rows_mix[...] = weight
    place = (col * COL + iota((1, COL), 1)).astype(F32)
    scale = 1.0 / jnp.sin(math.pi / 4.0 + (place + 0.5) * (math.pi / 2.0 / (COL * n_col)))

    def message_tables():
        copies[2].wait()
        spot = iota((1, SLOTS), 1)
        sides = jnp.where(spot < SIDE, jnp.maximum(slots_ref[:, 0:SLOTS], slots_ref[:, SIDE : SIDE + SLOTS]) + 1, 0)
        digits = jnp.concatenate([lax.div(sides, COL), lax.rem(sides, COL), jnp.zeros((6, SLOTS), I32)], axis=0)
        source, target = iota((SLOTS, SLOTS), 0), iota((SLOTS, SLOTS), 1)
        layer = jnp.where(target >= LON, 1, 0) + jnp.where(target >= 2 * LON, 1, 0)
        order = jnp.logical_and(target < SIDE, source == HALO * (target - LON * layer) + layer)
        digits = dot(digits.astype(F32).astype(BF16), jnp.where(order, 1.0, 0.0).astype(BF16)).astype(I32)
        sides = digits[0:1, :] * COL + digits[1:2, :] - 1
        idx_out[0:1, :] = sides[:, 0:COL]
        idx_out[1:2, :] = sides[:, COL : 2 * COL]
        for h in range(HALO):
            at = 2 * SIDE + h * COL
            idx_out[2 + h : 3 + h, :] = jnp.maximum(
                slots_ref[:, at : at + COL], slots_ref[:, at + HALO * COL : at + HALO * COL + COL]
            )
        idx_out[5:8, :] = jnp.full((3, COL), -1, I32)

    def other_tables():
        zero_rows = jnp.zeros((8, COL), F32)
        for f in range(FLAT):
            for part in range(2):
                frame[part, f * STRIDE : f * STRIDE + 8, :] = zero_rows
                frame[part, f * STRIDE + 8 + LON : (f + 1) * STRIDE, :] = zero_rows
        for f in range(3 * SHELLS):
            emf[f * STRIDE : f * STRIDE + 8, :] = zero_rows
            emf[f * STRIDE + 8 + LON : (f + 1) * STRIDE, :] = zero_rows

        for half in range(2):
            turned[half, :, :] = jnp.zeros((COL, COL), F32)

        apart = iota((COL, COL), 0) - iota((COL, COL), 1)
        reach = jnp.abs(apart)
        first = jnp.where(reach == 1, 45.0, jnp.where(reach == 2, -9.0, jnp.where(reach == 3, 1.0, 0.0)))
        first = jnp.where(apart < 0, -first, first).astype(BF16)
        second = jnp.where(
            reach == 0, -490.0, jnp.where(reach == 1, 270.0, jnp.where(reach == 2, -27.0, jnp.where(reach == 3, 2.0, 0.0)))
        ).astype(BF16)
        for part in range(2):
            band[part * COL : (part + 1) * COL, 0:COL] = first
            band[part * COL : (part + 1) * COL, COL : 2 * COL] = second
        weight_high, weight_low = split(jnp.concatenate([rows_mix[...], jnp.zeros((COL - LON, SLOTS), F32)], axis=0))
        rows_split[0:COL, :] = weight_high
        rows_split[COL : 2 * COL, :] = weight_high
        rows_split[2 * COL : 3 * COL, :] = weight_low

    def load_split(part, pair):
        block = jnp.concatenate(
            [frame[part, pl.ds(pl.multiple_of((8 * pair + q) * STRIDE + 8, 8), LON), :] for q in range(8)], axis=0
        )
        return split(block)

    def interpolate(part, half):
        for pair in range(PART // 8):
            high, low = load_split(part, 2 * half + pair)
            value = dot(jnp.concatenate([high, low, high], axis=1), mix[...])
            value = jnp.sum(value.reshape(8, LON, SLOTS) * rows_mix[...][None], axis=1)
            blocks[part, half, 8 * pair : 8 * pair + 8, :] = value

    def send(part, half):
        for step in AROUND:
            a_copy(part, step, half).start()

        @pl.when(core != half)
        def _():
            s_copy(part, half).start()

        @pl.when(core == half)
        def _():
            table[part, member] = blocks[part, half]

    def lane_pass(part):
        for pair in range(FLAT // 8):
            high, low = load_split(part, pair)
            both = jnp.concatenate([high, low], axis=1)
            lanes[8 * LON * pair : 8 * LON * (pair + 1), :] = dot(both, band[...])

    def cols_of(part):
        lane = iota((LON, COL), 1)
        for half in range(2):
            edge = jnp.zeros((LON, COL), F32)
            for g in range(FLAT // 2):
                at = (half * (FLAT // 2) + g) * STRIDE + 8
                moved = pltpu.roll(frame[part, at : at + LON, :], 8 * g + HALO, 1)
                edge = jnp.where(jnp.logical_and(lane >= 8 * g, lane < 8 * g + 2 * HALO), moved, edge)
            turned[half, :, 0:LON] = jnp.transpose(edge)
        for side in range(2):
            for j in range(HALO):
                first = (1 - side) * HALO + j
                for half in range(2):
                    col_own[part, side, j, half * (FLAT // 2) : (half + 1) * (FLAT // 2), :] = turned[
                        half, pl.ds(first, FLAT // 2, stride=8), :
                    ]
            col_out[part, side, 0] = jnp.where(
                iota((FLAT, COL), 1) < COL // 2, col_own[part, side, 0], pltpu.roll(col_own[part, side, 1], COL // 2, 1)
            )
            col_out[part, side, 1] = col_own[part, side, 2]

    def emf_pass(part):
        for r in range(SHELLS):
            def field(q):
                at = (q * SHELLS + r) * STRIDE + 8
                return frame[part, at : at + LON, :]

            m, b = [field(MR + i) for i in range(3)], [field(BR + i) for i in range(3)]
            for i, form in enumerate((cross_radial, cross_polar, cross_azimuthal)):
                at = (i * SHELLS + r) * STRIDE + 8
                emf[at : at + LON, :] = form(m, b)
        for i, at in ((0, FLAT), (2, FLAT + SHELLS)):
            block = jnp.concatenate(
                [emf[(i * SHELLS + r) * STRIDE + 8 : (i * SHELLS + r) * STRIDE + 8 + LON, :] for r in range(SHELLS)],
                axis=0,
            )
            high, low = split(block)
            lanes[at * LON : (at + SHELLS) * LON, 0:COL] = dot(
                jnp.concatenate([high, low], axis=1), band[:, 0:COL]
            )

    def main_pass(part, start, stop):
        def body(block, carry):
            here = pl.multiple_of(8 * block, 8)

            def near(f, apart):
                return frame[part, pl.ds(f * STRIDE + 8 + here + apart, 8), :]

            def near_emf(f, apart):
                return emf[pl.ds(f * STRIDE + 8 + here + apart, 8), :]

            def lane_first(f):
                return lanes[pl.ds(f * LON + here, 8), 0:COL]

            def lane_second(f):
                return lanes[pl.ds(f * LON + here, 8), COL : 2 * COL]

            def row_first(at):
                return 45.0 * (at[1] - at[-1]) - 9.0 * (at[2] - at[-2]) + (at[3] - at[-3])

            def row_second(at, centre):
                return (
                    270.0 * (at[1] + at[-1]) - 27.0 * (at[2] + at[-2]) + 2.0 * (at[3] + at[-3]) - 490.0 * centre
                )

            centre = [[near(q * SHELLS + r, 0) for r in range(SHELLS)] for q in range(QUANTITIES)]
            steps = [shell_steps(x) for x in centre]
            radial, radial_second = [x[0] for x in steps], [x[1] for x in steps]
            emf_centre = [[near_emf(i * SHELLS + r, 0) for r in range(SHELLS)] for i in range(3)]
            emf_radial = [None, shell_steps(emf_centre[1])[0], shell_steps(emf_centre[2])[0]]
            for r in range(SHELLS):
                own = [centre[q][r] for q in range(QUANTITIES)]
                g, lap = [], []
                for q in range(QUANTITIES):
                    f = q * SHELLS + r
                    at = {d: near(f, d) for d in (-3, -2, -1, 1, 2, 3)}
                    g.append((radial[q][r], lane_first(f), scale * row_first(at)))
                    if q == S:
                        lap.append(None)
                    else:
                        lap.append(
                            radial_second[q][r] + lane_second(f) + (scale * scale) * row_second(at, own[q])
                        )
                m, b = own[MR:BR], own[BR:WARM]

                def advect(q):
                    return m[0] * g[q][0] + m[1] * g[q][1] + m[2] * g[q][2]

                div = g[MR][0] + g[MT][1] + g[MP][2]
                current = (g[BP][1] - g[BT][2], g[BR][2] - g[BP][0], g[BT][0] - g[BR][1])
                lorentz = (
                    current[1] * b[2] - current[2] * b[1],
                    current[2] * b[0] - current[0] * b[2],
                    current[0] * b[1] - current[1] * b[0],
                )
                grow, thin = jnp.exp(own[WARM]), jnp.exp(-own[S])
                emf_rows = {}
                for i in (0, 1):
                    f = i * SHELLS + r
                    emf_rows[i] = scale * row_first({d: near_emf(f, d) for d in (-3, -2, -1, 1, 2, 3)})
                turn = (
                    lane_first(FLAT + SHELLS + r) - emf_rows[1],
                    emf_rows[0] - emf_radial[2][r],
                    emf_radial[1][r] - lane_first(FLAT + r),
                )
                result = [-advect(S) - div]
                for i in range(3):
                    result.append(
                        -advect(MR + i) - grow * (g[S][i] + g[WARM][i]) + thin * lorentz[i] + SPREAD * lap[MR + i]
                    )
                for i in range(3):
                    result.append(turn[i] + SPREAD * lap[BR + i])
                result.append(-advect(WARM) - (2.0 / 3.0) * div + SPREAD * lap[WARM])
                for q in range(QUANTITIES):
                    f = q * SHELLS + r
                    value = own[q] + (TIME_STEP / 60.0) * result[q]
                    if part == 0:
                        frame[1, pl.ds(f * STRIDE + 8 + here, 8), :] = value
                    else:
                        start = frame[0, pl.ds(f * STRIDE + 8 + here, 8), :]
                        out_ref[pl.ds(f * LON + here, 8), :] = 0.5 * (start + value)
            return carry

        lax.fori_loop(start, stop, body, 0)

    def rows_of(part):
        for h in range(HALO):
            row_out[part, 0, h] = frame[part, pl.ds(8 + h, FLAT, stride=STRIDE), :]
            row_out[part, 1, h] = frame[part, pl.ds(8 + LON - HALO + h, FLAT, stride=STRIDE), :]

    def prepare_picks():
        for tile in range(2 * TILES):
            if tile < TARGETS:
                slot = idx_in[tile, 0:1, :]
            elif tile < TARGETS + 2:
                first = (tile - TARGETS) * GROUPS
                slot = idx_in[first, 1:2, :]
                for q in range(1, GROUPS):
                    slot = jnp.maximum(slot, pltpu.roll(idx_in[first + q], SPARE * q, 1)[1:2, :])
            else:
                side, h = divmod(tile - TARGETS - 2, HALO)
                slot = idx_in[side * (TARGETS - 1), 2 + h : 3 + h, :]
            slot = slot - mine * (GROUP * OUT)
            who = jnp.zeros_like(slot)
            for q in range(1, GROUP):
                who = who + jnp.where(slot >= q * OUT, 1, 0)
            cell = slot - who * OUT
            who = jnp.where(jnp.logical_and(slot >= 0, slot < GROUP * OUT), who, -1)
            at = (tile % 2) * COL
            owner[tile // 2, :, at : at + COL] = jnp.broadcast_to(who, (8, COL))
            hot = jnp.where(iota((SLOTS, COL), 0) == cell, 1.0, 0.0).astype(BF16)
            onehot[tile // 2, :, at : at + COL] = hot

    def table_split(part):
        high, low = split(table[part].reshape(GROUP * PART, SLOTS))
        return jnp.concatenate([high, low], axis=0)

    def product(both, tile):
        return dot(both, onehot[tile])

    def chosen(value, tile):
        value = value[0 : GROUP * PART] + value[GROUP * PART :]
        who = jnp.broadcast_to(owner[tile, 0:1, :], (PART, SLOTS))
        total = jnp.zeros((PART, SLOTS), F32)
        for q in range(GROUP):
            total = jnp.where(who == q, value[q * PART : (q + 1) * PART, :], total)
        return total[:, 0:COL], total[:, COL : 2 * COL]

    def fold(rests):
        turn = (lax.div(iota((8, COL), 1), SPARE) - iota((8, COL), 0)) & 7
        for half, rest in enumerate(rests):
            for s in range(FOLD):
                total = jnp.zeros((8, COL), F32)
                for d in range(8):
                    moved = rest[8 * s : 8 * s + 8, :]
                    if d:
                        moved = pltpu.roll(pltpu.roll(moved, SPARE * d, 1), 8 - d, 0)
                    total = jnp.where(turn == d, moved, total)
                rest_rows[half, s] = total

    def pick_all(part, both):
        sides = [(core * (GROUPS // 2) + (mine >> 1)) ^ place for place in FAR_FIRST]
        extra = list(range(TARGETS // 2 + 1, TILES))
        ends, value = [], product(both, extra[0])
        for tile, after in zip(extra, extra[1:] + [None]):
            now = value
            if after is not None:
                value = product(both, after)
            ends += chosen(now, tile)
        for side in range(2):
            for h in range(HALO):
                picked_rows[part, side, h] = ends[side * HALO + h]
        for side in range(2):
            l_copy(part, side).start()

        @pl.when(col_edge)
        def _():
            now, value = product(both, TARGETS // 2), product(both, sides[0])
            fold(chosen(now, TARGETS // 2))
            for step, tile in enumerate(sides):
                now = value
                if step + 1 < len(sides):
                    value = product(both, sides[step + 1])
                for i, end in enumerate(chosen(now, tile)):
                    target = 2 * tile + i
                    picked[part, target, 0:PART, :] = end
                    for s in range(FOLD):
                        picked[part, target, PART + s : PART + s + 1, :] = rest_rows[
                            tile >> 2, s, pl.ds(target & (GROUPS - 1), 1), :
                        ]
                for i in range(2):
                    b_copy(part, 2 * tile + i).start()

    def corrections(part, side, along_lanes):
        halo_ref, own_ref, add_ref = (col_halo, col_own, col_add) if along_lanes else (row_halo, row_out, row_add)

        def scaled(value, power):
            for _ in range(0 if along_lanes else power):
                value = scale * value
            return value

        halo = [[halo_ref[side, h, q * SHELLS : (q + 1) * SHELLS, :] for q in range(QUANTITIES)] for h in range(HALO)]
        form = cross_azimuthal if along_lanes else cross_polar
        halo_emf = [(cross_radial(x[MR:BR], x[BR:WARM]), form(x[MR:BR], x[BR:WARM])) for x in halo]
        sign = -1.0 if side == 0 else 1.0
        firsts, seconds = (45.0 * sign, -9.0 * sign, sign), (270.0, -27.0, 2.0)
        for j in range(HALO):
            own = [own_ref[part, side, j, q * SHELLS : (q + 1) * SHELLS, :] for q in range(QUANTITIES)]

            def total(weights, of):
                result = None
                for m in (1, 2, 3):
                    h = j + 3 - m if side == 0 else m - 3 + j
                    if 0 <= h < HALO:
                        term = weights[m - 1] * of(h)
                        result = term if result is None else result + term
                return result

            d = [scaled(total(firsts, lambda h, q=q: halo[h][q]), 1) for q in range(QUANTITIES)]
            lap = [
                None if q == S else scaled(total(seconds, lambda h, q=q: halo[h][q]), 2) for q in range(QUANTITIES)
            ]
            radial = scaled(total(firsts, lambda h: halo_emf[h][0]), 1)
            second = scaled(total(firsts, lambda h: halo_emf[h][1]), 1)
            result = edge_rates(own, d, lap, second, radial, along_lanes)
            for q in range(QUANTITIES):
                add_ref[side, j, q * SHELLS : (q + 1) * SHELLS, :] = (TIME_STEP / 60.0 / (1 + part)) * result[q]

    def contribute(side, along_lanes):
        add_ref = col_add if along_lanes else row_add
        value = jnp.concatenate([add_ref[side, j] for j in range(HALO)], axis=0)
        if along_lanes:
            value = jnp.where(iota((HALO * FLAT, COL), 1) < LON, value, 0.0)
        high, low = split(value)
        value = dot(jnp.concatenate([high, low, high], axis=1), rows_split[...] if along_lanes else mix[...])
        total = jnp.zeros((FLAT, SLOTS), F32)
        for j in range(HALO):
            if along_lanes:
                at = j if side == 0 else COL - HALO + j
                weight = cols_mix[at : at + 1, :]
            else:
                at = j if side == 0 else LON - HALO + j
                weight = rows_mix[at : at + 1, :]
            total = total + weight * value[j * FLAT : (j + 1) * FLAT, :]
        for half in range(2):
            blocks[1, half] = blocks[1, half] + total[half * PART : (half + 1) * PART, :]

    def apply_edges():
        for side in range(2):
            for j in range(HALO):
                rows = pl.ds(8 + (j if side == 0 else LON - HALO + j), FLAT, stride=STRIDE)
                frame[1, rows, :] = frame[1, rows, :] + row_add[side, j]
        turn_edges(col_add, turned)
        for half in range(2):
            edge = jnp.transpose(turned[half])[0:LON, :]
            for g in range(FLAT // 2):
                at = (half * (FLAT // 2) + g) * STRIDE + 8
                frame[1, at : at + LON, :] = frame[1, at : at + LON, :] + field_edge(edge, g)

    def a_copy(part, step, half):
        return remote(
            blocks.at[part, half], table.at[part, member], a_send.at[part, half, step], a_recv.at[part, member],
            row_device(step, half),
        )

    def s_copy(part, half):
        return remote(
            blocks.at[part, half], table.at[part, member], s_send.at[part], a_recv.at[part, member], sibling
        )

    def a_arrival(part, step):
        there = (member + step) & (GROUP - 1)
        return remote(blocks.at[part, 0], table.at[part, there], s_send.at[part], a_recv.at[part, there], sibling)

    def b_copy(part, target):
        return remote(
            picked.at[part, target], got_cols.at[part, origin], b_send.at[part, target], b_recv.at[part, origin],
            target_device(target),
        )

    def b_arrival(part, source):
        return remote(
            picked.at[part, 0], got_cols.at[part, source], b_send.at[part, 0], b_recv.at[part, source],
            (other, lon, col),
        )

    def l_copy(part, side):
        return remote(
            picked_rows.at[part, side], got_rows.at[part, origin], l_send.at[part, side], l_recv.at[part, origin],
            target_device(side * (TARGETS - 1)),
        )

    def l_arrival(part, source):
        return remote(
            picked_rows.at[part, 0], got_rows.at[part, source], l_send.at[part, 0], l_recv.at[part, source],
            (other, lon, col),
        )

    def row_copy(part, side):
        return remote(
            row_out.at[part, 1 - side], row_in.at[part, side], r_send.at[part, side], r_recv.at[part, side],
            (panel, lon_up if side == 0 else lon_down, col),
        )

    def col_copy(part, side):
        return remote(
            col_out.at[part, 1 - side], col_in.at[part, side], c_send.at[part, side], c_recv.at[part, side],
            (panel, lon, col_up if side == 0 else col_down),
        )

    def idx_copy(target):
        return remote(
            idx_out, idx_in.at[origin], idx_send.at[target], idx_recv.at[origin], target_device(target)
        )

    def idx_arrival(source):
        return remote(idx_out, idx_in.at[source], idx_send.at[0], idx_recv.at[source], (other, lon, col))

    def inner_sides(part):
        for side in range(2):
            @pl.when(lon != (0 if side == 0 else n_lon - 1))
            def _():
                row_copy(part, side).wait_recv()
                row_halo[side] = row_in[part, side]
                corrections(part, side, False)
                if part == 0:
                    contribute(side, False)

            @pl.when(col != (0 if side == 0 else n_col - 1))
            def _():
                col_copy(part, side).wait_recv()
                pair = col_in[part, side, 0]
                col_halo[side, 0] = pair
                col_halo[side, 1] = pltpu.roll(pair, COL // 2, 1)
                col_halo[side, 2] = col_in[part, side, 1]
                corrections(part, side, True)
                if part == 0:
                    contribute(side, True)

    def outer_sides(part):
        for side in range(2):

            @pl.when(col == (0 if side == 0 else n_col - 1))
            def _():
                for source in range(TARGETS):
                    b_arrival(part, source).wait_recv()
                for half in range(2):
                    total = got_cols[part, half * GROUPS]
                    for group in range(1, GROUPS):
                        total = total + got_cols[part, half * GROUPS + group]
                    main = total[0:PART]
                    rows = slice(half * PART, (half + 1) * PART)
                    col_halo[side, 0, rows, :] = main
                    col_halo[side, 1, rows, :] = pltpu.roll(main, COL - LON, 1)
                    main = pltpu.roll(main, COL - 2 * LON, 1)
                    row, lane = iota((8, COL), 0), iota((8, COL), 1)
                    for s in range(FOLD):
                        value = main[8 * s : 8 * s + 8, :]
                        rest = jnp.broadcast_to(total[PART + s : PART + s + 1], (8, COL))
                        for q in range(8):
                            moved = pltpu.roll(rest, (2 * COL - 2 * LON - SPARE * q) % COL, 1)
                            value = jnp.where(jnp.logical_and(row == q, lane >= COL - 2 * LON), moved, value)
                        at = half * PART + 8 * s
                        col_halo[side, 2, at : at + 8, :] = value
                corrections(part, side, True)
                if part == 0:
                    contribute(side, True)

            @pl.when(lon == (0 if side == 0 else n_lon - 1))
            def _():
                for source in range(TARGETS):
                    l_arrival(part, source).wait_recv()
                for half in range(2):
                    total = got_rows[part, half * GROUPS]
                    for group in range(1, GROUPS):
                        total = total + got_rows[part, half * GROUPS + group]
                    row_halo[side, :, half * PART : (half + 1) * PART, :] = total
                corrections(part, side, False)
                if part == 0:
                    contribute(side, False)

    for part in range(2):
        if part == 0:
            message_tables()
            copies[3].wait()
            interpolate(0, 0)
            copies[4].wait()
            interpolate(0, 1)
            pl.semaphore_wait(barrier, 2 * len(AROUND) + 2 + TARGETS)
            send(0, 0)
            send(0, 1)
            for place in CROSS_ORDER:
                idx_copy(origin ^ place).start()
            other_tables()
        else:
            send(1, 0)
            send(1, 1)
            apply_edges()
        rows_of(part)
        for side in range(2):

            @pl.when(sends_rows[side])
            def _():
                row_copy(part, side).start()

        cols_of(part)
        for side in range(2):

            @pl.when(sends_cols[side])
            def _():
                col_copy(part, side).start()

        lane_pass(part)
        emf_pass(part)
        if part == 0:
            for source in range(TARGETS):
                idx_arrival(source).wait_recv()
            prepare_picks()
        for step in range(1, GROUP):
            a_arrival(part, step).wait_recv()
        both = table_split(part)
        pick_all(part, both)
        main_pass(part, 0, 6)
        if part == 0:
            interpolate(1, 0)
            interpolate(1, 1)
        inner_sides(part)
        outer_sides(part)

    for target in range(TARGETS):
        idx_copy(target).wait_send()
    for part in range(2):
        for half in range(2):
            for step in AROUND:
                a_copy(part, step, half).wait_send()
        s_copy(part, 0).wait_send()
        for side in range(2):
            l_copy(part, side).wait_send()

            @pl.when(sends_rows[side])
            def _():
                row_copy(part, side).wait_send()

            @pl.when(sends_cols[side])
            def _():
                col_copy(part, side).wait_send()


        @pl.when(col_edge)
        def _():
            for target in range(TARGETS):
                b_copy(part, target).wait_send()


def shards(state, send_base, send_frac, recv_slots):
    rows = FLAT * LON
    dma = pltpu.SemaphoreType.DMA
    vmem = pltpu.VMEM
    scratch = [
        vmem((2, FLAT, STRIDE, COL), F32),
        vmem((1, OUT), I32),
        vmem((2, OUT), F32),
        vmem((1, recv_slots.shape[-1]), I32),
        vmem((3 * SHELLS * STRIDE, COL), F32),
        vmem(((FLAT + 2 * SHELLS) * LON, 2 * COL), F32),
        vmem((3 * COL, SLOTS), BF16),
        vmem((COL, SLOTS), F32),
        vmem((LON, SLOTS), F32),
        vmem((3 * COL, SLOTS), BF16),
        vmem((2 * COL, 2 * COL), BF16),
        vmem((TILES, SLOTS, 2 * COL), BF16),
        vmem((TILES, 8, 2 * COL), I32),
        vmem((2, COL, COL), F32),
        vmem((2, 2, PART, SLOTS), F32),
        vmem((2, GROUP, PART, SLOTS), F32),
        vmem((8, COL), I32),
        vmem((TARGETS, 8, COL), I32),
        vmem((2, FOLD, 8, COL), F32),
        vmem((2, TARGETS, PART + FOLD, COL), F32),
        vmem((2, 2, HALO, PART, COL), F32),
        vmem((2, TARGETS, PART + FOLD, COL), F32),
        vmem((2, TARGETS, HALO, PART, COL), F32),
        vmem((2, 2, HALO, FLAT, COL), F32),
        vmem((2, 2, HALO, FLAT, COL), F32),
        vmem((2, 2, HALO, FLAT, COL), F32),
        vmem((2, 2, 2, FLAT, COL), F32),
        vmem((2, 2, 2, FLAT, COL), F32),
        vmem((2, HALO, FLAT, COL), F32),
        vmem((2, HALO, FLAT, COL), F32),
        dma((5,)),
        dma((TARGETS,)),
        dma((TARGETS,)),
        dma((2, 2, RING)),
        dma((2, GROUP)),
        dma((2,)),
        dma((2, TARGETS)),
        dma((2, TARGETS)),
        dma((2, 2)),
        dma((2, TARGETS)),
        dma((2, 2)),
        dma((2, 2)),
        dma((2, 2)),
        dma((2, 2)),
    ]
    edges = jax.ShapeDtypeStruct((2, HALO, FLAT, COL), F32)
    value, row_add, col_add = pl.pallas_call(
        kernel,
        out_shape=(jax.ShapeDtypeStruct((rows, COL), F32), edges, edges),
        in_specs=[pl.BlockSpec(memory_space=pltpu.HBM)] * 4,
        out_specs=[pl.BlockSpec(memory_space=pltpu.VMEM)] * 3,
        scratch_shapes=scratch,
        compiler_params=pltpu.CompilerParams(
            collective_id=0, has_side_effects=True, vmem_limit_bytes=40 * 1024 * 1024
        ),
    )(*(
        pltpu.with_memory_space_constraint(x, pltpu.HBM)
        for x in (state.reshape(FLAT, LON, COL), send_base[0], send_frac[0, 0], recv_slots[0])
    ))
    result = pl.pallas_call(
        closing,
        out_shape=jax.ShapeDtypeStruct((rows, COL), F32),
        in_specs=[pl.BlockSpec(memory_space=pltpu.VMEM)] * 3,
        out_specs=pl.BlockSpec(memory_space=pltpu.HBM),
        scratch_shapes=[vmem((2, COL, COL), F32), vmem((rows, COL), F32), dma((8,))],
        compiler_params=pltpu.CompilerParams(vmem_limit_bytes=16 * 1024 * 1024),
    )(value, row_add, col_add)
    return result.reshape(state.shape)


def solution(mesh):
    placed = (
        P("panel", None, None, "lon", "colat"),
        P("panel", ("lon", "colat"), None),
        P("panel", ("lon", "colat"), None, None),
        P("panel", ("lon", "colat"), None),
    )
    return jax.shard_map(
        shards,
        mesh=mesh,
        in_specs=placed,
        out_specs=P("panel", None, None, "lon", "colat"),
        check_vma=False,
    )
```
